32 devices in a mesh: fsdp: 4 (over z), ctx: 4 (over x, core), tp: 2 (over y).
Axes of the slice: x: 2, y: 2, z: 4, core: 2. Of those that a mesh axis runs over, the one named last changes fastest.
Arguments:
- inputs: float32 [4, 640, 1024], P('fsdp', 'ctx'), may hold values from -6 to 6
- lengths: int32 [4, 4], P('fsdp'), may hold values from 1 to 160, 513 in all within a row
- cotangent: float32 [4, 640, 1024], P('fsdp', 'ctx'), may hold values from -6 to 6
- norm_gains: bfloat16 [2, 2, 1024], P(None, None, 'fsdp'), may hold values from 0.5 to 1.5
- shifts: bfloat16 [2, 4, 1024], P(None, None, 'fsdp'), may hold values from -2 to 2
- qv_bias: bfloat16 [2, 2, 16, 64], P(None, None, 'tp', 'fsdp'), may hold values from -3 to 3
- fc1_bias: bfloat16 [2, 2, 2048], P(None, 'tp', 'fsdp'), may hold values from -3 to 3
- w_qkv: bfloat16 [2, 3, 1024, 1024], P(None, None, 'fsdp', 'tp'), may hold values from -1 to 1
- w_out: bfloat16 [2, 1024, 1024], P(None, 'tp', 'fsdp'), may hold values from -0.375 to 0.375
- w_fc1: bfloat16 [2, 1024, 4096], P(None, 'fsdp', 'tp'), may hold values from -0.1875 to 0.1875
- w_fc2: bfloat16 [2, 4096, 1024], P(None, 'tp', 'fsdp'), may hold values from -0.09375 to 0.09375
Outputs:
- outputs: float32 [4, 640, 1024], P('fsdp', 'ctx')
- grad_inputs: float32 [4, 640, 1024], P('fsdp', 'ctx')
- grad_gains: float32 [2, 2, 1024], P(None, None, 'fsdp')
- grad_shifts: float32 [2, 4, 1024], P(None, None, 'fsdp')
- grad_qv_bias: float32 [2, 2, 16, 64], P(None, None, 'tp', 'fsdp')
- grad_fc1_bias: float32 [2, 2, 2048], P(None, 'tp', 'fsdp')
- grad_w_qkv: float32 [2, 3, 1024, 1024], P(None, None, 'fsdp', 'tp')
- grad_w_out: float32 [2, 1024, 1024], P(None, 'tp', 'fsdp')
- grad_w_fc1: float32 [2, 1024, 4096], P(None, 'fsdp', 'tp')
- grad_w_fc2: float32 [2, 4096, 1024], P(None, 'tp', 'fsdp')
The draws below stay inside these ranges and needn't reach their ends.
Inputs may be any that keep to these rules, and one draw needn't show every extreme that they name: Each image's 4 block lengths sum to 513; block c holds the image's next tokens in order, the class token first in block 0; rows of a block past its length are padding; some block of every image holds exactly 160.
All inputs are finite; a program needn't handle non-finite values.
Results may differ from the reference program's by a relative error of at most 0.017.
Values may be sent and summed in bfloat16 or wider, within the bound.
No kernel may reach another device: no remote copies, remote signals or barrier semaphores. Data moves between devices by JAX's collectives and lax.ppermute only.
A program may use at most 256 MiB of HBM per device.

```python
import math
import jax
import jax.numpy as jnp
import numpy as np
from jax import lax

D = 1024
H = 16
HD = 64
FF = 4096
L = 2
CAP = 160
TOKENS = 513
ROWS = 640
IMAGES = 4
N_CTX = 4
N_TP = 2


def draw_w_qkv(key, part):
    key = jax.random.fold_in(key, 11)
    slice_scale = jnp.array([1.3, 1.3, 1.0], jnp.float32).reshape(1, 3, 1, 1) / math.sqrt(D)
    raw = jnp.clip(jax.random.normal(key, (L, 3, D, D), jnp.float32), -4.0, 4.0)
    return (raw * slice_scale).astype(jnp.bfloat16)


def block_levels(rng, extent, cuts, smallest, largest):
    def one(dim, parts):
        draws = jax.random.uniform(jax.random.fold_in(jax.random.fold_in(rng, 6), dim), (parts,), jnp.float32, smallest / len(cuts), largest / len(cuts))
        return jnp.repeat(jnp.exp(draws), extent[dim] // parts).reshape((-1,) + (1,) * (len(extent) - dim - 1))

    factor_of = one(*cuts[0])
    for cut in cuts[1:]:
        factor_of = factor_of * one(*cut)
    return factor_of


def length_profile(count, total, reach, skew):
    portions = [(1 << 20) // math.isqrt(standing ** skew) + 1 for standing in range(2, count + 1)]
    surplus, counts = total - reach - (count - 1), [1] * (count - 1)
    while surplus > 0:
        free = [i for i in range(count - 1) if counts[i] < reach]
        mass, left = sum([portions[i] for i in free]), surplus
        for i in free:
            more = min(reach - counts[i], max(1, left * portions[i] // mass), surplus)
            counts[i] = counts[i] + more
            surplus = surplus - more
    return np.array([reach] + counts)


def ragged(own_key, number_of, total, bound, lean):
    if number_of == 2:
        one = jax.random.randint(own_key, (), max(1, total - bound), min(bound, total - 1) + 1)
        return jnp.stack([one, total - one])
    sizes = jnp.asarray(length_profile(number_of, total, bound, lean), jnp.int32)
    pairs = (number_of - 1) // 2
    donor, receiver = sizes[1:1 + 2 * pairs:2], sizes[2:2 + 2 * pairs:2]
    slack = jnp.minimum(donor - 1, bound - receiver)
    moved = jax.random.randint(jax.random.fold_in(own_key, 1), (pairs,), 0, 1 << 20) % (slack + 1)
    sizes = sizes.at[1:1 + 2 * pairs:2].set(donor - moved).at[2:2 + 2 * pairs:2].set(receiver + moved)
    return sizes[jax.random.permutation(jax.random.fold_in(own_key, 2), number_of)]


def noise(rng, shape, width, bound, pieces=(), kind=jnp.bfloat16):
    values = jax.random.normal(rng, shape, jnp.float32) * width
    if len(pieces) > 0:
        values = block_levels(rng, shape, pieces, -0.22, 0.18) * values
    return jnp.clip(values, min=-bound, max=bound).astype(kind)


def setup_inputs(seed: int = 0) -> dict:
    streams_of = jax.random.split(jax.random.key(seed), 12)
    return {
        "inputs": noise(streams_of[0], (IMAGES, ROWS, D), 1.0, 6.0, ((0, 4), (1, 4)), jnp.float32),
        "lengths": jax.vmap(lambda own: ragged(own, N_CTX, TOKENS, CAP, 2))(jax.random.split(streams_of[1], IMAGES)).reshape((IMAGES, N_CTX)).astype(jnp.int32),
        "cotangent": noise(streams_of[2], (IMAGES, ROWS, D), 1.0, 6.0, ((0, 4), (1, 4)), jnp.float32),
        "norm_gains": jnp.clip(1.0 + 0.1 * jax.random.normal(streams_of[3], (L, 2, D), jnp.float32), 0.5, 1.5).astype(jnp.bfloat16),
        "shifts": noise(streams_of[4], (L, 4, D), 0.3, 2.0, ((2, 4),)),
        "qv_bias": noise(streams_of[5], (L, 2, H, HD), 0.5, 3.0, ((2, 2), (3, 4))),
        "fc1_bias": noise(streams_of[6], (L, N_TP, FF // N_TP), 0.5, 3.0, ((1, 2), (2, 4))),
        "w_qkv": draw_w_qkv(jax.random.fold_in(streams_of[11], 71), 0),
        "w_out": noise(streams_of[8], (L, D, D), (D // 4) ** -0.5, 0.375, ((1, 2), (2, 4))),
        "w_fc1": noise(streams_of[9], (L, D, FF), D ** -0.5, 0.1875, ((1, 4), (2, 2))),
        "w_fc2": noise(streams_of[10], (L, FF, D), FF ** -0.5, 0.09375, ((1, 2), (2, 4))),
    }


NORM_EPSILON = 1e-06
MASK_FILL = -1e+30
ROOT_HALF = 0.7071067811865476
INV_ROOT_TAU = 0.3989422804014327

def norm_forward(values, gain, shift):
    center = values - lax.optimization_barrier(jnp.mean(values, axis=-1, keepdims=True))
    inverse = lax.rsqrt(lax.optimization_barrier(jnp.mean(center * center, axis=-1, keepdims=True)) + NORM_EPSILON)
    normed = center * inverse
    return (normed * gain + shift, normed, inverse)

def norm_backward(upstream, normed, inverse, gain):
    scaled = upstream * gain
    result = inverse * (scaled - lax.optimization_barrier(jnp.mean(scaled, axis=-1, keepdims=True)) - normed * lax.optimization_barrier(jnp.mean(scaled * normed, axis=-1, keepdims=True)))
    return (result, lax.optimization_barrier(jnp.sum(upstream * normed, axis=0)), lax.optimization_barrier(jnp.sum(upstream, axis=0)))

def gelu_parts(hidden):
    normal_cdf = 0.5 * (1.0 + lax.erf(hidden * ROOT_HALF))
    density = jnp.exp(-0.5 * hidden * hidden) * INV_ROOT_TAU
    return (hidden * normal_cdf, normal_cdf + hidden * density)

def attend_forward(queries, keys, values, usable, score_scale):
    query_blocks = queries.reshape(-1, CAP, H, HD)
    keys_f = keys.astype(jnp.float32)
    values_f = values.astype(jnp.float32)

    def one_block(query_block):
        scores = jnp.einsum('qhd,khd->hqk', query_block.astype(jnp.float32), keys_f) * score_scale
        scores = jnp.where(usable[None, None, :], scores, MASK_FILL)
        highest = lax.optimization_barrier(jnp.max(scores, axis=-1, keepdims=True))
        log_norm = highest + jnp.log(lax.optimization_barrier(jnp.sum(jnp.exp(scores - highest), axis=-1, keepdims=True)))
        soft = jnp.exp(scores - log_norm).astype(jnp.bfloat16)
        attended = jnp.einsum('hqk,khd->qhd', soft.astype(jnp.float32), values_f).astype(jnp.bfloat16)
        return (attended, log_norm[..., 0])
    attended, log_norm = lax.map(one_block, query_blocks)
    return (attended.reshape(queries.shape), log_norm)

def attend_backward(queries, keys, values, attended, grad_attended, log_norm, usable, score_scale):
    keys_f = keys.astype(jnp.float32)
    values_f = values.astype(jnp.float32)
    query_blocks = queries.reshape(-1, CAP, H, HD)
    attended_blocks = attended.reshape(-1, CAP, H, HD)
    grad_blocks = grad_attended.reshape(-1, CAP, H, HD)

    def one_block(running, element):
        grad_keys, grad_values = running
        query_block, attended_block, grad_block, norm_block = element
        grad_block_f = grad_block.astype(jnp.float32)
        scores = jnp.einsum('qhd,khd->hqk', query_block.astype(jnp.float32), keys_f) * score_scale
        scores = jnp.where(usable[None, None, :], scores, MASK_FILL)
        soft_f = jnp.exp(scores - norm_block[..., None])
        soft_b = soft_f.astype(jnp.bfloat16).astype(jnp.float32)
        grad_values = grad_values + jnp.einsum('hqk,qhd->khd', soft_b, grad_block_f)
        grad_soft = jnp.einsum('qhd,khd->hqk', grad_block_f, values_f)
        row_dots = lax.optimization_barrier(jnp.sum(grad_block_f * attended_block.astype(jnp.float32), axis=-1)).T
        grad_scores = (soft_f * (grad_soft - row_dots[..., None])).astype(jnp.bfloat16).astype(jnp.float32)
        grad_queries = jnp.einsum('hqk,khd->qhd', grad_scores, keys_f) * score_scale
        grad_keys = grad_keys + jnp.einsum('hqk,qhd->khd', grad_scores, query_block.astype(jnp.float32)) * score_scale
        return ((grad_keys, grad_values), grad_queries)
    zeros_kv = jnp.zeros(keys.shape, jnp.float32)
    (grad_keys, grad_values), grad_queries = lax.scan(one_block, (zeros_kv, zeros_kv), (query_blocks, attended_blocks, grad_blocks, log_norm))
    return (grad_queries.reshape(queries.shape), grad_keys, grad_values)

def reference(inputs, lengths, cotangent, norm_gains, shifts, qv_bias, fc1_bias, w_qkv, w_out, w_fc1, w_fc2):
    rows_all = N_CTX * CAP
    score_scale = 1.0 / math.sqrt(HD)
    depth = w_qkv.shape[0]
    bf16 = jnp.bfloat16
    f32 = jnp.float32

    def layer_forward(stream, layer_index, usable):
        gain_pair = norm_gains[layer_index].astype(f32)
        shift_set = shifts[layer_index].astype(f32)
        qv_pair = qv_bias[layer_index].astype(f32).reshape(2, D)
        fc1_row = fc1_bias[layer_index].astype(f32).reshape(FF)
        weights = w_qkv[layer_index]
        first, normed_one, inverse_one = norm_forward(stream, gain_pair[0], shift_set[0])
        first_b = first.astype(bf16)
        queries = (jnp.dot(first_b, weights[0], preferred_element_type=f32) + qv_pair[0]).astype(bf16)
        keys = jnp.dot(first_b, weights[1], preferred_element_type=f32).astype(bf16)
        values = (jnp.dot(first_b, weights[2], preferred_element_type=f32) + qv_pair[1]).astype(bf16)
        attended, log_norm = attend_forward(queries.reshape(rows_all, H, HD), keys.reshape(rows_all, H, HD), values.reshape(rows_all, H, HD), usable, score_scale)
        attended_b = attended.reshape(rows_all, D)
        middle = stream + jnp.dot(attended_b, w_out[layer_index], preferred_element_type=f32) + shift_set[2]
        second, normed_two, inverse_two = norm_forward(middle, gain_pair[1], shift_set[1])
        second_b = second.astype(bf16)
        pre = jnp.dot(second_b, w_fc1[layer_index], preferred_element_type=f32) + fc1_row
        activated, slope = gelu_parts(pre)
        activated_b = activated.astype(bf16)
        output = middle + jnp.dot(activated_b, w_fc2[layer_index], preferred_element_type=f32) + shift_set[3]
        saved = (normed_one, inverse_one, first_b, queries, keys, values, attended_b, log_norm, normed_two, inverse_two, second_b, slope, activated_b)
        return (output, saved)

    def layer_backward(upstream, saved, layer_index, usable):
        normed_one, inverse_one, first_b, queries, keys, values, attended_b, log_norm, normed_two, inverse_two, second_b, slope, activated_b = saved
        gain_pair = norm_gains[layer_index].astype(f32)
        weights = w_qkv[layer_index]
        upstream_b = upstream.astype(bf16)
        grad_fc2 = jnp.dot(activated_b.T, upstream_b, preferred_element_type=f32)
        grad_c2 = lax.optimization_barrier(jnp.sum(upstream, axis=0))
        grad_pre = jnp.dot(upstream_b, w_fc2[layer_index].T, preferred_element_type=f32) * slope
        grad_pre_b = grad_pre.astype(bf16)
        grad_fc1 = jnp.dot(second_b.T, grad_pre_b, preferred_element_type=f32)
        grad_c1 = lax.optimization_barrier(jnp.sum(grad_pre, axis=0))
        grad_second = jnp.dot(grad_pre_b, w_fc1[layer_index].T, preferred_element_type=f32)
        back_two, grad_g2, grad_b2 = norm_backward(grad_second, normed_two, inverse_two, gain_pair[1])
        grad_middle = upstream + back_two
        middle_b = grad_middle.astype(bf16)
        grad_wo = jnp.dot(attended_b.T, middle_b, preferred_element_type=f32)
        grad_bo = lax.optimization_barrier(jnp.sum(grad_middle, axis=0))
        grad_attended = jnp.dot(middle_b, w_out[layer_index].T, preferred_element_type=f32).astype(bf16)
        grad_q, grad_k, grad_v = attend_backward(queries.reshape(rows_all, H, HD), keys.reshape(rows_all, H, HD), values.reshape(rows_all, H, HD), attended_b.reshape(rows_all, H, HD), grad_attended.reshape(rows_all, H, HD), log_norm, usable, score_scale)
        grad_q = grad_q.reshape(rows_all, D)
        grad_k = grad_k.reshape(rows_all, D)
        grad_v = grad_v.reshape(rows_all, D)
        grad_q_b = grad_q.astype(bf16)
        grad_k_b = grad_k.astype(bf16)
        grad_v_b = grad_v.astype(bf16)
        grad_qkv = jnp.stack([jnp.dot(first_b.T, grad_q_b, preferred_element_type=f32), jnp.dot(first_b.T, grad_k_b, preferred_element_type=f32), jnp.dot(first_b.T, grad_v_b, preferred_element_type=f32)])
        grad_first = jnp.dot(grad_q_b, weights[0].T, preferred_element_type=f32) + jnp.dot(grad_k_b, weights[1].T, preferred_element_type=f32) + jnp.dot(grad_v_b, weights[2].T, preferred_element_type=f32)
        back_one, grad_g1, grad_b1 = norm_backward(grad_first, normed_one, inverse_one, gain_pair[0])
        grads = (jnp.stack([grad_g1, grad_g2]), jnp.stack([grad_b1, grad_b2, grad_bo, grad_c2]), jnp.stack([lax.optimization_barrier(jnp.sum(grad_q, axis=0)), lax.optimization_barrier(jnp.sum(grad_v, axis=0))]).reshape(2, H, HD), grad_c1.reshape(N_TP, FF // N_TP), grad_qkv, grad_wo, grad_fc1, grad_fc2)
        return (grad_middle + back_one, grads)

    def image_pass(running, element):
        image_in, image_lengths, image_cot = element
        positions = jnp.arange(rows_all, dtype=jnp.int32)
        source = positions // CAP
        usable = positions - source * CAP < image_lengths[source]
        row_mask = usable.astype(f32)[:, None]
        stream = image_in
        saved_all = []
        for layer_index in range(depth):
            stream, saved = layer_forward(stream, layer_index, usable)
            saved_all.append(saved)
        image_out = stream * row_mask
        upstream = image_cot * row_mask
        grads_all = [None] * depth
        for layer_index in reversed(range(depth)):
            upstream, grads_all[layer_index] = layer_backward(upstream, saved_all[layer_index], layer_index, usable)
        image_grad = upstream * row_mask
        stacked = tuple((jnp.stack([grads_all[layer_index][member] for layer_index in range(depth)]) for member in range(8)))
        running = tuple((total_part + new_part for total_part, new_part in zip(running, stacked)))
        return (running, (image_out, image_grad))
    start_sums = (jnp.zeros(norm_gains.shape, f32), jnp.zeros(shifts.shape, f32), jnp.zeros(qv_bias.shape, f32), jnp.zeros(fc1_bias.shape, f32), jnp.zeros(w_qkv.shape, f32), jnp.zeros(w_out.shape, f32), jnp.zeros(w_fc1.shape, f32), jnp.zeros(w_fc2.shape, f32))
    sums, (outputs, grad_inputs) = lax.scan(image_pass, start_sums, (inputs, lengths, cotangent))
    return (outputs, grad_inputs, sums[0], sums[1], sums[2], sums[3], sums[4], sums[5], sums[6], sums[7])
```

```python
import math

import jax
import jax.numpy as jnp
from jax import lax
from jax.sharding import PartitionSpec as P

NORM_EPSILON = 1e-06
MASK_FILL = -1e30
ROOT_HALF = 0.7071067811865476
INV_ROOT_TAU = 0.3989422804014327
GROUP = 4
ORDER = (0, 1, 4, 5, 2, 3, 6, 7)

bf16 = jnp.bfloat16
f32 = jnp.float32


def dot(a, b):
    return lax.dot_general(a, b, (((1,), (0,)), ((), ())), preferred_element_type=f32)


def dot_nt(a, b):
    return lax.dot_general(a, b, (((1,), (1,)), ((), ())), preferred_element_type=f32)


def dot_tn(a, b):
    return lax.dot_general(a, b, (((0,), (0,)), ((), ())), preferred_element_type=f32)


def norm_forward(values, gain, shift):
    center = values - jnp.mean(values, axis=-1, keepdims=True)
    inverse = lax.rsqrt(jnp.mean(center * center, axis=-1, keepdims=True) + NORM_EPSILON)
    normed = center * inverse
    return (normed * gain + shift, normed, inverse)


def norm_backward(upstream, normed, inverse, gain):
    scaled = upstream * gain
    result = inverse * (
        scaled
        - jnp.mean(scaled, axis=-1, keepdims=True)
        - normed * jnp.mean(scaled * normed, axis=-1, keepdims=True)
    )
    return (result, jnp.sum(upstream * normed, axis=0), jnp.sum(upstream, axis=0))


def gelu_parts(hidden):
    normal_cdf = 0.5 * (1.0 + lax.erf(hidden * ROOT_HALF))
    density = jnp.exp(-0.5 * hidden * hidden) * INV_ROOT_TAU
    return (hidden * normal_cdf, normal_cdf + hidden * density)


def per_device(
    inputs, lengths, cotangent, norm_gains, shifts, qv_bias, fc1_bias, w_qkv, w_out, w_fc1, w_fc2
):
    depth = w_qkv.shape[0]
    width_own = w_qkv.shape[2]
    local_rows = inputs.shape[1]
    fsdp = lax.axis_size("fsdp")
    tp = lax.axis_size("tp")
    ctx = lax.axis_size("ctx")
    outer = ctx // GROUP
    own_rows = local_rows // tp
    all_rows = own_rows * tp * GROUP
    half_rows = all_rows // 2
    head_dim = qv_bias.shape[3] * fsdp
    heads = qv_bias.shape[2] // GROUP
    feats = heads * head_dim
    hidden = w_fc1.shape[2] // GROUP
    score_scale = 1.0 / math.sqrt(head_dim)
    c = lax.axis_index("ctx")
    t = lax.axis_index("tp")
    f = lax.axis_index("fsdp")
    ci = c % GROUP
    place = ci * tp + t

    def swap_core(value):
        return lax.ppermute(value, "ctx", [(i, i ^ 1) for i in range(ctx)])

    def swap_x(value):
        return lax.ppermute(value, "ctx", [(i, i ^ 2) for i in range(ctx)])

    def swap_y(value):
        return lax.ppermute(value, "tp", [(i, i ^ 1) for i in range(tp)])

    def swap_xy(value):
        pairs = [
            (i * tp + k, (i ^ 2) * tp + (k ^ 1)) for i in range(ctx) for k in range(tp)
        ]
        return lax.ppermute(value, ("ctx", "tp"), pairs)

    outer_groups = [[o * GROUP + i for o in range(outer)] for i in range(GROUP)]

    def gather_rows(own):
        near = jnp.concatenate([own, swap_y(own), swap_x(own), swap_xy(own)], axis=0)
        return jnp.concatenate([near, swap_core(near)], axis=0)

    def reduce_rows(partial):
        far = swap_core(partial[half_rows:].astype(bf16))
        near = partial[:half_rows] + far.astype(f32)
        near_b = near[own_rows:].astype(bf16)
        got_y = swap_y(near_b[:own_rows])
        got_x = swap_x(near_b[own_rows : 2 * own_rows])
        got_xy = swap_xy(near_b[2 * own_rows :])
        return near[:own_rows] + got_y.astype(f32) + got_x.astype(f32) + got_xy.astype(f32)

    offsets = jnp.arange(own_rows, dtype=jnp.int32)
    marks = []
    for o in range(outer):
        for d in ORDER:
            source = place ^ d
            length = lax.dynamic_index_in_dim(
                lengths[0], o * GROUP + source // tp, 0, keepdims=False
            )
            marks.append((source % tp) * own_rows + offsets < length)
    usable = jnp.concatenate(marks)
    own_length = lax.dynamic_index_in_dim(lengths[0], c, 0, keepdims=False)
    own_first = t * own_rows
    row_mask = (own_first + offsets < own_length).astype(f32)[:, None]

    def own_part(block):
        return lax.dynamic_slice_in_dim(block[0], own_first, own_rows, axis=0)

    def gather_small(value, axis):
        return lax.all_gather(value, "fsdp", axis=axis, tiled=True)

    small = jnp.concatenate([norm_gains, shifts], axis=1)
    small = gather_small(small, 2).astype(f32)
    gains_all, shifts_all = small[:, :2], small[:, 2:]
    qv_own = lax.dynamic_slice_in_dim(qv_bias, ci * heads, heads, axis=2)
    qv_all = gather_small(qv_own, 3).astype(f32).reshape(depth, 2, feats)
    fc1_all = gather_small(fc1_bias, 2)[:, 0]
    fc1_all = lax.dynamic_slice_in_dim(fc1_all, ci * hidden, hidden, axis=1).astype(f32)

    attn_w = []
    mlp_w = []
    for l in range(depth):
        qkv = lax.dynamic_slice_in_dim(w_qkv[l], ci * feats, feats, axis=2)
        out = lax.dynamic_slice_in_dim(w_out[l], ci * feats, feats, axis=0)
        fc1 = lax.dynamic_slice_in_dim(w_fc1[l], ci * hidden, hidden, axis=1)
        fc2 = lax.dynamic_slice_in_dim(w_fc2[l], ci * hidden, hidden, axis=0)
        attn_w.append(gather_small(jnp.concatenate([qkv[0], qkv[1], qkv[2], out.T], axis=1), 0))
        mlp_w.append(gather_small(jnp.concatenate([fc1, fc2.T], axis=1), 0))

    stream = own_part(inputs)
    upstream = own_part(cotangent) * row_mask
    upstream_all = gather_rows(upstream.astype(bf16))

    saved_all = []
    for l in range(depth):
        w_in = attn_w[l][:, : 3 * feats]
        w_o = attn_w[l][:, 3 * feats :]
        w_1 = mlp_w[l][:, :hidden]
        w_2 = mlp_w[l][:, hidden:]
        first, normed_one, inverse_one = norm_forward(stream, gains_all[l, 0], shifts_all[l, 0])
        first_all = gather_rows(first.astype(bf16))
        qkv = dot(first_all, w_in)
        queries = (qkv[:, :feats] + qv_all[l, 0]).astype(bf16)
        keys = qkv[:, feats : 2 * feats].astype(bf16)
        values = (qkv[:, 2 * feats :] + qv_all[l, 1]).astype(bf16)
        if outer > 1:
            keys, values = (
                lax.all_gather(v, "ctx", axis=0, tiled=True, axis_index_groups=outer_groups)
                for v in (keys, values)
            )
        attended = []
        norms = []
        for h in range(heads):
            cols = slice(h * head_dim, (h + 1) * head_dim)
            scores = dot_nt(queries[:, cols], keys[:, cols]) * score_scale
            scores = jnp.where(usable[None, :], scores, MASK_FILL)
            highest = jnp.max(scores, axis=-1, keepdims=True)
            log_norm = highest + jnp.log(
                jnp.sum(jnp.exp(scores - highest), axis=-1, keepdims=True)
            )
            soft = jnp.exp(scores - log_norm).astype(bf16)
            attended.append(dot(soft, values[:, cols]).astype(bf16))
            norms.append(log_norm)
        attended = jnp.concatenate(attended, axis=1)
        middle = stream + reduce_rows(dot_nt(attended, w_o)) + shifts_all[l, 2]
        second, normed_two, inverse_two = norm_forward(middle, gains_all[l, 1], shifts_all[l, 1])
        second_all = gather_rows(second.astype(bf16))
        pre = dot(second_all, w_1) + fc1_all[l]
        activated, slope = gelu_parts(pre)
        activated = activated.astype(bf16)
        stream = middle + reduce_rows(dot_nt(activated, w_2)) + shifts_all[l, 3]
        saved_all.append(
            (
                normed_one,
                inverse_one,
                first_all,
                queries,
                keys,
                values,
                attended,
                norms,
                normed_two,
                inverse_two,
                second_all,
                slope,
                activated,
            )
        )
    outputs_own = stream * row_mask

    small_grads = [None] * depth
    owned = [None] * depth
    for l in reversed(range(depth)):
        (
            normed_one,
            inverse_one,
            first_all,
            queries,
            keys,
            values,
            attended,
            norms,
            normed_two,
            inverse_two,
            second_all,
            slope,
            activated,
        ) = saved_all[l]
        w_in = attn_w[l][:, : 3 * feats]
        w_o = attn_w[l][:, 3 * feats :]
        w_1 = mlp_w[l][:, :hidden]
        w_2 = mlp_w[l][:, hidden:]
        grad_c2 = jnp.sum(upstream, axis=0)
        grad_pre = dot(upstream_all, w_2) * slope
        grad_pre_b = grad_pre.astype(bf16)
        grad_second = reduce_rows(dot_nt(grad_pre_b, w_1))
        grad_c1 = jnp.sum(grad_pre, axis=0)
        mlp_grad = jnp.concatenate(
            [
                dot_tn(second_all, grad_pre_b).astype(bf16),
                dot_tn(upstream_all, activated).astype(bf16),
            ],
            axis=1,
        )
        back_two, grad_g2, grad_b2 = norm_backward(
            grad_second, normed_two, inverse_two, gains_all[l, 1]
        )
        grad_middle = upstream + back_two
        grad_bo = jnp.sum(grad_middle, axis=0)
        middle_all = gather_rows(grad_middle.astype(bf16))
        grad_attended = dot(middle_all, w_o).astype(bf16)
        row_products = grad_attended.astype(f32) * attended.astype(f32)
        grad_q = []
        grad_k = []
        grad_v = []
        for h in range(heads):
            cols = slice(h * head_dim, (h + 1) * head_dim)
            row_dots = jnp.sum(row_products[:, cols], axis=-1, keepdims=True)
            scores = dot_nt(queries[:, cols], keys[:, cols]) * score_scale
            scores = jnp.where(usable[None, :], scores, MASK_FILL)
            soft_f = jnp.exp(scores - norms[h])
            grad_soft = dot_nt(grad_attended[:, cols], values[:, cols])
            grad_scores = (soft_f * (grad_soft - row_dots)).astype(bf16)
            grad_q.append(dot(grad_scores, keys[:, cols]) * score_scale)
            grad_k.append(dot_tn(grad_scores, queries[:, cols]) * score_scale)
            grad_v.append(dot_tn(soft_f.astype(bf16), grad_attended[:, cols]))
        grad_q = jnp.concatenate(grad_q, axis=1)
        grad_k = jnp.concatenate(grad_k, axis=1)
        grad_v = jnp.concatenate(grad_v, axis=1)
        if outer > 1:
            grad_k, grad_v = (
                lax.psum_scatter(
                    v, "ctx", scatter_dimension=0, tiled=True, axis_index_groups=outer_groups
                )
                for v in (grad_k, grad_v)
            )
        grad_qkv = jnp.concatenate([grad_q, grad_k, grad_v], axis=1).astype(bf16)
        grad_first = reduce_rows(dot_nt(grad_qkv, w_in))
        attn_grad = jnp.concatenate(
            [
                dot_tn(first_all, grad_qkv).astype(bf16),
                dot_tn(middle_all, attended).astype(bf16),
            ],
            axis=1,
        )
        grad_qv = jnp.stack([jnp.sum(grad_q, axis=0), jnp.sum(grad_v, axis=0)])
        back_one, grad_g1, grad_b1 = norm_backward(
            grad_first, normed_one, inverse_one, gains_all[l, 0]
        )
        upstream = grad_middle + back_one
        if l > 0:
            upstream_all = gather_rows(upstream.astype(bf16))
        owned_l = []
        for grad in (mlp_grad, attn_grad):
            part = lax.psum_scatter(grad, "fsdp", scatter_dimension=0, tiled=True)
            if outer > 1:
                part = lax.psum(part, "ctx", axis_index_groups=outer_groups)
                inner_groups = [[o * GROUP + i for i in range(GROUP)] for o in range(outer)]
                part = lax.all_gather(part, "ctx", axis=0, axis_index_groups=inner_groups)
            else:
                part = lax.all_gather(part, "ctx", axis=0)
            owned_l.append(part.astype(f32))
        owned[l] = owned_l
        small_grads[l] = (grad_g1, grad_g2, grad_b1, grad_b2, grad_bo, grad_c2, grad_qv, grad_c1)

    grad_inputs_own = upstream * row_mask

    def both_halves(own):
        other = swap_y(own)
        return jnp.where(
            t == 0,
            jnp.concatenate([own, other], axis=0),
            jnp.concatenate([other, own], axis=0),
        )[None]

    outputs = both_halves(outputs_own)
    grad_inputs = both_halves(grad_inputs_own)

    width = width_own * fsdp
    qv_full = jnp.zeros((depth, 2, tp * GROUP, feats), f32)
    qv_full = lax.dynamic_update_slice_in_dim(
        qv_full,
        jnp.stack([small_grads[l][6] for l in range(depth)])[:, :, None, :],
        t * GROUP + ci,
        axis=2,
    )
    c1_full = jnp.zeros((depth, tp * GROUP, hidden), f32)
    c1_full = lax.dynamic_update_slice_in_dim(
        c1_full,
        jnp.stack([small_grads[l][7] for l in range(depth)])[:, None, :],
        t * GROUP + ci,
        axis=1,
    )
    rows = jnp.stack([small_grads[l][k] for l in range(depth) for k in range(6)])
    packed = jnp.concatenate(
        [rows, qv_full.reshape(-1, width), c1_full.reshape(-1, width)], axis=0
    )
    packed = lax.psum(packed, ("fsdp", "ctx", "tp"))
    cut = 6 * depth
    rows = lax.dynamic_slice_in_dim(packed[:cut], f * width_own, width_own, axis=1)
    rows = rows.reshape(depth, 6, width_own)
    qv_count = qv_full.size // width
    qv_full = packed[cut : cut + qv_count].reshape(depth, 2, tp, GROUP * heads, head_dim)
    qv_full = lax.dynamic_index_in_dim(qv_full, t, 2, keepdims=False)
    grad_qv_bias = lax.dynamic_slice_in_dim(
        qv_full, f * (head_dim // fsdp), head_dim // fsdp, axis=3
    )
    c1_full = packed[cut + qv_count :].reshape(depth, tp, GROUP * hidden)
    c1_full = lax.dynamic_slice_in_dim(c1_full, t, 1, axis=1)
    c1_own = GROUP * hidden // fsdp
    grad_fc1_bias = lax.dynamic_slice_in_dim(c1_full, f * c1_own, c1_own, axis=2)

    def weight(l, kind, first, count):
        return owned[l][kind][:, :, first : first + count]

    grad_qkv = []
    grad_out = []
    grad_fc1 = []
    grad_fc2 = []
    for l in range(depth):
        piece = weight(l, 1, 0, 3 * feats).reshape(GROUP, width_own, 3, feats)
        grad_qkv.append(piece.transpose(2, 1, 0, 3).reshape(3, width_own, GROUP * feats))
        piece = weight(l, 1, 3 * feats, feats)
        grad_out.append(piece.transpose(0, 2, 1).reshape(GROUP * feats, width_own))
        piece = weight(l, 0, 0, hidden)
        grad_fc1.append(piece.transpose(1, 0, 2).reshape(width_own, GROUP * hidden))
        piece = weight(l, 0, hidden, hidden)
        grad_fc2.append(piece.transpose(0, 2, 1).reshape(GROUP * hidden, width_own))
    return (
        outputs,
        grad_inputs,
        rows[:, :2],
        rows[:, 2:],
        grad_qv_bias,
        grad_fc1_bias,
        jnp.stack(grad_qkv),
        jnp.stack(grad_out),
        jnp.stack(grad_fc1),
        jnp.stack(grad_fc2),
    )


def solution(mesh):
    rows = P("fsdp", "ctx", None)
    params = (
        P(None, None, "fsdp"),
        P(None, None, "fsdp"),
        P(None, None, "tp", "fsdp"),
        P(None, "tp", "fsdp"),
        P(None, None, "fsdp", "tp"),
        P(None, "tp", "fsdp"),
        P(None, "fsdp", "tp"),
        P(None, "tp", "fsdp"),
    )
    return jax.shard_map(
        per_device,
        mesh=mesh,
        in_specs=(rows, P("fsdp", None), rows) + params,
        out_specs=(rows, rows) + params,
        check_vma=False,
    )
```

```python
import functools
import math

import jax
import jax.numpy as jnp
from jax import lax
from jax.experimental import pallas as pl
from jax.experimental.pallas import tpu as pltpu
from jax.sharding import PartitionSpec as P

NORM_EPSILON = 1e-06
MASK_FILL = -1e30
ROOT_HALF = 0.7071067811865476
INV_ROOT_TAU = 0.3989422804014327
GROUP = 4
ORDER = (0, 1, 4, 5, 2, 3, 6, 7)
CHIPS = 4

bf16 = jnp.bfloat16
f32 = jnp.float32
VMEM = pl.BlockSpec(memory_space=pltpu.VMEM)
ANY = pl.BlockSpec(memory_space=pl.ANY)


def dot(a, b):
    return lax.dot_general(a, b, (((1,), (0,)), ((), ())), preferred_element_type=f32)


def dot_nt(a, b):
    return lax.dot_general(a, b, (((1,), (1,)), ((), ())), preferred_element_type=f32)


def dot_tn(a, b):
    return lax.dot_general(a, b, (((0,), (0,)), ((), ())), preferred_element_type=f32)


def kernel_call(body, outs, *args, name, flops=0, limit=16, scratch=(), specs=None):
    moved = sum(a.size * a.dtype.itemsize for a in args)
    moved += sum(math.prod(s) * jnp.dtype(d).itemsize for s, d in outs)
    return pl.pallas_call(
        body,
        out_shape=[jax.ShapeDtypeStruct(s, d) for s, d in outs],
        in_specs=[VMEM] * len(args) if specs is None else specs,
        out_specs=[VMEM] * len(outs),
        scratch_shapes=list(scratch),
        compiler_params=pltpu.CompilerParams(vmem_limit_bytes=limit << 20),
        cost_estimate=pl.CostEstimate(flops=flops, bytes_accessed=moved, transcendentals=0),
        name=name,
    )(*args)


def row_mean(value):
    return jnp.mean(value, axis=-1, keepdims=True)


def normalize(values):
    center = values - row_mean(values)
    inverse = lax.rsqrt(row_mean(center * center) + NORM_EPSILON)
    return center * inverse, inverse


def lanes_of(head, head_dim, width):
    lane = lax.broadcasted_iota(jnp.int32, (1, width), 1)
    return (lane >= head * head_dim) & (lane < (head + 1) * head_dim)


def assemble(chunks, target):
    rows = chunks[0].shape[0]
    for k, chunk in enumerate(chunks):
        target[k * rows : (k + 1) * rows, :] = chunk[...]


def pack_kernel(layer, feats, hidden, qkv_hbm, out_hbm, fc1_hbm, fc2_hbm, attn_ref, mlp_ref,
                qkv, out, fc1, fc2, sems):
    ci = lax.rem(lax.axis_index("ctx"), GROUP)
    head_cols = pl.ds(pl.multiple_of(ci * feats, feats), feats)
    hidden_cols = pl.ds(pl.multiple_of(ci * hidden, hidden), hidden)
    copies = [
        pltpu.make_async_copy(qkv_hbm.at[layer, :, :, head_cols], qkv, sems.at[0]),
        pltpu.make_async_copy(out_hbm.at[layer, head_cols, :], out, sems.at[1]),
        pltpu.make_async_copy(fc1_hbm.at[layer, :, hidden_cols], fc1, sems.at[2]),
        pltpu.make_async_copy(fc2_hbm.at[layer, hidden_cols, :], fc2, sems.at[3]),
    ]
    for copy in copies:
        copy.start()
    copies[0].wait()
    for k in range(3):
        attn_ref[:, k * feats : (k + 1) * feats] = qkv[k]
    copies[1].wait()
    attn_ref[:, 3 * feats :] = out[...].T
    copies[2].wait()
    mlp_ref[:, :hidden] = fc1[...]
    copies[3].wait()
    mlp_ref[:, hidden:] = fc2[...].T


def prep_kernel(tp, outer, rows, lengths, inputs, cotangent, vecs,
                stream_ref, first_ref, upstream_ref, upstream_b_ref, usable_ref, mask_ref):
    c = lax.axis_index("ctx")
    t = lax.axis_index("tp")
    place = lax.rem(c, GROUP) * tp + t
    start = pl.multiple_of(t * rows, rows)
    stream = inputs[0, pl.ds(start, rows), :]
    stream_ref[...] = stream
    normed, _ = normalize(stream)
    first_ref[...] = (normed * vecs[0:1, :] + vecs[4:5, :]).astype(bf16)
    row = lax.broadcasted_iota(jnp.int32, (rows, 128), 0)
    mask = jnp.where(row + start < lengths[0, c], 1.0, 0.0)
    mask_ref[...] = mask
    upstream = cotangent[0, pl.ds(start, rows), :] * mask[:, 0:1]
    upstream_ref[...] = upstream
    upstream_b_ref[...] = upstream.astype(bf16)
    lane = lax.broadcasted_iota(jnp.int32, usable_ref.shape, 1)
    limit = jnp.zeros(usable_ref.shape, jnp.int32)
    for o in range(outer):
        for k, d in enumerate(ORDER):
            source = place ^ d
            first_lane = (o * len(ORDER) + k) * rows
            count = lengths[0, o * GROUP + lax.div(source, tp)] - lax.rem(source, tp) * rows
            limit = jnp.where(lane >= first_lane, first_lane + count, limit)
            limit = jnp.where(lane >= first_lane + rows, 0, limit)
    usable_ref[...] = jnp.where(lane < limit, 1.0, 0.0)


def qkv_kernel(feats, c0, c1, c2, c3, w, bias, qkv_ref, x):
    assemble((c0, c1, c2, c3), x)
    qkv = dot(x[...], w[:, : 3 * feats])
    qkv_ref[:, :feats] = (qkv[:, :feats] + bias[0:1, :]).astype(bf16)
    qkv_ref[:, feats : 2 * feats] = qkv[:, feats : 2 * feats].astype(bf16)
    qkv_ref[:, 2 * feats :] = (qkv[:, 2 * feats :] + bias[1:2, :]).astype(bf16)


def load_keys(parts, feats, keys, values):
    first = 0
    for part in parts:
        rows, width = part.shape
        keys[first : first + rows, :] = part[:, width - 2 * feats : width - feats]
        values[first : first + rows, :] = part[:, width - feats :]
        first += rows


def attn_kernel(feats, heads, part_count, tile, *refs):
    q_ref, *rest = refs
    parts = rest[:part_count]
    w, usable, attended_ref, norm_ref, partial_ref, keys, values = rest[part_count:]
    head_dim = feats // heads
    scale = 1.0 / math.sqrt(head_dim)
    load_keys(parts, feats, keys, values)
    keep = usable[...] > 0.5
    rows = q_ref.shape[0]
    for first in range(0, rows, tile):
        span = slice(first, first + tile)
        q = q_ref[span, :feats]
        attended = None
        for h in range(heads):
            own = lanes_of(h, head_dim, feats)
            scores = dot_nt(jnp.where(own, q, jnp.zeros_like(q)), keys[...]) * scale
            scores = jnp.where(keep, scores, MASK_FILL)
            highest = jnp.max(scores, axis=-1, keepdims=True)
            raised = jnp.exp(scores - highest)
            total = jnp.sum(raised, axis=-1, keepdims=True)
            soft = (raised * (1.0 / total)).astype(bf16)
            result = dot(soft, values[...])
            log_norm = jnp.broadcast_to(highest + jnp.log(total), (tile, feats))
            if attended is None:
                attended, norms = result, log_norm
            else:
                attended = jnp.where(own, result, attended)
                norms = jnp.where(own, log_norm, norms)
        attended_ref[span, :] = attended.astype(bf16)
        norm_ref[span, :] = norms
    partial_ref[...] = dot_nt(attended_ref[...], w[:, 3 * feats :]).astype(bf16)


def core_sum_kernel(near, far, own_ref, y_ref, x_ref, xy_ref):
    rows = own_ref.shape[0]
    for k, ref in enumerate((own_ref, y_ref, x_ref, xy_ref)):
        span = slice(k * rows, (k + 1) * rows)
        ref[...] = (near[span, :].astype(f32) + far[span, :].astype(f32)).astype(ref.dtype)


def total_of(own, y, x, xy):
    return own[...] + y[...].astype(f32) + x[...].astype(f32) + xy[...].astype(f32)


def sum_norm_kernel(bias_row, gain_row, shift_row, own, y, x, xy, residual, vecs,
                    stream_ref, normed_ref):
    stream = residual[...] + total_of(own, y, x, xy) + vecs[bias_row : bias_row + 1, :]
    stream_ref[...] = stream
    normed, _ = normalize(stream)
    gain = vecs[gain_row : gain_row + 1, :]
    normed_ref[...] = (normed * gain + vecs[shift_row : shift_row + 1, :]).astype(bf16)


def sum_out_kernel(bias_row, own, y, x, xy, residual, vecs, mask, out_ref):
    stream = residual[...] + total_of(own, y, x, xy) + vecs[bias_row : bias_row + 1, :]
    out_ref[...] = stream * mask[:, 0:1]


def mlp_kernel(hidden, c0, c1, c2, c3, w, bias, partial_ref, act_ref, slope_ref, x):
    assemble((c0, c1, c2, c3), x)
    pre = dot(x[...], w[:, :hidden]) + bias[...]
    cdf = 0.5 * (1.0 + lax.erf(pre * ROOT_HALF))
    density = jnp.exp(-0.5 * pre * pre) * INV_ROOT_TAU
    slope_ref[...] = cdf + pre * density
    act_ref[...] = (pre * cdf).astype(bf16)
    partial_ref[...] = dot_nt(act_ref[...], w[:, hidden:]).astype(bf16)


def mlp_back_kernel(hidden, c0, c1, c2, c3, w, slope, partial_ref, grad_ref, sum_ref, x):
    assemble((c0, c1, c2, c3), x)
    grad = dot(x[...], w[:, hidden:]) * slope[...]
    grad_ref[...] = grad.astype(bf16)
    sum_ref[...] = jnp.sum(grad, axis=0, keepdims=True)
    partial_ref[...] = dot_nt(grad_ref[...], w[:, :hidden]).astype(bf16)


def grad_kernel(width, *refs):
    left_one, left_two = refs[0:8], refs[8:16]
    one_near, one_far, two_near, two_far, out_ref, x, z = refs[16:]
    rows = one_near.shape[0]
    assemble(left_one, x)
    z[:rows, :width] = one_near[...]
    z[rows:, :width] = one_far[...]
    out_ref[:, :width] = dot_tn(x[...], z[:, :width]).astype(bf16)
    assemble(left_two, x)
    rest = out_ref.shape[1] - width
    z[:rows, :rest] = two_near[...]
    z[rows:, :rest] = two_far[...]
    out_ref[:, width:] = dot_tn(x[...], z[:, :rest]).astype(bf16)


def norm_back(upstream, values, gain):
    normed, inverse = normalize(values)
    scaled = upstream * gain
    back = inverse * (scaled - row_mean(scaled) - normed * row_mean(scaled * normed))
    gain_grad = jnp.sum(upstream * normed, axis=0, keepdims=True)
    return back, gain_grad, jnp.sum(upstream, axis=0, keepdims=True)


def norm_back_two_kernel(gain_row, own, y, x, xy, values, upstream, vecs,
                         grad_ref, grad_b_ref, sums_ref):
    up = upstream[...]
    back, gain_grad, shift_grad = norm_back(
        total_of(own, y, x, xy), values[...], vecs[gain_row : gain_row + 1, :]
    )
    grad = up + back
    grad_ref[...] = grad
    grad_b_ref[...] = grad.astype(bf16)
    sums_ref[0:1, :] = gain_grad
    sums_ref[1:2, :] = shift_grad
    sums_ref[2:3, :] = jnp.sum(grad, axis=0, keepdims=True)
    sums_ref[3:4, :] = jnp.sum(up, axis=0, keepdims=True)


def norm_back_one_kernel(gain_row, own, y, x, xy, values, upstream, vecs, mask,
                         grad_ref, grad_b_ref, sums_ref):
    back, gain_grad, shift_grad = norm_back(
        total_of(own, y, x, xy), values[...], vecs[gain_row : gain_row + 1, :]
    )
    grad = upstream[...] + back
    if mask is not None:
        grad = grad * mask[:, 0:1]
    grad_ref[...] = grad
    if grad_b_ref is not None:
        grad_b_ref[...] = grad.astype(bf16)
    sums_ref[0:1, :] = gain_grad
    sums_ref[1:2, :] = shift_grad


def attn_back_kernel(feats, heads, part_count, tile, carried, *refs):
    c0, c1, c2, c3, w, q_ref, attended, norms, usable, *rest = refs
    parts = rest[:part_count]
    rest = rest[part_count:]
    if carried:
        keys_before, values_before, *rest = rest
    grad_q, grad_k, grad_v, x, keys, values, grad_att = rest
    head_dim = feats // heads
    scale = 1.0 / math.sqrt(head_dim)
    assemble((c0, c1, c2, c3), x)
    load_keys(parts, feats, keys, values)
    grad_att[...] = dot(x[...], w[:, 3 * feats :]).astype(bf16)
    keep = usable[...] > 0.5
    rows = q_ref.shape[0]
    if carried:
        sum_k, sum_v = keys_before[...], values_before[...]
    else:
        sum_k = jnp.zeros(grad_k.shape, f32)
        sum_v = jnp.zeros(grad_v.shape, f32)
    for first in range(0, rows, tile):
        span = slice(first, first + tile)
        q = q_ref[span, :feats]
        ga = grad_att[span, :]
        products = ga.astype(f32) * attended[span, :].astype(f32)
        gq = None
        for h in range(heads):
            own = lanes_of(h, head_dim, feats)
            own_f = jnp.where(own, 1.0, 0.0)
            q_h = jnp.where(own, q, jnp.zeros_like(q))
            ga_h = jnp.where(own, ga, jnp.zeros_like(ga))
            row_dots = jnp.sum(products * own_f, axis=-1, keepdims=True)
            scores = dot_nt(q_h, keys[...]) * scale
            scores = jnp.where(keep, scores, MASK_FILL)
            soft = jnp.exp(scores - norms[span, h * head_dim : h * head_dim + 1])
            grad_soft = dot_nt(ga_h, values[...])
            grad_scores = (soft * (grad_soft - row_dots)).astype(bf16)
            part = dot(grad_scores, keys[...])
            gq = part if gq is None else jnp.where(own, part, gq)
            sum_k = sum_k + dot_tn(grad_scores, q_h) * scale
            sum_v = sum_v + dot_tn(soft.astype(bf16), ga_h)
        grad_q[span, :] = gq * scale
    grad_k[...] = sum_k
    grad_v[...] = sum_v


def project_kernel(feats, first, gq, gk, gv, w, packed_ref, partial_ref, sums_ref):
    rows = gq.shape[0]
    span = slice(first, first + rows)
    packed_ref[:, :feats] = gq[...].astype(bf16)
    packed_ref[:, feats : 2 * feats] = gk[span, :].astype(bf16)
    packed_ref[:, 2 * feats :] = gv[span, :].astype(bf16)
    sums_ref[0:1, :] = jnp.sum(gq[...], axis=0, keepdims=True)
    sums_ref[1:2, :] = jnp.sum(gv[span, :], axis=0, keepdims=True)
    partial_ref[...] = dot_nt(packed_ref[...], w[:, : 3 * feats]).astype(bf16)


def place_mlp_kernel(layer, hidden, p0, p1, p2, p3, *refs):
    fc1_hbm, fc2_hbm, fc1, fc2, sems = refs[-5:]
    ci = lax.rem(lax.axis_index("ctx"), GROUP)
    copies = []
    for k, piece in enumerate((p0, p1, p2, p3)):
        span = pl.ds(pl.multiple_of((ci ^ k) * hidden, hidden), hidden)
        fc1[k] = piece[:, :hidden].astype(f32)
        copies.append(
            pltpu.make_async_copy(fc1.at[k], fc1_hbm.at[layer, :, span], sems.at[2 * k])
        )
        copies[-1].start()
        fc2[k] = piece[:, hidden:].astype(f32).T
        copies.append(
            pltpu.make_async_copy(fc2.at[k], fc2_hbm.at[layer, span, :], sems.at[2 * k + 1])
        )
        copies[-1].start()
    for copy in copies:
        copy.wait()


def place_attn_kernel(layer, feats, p0, p1, p2, p3, *refs):
    qkv_hbm, out_hbm, qkv, out, sems = refs[-5:]
    ci = lax.rem(lax.axis_index("ctx"), GROUP)
    copies = []
    for k, piece in enumerate((p0, p1, p2, p3)):
        span = pl.ds(pl.multiple_of((ci ^ k) * feats, feats), feats)
        for j in range(3):
            qkv[k, j] = piece[:, j * feats : (j + 1) * feats].astype(f32)
        copies.append(
            pltpu.make_async_copy(qkv.at[k], qkv_hbm.at[layer, :, :, span], sems.at[2 * k])
        )
        copies[-1].start()
        out[k] = piece[:, 3 * feats :].astype(f32).T
        copies.append(
            pltpu.make_async_copy(out.at[k], out_hbm.at[layer, span, :], sems.at[2 * k + 1])
        )
        copies[-1].start()
    for copy in copies:
        copy.wait()


def place_call(body, pieces, before, outs, scratch, name):
    aliases = {} if before is None else {4: 0, 5: 1}
    extra = () if before is None else tuple(before)
    return pl.pallas_call(
        body,
        out_shape=[jax.ShapeDtypeStruct(s, f32) for s in outs],
        in_specs=[VMEM] * 4 + [ANY] * len(extra),
        out_specs=[ANY] * 2,
        scratch_shapes=[pltpu.VMEM(s, f32) for s in scratch] + [pltpu.SemaphoreType.DMA((8,))],
        input_output_aliases=aliases,
        compiler_params=pltpu.CompilerParams(vmem_limit_bytes=16 << 20),
        cost_estimate=pl.CostEstimate(
            flops=0, bytes_accessed=12 * pieces[0].size * 4, transcendentals=0
        ),
        name=name,
    )(*pieces, *extra)


def per_device(
    inputs, lengths, cotangent, norm_gains, shifts, qv_bias, fc1_bias, w_qkv, w_out, w_fc1, w_fc2
):
    depth = w_qkv.shape[0]
    width_own = w_qkv.shape[2]
    fsdp = lax.axis_size("fsdp")
    tp = lax.axis_size("tp")
    ctx = lax.axis_size("ctx")
    outer = ctx // GROUP
    rows = inputs.shape[1] // tp
    half = rows * CHIPS
    all_rows = 2 * half
    head_own = qv_bias.shape[3]
    head_dim = head_own * fsdp
    heads = qv_bias.shape[2] // GROUP
    feats = heads * head_dim
    hidden = w_fc1.shape[2] // GROUP
    width = width_own * fsdp
    t = lax.axis_index("tp")
    f = lax.axis_index("fsdp")
    ci = lax.axis_index("ctx") % GROUP
    tile = half // 2

    def swap_core(value):
        return lax.ppermute(value, "ctx", [(i, i ^ 1) for i in range(ctx)])

    def swap_x(value):
        return lax.ppermute(value, "ctx", [(i, i ^ 2) for i in range(ctx)])

    def swap_y(value):
        return lax.ppermute(value, "tp", [(i, i ^ 1) for i in range(tp)])

    def swap_xy(value):
        pairs = [
            (i * tp + k, (i ^ 2) * tp + (k ^ 1)) for i in range(ctx) for k in range(tp)
        ]
        return lax.ppermute(value, ("ctx", "tp"), pairs)

    outer_groups = [[o * GROUP + i for o in range(outer)] for i in range(GROUP)]

    def gather_rows(own):
        near = (own, swap_y(own), swap_x(own), swap_xy(own))
        return near, tuple(swap_core(chunk) for chunk in near)

    def reduce_rows(near, far):
        own, y, x, xy = kernel_call(
            core_sum_kernel,
            [((rows, width), f32)] + [((rows, width), bf16)] * 3,
            near,
            swap_core(far),
            name="core_sum",
        )
        return own, swap_y(y), swap_x(x), swap_xy(xy)

    attn_w = []
    mlp_w = []
    for l in range(depth):
        attn_own, mlp_own = kernel_call(
            functools.partial(pack_kernel, l, feats, hidden),
            [((width_own, 4 * feats), bf16), ((width_own, 2 * hidden), bf16)],
            w_qkv,
            w_out,
            w_fc1,
            w_fc2,
            name="pack",
            specs=[ANY] * 4,
            scratch=[
                pltpu.VMEM((3, width_own, feats), bf16),
                pltpu.VMEM((feats, width_own), bf16),
                pltpu.VMEM((width_own, hidden), bf16),
                pltpu.VMEM((hidden, width_own), bf16),
                pltpu.SemaphoreType.DMA((4,)),
            ],
        )
        attn_w.append(lax.all_gather(attn_own, "fsdp", axis=0, tiled=True))
        mlp_w.append(lax.all_gather(mlp_own, "fsdp", axis=0, tiled=True))

    qv_own = lax.dynamic_slice_in_dim(qv_bias, ci * heads, heads, axis=2)
    vec_rows = depth * 6
    c1_rows = depth * fc1_bias.shape[2] // width_own
    qv_own = qv_own.reshape(1, -1)
    small_own = jnp.concatenate(
        [
            norm_gains.reshape(-1, width_own),
            shifts.reshape(-1, width_own),
            fc1_bias.reshape(-1, width_own),
            jnp.pad(qv_own, ((0, 0), (0, width_own - qv_own.shape[1]))),
        ],
        axis=0,
    )
    shifted = [small_own] + [
        lax.ppermute(small_own, "fsdp", [(i, (i + d) % fsdp) for i in range(fsdp)])
        for d in range(1, fsdp)
    ]

    def shard(a):
        picked = shifted[0]
        for d in range(1, fsdp):
            picked = jnp.where((f - d) % fsdp == a, shifted[d], picked)
        return picked.astype(f32)

    shards = [shard(a) for a in range(fsdp)]
    vecs = jnp.concatenate([s[:vec_rows] for s in shards], axis=1)
    fc1_all = shard(ci)[vec_rows : vec_rows + c1_rows].reshape(depth, 1, hidden)
    qv_all = jnp.stack(
        [s[vec_rows + c1_rows, : qv_own.shape[1]].reshape(depth, 2, heads, head_own) for s in shards],
        axis=3,
    ).reshape(depth, 2, feats)

    def gain_row(l, i):
        return 2 * l + i

    def shift_row(l, i):
        return 2 * depth + 4 * l + i

    key_rows = outer * all_rows
    stream, first, upstream, upstream_b, usable, mask = kernel_call(
        functools.partial(prep_kernel, tp, outer, rows),
        [
            ((rows, width), f32),
            ((rows, width), bf16),
            ((rows, width), f32),
            ((rows, width), bf16),
            ((1, key_rows), f32),
            ((rows, 128), f32),
        ],
        lengths,
        inputs,
        cotangent,
        vecs,
        name="prep",
        specs=[pl.BlockSpec(memory_space=pltpu.SMEM), VMEM, VMEM, VMEM],
    )
    first_chunks = gather_rows(first)
    upstream_chunks = gather_rows(upstream_b)

    chunk_scratch = pltpu.VMEM((half, width), bf16)
    key_scratch = pltpu.VMEM((key_rows, feats), bf16)
    partial_out = ((half, width), bf16)
    saved_all = []
    for l in range(depth):
        qkv = [
            kernel_call(
                functools.partial(qkv_kernel, feats),
                [((half, 3 * feats), bf16)],
                *chunks,
                attn_w[l],
                qv_all[l],
                name="qkv",
                flops=2 * half * width * 3 * feats,
                scratch=[chunk_scratch],
            )[0]
            for chunks in first_chunks
        ]
        if outer > 1:
            pairs = jnp.concatenate([part[:, feats:] for part in qkv], axis=0)
            pairs = lax.all_gather(
                pairs, "ctx", axis=0, tiled=True, axis_index_groups=outer_groups
            )
            key_parts = (pairs,)
        else:
            key_parts = tuple(qkv)
        attn = [
            kernel_call(
                functools.partial(attn_kernel, feats, heads, len(key_parts), tile),
                [((half, feats), bf16), ((half, feats), f32), partial_out],
                qkv[side],
                *key_parts,
                attn_w[l],
                usable,
                name="attn",
                flops=2 * half * (width * feats + 4 * heads * key_rows * feats),
                scratch=[key_scratch, key_scratch],
            )
            for side in (1, 0)
        ][::-1]
        sums = reduce_rows(attn[0][2], attn[1][2])
        middle, second = kernel_call(
            functools.partial(sum_norm_kernel, shift_row(l, 2), gain_row(l, 1), shift_row(l, 1)),
            [((rows, width), f32), ((rows, width), bf16)],
            *sums,
            stream,
            vecs,
            name="sum_norm",
        )
        second_chunks = gather_rows(second)
        mlp = [
            kernel_call(
                functools.partial(mlp_kernel, hidden),
                [partial_out, ((half, hidden), bf16), ((half, hidden), f32)],
                *second_chunks[side],
                mlp_w[l],
                fc1_all[l],
                name="mlp",
                flops=4 * half * width * hidden,
                scratch=[chunk_scratch],
            )
            for side in (1, 0)
        ][::-1]
        sums = reduce_rows(mlp[0][0], mlp[1][0])
        saved_all.append(
            (stream, first_chunks, qkv, key_parts, attn, middle, second_chunks, mlp)
        )
        if l + 1 < depth:
            stream, first = kernel_call(
                functools.partial(
                    sum_norm_kernel, shift_row(l, 3), gain_row(l + 1, 0), shift_row(l + 1, 0)
                ),
                [((rows, width), f32), ((rows, width), bf16)],
                *sums,
                middle,
                vecs,
                name="sum_norm",
            )
            first_chunks = gather_rows(first)
        else:
            outputs_own = kernel_call(
                functools.partial(sum_out_kernel, shift_row(l, 3)),
                [((rows, width), f32)],
                *sums,
                middle,
                vecs,
                mask,
                name="sum_out",
            )[0]

    def both_halves(own):
        other = swap_y(own)
        return jnp.where(
            t == 0,
            jnp.concatenate([own, other], axis=0),
            jnp.concatenate([other, own], axis=0),
        )[None]

    outputs = both_halves(outputs_own)

    def reduce_grads(grad):
        part = lax.psum_scatter(grad, "fsdp", scatter_dimension=0, tiled=True)
        if outer > 1:
            part = lax.psum(part, "ctx", axis_index_groups=outer_groups)
        other = swap_x(part)
        return part, swap_core(part), other, swap_core(other)

    row_sums = [None] * depth
    unit_sums = [None] * depth
    head_sums = [None] * depth
    placed_mlp = None
    placed_attn = None
    for l in reversed(range(depth)):
        stream, first_chunks, qkv, key_parts, attn, middle, second_chunks, mlp = saved_all[l]
        back = [
            kernel_call(
                functools.partial(mlp_back_kernel, hidden),
                [partial_out, ((half, hidden), bf16), ((1, hidden), f32)],
                *upstream_chunks[side],
                mlp_w[l],
                mlp[side][2],
                name="mlp_back",
                flops=4 * half * width * hidden,
                scratch=[chunk_scratch],
            )
            for side in (1, 0)
        ][::-1]
        sums = reduce_rows(back[0][0], back[1][0])
        mlp_grad = kernel_call(
            functools.partial(grad_kernel, hidden),
            [((width, 2 * hidden), bf16)],
            *second_chunks[0],
            *second_chunks[1],
            *upstream_chunks[0],
            *upstream_chunks[1],
            back[0][1],
            back[1][1],
            mlp[0][1],
            mlp[1][1],
            name="mlp_grad",
            flops=4 * all_rows * width * hidden,
            scratch=[pltpu.VMEM((all_rows, width), bf16), pltpu.VMEM((all_rows, hidden), bf16)],
        )[0]
        pieces = reduce_grads(mlp_grad)
        placed_mlp = place_call(
            functools.partial(place_mlp_kernel, l, hidden),
            pieces,
            placed_mlp,
            [w_fc1.shape, w_fc2.shape],
            [(GROUP, width_own, hidden), (GROUP, hidden, width_own)],
            "place_mlp",
        )
        unit_sums[l] = back[0][2] + back[1][2]
        grad_middle, middle_b, sums_two = kernel_call(
            functools.partial(norm_back_two_kernel, gain_row(l, 1)),
            [((rows, width), f32), ((rows, width), bf16), ((4, width), f32)],
            *sums,
            middle,
            upstream,
            vecs,
            name="norm_back_two",
        )
        middle_chunks = gather_rows(middle_b)
        grad_q = [None, None]
        carried = ()
        for side in (0, 1):
            grad_q[side], *carried = kernel_call(
                functools.partial(
                    attn_back_kernel, feats, heads, len(key_parts), tile, len(carried) > 0
                ),
                [((half, feats), f32), ((key_rows, feats), f32), ((key_rows, feats), f32)],
                *middle_chunks[side],
                attn_w[l],
                qkv[side],
                attn[side][0],
                attn[side][1],
                usable,
                *key_parts,
                *carried,
                name="attn_back",
                flops=2 * half * (width * feats + 10 * heads * key_rows * feats),
                scratch=[chunk_scratch, key_scratch, key_scratch, pltpu.VMEM((half, feats), bf16)],
                limit=32,
            )
        grad_k, grad_v = carried
        if outer > 1:
            grad_k, grad_v = (
                lax.psum_scatter(
                    v, "ctx", scatter_dimension=0, tiled=True, axis_index_groups=outer_groups
                )
                for v in (grad_k, grad_v)
            )
        project = [
            kernel_call(
                functools.partial(project_kernel, feats, side * half),
                [((half, 3 * feats), bf16), partial_out, ((2, feats), f32)],
                grad_q[side],
                grad_k,
                grad_v,
                attn_w[l],
                name="project",
                flops=2 * half * width * 3 * feats,
            )
            for side in (1, 0)
        ][::-1]
        sums = reduce_rows(project[0][1], project[1][1])
        attn_grad = kernel_call(
            functools.partial(grad_kernel, 3 * feats),
            [((width, 4 * feats), bf16)],
            *first_chunks[0],
            *first_chunks[1],
            *middle_chunks[0],
            *middle_chunks[1],
            project[0][0],
            project[1][0],
            attn[0][0],
            attn[1][0],
            name="attn_grad",
            flops=2 * all_rows * width * 4 * feats,
            scratch=[
                pltpu.VMEM((all_rows, width), bf16),
                pltpu.VMEM((all_rows, 3 * feats), bf16),
            ],
        )[0]
        pieces = reduce_grads(attn_grad)
        placed_attn = place_call(
            functools.partial(place_attn_kernel, l, feats),
            pieces,
            placed_attn,
            [w_qkv.shape, w_out.shape],
            [(GROUP, 3, width_own, feats), (GROUP, feats, width_own)],
            "place_attn",
        )
        head_sums[l] = project[0][2] + project[1][2]
        back_outs = [((rows, width), f32), ((rows, width), bf16), ((2, width), f32)]
        if l > 0:
            upstream, upstream_b, sums_one = kernel_call(
                lambda *refs, row=gain_row(l, 0): norm_back_one_kernel(
                    row, *refs[:7], None, *refs[7:]
                ),
                back_outs,
                *sums,
                stream,
                grad_middle,
                vecs,
                name="norm_back_one",
            )[:3]
            upstream_chunks = gather_rows(upstream_b)
        else:
            grad_inputs_own, sums_one = kernel_call(
                lambda *refs, row=gain_row(l, 0): norm_back_one_kernel(
                    row, *refs[:8], refs[8], None, refs[9]
                ),
                [back_outs[0], back_outs[2]],
                *sums,
                stream,
                grad_middle,
                vecs,
                mask,
                name="norm_back_one",
            )
        row_sums[l] = (sums_one, sums_two)

    grad_inputs = both_halves(grad_inputs_own)

    vec_part = jnp.concatenate(
        [
            piece
            for l in range(depth)
            for piece in (
                row_sums[l][0][0:1],
                row_sums[l][1][0:1],
                row_sums[l][0][1:2],
                row_sums[l][1][1:4],
            )
        ],
        axis=0,
    )
    unit_part = jnp.concatenate(unit_sums, axis=0)
    head_part = jnp.concatenate(head_sums, axis=0)
    unit_lines = unit_part.reshape(-1, width)
    head_lines = head_part.reshape(1, -1)
    head_lines = jnp.pad(head_lines, ((0, 0), (0, width - head_lines.shape[1])))
    packed = jnp.concatenate([vec_part, unit_lines, head_lines], axis=0)
    if outer > 1:
        packed = lax.psum(packed, "ctx", axis_index_groups=outer_groups)
    step = 1
    while step < fsdp:
        packed = packed + lax.ppermute(packed, "fsdp", [(i, i ^ step) for i in range(fsdp)])
        step *= 2
    vec_sum = lax.dynamic_slice_in_dim(packed[:vec_rows], f * width_own, width_own, axis=1)
    rest = packed[vec_rows:]
    vec_sum = vec_sum + swap_y(vec_sum)
    rest_core = swap_core(rest)
    vec_sum = vec_sum + swap_core(vec_sum)
    rest_two = jnp.stack([rest, rest_core])
    vec_sum = vec_sum + swap_x(vec_sum)
    rest_four = jnp.concatenate([rest_two, swap_x(rest_two)], axis=0)
    vec_sum = vec_sum.reshape(depth, 6, width_own)
    unit_count = unit_lines.shape[0]

    def of_place(c):
        return lax.dynamic_index_in_dim(rest_four, ci ^ c, 0, keepdims=False)

    grad_fc1_bias = of_place(f)[:unit_count].reshape(depth, 1, hidden)
    grad_qv_bias = jnp.stack(
        [
            lax.dynamic_slice_in_dim(
                of_place(c)[unit_count, : head_part.size].reshape(depth, 2, heads, head_dim),
                f * head_own,
                head_own,
                axis=3,
            )
            for c in range(GROUP)
        ],
        axis=2,
    ).reshape(qv_bias.shape)
    return (
        outputs,
        grad_inputs,
        vec_sum[:, :2],
        vec_sum[:, 2:],
        grad_qv_bias,
        grad_fc1_bias,
        placed_attn[0],
        placed_attn[1],
        placed_mlp[0],
        placed_mlp[1],
    )


def solution(mesh):
    rows = P("fsdp", "ctx", None)
    params = (
        P(None, None, "fsdp"),
        P(None, None, "fsdp"),
        P(None, None, "tp", "fsdp"),
        P(None, "tp", "fsdp"),
        P(None, None, "fsdp", "tp"),
        P(None, "tp", "fsdp"),
        P(None, "fsdp", "tp"),
        P(None, "tp", "fsdp"),
    )
    return jax.shard_map(
        per_device,
        mesh=mesh,
        in_specs=(rows, P("fsdp", None), rows) + params,
        out_specs=(rows, rows) + params,
        check_vma=False,
    )
```

```python
import functools
import math

import jax
import jax.numpy as jnp
from jax import lax
from jax.experimental import pallas as pl
from jax.experimental.pallas import tpu as pltpu
from jax.sharding import PartitionSpec as P

NORM_EPSILON = 1e-06
MASK_FILL = -1e30
ROOT_HALF = 0.7071067811865476
INV_ROOT_TAU = 0.3989422804014327
GROUP = 4
ORDER = (0, 1, 4, 5, 2, 3, 6, 7)
CHIPS = 4

bf16 = jnp.bfloat16
f32 = jnp.float32
VMEM = pl.BlockSpec(memory_space=pltpu.VMEM)
SMEM = pl.BlockSpec(memory_space=pltpu.SMEM)
HBM = pl.BlockSpec(memory_space=pltpu.HBM)
DMA = pltpu.SemaphoreType.DMA
TOKEN = ((8, 128), f32)


def dot(a, b):
    return lax.dot_general(a, b, (((1,), (0,)), ((), ())), preferred_element_type=f32)


def dot_nt(a, b):
    return lax.dot_general(a, b, (((1,), (1,)), ((), ())), preferred_element_type=f32)


def dot_tn(a, b):
    return lax.dot_general(a, b, (((0,), (0,)), ((), ())), preferred_element_type=f32)


class Far:
    def __init__(self, value):
        self.value = value


class Scalars:
    def __init__(self, value):
        self.value = value


def saved(shape, dtype):
    return pltpu.HBM(shape, dtype)


def kernel_call(body, outs, *args, name, limit=12, scratch=(), after=(), aliases=None):
    values, specs = [], []
    for arg in (*args, *after):
        if isinstance(arg, Far):
            values.append(pltpu.with_memory_space_constraint(arg.value, pltpu.HBM))
            specs.append(HBM)
        elif isinstance(arg, Scalars):
            values.append(arg.value)
            specs.append(SMEM)
        else:
            values.append(arg)
            specs.append(VMEM)
    first, last = len(args), len(args) + len(after)

    def run(*refs):
        body(*refs[:first], *refs[last:])

    out_shape, out_specs = [], []
    for out in outs:
        if isinstance(out, tuple):
            out_shape.append(jax.ShapeDtypeStruct(*out))
            out_specs.append(VMEM)
        else:
            out_shape.append(out)
            out_specs.append(HBM)
    return pl.pallas_call(
        run,
        out_shape=out_shape,
        in_specs=specs,
        out_specs=out_specs,
        scratch_shapes=list(scratch),
        input_output_aliases=aliases or {},
        compiler_params=pltpu.CompilerParams(vmem_limit_bytes=limit << 20),
        cost_estimate=pl.CostEstimate(flops=0, bytes_accessed=0, transcendentals=0),
        name=name,
    )(*values)


def start_copies(pairs, sems):
    copies = [
        pltpu.make_async_copy(source, target, sems.at[k])
        for k, (source, target) in enumerate(pairs)
    ]
    for copy in copies:
        copy.start()
    return copies


def row_mean(value):
    return jnp.mean(value, axis=-1, keepdims=True)


def normalize(values):
    center = values - row_mean(values)
    inverse = lax.rsqrt(row_mean(center * center) + NORM_EPSILON)
    return center * inverse, inverse


def lanes_of(head, head_dim, width):
    lane = lax.broadcasted_iota(jnp.int32, (1, width), 1)
    return (lane >= head * head_dim) & (lane < (head + 1) * head_dim)


def assemble(chunks, target):
    rows = chunks[0].shape[0]
    for k, chunk in enumerate(chunks):
        target[k * rows : (k + 1) * rows, :] = chunk[...]


def only(flag, value):
    return jnp.where(flag, value, jnp.zeros_like(value))


def shards(weights):
    if len(weights) == 1:
        rows = weights[0].shape[0]
        return [(pl.ds(0, rows), weights[0])]
    count = len(weights)
    rows = weights[0].shape[0]
    f = lax.axis_index("fsdp")
    found = []
    for d, ref in enumerate(weights):
        place = lax.rem(f + (count - d), count)
        found.append((pl.ds(pl.multiple_of(place * rows, rows), rows), ref))
    return found


def pack_attn_kernel(layer, feats, qkv_hbm, out_hbm, packed_ref, qkv, out, sems):
    ci = lax.rem(lax.axis_index("ctx"), GROUP)
    span = pl.ds(pl.multiple_of(ci * feats, feats), feats)
    copies = start_copies(
        [(qkv_hbm.at[layer, :, :, span], qkv), (out_hbm.at[layer, span, :], out)], sems
    )
    copies[0].wait()
    for k in range(3):
        packed_ref[:, k * feats : (k + 1) * feats] = qkv[k]
    copies[1].wait()
    packed_ref[:, 3 * feats :] = out[...].T


def pack_mlp_kernel(layer, hidden, fc1_hbm, fc2_hbm, packed_ref, fc1, fc2, sems):
    ci = lax.rem(lax.axis_index("ctx"), GROUP)
    span = pl.ds(pl.multiple_of(ci * hidden, hidden), hidden)
    copies = start_copies(
        [(fc1_hbm.at[layer, :, span], fc1), (fc2_hbm.at[layer, span, :], fc2)], sems
    )
    copies[0].wait()
    packed_ref[:, :hidden] = fc1[...]
    copies[1].wait()
    packed_ref[:, hidden:] = fc2[...].T


def prep_upstream_kernel(tp, outer, lengths, cotangent_hbm,
                         upstream_ref, upstream_b_ref, usable_ref, mask_ref, rows_in, sems):
    rows = rows_in.shape[0]
    c = lax.axis_index("ctx")
    t = lax.axis_index("tp")
    place = lax.rem(c, GROUP) * tp + t
    start = pl.multiple_of(t * rows, rows)
    copies = start_copies([(cotangent_hbm.at[0, pl.ds(start, rows), :], rows_in)], sems)
    lane = lax.broadcasted_iota(jnp.int32, usable_ref.shape, 1)
    limit = jnp.zeros(usable_ref.shape, jnp.int32)
    for o in range(outer):
        for k, d in enumerate(ORDER):
            source = place ^ d
            first_lane = (o * len(ORDER) + k) * rows
            count = lengths[0, o * GROUP + lax.div(source, tp)] - lax.rem(source, tp) * rows
            limit = jnp.where(lane >= first_lane, first_lane + jnp.clip(count, 0, rows), limit)
    usable_ref[...] = jnp.where(lane < limit, 1.0, 0.0)
    row = lax.broadcasted_iota(jnp.int32, mask_ref.shape, 0)
    mask = jnp.where(row + start < lengths[0, c], 1.0, 0.0)
    mask_ref[...] = mask
    copies[0].wait()
    upstream = rows_in[...] * mask[:, 0:1]
    upstream_ref[...] = upstream
    upstream_b_ref[...] = upstream.astype(bf16)


def prep_first_kernel(depth, inputs_hbm, vecs, stream_ref, first_ref, sems):
    rows = stream_ref.shape[0]
    start = pl.multiple_of(lax.axis_index("tp") * rows, rows)
    copies = start_copies([(inputs_hbm.at[0, pl.ds(start, rows), :], stream_ref)], sems)
    copies[0].wait()
    normed, _ = normalize(stream_ref[...])
    shift = vecs[2 * depth : 2 * depth + 1, :]
    first_ref[...] = (normed * vecs[0:1, :] + shift).astype(bf16)


def keep_rows_kernel(*refs):
    chunks, (near_hbm, far_hbm, token, near, far, sems) = refs[:8], refs[8:]
    assemble(chunks[:4], near)
    assemble(chunks[4:], far)
    for copy in start_copies([(near, near_hbm), (far, far_hbm)], sems):
        copy.wait()
    token[...] = jnp.zeros_like(token)


def qkv_kernel(feats, weight_count, *refs):
    c0, c1, c2, c3, *rest = refs
    weights = rest[:weight_count]
    bias, qkv_ref, x = rest[weight_count:]
    assemble((c0, c1, c2, c3), x)
    qkv = sum(dot(x[:, span], w[:, : 3 * feats]) for span, w in shards(weights))
    qkv_ref[:, :feats] = (qkv[:, :feats] + bias[0:1, :]).astype(bf16)
    qkv_ref[:, feats : 2 * feats] = qkv[:, feats : 2 * feats].astype(bf16)
    qkv_ref[:, 2 * feats :] = (qkv[:, 2 * feats :] + bias[1:2, :]).astype(bf16)


def attn_kernel(feats, heads, weight_count, part_count, keep_count, tile, *refs):
    q_ref, *rest = refs
    parts = rest[:part_count]
    weights = rest[part_count : part_count + weight_count]
    rest = rest[part_count + weight_count :]
    usable, *rest = rest
    kept, rest = rest[:keep_count], rest[keep_count:]
    partial_ref, attended_hbm, norm_hbm, *rest = rest
    kept_hbm, rest = rest[:keep_count], rest[keep_count:]
    keys, values, attended_ref, norm_ref, sems = rest
    head_dim = feats // heads
    scale = 1.0 / math.sqrt(head_dim)
    copies = start_copies(list(zip(kept, kept_hbm)), sems)
    first = 0
    for part in parts:
        rows, width = part.shape
        keys[first : first + rows, :] = part[:, width - 2 * feats : width - feats]
        values[first : first + rows, :] = part[:, width - feats :]
        first += rows
    keep = usable[...] > 0.5
    rows = q_ref.shape[0]
    for first in range(0, rows, tile):
        span = slice(first, first + tile)
        q = q_ref[span, :feats]
        attended = None
        for h in range(heads):
            own = lanes_of(h, head_dim, feats)
            scores = dot_nt(only(own, q), keys[...]) * scale
            scores = jnp.where(keep, scores, MASK_FILL)
            highest = jnp.max(scores, axis=-1, keepdims=True)
            raised = jnp.exp(scores - highest)
            total = jnp.sum(raised, axis=-1, keepdims=True)
            soft = (raised * (1.0 / total)).astype(bf16)
            result = dot(soft, values[...])
            log_norm = jnp.broadcast_to(highest + jnp.log(total), (tile, feats))
            if attended is None:
                attended, norms = result, log_norm
            else:
                attended = jnp.where(own, result, attended)
                norms = jnp.where(own, log_norm, norms)
        attended_ref[span, :] = attended.astype(bf16)
        norm_ref[span, :] = norms
    copies += start_copies(
        [(attended_ref, attended_hbm), (norm_ref, norm_hbm)],
        sems.at[pl.ds(keep_count, 2)],
    )
    for span, w in shards(weights):
        partial_ref[:, span] = dot_nt(attended_ref[...], w[:, 3 * feats :]).astype(bf16)
    for copy in copies:
        copy.wait()


def core_sum_kernel(near, far, own_ref, y_ref, x_ref, xy_ref):
    rows = own_ref.shape[0]
    for k, ref in enumerate((own_ref, y_ref, x_ref, xy_ref)):
        span = slice(k * rows, (k + 1) * rows)
        ref[...] = (near[span, :].astype(f32) + far[span, :].astype(f32)).astype(ref.dtype)


def total_of(own, y, x, xy):
    return own[...] + y[...].astype(f32) + x[...].astype(f32) + xy[...].astype(f32)


def sum_norm_kernel(bias_row, gain_row, shift_row, own, y, x, xy, residual, vecs,
                    stream_ref, normed_ref):
    stream = residual[...] + total_of(own, y, x, xy) + vecs[bias_row : bias_row + 1, :]
    stream_ref[...] = stream
    normed, _ = normalize(stream)
    gain = vecs[gain_row : gain_row + 1, :]
    normed_ref[...] = (normed * gain + vecs[shift_row : shift_row + 1, :]).astype(bf16)


def sum_out_kernel(bias_row, own, y, x, xy, residual, vecs, mask, out_ref):
    stream = residual[...] + total_of(own, y, x, xy) + vecs[bias_row : bias_row + 1, :]
    out_ref[...] = stream * mask[:, 0:1]


def mlp_kernel(hidden, keep_count, c0, c1, c2, c3, w, bias, *refs):
    kept, rest = refs[:keep_count], refs[keep_count:]
    partial_ref, x_hbm, act_hbm, slope_hbm, *rest = rest
    kept_hbm, (x, act_ref, slope_ref, sems) = rest[:keep_count], rest[keep_count:]
    assemble((c0, c1, c2, c3), x)
    copies = start_copies([(x, x_hbm), *zip(kept, kept_hbm)], sems)
    block = hidden // 2
    for k in range(2):
        span = slice(k * block, (k + 1) * block)
        pre = dot(x[...], w[:, span]) + bias[:, span]
        cdf = 0.5 * (1.0 + lax.erf(pre * ROOT_HALF))
        density = jnp.exp(-0.5 * pre * pre) * INV_ROOT_TAU
        slope_ref[k] = cdf + pre * density
        act_ref[:, span] = (pre * cdf).astype(bf16)
        copies += start_copies(
            [(slope_ref.at[k], slope_hbm.at[k])], sems.at[pl.ds(1 + keep_count + k, 1)]
        )
    copies += start_copies([(act_ref, act_hbm)], sems.at[pl.ds(3 + keep_count, 1)])
    partial_ref[...] = dot_nt(act_ref[...], w[:, hidden:]).astype(bf16)
    for copy in copies:
        copy.wait()


def mlp_back_kernel(hidden, chunk_count, *refs):
    chunks, (w, slope_hbm, *rest) = refs[:chunk_count], refs[chunk_count:]
    partial_ref, grad_ref, sum_ref, x, slope, sems = rest
    copies = start_copies([(slope_hbm, slope)], sems)
    if chunk_count == 1:
        copies += start_copies([(chunks[0], x)], sems.at[pl.ds(1, 1)])
        copies[1].wait()
    else:
        assemble(chunks, x)
    grad = dot(x[...], w[:, hidden:])
    copies[0].wait()
    block = hidden // 2
    for k in range(2):
        span = slice(k * block, (k + 1) * block)
        part = grad[:, span] * slope[k]
        grad_ref[:, span] = part.astype(bf16)
        sum_ref[:, span] = jnp.sum(part, axis=0, keepdims=True)
    partial_ref[...] = dot_nt(grad_ref[...], w[:, :hidden]).astype(bf16)


def mlp_grad_kernel(hidden, second_near, second_far, act_near, act_far, up_near, up_far,
                    grad_near, grad_far, out_ref, token, second, act, up, grad, sems):
    rows = up_near.shape[0]
    near, far = pl.ds(0, rows), pl.ds(rows, rows)
    copies = start_copies(
        [
            (second_near, second.at[near]),
            (second_far, second.at[far]),
            (act_near, act.at[near]),
            (act_far, act.at[far]),
        ],
        sems,
    )
    up[:rows, :] = up_near[...]
    up[rows:, :] = up_far[...]
    grad[:rows, :] = grad_near[...]
    grad[rows:, :] = grad_far[...]
    for copy in copies:
        copy.wait()
    out_ref[:, hidden:] = dot_tn(up[...], act[...]).astype(bf16)
    out_ref[:, :hidden] = dot_tn(second[...], grad[...]).astype(bf16)
    token[...] = jnp.zeros_like(token)


def norm_back(upstream, values, gain):
    normed, inverse = normalize(values)
    scaled = upstream * gain
    back = inverse * (scaled - row_mean(scaled) - normed * row_mean(scaled * normed))
    gain_grad = jnp.sum(upstream * normed, axis=0, keepdims=True)
    return back, gain_grad, jnp.sum(upstream, axis=0, keepdims=True)


def norm_back_two_kernel(gain_row, own, y, x, xy, values_hbm, upstream, vecs,
                         grad_ref, grad_b_ref, sums_ref, values, sems):
    copies = start_copies([(values_hbm, values)], sems)
    up = upstream[...]
    total = total_of(own, y, x, xy)
    copies[0].wait()
    back, gain_grad, shift_grad = norm_back(
        total, values[...], vecs[gain_row : gain_row + 1, :]
    )
    grad = up + back
    grad_ref[...] = grad
    grad_b_ref[...] = grad.astype(bf16)
    sums_ref[0:1, :] = gain_grad
    sums_ref[1:2, :] = shift_grad
    sums_ref[2:3, :] = jnp.sum(grad, axis=0, keepdims=True)
    sums_ref[3:4, :] = jnp.sum(up, axis=0, keepdims=True)


def norm_back_one_kernel(gain_row, own, y, x, xy, values_hbm, upstream, vecs, mask,
                         grad_ref, grad_b_ref, sums_ref, values, sems):
    copies = start_copies([(values_hbm, values)], sems)
    total = total_of(own, y, x, xy)
    copies[0].wait()
    back, gain_grad, shift_grad = norm_back(
        total, values[...], vecs[gain_row : gain_row + 1, :]
    )
    grad = upstream[...] + back
    if mask is not None:
        grad = grad * mask[:, 0:1]
    grad_ref[...] = grad
    grad_b_ref[...] = grad.astype(bf16)
    sums_ref[0:1, :] = gain_grad
    sums_ref[1:2, :] = shift_grad


def attn_back_kernel(feats, heads, weight_count, part_count, tile, carried, *refs):
    c0, c1, c2, c3, *rest = refs
    weights, rest = rest[:weight_count], rest[weight_count:]
    usable, q_hbm, attended_hbm, norm_hbm, *rest = rest
    parts, rest = rest[:part_count], rest[part_count:]
    if carried:
        keys_before, values_before, *rest = rest
    x, grad_q, grad_k, grad_v, pairs, q_ref, attended, norms, grad_att, sems = rest
    head_dim = feats // heads
    scale = 1.0 / math.sqrt(head_dim)
    moves = [(q_hbm.at[:, pl.ds(0, feats)], q_ref), (attended_hbm, attended), (norm_hbm, norms)]
    first = 0
    for part in parts:
        rows, width = part.shape
        moves.append(
            (part.at[:, pl.ds(width - 2 * feats, 2 * feats)], pairs.at[pl.ds(first, rows)])
        )
        first += rows
    copies = start_copies(moves, sems)
    assemble((c0, c1, c2, c3), x)
    grad_att[...] = sum(
        dot(x[:, span], w[:, 3 * feats :]) for span, w in shards(weights)
    ).astype(bf16)
    keep = usable[...] > 0.5
    rows = q_ref.shape[0]
    if carried:
        sum_k, sum_v = keys_before[...], values_before[...]
    else:
        sum_k = jnp.zeros(grad_k.shape, f32)
        sum_v = jnp.zeros(grad_v.shape, f32)
    for copy in copies:
        copy.wait()
    keys, values = pairs[:, :feats], pairs[:, feats:]
    for first in range(0, rows, tile):
        span = slice(first, first + tile)
        q = q_ref[span, :]
        ga = grad_att[span, :]
        products = ga.astype(f32) * attended[span, :].astype(f32)
        gq = None
        for h in range(heads):
            own = lanes_of(h, head_dim, feats)
            q_h = only(own, q)
            ga_h = only(own, ga)
            row_dots = jnp.sum(only(own, products), axis=-1, keepdims=True)
            scores = dot_nt(q_h, keys) * scale
            scores = jnp.where(keep, scores, MASK_FILL)
            soft = jnp.exp(scores - norms[span, h * head_dim : h * head_dim + 1])
            grad_soft = dot_nt(ga_h, values)
            grad_scores = (soft * (grad_soft - row_dots)).astype(bf16)
            part = dot(grad_scores, keys)
            gq = part if gq is None else jnp.where(own, part, gq)
            sum_k = sum_k + dot_tn(grad_scores, q_h) * scale
            sum_v = sum_v + dot_tn(soft.astype(bf16), ga_h)
        grad_q[span, :] = gq * scale
    grad_k[...] = sum_k
    grad_v[...] = sum_v


def project_kernel(feats, first, weight_count, gq, gk, gv, *refs):
    weights, (partial_ref, packed) = refs[:weight_count], refs[weight_count:]
    rows = gq.shape[0]
    span = slice(first, first + rows)
    packed[:, :feats] = gq[...].astype(bf16)
    packed[:, feats : 2 * feats] = gk[span, :].astype(bf16)
    packed[:, 2 * feats :] = gv[span, :].astype(bf16)
    for columns, w in shards(weights):
        partial_ref[:, columns] = dot_nt(packed[...], w[:, : 3 * feats]).astype(bf16)


def attn_grad_kernel(feats, count, first_near, first_far, att_near, att_far, up_near, up_far,
                     gq_near, gq_far, gk, gv, *refs):
    outs = refs[:count]
    sums_ref, token, first, att, up, packed, sems = refs[count:]
    rows = up_near.shape[0]
    width_own = outs[0].shape[0]
    near, far = pl.ds(0, rows), pl.ds(rows, rows)
    copies = start_copies(
        [
            (first_near, first.at[near]),
            (first_far, first.at[far]),
            (att_near, att.at[near]),
            (att_far, att.at[far]),
        ],
        sems,
    )
    up[:rows, :] = up_near[...]
    up[rows:, :] = up_far[...]
    packed[:rows, :feats] = gq_near[...].astype(bf16)
    packed[rows:, :feats] = gq_far[...].astype(bf16)
    packed[:, feats : 2 * feats] = gk[...].astype(bf16)
    packed[:, 2 * feats :] = gv[...].astype(bf16)
    sums_ref[0:1, :] = jnp.sum(gq_near[...], axis=0, keepdims=True) + jnp.sum(
        gq_far[...], axis=0, keepdims=True
    )
    sums_ref[1:2, :] = jnp.sum(gv[...], axis=0, keepdims=True)
    f = lax.axis_index("fsdp")
    for copy in copies:
        copy.wait()
    for d in reversed(range(count)):
        place = lax.rem(f + d, count)
        span = pl.ds(pl.multiple_of(place * width_own, width_own), width_own)
        dtype = outs[d].dtype
        outs[d][:, : 3 * feats] = dot_tn(first[:, span], packed[...]).astype(dtype)
        outs[d][:, 3 * feats :] = dot_tn(up[:, span], att[...]).astype(dtype)
    token[...] = jnp.zeros_like(token)


def shard_sum_kernel(own, *refs):
    *others, out_ref, token = refs
    total = own[...]
    for other in others:
        total = total + other[...].astype(f32)
    out_ref[...] = total.astype(bf16)
    token[...] = jnp.zeros_like(token)


def place_mlp_kernel(layer, hidden, p0, p1, p2, p3, *refs):
    fc1_hbm, fc2_hbm, token, fc1, fc2, sems = refs[-6:]
    ci = lax.rem(lax.axis_index("ctx"), GROUP)
    copies = []
    for k, piece in enumerate((p0, p1, p2, p3)):
        span = pl.ds(pl.multiple_of((ci ^ k) * hidden, hidden), hidden)
        fc1[k] = piece[:, :hidden].astype(f32)
        copies += start_copies(
            [(fc1.at[k], fc1_hbm.at[layer, :, span])], sems.at[pl.ds(2 * k, 1)]
        )
        fc2[k] = piece[:, hidden:].astype(f32).T
        copies += start_copies(
            [(fc2.at[k], fc2_hbm.at[layer, span, :])], sems.at[pl.ds(2 * k + 1, 1)]
        )
    token[...] = jnp.zeros_like(token)
    for copy in copies:
        copy.wait()


def place_attn_kernel(layer, feats, p0, p1, p2, p3, *refs):
    qkv_hbm, out_hbm, token, qkv, out, sems = refs[-6:]
    ci = lax.rem(lax.axis_index("ctx"), GROUP)
    copies = []
    for k, piece in enumerate((p0, p1, p2, p3)):
        span = pl.ds(pl.multiple_of((ci ^ k) * feats, feats), feats)
        for j in range(3):
            qkv[k, j] = piece[:, j * feats : (j + 1) * feats].astype(f32)
        copies += start_copies(
            [(qkv.at[k], qkv_hbm.at[layer, :, :, span])], sems.at[pl.ds(2 * k, 1)]
        )
        out[k] = piece[:, 3 * feats :].astype(f32).T
        copies += start_copies(
            [(out.at[k], out_hbm.at[layer, span, :])], sems.at[pl.ds(2 * k + 1, 1)]
        )
    token[...] = jnp.zeros_like(token)
    for copy in copies:
        copy.wait()


def place_call(body, pieces, before, outs, scratch, name):
    extra = () if before is None else (Far(before[0]), Far(before[1]))
    return kernel_call(
        body,
        [saved(s, f32) for s in outs] + [TOKEN],
        *pieces,
        *extra,
        name=name,
        scratch=[pltpu.VMEM(s, f32) for s in scratch] + [DMA((8,))],
        aliases={} if before is None else {4: 0, 5: 1},
    )


def place_rows_kernel(own, other, out_hbm, sems):
    rows = own.shape[0]
    start = pl.multiple_of(lax.axis_index("tp") * rows, rows)
    copies = start_copies(
        [
            (own, out_hbm.at[0, pl.ds(start, rows), :]),
            (other, out_hbm.at[0, pl.ds(pl.multiple_of(rows - start, rows), rows), :]),
        ],
        sems,
    )
    for copy in copies:
        copy.wait()


def per_device(
    inputs, lengths, cotangent, norm_gains, shifts, qv_bias, fc1_bias, w_qkv, w_out, w_fc1, w_fc2
):
    depth = w_qkv.shape[0]
    width_own = w_qkv.shape[2]
    fsdp = lax.axis_size("fsdp")
    tp = lax.axis_size("tp")
    ctx = lax.axis_size("ctx")
    outer = ctx // GROUP
    rows = inputs.shape[1] // tp
    half = rows * CHIPS
    all_rows = 2 * half
    head_own = qv_bias.shape[3]
    head_dim = head_own * fsdp
    heads = qv_bias.shape[2] // GROUP
    feats = heads * head_dim
    hidden = w_fc1.shape[2] // GROUP
    width = width_own * fsdp
    t = lax.axis_index("tp")
    f = lax.axis_index("fsdp")
    ci = lax.axis_index("ctx") % GROUP
    tile = half // 2
    attn_limit = 12 if outer == 1 else 48

    def swap_core(value):
        return lax.ppermute(value, "ctx", [(i, i ^ 1) for i in range(ctx)])

    def swap_x(value):
        return lax.ppermute(value, "ctx", [(i, i ^ 2) for i in range(ctx)])

    def swap_y(value):
        return lax.ppermute(value, "tp", [(i, i ^ 1) for i in range(tp)])

    def swap_xy(value):
        pairs = [
            (i * tp + k, (i ^ 2) * tp + (k ^ 1)) for i in range(ctx) for k in range(tp)
        ]
        return lax.ppermute(value, ("ctx", "tp"), pairs)

    def shift_z(value, d):
        return lax.ppermute(value, "fsdp", [(i, (i + d) % fsdp) for i in range(fsdp)])

    outer_groups = [[o * GROUP + i for o in range(outer)] for i in range(GROUP)]

    def gather_rows(own):
        near = (own, swap_y(own), swap_x(own), swap_xy(own))
        return near, tuple(swap_core(chunk) for chunk in near)

    def reduce_rows(near, far):
        own, y, x, xy = kernel_call(
            core_sum_kernel,
            [((rows, width), f32)] + [((rows, width), bf16)] * 3,
            near,
            swap_core(far),
            name="core_sum",
        )
        return own, swap_y(y), swap_x(x), swap_xy(xy)

    def pack_attn(l, after=()):
        return kernel_call(
            functools.partial(pack_attn_kernel, l, feats),
            [((width_own, 4 * feats), bf16)],
            Far(w_qkv),
            Far(w_out),
            name="pack_attn",
            scratch=[
                pltpu.VMEM((3, width_own, feats), bf16),
                pltpu.VMEM((feats, width_own), bf16),
                DMA((2,)),
            ],
        )[0]

    def pack_mlp(l):
        return kernel_call(
            functools.partial(pack_mlp_kernel, l, hidden),
            [((width_own, 2 * hidden), bf16)],
            Far(w_fc1),
            Far(w_fc2),
            name="pack_mlp",
            scratch=[
                pltpu.VMEM((width_own, hidden), bf16),
                pltpu.VMEM((hidden, width_own), bf16),
                DMA((2,)),
            ],
        )[0]

    attn_w = []
    mlp_w = []
    for l in range(depth):
        own = pack_attn(l)
        if l == 0:
            attn_w.append((own,) + tuple(shift_z(own, d) for d in range(1, fsdp)))
        else:
            attn_w.append((lax.all_gather(own, "fsdp", axis=0, tiled=True),))
        mlp_w.append(lax.all_gather(pack_mlp(l), "fsdp", axis=0, tiled=True))

    qv_own = lax.dynamic_slice_in_dim(qv_bias, ci * heads, heads, axis=2)
    vec_rows = depth * 6
    c1_rows = depth * fc1_bias.shape[2] // width_own
    qv_own = qv_own.reshape(1, -1)
    small_own = jnp.concatenate(
        [
            norm_gains.reshape(-1, width_own),
            shifts.reshape(-1, width_own),
            fc1_bias.reshape(-1, width_own),
            jnp.pad(qv_own, ((0, 0), (0, width_own - qv_own.shape[1]))),
        ],
        axis=0,
    )
    shifted = [small_own] + [shift_z(small_own, d) for d in range(1, fsdp)]

    def shard(a):
        picked = shifted[0]
        for d in range(1, fsdp):
            picked = jnp.where((f - d) % fsdp == a, shifted[d], picked)
        return picked.astype(f32)

    small = [shard(a) for a in range(fsdp)]
    vecs = jnp.concatenate([s[:vec_rows] for s in small], axis=1)
    fc1_all = shard(ci)[vec_rows : vec_rows + c1_rows].reshape(depth, 1, hidden)
    qv_all = jnp.stack(
        [s[vec_rows + c1_rows, : qv_own.shape[1]].reshape(depth, 2, heads, head_own) for s in small],
        axis=3,
    ).reshape(depth, 2, feats)

    def gain_row(l, i):
        return 2 * l + i

    def shift_row(l, i):
        return 2 * depth + 4 * l + i

    key_rows = outer * all_rows
    row_f32 = ((rows, width), f32)
    row_bf16 = ((rows, width), bf16)
    upstream, upstream_b, usable, mask = kernel_call(
        functools.partial(prep_upstream_kernel, tp, outer),
        [row_f32, row_bf16, ((1, key_rows), f32), ((rows, 128), f32)],
        Scalars(lengths),
        Far(cotangent),
        name="prep_upstream",
        scratch=[pltpu.VMEM((rows, width), f32), DMA((1,))],
    )
    near, far = gather_rows(upstream_b)
    half_x = pltpu.VMEM((half, width), bf16)
    *upstream_rows, upstream_token = kernel_call(
        keep_rows_kernel,
        [saved((half, width), bf16)] * 2 + [TOKEN],
        *near,
        *far,
        name="keep_rows",
        scratch=[half_x, half_x, DMA((2,))],
    )
    upstream_chunks = [(Far(x),) for x in upstream_rows]
    stream, first = kernel_call(
        functools.partial(prep_first_kernel, depth),
        [row_f32, row_bf16],
        Far(inputs),
        vecs,
        name="prep_first",
        scratch=[DMA((1,))],
    )
    first_chunks = gather_rows(first)

    partial_out = ((half, width), bf16)
    saved_all = []
    for l in range(depth):
        qkv = []
        first_x = []
        for side in (0, 1):
            qkv_half, x_half = kernel_call(
                functools.partial(qkv_kernel, feats, len(attn_w[l])),
                [((half, 3 * feats), bf16), ((half, width), bf16)],
                *first_chunks[side],
                *attn_w[l],
                qv_all[l],
                name="qkv",
                after=(upstream_token,) if l == 0 and side == 0 else (),
            )
            qkv.append(qkv_half)
            first_x.append(x_half)
        if outer > 1:
            pairs = jnp.concatenate([part[:, feats:] for part in qkv], axis=0)
            pairs = lax.all_gather(
                pairs, "ctx", axis=0, tiled=True, axis_index_groups=outer_groups
            )
            key_parts = (pairs,)
        else:
            key_parts = tuple(qkv)
        attn = [None, None]
        for side in (1, 0):
            kept = (first_x[side], qkv[side]) + ((stream,) if side == 1 else ())
            attn[side] = kernel_call(
                functools.partial(
                    attn_kernel, feats, heads, len(attn_w[l]), len(key_parts), len(kept), tile
                ),
                [partial_out, saved((half, feats), bf16), saved((half, feats), f32)]
                + [saved(k.shape, k.dtype) for k in kept],
                qkv[side],
                *key_parts,
                *attn_w[l],
                usable,
                *kept,
                name="attn",
                limit=attn_limit,
                scratch=[
                    pltpu.VMEM((key_rows, feats), bf16),
                    pltpu.VMEM((key_rows, feats), bf16),
                    pltpu.VMEM((half, feats), bf16),
                    pltpu.VMEM((half, feats), f32),
                    DMA((len(kept) + 2,)),
                ],
            )
        sums = reduce_rows(attn[0][0], attn[1][0])
        middle, second = kernel_call(
            functools.partial(sum_norm_kernel, shift_row(l, 2), gain_row(l, 1), shift_row(l, 1)),
            [row_f32, row_bf16],
            *sums,
            stream,
            vecs,
            name="sum_norm",
        )
        second_chunks = gather_rows(second)
        mlp = [None, None]
        for side in (1, 0):
            kept = (middle,) if side == 1 else ()
            mlp[side] = kernel_call(
                functools.partial(mlp_kernel, hidden, len(kept)),
                [
                    partial_out,
                    saved((half, width), bf16),
                    saved((half, hidden), bf16),
                    saved((2, half, hidden // 2), f32),
                ]
                + [saved(k.shape, k.dtype) for k in kept],
                *second_chunks[side],
                mlp_w[l],
                fc1_all[l],
                *kept,
                name="mlp",
                scratch=[
                    half_x,
                    pltpu.VMEM((half, hidden), bf16),
                    pltpu.VMEM((2, half, hidden // 2), f32),
                    DMA((4 + len(kept),)),
                ],
            )
        sums = reduce_rows(mlp[0][0], mlp[1][0])
        saved_all.append((attn, pairs if outer > 1 else None, mlp))
        if l + 1 < depth:
            stream, first = kernel_call(
                functools.partial(
                    sum_norm_kernel, shift_row(l, 3), gain_row(l + 1, 0), shift_row(l + 1, 0)
                ),
                [row_f32, row_bf16],
                *sums,
                middle,
                vecs,
                name="sum_norm",
            )
            first_chunks = gather_rows(first)
        else:
            outputs_own = kernel_call(
                functools.partial(sum_out_kernel, shift_row(l, 3)),
                [row_f32],
                *sums,
                middle,
                vecs,
                mask,
                name="sum_out",
            )[0]

    def both_halves(own):
        return kernel_call(
            place_rows_kernel,
            [saved(inputs.shape, f32)],
            own,
            swap_y(own),
            name="place_rows",
            scratch=[DMA((2,))],
        )[0]

    outputs = both_halves(outputs_own)

    def spread_grads(part):
        if outer > 1:
            part = lax.psum(part, "ctx", axis_index_groups=outer_groups)
        other = swap_x(part)
        return part, swap_core(part), other, swap_core(other)

    row_sums = [None] * depth
    unit_sums = [None] * depth
    head_sums = [None] * depth
    placed_mlp = None
    placed_attn = None
    shard_token = ()
    mlp_token = ()
    for l in reversed(range(depth)):
        attn, pairs, mlp = saved_all[l]
        back = [None, None]
        for side in (1, 0):
            back[side] = kernel_call(
                functools.partial(mlp_back_kernel, hidden, len(upstream_chunks[side])),
                [partial_out, ((half, hidden), bf16), ((1, hidden), f32), ((half, width), bf16)],
                *upstream_chunks[side],
                mlp_w[l],
                Far(mlp[side][3]),
                name="mlp_back",
                scratch=[pltpu.VMEM((2, half, hidden // 2), f32), DMA((2,))],
            )
        sums = reduce_rows(back[0][0], back[1][0])
        mlp_grad, grad_token = kernel_call(
            functools.partial(mlp_grad_kernel, hidden),
            [((width, 2 * hidden), bf16), TOKEN],
            Far(mlp[0][1]),
            Far(mlp[1][1]),
            Far(mlp[0][2]),
            Far(mlp[1][2]),
            back[0][3],
            back[1][3],
            back[0][1],
            back[1][1],
            name="mlp_grad",
            after=(sums[0],),
            scratch=[
                pltpu.VMEM((all_rows, width), bf16),
                pltpu.VMEM((all_rows, hidden), bf16),
                pltpu.VMEM((all_rows, width), bf16),
                pltpu.VMEM((all_rows, hidden), bf16),
                DMA((4,)),
            ],
            limit=16,
        )
        mlp_part = lax.psum_scatter(mlp_grad, "fsdp", scatter_dimension=0, tiled=True)
        placed_mlp = place_call(
            functools.partial(place_mlp_kernel, l, hidden),
            spread_grads(mlp_part),
            placed_mlp,
            [w_fc1.shape, w_fc2.shape],
            [(GROUP, width_own, hidden), (GROUP, hidden, width_own)],
            "place_mlp",
        )
        unit_sums[l] = back[0][2] + back[1][2]
        grad_middle, middle_b, sums_two = kernel_call(
            functools.partial(norm_back_two_kernel, gain_row(l, 1)),
            [row_f32, row_bf16, ((4, width), f32)],
            *sums,
            Far(mlp[1][4]),
            upstream,
            vecs,
            name="norm_back_two",
            after=(grad_token, *shard_token),
            scratch=[pltpu.VMEM((rows, width), f32), DMA((1,))],
        )
        middle_chunks = gather_rows(middle_b)
        grad_q = [None, None]
        middle_x = [None, None]
        carried = ()
        for side in (0, 1):
            key_parts = (pairs,) if outer > 1 else (attn[0][4], attn[1][4])
            middle_x[side], grad_q[side], *carried = kernel_call(
                functools.partial(
                    attn_back_kernel,
                    feats,
                    heads,
                    len(attn_w[l]),
                    len(key_parts),
                    tile,
                    len(carried) > 0,
                ),
                [
                    ((half, width), bf16),
                    ((half, feats), f32),
                    ((key_rows, feats), f32),
                    ((key_rows, feats), f32),
                ],
                *middle_chunks[side],
                *attn_w[l],
                usable,
                Far(attn[side][4]),
                Far(attn[side][1]),
                Far(attn[side][2]),
                *[Far(part) for part in key_parts],
                *carried,
                name="attn_back",
                scratch=[
                    pltpu.VMEM((key_rows, 2 * feats), bf16),
                    pltpu.VMEM((half, feats), bf16),
                    pltpu.VMEM((half, feats), bf16),
                    pltpu.VMEM((half, feats), f32),
                    pltpu.VMEM((half, feats), bf16),
                    DMA((3 + len(key_parts),)),
                ],
                limit=attn_limit,
            )
        grad_k, grad_v = carried
        if outer > 1:
            grad_k, grad_v = (
                lax.psum_scatter(
                    v, "ctx", scatter_dimension=0, tiled=True, axis_index_groups=outer_groups
                )
                for v in (grad_k, grad_v)
            )

        def project(side, after):
            return kernel_call(
                functools.partial(project_kernel, feats, side * half, len(attn_w[l])),
                [partial_out],
                grad_q[side],
                grad_k,
                grad_v,
                *attn_w[l],
                name="project",
                after=after,
                scratch=[pltpu.VMEM((half, 3 * feats), bf16)],
            )[0]

        def weight_grad(after):
            *parts, head_sum, token = kernel_call(
                functools.partial(attn_grad_kernel, feats, fsdp),
                [((width_own, 4 * feats), f32)]
                + [((width_own, 4 * feats), bf16)] * (fsdp - 1)
                + [((2, feats), f32), TOKEN],
                Far(attn[0][3]),
                Far(attn[1][3]),
                Far(attn[0][1]),
                Far(attn[1][1]),
                *middle_x,
                *grad_q,
                grad_k,
                grad_v,
                name="attn_grad",
                after=after,
                scratch=[
                    pltpu.VMEM((all_rows, width), bf16),
                    pltpu.VMEM((all_rows, feats), bf16),
                    pltpu.VMEM((all_rows, width), bf16),
                    pltpu.VMEM((all_rows, 3 * feats), bf16),
                    DMA((4,)),
                ],
            )
            return parts, head_sum, token

        if l > 0:
            far_part = project(1, ())
            near_part = project(0, ())
            sums = reduce_rows(near_part, far_part)
            parts, head_sums[l], grad_token = weight_grad((sums[0],))
            one_after = (grad_token,)
        else:
            parts, head_sums[l], grad_token = weight_grad(mlp_token)
            far_part = project(1, (grad_token,))
            near_part = project(0, ())
            sums = reduce_rows(near_part, far_part)
            one_after = ()
        attn_part, token = kernel_call(
            shard_sum_kernel,
            [((width_own, 4 * feats), bf16), TOKEN],
            parts[0],
            *[shift_z(parts[d], d) for d in range(1, fsdp)],
            name="shard_sum",
        )
        shard_token = (token,)
        placed_attn = place_call(
            functools.partial(place_attn_kernel, l, feats),
            spread_grads(attn_part),
            placed_attn,
            [w_qkv.shape, w_out.shape],
            [(GROUP, 3, width_own, feats), (GROUP, feats, width_own)],
            "place_attn",
        )
        mlp_token = (placed_mlp[2],)
        body = functools.partial(norm_back_one_kernel, gain_row(l, 0))
        if l > 0:
            masked = ()
            body = lambda *refs, body=body: body(*refs[:7], None, *refs[7:])
        else:
            masked = (mask,)
        upstream, upstream_b, sums_one = kernel_call(
            body,
            [row_f32, row_bf16, ((2, width), f32)],
            *sums,
            Far(attn[1][5]),
            grad_middle,
            vecs,
            *masked,
            name="norm_back_one",
            after=one_after,
            scratch=[pltpu.VMEM((rows, width), f32), DMA((1,))],
        )
        if l > 0:
            upstream_chunks = gather_rows(upstream_b)
        row_sums[l] = (sums_one, sums_two)

    grad_inputs = both_halves(upstream)

    vec_part = jnp.concatenate(
        [
            piece
            for l in range(depth)
            for piece in (
                row_sums[l][0][0:1],
                row_sums[l][1][0:1],
                row_sums[l][0][1:2],
                row_sums[l][1][1:4],
            )
        ],
        axis=0,
    )
    unit_part = jnp.concatenate(unit_sums, axis=0)
    head_part = jnp.concatenate(head_sums, axis=0)
    unit_lines = unit_part.reshape(-1, width)
    head_lines = head_part.reshape(1, -1)
    head_lines = jnp.pad(head_lines, ((0, 0), (0, width - head_lines.shape[1])))
    packed = jnp.concatenate([vec_part, unit_lines, head_lines], axis=0)
    if outer > 1:
        packed = lax.psum(packed, "ctx", axis_index_groups=outer_groups)
    step = 1
    while step < fsdp:
        packed = packed + lax.ppermute(packed, "fsdp", [(i, i ^ step) for i in range(fsdp)])
        step *= 2
    vec_sum = lax.dynamic_slice_in_dim(packed[:vec_rows], f * width_own, width_own, axis=1)
    rest = packed[vec_rows:]
    vec_sum = vec_sum + swap_y(vec_sum)
    rest_core = swap_core(rest)
    vec_sum = vec_sum + swap_core(vec_sum)
    rest_two = jnp.stack([rest, rest_core])
    vec_sum = vec_sum + swap_x(vec_sum)
    rest_four = jnp.concatenate([rest_two, swap_x(rest_two)], axis=0)
    vec_sum = vec_sum.reshape(depth, 6, width_own)
    unit_count = unit_lines.shape[0]

    def of_place(c):
        return lax.dynamic_index_in_dim(rest_four, ci ^ c, 0, keepdims=False)

    grad_fc1_bias = of_place(f)[:unit_count].reshape(depth, 1, hidden)
    grad_qv_bias = jnp.stack(
        [
            lax.dynamic_slice_in_dim(
                of_place(c)[unit_count, : head_part.size].reshape(depth, 2, heads, head_dim),
                f * head_own,
                head_own,
                axis=3,
            )
            for c in range(GROUP)
        ],
        axis=2,
    ).reshape(qv_bias.shape)
    return (
        outputs,
        grad_inputs,
        vec_sum[:, :2],
        vec_sum[:, 2:],
        grad_qv_bias,
        grad_fc1_bias,
        placed_attn[0],
        placed_attn[1],
        placed_mlp[0],
        placed_mlp[1],
    )


def solution(mesh):
    rows = P("fsdp", "ctx", None)
    params = (
        P(None, None, "fsdp"),
        P(None, None, "fsdp"),
        P(None, None, "tp", "fsdp"),
        P(None, "tp", "fsdp"),
        P(None, None, "fsdp", "tp"),
        P(None, "tp", "fsdp"),
        P(None, "fsdp", "tp"),
        P(None, "tp", "fsdp"),
    )
    return jax.shard_map(
        per_device,
        mesh=mesh,
        in_specs=(rows, P("fsdp", None), rows) + params,
        out_specs=(rows, rows) + params,
        check_vma=False,
    )
```

```python
import functools
import math

import jax
import jax.numpy as jnp
from jax import lax
from jax.experimental import pallas as pl
from jax.experimental.pallas import tpu as pltpu
from jax.sharding import PartitionSpec as P

NORM_EPSILON = 1e-06
MASK_FILL = -1e30
ROOT_HALF = 0.7071067811865476
INV_ROOT_TAU = 0.3989422804014327
GROUP = 4
ORDER = (0, 1, 4, 5, 2, 3, 6, 7)
CHIPS = 4

bf16 = jnp.bfloat16
f32 = jnp.float32
VMEM = pl.BlockSpec(memory_space=pltpu.VMEM)
SMEM = pl.BlockSpec(memory_space=pltpu.SMEM)
HBM = pl.BlockSpec(memory_space=pltpu.HBM)
DMA = pltpu.SemaphoreType.DMA
TOKEN = ((8, 128), f32)


def dot(a, b):
    return lax.dot_general(a, b, (((1,), (0,)), ((), ())), preferred_element_type=f32)


def dot_nt(a, b):
    return lax.dot_general(a, b, (((1,), (1,)), ((), ())), preferred_element_type=f32)


def dot_tn(a, b):
    return lax.dot_general(a, b, (((0,), (0,)), ((), ())), preferred_element_type=f32)


class Far:
    def __init__(self, value):
        self.value = value


class Scalars:
    def __init__(self, value):
        self.value = value


def saved(shape, dtype):
    return pltpu.HBM(shape, dtype)


def kernel_call(body, outs, *args, name, limit=12, scratch=(), after=(), aliases=None, us=0):
    values, specs = [], []
    for arg in (*args, *after):
        if isinstance(arg, Far):
            values.append(pltpu.with_memory_space_constraint(arg.value, pltpu.HBM))
            specs.append(HBM)
        elif isinstance(arg, Scalars):
            values.append(arg.value)
            specs.append(SMEM)
        else:
            values.append(arg)
            specs.append(VMEM)
    first, last = len(args), len(args) + len(after)

    def run(*refs):
        body(*refs[:first], *refs[last:])

    out_shape, out_specs = [], []
    for out in outs:
        if isinstance(out, tuple):
            out_shape.append(jax.ShapeDtypeStruct(*out))
            out_specs.append(VMEM)
        else:
            out_shape.append(out)
            out_specs.append(HBM)
    return pl.pallas_call(
        run,
        out_shape=out_shape,
        in_specs=specs,
        out_specs=out_specs,
        scratch_shapes=list(scratch),
        input_output_aliases=aliases or {},
        compiler_params=pltpu.CompilerParams(vmem_limit_bytes=limit << 20),
        cost_estimate=pl.CostEstimate(flops=us * 10**9, bytes_accessed=0, transcendentals=0),
        name=name,
    )(*values)


def start_copies(pairs, sems):
    copies = [
        pltpu.make_async_copy(source, target, sems.at[k])
        for k, (source, target) in enumerate(pairs)
    ]
    for copy in copies:
        copy.start()
    return copies


def row_mean(value):
    return jnp.mean(value, axis=-1, keepdims=True)


def normalize(values):
    center = values - row_mean(values)
    inverse = lax.rsqrt(row_mean(center * center) + NORM_EPSILON)
    return center * inverse, inverse


def lanes_of(head, head_dim, width):
    lane = lax.broadcasted_iota(jnp.int32, (1, width), 1)
    return (lane >= head * head_dim) & (lane < (head + 1) * head_dim)


def assemble(chunks, target):
    rows = chunks[0].shape[0]
    for k, chunk in enumerate(chunks):
        target[k * rows : (k + 1) * rows, :] = chunk[...]


def only(flag, value):
    return jnp.where(flag, value, jnp.zeros_like(value))


def shards(weights):
    if len(weights) == 1:
        rows = weights[0].shape[0]
        return [(pl.ds(0, rows), weights[0])]
    count = len(weights)
    rows = weights[0].shape[0]
    f = lax.axis_index("fsdp")
    found = []
    for d, ref in enumerate(weights):
        place = lax.rem(f + (count - d), count)
        found.append((pl.ds(pl.multiple_of(place * rows, rows), rows), ref))
    return found


def pack_attn_kernel(layer, feats, qkv_hbm, out_hbm, packed_ref, token, qkv, out, sems):
    ci = lax.rem(lax.axis_index("ctx"), GROUP)
    span = pl.ds(pl.multiple_of(ci * feats, feats), feats)
    copies = start_copies(
        [(qkv_hbm.at[layer, :, :, span], qkv), (out_hbm.at[layer, span, :], out)], sems
    )
    copies[0].wait()
    for k in range(3):
        packed_ref[:, k * feats : (k + 1) * feats] = qkv[k]
    copies[1].wait()
    packed_ref[:, 3 * feats :] = out[...].T
    token[...] = jnp.zeros_like(token)


def pack_mlp_kernel(layer, hidden, fc1_hbm, fc2_hbm, packed_ref, token, fc1, fc2, sems):
    ci = lax.rem(lax.axis_index("ctx"), GROUP)
    span = pl.ds(pl.multiple_of(ci * hidden, hidden), hidden)
    copies = start_copies(
        [(fc1_hbm.at[layer, :, span], fc1), (fc2_hbm.at[layer, span, :], fc2)], sems
    )
    copies[0].wait()
    packed_ref[:, :hidden] = fc1[...]
    copies[1].wait()
    packed_ref[:, hidden:] = fc2[...].T
    token[...] = jnp.zeros_like(token)


def prep_upstream_kernel(tp, outer, lengths, cotangent_hbm,
                         upstream_ref, upstream_b_ref, usable_ref, mask_ref, rows_in, sems):
    rows = rows_in.shape[0]
    c = lax.axis_index("ctx")
    t = lax.axis_index("tp")
    place = lax.rem(c, GROUP) * tp + t
    start = pl.multiple_of(t * rows, rows)
    copies = start_copies([(cotangent_hbm.at[0, pl.ds(start, rows), :], rows_in)], sems)
    lane = lax.broadcasted_iota(jnp.int32, usable_ref.shape, 1)
    limit = jnp.zeros(usable_ref.shape, jnp.int32)
    for o in range(outer):
        for k, d in enumerate(ORDER):
            source = place ^ d
            first_lane = (o * len(ORDER) + k) * rows
            count = lengths[0, o * GROUP + lax.div(source, tp)] - lax.rem(source, tp) * rows
            limit = jnp.where(lane >= first_lane, first_lane + jnp.clip(count, 0, rows), limit)
    usable_ref[...] = jnp.where(lane < limit, 1.0, 0.0)
    row = lax.broadcasted_iota(jnp.int32, mask_ref.shape, 0)
    mask = jnp.where(row + start < lengths[0, c], 1.0, 0.0)
    mask_ref[...] = mask
    copies[0].wait()
    upstream = rows_in[...] * mask[:, 0:1]
    upstream_ref[...] = upstream
    upstream_b_ref[...] = upstream.astype(bf16)


def prep_first_kernel(depth, inputs_hbm, vecs, stream_ref, first_ref, sems):
    rows = stream_ref.shape[0]
    start = pl.multiple_of(lax.axis_index("tp") * rows, rows)
    copies = start_copies([(inputs_hbm.at[0, pl.ds(start, rows), :], stream_ref)], sems)
    copies[0].wait()
    normed, _ = normalize(stream_ref[...])
    shift = vecs[2 * depth : 2 * depth + 1, :]
    first_ref[...] = (normed * vecs[0:1, :] + shift).astype(bf16)


def keep_rows_kernel(*refs):
    chunks, (near_hbm, far_hbm, token, near, far, sems) = refs[:8], refs[8:]
    assemble(chunks[:4], near)
    assemble(chunks[4:], far)
    for copy in start_copies([(near, near_hbm), (far, far_hbm)], sems):
        copy.wait()
    token[...] = jnp.zeros_like(token)


def qkv_kernel(feats, weight_count, *refs):
    c0, c1, c2, c3, *rest = refs
    weights = rest[:weight_count]
    bias, qkv_ref, x = rest[weight_count:]
    assemble((c0, c1, c2, c3), x)
    qkv = sum(dot(x[:, span], w[:, : 3 * feats]) for span, w in shards(weights))
    qkv_ref[:, :feats] = (qkv[:, :feats] + bias[0:1, :]).astype(bf16)
    qkv_ref[:, feats : 2 * feats] = qkv[:, feats : 2 * feats].astype(bf16)
    qkv_ref[:, 2 * feats :] = (qkv[:, 2 * feats :] + bias[1:2, :]).astype(bf16)


def attn_kernel(feats, heads, weight_count, part_count, keep_count, tile, *refs):
    q_ref, *rest = refs
    parts = rest[:part_count]
    weights = rest[part_count : part_count + weight_count]
    rest = rest[part_count + weight_count :]
    usable, *rest = rest
    kept, rest = rest[:keep_count], rest[keep_count:]
    partial_ref, attended_hbm, norm_hbm, *rest = rest
    kept_hbm, rest = rest[:keep_count], rest[keep_count:]
    keys, values, attended_ref, norm_ref, sems = rest
    head_dim = feats // heads
    scale = 1.0 / math.sqrt(head_dim)
    copies = start_copies(list(zip(kept, kept_hbm)), sems)
    first = 0
    for part in parts:
        rows, width = part.shape
        keys[first : first + rows, :] = part[:, width - 2 * feats : width - feats]
        values[first : first + rows, :] = part[:, width - feats :]
        first += rows
    keep = usable[...] > 0.5
    rows = q_ref.shape[0]
    for first in range(0, rows, tile):
        span = slice(first, first + tile)
        q = q_ref[span, :feats]
        attended = None
        for h in range(heads):
            own = lanes_of(h, head_dim, feats)
            scores = dot_nt(only(own, q), keys[...]) * scale
            scores = jnp.where(keep, scores, MASK_FILL)
            highest = jnp.max(scores, axis=-1, keepdims=True)
            raised = jnp.exp(scores - highest)
            total = jnp.sum(raised, axis=-1, keepdims=True)
            soft = (raised * (1.0 / total)).astype(bf16)
            result = dot(soft, values[...])
            log_norm = jnp.broadcast_to(highest + jnp.log(total), (tile, feats))
            if attended is None:
                attended, norms = result, log_norm
            else:
                attended = jnp.where(own, result, attended)
                norms = jnp.where(own, log_norm, norms)
        attended_ref[span, :] = attended.astype(bf16)
        norm_ref[span, :] = norms
    copies += start_copies(
        [(attended_ref, attended_hbm), (norm_ref, norm_hbm)],
        sems.at[pl.ds(keep_count, 2)],
    )
    for span, w in shards(weights):
        partial_ref[:, span] = dot_nt(attended_ref[...], w[:, 3 * feats :]).astype(bf16)
    for copy in copies:
        copy.wait()


def core_sum_kernel(near, far, own_ref, y_ref, x_ref, xy_ref):
    rows = own_ref.shape[0]
    for k, ref in enumerate((own_ref, y_ref, x_ref, xy_ref)):
        span = slice(k * rows, (k + 1) * rows)
        ref[...] = (near[span, :].astype(f32) + far[span, :].astype(f32)).astype(ref.dtype)


def total_of(own, y, x, xy):
    return own[...] + y[...].astype(f32) + x[...].astype(f32) + xy[...].astype(f32)


def sum_norm_kernel(bias_row, gain_row, shift_row, own, y, x, xy, residual_hbm, vecs,
                    stream_ref, normed_ref, residual, sems):
    copies = start_copies([(residual_hbm, residual)], sems)
    total = total_of(own, y, x, xy) + vecs[bias_row : bias_row + 1, :]
    copies[0].wait()
    stream = residual[...] + total
    stream_ref[...] = stream
    normed, _ = normalize(stream)
    gain = vecs[gain_row : gain_row + 1, :]
    normed_ref[...] = (normed * gain + vecs[shift_row : shift_row + 1, :]).astype(bf16)


def sum_out_kernel(bias_row, own, y, x, xy, residual, vecs, mask, out_ref):
    stream = residual[...] + total_of(own, y, x, xy) + vecs[bias_row : bias_row + 1, :]
    out_ref[...] = stream * mask[:, 0:1]


def mlp_kernel(hidden, keep_count, c0, c1, c2, c3, w, bias, *refs):
    kept, rest = refs[:keep_count], refs[keep_count:]
    partial_ref, x_hbm, act_hbm, slope_hbm, *rest = rest
    kept_hbm, (x, act_ref, slope_ref, sems) = rest[:keep_count], rest[keep_count:]
    assemble((c0, c1, c2, c3), x)
    copies = start_copies([(x, x_hbm), *zip(kept, kept_hbm)], sems)
    block = hidden // 2
    for k in range(2):
        span = slice(k * block, (k + 1) * block)
        pre = dot(x[...], w[:, span]) + bias[:, span]
        cdf = 0.5 * (1.0 + lax.erf(pre * ROOT_HALF))
        density = jnp.exp(-0.5 * pre * pre) * INV_ROOT_TAU
        slope_ref[k] = cdf + pre * density
        act_ref[:, span] = (pre * cdf).astype(bf16)
        copies += start_copies(
            [(slope_ref.at[k], slope_hbm.at[k])], sems.at[pl.ds(1 + keep_count + k, 1)]
        )
    copies += start_copies([(act_ref, act_hbm)], sems.at[pl.ds(3 + keep_count, 1)])
    partial_ref[...] = dot_nt(act_ref[...], w[:, hidden:]).astype(bf16)
    for copy in copies:
        copy.wait()


def mlp_back_kernel(hidden, chunk_count, *refs):
    chunks, (w, slope_hbm, *rest) = refs[:chunk_count], refs[chunk_count:]
    partial_ref, grad_ref, sum_ref, x, slope, sems = rest
    copies = start_copies([(slope_hbm, slope)], sems)
    if chunk_count == 1:
        copies += start_copies([(chunks[0], x)], sems.at[pl.ds(1, 1)])
        copies[1].wait()
    else:
        assemble(chunks, x)
    grad = dot(x[...], w[:, hidden:])
    copies[0].wait()
    block = hidden // 2
    for k in range(2):
        span = slice(k * block, (k + 1) * block)
        part = grad[:, span] * slope[k]
        grad_ref[:, span] = part.astype(bf16)
        sum_ref[:, span] = jnp.sum(part, axis=0, keepdims=True)
    partial_ref[...] = dot_nt(grad_ref[...], w[:, :hidden]).astype(bf16)


def mlp_grad_kernel(hidden, second_near, second_far, act_near, act_far, up_near, up_far,
                    grad_near, grad_far, out_ref, token, second, act, up, grad, sems):
    rows = up_near.shape[0]
    near, far = pl.ds(0, rows), pl.ds(rows, rows)
    copies = start_copies(
        [
            (second_near, second.at[near]),
            (second_far, second.at[far]),
            (act_near, act.at[near]),
            (act_far, act.at[far]),
        ],
        sems,
    )
    up[:rows, :] = up_near[...]
    up[rows:, :] = up_far[...]
    grad[:rows, :] = grad_near[...]
    grad[rows:, :] = grad_far[...]
    for copy in copies:
        copy.wait()
    out_ref[:, hidden:] = dot_tn(up[...], act[...]).astype(bf16)
    out_ref[:, :hidden] = dot_tn(second[...], grad[...]).astype(bf16)
    token[...] = jnp.zeros_like(token)


def norm_back(upstream, values, gain):
    normed, inverse = normalize(values)
    scaled = upstream * gain
    back = inverse * (scaled - row_mean(scaled) - normed * row_mean(scaled * normed))
    gain_grad = jnp.sum(upstream * normed, axis=0, keepdims=True)
    return back, gain_grad, jnp.sum(upstream, axis=0, keepdims=True)


def norm_back_two_kernel(gain_row, own, y, x, xy, values_hbm, upstream, vecs,
                         grad_ref, grad_b_ref, sums_ref, values, sems):
    copies = start_copies([(values_hbm, values)], sems)
    up = upstream[...]
    total = total_of(own, y, x, xy)
    copies[0].wait()
    back, gain_grad, shift_grad = norm_back(
        total, values[...], vecs[gain_row : gain_row + 1, :]
    )
    grad = up + back
    grad_ref[...] = grad
    grad_b_ref[...] = grad.astype(bf16)
    sums_ref[0:1, :] = gain_grad
    sums_ref[1:2, :] = shift_grad
    sums_ref[2:3, :] = jnp.sum(grad, axis=0, keepdims=True)
    sums_ref[3:4, :] = jnp.sum(up, axis=0, keepdims=True)


def norm_back_one_kernel(gain_row, own, y, x, xy, values_hbm, upstream, vecs, mask,
                         grad_ref, grad_b_ref, sums_ref, values, sems):
    copies = start_copies([(values_hbm, values)], sems)
    total = total_of(own, y, x, xy)
    copies[0].wait()
    back, gain_grad, shift_grad = norm_back(
        total, values[...], vecs[gain_row : gain_row + 1, :]
    )
    grad = upstream[...] + back
    if mask is not None:
        grad = grad * mask[:, 0:1]
    grad_ref[...] = grad
    grad_b_ref[...] = grad.astype(bf16)
    sums_ref[0:1, :] = gain_grad
    sums_ref[1:2, :] = shift_grad


def attn_back_kernel(feats, heads, weight_count, part_count, tile, carried, *refs):
    c0, c1, c2, c3, *rest = refs
    weights, rest = rest[:weight_count], rest[weight_count:]
    usable, q_hbm, attended_hbm, norm_hbm, *rest = rest
    parts, rest = rest[:part_count], rest[part_count:]
    if carried:
        keys_before, values_before, *rest = rest
    x, grad_q, grad_k, grad_v, pairs, q_ref, attended, norms, grad_att, sems = rest
    head_dim = feats // heads
    scale = 1.0 / math.sqrt(head_dim)
    moves = [(q_hbm.at[:, pl.ds(0, feats)], q_ref), (attended_hbm, attended), (norm_hbm, norms)]
    first = 0
    for part in parts:
        rows, width = part.shape
        moves.append(
            (part.at[:, pl.ds(width - 2 * feats, 2 * feats)], pairs.at[pl.ds(first, rows)])
        )
        first += rows
    copies = start_copies(moves, sems)
    assemble((c0, c1, c2, c3), x)
    grad_att[...] = sum(
        dot(x[:, span], w[:, 3 * feats :]) for span, w in shards(weights)
    ).astype(bf16)
    keep = usable[...] > 0.5
    rows = q_ref.shape[0]
    if carried:
        sum_k, sum_v = keys_before[...], values_before[...]
    else:
        sum_k = jnp.zeros(grad_k.shape, f32)
        sum_v = jnp.zeros(grad_v.shape, f32)
    for copy in copies:
        copy.wait()
    keys, values = pairs[:, :feats], pairs[:, feats:]
    for first in range(0, rows, tile):
        span = slice(first, first + tile)
        q = q_ref[span, :]
        ga = grad_att[span, :]
        products = ga.astype(f32) * attended[span, :].astype(f32)
        gq = None
        for h in range(heads):
            own = lanes_of(h, head_dim, feats)
            q_h = only(own, q)
            ga_h = only(own, ga)
            row_dots = jnp.sum(only(own, products), axis=-1, keepdims=True)
            scores = dot_nt(q_h, keys) * scale
            scores = jnp.where(keep, scores, MASK_FILL)
            soft = jnp.exp(scores - norms[span, h * head_dim : h * head_dim + 1])
            grad_soft = dot_nt(ga_h, values)
            grad_scores = (soft * (grad_soft - row_dots)).astype(bf16)
            part = dot(grad_scores, keys)
            gq = part if gq is None else jnp.where(own, part, gq)
            sum_k = sum_k + dot_tn(grad_scores, q_h) * scale
            sum_v = sum_v + dot_tn(soft.astype(bf16), ga_h)
        grad_q[span, :] = gq * scale
    grad_k[...] = sum_k
    grad_v[...] = sum_v


def project_kernel(feats, first, weight_count, gq, gk, gv, *refs):
    weights, (partial_ref, packed) = refs[:weight_count], refs[weight_count:]
    rows = gq.shape[0]
    span = slice(first, first + rows)
    packed[:, :feats] = gq[...].astype(bf16)
    packed[:, feats : 2 * feats] = gk[span, :].astype(bf16)
    packed[:, 2 * feats :] = gv[span, :].astype(bf16)
    for columns, w in shards(weights):
        partial_ref[:, columns] = dot_nt(packed[...], w[:, : 3 * feats]).astype(bf16)


def attn_grad_kernel(feats, first_near, first_far, att_near, att_far, up_near, up_far,
                     gq_near, gq_far, gk, gv, out_ref, sums_ref, token,
                     first, att, up, packed, sems):
    rows = up_near.shape[0]
    near, far = pl.ds(0, rows), pl.ds(rows, rows)
    copies = start_copies(
        [
            (first_near, first.at[near]),
            (first_far, first.at[far]),
            (att_near, att.at[near]),
            (att_far, att.at[far]),
        ],
        sems,
    )
    up[:rows, :] = up_near[...]
    up[rows:, :] = up_far[...]
    packed[:rows, :feats] = gq_near[...].astype(bf16)
    packed[rows:, :feats] = gq_far[...].astype(bf16)
    packed[:, feats : 2 * feats] = gk[...].astype(bf16)
    packed[:, 2 * feats :] = gv[...].astype(bf16)
    sums_ref[0:1, :] = jnp.sum(gq_near[...], axis=0, keepdims=True) + jnp.sum(
        gq_far[...], axis=0, keepdims=True
    )
    sums_ref[1:2, :] = jnp.sum(gv[...], axis=0, keepdims=True)
    for copy in copies:
        copy.wait()
    out_ref[:, : 3 * feats] = dot_tn(first[...], packed[...]).astype(bf16)
    out_ref[:, 3 * feats :] = dot_tn(up[...], att[...]).astype(bf16)
    token[...] = jnp.zeros_like(token)


def place_mlp_kernel(layer, hidden, p0, p1, p2, p3, *refs):
    fc1_hbm, fc2_hbm, token, fc1, fc2, sems = refs[-6:]
    ci = lax.rem(lax.axis_index("ctx"), GROUP)
    copies = []
    for k, piece in enumerate((p0, p1, p2, p3)):
        span = pl.ds(pl.multiple_of((ci ^ k) * hidden, hidden), hidden)
        fc1[k] = piece[:, :hidden].astype(f32)
        copies += start_copies(
            [(fc1.at[k], fc1_hbm.at[layer, :, span])], sems.at[pl.ds(2 * k, 1)]
        )
        fc2[k] = piece[:, hidden:].astype(f32).T
        copies += start_copies(
            [(fc2.at[k], fc2_hbm.at[layer, span, :])], sems.at[pl.ds(2 * k + 1, 1)]
        )
    token[...] = jnp.zeros_like(token)
    for copy in copies:
        copy.wait()


def place_attn_kernel(layer, feats, p0, p1, p2, p3, *refs):
    qkv_hbm, out_hbm, token, qkv, out, sems = refs[-6:]
    ci = lax.rem(lax.axis_index("ctx"), GROUP)
    copies = []
    for k, piece in enumerate((p0, p1, p2, p3)):
        span = pl.ds(pl.multiple_of((ci ^ k) * feats, feats), feats)
        for j in range(3):
            qkv[k, j] = piece[:, j * feats : (j + 1) * feats].astype(f32)
        copies += start_copies(
            [(qkv.at[k], qkv_hbm.at[layer, :, :, span])], sems.at[pl.ds(2 * k, 1)]
        )
        out[k] = piece[:, 3 * feats :].astype(f32).T
        copies += start_copies(
            [(out.at[k], out_hbm.at[layer, span, :])], sems.at[pl.ds(2 * k + 1, 1)]
        )
    token[...] = jnp.zeros_like(token)
    for copy in copies:
        copy.wait()


def place_call(body, pieces, before, outs, scratch, name):
    extra = () if before is None else (Far(before[0]), Far(before[1]))
    return kernel_call(
        body,
        [saved(s, f32) for s in outs] + [TOKEN],
        *pieces,
        *extra,
        name=name,
        scratch=[pltpu.VMEM(s, f32) for s in scratch] + [DMA((8,))],
        aliases={} if before is None else {4: 0, 5: 1},
    )


def place_rows_kernel(own, other, out_hbm, sems):
    rows = own.shape[0]
    start = pl.multiple_of(lax.axis_index("tp") * rows, rows)
    copies = start_copies(
        [
            (own, out_hbm.at[0, pl.ds(start, rows), :]),
            (other, out_hbm.at[0, pl.ds(pl.multiple_of(rows - start, rows), rows), :]),
        ],
        sems,
    )
    for copy in copies:
        copy.wait()


def per_device(
    inputs, lengths, cotangent, norm_gains, shifts, qv_bias, fc1_bias, w_qkv, w_out, w_fc1, w_fc2
):
    depth = w_qkv.shape[0]
    width_own = w_qkv.shape[2]
    fsdp = lax.axis_size("fsdp")
    tp = lax.axis_size("tp")
    ctx = lax.axis_size("ctx")
    outer = ctx // GROUP
    rows = inputs.shape[1] // tp
    half = rows * CHIPS
    all_rows = 2 * half
    head_own = qv_bias.shape[3]
    head_dim = head_own * fsdp
    heads = qv_bias.shape[2] // GROUP
    feats = heads * head_dim
    hidden = w_fc1.shape[2] // GROUP
    width = width_own * fsdp
    t = lax.axis_index("tp")
    f = lax.axis_index("fsdp")
    ci = lax.axis_index("ctx") % GROUP
    tile = half // 2
    attn_limit = 12 if outer == 1 else 48

    def swap_core(value):
        return lax.ppermute(value, "ctx", [(i, i ^ 1) for i in range(ctx)])

    def swap_x(value):
        return lax.ppermute(value, "ctx", [(i, i ^ 2) for i in range(ctx)])

    def swap_y(value):
        return lax.ppermute(value, "tp", [(i, i ^ 1) for i in range(tp)])

    def swap_xy(value):
        pairs = [
            (i * tp + k, (i ^ 2) * tp + (k ^ 1)) for i in range(ctx) for k in range(tp)
        ]
        return lax.ppermute(value, ("ctx", "tp"), pairs)

    def shift_z(value, d):
        return lax.ppermute(value, "fsdp", [(i, (i + d) % fsdp) for i in range(fsdp)])

    outer_groups = [[o * GROUP + i for o in range(outer)] for i in range(GROUP)]

    def gather_rows(own):
        near = (own, swap_y(own), swap_x(own), swap_xy(own))
        return near, tuple(swap_core(chunk) for chunk in near)

    def reduce_rows(near, far):
        own, y, x, xy = kernel_call(
            core_sum_kernel,
            [((rows, width), f32)] + [((rows, width), bf16)] * 3,
            near,
            swap_core(far),
            name="core_sum",
        )
        xy, x, y = swap_xy(xy), swap_x(x), swap_y(y)
        return own, y, x, xy

    def pack_attn(l, after):
        return kernel_call(
            functools.partial(pack_attn_kernel, l, feats),
            [((width_own, 4 * feats), bf16), TOKEN],
            Far(w_qkv),
            Far(w_out),
            name="pack_attn",
            after=after,
            scratch=[
                pltpu.VMEM((3, width_own, feats), bf16),
                pltpu.VMEM((feats, width_own), bf16),
                DMA((2,)),
            ],
        )

    def pack_mlp(l, after):
        return kernel_call(
            functools.partial(pack_mlp_kernel, l, hidden),
            [((width_own, 2 * hidden), bf16), TOKEN],
            Far(w_fc1),
            Far(w_fc2),
            name="pack_mlp",
            after=after,
            scratch=[
                pltpu.VMEM((width_own, hidden), bf16),
                pltpu.VMEM((hidden, width_own), bf16),
                DMA((2,)),
            ],
        )

    attn_w = []
    mlp_w = []
    token = None
    for l in range(depth):
        own, token = pack_attn(l, () if token is None else (token,))
        attn_w.append((lax.all_gather(own, "fsdp", axis=0, tiled=True),))
        own, token = pack_mlp(l, (token,))
        mlp_w.append(lax.all_gather(own, "fsdp", axis=0, tiled=True))
        if l == 0:
            pack_token = token

    qv_own = lax.dynamic_slice_in_dim(qv_bias, ci * heads, heads, axis=2)
    vec_rows = depth * 6
    c1_rows = depth * fc1_bias.shape[2] // width_own
    qv_own = qv_own.reshape(1, -1)
    small_own = jnp.concatenate(
        [
            norm_gains.reshape(-1, width_own),
            shifts.reshape(-1, width_own),
            fc1_bias.reshape(-1, width_own),
            jnp.pad(qv_own, ((0, 0), (0, width_own - qv_own.shape[1]))),
        ],
        axis=0,
    )
    shifted = [small_own] + [shift_z(small_own, d) for d in range(1, fsdp)]

    def shard(a):
        picked = shifted[0]
        for d in range(1, fsdp):
            picked = jnp.where((f - d) % fsdp == a, shifted[d], picked)
        return picked.astype(f32)

    small = [shard(a) for a in range(fsdp)]
    vecs = jnp.concatenate([s[:vec_rows] for s in small], axis=1)
    fc1_all = shard(ci)[vec_rows : vec_rows + c1_rows].reshape(depth, 1, hidden)
    qv_all = jnp.stack(
        [s[vec_rows + c1_rows, : qv_own.shape[1]].reshape(depth, 2, heads, head_own) for s in small],
        axis=3,
    ).reshape(depth, 2, feats)

    def gain_row(l, i):
        return 2 * l + i

    def shift_row(l, i):
        return 2 * depth + 4 * l + i

    key_rows = outer * all_rows
    row_f32 = ((rows, width), f32)
    row_bf16 = ((rows, width), bf16)
    upstream, upstream_b, usable, mask = kernel_call(
        functools.partial(prep_upstream_kernel, tp, outer),
        [row_f32, row_bf16, ((1, key_rows), f32), ((rows, 128), f32)],
        Scalars(lengths),
        Far(cotangent),
        name="prep_upstream",
        after=(pack_token,),
        scratch=[pltpu.VMEM((rows, width), f32), DMA((1,))],
    )
    near, far = gather_rows(upstream_b)
    half_x = pltpu.VMEM((half, width), bf16)
    *upstream_rows, upstream_token = kernel_call(
        keep_rows_kernel,
        [saved((half, width), bf16)] * 2 + [TOKEN],
        *near,
        *far,
        name="keep_rows",
        scratch=[half_x, half_x, DMA((2,))],
    )
    upstream_chunks = [(Far(x),) for x in upstream_rows]
    stream, first = kernel_call(
        functools.partial(prep_first_kernel, depth),
        [row_f32, row_bf16],
        Far(inputs),
        vecs,
        name="prep_first",
        scratch=[DMA((1,))],
    )
    first_chunks = gather_rows(first)

    partial_out = ((half, width), bf16)
    saved_all = []
    for l in range(depth):
        qkv = []
        first_x = []
        for side in (0, 1):
            qkv_half, x_half = kernel_call(
                functools.partial(qkv_kernel, feats, len(attn_w[l])),
                [((half, 3 * feats), bf16), ((half, width), bf16)],
                *first_chunks[side],
                *attn_w[l],
                qv_all[l],
                name="qkv",
                after=(upstream_token,) if l == 0 and side == 0 else (),
            )
            qkv.append(qkv_half)
            first_x.append(x_half)
        if outer > 1:
            pairs = jnp.concatenate([part[:, feats:] for part in qkv], axis=0)
            pairs = lax.all_gather(
                pairs, "ctx", axis=0, tiled=True, axis_index_groups=outer_groups
            )
            key_parts = (pairs,)
        else:
            key_parts = tuple(qkv)
        attn = [None, None]
        for side in (1, 0):
            kept = (first_x[side], qkv[side]) + ((stream,) if side == 1 else ())
            attn[side] = kernel_call(
                functools.partial(
                    attn_kernel, feats, heads, len(attn_w[l]), len(key_parts), len(kept), tile
                ),
                [partial_out, saved((half, feats), bf16), saved((half, feats), f32)]
                + [saved(k.shape, k.dtype) for k in kept],
                qkv[side],
                *key_parts,
                *attn_w[l],
                usable,
                *kept,
                name="attn",
                limit=attn_limit,
                scratch=[
                    pltpu.VMEM((key_rows, feats), bf16),
                    pltpu.VMEM((key_rows, feats), bf16),
                    pltpu.VMEM((half, feats), bf16),
                    pltpu.VMEM((half, feats), f32),
                    DMA((len(kept) + 2,)),
                ],
            )
        sums = reduce_rows(attn[0][0], attn[1][0])
        middle, second = kernel_call(
            functools.partial(sum_norm_kernel, shift_row(l, 2), gain_row(l, 1), shift_row(l, 1)),
            [row_f32, row_bf16],
            *sums,
            Far(attn[1][5]),
            vecs,
            name="sum_norm",
            scratch=[pltpu.VMEM((rows, width), f32), DMA((1,))],
        )
        second_chunks = gather_rows(second)
        mlp = [None, None]
        for side in (1, 0):
            kept = (middle,) if side == 1 else ()
            mlp[side] = kernel_call(
                functools.partial(mlp_kernel, hidden, len(kept)),
                [
                    partial_out,
                    saved((half, width), bf16),
                    saved((half, hidden), bf16),
                    saved((2, half, hidden // 2), f32),
                ]
                + [saved(k.shape, k.dtype) for k in kept],
                *second_chunks[side],
                mlp_w[l],
                fc1_all[l],
                *kept,
                name="mlp",
                scratch=[
                    half_x,
                    pltpu.VMEM((half, hidden), bf16),
                    pltpu.VMEM((2, half, hidden // 2), f32),
                    DMA((4 + len(kept),)),
                ],
            )
        sums = reduce_rows(mlp[0][0], mlp[1][0])
        saved_all.append((attn, pairs if outer > 1 else None, mlp))
        if l + 1 < depth:
            stream, first = kernel_call(
                functools.partial(
                    sum_norm_kernel, shift_row(l, 3), gain_row(l + 1, 0), shift_row(l + 1, 0)
                ),
                [row_f32, row_bf16],
                *sums,
                Far(mlp[1][4]),
                vecs,
                name="sum_norm",
                scratch=[pltpu.VMEM((rows, width), f32), DMA((1,))],
            )
            first_chunks = gather_rows(first)
        else:
            outputs_own = kernel_call(
                functools.partial(sum_out_kernel, shift_row(l, 3)),
                [row_f32],
                *sums,
                middle,
                vecs,
                mask,
                name="sum_out",
            )[0]

    def both_halves(own):
        return kernel_call(
            place_rows_kernel,
            [saved(inputs.shape, f32)],
            own,
            swap_y(own),
            name="place_rows",
            scratch=[DMA((2,))],
        )[0]

    outputs = both_halves(outputs_own)

    def spread_grads(part):
        if outer > 1:
            part = lax.psum(part, "ctx", axis_index_groups=outer_groups)
        other = swap_x(part)
        return part, swap_core(part), other, swap_core(other)

    row_sums = [None] * depth
    unit_sums = [None] * depth
    head_sums = [None] * depth
    placed_mlp = None
    placed_attn = None
    mlp_token = ()
    for l in reversed(range(depth)):
        attn, pairs, mlp = saved_all[l]
        back = [None, None]
        for side in (1, 0):
            back[side] = kernel_call(
                functools.partial(mlp_back_kernel, hidden, len(upstream_chunks[side])),
                [partial_out, ((half, hidden), bf16), ((1, hidden), f32), ((half, width), bf16)],
                *upstream_chunks[side],
                mlp_w[l],
                Far(mlp[side][3]),
                name="mlp_back",
                scratch=[pltpu.VMEM((2, half, hidden // 2), f32), DMA((2,))],
            )
        sums = reduce_rows(back[0][0], back[1][0])
        mlp_grad, grad_token = kernel_call(
            functools.partial(mlp_grad_kernel, hidden),
            [((width, 2 * hidden), bf16), TOKEN],
            Far(mlp[0][1]),
            Far(mlp[1][1]),
            Far(mlp[0][2]),
            Far(mlp[1][2]),
            back[0][3],
            back[1][3],
            back[0][1],
            back[1][1],
            name="mlp_grad",
            after=(sums[0],),
            scratch=[
                pltpu.VMEM((all_rows, width), bf16),
                pltpu.VMEM((all_rows, hidden), bf16),
                pltpu.VMEM((all_rows, width), bf16),
                pltpu.VMEM((all_rows, hidden), bf16),
                DMA((4,)),
            ],
            limit=16,
            us=3,
        )
        mlp_part = lax.psum_scatter(mlp_grad, "fsdp", scatter_dimension=0, tiled=True)
        placed_mlp = place_call(
            functools.partial(place_mlp_kernel, l, hidden),
            spread_grads(mlp_part),
            placed_mlp,
            [w_fc1.shape, w_fc2.shape],
            [(GROUP, width_own, hidden), (GROUP, hidden, width_own)],
            "place_mlp",
        )
        unit_sums[l] = back[0][2] + back[1][2]
        grad_middle, middle_b, sums_two = kernel_call(
            functools.partial(norm_back_two_kernel, gain_row(l, 1)),
            [row_f32, row_bf16, ((4, width), f32)],
            *sums,
            Far(mlp[1][4]),
            upstream,
            vecs,
            name="norm_back_two",
            after=(grad_token,),
            scratch=[pltpu.VMEM((rows, width), f32), DMA((1,))],
        )
        middle_chunks = gather_rows(middle_b)
        grad_q = [None, None]
        middle_x = [None, None]
        carried = ()
        for side in (0, 1):
            key_parts = (pairs,) if outer > 1 else (attn[0][4], attn[1][4])
            middle_x[side], grad_q[side], *carried = kernel_call(
                functools.partial(
                    attn_back_kernel,
                    feats,
                    heads,
                    len(attn_w[l]),
                    len(key_parts),
                    tile,
                    len(carried) > 0,
                ),
                [
                    ((half, width), bf16),
                    ((half, feats), f32),
                    ((key_rows, feats), f32),
                    ((key_rows, feats), f32),
                ],
                *middle_chunks[side],
                *attn_w[l],
                usable,
                Far(attn[side][4]),
                Far(attn[side][1]),
                Far(attn[side][2]),
                *[Far(part) for part in key_parts],
                *carried,
                name="attn_back",
                scratch=[
                    pltpu.VMEM((key_rows, 2 * feats), bf16),
                    pltpu.VMEM((half, feats), bf16),
                    pltpu.VMEM((half, feats), bf16),
                    pltpu.VMEM((half, feats), f32),
                    pltpu.VMEM((half, feats), bf16),
                    DMA((3 + len(key_parts),)),
                ],
                limit=attn_limit,
            )
        grad_k, grad_v = carried
        if outer > 1:
            grad_k, grad_v = (
                lax.psum_scatter(
                    v, "ctx", scatter_dimension=0, tiled=True, axis_index_groups=outer_groups
                )
                for v in (grad_k, grad_v)
            )

        def project(side, after):
            return kernel_call(
                functools.partial(project_kernel, feats, side * half, len(attn_w[l])),
                [partial_out],
                grad_q[side],
                grad_k,
                grad_v,
                *attn_w[l],
                name="project",
                after=after,
                scratch=[pltpu.VMEM((half, 3 * feats), bf16)],
            )[0]

        def weight_grad(after):
            return kernel_call(
                functools.partial(attn_grad_kernel, feats),
                [((width, 4 * feats), bf16), ((2, feats), f32), TOKEN],
                Far(attn[0][3]),
                Far(attn[1][3]),
                Far(attn[0][1]),
                Far(attn[1][1]),
                *middle_x,
                *grad_q,
                grad_k,
                grad_v,
                name="attn_grad",
                after=after,
                scratch=[
                    pltpu.VMEM((all_rows, width), bf16),
                    pltpu.VMEM((all_rows, feats), bf16),
                    pltpu.VMEM((all_rows, width), bf16),
                    pltpu.VMEM((all_rows, 3 * feats), bf16),
                    DMA((4,)),
                ],
                us=3,
            )

        if l > 0:
            far_part = project(1, ())
            near_part = project(0, ())
            sums = reduce_rows(near_part, far_part)
            attn_grad, head_sums[l], grad_token = weight_grad((sums[0],))
            one_after = (grad_token,)
        else:
            attn_grad, head_sums[l], grad_token = weight_grad(mlp_token)
            far_part = project(1, (grad_token,))
            near_part = project(0, ())
            sums = reduce_rows(near_part, far_part)
            one_after = ()
        attn_part = lax.psum_scatter(attn_grad, "fsdp", scatter_dimension=0, tiled=True)
        placed_attn = place_call(
            functools.partial(place_attn_kernel, l, feats),
            spread_grads(attn_part),
            placed_attn,
            [w_qkv.shape, w_out.shape],
            [(GROUP, 3, width_own, feats), (GROUP, feats, width_own)],
            "place_attn",
        )
        mlp_token = (placed_mlp[2],)
        body = functools.partial(norm_back_one_kernel, gain_row(l, 0))
        if l > 0:
            masked = ()
            body = lambda *refs, body=body: body(*refs[:7], None, *refs[7:])
        else:
            masked = (mask,)
        upstream, upstream_b, sums_one = kernel_call(
            body,
            [row_f32, row_bf16, ((2, width), f32)],
            *sums,
            Far(attn[1][5]),
            grad_middle,
            vecs,
            *masked,
            name="norm_back_one",
            after=one_after,
            scratch=[pltpu.VMEM((rows, width), f32), DMA((1,))],
        )
        if l > 0:
            upstream_chunks = gather_rows(upstream_b)
        row_sums[l] = (sums_one, sums_two)

    grad_inputs = both_halves(upstream)

    vec_part = jnp.concatenate(
        [
            piece
            for l in range(depth)
            for piece in (
                row_sums[l][0][0:1],
                row_sums[l][1][0:1],
                row_sums[l][0][1:2],
                row_sums[l][1][1:4],
            )
        ],
        axis=0,
    )
    unit_part = jnp.concatenate(unit_sums, axis=0)
    head_part = jnp.concatenate(head_sums, axis=0)
    unit_lines = unit_part.reshape(-1, width)
    head_lines = head_part.reshape(1, -1)
    head_lines = jnp.pad(head_lines, ((0, 0), (0, width - head_lines.shape[1])))
    packed = jnp.concatenate([vec_part, unit_lines, head_lines], axis=0)
    if outer > 1:
        packed = lax.psum(packed, "ctx", axis_index_groups=outer_groups)
    step = 1
    while step < fsdp:
        packed = packed + lax.ppermute(packed, "fsdp", [(i, i ^ step) for i in range(fsdp)])
        step *= 2
    vec_sum = lax.dynamic_slice_in_dim(packed[:vec_rows], f * width_own, width_own, axis=1)
    rest = packed[vec_rows:]
    vec_sum = vec_sum + swap_y(vec_sum)
    rest_core = swap_core(rest)
    vec_sum = vec_sum + swap_core(vec_sum)
    rest_two = jnp.stack([rest, rest_core])
    vec_sum = vec_sum + swap_x(vec_sum)
    rest_four = jnp.concatenate([rest_two, swap_x(rest_two)], axis=0)
    vec_sum = vec_sum.reshape(depth, 6, width_own)
    unit_count = unit_lines.shape[0]

    def of_place(c):
        return lax.dynamic_index_in_dim(rest_four, ci ^ c, 0, keepdims=False)

    grad_fc1_bias = of_place(f)[:unit_count].reshape(depth, 1, hidden)
    grad_qv_bias = jnp.stack(
        [
            lax.dynamic_slice_in_dim(
                of_place(c)[unit_count, : head_part.size].reshape(depth, 2, heads, head_dim),
                f * head_own,
                head_own,
                axis=3,
            )
            for c in range(GROUP)
        ],
        axis=2,
    ).reshape(qv_bias.shape)
    return (
        outputs,
        grad_inputs,
        vec_sum[:, :2],
        vec_sum[:, 2:],
        grad_qv_bias,
        grad_fc1_bias,
        placed_attn[0],
        placed_attn[1],
        placed_mlp[0],
        placed_mlp[1],
    )


def solution(mesh):
    rows = P("fsdp", "ctx", None)
    params = (
        P(None, None, "fsdp"),
        P(None, None, "fsdp"),
        P(None, None, "tp", "fsdp"),
        P(None, "tp", "fsdp"),
        P(None, None, "fsdp", "tp"),
        P(None, "tp", "fsdp"),
        P(None, "fsdp", "tp"),
        P(None, "tp", "fsdp"),
    )
    return jax.shard_map(
        per_device,
        mesh=mesh,
        in_specs=(rows, P("fsdp", None), rows) + params,
        out_specs=(rows, rows) + params,
        check_vma=False,
    )
```

```python
import functools
import math

import jax
import jax.numpy as jnp
from jax import lax
from jax.experimental import pallas as pl
from jax.experimental.pallas import tpu as pltpu
from jax.sharding import PartitionSpec as P

NORM_EPSILON = 1e-06
MASK_FILL = -1e30
ROOT_HALF = 0.7071067811865476
INV_ROOT_TAU = 0.3989422804014327
GROUP = 4
ORDER = (0, 5, 4, 1, 2, 7, 6, 3)
CHIPS = 4

bf16 = jnp.bfloat16
f32 = jnp.float32
VMEM = pl.BlockSpec(memory_space=pltpu.VMEM)
SMEM = pl.BlockSpec(memory_space=pltpu.SMEM)
HBM = pl.BlockSpec(memory_space=pltpu.HBM)
DMA = pltpu.SemaphoreType.DMA
TOKEN = ((8, 128), f32)


def dot(a, b):
    return lax.dot_general(a, b, (((1,), (0,)), ((), ())), preferred_element_type=f32)


def dot_nt(a, b):
    return lax.dot_general(a, b, (((1,), (1,)), ((), ())), preferred_element_type=f32)


def dot_tn(a, b):
    return lax.dot_general(a, b, (((0,), (0,)), ((), ())), preferred_element_type=f32)


class Far:
    def __init__(self, value):
        self.value = value


class Scalars:
    def __init__(self, value):
        self.value = value


def saved(shape, dtype):
    return pltpu.HBM(shape, dtype)


def kernel_call(body, outs, *args, name, limit=12, scratch=(), after=(), aliases=None, us=0):
    values, specs = [], []
    for arg in (*args, *after):
        if isinstance(arg, Far):
            values.append(pltpu.with_memory_space_constraint(arg.value, pltpu.HBM))
            specs.append(HBM)
        elif isinstance(arg, Scalars):
            values.append(arg.value)
            specs.append(SMEM)
        else:
            values.append(arg)
            specs.append(VMEM)
    first, last = len(args), len(args) + len(after)

    def run(*refs):
        body(*refs[:first], *refs[last:])

    out_shape, out_specs = [], []
    for out in outs:
        if isinstance(out, tuple):
            out_shape.append(jax.ShapeDtypeStruct(*out))
            out_specs.append(VMEM)
        else:
            out_shape.append(out)
            out_specs.append(HBM)
    return pl.pallas_call(
        run,
        out_shape=out_shape,
        in_specs=specs,
        out_specs=out_specs,
        scratch_shapes=list(scratch),
        input_output_aliases=aliases or {},
        compiler_params=pltpu.CompilerParams(vmem_limit_bytes=limit << 20),
        cost_estimate=pl.CostEstimate(flops=us * 10**9, bytes_accessed=0, transcendentals=0),
        name=name,
    )(*values)


def start_copies(pairs, sems):
    copies = [
        pltpu.make_async_copy(source, target, sems.at[k])
        for k, (source, target) in enumerate(pairs)
    ]
    for copy in copies:
        copy.start()
    return copies


def row_mean(value):
    return jnp.mean(value, axis=-1, keepdims=True)


def normalize(values):
    center = values - row_mean(values)
    inverse = lax.rsqrt(row_mean(center * center) + NORM_EPSILON)
    return center * inverse, inverse


def lanes_of(head, head_dim, width):
    lane = lax.broadcasted_iota(jnp.int32, (1, width), 1)
    return (lane >= head * head_dim) & (lane < (head + 1) * head_dim)


def assemble(chunks, target):
    rows = chunks[0].shape[0]
    for k, chunk in enumerate(chunks):
        target[k * rows : (k + 1) * rows, :] = chunk[...]


def only(flag, value):
    return jnp.where(flag, value, jnp.zeros_like(value))


def shards(weights):
    if len(weights) == 1:
        rows = weights[0].shape[0]
        return [(pl.ds(0, rows), weights[0])]
    count = len(weights)
    rows = weights[0].shape[0]
    f = lax.axis_index("fsdp")
    found = []
    for d, ref in enumerate(weights):
        place = lax.rem(f + (count - d), count)
        found.append((pl.ds(pl.multiple_of(place * rows, rows), rows), ref))
    return found


def pack_attn_kernel(layer, feats, qkv_hbm, out_hbm, packed_ref, token, qkv, out, sems):
    ci = lax.rem(lax.axis_index("ctx"), GROUP)
    span = pl.ds(pl.multiple_of(ci * feats, feats), feats)
    copies = start_copies(
        [(qkv_hbm.at[layer, :, :, span], qkv), (out_hbm.at[layer, span, :], out)], sems
    )
    copies[0].wait()
    for k in range(3):
        packed_ref[:, k * feats : (k + 1) * feats] = qkv[k]
    copies[1].wait()
    packed_ref[:, 3 * feats :] = out[...].T
    token[...] = jnp.zeros_like(token)


def pack_mlp_kernel(layer, hidden, fc1_hbm, fc2_hbm, packed_ref, token, fc1, fc2, sems):
    ci = lax.rem(lax.axis_index("ctx"), GROUP)
    span = pl.ds(pl.multiple_of(ci * hidden, hidden), hidden)
    copies = start_copies(
        [(fc1_hbm.at[layer, :, span], fc1), (fc2_hbm.at[layer, span, :], fc2)], sems
    )
    copies[0].wait()
    packed_ref[:, :hidden] = fc1[...]
    copies[1].wait()
    packed_ref[:, hidden:] = fc2[...].T
    token[...] = jnp.zeros_like(token)


def prep_upstream_kernel(tp, outer, lengths, cotangent_hbm,
                         upstream_ref, upstream_b_ref, usable_ref, mask_ref, rows_in, sems):
    rows = rows_in.shape[0]
    c = lax.axis_index("ctx")
    t = lax.axis_index("tp")
    place = lax.rem(c, GROUP) * tp + t
    start = pl.multiple_of(t * rows, rows)
    copies = start_copies([(cotangent_hbm.at[0, pl.ds(start, rows), :], rows_in)], sems)
    lane = lax.broadcasted_iota(jnp.int32, usable_ref.shape, 1)
    limit = jnp.zeros(usable_ref.shape, jnp.int32)
    for o in range(outer):
        for k, d in enumerate(ORDER):
            source = place ^ d
            first_lane = (o * len(ORDER) + k) * rows
            count = lengths[0, o * GROUP + lax.div(source, tp)] - lax.rem(source, tp) * rows
            limit = jnp.where(lane >= first_lane, first_lane + jnp.clip(count, 0, rows), limit)
    usable_ref[...] = jnp.where(lane < limit, 1.0, 0.0)
    row = lax.broadcasted_iota(jnp.int32, mask_ref.shape, 0)
    mask = jnp.where(row + start < lengths[0, c], 1.0, 0.0)
    mask_ref[...] = mask
    copies[0].wait()
    upstream = rows_in[...] * mask[:, 0:1]
    upstream_ref[...] = upstream
    upstream_b_ref[...] = upstream.astype(bf16)


def prep_first_kernel(depth, inputs_hbm, vecs, stream_ref, first_ref, sems):
    rows = stream_ref.shape[0]
    start = pl.multiple_of(lax.axis_index("tp") * rows, rows)
    copies = start_copies([(inputs_hbm.at[0, pl.ds(start, rows), :], stream_ref)], sems)
    copies[0].wait()
    normed, _ = normalize(stream_ref[...])
    shift = vecs[2 * depth : 2 * depth + 1, :]
    first_ref[...] = (normed * vecs[0:1, :] + shift).astype(bf16)


def keep_rows_kernel(*refs):
    chunks, (near_hbm, far_hbm, token, near, far, sems) = refs[:8], refs[8:]
    assemble(chunks[:4], near)
    assemble(chunks[4:], far)
    for copy in start_copies([(near, near_hbm), (far, far_hbm)], sems):
        copy.wait()
    token[...] = jnp.zeros_like(token)


def qkv_kernel(feats, weight_count, *refs):
    c0, c1, c2, c3, *rest = refs
    weights = rest[:weight_count]
    bias, qkv_ref, x = rest[weight_count:]
    assemble((c0, c1, c2, c3), x)
    qkv = sum(dot(x[:, span], w[:, : 3 * feats]) for span, w in shards(weights))
    qkv_ref[:, :feats] = (qkv[:, :feats] + bias[0:1, :]).astype(bf16)
    qkv_ref[:, feats : 2 * feats] = qkv[:, feats : 2 * feats].astype(bf16)
    qkv_ref[:, 2 * feats :] = (qkv[:, 2 * feats :] + bias[1:2, :]).astype(bf16)


def attn_kernel(feats, heads, weight_count, part_count, keep_count, tile, *refs):
    q_ref, *rest = refs
    parts = rest[:part_count]
    weights = rest[part_count : part_count + weight_count]
    rest = rest[part_count + weight_count :]
    usable, *rest = rest
    kept, rest = rest[:keep_count], rest[keep_count:]
    partial_ref, attended_hbm, norm_hbm, *rest = rest
    kept_hbm, rest = rest[:keep_count], rest[keep_count:]
    keys, values, attended_ref, norm_ref, sems = rest
    head_dim = feats // heads
    scale = 1.0 / math.sqrt(head_dim)
    copies = start_copies(list(zip(kept, kept_hbm)), sems)
    first = 0
    for part in parts:
        rows, width = part.shape
        keys[first : first + rows, :] = part[:, width - 2 * feats : width - feats]
        values[first : first + rows, :] = part[:, width - feats :]
        first += rows
    keep = usable[...] > 0.5
    rows = q_ref.shape[0]
    for first in range(0, rows, tile):
        span = slice(first, first + tile)
        q = q_ref[span, :feats]
        attended = None
        for h in range(heads):
            own = lanes_of(h, head_dim, feats)
            scores = dot_nt(only(own, q), keys[...]) * scale
            scores = jnp.where(keep, scores, MASK_FILL)
            highest = jnp.max(scores, axis=-1, keepdims=True)
            raised = jnp.exp(scores - highest)
            total = jnp.sum(raised, axis=-1, keepdims=True)
            soft = (raised * (1.0 / total)).astype(bf16)
            result = dot(soft, values[...])
            log_norm = jnp.broadcast_to(highest + jnp.log(total), (tile, feats))
            if attended is None:
                attended, norms = result, log_norm
            else:
                attended = jnp.where(own, result, attended)
                norms = jnp.where(own, log_norm, norms)
        attended_ref[span, :] = attended.astype(bf16)
        norm_ref[span, :] = norms
    copies += start_copies(
        [(attended_ref, attended_hbm), (norm_ref, norm_hbm)],
        sems.at[pl.ds(keep_count, 2)],
    )
    for span, w in shards(weights):
        partial_ref[:, span] = dot_nt(attended_ref[...], w[:, 3 * feats :]).astype(bf16)
    for copy in copies:
        copy.wait()


def touch_kernel(source, token):
    token[...] = jnp.zeros_like(token)


def vector_sum_kernel(*refs):
    *terms, out_ref, token = refs
    total = terms[0][...]
    for term in terms[1:]:
        total = total + term[...]
    out_ref[...] = total
    token[...] = jnp.zeros_like(token)


def copy_kernel(source, target):
    target[...] = source[...]


def core_sum_kernel(count, *refs):
    pairs, owns = refs[: 2 * count], refs[2 * count : 3 * count]
    peers = refs[3 * count :]
    rows = owns[0].shape[0]
    for j in range(count):
        near, far = pairs[2 * j], pairs[2 * j + 1]
        for k in range(1 + len(peers)):
            span = slice(k * rows, (k + 1) * rows)
            total = near[span, :].astype(f32) + far[span, :].astype(f32)
            if k == 0:
                owns[j][...] = total
            else:
                peers[k - 1][j * rows : (j + 1) * rows, :] = total.astype(bf16)


def total_of(own, xy, x, y, part=0):
    rows = own.shape[0]
    span = slice(part * rows, (part + 1) * rows)
    return (
        own[...] + y[span, :].astype(f32) + x[span, :].astype(f32) + xy[span, :].astype(f32)
    )


def sum_norm_kernel(bias_row, gain_row, shift_row, own, xy, x, y, residual_hbm, vecs,
                    stream_ref, normed_ref, residual, sems):
    copies = start_copies([(residual_hbm, residual)], sems)
    total = total_of(own, xy, x, y) + vecs[bias_row : bias_row + 1, :]
    copies[0].wait()
    stream = residual[...] + total
    stream_ref[...] = stream
    normed, _ = normalize(stream)
    gain = vecs[gain_row : gain_row + 1, :]
    normed_ref[...] = (normed * gain + vecs[shift_row : shift_row + 1, :]).astype(bf16)


def sum_out_kernel(bias_row, own, xy, x, y, residual_hbm, vecs, mask, out_ref, residual, sems):
    copies = start_copies([(residual_hbm, residual)], sems)
    total = total_of(own, xy, x, y, 1) + vecs[bias_row : bias_row + 1, :]
    copies[0].wait()
    out_ref[...] = (residual[...] + total) * mask[:, 0:1]


def mlp_kernel(hidden, keep_count, saves, c0, c1, c2, c3, w, bias, *refs):
    kept, rest = refs[:keep_count], refs[keep_count:]
    partial_ref, x_out, act_out, slope_out, *rest = rest
    kept_hbm, rest = rest[:keep_count], rest[keep_count:]
    if saves:
        x, act_ref, slope_ref, sems = rest
    else:
        x, act_ref, slope_ref = x_out, act_out, slope_out
        (sems,) = rest
    copies = start_copies(list(zip(kept, kept_hbm)), sems)
    assemble((c0, c1, c2, c3), x)
    if saves:
        copies += start_copies([(x, x_out)], sems.at[pl.ds(keep_count, 1)])
    block = hidden // 2
    for k in range(2):
        span = slice(k * block, (k + 1) * block)
        pre = dot(x[...], w[:, span]) + bias[:, span]
        cdf = 0.5 * (1.0 + lax.erf(pre * ROOT_HALF))
        density = jnp.exp(-0.5 * pre * pre) * INV_ROOT_TAU
        slope_ref[k] = cdf + pre * density
        act_ref[:, span] = (pre * cdf).astype(bf16)
        if saves:
            copies += start_copies(
                [(slope_ref.at[k], slope_out.at[k])], sems.at[pl.ds(1 + keep_count + k, 1)]
            )
    if saves:
        copies += start_copies([(act_ref, act_out)], sems.at[pl.ds(3 + keep_count, 1)])
    partial_ref[...] = dot_nt(act_ref[...], w[:, hidden:]).astype(bf16)
    for copy in copies:
        copy.wait()


def mlp_back_kernel(hidden, chunk_count, *refs):
    chunks, (w, slope_hbm, *rest) = refs[:chunk_count], refs[chunk_count:]
    partial_ref, grad_ref, sum_ref, x, slope, sems = rest
    copies = start_copies([(slope_hbm, slope)], sems)
    if chunk_count == 1:
        copies += start_copies([(chunks[0], x)], sems.at[pl.ds(1, 1)])
        copies[1].wait()
    else:
        assemble(chunks, x)
    grad = dot(x[...], w[:, hidden:])
    copies[0].wait()
    block = hidden // 2
    for k in range(2):
        span = slice(k * block, (k + 1) * block)
        part = grad[:, span] * slope[k]
        grad_ref[:, span] = part.astype(bf16)
        sum_ref[:, span] = jnp.sum(part, axis=0, keepdims=True)
    partial_ref[...] = dot_nt(grad_ref[...], w[:, :hidden]).astype(bf16)


def mlp_grad_kernel(hidden, second_near, second_far, act_near, act_far, up_near, up_far,
                    grad_near, grad_far, out_ref, token, second, act, up, grad, sems):
    rows = up_near.shape[0]
    near, far = pl.ds(0, rows), pl.ds(rows, rows)
    copies = start_copies(
        [
            (second_near, second.at[near]),
            (second_far, second.at[far]),
            (act_near, act.at[near]),
            (act_far, act.at[far]),
        ],
        sems,
    )
    up[:rows, :] = up_near[...]
    up[rows:, :] = up_far[...]
    grad[:rows, :] = grad_near[...]
    grad[rows:, :] = grad_far[...]
    for copy in copies:
        copy.wait()
    out_ref[:, hidden:] = dot_tn(up[...], act[...]).astype(bf16)
    out_ref[:, :hidden] = dot_tn(second[...], grad[...]).astype(bf16)
    token[...] = jnp.zeros_like(token)


def norm_back(upstream, values, gain):
    normed, inverse = normalize(values)
    scaled = upstream * gain
    back = inverse * (scaled - row_mean(scaled) - normed * row_mean(scaled * normed))
    gain_grad = jnp.sum(upstream * normed, axis=0, keepdims=True)
    return back, gain_grad, jnp.sum(upstream, axis=0, keepdims=True)


def norm_back_two_kernel(gain_row, own, xy, x, y, values_hbm, upstream, vecs,
                         grad_ref, grad_b_ref, sums_ref, values, sems):
    copies = start_copies([(values_hbm, values)], sems)
    up = upstream[...]
    total = total_of(own, xy, x, y)
    copies[0].wait()
    back, gain_grad, shift_grad = norm_back(
        total, values[...], vecs[gain_row : gain_row + 1, :]
    )
    grad = up + back
    grad_ref[...] = grad
    grad_b_ref[...] = grad.astype(bf16)
    sums_ref[0:1, :] = gain_grad
    sums_ref[1:2, :] = shift_grad
    sums_ref[2:3, :] = jnp.sum(grad, axis=0, keepdims=True)
    sums_ref[3:4, :] = jnp.sum(up, axis=0, keepdims=True)


def norm_back_one_kernel(gain_row, own, xy, x, y, values_hbm, upstream, vecs, mask,
                         grad_ref, grad_b_ref, sums_ref, values, sems):
    copies = start_copies([(values_hbm, values)], sems)
    total = total_of(own, xy, x, y)
    copies[0].wait()
    back, gain_grad, shift_grad = norm_back(
        total, values[...], vecs[gain_row : gain_row + 1, :]
    )
    grad = upstream[...] + back
    if mask is not None:
        grad = grad * mask[:, 0:1]
    grad_ref[...] = grad
    grad_b_ref[...] = grad.astype(bf16)
    sums_ref[0:1, :] = gain_grad
    sums_ref[1:2, :] = shift_grad


def attn_back_kernel(feats, heads, weight_count, part_count, tile, carried, *refs):
    c0, c1, c2, c3, *rest = refs
    weights, rest = rest[:weight_count], rest[weight_count:]
    usable, q_hbm, attended_hbm, norm_hbm, *rest = rest
    parts, rest = rest[:part_count], rest[part_count:]
    if carried:
        keys_before, values_before, *rest = rest
    x, grad_q, grad_k, grad_v, pairs, q_ref, attended, norms, grad_att, sems = rest
    head_dim = feats // heads
    scale = 1.0 / math.sqrt(head_dim)
    moves = [(q_hbm.at[:, pl.ds(0, feats)], q_ref), (attended_hbm, attended), (norm_hbm, norms)]
    first = 0
    for part in parts:
        rows, width = part.shape
        moves.append(
            (part.at[:, pl.ds(width - 2 * feats, 2 * feats)], pairs.at[pl.ds(first, rows)])
        )
        first += rows
    copies = start_copies(moves, sems)
    assemble((c0, c1, c2, c3), x)
    grad_att[...] = sum(
        dot(x[:, span], w[:, 3 * feats :]) for span, w in shards(weights)
    ).astype(bf16)
    keep = usable[...] > 0.5
    rows = q_ref.shape[0]
    if carried:
        sum_k, sum_v = keys_before[...], values_before[...]
    else:
        sum_k = jnp.zeros(grad_k.shape, f32)
        sum_v = jnp.zeros(grad_v.shape, f32)
    for copy in copies:
        copy.wait()
    keys, values = pairs[:, :feats], pairs[:, feats:]
    for first in range(0, rows, tile):
        span = slice(first, first + tile)
        q = q_ref[span, :]
        ga = grad_att[span, :]
        products = ga.astype(f32) * attended[span, :].astype(f32)
        gq = None
        for h in range(heads):
            own = lanes_of(h, head_dim, feats)
            q_h = only(own, q)
            ga_h = only(own, ga)
            row_dots = jnp.sum(only(own, products), axis=-1, keepdims=True)
            scores = dot_nt(q_h, keys) * scale
            scores = jnp.where(keep, scores, MASK_FILL)
            soft = jnp.exp(scores - norms[span, h * head_dim : h * head_dim + 1])
            grad_soft = dot_nt(ga_h, values)
            grad_scores = (soft * (grad_soft - row_dots)).astype(bf16)
            part = dot(grad_scores, keys)
            gq = part if gq is None else jnp.where(own, part, gq)
            sum_k = sum_k + dot_tn(grad_scores, q_h) * scale
            sum_v = sum_v + dot_tn(soft.astype(bf16), ga_h)
        grad_q[span, :] = gq * scale
    grad_k[...] = sum_k
    grad_v[...] = sum_v


def project_kernel(feats, first, weight_count, gq, gk, gv, *refs):
    weights, (partial_ref, packed) = refs[:weight_count], refs[weight_count:]
    rows = gq.shape[0]
    span = slice(first, first + rows)
    packed[:, :feats] = gq[...].astype(bf16)
    packed[:, feats : 2 * feats] = gk[span, :].astype(bf16)
    packed[:, 2 * feats :] = gv[span, :].astype(bf16)
    for columns, w in shards(weights):
        partial_ref[:, columns] = dot_nt(packed[...], w[:, : 3 * feats]).astype(bf16)


def attn_grad_kernel(feats, first_near, first_far, att_near, att_far, up_near, up_far,
                     gq_near, gq_far, gk, gv, *refs):
    *outs, sums_ref, token, first, att, up, packed, sems = refs
    rows = up_near.shape[0]
    near, far = pl.ds(0, rows), pl.ds(rows, rows)
    copies = start_copies(
        [
            (first_near, first.at[near]),
            (first_far, first.at[far]),
            (att_near, att.at[near]),
            (att_far, att.at[far]),
        ],
        sems,
    )
    up[:rows, :] = up_near[...]
    up[rows:, :] = up_far[...]
    packed[:rows, :feats] = gq_near[...].astype(bf16)
    packed[rows:, :feats] = gq_far[...].astype(bf16)
    packed[:, feats : 2 * feats] = gk[...].astype(bf16)
    packed[:, 2 * feats :] = gv[...].astype(bf16)
    sums_ref[0:1, :] = jnp.sum(gq_near[...], axis=0, keepdims=True) + jnp.sum(
        gq_far[...], axis=0, keepdims=True
    )
    sums_ref[1:2, :] = jnp.sum(gv[...], axis=0, keepdims=True)
    for copy in copies:
        copy.wait()
    width_own = outs[0].shape[0]
    for d, out_ref in enumerate(outs):
        place = lax.rem(lax.axis_index("fsdp") + d, len(outs)) if len(outs) > 1 else 0
        span = pl.ds(place * width_own, width_own)
        if len(outs) > 1:
            span = pl.ds(pl.multiple_of(place * width_own, width_own), width_own)
        out_ref[:, : 3 * feats] = dot_tn(first[:, span], packed[...]).astype(bf16)
        out_ref[:, 3 * feats :] = dot_tn(up[:, span], att[...]).astype(bf16)
    token[...] = jnp.zeros_like(token)


def shard_sum_kernel(*refs):
    *terms, out_ref = refs
    out_ref[...] = sum(term[...].astype(f32) for term in terms).astype(out_ref.dtype)


def place_mlp_kernel(layer, hidden, p0, p1, p2, p3, *refs):
    fc1_hbm, fc2_hbm, token, fc1, fc2, sems = refs[-6:]
    ci = lax.rem(lax.axis_index("ctx"), GROUP)
    copies = []
    for k, piece in enumerate((p0, p1, p2, p3)):
        span = pl.ds(pl.multiple_of((ci ^ k) * hidden, hidden), hidden)
        fc1[k] = piece[:, :hidden].astype(f32)
        copies += start_copies(
            [(fc1.at[k], fc1_hbm.at[layer, :, span])], sems.at[pl.ds(2 * k, 1)]
        )
        fc2[k] = piece[:, hidden:].astype(f32).T
        copies += start_copies(
            [(fc2.at[k], fc2_hbm.at[layer, span, :])], sems.at[pl.ds(2 * k + 1, 1)]
        )
    token[...] = jnp.zeros_like(token)
    for copy in copies:
        copy.wait()


def place_attn_kernel(layer, feats, p0, p1, p2, p3, *refs):
    qkv_hbm, out_hbm, token, qkv, out, sems = refs[-6:]
    ci = lax.rem(lax.axis_index("ctx"), GROUP)
    copies = []
    for k, piece in enumerate((p0, p1, p2, p3)):
        span = pl.ds(pl.multiple_of((ci ^ k) * feats, feats), feats)
        for j in range(3):
            qkv[k, j] = piece[:, j * feats : (j + 1) * feats].astype(f32)
        copies += start_copies(
            [(qkv.at[k], qkv_hbm.at[layer, :, :, span])], sems.at[pl.ds(2 * k, 1)]
        )
        out[k] = piece[:, 3 * feats :].astype(f32).T
        copies += start_copies(
            [(out.at[k], out_hbm.at[layer, span, :])], sems.at[pl.ds(2 * k + 1, 1)]
        )
    token[...] = jnp.zeros_like(token)
    for copy in copies:
        copy.wait()


def place_call(body, pieces, before, outs, scratch, name):
    extra = () if before is None else (Far(before[0]), Far(before[1]))
    return kernel_call(
        body,
        [saved(s, f32) for s in outs] + [TOKEN],
        *pieces,
        *extra,
        name=name,
        scratch=[pltpu.VMEM(s, f32) for s in scratch] + [DMA((8,))],
        aliases={} if before is None else {4: 0, 5: 1},
    )


def place_rows_kernel(own, other, out_hbm, sems):
    rows = own.shape[0]
    start = pl.multiple_of(lax.axis_index("tp") * rows, rows)
    copies = start_copies(
        [
            (own, out_hbm.at[0, pl.ds(start, rows), :]),
            (other, out_hbm.at[0, pl.ds(pl.multiple_of(rows - start, rows), rows), :]),
        ],
        sems,
    )
    for copy in copies:
        copy.wait()


def per_device(
    inputs, lengths, cotangent, norm_gains, shifts, qv_bias, fc1_bias, w_qkv, w_out, w_fc1, w_fc2
):
    depth = w_qkv.shape[0]
    width_own = w_qkv.shape[2]
    fsdp = lax.axis_size("fsdp")
    tp = lax.axis_size("tp")
    ctx = lax.axis_size("ctx")
    outer = ctx // GROUP
    rows = inputs.shape[1] // tp
    half = rows * CHIPS
    all_rows = 2 * half
    head_own = qv_bias.shape[3]
    head_dim = head_own * fsdp
    heads = qv_bias.shape[2] // GROUP
    feats = heads * head_dim
    hidden = w_fc1.shape[2] // GROUP
    width = width_own * fsdp
    t = lax.axis_index("tp")
    f = lax.axis_index("fsdp")
    ci = lax.axis_index("ctx") % GROUP
    tile = half // 2
    attn_limit = 12 if outer == 1 else 48

    def swap_core(value):
        return lax.ppermute(value, "ctx", [(i, i ^ 1) for i in range(ctx)])

    def swap_x(value):
        return lax.ppermute(value, "ctx", [(i, i ^ 2) for i in range(ctx)])

    def swap_y(value):
        return lax.ppermute(value, "tp", [(i, i ^ 1) for i in range(tp)])

    def swap_xy(value):
        pairs = [
            (i * tp + k, (i ^ 2) * tp + (k ^ 1)) for i in range(ctx) for k in range(tp)
        ]
        return lax.ppermute(value, ("ctx", "tp"), pairs)

    def shift_z(value, d):
        return lax.ppermute(value, "fsdp", [(i, (i + d) % fsdp) for i in range(fsdp)])

    outer_groups = [[o * GROUP + i for o in range(outer)] for i in range(GROUP)]

    def gather_rows(own):
        near = (own, swap_xy(own), swap_x(own), swap_y(own))
        return near, tuple(swap_core(chunk) for chunk in near)

    def gate(value, after):
        return kernel_call(
            copy_kernel, [(value.shape, value.dtype)], value, name="gate", after=after
        )[0]

    def touch(value):
        return kernel_call(touch_kernel, [TOKEN], value, name="touch")[0]

    def reduce_rows(*pairs, after=()):
        count = len(pairs)
        *owns, xy, x, y = kernel_call(
            functools.partial(core_sum_kernel, count),
            [((rows, width), f32)] * count + [((count * rows, width), bf16)] * 3,
            *[v for near, far in pairs for v in (near, swap_core(far))],
            name="core_sum",
            after=after,
        )
        peers = (swap_xy(xy), swap_x(x), swap_y(y))
        return [(own, *peers) for own in owns]

    def pack_attn(l, after):
        return kernel_call(
            functools.partial(pack_attn_kernel, l, feats),
            [((width_own, 4 * feats), bf16), TOKEN],
            Far(w_qkv),
            Far(w_out),
            name="pack_attn",
            after=after,
            scratch=[
                pltpu.VMEM((3, width_own, feats), bf16),
                pltpu.VMEM((feats, width_own), bf16),
                DMA((2,)),
            ],
        )

    def pack_mlp(l, after):
        return kernel_call(
            functools.partial(pack_mlp_kernel, l, hidden),
            [((width_own, 2 * hidden), bf16), TOKEN],
            Far(w_fc1),
            Far(w_fc2),
            name="pack_mlp",
            after=after,
            scratch=[
                pltpu.VMEM((width_own, hidden), bf16),
                pltpu.VMEM((hidden, width_own), bf16),
                DMA((2,)),
            ],
        )

    attn_w = []
    mlp_w = []
    token = None
    for l in range(depth):
        own, token = pack_attn(l, () if token is None else (token,))
        attn_w.append((lax.all_gather(own, "fsdp", axis=0, tiled=True),))
        own, token = pack_mlp(l, (token,))
        mlp_w.append(lax.all_gather(own, "fsdp", axis=0, tiled=True))
        if l == 0:
            pack_token = token

    qv_own = lax.dynamic_slice_in_dim(qv_bias, ci * heads, heads, axis=2)
    vec_rows = depth * 6
    c1_rows = depth * fc1_bias.shape[2] // width_own
    qv_own = qv_own.reshape(1, -1)
    small_own = jnp.concatenate(
        [
            norm_gains.reshape(-1, width_own),
            shifts.reshape(-1, width_own),
            fc1_bias.reshape(-1, width_own),
            jnp.pad(qv_own, ((0, 0), (0, width_own - qv_own.shape[1]))),
        ],
        axis=0,
    )
    shifted = [small_own] + [shift_z(small_own, d) for d in range(1, fsdp)]

    def shard(a):
        picked = shifted[0]
        for d in range(1, fsdp):
            picked = jnp.where((f - d) % fsdp == a, shifted[d], picked)
        return picked.astype(f32)

    small = [shard(a) for a in range(fsdp)]
    vecs = jnp.concatenate([s[:vec_rows] for s in small], axis=1)
    fc1_all = shard(ci)[vec_rows : vec_rows + c1_rows].reshape(depth, 1, hidden)
    qv_all = jnp.stack(
        [s[vec_rows + c1_rows, : qv_own.shape[1]].reshape(depth, 2, heads, head_own) for s in small],
        axis=3,
    ).reshape(depth, 2, feats)

    def gain_row(l, i):
        return 2 * l + i

    def shift_row(l, i):
        return 2 * depth + 4 * l + i

    key_rows = outer * all_rows
    row_f32 = ((rows, width), f32)
    row_bf16 = ((rows, width), bf16)
    upstream, upstream_b, usable, mask = kernel_call(
        functools.partial(prep_upstream_kernel, tp, outer),
        [row_f32, row_bf16, ((1, key_rows), f32), ((rows, 128), f32)],
        Scalars(lengths),
        Far(cotangent),
        name="prep_upstream",
        after=(pack_token,),
        scratch=[pltpu.VMEM((rows, width), f32), DMA((1,))],
    )
    near, far = gather_rows(upstream_b)
    half_x = pltpu.VMEM((half, width), bf16)
    *upstream_rows, upstream_token = kernel_call(
        keep_rows_kernel,
        [saved((half, width), bf16)] * 2 + [TOKEN],
        *near,
        *far,
        name="keep_rows",
        scratch=[half_x, half_x, DMA((2,))],
    )
    upstream_chunks = [(Far(x),) for x in upstream_rows]
    stream, first = kernel_call(
        functools.partial(prep_first_kernel, depth),
        [row_f32, row_bf16],
        Far(inputs),
        vecs,
        name="prep_first",
        scratch=[DMA((1,))],
    )
    first_chunks = gather_rows(first)

    partial_out = ((half, width), bf16)
    saved_all = []
    for l in range(depth):
        qkv = []
        first_x = []
        for side in (0, 1):
            qkv_half, x_half = kernel_call(
                functools.partial(qkv_kernel, feats, len(attn_w[l])),
                [((half, 3 * feats), bf16), ((half, width), bf16)],
                *first_chunks[side],
                *attn_w[l],
                qv_all[l],
                name="qkv",
                after=(upstream_token,) if l == 0 and side == 0 else (),
            )
            qkv.append(qkv_half)
            first_x.append(x_half)
        if outer > 1:
            pairs = jnp.concatenate([part[:, feats:] for part in qkv], axis=0)
            pairs = lax.all_gather(
                pairs, "ctx", axis=0, tiled=True, axis_index_groups=outer_groups
            )
            key_parts = (pairs,)
        else:
            key_parts = tuple(qkv)
        attn = [None, None]
        for side in (1, 0):
            kept = (first_x[side], qkv[side]) + ((stream,) if side == 1 else ())
            attn[side] = kernel_call(
                functools.partial(
                    attn_kernel, feats, heads, len(attn_w[l]), len(key_parts), len(kept), tile
                ),
                [partial_out, saved((half, feats), bf16), saved((half, feats), f32)]
                + [saved(k.shape, k.dtype) for k in kept],
                qkv[side],
                *key_parts,
                *attn_w[l],
                usable,
                *kept,
                name="attn",
                limit=attn_limit,
                scratch=[
                    pltpu.VMEM((key_rows, feats), bf16),
                    pltpu.VMEM((key_rows, feats), bf16),
                    pltpu.VMEM((half, feats), bf16),
                    pltpu.VMEM((half, feats), f32),
                    DMA((len(kept) + 2,)),
                ],
            )
        (sums,) = reduce_rows((attn[0][0], attn[1][0]))
        middle, second = kernel_call(
            functools.partial(sum_norm_kernel, shift_row(l, 2), gain_row(l, 1), shift_row(l, 1)),
            [row_f32, row_bf16],
            *sums,
            Far(attn[1][5]),
            vecs,
            name="sum_norm",
            scratch=[pltpu.VMEM((rows, width), f32), DMA((1,))],
        )
        second_chunks = gather_rows(second)
        mlp = [None, None]
        for side in (1, 0):
            kept = (middle,) if side == 1 else ()
            saves = l + 1 < depth
            shapes = [
                ((half, width), bf16),
                ((half, hidden), bf16),
                ((2, half, hidden // 2), f32),
            ]
            mlp[side] = kernel_call(
                functools.partial(mlp_kernel, hidden, len(kept), saves),
                [partial_out]
                + [saved(*shape) if saves else shape for shape in shapes]
                + [saved(k.shape, k.dtype) for k in kept],
                *second_chunks[side],
                mlp_w[l],
                fc1_all[l],
                *kept,
                name="mlp",
                scratch=[pltpu.VMEM(*shape) for shape in shapes if saves]
                + [DMA((4 + len(kept),))],
            )
            if saves:
                mlp[side] = [mlp[side][0], *[Far(v) for v in mlp[side][1:4]], *mlp[side][4:]]
        saved_all.append((attn, pairs if outer > 1 else None, mlp))
        if l + 1 < depth:
            (sums,) = reduce_rows((mlp[0][0], mlp[1][0]))
            stream, first = kernel_call(
                functools.partial(
                    sum_norm_kernel, shift_row(l, 3), gain_row(l + 1, 0), shift_row(l + 1, 0)
                ),
                [row_f32, row_bf16],
                *sums,
                Far(mlp[1][4]),
                vecs,
                name="sum_norm",
                scratch=[pltpu.VMEM((rows, width), f32), DMA((1,))],
            )
            first_chunks = gather_rows(first)

    def scatter_grads(grad):
        part = lax.psum_scatter(grad, "fsdp", scatter_dimension=0, tiled=True)
        if outer > 1:
            part = lax.psum(part, "ctx", axis_index_groups=outer_groups)
        return part

    row_sums = [None] * depth
    unit_sums = [None] * depth
    head_sums = [None] * depth
    mlp_parts = [None] * depth
    attn_parts = [None] * depth
    for l in reversed(range(depth)):
        attn, pairs, mlp = saved_all[l]
        back = [None, None]
        for side in (1, 0):
            back[side] = kernel_call(
                functools.partial(mlp_back_kernel, hidden, len(upstream_chunks[side])),
                [partial_out, ((half, hidden), bf16), ((1, hidden), f32), ((half, width), bf16)],
                *upstream_chunks[side],
                mlp_w[l],
                mlp[side][3],
                name="mlp_back",
                scratch=[pltpu.VMEM((2, half, hidden // 2), f32), DMA((2,))],
            )
        mlp_grad, grad_token = kernel_call(
            functools.partial(mlp_grad_kernel, hidden),
            [((width, 2 * hidden), bf16), TOKEN],
            mlp[0][1],
            mlp[1][1],
            mlp[0][2],
            mlp[1][2],
            back[0][3],
            back[1][3],
            back[0][1],
            back[1][1],
            name="mlp_grad",
            after=() if l + 1 == depth else (touch(mlp_parts[l + 1]),),
            scratch=[
                pltpu.VMEM((all_rows, width), bf16),
                pltpu.VMEM((all_rows, hidden), bf16),
                pltpu.VMEM((all_rows, width), bf16),
                pltpu.VMEM((all_rows, hidden), bf16),
                DMA((4,)),
            ],
            limit=16,
        )
        pairs_now = [(back[0][0], back[1][0])]
        if l + 1 == depth:
            pairs_now.append((mlp[0][0], mlp[1][0]))
        sums, *output_sums = reduce_rows(*pairs_now, after=(grad_token,))
        if l + 1 == depth:
            output_term = output_sums[0]
        mlp_parts[l] = scatter_grads(mlp_grad)
        unit_sums[l] = back[0][2] + back[1][2]
        grad_middle, middle_b, sums_two = kernel_call(
            functools.partial(norm_back_two_kernel, gain_row(l, 1)),
            [row_f32, row_bf16, ((4, width), f32)],
            *sums,
            Far(mlp[1][4]),
            upstream,
            vecs,
            name="norm_back_two",
            scratch=[pltpu.VMEM((rows, width), f32), DMA((1,))],
        )
        middle_chunks = gather_rows(middle_b)
        grad_q = [None, None]
        middle_x = [None, None]
        carried = ()
        for side in (0, 1):
            key_parts = (pairs,) if outer > 1 else (attn[0][4], attn[1][4])
            middle_x[side], grad_q[side], *carried = kernel_call(
                functools.partial(
                    attn_back_kernel,
                    feats,
                    heads,
                    len(attn_w[l]),
                    len(key_parts),
                    tile,
                    len(carried) > 0,
                ),
                [
                    ((half, width), bf16),
                    ((half, feats), f32),
                    ((key_rows, feats), f32),
                    ((key_rows, feats), f32),
                ],
                *middle_chunks[side],
                *attn_w[l],
                usable,
                Far(attn[side][4]),
                Far(attn[side][1]),
                Far(attn[side][2]),
                *[Far(part) for part in key_parts],
                *carried,
                name="attn_back",
                scratch=[
                    pltpu.VMEM((key_rows, 2 * feats), bf16),
                    pltpu.VMEM((half, feats), bf16),
                    pltpu.VMEM((half, feats), bf16),
                    pltpu.VMEM((half, feats), f32),
                    pltpu.VMEM((half, feats), bf16),
                    DMA((3 + len(key_parts),)),
                ],
                limit=attn_limit,
            )
        grad_k, grad_v = carried
        if outer > 1:
            grad_k, grad_v = (
                lax.psum_scatter(
                    v, "ctx", scatter_dimension=0, tiled=True, axis_index_groups=outer_groups
                )
                for v in (grad_k, grad_v)
            )

        def project(side, after):
            return kernel_call(
                functools.partial(project_kernel, feats, side * half, len(attn_w[l])),
                [partial_out],
                grad_q[side],
                grad_k,
                grad_v,
                *attn_w[l],
                name="project",
                after=after,
                scratch=[pltpu.VMEM((half, 3 * feats), bf16)],
            )[0]

        def weight_grad(after=()):
            count = 1 if l > 0 else fsdp
            *parts, head_sum, token = kernel_call(
                functools.partial(attn_grad_kernel, feats),
                [((width // count, 4 * feats), bf16)] * count + [((2, feats), f32), TOKEN],
                Far(attn[0][3]),
                Far(attn[1][3]),
                Far(attn[0][1]),
                Far(attn[1][1]),
                *middle_x,
                *grad_q,
                grad_k,
                grad_v,
                name="attn_grad",
                after=after,
                scratch=[
                    pltpu.VMEM((all_rows, width), bf16),
                    pltpu.VMEM((all_rows, feats), bf16),
                    pltpu.VMEM((all_rows, width), bf16),
                    pltpu.VMEM((all_rows, 3 * feats), bf16),
                    DMA((4,)),
                ],
            )

            return parts, head_sum, token

        far_part = project(1, ())
        near_part = project(0, ())
        attn_grads, head_sums[l], grad_token = weight_grad(
            () if l + 1 == depth else (touch(attn_parts[l + 1]),)
        )
        (sums,) = reduce_rows((near_part, far_part), after=(grad_token,))
        if l > 0:
            attn_parts[l] = scatter_grads(attn_grads[0])
        body = functools.partial(norm_back_one_kernel, gain_row(l, 0))
        if l > 0:
            masked = ()
            body = lambda *refs, body=body: body(*refs[:7], None, *refs[7:])
        else:
            masked = (mask,)
        upstream, upstream_b, sums_one = kernel_call(
            body,
            [row_f32, row_bf16, ((2, width), f32)],
            *sums,
            Far(attn[1][5]),
            grad_middle,
            vecs,
            *masked,
            name="norm_back_one",
            scratch=[pltpu.VMEM((rows, width), f32), DMA((1,))],
        )
        if l > 0:
            upstream_chunks = gather_rows(upstream_b)
        row_sums[l] = (sums_one, sums_two)

    vec_part = jnp.concatenate(
        [
            piece
            for l in range(depth)
            for piece in (
                row_sums[l][0][0:1],
                row_sums[l][1][0:1],
                row_sums[l][0][1:2],
                row_sums[l][1][1:4],
            )
        ],
        axis=0,
    )
    unit_part = jnp.concatenate(unit_sums, axis=0)
    head_part = jnp.concatenate(head_sums, axis=0)
    unit_lines = unit_part.reshape(-1, width)
    head_lines = head_part.reshape(1, -1)
    head_lines = jnp.pad(head_lines, ((0, 0), (0, width - head_lines.shape[1])))
    packed = jnp.concatenate([vec_part, unit_lines, head_lines], axis=0)
    if outer > 1:
        packed = lax.psum(packed, "ctx", axis_index_groups=outer_groups)
    early = [(l, kind) for l in range(depth) for kind in (0, 1) if (l, kind) != (0, 1)]
    parts = {key: gate((mlp_parts, attn_parts)[key[1]][key[0]], (sums_one,)) for key in early}
    outputs_own = kernel_call(
        functools.partial(sum_out_kernel, shift_row(depth - 1, 3)),
        [row_f32],
        *output_term,
        Far(saved_all[depth - 1][2][1][4]),
        vecs,
        mask,
        name="sum_out",
        after=(sums_one,),
        scratch=[pltpu.VMEM((rows, width), f32), DMA((1,))],
    )[0]
    last_terms = (attn_grads[0], *[shift_z(attn_grads[d], d) for d in range(1, fsdp)])
    crossed = {key: swap_x(parts[key]) for key in early}
    others = (swap_y(upstream), swap_y(outputs_own))
    packed, hub_token = kernel_call(
        vector_sum_kernel,
        [(packed.shape, f32), TOKEN],
        packed,
        *[shift_z(packed, d) for d in range(1, fsdp)],
        name="vector_sum",
        after=(*crossed.values(), *others, *last_terms[1:]),
    )
    grad_inputs, outputs = (
        kernel_call(
            place_rows_kernel,
            [saved(inputs.shape, f32)],
            own,
            other,
            name="place_rows",
            scratch=[DMA((2,))],
        )[0]
        for own, other in zip((upstream, outputs_own), others)
    )
    vec_sum = lax.dynamic_slice_in_dim(packed[:vec_rows], f * width_own, width_own, axis=1)
    vec_sum = vec_sum.reshape(-1, width)
    vec_lines = vec_sum.shape[0]
    rest = packed[vec_rows:]
    mine = jnp.concatenate([vec_sum, rest], axis=0)
    from_x = swap_x(mine)
    vec_sum = vec_sum + swap_xy(vec_sum) + from_x[:vec_lines] + swap_y(vec_sum)
    mine = jnp.concatenate([vec_sum, rest, from_x[vec_lines:]], axis=0)
    from_core = swap_core(mine)
    vec_sum = (vec_sum + from_core[:vec_lines]).reshape(depth, 6, width_own)
    count = rest.shape[0]
    rest_four = jnp.stack(
        [
            rest,
            from_core[vec_lines : vec_lines + count],
            mine[vec_lines + count :],
            from_core[vec_lines + count :],
        ]
    )
    unit_count = unit_lines.shape[0]

    def of_place(c):
        return lax.dynamic_index_in_dim(rest_four, ci ^ c, 0, keepdims=False)

    grad_fc1_bias = of_place(f)[:unit_count].reshape(depth, 1, hidden)
    grad_qv_bias = jnp.stack(
        [
            lax.dynamic_slice_in_dim(
                of_place(c)[unit_count, : head_part.size].reshape(depth, 2, heads, head_dim),
                f * head_own,
                head_own,
                axis=3,
            )
            for c in range(GROUP)
        ],
        axis=2,
    ).reshape(qv_bias.shape)
    placed = [None, None]
    for l, kind in early + [(0, 1)]:
        if (l, kind) in parts:
            part, other = parts[l, kind], crossed[l, kind]
        else:
            part = kernel_call(
                shard_sum_kernel,
                [((width_own, 4 * feats), bf16)],
                *last_terms,
                name="shard_sum",
                after=(hub_token,),
            )[0]
            if outer > 1:
                part = lax.psum(part, "ctx", axis_index_groups=outer_groups)
            other = swap_x(part)
        pieces = (part, swap_core(part), other, swap_core(other))
        if kind == 0:
            placed[0] = place_call(
                functools.partial(place_mlp_kernel, l, hidden),
                pieces,
                placed[0],
                [w_fc1.shape, w_fc2.shape],
                [(GROUP, width_own, hidden), (GROUP, hidden, width_own)],
                "place_mlp",
            )
        else:
            placed[1] = place_call(
                functools.partial(place_attn_kernel, l, feats),
                pieces,
                placed[1],
                [w_qkv.shape, w_out.shape],
                [(GROUP, 3, width_own, feats), (GROUP, feats, width_own)],
                "place_attn",
            )
    return (
        outputs,
        grad_inputs,
        vec_sum[:, :2],
        vec_sum[:, 2:],
        grad_qv_bias,
        grad_fc1_bias,
        placed[1][0],
        placed[1][1],
        placed[0][0],
        placed[0][1],
    )


def solution(mesh):
    rows = P("fsdp", "ctx", None)
    params = (
        P(None, None, "fsdp"),
        P(None, None, "fsdp"),
        P(None, None, "tp", "fsdp"),
        P(None, "tp", "fsdp"),
        P(None, None, "fsdp", "tp"),
        P(None, "tp", "fsdp"),
        P(None, "fsdp", "tp"),
        P(None, "tp", "fsdp"),
    )
    return jax.shard_map(
        per_device,
        mesh=mesh,
        in_specs=(rows, P("fsdp", None), rows) + params,
        out_specs=(rows, rows) + params,
        check_vma=False,
    )
```

```python
import functools
import math

import jax
import jax.numpy as jnp
from jax import lax
from jax.experimental import pallas as pl
from jax.experimental.pallas import tpu as pltpu
from jax.sharding import PartitionSpec as P

NORM_EPSILON = 1e-06
MASK_FILL = -1e30
ROOT_HALF = 0.7071067811865476
INV_ROOT_TAU = 0.3989422804014327
GROUP = 4
ORDER = (0, 5, 4, 1, 2, 7, 6, 3)
CHIPS = 4

bf16 = jnp.bfloat16
f32 = jnp.float32
VMEM = pl.BlockSpec(memory_space=pltpu.VMEM)
SMEM = pl.BlockSpec(memory_space=pltpu.SMEM)
HBM = pl.BlockSpec(memory_space=pltpu.HBM)
DMA = pltpu.SemaphoreType.DMA
TOKEN = ((8, 128), f32)


def dot(a, b):
    return lax.dot_general(a, b, (((1,), (0,)), ((), ())), preferred_element_type=f32)


def dot_nt(a, b):
    return lax.dot_general(a, b, (((1,), (1,)), ((), ())), preferred_element_type=f32)


def dot_tn(a, b):
    return lax.dot_general(a, b, (((0,), (0,)), ((), ())), preferred_element_type=f32)


class Far:
    def __init__(self, value):
        self.value = value


class Scalars:
    def __init__(self, value):
        self.value = value


def saved(shape, dtype):
    return pltpu.HBM(shape, dtype)


def kernel_call(body, outs, *args, name, limit=12, scratch=(), after=(), aliases=None, us=0):
    values, specs = [], []
    for arg in (*args, *after):
        if isinstance(arg, Far):
            values.append(pltpu.with_memory_space_constraint(arg.value, pltpu.HBM))
            specs.append(HBM)
        elif isinstance(arg, Scalars):
            values.append(arg.value)
            specs.append(SMEM)
        else:
            values.append(arg)
            specs.append(VMEM)
    first, last = len(args), len(args) + len(after)

    def run(*refs):
        body(*refs[:first], *refs[last:])

    out_shape, out_specs = [], []
    for out in outs:
        if isinstance(out, tuple):
            out_shape.append(jax.ShapeDtypeStruct(*out))
            out_specs.append(VMEM)
        else:
            out_shape.append(out)
            out_specs.append(HBM)
    return pl.pallas_call(
        run,
        out_shape=out_shape,
        in_specs=specs,
        out_specs=out_specs,
        scratch_shapes=list(scratch),
        input_output_aliases=aliases or {},
        compiler_params=pltpu.CompilerParams(vmem_limit_bytes=limit << 20),
        cost_estimate=pl.CostEstimate(flops=us * 10**9, bytes_accessed=0, transcendentals=0),
        name=name,
    )(*values)


def start_copies(pairs, sems):
    copies = [
        pltpu.make_async_copy(source, target, sems.at[k])
        for k, (source, target) in enumerate(pairs)
    ]
    for copy in copies:
        copy.start()
    return copies


def row_mean(value):
    return jnp.mean(value, axis=-1, keepdims=True)


def normalize(values):
    center = values - row_mean(values)
    inverse = lax.rsqrt(row_mean(center * center) + NORM_EPSILON)
    return center * inverse, inverse


def lanes_of(head, head_dim, width):
    lane = lax.broadcasted_iota(jnp.int32, (1, width), 1)
    return (lane >= head * head_dim) & (lane < (head + 1) * head_dim)


def assemble(chunks, target):
    rows = chunks[0].shape[0]
    for k, chunk in enumerate(chunks):
        target[k * rows : (k + 1) * rows, :] = chunk[...]


def only(flag, value):
    return jnp.where(flag, value, jnp.zeros_like(value))


def shards(weights):
    if len(weights) == 1:
        rows = weights[0].shape[0]
        return [(pl.ds(0, rows), weights[0])]
    count = len(weights)
    rows = weights[0].shape[0]
    f = lax.axis_index("fsdp")
    found = []
    for d, ref in enumerate(weights):
        place = lax.rem(f + (count - d), count)
        found.append((pl.ds(pl.multiple_of(place * rows, rows), rows), ref))
    return found


def pack_attn_kernel(layer, feats, qkv_hbm, out_hbm, packed_ref, token, qkv, out, sems):
    ci = lax.rem(lax.axis_index("ctx"), GROUP)
    span = pl.ds(pl.multiple_of(ci * feats, feats), feats)
    copies = start_copies(
        [(qkv_hbm.at[layer, :, :, span], qkv), (out_hbm.at[layer, span, :], out)], sems
    )
    copies[0].wait()
    for k in range(3):
        packed_ref[:, k * feats : (k + 1) * feats] = qkv[k]
    copies[1].wait()
    packed_ref[:, 3 * feats :] = out[...].T
    token[...] = jnp.zeros_like(token)


def pack_mlp_kernel(layer, hidden, fc1_hbm, fc2_hbm, packed_ref, token, fc1, fc2, sems):
    ci = lax.rem(lax.axis_index("ctx"), GROUP)
    span = pl.ds(pl.multiple_of(ci * hidden, hidden), hidden)
    copies = start_copies(
        [(fc1_hbm.at[layer, :, span], fc1), (fc2_hbm.at[layer, span, :], fc2)], sems
    )
    copies[0].wait()
    packed_ref[:, :hidden] = fc1[...]
    copies[1].wait()
    packed_ref[:, hidden:] = fc2[...].T
    token[...] = jnp.zeros_like(token)


def prep_upstream_kernel(tp, outer, lengths, cotangent_hbm,
                         upstream_hbm, upstream_b_ref, usable_ref, mask_ref,
                         rows_in, upstream_ref, sems):
    rows = rows_in.shape[0]
    c = lax.axis_index("ctx")
    t = lax.axis_index("tp")
    place = lax.rem(c, GROUP) * tp + t
    start = pl.multiple_of(t * rows, rows)
    copies = start_copies(
        [(cotangent_hbm.at[0, pl.ds(start, rows), :], rows_in)], sems.at[pl.ds(0, 1)]
    )
    lane = lax.broadcasted_iota(jnp.int32, usable_ref.shape, 1)
    limit = jnp.zeros(usable_ref.shape, jnp.int32)
    for o in range(outer):
        for k, d in enumerate(ORDER):
            source = place ^ d
            first_lane = (o * len(ORDER) + k) * rows
            count = lengths[0, o * GROUP + lax.div(source, tp)] - lax.rem(source, tp) * rows
            limit = jnp.where(lane >= first_lane, first_lane + jnp.clip(count, 0, rows), limit)
    usable_ref[...] = jnp.where(lane < limit, 1.0, 0.0)
    row = lax.broadcasted_iota(jnp.int32, mask_ref.shape, 0)
    mask = jnp.where(row + start < lengths[0, c], 1.0, 0.0)
    mask_ref[...] = mask
    copies[0].wait()
    upstream = rows_in[...] * mask[:, 0:1]
    upstream_ref[...] = upstream
    sent = start_copies([(upstream_ref, upstream_hbm)], sems.at[pl.ds(1, 1)])
    upstream_b_ref[...] = upstream.astype(bf16)
    sent[0].wait()


def prep_first_kernel(depth, inputs_hbm, vecs, stream_ref, first_ref, sems):
    rows = stream_ref.shape[0]
    start = pl.multiple_of(lax.axis_index("tp") * rows, rows)
    copies = start_copies([(inputs_hbm.at[0, pl.ds(start, rows), :], stream_ref)], sems)
    copies[0].wait()
    normed, _ = normalize(stream_ref[...])
    shift = vecs[2 * depth : 2 * depth + 1, :]
    first_ref[...] = (normed * vecs[0:1, :] + shift).astype(bf16)


def keep_rows_kernel(*refs):
    chunks, (near_hbm, far_hbm, token, near, far, sems) = refs[:8], refs[8:]
    assemble(chunks[:4], near)
    assemble(chunks[4:], far)
    for copy in start_copies([(near, near_hbm), (far, far_hbm)], sems):
        copy.wait()
    token[...] = jnp.zeros_like(token)


def qkv_kernel(feats, weight_count, *refs):
    c0, c1, c2, c3, *rest = refs
    weights = rest[:weight_count]
    bias, qkv_ref, x = rest[weight_count:]
    assemble((c0, c1, c2, c3), x)
    qkv = sum(dot(x[:, span], w[:, : 3 * feats]) for span, w in shards(weights))
    qkv_ref[:, :feats] = (qkv[:, :feats] + bias[0:1, :]).astype(bf16)
    qkv_ref[:, feats : 2 * feats] = qkv[:, feats : 2 * feats].astype(bf16)
    qkv_ref[:, 2 * feats :] = (qkv[:, 2 * feats :] + bias[1:2, :]).astype(bf16)


def attn_kernel(feats, heads, weight_count, part_count, keep_count, tile, *refs):
    q_ref, *rest = refs
    parts = rest[:part_count]
    weights = rest[part_count : part_count + weight_count]
    rest = rest[part_count + weight_count :]
    usable, *rest = rest
    kept, rest = rest[:keep_count], rest[keep_count:]
    partial_ref, attended_hbm, norm_hbm, *rest = rest
    kept_hbm, rest = rest[:keep_count], rest[keep_count:]
    keys, values, attended_ref, norm_ref, sems = rest
    head_dim = feats // heads
    scale = 1.0 / math.sqrt(head_dim)
    copies = start_copies(list(zip(kept, kept_hbm)), sems)
    first = 0
    for part in parts:
        rows, width = part.shape
        keys[first : first + rows, :] = part[:, width - 2 * feats : width - feats]
        values[first : first + rows, :] = part[:, width - feats :]
        first += rows
    keep = usable[...] > 0.5
    rows = q_ref.shape[0]
    for first in range(0, rows, tile):
        span = slice(first, first + tile)
        q = q_ref[span, :feats]
        attended = None
        for h in range(heads):
            own = lanes_of(h, head_dim, feats)
            scores = dot_nt(only(own, q), keys[...]) * scale
            scores = jnp.where(keep, scores, MASK_FILL)
            highest = jnp.max(scores, axis=-1, keepdims=True)
            raised = jnp.exp(scores - highest)
            total = jnp.sum(raised, axis=-1, keepdims=True)
            soft = (raised * (1.0 / total)).astype(bf16)
            result = dot(soft, values[...])
            log_norm = jnp.broadcast_to(highest + jnp.log(total), (tile, feats))
            if attended is None:
                attended, norms = result, log_norm
            else:
                attended = jnp.where(own, result, attended)
                norms = jnp.where(own, log_norm, norms)
        attended_ref[span, :] = attended.astype(bf16)
        norm_ref[span, :] = norms
    copies += start_copies(
        [(attended_ref, attended_hbm), (norm_ref, norm_hbm)],
        sems.at[pl.ds(keep_count, 2)],
    )
    for span, w in shards(weights):
        partial_ref[:, span] = dot_nt(attended_ref[...], w[:, 3 * feats :]).astype(bf16)
    for copy in copies:
        copy.wait()


def core_sum_kernel(count, *refs):
    pairs, owns = refs[: 2 * count], refs[2 * count : 3 * count]
    peers = refs[3 * count :]
    rows = owns[0].shape[0]
    for j in range(count):
        near, far = pairs[2 * j], pairs[2 * j + 1]
        for k in range(1 + len(peers)):
            span = slice(k * rows, (k + 1) * rows)
            total = near[span, :].astype(f32) + far[span, :].astype(f32)
            if k == 0:
                owns[j][...] = total
            else:
                peers[k - 1][j * rows : (j + 1) * rows, :] = total.astype(bf16)


def total_of(own, xy, x, y, part=0):
    rows = own.shape[0]
    span = slice(part * rows, (part + 1) * rows)
    return (
        own[...] + y[span, :].astype(f32) + x[span, :].astype(f32) + xy[span, :].astype(f32)
    )


def sum_norm_kernel(bias_row, gain_row, shift_row, own, xy, x, y, residual_hbm, vecs,
                    stream_ref, normed_ref, residual, sems):
    copies = start_copies([(residual_hbm, residual)], sems)
    total = total_of(own, xy, x, y) + vecs[bias_row : bias_row + 1, :]
    copies[0].wait()
    stream = residual[...] + total
    stream_ref[...] = stream
    normed, _ = normalize(stream)
    gain = vecs[gain_row : gain_row + 1, :]
    normed_ref[...] = (normed * gain + vecs[shift_row : shift_row + 1, :]).astype(bf16)


def sum_out_kernel(bias_row, own, xy, x, y, residual_hbm, vecs, mask, out_hbm, token,
                   residual, out_ref, sems):
    copies = start_copies([(residual_hbm, residual)], sems.at[pl.ds(0, 1)])
    total = total_of(own, xy, x, y, 1) + vecs[bias_row : bias_row + 1, :]
    copies[0].wait()
    out_ref[...] = (residual[...] + total) * mask[:, 0:1]
    token[...] = jnp.zeros_like(token)
    for copy in start_copies([(out_ref, out_hbm)], sems.at[pl.ds(1, 1)]):
        copy.wait()


def mlp_kernel(hidden, keep_count, saves, c0, c1, c2, c3, w, bias, *refs):
    kept, rest = refs[:keep_count], refs[keep_count:]
    partial_ref, x_out, act_out, slope_out, *rest = rest
    kept_hbm, rest = rest[:keep_count], rest[keep_count:]
    if saves:
        x, act_ref, slope_ref, sems = rest
    else:
        x, act_ref, slope_ref = x_out, act_out, slope_out
        (sems,) = rest
    copies = start_copies(list(zip(kept, kept_hbm)), sems)
    assemble((c0, c1, c2, c3), x)
    if saves:
        copies += start_copies([(x, x_out)], sems.at[pl.ds(keep_count, 1)])
    block = hidden // 2
    for k in range(2):
        span = slice(k * block, (k + 1) * block)
        pre = dot(x[...], w[:, span]) + bias[:, span]
        cdf = 0.5 * (1.0 + lax.erf(pre * ROOT_HALF))
        density = jnp.exp(-0.5 * pre * pre) * INV_ROOT_TAU
        slope_ref[k] = cdf + pre * density
        act_ref[:, span] = (pre * cdf).astype(bf16)
        if saves:
            copies += start_copies(
                [(slope_ref.at[k], slope_out.at[k])], sems.at[pl.ds(1 + keep_count + k, 1)]
            )
    if saves:
        copies += start_copies([(act_ref, act_out)], sems.at[pl.ds(3 + keep_count, 1)])
    partial_ref[...] = dot_nt(act_ref[...], w[:, hidden:]).astype(bf16)
    for copy in copies:
        copy.wait()


def mlp_back_kernel(hidden, chunk_count, *refs):
    chunks, (w, slope_hbm, *rest) = refs[:chunk_count], refs[chunk_count:]
    partial_ref, grad_ref, sum_hbm, x, slope, sum_ref, sems = rest
    copies = start_copies([(slope_hbm, slope)], sems)
    if chunk_count == 1:
        copies += start_copies([(chunks[0], x)], sems.at[pl.ds(1, 1)])
        copies[1].wait()
    else:
        assemble(chunks, x)
    grad = dot(x[...], w[:, hidden:])
    copies[0].wait()
    block = hidden // 2
    for k in range(2):
        span = slice(k * block, (k + 1) * block)
        part = grad[:, span] * slope[k]
        grad_ref[:, span] = part.astype(bf16)
        sum_ref[:, span] = jnp.sum(part, axis=0, keepdims=True)
    sent = start_copies([(sum_ref, sum_hbm)], sems.at[pl.ds(2, 1)])
    partial_ref[...] = dot_nt(grad_ref[...], w[:, :hidden]).astype(bf16)
    sent[0].wait()


def mlp_grad_kernel(hidden, second_near, second_far, act_near, act_far, up_near, up_far,
                    grad_near, grad_far, passed, sums, middle, out_hbm, passed_ref, sums_hbm,
                    middle_hbm, second, act, up, grad, out_one, out_two, sems):
    rows = up_near.shape[0]
    sent = start_copies([(sums, sums_hbm), (middle, middle_hbm)], sems.at[pl.ds(6, 2)])
    near, far = pl.ds(0, rows), pl.ds(rows, rows)
    copies = start_copies(
        [
            (act_near, act.at[near]),
            (act_far, act.at[far]),
            (second_near, second.at[near]),
            (second_far, second.at[far]),
        ],
        sems,
    )
    passed_ref[...] = passed[...]
    up[:rows, :] = up_near[...]
    up[rows:, :] = up_far[...]
    grad[:rows, :] = grad_near[...]
    grad[rows:, :] = grad_far[...]
    for copy in copies[:2]:
        copy.wait()
    out_two[...] = dot_tn(up[...], act[...]).astype(bf16)
    sent += start_copies(
        [(out_two, out_hbm.at[:, pl.ds(hidden, hidden)])], sems.at[pl.ds(4, 1)]
    )
    for copy in copies[2:]:
        copy.wait()
    out_one[...] = dot_tn(second[...], grad[...]).astype(bf16)
    sent += start_copies([(out_one, out_hbm.at[:, pl.ds(0, hidden)])], sems.at[pl.ds(5, 1)])
    for copy in sent:
        copy.wait()


def norm_back(upstream, values, gain):
    normed, inverse = normalize(values)
    scaled = upstream * gain
    back = inverse * (scaled - row_mean(scaled) - normed * row_mean(scaled * normed))
    gain_grad = jnp.sum(upstream * normed, axis=0, keepdims=True)
    return back, gain_grad, jnp.sum(upstream, axis=0, keepdims=True)


def norm_back_two_kernel(gain_row, own, xy, x, y, values_hbm, upstream_hbm, vecs,
                         grad_ref, grad_b_ref, sums_ref, values, upstream, sems):
    copies = start_copies([(values_hbm, values), (upstream_hbm, upstream)], sems)
    total = total_of(own, xy, x, y)
    for copy in copies:
        copy.wait()
    up = upstream[...]
    back, gain_grad, shift_grad = norm_back(
        total, values[...], vecs[gain_row : gain_row + 1, :]
    )
    grad = up + back
    grad_ref[...] = grad
    grad_b_ref[...] = grad.astype(bf16)
    sums_ref[0:1, :] = gain_grad
    sums_ref[1:2, :] = shift_grad
    sums_ref[2:3, :] = jnp.sum(grad, axis=0, keepdims=True)
    sums_ref[3:4, :] = jnp.sum(up, axis=0, keepdims=True)


def norm_back_one_kernel(gain_row, own, xy, x, y, values_hbm, upstream_hbm, vecs, mask,
                         grad_ref, grad_b_ref, sums_ref, values, upstream, sems):
    copies = start_copies([(values_hbm, values), (upstream_hbm, upstream)], sems)
    total = total_of(own, xy, x, y)
    for copy in copies:
        copy.wait()
    back, gain_grad, shift_grad = norm_back(
        total, values[...], vecs[gain_row : gain_row + 1, :]
    )
    grad = upstream[...] + back
    if mask is not None:
        grad = grad * mask[:, 0:1]
    grad_ref[...] = grad
    grad_b_ref[...] = grad.astype(bf16)
    sums_ref[0:1, :] = gain_grad
    sums_ref[1:2, :] = shift_grad


def attn_back_kernel(feats, heads, weight_count, part_count, tile, carried, *refs):
    c0, c1, c2, c3, *rest = refs
    weights, rest = rest[:weight_count], rest[weight_count:]
    usable, q_hbm, attended_hbm, norm_hbm, *rest = rest
    parts, rest = rest[:part_count], rest[part_count:]
    if carried:
        keys_before, values_before, *rest = rest
    x, grad_q, grad_k, grad_v, pairs, q_ref, attended, norms, grad_att, sems = rest
    head_dim = feats // heads
    scale = 1.0 / math.sqrt(head_dim)
    moves = [(q_hbm.at[:, pl.ds(0, feats)], q_ref), (attended_hbm, attended), (norm_hbm, norms)]
    first = 0
    for part in parts:
        rows, width = part.shape
        moves.append(
            (part.at[:, pl.ds(width - 2 * feats, 2 * feats)], pairs.at[pl.ds(first, rows)])
        )
        first += rows
    copies = start_copies(moves, sems)
    assemble((c0, c1, c2, c3), x)
    grad_att[...] = sum(
        dot(x[:, span], w[:, 3 * feats :]) for span, w in shards(weights)
    ).astype(bf16)
    keep = usable[...] > 0.5
    rows = q_ref.shape[0]
    if carried:
        sum_k, sum_v = keys_before[...], values_before[...]
    else:
        sum_k = jnp.zeros(grad_k.shape, f32)
        sum_v = jnp.zeros(grad_v.shape, f32)
    for copy in copies:
        copy.wait()
    keys, values = pairs[:, :feats], pairs[:, feats:]
    for first in range(0, rows, tile):
        span = slice(first, first + tile)
        q = q_ref[span, :]
        ga = grad_att[span, :]
        products = ga.astype(f32) * attended[span, :].astype(f32)
        gq = None
        for h in range(heads):
            own = lanes_of(h, head_dim, feats)
            q_h = only(own, q)
            ga_h = only(own, ga)
            row_dots = jnp.sum(only(own, products), axis=-1, keepdims=True)
            scores = dot_nt(q_h, keys) * scale
            scores = jnp.where(keep, scores, MASK_FILL)
            soft = jnp.exp(scores - norms[span, h * head_dim : h * head_dim + 1])
            grad_soft = dot_nt(ga_h, values)
            grad_scores = (soft * (grad_soft - row_dots)).astype(bf16)
            part = dot(grad_scores, keys)
            gq = part if gq is None else jnp.where(own, part, gq)
            sum_k = sum_k + dot_tn(grad_scores, q_h) * scale
            sum_v = sum_v + dot_tn(soft.astype(bf16), ga_h)
        grad_q[span, :] = gq * scale
    grad_k[...] = sum_k
    grad_v[...] = sum_v


def project_kernel(feats, first, weight_count, gq, gk, gv, *refs):
    weights, (partial_ref, packed) = refs[:weight_count], refs[weight_count:]
    rows = gq.shape[0]
    span = slice(first, first + rows)
    packed[:, :feats] = gq[...].astype(bf16)
    packed[:, feats : 2 * feats] = gk[span, :].astype(bf16)
    packed[:, 2 * feats :] = gv[span, :].astype(bf16)
    for columns, w in shards(weights):
        partial_ref[:, columns] = dot_nt(packed[...], w[:, : 3 * feats]).astype(bf16)


def attn_grad_kernel(feats, count, first_near, first_far, att_near, att_far, up_near, up_far,
                     gq_near, gq_far, gk, gv, passed, sums, stream, *refs):
    outs, rest = refs[:count], refs[count:]
    heads_hbm, passed_ref, sums_hbm, stream_hbm, *rest = rest
    first, att, up, packed, sums_ref, *staged, sems = rest
    rows = up_near.shape[0]
    sent = start_copies([(sums, sums_hbm), (stream, stream_hbm)], sems.at[pl.ds(6, 2)])
    near, far = pl.ds(0, rows), pl.ds(rows, rows)
    copies = start_copies(
        [
            (att_near, att.at[near]),
            (att_far, att.at[far]),
            (first_near, first.at[near]),
            (first_far, first.at[far]),
        ],
        sems,
    )
    passed_ref[...] = passed[...]
    up[:rows, :] = up_near[...]
    up[rows:, :] = up_far[...]
    packed[:rows, :feats] = gq_near[...].astype(bf16)
    packed[rows:, :feats] = gq_far[...].astype(bf16)
    packed[:, feats : 2 * feats] = gk[...].astype(bf16)
    packed[:, 2 * feats :] = gv[...].astype(bf16)
    sums_ref[0:1, :] = jnp.sum(gq_near[...], axis=0, keepdims=True) + jnp.sum(
        gq_far[...], axis=0, keepdims=True
    )
    sums_ref[1:2, :] = jnp.sum(gv[...], axis=0, keepdims=True)
    sent += start_copies([(sums_ref, heads_hbm)], sems.at[pl.ds(8, 1)])
    if count == 1:
        out_one, out_two = staged
        for copy in copies[:2]:
            copy.wait()
        out_two[...] = dot_tn(up[...], att[...]).astype(bf16)
        sent += start_copies(
            [(out_two, outs[0].at[:, pl.ds(3 * feats, feats)])], sems.at[pl.ds(4, 1)]
        )
        for copy in copies[2:]:
            copy.wait()
        out_one[...] = dot_tn(first[...], packed[...]).astype(bf16)
        sent += start_copies(
            [(out_one, outs[0].at[:, pl.ds(0, 3 * feats)])], sems.at[pl.ds(5, 1)]
        )
        for copy in sent:
            copy.wait()
        return
    for copy in copies:
        copy.wait()
    width_own = outs[0].shape[0]
    for d, out_ref in enumerate(outs):
        place = lax.rem(lax.axis_index("fsdp") + d, count)
        span = pl.ds(pl.multiple_of(place * width_own, width_own), width_own)
        out_ref[:, : 3 * feats] = dot_tn(first[:, span], packed[...]).astype(bf16)
        out_ref[:, 3 * feats :] = dot_tn(up[:, span], att[...]).astype(bf16)
    for copy in sent:
        copy.wait()


def settle_kernel(passed, *refs):
    passed_ref = refs[-1]
    passed_ref[...] = passed[...]


def fetch_kernel(count, *refs):
    sources, targets, (token, sems) = refs[:count], refs[count : 2 * count], refs[2 * count :]
    token[...] = jnp.zeros_like(token)
    for copy in start_copies(list(zip(sources, targets)), sems):
        copy.wait()


def shard_sum_kernel(*refs):
    *terms, out_ref = refs
    out_ref[...] = sum(term[...].astype(f32) for term in terms).astype(out_ref.dtype)


def place_kernel(depth, hidden, feats, *refs):
    pieces = refs[: 8 * depth]
    outs, (fc1, fc2, qkv, out, sems) = refs[8 * depth : 8 * depth + 4], refs[8 * depth + 4 :]
    qkv_hbm, out_hbm, fc1_hbm, fc2_hbm = outs
    ci = lax.rem(lax.axis_index("ctx"), GROUP)
    copies = []

    def send(source, target):
        copies.extend(start_copies([(source, target)], sems.at[pl.ds(len(copies), 1)]))

    for l in reversed(range(depth)):
        for k in range(GROUP):
            piece = pieces[8 * l + k]
            span = pl.ds(pl.multiple_of((ci ^ k) * hidden, hidden), hidden)
            fc1[l, k] = piece[:, :hidden].astype(f32)
            send(fc1.at[l, k], fc1_hbm.at[l, :, span])
            fc2[l, k] = piece[:, hidden:].T.astype(f32)
            send(fc2.at[l, k], fc2_hbm.at[l, span, :])
    for l in reversed(range(depth)):
        for k in range(GROUP):
            piece = pieces[8 * l + 4 + k]
            span = pl.ds(pl.multiple_of((ci ^ k) * feats, feats), feats)
            for j in range(3):
                qkv[l, k, j] = piece[:, j * feats : (j + 1) * feats].astype(f32)
            send(qkv.at[l, k], qkv_hbm.at[l, :, :, span])
            out[l, k] = piece[:, 3 * feats :].T.astype(f32)
            send(out.at[l, k], out_hbm.at[l, span, :])
    for copy in copies:
        copy.wait()


def vector_pack_kernel(depth, *refs):
    count = 5 * depth
    out_ref, *terms, sems = refs[count:]
    copies = start_copies(list(zip(refs[:count], terms)), sems)
    out_ref[...] = jnp.zeros_like(out_ref)
    for copy in copies:
        copy.wait()
    for l in range(depth):
        one, two, unit_near, unit_far, head = terms[5 * l : 5 * l + 5]
        out_ref[6 * l : 6 * l + 1, :] = one[0:1, :]
        out_ref[6 * l + 1 : 6 * l + 2, :] = two[0:1, :]
        out_ref[6 * l + 2 : 6 * l + 3, :] = one[1:2, :]
        out_ref[6 * l + 3 : 6 * l + 6, :] = two[1:4, :]
        units = unit_near.shape[1]
        feats = head.shape[1]
        row = 6 * depth
        out_ref[row : row + 1, l * units : (l + 1) * units] = unit_near[...] + unit_far[...]
        for j in range(2):
            first = (2 * l + j) * feats
            out_ref[row + 1 : row + 2, first : first + feats] = head[j : j + 1, :]


def vector_own_kernel(depth, width_own, own, *refs):
    *others, out_ref, token = refs
    total = own[...]
    for other in others:
        total = total + other[...]
    f = lax.axis_index("fsdp")
    count = total.shape[1] // width_own
    mine = jnp.zeros((6 * depth, width_own), f32)
    for a in range(count):
        piece = total[: 6 * depth, a * width_own : (a + 1) * width_own]
        mine = jnp.where(f == a, piece, mine)
        for r in range(2):
            row = 6 * depth + r
            out_ref[16 + count * r + a : 17 + count * r + a, :] = total[
                row : row + 1, a * width_own : (a + 1) * width_own
            ]
    out_ref[: 6 * depth, :] = mine
    token[...] = jnp.zeros_like(token)


def vector_plane_kernel(depth, own, xy, x, y, out_ref):
    last = 6 * depth
    out_ref[:last, :] = own[:last, :] + xy[:last, :] + x[:last, :] + y[:last, :]
    out_ref[16:24, :] = own[16:24, :]
    out_ref[24:32, :] = x[16:24, :]


def vector_place_kernel(depth, head_dim, own, far, gains_ref, shifts_ref, unit_ref, heads_ref):
    total = own[: 6 * depth, :] + far[: 6 * depth, :]
    for l in range(depth):
        gains_ref[l] = total[6 * l : 6 * l + 2, :]
        shifts_ref[l] = total[6 * l + 2 : 6 * l + 6, :]
    pieces = (own[16:24, :], far[16:24, :], own[24:32, :], far[24:32, :])
    ci = lax.rem(lax.axis_index("ctx"), GROUP)
    f = lax.axis_index("fsdp")

    def of_place(c):
        k = ci ^ c
        found = pieces[0]
        for j in range(1, GROUP):
            found = jnp.where(k == j, pieces[j], found)
        return found

    width_own = own.shape[1]
    units = of_place(f)
    parts = unit_ref.shape[2] // width_own
    for l in range(depth):
        for j in range(parts):
            row = l * parts + j
            unit_ref[l, :, j * width_own : (j + 1) * width_own] = units[row : row + 1, :]
    head_own = heads_ref.shape[3]
    heads = heads_ref.shape[2] // GROUP
    for c in range(GROUP):
        found = of_place(c)
        for l in range(depth):
            for j in range(2):
                for h in range(heads):
                    first = ((2 * l + j) * heads + h) * head_dim
                    row, lane = 4 + first // width_own, first % width_own
                    value = found[row : row + 1, lane : lane + head_own]
                    for a in range(1, head_dim // head_own):
                        start = lane + a * head_own
                        value = jnp.where(
                            f == a, found[row : row + 1, start : start + head_own], value
                        )
                    heads_ref[l, j, c * heads + h : c * heads + h + 1, :] = value


def place_rows_kernel(own, other, out_hbm, sems):
    rows = own.shape[0]
    start = pl.multiple_of(lax.axis_index("tp") * rows, rows)
    copies = start_copies(
        [
            (own, out_hbm.at[0, pl.ds(start, rows), :]),
            (other, out_hbm.at[0, pl.ds(pl.multiple_of(rows - start, rows), rows), :]),
        ],
        sems,
    )
    for copy in copies:
        copy.wait()


def per_device(
    inputs, lengths, cotangent, norm_gains, shifts, qv_bias, fc1_bias, w_qkv, w_out, w_fc1, w_fc2
):
    depth = w_qkv.shape[0]
    width_own = w_qkv.shape[2]
    fsdp = lax.axis_size("fsdp")
    tp = lax.axis_size("tp")
    ctx = lax.axis_size("ctx")
    outer = ctx // GROUP
    rows = inputs.shape[1] // tp
    half = rows * CHIPS
    all_rows = 2 * half
    head_own = qv_bias.shape[3]
    head_dim = head_own * fsdp
    heads = qv_bias.shape[2] // GROUP
    feats = heads * head_dim
    hidden = w_fc1.shape[2] // GROUP
    width = width_own * fsdp
    t = lax.axis_index("tp")
    f = lax.axis_index("fsdp")
    ci = lax.axis_index("ctx") % GROUP
    tile = half // 2
    attn_limit = 12 if outer == 1 else 48

    def swap_core(value):
        return lax.ppermute(value, "ctx", [(i, i ^ 1) for i in range(ctx)])

    def swap_x(value):
        return lax.ppermute(value, "ctx", [(i, i ^ 2) for i in range(ctx)])

    def swap_y(value):
        return lax.ppermute(value, "tp", [(i, i ^ 1) for i in range(tp)])

    def swap_xy(value):
        pairs = [
            (i * tp + k, (i ^ 2) * tp + (k ^ 1)) for i in range(ctx) for k in range(tp)
        ]
        return lax.ppermute(value, ("ctx", "tp"), pairs)

    def shift_z(value, d):
        return lax.ppermute(value, "fsdp", [(i, (i + d) % fsdp) for i in range(fsdp)])

    outer_groups = [[o * GROUP + i for o in range(outer)] for i in range(GROUP)]

    def gather_rows(own):
        near = (own, swap_xy(own), swap_x(own), swap_y(own))
        return near, tuple(swap_core(chunk) for chunk in near)

    def settle(value, *after):
        return kernel_call(
            settle_kernel, [(value.shape, value.dtype)], value, name="settle", after=after
        )[0]

    def reduce_rows(*pairs, after=()):
        count = len(pairs)
        *owns, xy, x, y = kernel_call(
            functools.partial(core_sum_kernel, count),
            [((rows, width), f32)] * count + [((count * rows, width), bf16)] * 3,
            *[v for near, far in pairs for v in (near, swap_core(far))],
            name="core_sum",
            after=after,
        )
        peers = (swap_xy(xy), swap_x(x), swap_y(y))
        return [(own, *peers) for own in owns]

    def pack_attn(l, after):
        return kernel_call(
            functools.partial(pack_attn_kernel, l, feats),
            [((width_own, 4 * feats), bf16), TOKEN],
            Far(w_qkv),
            Far(w_out),
            name="pack_attn",
            after=after,
            scratch=[
                pltpu.VMEM((3, width_own, feats), bf16),
                pltpu.VMEM((feats, width_own), bf16),
                DMA((2,)),
            ],
        )

    def pack_mlp(l, after):
        return kernel_call(
            functools.partial(pack_mlp_kernel, l, hidden),
            [((width_own, 2 * hidden), bf16), TOKEN],
            Far(w_fc1),
            Far(w_fc2),
            name="pack_mlp",
            after=after,
            scratch=[
                pltpu.VMEM((width_own, hidden), bf16),
                pltpu.VMEM((hidden, width_own), bf16),
                DMA((2,)),
            ],
        )

    attn_w = []
    mlp_w = []
    token = None
    for l in range(depth):
        own, token = pack_attn(l, () if token is None else (token,))
        attn_w.append((lax.all_gather(own, "fsdp", axis=0, tiled=True),))
        own, token = pack_mlp(l, (token,))
        mlp_w.append(lax.all_gather(own, "fsdp", axis=0, tiled=True))
        if l == 0:
            pack_token = token

    qv_own = lax.dynamic_slice_in_dim(qv_bias, ci * heads, heads, axis=2)
    vec_rows = depth * 6
    c1_rows = depth * fc1_bias.shape[2] // width_own
    qv_own = qv_own.reshape(1, -1)
    small_own = jnp.concatenate(
        [
            norm_gains.reshape(-1, width_own),
            shifts.reshape(-1, width_own),
            fc1_bias.reshape(-1, width_own),
            jnp.pad(qv_own, ((0, 0), (0, width_own - qv_own.shape[1]))),
        ],
        axis=0,
    )
    shifted = [small_own] + [shift_z(small_own, d) for d in range(1, fsdp)]

    def shard(a):
        picked = shifted[0]
        for d in range(1, fsdp):
            picked = jnp.where((f - d) % fsdp == a, shifted[d], picked)
        return picked.astype(f32)

    small = [shard(a) for a in range(fsdp)]
    vecs = jnp.concatenate([s[:vec_rows] for s in small], axis=1)
    fc1_all = shard(ci)[vec_rows : vec_rows + c1_rows].reshape(depth, 1, hidden)
    qv_all = jnp.stack(
        [s[vec_rows + c1_rows, : qv_own.shape[1]].reshape(depth, 2, heads, head_own) for s in small],
        axis=3,
    ).reshape(depth, 2, feats)

    def gain_row(l, i):
        return 2 * l + i

    def shift_row(l, i):
        return 2 * depth + 4 * l + i

    key_rows = outer * all_rows
    row_f32 = ((rows, width), f32)
    row_bf16 = ((rows, width), bf16)
    upstream, upstream_b, usable, mask = kernel_call(
        functools.partial(prep_upstream_kernel, tp, outer),
        [saved((rows, width), f32), row_bf16, ((1, key_rows), f32), ((rows, 128), f32)],
        Scalars(lengths),
        Far(cotangent),
        name="prep_upstream",
        after=(pack_token,),
        scratch=[pltpu.VMEM((rows, width), f32), pltpu.VMEM((rows, width), f32), DMA((2,))],
    )
    near, far = gather_rows(upstream_b)
    half_x = pltpu.VMEM((half, width), bf16)
    *upstream_rows, upstream_token = kernel_call(
        keep_rows_kernel,
        [saved((half, width), bf16)] * 2 + [TOKEN],
        *near,
        *far,
        name="keep_rows",
        scratch=[half_x, half_x, DMA((2,))],
    )
    upstream_chunks = [(Far(x),) for x in upstream_rows]
    stream, first = kernel_call(
        functools.partial(prep_first_kernel, depth),
        [row_f32, row_bf16],
        Far(inputs),
        vecs,
        name="prep_first",
        scratch=[DMA((1,))],
    )
    first_chunks = gather_rows(first)

    partial_out = ((half, width), bf16)
    saved_all = []
    for l in range(depth):
        qkv = []
        first_x = []
        for side in (0, 1):
            qkv_half, x_half = kernel_call(
                functools.partial(qkv_kernel, feats, len(attn_w[l])),
                [((half, 3 * feats), bf16), ((half, width), bf16)],
                *first_chunks[side],
                *attn_w[l],
                qv_all[l],
                name="qkv",
                after=(upstream_token,) if l == 0 and side == 0 else (),
            )
            qkv.append(qkv_half)
            first_x.append(x_half)
        if outer > 1:
            pairs = jnp.concatenate([part[:, feats:] for part in qkv], axis=0)
            pairs = lax.all_gather(
                pairs, "ctx", axis=0, tiled=True, axis_index_groups=outer_groups
            )
            key_parts = (pairs,)
        else:
            key_parts = tuple(qkv)
        attn = [None, None]
        for side in (1, 0):
            kept = (first_x[side], qkv[side]) + ((stream,) if side == 1 else ())
            attn[side] = kernel_call(
                functools.partial(
                    attn_kernel, feats, heads, len(attn_w[l]), len(key_parts), len(kept), tile
                ),
                [partial_out, saved((half, feats), bf16), saved((half, feats), f32)]
                + [saved(k.shape, k.dtype) for k in kept],
                qkv[side],
                *key_parts,
                *attn_w[l],
                usable,
                *kept,
                name="attn",
                limit=attn_limit,
                scratch=[
                    pltpu.VMEM((key_rows, feats), bf16),
                    pltpu.VMEM((key_rows, feats), bf16),
                    pltpu.VMEM((half, feats), bf16),
                    pltpu.VMEM((half, feats), f32),
                    DMA((len(kept) + 2,)),
                ],
            )
        (sums,) = reduce_rows((attn[0][0], attn[1][0]))
        middle, second = kernel_call(
            functools.partial(sum_norm_kernel, shift_row(l, 2), gain_row(l, 1), shift_row(l, 1)),
            [row_f32, row_bf16],
            *sums,
            Far(attn[1][5]),
            vecs,
            name="sum_norm",
            scratch=[pltpu.VMEM((rows, width), f32), DMA((1,))],
        )
        second_chunks = gather_rows(second)
        mlp = [None, None]
        for side in (1, 0):
            kept = (middle,) if side == 1 else ()
            saves = l + 1 < depth
            shapes = [
                ((half, width), bf16),
                ((half, hidden), bf16),
                ((2, half, hidden // 2), f32),
            ]
            mlp[side] = kernel_call(
                functools.partial(mlp_kernel, hidden, len(kept), saves),
                [partial_out]
                + [saved(*shape) if saves else shape for shape in shapes]
                + [saved(k.shape, k.dtype) for k in kept],
                *second_chunks[side],
                mlp_w[l],
                fc1_all[l],
                *kept,
                name="mlp",
                scratch=[pltpu.VMEM(*shape) for shape in shapes if saves]
                + [DMA((4 + len(kept),))],
            )
            if saves:
                mlp[side] = [mlp[side][0], *[Far(v) for v in mlp[side][1:4]], *mlp[side][4:]]
        saved_all.append((attn, pairs if outer > 1 else None, mlp))
        if l + 1 < depth:
            (sums,) = reduce_rows((mlp[0][0], mlp[1][0]))
            stream, first = kernel_call(
                functools.partial(
                    sum_norm_kernel, shift_row(l, 3), gain_row(l + 1, 0), shift_row(l + 1, 0)
                ),
                [row_f32, row_bf16],
                *sums,
                Far(mlp[1][4]),
                vecs,
                name="sum_norm",
                scratch=[pltpu.VMEM((rows, width), f32), DMA((1,))],
            )
            first_chunks = gather_rows(first)

    def scatter_grads(grad):
        part = lax.psum_scatter(grad, "fsdp", scatter_dimension=0, tiled=True)
        if outer > 1:
            part = lax.psum(part, "ctx", axis_index_groups=outer_groups)
        return part

    row_sums = [None] * depth
    unit_sums = [None] * depth
    head_sums = [None] * depth
    mlp_parts = [None] * depth
    attn_parts = [None] * depth
    for l in reversed(range(depth)):
        attn, pairs, mlp = saved_all[l]
        back = [None, None]
        for side in (1, 0):
            back[side] = kernel_call(
                functools.partial(mlp_back_kernel, hidden, len(upstream_chunks[side])),
                [
                    partial_out,
                    ((half, hidden), bf16),
                    saved((1, hidden), f32),
                    ((half, width), bf16),
                ],
                *upstream_chunks[side],
                mlp_w[l],
                mlp[side][3],
                name="mlp_back",
                scratch=[
                    pltpu.VMEM((2, half, hidden // 2), f32),
                    pltpu.VMEM((1, hidden), f32),
                    DMA((3,)),
                ],
            )
        pairs_now = [(back[0][0], back[1][0])]
        if l + 1 == depth:
            pairs_now.append((mlp[0][0], mlp[1][0]))
        sums, *output_sums = reduce_rows(*pairs_now)
        if l + 1 == depth:
            outputs_own, output_token = kernel_call(
                functools.partial(sum_out_kernel, shift_row(l, 3)),
                [saved((rows, width), f32), TOKEN],
                *output_sums[0],
                Far(mlp[1][4]),
                vecs,
                mask,
                name="sum_out",
                scratch=[pltpu.VMEM((rows, width), f32)] * 2 + [DMA((2,))],
            )
            after = (output_token,)
        else:
            after = ()
        unit_sums[l] = (back[0][2], back[1][2])
        grad_middle, middle_b, sums_two = kernel_call(
            functools.partial(norm_back_two_kernel, gain_row(l, 1)),
            [row_f32, row_bf16, ((4, width), f32)],
            *sums,
            Far(mlp[1][4]),
            Far(upstream),
            vecs,
            name="norm_back_two",
            scratch=[pltpu.VMEM((rows, width), f32)] * 2 + [DMA((2,))],
        )
        mlp_grad, middle_b, sums_two, grad_middle = kernel_call(
            functools.partial(mlp_grad_kernel, hidden),
            [
                saved((width, 2 * hidden), bf16),
                row_bf16,
                saved((4, width), f32),
                saved((rows, width), f32),
            ],
            mlp[0][1],
            mlp[1][1],
            mlp[0][2],
            mlp[1][2],
            back[0][3],
            back[1][3],
            back[0][1],
            back[1][1],
            middle_b,
            sums_two,
            grad_middle,
            name="mlp_grad",
            after=after,
            scratch=[
                pltpu.VMEM((all_rows, width), bf16),
                pltpu.VMEM((all_rows, hidden), bf16),
                pltpu.VMEM((all_rows, width), bf16),
                pltpu.VMEM((all_rows, hidden), bf16),
                pltpu.VMEM((width, hidden), bf16),
                pltpu.VMEM((width, hidden), bf16),
                DMA((8,)),
            ],
            limit=16,
        )
        mlp_parts[l] = scatter_grads(mlp_grad)
        if l + 1 < depth:
            middle_b = settle(middle_b, Far(mlp_parts[l + 1]))
        middle_chunks = gather_rows(middle_b)
        grad_q = [None, None]
        middle_x = [None, None]
        carried = ()
        for side in (0, 1):
            key_parts = (pairs,) if outer > 1 else (attn[0][4], attn[1][4])
            middle_x[side], grad_q[side], *carried = kernel_call(
                functools.partial(
                    attn_back_kernel,
                    feats,
                    heads,
                    len(attn_w[l]),
                    len(key_parts),
                    tile,
                    len(carried) > 0,
                ),
                [
                    ((half, width), bf16),
                    ((half, feats), f32),
                    ((key_rows, feats), f32),
                    ((key_rows, feats), f32),
                ],
                *middle_chunks[side],
                *attn_w[l],
                usable,
                Far(attn[side][4]),
                Far(attn[side][1]),
                Far(attn[side][2]),
                *[Far(part) for part in key_parts],
                *carried,
                name="attn_back",
                scratch=[
                    pltpu.VMEM((key_rows, 2 * feats), bf16),
                    pltpu.VMEM((half, feats), bf16),
                    pltpu.VMEM((half, feats), bf16),
                    pltpu.VMEM((half, feats), f32),
                    pltpu.VMEM((half, feats), bf16),
                    DMA((3 + len(key_parts),)),
                ],
                limit=attn_limit,
            )
        grad_k, grad_v = carried
        if outer > 1:
            grad_k, grad_v = (
                lax.psum_scatter(
                    v, "ctx", scatter_dimension=0, tiled=True, axis_index_groups=outer_groups
                )
                for v in (grad_k, grad_v)
            )

        def project(side, after):
            return kernel_call(
                functools.partial(project_kernel, feats, side * half, len(attn_w[l])),
                [partial_out],
                grad_q[side],
                grad_k,
                grad_v,
                *attn_w[l],
                name="project",
                after=after,
                scratch=[pltpu.VMEM((half, 3 * feats), bf16)],
            )[0]

        far_part = project(1, ())
        near_part = project(0, ())
        (sums,) = reduce_rows((near_part, far_part))
        body = functools.partial(norm_back_one_kernel, gain_row(l, 0))
        if l > 0:
            masked = ()
            body = lambda *refs, body=body: body(*refs[:7], None, *refs[7:])
        else:
            masked = (mask,)
        upstream, upstream_b, sums_one = kernel_call(
            body,
            [row_f32, row_bf16, ((2, width), f32)],
            *sums,
            Far(attn[1][5]),
            Far(grad_middle),
            vecs,
            *masked,
            name="norm_back_one",
            scratch=[pltpu.VMEM((rows, width), f32)] * 2 + [DMA((2,))],
        )
        after = ()
        if l == 0:
            early = [(k, kind) for k in range(depth) for kind in (0, 1) if (k, kind) != (0, 1)]
            sources = [(mlp_parts, attn_parts)[kind][k] for k, kind in early]
            *fetched, token = kernel_call(
                functools.partial(fetch_kernel, len(early)),
                [(v.shape, v.dtype) for v in sources] + [TOKEN],
                *[Far(v) for v in sources],
                name="fetch",
                after=(sums_one,),
                scratch=[DMA((len(early),))],
            )
            after = (token,)
        count = 1 if l > 0 else fsdp
        shapes = [((width, 3 * feats), bf16), ((width, feats), bf16)]
        *attn_grads, head_sums[l], upstream_b, sums_one, upstream = kernel_call(
            functools.partial(attn_grad_kernel, feats, count),
            [saved((width, 4 * feats), bf16) if l > 0 else ((width_own, 4 * feats), bf16)] * count
            + [
                saved((2, feats), f32),
                row_bf16,
                saved((2, width), f32),
                saved((rows, width), f32),
            ],
            Far(attn[0][3]),
            Far(attn[1][3]),
            Far(attn[0][1]),
            Far(attn[1][1]),
            *middle_x,
            *grad_q,
            grad_k,
            grad_v,
            upstream_b,
            sums_one,
            upstream,
            name="attn_grad",
            after=after,
            scratch=[
                pltpu.VMEM((all_rows, width), bf16),
                pltpu.VMEM((all_rows, feats), bf16),
                pltpu.VMEM((all_rows, width), bf16),
                pltpu.VMEM((all_rows, 3 * feats), bf16),
                pltpu.VMEM((2, feats), f32),
            ]
            + [pltpu.VMEM(*shape) for shape in shapes if count == 1]
            + [DMA((9,))],
        )
        if l > 0:
            attn_parts[l] = scatter_grads(attn_grads[0])
            upstream_chunks = gather_rows(upstream_b)
        row_sums[l] = (sums_one, sums_two)

    parts = dict(zip(early, fetched))
    vector_rows = 6 * depth + 2
    terms = [v for l in range(depth) for v in (*row_sums[l], *unit_sums[l], head_sums[l])]
    packed = kernel_call(
        functools.partial(vector_pack_kernel, depth),
        [((vector_rows, width), f32)],
        *[Far(v) for v in terms],
        name="vector_pack",
        scratch=[pltpu.VMEM(v.shape, f32) for v in terms] + [DMA((len(terms),))],
    )[0]
    if outer > 1:
        packed = lax.psum(packed, "ctx", axis_index_groups=outer_groups)
    last_terms = (attn_grads[0], *[shift_z(attn_grads[d], d) for d in range(1, fsdp)])
    crossed = {key: swap_x(parts[key]) for key in early}
    others = (swap_y(upstream), swap_y(outputs_own))
    mine, hub_token = kernel_call(
        functools.partial(vector_own_kernel, depth, width_own),
        [((24, width_own), f32), TOKEN],
        packed,
        *[shift_z(packed, d) for d in range(1, fsdp)],
        name="vector_own",
        after=(*crossed.values(), *others, *last_terms[1:]),
    )
    part = kernel_call(
        shard_sum_kernel,
        [((width_own, 4 * feats), bf16)],
        *last_terms,
        name="shard_sum",
        after=(hub_token,),
    )[0]
    if outer > 1:
        part = lax.psum(part, "ctx", axis_index_groups=outer_groups)
    parts[0, 1], crossed[0, 1] = part, swap_x(part)
    pieces = {
        key: (parts[key], swap_core(parts[key]), crossed[key], swap_core(crossed[key]))
        for key in parts
    }
    mine = kernel_call(
        functools.partial(vector_plane_kernel, depth),
        [((32, width_own), f32)],
        mine,
        swap_xy(mine),
        swap_x(mine),
        swap_y(mine),
        name="vector_plane",
        after=(crossed[0, 1],),
    )[0]
    grad_gains, grad_shifts, grad_fc1_bias, grad_qv_bias = kernel_call(
        functools.partial(vector_place_kernel, depth, head_dim),
        [
            (norm_gains.shape, f32),
            (shifts.shape, f32),
            (fc1_bias.shape, f32),
            (qv_bias.shape, f32),
        ],
        mine,
        swap_core(mine),
        name="vector_place",
    )
    grad_inputs, outputs = (
        kernel_call(
            place_rows_kernel,
            [saved(inputs.shape, f32)],
            Far(own),
            other,
            name="place_rows",
            scratch=[DMA((2,))],
        )[0]
        for own, other in zip((upstream, outputs_own), others)
    )
    placed = kernel_call(
        functools.partial(place_kernel, depth, hidden, feats),
        [saved(v.shape, f32) for v in (w_qkv, w_out, w_fc1, w_fc2)],
        *[piece for l in range(depth) for kind in (0, 1) for piece in pieces[l, kind]],
        name="place",
        limit=24,
        scratch=[
            pltpu.VMEM((depth, GROUP, width_own, hidden), f32),
            pltpu.VMEM((depth, GROUP, hidden, width_own), f32),
            pltpu.VMEM((depth, GROUP, 3, width_own, feats), f32),
            pltpu.VMEM((depth, GROUP, feats, width_own), f32),
            DMA((16 * depth,)),
        ],
    )
    return (
        outputs,
        grad_inputs,
        grad_gains,
        grad_shifts,
        grad_qv_bias,
        grad_fc1_bias,
        *placed,
    )


def solution(mesh):
    rows = P("fsdp", "ctx", None)
    params = (
        P(None, None, "fsdp"),
        P(None, None, "fsdp"),
        P(None, None, "tp", "fsdp"),
        P(None, "tp", "fsdp"),
        P(None, None, "fsdp", "tp"),
        P(None, "tp", "fsdp"),
        P(None, "fsdp", "tp"),
        P(None, "tp", "fsdp"),
    )
    return jax.shard_map(
        per_device,
        mesh=mesh,
        in_specs=(rows, P("fsdp", None), rows) + params,
        out_specs=(rows, rows) + params,
        check_vma=False,
    )
```

```python
import functools
import math

import jax
import jax.numpy as jnp
from jax import lax
from jax.experimental import pallas as pl
from jax.experimental.pallas import tpu as pltpu
from jax.sharding import PartitionSpec as P

NORM_EPSILON = 1e-06
MASK_FILL = -1e30
ROOT_HALF = 0.7071067811865476
INV_ROOT_TAU = 0.3989422804014327
GROUP = 4
ORDER = (0, 5, 4, 1, 2, 7, 6, 3)
CHIPS = 4

bf16 = jnp.bfloat16
f32 = jnp.float32
VMEM = pl.BlockSpec(memory_space=pltpu.VMEM)
SMEM = pl.BlockSpec(memory_space=pltpu.SMEM)
HBM = pl.BlockSpec(memory_space=pltpu.HBM)
DMA = pltpu.SemaphoreType.DMA
TOKEN = ((8, 128), f32)


def dot(a, b):
    return lax.dot_general(a, b, (((1,), (0,)), ((), ())), preferred_element_type=f32)


def dot_nt(a, b):
    return lax.dot_general(a, b, (((1,), (1,)), ((), ())), preferred_element_type=f32)


def dot_tn(a, b):
    return lax.dot_general(a, b, (((0,), (0,)), ((), ())), preferred_element_type=f32)


class Far:
    def __init__(self, value):
        self.value = value


class Scalars:
    def __init__(self, value):
        self.value = value


def saved(shape, dtype):
    return pltpu.HBM(shape, dtype)


def kernel_call(body, outs, *args, name, limit=12, scratch=(), after=(), aliases=None, us=0):
    values, specs = [], []
    for arg in (*args, *after):
        if isinstance(arg, Far):
            values.append(pltpu.with_memory_space_constraint(arg.value, pltpu.HBM))
            specs.append(HBM)
        elif isinstance(arg, Scalars):
            values.append(arg.value)
            specs.append(SMEM)
        else:
            values.append(arg)
            specs.append(VMEM)
    first, last = len(args), len(args) + len(after)

    def run(*refs):
        body(*refs[:first], *refs[last:])

    out_shape, out_specs = [], []
    for out in outs:
        if isinstance(out, tuple):
            out_shape.append(jax.ShapeDtypeStruct(*out))
            out_specs.append(VMEM)
        else:
            out_shape.append(out)
            out_specs.append(HBM)
    return pl.pallas_call(
        run,
        out_shape=out_shape,
        in_specs=specs,
        out_specs=out_specs,
        scratch_shapes=list(scratch),
        input_output_aliases=aliases or {},
        compiler_params=pltpu.CompilerParams(vmem_limit_bytes=limit << 20),
        cost_estimate=pl.CostEstimate(flops=us * 10**9, bytes_accessed=0, transcendentals=0),
        name=name,
    )(*values)


def start_copies(pairs, sems):
    copies = [
        pltpu.make_async_copy(source, target, sems.at[k])
        for k, (source, target) in enumerate(pairs)
    ]
    for copy in copies:
        copy.start()
    return copies


def row_mean(value):
    return jnp.mean(value, axis=-1, keepdims=True)


def normalize(values):
    center = values - row_mean(values)
    inverse = lax.rsqrt(row_mean(center * center) + NORM_EPSILON)
    return center * inverse, inverse


def lanes_of(head, head_dim, width):
    lane = lax.broadcasted_iota(jnp.int32, (1, width), 1)
    return (lane >= head * head_dim) & (lane < (head + 1) * head_dim)


def assemble(chunks, target):
    rows = chunks[0].shape[0]
    for k, chunk in enumerate(chunks):
        target[k * rows : (k + 1) * rows, :] = chunk[...]


def only(flag, value):
    return jnp.where(flag, value, jnp.zeros_like(value))


def shards(weights):
    if len(weights) == 1:
        rows = weights[0].shape[0]
        return [(pl.ds(0, rows), weights[0])]
    count = len(weights)
    rows = weights[0].shape[0]
    f = lax.axis_index("fsdp")
    found = []
    for d, ref in enumerate(weights):
        place = lax.rem(f + (count - d), count)
        found.append((pl.ds(pl.multiple_of(place * rows, rows), rows), ref))
    return found


def pack_attn_kernel(layer, feats, qkv_hbm, out_hbm, packed_ref, token, qkv, out, sems):
    ci = lax.rem(lax.axis_index("ctx"), GROUP)
    span = pl.ds(pl.multiple_of(ci * feats, feats), feats)
    copies = start_copies(
        [(qkv_hbm.at[layer, :, :, span], qkv), (out_hbm.at[layer, span, :], out)], sems
    )
    copies[0].wait()
    for k in range(3):
        packed_ref[:, k * feats : (k + 1) * feats] = qkv[k]
    copies[1].wait()
    packed_ref[:, 3 * feats :] = out[...].T
    token[...] = jnp.zeros_like(token)


def pack_mlp_kernel(layer, hidden, fc1_hbm, fc2_hbm, packed_ref, token, fc1, fc2, sems):
    ci = lax.rem(lax.axis_index("ctx"), GROUP)
    span = pl.ds(pl.multiple_of(ci * hidden, hidden), hidden)
    copies = start_copies(
        [(fc1_hbm.at[layer, :, span], fc1), (fc2_hbm.at[layer, span, :], fc2)], sems
    )
    copies[0].wait()
    packed_ref[:, :hidden] = fc1[...]
    copies[1].wait()
    packed_ref[:, hidden:] = fc2[...].T
    token[...] = jnp.zeros_like(token)


def prep_upstream_kernel(tp, outer, lengths, cotangent_hbm,
                         upstream_hbm, upstream_b_ref, usable_ref, mask_ref,
                         rows_in, upstream_ref, sems):
    rows = rows_in.shape[0]
    c = lax.axis_index("ctx")
    t = lax.axis_index("tp")
    place = lax.rem(c, GROUP) * tp + t
    start = pl.multiple_of(t * rows, rows)
    copies = start_copies(
        [(cotangent_hbm.at[0, pl.ds(start, rows), :], rows_in)], sems.at[pl.ds(0, 1)]
    )
    lane = lax.broadcasted_iota(jnp.int32, usable_ref.shape, 1)
    limit = jnp.zeros(usable_ref.shape, jnp.int32)
    for o in range(outer):
        for k, d in enumerate(ORDER):
            source = place ^ d
            first_lane = (o * len(ORDER) + k) * rows
            count = lengths[0, o * GROUP + lax.div(source, tp)] - lax.rem(source, tp) * rows
            limit = jnp.where(lane >= first_lane, first_lane + jnp.clip(count, 0, rows), limit)
    usable_ref[...] = jnp.where(lane < limit, 1.0, 0.0)
    row = lax.broadcasted_iota(jnp.int32, mask_ref.shape, 0)
    mask = jnp.where(row + start < lengths[0, c], 1.0, 0.0)
    mask_ref[...] = mask
    copies[0].wait()
    upstream = rows_in[...] * mask[:, 0:1]
    upstream_ref[...] = upstream
    sent = start_copies([(upstream_ref, upstream_hbm)], sems.at[pl.ds(1, 1)])
    upstream_b_ref[...] = upstream.astype(bf16)
    sent[0].wait()


def prep_first_kernel(depth, inputs_hbm, vecs, stream_ref, first_ref, sems):
    rows = stream_ref.shape[0]
    start = pl.multiple_of(lax.axis_index("tp") * rows, rows)
    copies = start_copies([(inputs_hbm.at[0, pl.ds(start, rows), :], stream_ref)], sems)
    copies[0].wait()
    normed, _ = normalize(stream_ref[...])
    shift = vecs[2 * depth : 2 * depth + 1, :]
    first_ref[...] = (normed * vecs[0:1, :] + shift).astype(bf16)


def keep_rows_kernel(*refs):
    chunks, (near_hbm, far_hbm, token, near, far, sems) = refs[:8], refs[8:]
    assemble(chunks[:4], near)
    assemble(chunks[4:], far)
    for copy in start_copies([(near, near_hbm), (far, far_hbm)], sems):
        copy.wait()
    token[...] = jnp.zeros_like(token)


def qkv_kernel(feats, weight_count, *refs):
    c0, c1, c2, c3, *rest = refs
    weights = rest[:weight_count]
    bias, qkv_ref, x = rest[weight_count:]
    assemble((c0, c1, c2, c3), x)
    qkv = sum(dot(x[:, span], w[:, : 3 * feats]) for span, w in shards(weights))
    qkv_ref[:, :feats] = (qkv[:, :feats] + bias[0:1, :]).astype(bf16)
    qkv_ref[:, feats : 2 * feats] = qkv[:, feats : 2 * feats].astype(bf16)
    qkv_ref[:, 2 * feats :] = (qkv[:, 2 * feats :] + bias[1:2, :]).astype(bf16)


def attn_kernel(feats, heads, weight_count, part_count, keep_count, tile, *refs):
    q_ref, *rest = refs
    parts = rest[:part_count]
    weights = rest[part_count : part_count + weight_count]
    rest = rest[part_count + weight_count :]
    usable, *rest = rest
    kept, rest = rest[:keep_count], rest[keep_count:]
    partial_ref, attended_hbm, norm_hbm, *rest = rest
    kept_hbm, rest = rest[:keep_count], rest[keep_count:]
    keys, values, attended_ref, norm_ref, sems = rest
    head_dim = feats // heads
    scale = 1.0 / math.sqrt(head_dim)
    copies = start_copies(list(zip(kept, kept_hbm)), sems)
    first = 0
    for part in parts:
        rows, width = part.shape
        keys[first : first + rows, :] = part[:, width - 2 * feats : width - feats]
        values[first : first + rows, :] = part[:, width - feats :]
        first += rows
    keep = usable[...] > 0.5
    rows = q_ref.shape[0]
    for first in range(0, rows, tile):
        span = slice(first, first + tile)
        q = q_ref[span, :feats]
        attended = None
        for h in range(heads):
            own = lanes_of(h, head_dim, feats)
            scores = dot_nt(only(own, q), keys[...]) * scale
            scores = jnp.where(keep, scores, MASK_FILL)
            highest = jnp.max(scores, axis=-1, keepdims=True)
            raised = jnp.exp(scores - highest)
            total = jnp.sum(raised, axis=-1, keepdims=True)
            soft = (raised * (1.0 / total)).astype(bf16)
            result = dot(soft, values[...])
            log_norm = jnp.broadcast_to(highest + jnp.log(total), (tile, feats))
            if attended is None:
                attended, norms = result, log_norm
            else:
                attended = jnp.where(own, result, attended)
                norms = jnp.where(own, log_norm, norms)
        attended_ref[span, :] = attended.astype(bf16)
        norm_ref[span, :] = norms
    copies += start_copies(
        [(attended_ref, attended_hbm), (norm_ref, norm_hbm)],
        sems.at[pl.ds(keep_count, 2)],
    )
    for span, w in shards(weights):
        partial_ref[:, span] = dot_nt(attended_ref[...], w[:, 3 * feats :]).astype(bf16)
    for copy in copies:
        copy.wait()


def core_sum_kernel(count, *refs):
    pairs, owns = refs[: 2 * count], refs[2 * count : 3 * count]
    peers = refs[3 * count :]
    rows = owns[0].shape[0]
    for j in range(count):
        near, far = pairs[2 * j], pairs[2 * j + 1]
        for k in range(1 + len(peers)):
            span = slice(k * rows, (k + 1) * rows)
            total = near[span, :].astype(f32) + far[span, :].astype(f32)
            if k == 0:
                owns[j][...] = total
            else:
                peers[k - 1][j * rows : (j + 1) * rows, :] = total.astype(bf16)


def total_of(own, xy, x, y, part=0):
    rows = own.shape[0]
    span = slice(part * rows, (part + 1) * rows)
    return (
        own[...] + y[span, :].astype(f32) + x[span, :].astype(f32) + xy[span, :].astype(f32)
    )


def sum_norm_kernel(bias_row, gain_row, shift_row, own, xy, x, y, residual_hbm, vecs,
                    stream_ref, normed_ref, residual, sems):
    copies = start_copies([(residual_hbm, residual)], sems)
    total = total_of(own, xy, x, y) + vecs[bias_row : bias_row + 1, :]
    copies[0].wait()
    stream = residual[...] + total
    stream_ref[...] = stream
    normed, _ = normalize(stream)
    gain = vecs[gain_row : gain_row + 1, :]
    normed_ref[...] = (normed * gain + vecs[shift_row : shift_row + 1, :]).astype(bf16)


def sum_out_kernel(bias_row, own, xy, x, y, residual_hbm, vecs, mask, out_hbm, token,
                   residual, out_ref, sems):
    copies = start_copies([(residual_hbm, residual)], sems.at[pl.ds(0, 1)])
    total = total_of(own, xy, x, y, 1) + vecs[bias_row : bias_row + 1, :]
    copies[0].wait()
    out_ref[...] = (residual[...] + total) * mask[:, 0:1]
    token[...] = jnp.zeros_like(token)
    for copy in start_copies([(out_ref, out_hbm)], sems.at[pl.ds(1, 1)]):
        copy.wait()


def mlp_kernel(hidden, keep_count, saves, c0, c1, c2, c3, w, bias, *refs):
    kept, rest = refs[:keep_count], refs[keep_count:]
    partial_ref, x_out, act_out, slope_out, *rest = rest
    kept_hbm, rest = rest[:keep_count], rest[keep_count:]
    if saves:
        x, act_ref, slope_ref, sems = rest
    else:
        x, act_ref, slope_ref = x_out, act_out, slope_out
        (sems,) = rest
    copies = start_copies(list(zip(kept, kept_hbm)), sems)
    assemble((c0, c1, c2, c3), x)
    if saves:
        copies += start_copies([(x, x_out)], sems.at[pl.ds(keep_count, 1)])
    block = hidden // 2
    for k in range(2):
        span = slice(k * block, (k + 1) * block)
        pre = dot(x[...], w[:, span]) + bias[:, span]
        cdf = 0.5 * (1.0 + lax.erf(pre * ROOT_HALF))
        density = jnp.exp(-0.5 * pre * pre) * INV_ROOT_TAU
        slope_ref[k] = cdf + pre * density
        act_ref[:, span] = (pre * cdf).astype(bf16)
        if saves:
            copies += start_copies(
                [(slope_ref.at[k], slope_out.at[k])], sems.at[pl.ds(1 + keep_count + k, 1)]
            )
    if saves:
        copies += start_copies([(act_ref, act_out)], sems.at[pl.ds(3 + keep_count, 1)])
    partial_ref[...] = dot_nt(act_ref[...], w[:, hidden:]).astype(bf16)
    for copy in copies:
        copy.wait()


def mlp_back_kernel(hidden, chunk_count, *refs):
    chunks, (w, slope_hbm, *rest) = refs[:chunk_count], refs[chunk_count:]
    partial_ref, grad_ref, sum_hbm, x, slope, sum_ref, sems = rest
    copies = start_copies([(slope_hbm, slope)], sems)
    if chunk_count == 1:
        copies += start_copies([(chunks[0], x)], sems.at[pl.ds(1, 1)])
        copies[1].wait()
    else:
        assemble(chunks, x)
    grad = dot(x[...], w[:, hidden:])
    copies[0].wait()
    block = hidden // 2
    for k in range(2):
        span = slice(k * block, (k + 1) * block)
        part = grad[:, span] * slope[k]
        grad_ref[:, span] = part.astype(bf16)
        sum_ref[:, span] = jnp.sum(part, axis=0, keepdims=True)
    sent = start_copies([(sum_ref, sum_hbm)], sems.at[pl.ds(2, 1)])
    partial_ref[...] = dot_nt(grad_ref[...], w[:, :hidden]).astype(bf16)
    sent[0].wait()


def mlp_grad_kernel(hidden, second_near, second_far, act_near, act_far, up_near, up_far,
                    grad_near, grad_far, passed, sums, middle, out_hbm, passed_ref, sums_hbm,
                    middle_hbm, second, act, up, grad, out_one, out_two, sems):
    rows = up_near.shape[0]
    sent = start_copies([(sums, sums_hbm), (middle, middle_hbm)], sems.at[pl.ds(6, 2)])
    near, far = pl.ds(0, rows), pl.ds(rows, rows)
    copies = start_copies(
        [
            (act_near, act.at[near]),
            (act_far, act.at[far]),
            (second_near, second.at[near]),
            (second_far, second.at[far]),
        ],
        sems,
    )
    passed_ref[...] = passed[...]
    up[:rows, :] = up_near[...]
    up[rows:, :] = up_far[...]
    grad[:rows, :] = grad_near[...]
    grad[rows:, :] = grad_far[...]
    for copy in copies[:2]:
        copy.wait()
    out_two[...] = dot_tn(up[...], act[...]).astype(bf16)
    sent += start_copies(
        [(out_two, out_hbm.at[:, pl.ds(hidden, hidden)])], sems.at[pl.ds(4, 1)]
    )
    for copy in copies[2:]:
        copy.wait()
    out_one[...] = dot_tn(second[...], grad[...]).astype(bf16)
    sent += start_copies([(out_one, out_hbm.at[:, pl.ds(0, hidden)])], sems.at[pl.ds(5, 1)])
    for copy in sent:
        copy.wait()


def norm_back(upstream, values, gain):
    normed, inverse = normalize(values)
    scaled = upstream * gain
    back = inverse * (scaled - row_mean(scaled) - normed * row_mean(scaled * normed))
    gain_grad = jnp.sum(upstream * normed, axis=0, keepdims=True)
    return back, gain_grad, jnp.sum(upstream, axis=0, keepdims=True)


def norm_back_two_kernel(gain_row, own, xy, x, y, values_hbm, upstream_hbm, vecs,
                         grad_ref, grad_b_ref, sums_ref, values, upstream, sems):
    copies = start_copies([(values_hbm, values), (upstream_hbm, upstream)], sems)
    total = total_of(own, xy, x, y)
    for copy in copies:
        copy.wait()
    up = upstream[...]
    back, gain_grad, shift_grad = norm_back(
        total, values[...], vecs[gain_row : gain_row + 1, :]
    )
    grad = up + back
    grad_ref[...] = grad
    grad_b_ref[...] = grad.astype(bf16)
    sums_ref[0:1, :] = gain_grad
    sums_ref[1:2, :] = shift_grad
    sums_ref[2:3, :] = jnp.sum(grad, axis=0, keepdims=True)
    sums_ref[3:4, :] = jnp.sum(up, axis=0, keepdims=True)


def norm_back_one_kernel(gain_row, own, xy, x, y, values_hbm, upstream_hbm, vecs, mask,
                         grad_ref, grad_b_ref, sums_ref, values, upstream, sems):
    copies = start_copies([(values_hbm, values), (upstream_hbm, upstream)], sems)
    total = total_of(own, xy, x, y)
    for copy in copies:
        copy.wait()
    back, gain_grad, shift_grad = norm_back(
        total, values[...], vecs[gain_row : gain_row + 1, :]
    )
    grad = upstream[...] + back
    if mask is not None:
        grad = grad * mask[:, 0:1]
    grad_ref[...] = grad
    grad_b_ref[...] = grad.astype(bf16)
    sums_ref[0:1, :] = gain_grad
    sums_ref[1:2, :] = shift_grad


def attn_back_kernel(feats, heads, weight_count, part_count, tile, carried, *refs):
    c0, c1, c2, c3, *rest = refs
    weights, rest = rest[:weight_count], rest[weight_count:]
    usable, q_hbm, attended_hbm, norm_hbm, *rest = rest
    parts, rest = rest[:part_count], rest[part_count:]
    if carried:
        keys_before, values_before, *rest = rest
    x, grad_q, grad_k, grad_v, pairs, q_ref, attended, norms, grad_att, sems = rest
    head_dim = feats // heads
    scale = 1.0 / math.sqrt(head_dim)
    moves = [(q_hbm.at[:, pl.ds(0, feats)], q_ref), (attended_hbm, attended), (norm_hbm, norms)]
    first = 0
    for part in parts:
        rows, width = part.shape
        moves.append(
            (part.at[:, pl.ds(width - 2 * feats, 2 * feats)], pairs.at[pl.ds(first, rows)])
        )
        first += rows
    copies = start_copies(moves, sems)
    assemble((c0, c1, c2, c3), x)
    grad_att[...] = sum(
        dot(x[:, span], w[:, 3 * feats :]) for span, w in shards(weights)
    ).astype(bf16)
    keep = usable[...] > 0.5
    rows = q_ref.shape[0]
    if carried:
        sum_k, sum_v = keys_before[...], values_before[...]
    else:
        sum_k = jnp.zeros(grad_k.shape, f32)
        sum_v = jnp.zeros(grad_v.shape, f32)
    for copy in copies:
        copy.wait()
    keys, values = pairs[:, :feats], pairs[:, feats:]
    for first in range(0, rows, tile):
        span = slice(first, first + tile)
        q = q_ref[span, :]
        ga = grad_att[span, :]
        products = ga.astype(f32) * attended[span, :].astype(f32)
        gq = None
        for h in range(heads):
            own = lanes_of(h, head_dim, feats)
            q_h = only(own, q)
            ga_h = only(own, ga)
            row_dots = jnp.sum(only(own, products), axis=-1, keepdims=True)
            scores = dot_nt(q_h, keys) * scale
            scores = jnp.where(keep, scores, MASK_FILL)
            soft = jnp.exp(scores - norms[span, h * head_dim : h * head_dim + 1])
            grad_soft = dot_nt(ga_h, values)
            grad_scores = (soft * (grad_soft - row_dots)).astype(bf16)
            part = dot(grad_scores, keys)
            gq = part if gq is None else jnp.where(own, part, gq)
            sum_k = sum_k + dot_tn(grad_scores, q_h) * scale
            sum_v = sum_v + dot_tn(soft.astype(bf16), ga_h)
        grad_q[span, :] = gq * scale
    grad_k[...] = sum_k
    grad_v[...] = sum_v


def project_kernel(feats, first, weight_count, gq, gk, gv, *refs):
    weights, (partial_ref, packed) = refs[:weight_count], refs[weight_count:]
    rows = gq.shape[0]
    span = slice(first, first + rows)
    packed[:, :feats] = gq[...].astype(bf16)
    packed[:, feats : 2 * feats] = gk[span, :].astype(bf16)
    packed[:, 2 * feats :] = gv[span, :].astype(bf16)
    for columns, w in shards(weights):
        partial_ref[:, columns] = dot_nt(packed[...], w[:, : 3 * feats]).astype(bf16)


def attn_grad_kernel(feats, count, first_near, first_far, att_near, att_far, up_near, up_far,
                     gq_near, gq_far, gk, gv, passed, sums, stream, lines, *refs):
    outs, rest = refs[:count], refs[count:]
    heads_hbm, passed_ref, sums_hbm, stream_hbm, *rest = rest
    first, att, up, packed, sums_ref, *staged, sems = rest
    rows = up_near.shape[0]
    sent = start_copies([(sums, sums_hbm), (stream, stream_hbm)], sems.at[pl.ds(6, 2)])
    near, far = pl.ds(0, rows), pl.ds(rows, rows)
    copies = start_copies(
        [
            (att_near, att.at[near]),
            (att_far, att.at[far]),
            (first_near, first.at[near]),
            (first_far, first.at[far]),
        ],
        sems,
    )
    passed_ref[...] = passed[...]
    up[:rows, :] = up_near[...]
    up[rows:, :] = up_far[...]
    packed[:rows, :feats] = gq_near[...].astype(bf16)
    packed[rows:, :feats] = gq_far[...].astype(bf16)
    packed[:, feats : 2 * feats] = gk[...].astype(bf16)
    packed[:, 2 * feats :] = gv[...].astype(bf16)
    sums_ref[0:1, :] = jnp.sum(gq_near[...], axis=0, keepdims=True) + jnp.sum(
        gq_far[...], axis=0, keepdims=True
    )
    sums_ref[1:2, :] = jnp.sum(gv[...], axis=0, keepdims=True)
    sent += start_copies([(sums_ref, heads_hbm)], sems.at[pl.ds(8, 1)])
    if count == 1:
        out_one, out_two = staged
        for copy in copies[:2]:
            copy.wait()
        out_two[...] = dot_tn(up[...], att[...]).astype(bf16)
        sent += start_copies(
            [(out_two, outs[0].at[:, pl.ds(3 * feats, feats)])], sems.at[pl.ds(4, 1)]
        )
        for copy in copies[2:]:
            copy.wait()
        out_one[...] = dot_tn(first[...], packed[...]).astype(bf16)
        sent += start_copies(
            [(out_one, outs[0].at[:, pl.ds(0, 3 * feats)])], sems.at[pl.ds(5, 1)]
        )
        for copy in sent:
            copy.wait()
        return
    (stage,) = staged
    for copy in copies:
        copy.wait()
    below = lines.shape[1]
    width_own = outs[0].shape[0] - below
    for d in reversed(range(count)):
        place = lax.rem(lax.axis_index("fsdp") + d, count)
        span = pl.ds(pl.multiple_of(place * width_own, width_own), width_own)
        stage[d, :width_own, : 3 * feats] = dot_tn(first[:, span], packed[...]).astype(bf16)
        stage[d, :width_own, 3 * feats :] = dot_tn(up[:, span], att[...]).astype(bf16)
        stage[d, width_own:, :] = lines[d]
        sent += start_copies([(stage.at[d], outs[d])], sems.at[pl.ds(9 + d, 1)])
    for copy in sent:
        copy.wait()


def settle_kernel(passed, *refs):
    passed_ref = refs[-1]
    passed_ref[...] = passed[...]


def fetch_kernel(count, *refs):
    sources, (target, sems) = refs[:count], refs[count:]
    columns = target.shape[1]
    moves = []
    row = 0
    for source in sources:
        rows = source.shape[0]
        for first in range(0, source.shape[1], columns):
            moves.append(
                (source.at[:, pl.ds(first, columns)], target.at[pl.ds(row, rows), :])
            )
            row += rows
    for copy in start_copies(moves, sems):
        copy.wait()


def shard_sum_kernel(depth, own_hbm, *refs):
    *others, part_ref, mine_ref, own, sems = refs
    (copy,) = start_copies([(own_hbm, own)], sems)
    copy.wait()
    rows, width = part_ref.shape[0], mine_ref.shape[1]
    terms = [ref[...].astype(f32) for ref in (own, *others)]
    total = terms[0]
    for term in terms[1:]:
        total = total + term
    part_ref[...] = total[:rows, :].astype(bf16)
    lines = total[rows:, :width] + total[rows:, width:]
    mine_ref[: 6 * depth, :] = lines[: 6 * depth, :]
    for k in range(mine_ref.shape[0] - 16):
        mine_ref[16 + k : 17 + k, :] = lines[6 * depth + k : 6 * depth + k + 1, :]


def place_kernel(depth, hidden, feats, *refs):
    slices = [(refs[k], refs[GROUP + k]) for k in range(GROUP)]
    qkv_hbm, out_hbm, fc1_hbm, fc2_hbm, fc1, fc2, qkv, out, sems = refs[2 * GROUP :]
    ci = lax.rem(lax.axis_index("ctx"), GROUP)
    rows = fc1.shape[2]
    copies = []

    def send(source, target):
        copies.extend(start_copies([(source, target)], sems.at[pl.ds(len(copies), 1)]))

    for l in range(depth):
        for k in range(GROUP):
            _, stacked = slices[k]
            first = 0 if l == 0 else (3 * l - 1) * rows
            span = pl.ds(pl.multiple_of((ci ^ k) * hidden, hidden), hidden)
            fc1[l, k] = stacked[first : first + rows, :].astype(f32)
            send(fc1.at[l, k], fc1_hbm.at[l, :, span])
            fc2[l, k] = stacked[first + rows : first + 2 * rows, :].T.astype(f32)
            send(fc2.at[l, k], fc2_hbm.at[l, span, :])
    for l in reversed(range(depth)):
        for k in range(GROUP):
            alone, stacked = slices[k]
            piece = alone if l == 0 else stacked.at[pl.ds((3 * l + 1) * rows, rows), :]
            span = pl.ds(pl.multiple_of((ci ^ k) * feats, feats), feats)
            for j in range(3):
                qkv[l, k, j] = piece[:, j * feats : (j + 1) * feats].astype(f32)
            send(qkv.at[l, k], qkv_hbm.at[l, :, :, span])
            out[l, k] = piece[:, 3 * feats :].T.astype(f32)
            send(out.at[l, k], out_hbm.at[l, span, :])
    for copy in copies:
        copy.wait()


def vector_pack_kernel(depth, one_now, gq_near, gq_far, gv, *refs):
    count = 5 * depth - 2
    out_ref, *found, sems = refs[count:]
    copies = start_copies(list(zip(refs[:count], found)), sems)
    out_ref[...] = jnp.zeros_like(out_ref)
    feats = gv.shape[1]
    head_now = [
        jnp.sum(gq_near[...], axis=0, keepdims=True) + jnp.sum(gq_far[...], axis=0, keepdims=True),
        jnp.sum(gv[...], axis=0, keepdims=True),
    ]
    for copy in copies:
        copy.wait()
    for l in range(depth):
        if l == 0:
            one, (two, unit_near, unit_far) = one_now, found[:3]
            heads = head_now
        else:
            one, two, unit_near, unit_far, head = found[5 * l - 2 : 5 * l + 3]
            heads = [head[0:1, :], head[1:2, :]]
        out_ref[6 * l : 6 * l + 1, :] = one[0:1, :]
        out_ref[6 * l + 1 : 6 * l + 2, :] = two[0:1, :]
        out_ref[6 * l + 2 : 6 * l + 3, :] = one[1:2, :]
        out_ref[6 * l + 3 : 6 * l + 6, :] = two[1:4, :]
        units = unit_near.shape[1]
        row = 6 * depth
        out_ref[row : row + 1, l * units : (l + 1) * units] = unit_near[...] + unit_far[...]
        for j in range(2):
            start = (2 * l + j) * feats
            out_ref[row + 1 : row + 2, start : start + feats] = heads[j]


def vector_lines_kernel(depth, width_own, packed, lines_ref):
    count = lines_ref.shape[0]
    f = lax.axis_index("fsdp")
    total = packed[...]
    high = total.astype(bf16).astype(f32)
    low = total - high
    lines_ref[...] = jnp.zeros_like(lines_ref)
    last = 6 * depth
    for k, value in enumerate((high, low)):
        lanes = slice(k * width_own, (k + 1) * width_own)
        columns = [value[:, a * width_own : (a + 1) * width_own] for a in range(count)]
        for d in range(count):
            mine = columns[0]
            for a in range(1, count):
                mine = jnp.where(lax.rem(f + d, count) == a, columns[a], mine)
            rows = [mine[:last, :]]
            for r in range(2):
                for a in range(count):
                    rows.append(columns[a][last + r : last + r + 1, :])
            rows.append(jnp.zeros((lines_ref.shape[1] - last - 2 * count, width_own), f32))
            lines_ref[d, :, lanes] = jnp.concatenate(rows, axis=0).astype(bf16)


def vector_plane_kernel(depth, own, xy, x, y, out_ref):
    last = 6 * depth
    out_ref[:last, :] = own[:last, :] + xy[:last, :] + x[:last, :] + y[:last, :]
    out_ref[16:24, :] = own[16:24, :]
    out_ref[24:32, :] = x[16:24, :]


def vector_place_kernel(depth, head_dim, own, far, gains_ref, shifts_ref, unit_ref, heads_ref):
    total = own[: 6 * depth, :] + far[: 6 * depth, :]
    for l in range(depth):
        gains_ref[l] = total[6 * l : 6 * l + 2, :]
        shifts_ref[l] = total[6 * l + 2 : 6 * l + 6, :]
    pieces = (own[16:24, :], far[16:24, :], own[24:32, :], far[24:32, :])
    ci = lax.rem(lax.axis_index("ctx"), GROUP)
    f = lax.axis_index("fsdp")

    def of_place(c):
        k = ci ^ c
        found = pieces[0]
        for j in range(1, GROUP):
            found = jnp.where(k == j, pieces[j], found)
        return found

    width_own = own.shape[1]
    units = of_place(f)
    parts = unit_ref.shape[2] // width_own
    for l in range(depth):
        for j in range(parts):
            row = l * parts + j
            unit_ref[l, :, j * width_own : (j + 1) * width_own] = units[row : row + 1, :]
    head_own = heads_ref.shape[3]
    heads = heads_ref.shape[2] // GROUP
    for c in range(GROUP):
        found = of_place(c)
        for l in range(depth):
            for j in range(2):
                for h in range(heads):
                    first = ((2 * l + j) * heads + h) * head_dim
                    row, lane = 4 + first // width_own, first % width_own
                    value = found[row : row + 1, lane : lane + head_own]
                    for a in range(1, head_dim // head_own):
                        start = lane + a * head_own
                        value = jnp.where(
                            f == a, found[row : row + 1, start : start + head_own], value
                        )
                    heads_ref[l, j, c * heads + h : c * heads + h + 1, :] = value


def place_rows_kernel(own, other, out_hbm, sems):
    rows = own.shape[0]
    start = pl.multiple_of(lax.axis_index("tp") * rows, rows)
    copies = start_copies(
        [
            (own, out_hbm.at[0, pl.ds(start, rows), :]),
            (other, out_hbm.at[0, pl.ds(pl.multiple_of(rows - start, rows), rows), :]),
        ],
        sems,
    )
    for copy in copies:
        copy.wait()


def per_device(
    inputs, lengths, cotangent, norm_gains, shifts, qv_bias, fc1_bias, w_qkv, w_out, w_fc1, w_fc2
):
    depth = w_qkv.shape[0]
    width_own = w_qkv.shape[2]
    fsdp = lax.axis_size("fsdp")
    tp = lax.axis_size("tp")
    ctx = lax.axis_size("ctx")
    outer = ctx // GROUP
    rows = inputs.shape[1] // tp
    half = rows * CHIPS
    all_rows = 2 * half
    head_own = qv_bias.shape[3]
    head_dim = head_own * fsdp
    heads = qv_bias.shape[2] // GROUP
    feats = heads * head_dim
    hidden = w_fc1.shape[2] // GROUP
    width = width_own * fsdp
    t = lax.axis_index("tp")
    f = lax.axis_index("fsdp")
    ci = lax.axis_index("ctx") % GROUP
    tile = half // 2
    attn_limit = 12 if outer == 1 else 48

    def swap_core(value):
        return lax.ppermute(value, "ctx", [(i, i ^ 1) for i in range(ctx)])

    def swap_x(value):
        return lax.ppermute(value, "ctx", [(i, i ^ 2) for i in range(ctx)])

    def swap_y(value):
        return lax.ppermute(value, "tp", [(i, i ^ 1) for i in range(tp)])

    def swap_xy(value):
        pairs = [
            (i * tp + k, (i ^ 2) * tp + (k ^ 1)) for i in range(ctx) for k in range(tp)
        ]
        return lax.ppermute(value, ("ctx", "tp"), pairs)

    def shift_z(value, d):
        return lax.ppermute(value, "fsdp", [(i, (i + d) % fsdp) for i in range(fsdp)])

    outer_groups = [[o * GROUP + i for o in range(outer)] for i in range(GROUP)]

    def gather_rows(own):
        near = (own, swap_xy(own), swap_x(own), swap_y(own))
        return near, tuple(swap_core(chunk) for chunk in near)

    def settle(value, *after):
        return kernel_call(
            settle_kernel, [(value.shape, value.dtype)], value, name="settle", after=after
        )[0]

    def reduce_rows(*pairs, after=()):
        count = len(pairs)
        *owns, xy, x, y = kernel_call(
            functools.partial(core_sum_kernel, count),
            [((rows, width), f32)] * count + [((count * rows, width), bf16)] * 3,
            *[v for near, far in pairs for v in (near, swap_core(far))],
            name="core_sum",
            after=after,
        )
        peers = (swap_xy(xy), swap_x(x), swap_y(y))
        return [(own, *peers) for own in owns]

    def pack_attn(l, after):
        return kernel_call(
            functools.partial(pack_attn_kernel, l, feats),
            [((width_own, 4 * feats), bf16), TOKEN],
            Far(w_qkv),
            Far(w_out),
            name="pack_attn",
            after=after,
            scratch=[
                pltpu.VMEM((3, width_own, feats), bf16),
                pltpu.VMEM((feats, width_own), bf16),
                DMA((2,)),
            ],
        )

    def pack_mlp(l, after):
        return kernel_call(
            functools.partial(pack_mlp_kernel, l, hidden),
            [((width_own, 2 * hidden), bf16), TOKEN],
            Far(w_fc1),
            Far(w_fc2),
            name="pack_mlp",
            after=after,
            scratch=[
                pltpu.VMEM((width_own, hidden), bf16),
                pltpu.VMEM((hidden, width_own), bf16),
                DMA((2,)),
            ],
        )

    attn_w = []
    mlp_w = []
    token = None
    for l in range(depth):
        own, token = pack_attn(l, () if token is None else (token,))
        attn_w.append((lax.all_gather(own, "fsdp", axis=0, tiled=True),))
        own, token = pack_mlp(l, (token,))
        mlp_w.append(lax.all_gather(own, "fsdp", axis=0, tiled=True))
        if l == 0:
            pack_token = token

    qv_own = lax.dynamic_slice_in_dim(qv_bias, ci * heads, heads, axis=2)
    vec_rows = depth * 6
    c1_rows = depth * fc1_bias.shape[2] // width_own
    qv_own = qv_own.reshape(1, -1)
    small_own = jnp.concatenate(
        [
            norm_gains.reshape(-1, width_own),
            shifts.reshape(-1, width_own),
            fc1_bias.reshape(-1, width_own),
            jnp.pad(qv_own, ((0, 0), (0, width_own - qv_own.shape[1]))),
        ],
        axis=0,
    )
    shifted = [small_own] + [shift_z(small_own, d) for d in range(1, fsdp)]

    def shard(a):
        picked = shifted[0]
        for d in range(1, fsdp):
            picked = jnp.where((f - d) % fsdp == a, shifted[d], picked)
        return picked.astype(f32)

    small = [shard(a) for a in range(fsdp)]
    vecs = jnp.concatenate([s[:vec_rows] for s in small], axis=1)
    fc1_all = shard(ci)[vec_rows : vec_rows + c1_rows].reshape(depth, 1, hidden)
    qv_all = jnp.stack(
        [s[vec_rows + c1_rows, : qv_own.shape[1]].reshape(depth, 2, heads, head_own) for s in small],
        axis=3,
    ).reshape(depth, 2, feats)

    def gain_row(l, i):
        return 2 * l + i

    def shift_row(l, i):
        return 2 * depth + 4 * l + i

    key_rows = outer * all_rows
    row_f32 = ((rows, width), f32)
    row_bf16 = ((rows, width), bf16)
    upstream, upstream_b, usable, mask = kernel_call(
        functools.partial(prep_upstream_kernel, tp, outer),
        [saved((rows, width), f32), row_bf16, ((1, key_rows), f32), ((rows, 128), f32)],
        Scalars(lengths),
        Far(cotangent),
        name="prep_upstream",
        after=(pack_token,),
        scratch=[pltpu.VMEM((rows, width), f32), pltpu.VMEM((rows, width), f32), DMA((2,))],
    )
    near, far = gather_rows(upstream_b)
    half_x = pltpu.VMEM((half, width), bf16)
    *upstream_rows, upstream_token = kernel_call(
        keep_rows_kernel,
        [saved((half, width), bf16)] * 2 + [TOKEN],
        *near,
        *far,
        name="keep_rows",
        scratch=[half_x, half_x, DMA((2,))],
    )
    upstream_chunks = [(Far(x),) for x in upstream_rows]
    stream, first = kernel_call(
        functools.partial(prep_first_kernel, depth),
        [row_f32, row_bf16],
        Far(inputs),
        vecs,
        name="prep_first",
        scratch=[DMA((1,))],
    )
    first_chunks = gather_rows(first)

    partial_out = ((half, width), bf16)
    saved_all = []
    for l in range(depth):
        qkv = []
        first_x = []
        for side in (0, 1):
            qkv_half, x_half = kernel_call(
                functools.partial(qkv_kernel, feats, len(attn_w[l])),
                [((half, 3 * feats), bf16), ((half, width), bf16)],
                *first_chunks[side],
                *attn_w[l],
                qv_all[l],
                name="qkv",
                after=(upstream_token,) if l == 0 and side == 0 else (),
            )
            qkv.append(qkv_half)
            first_x.append(x_half)
        if outer > 1:
            pairs = jnp.concatenate([part[:, feats:] for part in qkv], axis=0)
            pairs = lax.all_gather(
                pairs, "ctx", axis=0, tiled=True, axis_index_groups=outer_groups
            )
            key_parts = (pairs,)
        else:
            key_parts = tuple(qkv)
        attn = [None, None]
        for side in (1, 0):
            kept = (first_x[side], qkv[side]) + ((stream,) if side == 1 else ())
            attn[side] = kernel_call(
                functools.partial(
                    attn_kernel, feats, heads, len(attn_w[l]), len(key_parts), len(kept), tile
                ),
                [partial_out, saved((half, feats), bf16), saved((half, feats), f32)]
                + [saved(k.shape, k.dtype) for k in kept],
                qkv[side],
                *key_parts,
                *attn_w[l],
                usable,
                *kept,
                name="attn",
                limit=attn_limit,
                scratch=[
                    pltpu.VMEM((key_rows, feats), bf16),
                    pltpu.VMEM((key_rows, feats), bf16),
                    pltpu.VMEM((half, feats), bf16),
                    pltpu.VMEM((half, feats), f32),
                    DMA((len(kept) + 2,)),
                ],
            )
        (sums,) = reduce_rows((attn[0][0], attn[1][0]))
        middle, second = kernel_call(
            functools.partial(sum_norm_kernel, shift_row(l, 2), gain_row(l, 1), shift_row(l, 1)),
            [row_f32, row_bf16],
            *sums,
            Far(attn[1][5]),
            vecs,
            name="sum_norm",
            scratch=[pltpu.VMEM((rows, width), f32), DMA((1,))],
        )
        second_chunks = gather_rows(second)
        mlp = [None, None]
        for side in (1, 0):
            kept = (middle,) if side == 1 else ()
            saves = l + 1 < depth
            shapes = [
                ((half, width), bf16),
                ((half, hidden), bf16),
                ((2, half, hidden // 2), f32),
            ]
            mlp[side] = kernel_call(
                functools.partial(mlp_kernel, hidden, len(kept), saves),
                [partial_out]
                + [saved(*shape) if saves else shape for shape in shapes]
                + [saved(k.shape, k.dtype) for k in kept],
                *second_chunks[side],
                mlp_w[l],
                fc1_all[l],
                *kept,
                name="mlp",
                scratch=[pltpu.VMEM(*shape) for shape in shapes if saves]
                + [DMA((4 + len(kept),))],
            )
            if saves:
                mlp[side] = [mlp[side][0], *[Far(v) for v in mlp[side][1:4]], *mlp[side][4:]]
        saved_all.append((attn, pairs if outer > 1 else None, mlp))
        if l + 1 < depth:
            (sums,) = reduce_rows((mlp[0][0], mlp[1][0]))
            stream, first = kernel_call(
                functools.partial(
                    sum_norm_kernel, shift_row(l, 3), gain_row(l + 1, 0), shift_row(l + 1, 0)
                ),
                [row_f32, row_bf16],
                *sums,
                Far(mlp[1][4]),
                vecs,
                name="sum_norm",
                scratch=[pltpu.VMEM((rows, width), f32), DMA((1,))],
            )
            first_chunks = gather_rows(first)

    def scatter_grads(grad):
        part = lax.psum_scatter(grad, "fsdp", scatter_dimension=0, tiled=True)
        if outer > 1:
            part = lax.psum(part, "ctx", axis_index_groups=outer_groups)
        return part

    row_sums = [None] * depth
    unit_sums = [None] * depth
    head_sums = [None] * depth
    mlp_parts = [None] * depth
    attn_parts = [None] * depth
    for l in reversed(range(depth)):
        attn, pairs, mlp = saved_all[l]
        back = [None, None]
        for side in (1, 0):
            back[side] = kernel_call(
                functools.partial(mlp_back_kernel, hidden, len(upstream_chunks[side])),
                [
                    partial_out,
                    ((half, hidden), bf16),
                    saved((1, hidden), f32),
                    ((half, width), bf16),
                ],
                *upstream_chunks[side],
                mlp_w[l],
                mlp[side][3],
                name="mlp_back",
                scratch=[
                    pltpu.VMEM((2, half, hidden // 2), f32),
                    pltpu.VMEM((1, hidden), f32),
                    DMA((3,)),
                ],
            )
        pairs_now = [(back[0][0], back[1][0])]
        if l + 1 == depth:
            pairs_now.append((mlp[0][0], mlp[1][0]))
        sums, *output_sums = reduce_rows(*pairs_now)
        if l + 1 == depth:
            outputs_own, output_token = kernel_call(
                functools.partial(sum_out_kernel, shift_row(l, 3)),
                [saved((rows, width), f32), TOKEN],
                *output_sums[0],
                Far(mlp[1][4]),
                vecs,
                mask,
                name="sum_out",
                scratch=[pltpu.VMEM((rows, width), f32)] * 2 + [DMA((2,))],
            )
            after = (output_token,)
        else:
            after = ()
        unit_sums[l] = (back[0][2], back[1][2])
        grad_middle, middle_b, sums_two = kernel_call(
            functools.partial(norm_back_two_kernel, gain_row(l, 1)),
            [row_f32, row_bf16, ((4, width), f32)],
            *sums,
            Far(mlp[1][4]),
            Far(upstream),
            vecs,
            name="norm_back_two",
            scratch=[pltpu.VMEM((rows, width), f32)] * 2 + [DMA((2,))],
        )
        mlp_grad, middle_b, sums_two, grad_middle = kernel_call(
            functools.partial(mlp_grad_kernel, hidden),
            [
                saved((width, 2 * hidden), bf16),
                row_bf16,
                saved((4, width), f32),
                saved((rows, width), f32),
            ],
            mlp[0][1],
            mlp[1][1],
            mlp[0][2],
            mlp[1][2],
            back[0][3],
            back[1][3],
            back[0][1],
            back[1][1],
            middle_b,
            sums_two,
            grad_middle,
            name="mlp_grad",
            after=after,
            scratch=[
                pltpu.VMEM((all_rows, width), bf16),
                pltpu.VMEM((all_rows, hidden), bf16),
                pltpu.VMEM((all_rows, width), bf16),
                pltpu.VMEM((all_rows, hidden), bf16),
                pltpu.VMEM((width, hidden), bf16),
                pltpu.VMEM((width, hidden), bf16),
                DMA((8,)),
            ],
            limit=16,
        )
        mlp_parts[l] = scatter_grads(mlp_grad)
        if l + 1 < depth:
            middle_b = settle(middle_b, Far(mlp_parts[l + 1]))
        middle_chunks = gather_rows(middle_b)
        grad_q = [None, None]
        middle_x = [None, None]
        carried = ()
        for side in (0, 1):
            key_parts = (pairs,) if outer > 1 else (attn[0][4], attn[1][4])
            middle_x[side], grad_q[side], *carried = kernel_call(
                functools.partial(
                    attn_back_kernel,
                    feats,
                    heads,
                    len(attn_w[l]),
                    len(key_parts),
                    tile,
                    len(carried) > 0,
                ),
                [
                    ((half, width), bf16),
                    ((half, feats), f32),
                    ((key_rows, feats), f32),
                    ((key_rows, feats), f32),
                ],
                *middle_chunks[side],
                *attn_w[l],
                usable,
                Far(attn[side][4]),
                Far(attn[side][1]),
                Far(attn[side][2]),
                *[Far(part) for part in key_parts],
                *carried,
                name="attn_back",
                scratch=[
                    pltpu.VMEM((key_rows, 2 * feats), bf16),
                    pltpu.VMEM((half, feats), bf16),
                    pltpu.VMEM((half, feats), bf16),
                    pltpu.VMEM((half, feats), f32),
                    pltpu.VMEM((half, feats), bf16),
                    DMA((3 + len(key_parts),)),
                ],
                limit=attn_limit,
            )
        grad_k, grad_v = carried
        if outer > 1:
            grad_k, grad_v = (
                lax.psum_scatter(
                    v, "ctx", scatter_dimension=0, tiled=True, axis_index_groups=outer_groups
                )
                for v in (grad_k, grad_v)
            )

        def project(side, after):
            return kernel_call(
                functools.partial(project_kernel, feats, side * half, len(attn_w[l])),
                [partial_out],
                grad_q[side],
                grad_k,
                grad_v,
                *attn_w[l],
                name="project",
                after=after,
                scratch=[pltpu.VMEM((half, 3 * feats), bf16)],
            )[0]

        far_part = project(1, ())
        near_part = project(0, ())
        (sums,) = reduce_rows((near_part, far_part))
        body = functools.partial(norm_back_one_kernel, gain_row(l, 0))
        if l > 0:
            masked = ()
            body = lambda *refs, body=body: body(*refs[:7], None, *refs[7:])
        else:
            masked = (mask,)
        upstream, upstream_b, sums_one = kernel_call(
            body,
            [row_f32, row_bf16, ((2, width), f32)],
            *sums,
            Far(attn[1][5]),
            Far(grad_middle),
            vecs,
            *masked,
            name="norm_back_one",
            scratch=[pltpu.VMEM((rows, width), f32)] * 2 + [DMA((2,))],
        )
        lines = ()
        if l == 0:
            terms = [sums_two, *unit_sums[0]]
            for k in range(1, depth):
                terms += [*row_sums[k], *unit_sums[k], head_sums[k]]
            packed = kernel_call(
                functools.partial(vector_pack_kernel, depth),
                [((6 * depth + 2, width), f32)],
                sums_one,
                *grad_q,
                grad_v,
                *[Far(v) for v in terms],
                name="vector_pack",
                scratch=[pltpu.VMEM(v.shape, f32) for v in terms] + [DMA((len(terms),))],
            )[0]
            if outer > 1:
                packed = lax.psum(packed, "ctx", axis_index_groups=outer_groups)
            lines = kernel_call(
                functools.partial(vector_lines_kernel, depth, width_own),
                [((fsdp, 32, 2 * width_own), bf16)],
                packed,
                name="vector_lines",
            )
        count = 1 if l > 0 else fsdp
        shapes = [((width, 3 * feats), bf16), ((width, feats), bf16)]
        if l == 0:
            shapes = [((fsdp, width_own + 32, 4 * feats), bf16)]
        *attn_grads, head_sums[l], upstream_b, sums_one, upstream = kernel_call(
            functools.partial(attn_grad_kernel, feats, count),
            [saved((width if l > 0 else width_own + 32, 4 * feats), bf16)] * count
            + [
                saved((2, feats), f32),
                row_bf16,
                saved((2, width), f32),
                saved((rows, width), f32),
            ],
            Far(attn[0][3]),
            Far(attn[1][3]),
            Far(attn[0][1]),
            Far(attn[1][1]),
            *middle_x,
            *grad_q,
            grad_k,
            grad_v,
            upstream_b,
            sums_one,
            upstream,
            *(lines or (sums_one,)),
            name="attn_grad",
            scratch=[
                pltpu.VMEM((all_rows, width), bf16),
                pltpu.VMEM((all_rows, feats), bf16),
                pltpu.VMEM((all_rows, width), bf16),
                pltpu.VMEM((all_rows, 3 * feats), bf16),
                pltpu.VMEM((2, feats), f32),
            ]
            + [pltpu.VMEM(*shape) for shape in shapes]
            + [DMA((9 + count,))],
        )
        if l > 0:
            attn_parts[l] = scatter_grads(attn_grads[0])
            upstream_chunks = gather_rows(upstream_b)
        row_sums[l] = (sums_one, sums_two)

    sources = [mlp_parts[0]]
    for l in range(1, depth):
        sources += [mlp_parts[l], attn_parts[l]]
    blocks = 3 * depth - 1
    (stacked,) = kernel_call(
        functools.partial(fetch_kernel, len(sources)),
        [((blocks * width_own, hidden), bf16)],
        *[Far(v) for v in sources],
        name="fetch",
        after=(upstream_b,),
        scratch=[DMA((blocks,))],
    )
    own_term, *other_terms = attn_grads
    other_terms = [shift_z(term, d + 1) for d, term in enumerate(other_terms)]
    crossed = swap_x(stacked)
    others = (swap_y(upstream), swap_y(outputs_own))
    part, mine = kernel_call(
        functools.partial(shard_sum_kernel, depth),
        [((width_own, 4 * feats), bf16), ((24, width_own), f32)],
        Far(own_term),
        *other_terms,
        name="shard_sum",
        after=(crossed, *others),
        scratch=[pltpu.VMEM(own_term.shape, bf16), DMA((1,))],
    )
    if outer > 1:
        part = lax.psum(part, "ctx", axis_index_groups=outer_groups)
    part_crossed = swap_x(part)
    pieces = [
        *(part, swap_core(part), part_crossed, swap_core(part_crossed)),
        *(stacked, swap_core(stacked), crossed, swap_core(crossed)),
    ]
    mine = kernel_call(
        functools.partial(vector_plane_kernel, depth),
        [((32, width_own), f32)],
        mine,
        swap_xy(mine),
        swap_x(mine),
        swap_y(mine),
        name="vector_plane",
        after=(part_crossed,),
    )[0]
    grad_gains, grad_shifts, grad_fc1_bias, grad_qv_bias = kernel_call(
        functools.partial(vector_place_kernel, depth, head_dim),
        [
            (norm_gains.shape, f32),
            (shifts.shape, f32),
            (fc1_bias.shape, f32),
            (qv_bias.shape, f32),
        ],
        mine,
        swap_core(mine),
        name="vector_place",
    )
    grad_inputs, outputs = (
        kernel_call(
            place_rows_kernel,
            [saved(inputs.shape, f32)],
            own,
            other,
            name="place_rows",
            scratch=[DMA((2,))],
        )[0]
        for own, other in zip((upstream, outputs_own), others)
    )
    placed = kernel_call(
        functools.partial(place_kernel, depth, hidden, feats),
        [saved(v.shape, f32) for v in (w_qkv, w_out, w_fc1, w_fc2)],
        *pieces,
        name="place",
        limit=24,
        scratch=[
            pltpu.VMEM((depth, GROUP, width_own, hidden), f32),
            pltpu.VMEM((depth, GROUP, hidden, width_own), f32),
            pltpu.VMEM((depth, GROUP, 3, width_own, feats), f32),
            pltpu.VMEM((depth, GROUP, feats, width_own), f32),
            DMA((16 * depth,)),
        ],
    )
    return (
        outputs,
        grad_inputs,
        grad_gains,
        grad_shifts,
        grad_qv_bias,
        grad_fc1_bias,
        *placed,
    )


def solution(mesh):
    rows = P("fsdp", "ctx", None)
    params = (
        P(None, None, "fsdp"),
        P(None, None, "fsdp"),
        P(None, None, "tp", "fsdp"),
        P(None, "tp", "fsdp"),
        P(None, None, "fsdp", "tp"),
        P(None, "tp", "fsdp"),
        P(None, "fsdp", "tp"),
        P(None, "tp", "fsdp"),
    )
    return jax.shard_map(
        per_device,
        mesh=mesh,
        in_specs=(rows, P("fsdp", None), rows) + params,
        out_specs=(rows, rows) + params,
        check_vma=False,
    )
```

```python
import functools
import math

import jax
import jax.numpy as jnp
from jax import lax
from jax.experimental import pallas as pl
from jax.experimental.pallas import tpu as pltpu
from jax.sharding import PartitionSpec as P

NORM_EPSILON = 1e-06
MASK_FILL = -1e30
ROOT_HALF = 0.7071067811865476
INV_ROOT_TAU = 0.3989422804014327
GROUP = 4
ORDER = (0, 5, 4, 1, 2, 7, 6, 3)
CHIPS = 4

bf16 = jnp.bfloat16
f32 = jnp.float32
VMEM = pl.BlockSpec(memory_space=pltpu.VMEM)
SMEM = pl.BlockSpec(memory_space=pltpu.SMEM)
HBM = pl.BlockSpec(memory_space=pltpu.HBM)
DMA = pltpu.SemaphoreType.DMA
TOKEN = ((8, 128), f32)


def dot(a, b):
    return lax.dot_general(a, b, (((1,), (0,)), ((), ())), preferred_element_type=f32)


def dot_nt(a, b):
    return lax.dot_general(a, b, (((1,), (1,)), ((), ())), preferred_element_type=f32)


def dot_tn(a, b):
    return lax.dot_general(a, b, (((0,), (0,)), ((), ())), preferred_element_type=f32)


class Far:
    def __init__(self, value):
        self.value = value


class Scalars:
    def __init__(self, value):
        self.value = value


def saved(shape, dtype):
    return pltpu.HBM(shape, dtype)


def kernel_call(body, outs, *args, name, limit=12, scratch=(), after=(), aliases=None, us=0):
    values, specs = [], []
    for arg in (*args, *after):
        if isinstance(arg, Far):
            values.append(pltpu.with_memory_space_constraint(arg.value, pltpu.HBM))
            specs.append(HBM)
        elif isinstance(arg, Scalars):
            values.append(arg.value)
            specs.append(SMEM)
        else:
            values.append(arg)
            specs.append(VMEM)
    first, last = len(args), len(args) + len(after)

    def run(*refs):
        body(*refs[:first], *refs[last:])

    out_shape, out_specs = [], []
    for out in outs:
        if isinstance(out, tuple):
            out_shape.append(jax.ShapeDtypeStruct(*out))
            out_specs.append(VMEM)
        else:
            out_shape.append(out)
            out_specs.append(HBM)
    return pl.pallas_call(
        run,
        out_shape=out_shape,
        in_specs=specs,
        out_specs=out_specs,
        scratch_shapes=list(scratch),
        input_output_aliases=aliases or {},
        compiler_params=pltpu.CompilerParams(vmem_limit_bytes=limit << 20),
        cost_estimate=pl.CostEstimate(flops=us * 10**9, bytes_accessed=0, transcendentals=0),
        name=name,
    )(*values)


def start_copies(pairs, sems):
    copies = [
        pltpu.make_async_copy(source, target, sems.at[k])
        for k, (source, target) in enumerate(pairs)
    ]
    for copy in copies:
        copy.start()
    return copies


def row_mean(value):
    return jnp.mean(value, axis=-1, keepdims=True)


def normalize(values):
    center = values - row_mean(values)
    inverse = lax.rsqrt(row_mean(center * center) + NORM_EPSILON)
    return center * inverse, inverse


def lanes_of(head, head_dim, width):
    lane = lax.broadcasted_iota(jnp.int32, (1, width), 1)
    return (lane >= head * head_dim) & (lane < (head + 1) * head_dim)


def assemble(chunks, target):
    rows = chunks[0].shape[0]
    for k, chunk in enumerate(chunks):
        target[k * rows : (k + 1) * rows, :] = chunk[...]


def only(flag, value):
    return jnp.where(flag, value, jnp.zeros_like(value))


def shards(weights):
    if len(weights) == 1:
        rows = weights[0].shape[0]
        return [(pl.ds(0, rows), weights[0])]
    count = len(weights)
    rows = weights[0].shape[0]
    f = lax.axis_index("fsdp")
    found = []
    for d, ref in enumerate(weights):
        place = lax.rem(f + (count - d), count)
        found.append((pl.ds(pl.multiple_of(place * rows, rows), rows), ref))
    return found


def pack_attn_kernel(layer, feats, qkv_hbm, out_hbm, packed_ref, token, qkv, out, sems):
    ci = lax.rem(lax.axis_index("ctx"), GROUP)
    span = pl.ds(pl.multiple_of(ci * feats, feats), feats)
    copies = start_copies(
        [(qkv_hbm.at[layer, :, :, span], qkv), (out_hbm.at[layer, span, :], out)], sems
    )
    copies[0].wait()
    for k in range(3):
        packed_ref[:, k * feats : (k + 1) * feats] = qkv[k]
    copies[1].wait()
    packed_ref[:, 3 * feats :] = out[...].T
    token[...] = jnp.zeros_like(token)


def pack_mlp_kernel(layer, hidden, fc1_hbm, fc2_hbm, packed_ref, token, fc1, fc2, sems):
    ci = lax.rem(lax.axis_index("ctx"), GROUP)
    span = pl.ds(pl.multiple_of(ci * hidden, hidden), hidden)
    copies = start_copies(
        [(fc1_hbm.at[layer, :, span], fc1), (fc2_hbm.at[layer, span, :], fc2)], sems
    )
    copies[0].wait()
    packed_ref[:, :hidden] = fc1[...]
    copies[1].wait()
    packed_ref[:, hidden:] = fc2[...].T
    token[...] = jnp.zeros_like(token)


def prep_upstream_kernel(tp, outer, lengths, cotangent_hbm,
                         upstream_hbm, upstream_b_ref, usable_ref, mask_ref,
                         rows_in, upstream_ref, sems):
    rows = rows_in.shape[0]
    c = lax.axis_index("ctx")
    t = lax.axis_index("tp")
    place = lax.rem(c, GROUP) * tp + t
    start = pl.multiple_of(t * rows, rows)
    copies = start_copies(
        [(cotangent_hbm.at[0, pl.ds(start, rows), :], rows_in)], sems.at[pl.ds(0, 1)]
    )
    lane = lax.broadcasted_iota(jnp.int32, usable_ref.shape, 1)
    limit = jnp.zeros(usable_ref.shape, jnp.int32)
    for o in range(outer):
        for k, d in enumerate(ORDER):
            source = place ^ d
            first_lane = (o * len(ORDER) + k) * rows
            count = lengths[0, o * GROUP + lax.div(source, tp)] - lax.rem(source, tp) * rows
            limit = jnp.where(lane >= first_lane, first_lane + jnp.clip(count, 0, rows), limit)
    usable_ref[...] = jnp.where(lane < limit, 1.0, 0.0)
    row = lax.broadcasted_iota(jnp.int32, mask_ref.shape, 0)
    mask = jnp.where(row + start < lengths[0, c], 1.0, 0.0)
    mask_ref[...] = mask
    copies[0].wait()
    upstream = rows_in[...] * mask[:, 0:1]
    upstream_ref[...] = upstream
    sent = start_copies([(upstream_ref, upstream_hbm)], sems.at[pl.ds(1, 1)])
    upstream_b_ref[...] = upstream.astype(bf16)
    sent[0].wait()


def prep_first_kernel(depth, inputs_hbm, vecs, stream_ref, first_ref, sems):
    rows = stream_ref.shape[0]
    start = pl.multiple_of(lax.axis_index("tp") * rows, rows)
    copies = start_copies([(inputs_hbm.at[0, pl.ds(start, rows), :], stream_ref)], sems)
    copies[0].wait()
    normed, _ = normalize(stream_ref[...])
    shift = vecs[2 * depth : 2 * depth + 1, :]
    first_ref[...] = (normed * vecs[0:1, :] + shift).astype(bf16)


def keep_rows_kernel(*refs):
    chunks, (near_hbm, far_hbm, token, near, far, sems) = refs[:8], refs[8:]
    assemble(chunks[:4], near)
    assemble(chunks[4:], far)
    for copy in start_copies([(near, near_hbm), (far, far_hbm)], sems):
        copy.wait()
    token[...] = jnp.zeros_like(token)


def qkv_kernel(feats, weight_count, *refs):
    c0, c1, c2, c3, *rest = refs
    weights = rest[:weight_count]
    bias, qkv_ref, x = rest[weight_count:]
    assemble((c0, c1, c2, c3), x)
    qkv = sum(dot(x[:, span], w[:, : 3 * feats]) for span, w in shards(weights))
    qkv_ref[:, :feats] = (qkv[:, :feats] + bias[0:1, :]).astype(bf16)
    qkv_ref[:, feats : 2 * feats] = qkv[:, feats : 2 * feats].astype(bf16)
    qkv_ref[:, 2 * feats :] = (qkv[:, 2 * feats :] + bias[1:2, :]).astype(bf16)


def attn_kernel(feats, heads, weight_count, part_count, keep_count, tile, *refs):
    q_ref, *rest = refs
    parts = rest[:part_count]
    weights = rest[part_count : part_count + weight_count]
    rest = rest[part_count + weight_count :]
    usable, *rest = rest
    kept, rest = rest[:keep_count], rest[keep_count:]
    partial_ref, attended_hbm, norm_hbm, *rest = rest
    kept_hbm, rest = rest[:keep_count], rest[keep_count:]
    keys, values, attended_ref, norm_ref, sems = rest
    head_dim = feats // heads
    scale = 1.0 / math.sqrt(head_dim)
    copies = start_copies(list(zip(kept, kept_hbm)), sems)
    first = 0
    for part in parts:
        rows, width = part.shape
        keys[first : first + rows, :] = part[:, width - 2 * feats : width - feats]
        values[first : first + rows, :] = part[:, width - feats :]
        first += rows
    keep = usable[...] > 0.5
    rows = q_ref.shape[0]
    for first in range(0, rows, tile):
        span = slice(first, first + tile)
        q = q_ref[span, :feats]
        attended = None
        for h in range(heads):
            own = lanes_of(h, head_dim, feats)
            scores = dot_nt(only(own, q), keys[...]) * scale
            scores = jnp.where(keep, scores, MASK_FILL)
            highest = jnp.max(scores, axis=-1, keepdims=True)
            raised = jnp.exp(scores - highest)
            total = jnp.sum(raised, axis=-1, keepdims=True)
            soft = (raised * (1.0 / total)).astype(bf16)
            result = dot(soft, values[...])
            log_norm = jnp.broadcast_to(highest + jnp.log(total), (tile, feats))
            if attended is None:
                attended, norms = result, log_norm
            else:
                attended = jnp.where(own, result, attended)
                norms = jnp.where(own, log_norm, norms)
        attended_ref[span, :] = attended.astype(bf16)
        norm_ref[span, :] = norms
    copies += start_copies(
        [(attended_ref, attended_hbm), (norm_ref, norm_hbm)],
        sems.at[pl.ds(keep_count, 2)],
    )
    for span, w in shards(weights):
        partial_ref[:, span] = dot_nt(attended_ref[...], w[:, 3 * feats :]).astype(bf16)
    for copy in copies:
        copy.wait()


def core_sum_kernel(count, *refs):
    pairs, owns = refs[: 2 * count], refs[2 * count : 3 * count]
    peers = refs[3 * count :]
    rows = owns[0].shape[0]
    for j in range(count):
        near, far = pairs[2 * j], pairs[2 * j + 1]
        for k in range(1 + len(peers)):
            span = slice(k * rows, (k + 1) * rows)
            total = near[span, :].astype(f32) + far[span, :].astype(f32)
            if k == 0:
                owns[j][...] = total
            else:
                peers[k - 1][j * rows : (j + 1) * rows, :] = total.astype(bf16)


def total_of(own, xy, x, y, part=0):
    rows = own.shape[0]
    span = slice(part * rows, (part + 1) * rows)
    return (
        own[...] + y[span, :].astype(f32) + x[span, :].astype(f32) + xy[span, :].astype(f32)
    )


def sum_norm_kernel(bias_row, gain_row, shift_row, own, xy, x, y, residual_hbm, vecs,
                    stream_ref, normed_ref, residual, sems):
    copies = start_copies([(residual_hbm, residual)], sems)
    total = total_of(own, xy, x, y) + vecs[bias_row : bias_row + 1, :]
    copies[0].wait()
    stream = residual[...] + total
    stream_ref[...] = stream
    normed, _ = normalize(stream)
    gain = vecs[gain_row : gain_row + 1, :]
    normed_ref[...] = (normed * gain + vecs[shift_row : shift_row + 1, :]).astype(bf16)


def sum_out_kernel(bias_row, own, xy, x, y, residual_hbm, vecs, mask, out_hbm, token,
                   residual, out_ref, sems):
    copies = start_copies([(residual_hbm, residual)], sems.at[pl.ds(0, 1)])
    total = total_of(own, xy, x, y, 1) + vecs[bias_row : bias_row + 1, :]
    copies[0].wait()
    out_ref[...] = (residual[...] + total) * mask[:, 0:1]
    token[...] = jnp.zeros_like(token)
    for copy in start_copies([(out_ref, out_hbm)], sems.at[pl.ds(1, 1)]):
        copy.wait()


def mlp_kernel(hidden, keep_count, saves, c0, c1, c2, c3, w, bias, *refs):
    kept, rest = refs[:keep_count], refs[keep_count:]
    partial_ref, x_out, act_out, slope_out, *rest = rest
    kept_hbm, rest = rest[:keep_count], rest[keep_count:]
    if saves:
        x, act_ref, slope_ref, sems = rest
    else:
        x, act_ref, slope_ref = x_out, act_out, slope_out
        (sems,) = rest
    copies = start_copies(list(zip(kept, kept_hbm)), sems)
    assemble((c0, c1, c2, c3), x)
    if saves:
        copies += start_copies([(x, x_out)], sems.at[pl.ds(keep_count, 1)])
    block = hidden // 2
    for k in range(2):
        span = slice(k * block, (k + 1) * block)
        pre = dot(x[...], w[:, span]) + bias[:, span]
        cdf = 0.5 * (1.0 + lax.erf(pre * ROOT_HALF))
        density = jnp.exp(-0.5 * pre * pre) * INV_ROOT_TAU
        slope_ref[k] = cdf + pre * density
        act_ref[:, span] = (pre * cdf).astype(bf16)
        if saves:
            copies += start_copies(
                [(slope_ref.at[k], slope_out.at[k])], sems.at[pl.ds(1 + keep_count + k, 1)]
            )
    if saves:
        copies += start_copies([(act_ref, act_out)], sems.at[pl.ds(3 + keep_count, 1)])
    partial_ref[...] = dot_nt(act_ref[...], w[:, hidden:]).astype(bf16)
    for copy in copies:
        copy.wait()


def mlp_back_kernel(hidden, chunk_count, *refs):
    chunks, (w, slope_hbm, *rest) = refs[:chunk_count], refs[chunk_count:]
    partial_ref, grad_ref, sum_hbm, x, slope, sum_ref, sems = rest
    copies = start_copies([(slope_hbm, slope)], sems)
    if chunk_count == 1:
        copies += start_copies([(chunks[0], x)], sems.at[pl.ds(1, 1)])
        copies[1].wait()
    else:
        assemble(chunks, x)
    grad = dot(x[...], w[:, hidden:])
    copies[0].wait()
    block = hidden // 2
    for k in range(2):
        span = slice(k * block, (k + 1) * block)
        part = grad[:, span] * slope[k]
        grad_ref[:, span] = part.astype(bf16)
        sum_ref[:, span] = jnp.sum(part, axis=0, keepdims=True)
    sent = start_copies([(sum_ref, sum_hbm)], sems.at[pl.ds(2, 1)])
    partial_ref[...] = dot_nt(grad_ref[...], w[:, :hidden]).astype(bf16)
    sent[0].wait()


def mlp_grad_kernel(hidden, second_near, second_far, act_near, act_far, up_near, up_far,
                    grad_near, grad_far, passed, sums, middle, out_hbm, passed_ref, sums_hbm,
                    middle_hbm, second, act, up, grad, out_one, out_two, sems):
    rows = up_near.shape[0]
    sent = start_copies([(sums, sums_hbm), (middle, middle_hbm)], sems.at[pl.ds(6, 2)])
    near, far = pl.ds(0, rows), pl.ds(rows, rows)
    copies = start_copies(
        [
            (act_near, act.at[near]),
            (act_far, act.at[far]),
            (second_near, second.at[near]),
            (second_far, second.at[far]),
        ],
        sems,
    )
    passed_ref[...] = passed[...]
    up[:rows, :] = up_near[...]
    up[rows:, :] = up_far[...]
    grad[:rows, :] = grad_near[...]
    grad[rows:, :] = grad_far[...]
    for copy in copies[:2]:
        copy.wait()
    out_two[...] = dot_tn(up[...], act[...]).astype(bf16)
    sent += start_copies(
        [(out_two, out_hbm.at[:, pl.ds(hidden, hidden)])], sems.at[pl.ds(4, 1)]
    )
    for copy in copies[2:]:
        copy.wait()
    out_one[...] = dot_tn(second[...], grad[...]).astype(bf16)
    sent += start_copies([(out_one, out_hbm.at[:, pl.ds(0, hidden)])], sems.at[pl.ds(5, 1)])
    for copy in sent:
        copy.wait()


def norm_back(upstream, values, gain):
    normed, inverse = normalize(values)
    scaled = upstream * gain
    back = inverse * (scaled - row_mean(scaled) - normed * row_mean(scaled * normed))
    gain_grad = jnp.sum(upstream * normed, axis=0, keepdims=True)
    return back, gain_grad, jnp.sum(upstream, axis=0, keepdims=True)


def norm_back_two_kernel(gain_row, own, xy, x, y, values_hbm, upstream_hbm, vecs,
                         grad_ref, grad_b_ref, sums_ref, values, upstream, sems):
    copies = start_copies([(values_hbm, values), (upstream_hbm, upstream)], sems)
    total = total_of(own, xy, x, y)
    for copy in copies:
        copy.wait()
    up = upstream[...]
    back, gain_grad, shift_grad = norm_back(
        total, values[...], vecs[gain_row : gain_row + 1, :]
    )
    grad = up + back
    grad_ref[...] = grad
    grad_b_ref[...] = grad.astype(bf16)
    sums_ref[0:1, :] = gain_grad
    sums_ref[1:2, :] = shift_grad
    sums_ref[2:3, :] = jnp.sum(grad, axis=0, keepdims=True)
    sums_ref[3:4, :] = jnp.sum(up, axis=0, keepdims=True)


def norm_back_one_kernel(gain_row, own, xy, x, y, values_hbm, upstream_hbm, vecs, mask,
                         grad_ref, grad_b_ref, sums_ref, values, upstream, sems):
    copies = start_copies([(values_hbm, values), (upstream_hbm, upstream)], sems)
    total = total_of(own, xy, x, y)
    for copy in copies:
        copy.wait()
    back, gain_grad, shift_grad = norm_back(
        total, values[...], vecs[gain_row : gain_row + 1, :]
    )
    grad = upstream[...] + back
    if mask is not None:
        grad = grad * mask[:, 0:1]
    grad_ref[...] = grad
    grad_b_ref[...] = grad.astype(bf16)
    sums_ref[0:1, :] = gain_grad
    sums_ref[1:2, :] = shift_grad


def attn_back_kernel(feats, heads, weight_count, part_count, tile, carried, *refs):
    c0, c1, c2, c3, *rest = refs
    weights, rest = rest[:weight_count], rest[weight_count:]
    usable, q_hbm, attended_hbm, norm_hbm, *rest = rest
    parts, rest = rest[:part_count], rest[part_count:]
    if carried:
        keys_before, values_before, *rest = rest
    x, grad_q, grad_k, grad_v, pairs, q_ref, attended, norms, grad_att, sems = rest
    head_dim = feats // heads
    scale = 1.0 / math.sqrt(head_dim)
    moves = [(q_hbm.at[:, pl.ds(0, feats)], q_ref), (attended_hbm, attended), (norm_hbm, norms)]
    first = 0
    for part in parts:
        rows, width = part.shape
        moves.append(
            (part.at[:, pl.ds(width - 2 * feats, 2 * feats)], pairs.at[pl.ds(first, rows)])
        )
        first += rows
    copies = start_copies(moves, sems)
    assemble((c0, c1, c2, c3), x)
    grad_att[...] = sum(
        dot(x[:, span], w[:, 3 * feats :]) for span, w in shards(weights)
    ).astype(bf16)
    keep = usable[...] > 0.5
    rows = q_ref.shape[0]
    if carried:
        sum_k, sum_v = keys_before[...], values_before[...]
    else:
        sum_k = jnp.zeros(grad_k.shape, f32)
        sum_v = jnp.zeros(grad_v.shape, f32)
    for copy in copies:
        copy.wait()
    keys, values = pairs[:, :feats], pairs[:, feats:]
    for first in range(0, rows, tile):
        span = slice(first, first + tile)
        q = q_ref[span, :]
        ga = grad_att[span, :]
        products = ga.astype(f32) * attended[span, :].astype(f32)
        gq = None
        for h in range(heads):
            own = lanes_of(h, head_dim, feats)
            q_h = only(own, q)
            ga_h = only(own, ga)
            row_dots = jnp.sum(only(own, products), axis=-1, keepdims=True)
            scores = dot_nt(q_h, keys) * scale
            scores = jnp.where(keep, scores, MASK_FILL)
            soft = jnp.exp(scores - norms[span, h * head_dim : h * head_dim + 1])
            grad_soft = dot_nt(ga_h, values)
            grad_scores = (soft * (grad_soft - row_dots)).astype(bf16)
            part = dot(grad_scores, keys)
            gq = part if gq is None else jnp.where(own, part, gq)
            sum_k = sum_k + dot_tn(grad_scores, q_h) * scale
            sum_v = sum_v + dot_tn(soft.astype(bf16), ga_h)
        grad_q[span, :] = gq * scale
    grad_k[...] = sum_k
    grad_v[...] = sum_v


def project_kernel(feats, first, weight_count, gq, gk, gv, *refs):
    weights, (partial_ref, packed) = refs[:weight_count], refs[weight_count:]
    rows = gq.shape[0]
    span = slice(first, first + rows)
    packed[:, :feats] = gq[...].astype(bf16)
    packed[:, feats : 2 * feats] = gk[span, :].astype(bf16)
    packed[:, 2 * feats :] = gv[span, :].astype(bf16)
    for columns, w in shards(weights):
        partial_ref[:, columns] = dot_nt(packed[...], w[:, : 3 * feats]).astype(bf16)


def attn_grad_kernel(feats, count, first_near, first_far, att_near, att_far, up_near, up_far,
                     gq_near, gq_far, gk, gv, passed, sums, stream, lines, *refs):
    outs, rest = refs[:count], refs[count:]
    heads_hbm, passed_ref, sums_hbm, stream_hbm, *rest = rest
    first, att, up, packed, sums_ref, *staged, sems = rest
    rows = up_near.shape[0]
    sent = start_copies([(sums, sums_hbm), (stream, stream_hbm)], sems.at[pl.ds(6, 2)])
    near, far = pl.ds(0, rows), pl.ds(rows, rows)
    copies = start_copies(
        [
            (att_near, att.at[near]),
            (att_far, att.at[far]),
            (first_near, first.at[near]),
            (first_far, first.at[far]),
        ],
        sems,
    )
    passed_ref[...] = passed[...]
    up[:rows, :] = up_near[...]
    up[rows:, :] = up_far[...]
    packed[:rows, :feats] = gq_near[...].astype(bf16)
    packed[rows:, :feats] = gq_far[...].astype(bf16)
    packed[:, feats : 2 * feats] = gk[...].astype(bf16)
    packed[:, 2 * feats :] = gv[...].astype(bf16)
    sums_ref[0:1, :] = jnp.sum(gq_near[...], axis=0, keepdims=True) + jnp.sum(
        gq_far[...], axis=0, keepdims=True
    )
    sums_ref[1:2, :] = jnp.sum(gv[...], axis=0, keepdims=True)
    sent += start_copies([(sums_ref, heads_hbm)], sems.at[pl.ds(8, 1)])
    if count == 1:
        out_one, out_two = staged
        for copy in copies[:2]:
            copy.wait()
        out_two[...] = dot_tn(up[...], att[...]).astype(bf16)
        sent += start_copies(
            [(out_two, outs[0].at[:, pl.ds(3 * feats, feats)])], sems.at[pl.ds(4, 1)]
        )
        for copy in copies[2:]:
            copy.wait()
        out_one[...] = dot_tn(first[...], packed[...]).astype(bf16)
        sent += start_copies(
            [(out_one, outs[0].at[:, pl.ds(0, 3 * feats)])], sems.at[pl.ds(5, 1)]
        )
        for copy in sent:
            copy.wait()
        return
    (stage,) = staged
    for copy in copies:
        copy.wait()
    below = lines.shape[1]
    width_own = outs[0].shape[0] - below
    for d in reversed(range(count)):
        place = lax.rem(lax.axis_index("fsdp") + d, count)
        span = pl.ds(pl.multiple_of(place * width_own, width_own), width_own)
        stage[d, :width_own, : 3 * feats] = dot_tn(first[:, span], packed[...]).astype(bf16)
        stage[d, :width_own, 3 * feats :] = dot_tn(up[:, span], att[...]).astype(bf16)
        stage[d, width_own:, :] = lines[d]
        sent += start_copies([(stage.at[d], outs[d])], sems.at[pl.ds(9 + d, 1)])
    for copy in sent:
        copy.wait()


def settle_kernel(passed, *refs):
    passed_ref = refs[-1]
    passed_ref[...] = passed[...]


def fetch_kernel(count, *refs):
    sources, (target, sems) = refs[:count], refs[count:]
    columns = target.shape[1]
    moves = []
    row = 0
    for source in sources:
        rows = source.shape[0]
        for first in range(0, source.shape[1], columns):
            moves.append(
                (source.at[:, pl.ds(first, columns)], target.at[pl.ds(row, rows), :])
            )
            row += rows
    for copy in start_copies(moves, sems):
        copy.wait()


def shard_sum_kernel(depth, own_hbm, stacked, crossed, *refs):
    *others, part_ref, mine_ref, pair_ref, own, sems = refs
    count = stacked.shape[0]
    first, *copies = start_copies(
        [
            (own_hbm, own),
            (stacked, pair_ref.at[pl.ds(0, count), :]),
            (crossed, pair_ref.at[pl.ds(count, count), :]),
        ],
        sems,
    )
    first.wait()
    rows, width = part_ref.shape[0], mine_ref.shape[1]
    terms = [ref[...].astype(f32) for ref in (own, *others)]
    total = terms[0]
    for term in terms[1:]:
        total = total + term
    part_ref[...] = total[:rows, :].astype(bf16)
    lines = total[rows:, :width] + total[rows:, width:]
    mine_ref[: 6 * depth, :] = lines[: 6 * depth, :]
    for k in range(mine_ref.shape[0] - 16):
        mine_ref[16 + k : 17 + k, :] = lines[6 * depth + k : 6 * depth + k + 1, :]
    for copy in copies:
        copy.wait()


def place_kernel(depth, hidden, feats, *refs):
    alone_refs, pairs, rest = refs[:GROUP], refs[GROUP : GROUP + 2], refs[GROUP + 2 :]
    count = pairs[0].shape[0] // 2
    slices = [
        (alone_refs[k], pairs[k % 2].at[pl.ds(k // 2 * count, count), :]) for k in range(GROUP)
    ]
    qkv_hbm, out_hbm, fc1_hbm, fc2_hbm, fc1, fc2, qkv, out, sems = rest
    ci = lax.rem(lax.axis_index("ctx"), GROUP)
    rows = fc1.shape[2]
    copies = []

    def send(source, target):
        copies.extend(start_copies([(source, target)], sems.at[pl.ds(len(copies), 1)]))

    for l in range(depth):
        for k in range(GROUP):
            _, stacked = slices[k]
            first = 0 if l == 0 else (3 * l - 1) * rows
            span = pl.ds(pl.multiple_of((ci ^ k) * hidden, hidden), hidden)
            fc1[l, k] = stacked[first : first + rows, :].astype(f32)
            send(fc1.at[l, k], fc1_hbm.at[l, :, span])
            fc2[l, k] = stacked[first + rows : first + 2 * rows, :].T.astype(f32)
            send(fc2.at[l, k], fc2_hbm.at[l, span, :])
    for l in reversed(range(depth)):
        for k in range(GROUP):
            alone, stacked = slices[k]
            piece = alone if l == 0 else stacked.at[pl.ds((3 * l + 1) * rows, rows), :]
            span = pl.ds(pl.multiple_of((ci ^ k) * feats, feats), feats)
            for j in range(3):
                qkv[l, k, j] = piece[:, j * feats : (j + 1) * feats].astype(f32)
            send(qkv.at[l, k], qkv_hbm.at[l, :, :, span])
            out[l, k] = piece[:, 3 * feats :].T.astype(f32)
            send(out.at[l, k], out_hbm.at[l, span, :])
    for copy in copies:
        copy.wait()


def vector_pack_kernel(depth, one_now, gq_near, gq_far, gv, *refs):
    count = 5 * depth - 2
    out_ref, *found, sems = refs[count:]
    copies = start_copies(list(zip(refs[:count], found)), sems)
    out_ref[...] = jnp.zeros_like(out_ref)
    feats = gv.shape[1]
    head_now = [
        jnp.sum(gq_near[...], axis=0, keepdims=True) + jnp.sum(gq_far[...], axis=0, keepdims=True),
        jnp.sum(gv[...], axis=0, keepdims=True),
    ]
    for copy in copies:
        copy.wait()
    for l in range(depth):
        if l == 0:
            one, (two, unit_near, unit_far) = one_now, found[:3]
            heads = head_now
        else:
            one, two, unit_near, unit_far, head = found[5 * l - 2 : 5 * l + 3]
            heads = [head[0:1, :], head[1:2, :]]
        out_ref[6 * l : 6 * l + 1, :] = one[0:1, :]
        out_ref[6 * l + 1 : 6 * l + 2, :] = two[0:1, :]
        out_ref[6 * l + 2 : 6 * l + 3, :] = one[1:2, :]
        out_ref[6 * l + 3 : 6 * l + 6, :] = two[1:4, :]
        units = unit_near.shape[1]
        row = 6 * depth
        out_ref[row : row + 1, l * units : (l + 1) * units] = unit_near[...] + unit_far[...]
        for j in range(2):
            start = (2 * l + j) * feats
            out_ref[row + 1 : row + 2, start : start + feats] = heads[j]


def vector_lines_kernel(depth, width_own, packed, lines_ref):
    count = lines_ref.shape[0]
    f = lax.axis_index("fsdp")
    total = packed[...]
    high = total.astype(bf16).astype(f32)
    low = total - high
    lines_ref[...] = jnp.zeros_like(lines_ref)
    last = 6 * depth
    for k, value in enumerate((high, low)):
        lanes = slice(k * width_own, (k + 1) * width_own)
        columns = [value[:, a * width_own : (a + 1) * width_own] for a in range(count)]
        for d in range(count):
            mine = columns[0]
            for a in range(1, count):
                mine = jnp.where(lax.rem(f + d, count) == a, columns[a], mine)
            rows = [mine[:last, :]]
            for r in range(2):
                for a in range(count):
                    rows.append(columns[a][last + r : last + r + 1, :])
            rows.append(jnp.zeros((lines_ref.shape[1] - last - 2 * count, width_own), f32))
            lines_ref[d, :, lanes] = jnp.concatenate(rows, axis=0).astype(bf16)


def vector_plane_kernel(depth, own, xy, x, y, out_ref):
    last = 6 * depth
    out_ref[:last, :] = own[:last, :] + xy[:last, :] + x[:last, :] + y[:last, :]
    out_ref[16:24, :] = own[16:24, :]
    out_ref[24:32, :] = x[16:24, :]


def vector_place_kernel(depth, head_dim, own, far, gains_ref, shifts_ref, unit_ref, heads_ref):
    total = own[: 6 * depth, :] + far[: 6 * depth, :]
    for l in range(depth):
        gains_ref[l] = total[6 * l : 6 * l + 2, :]
        shifts_ref[l] = total[6 * l + 2 : 6 * l + 6, :]
    pieces = (own[16:24, :], far[16:24, :], own[24:32, :], far[24:32, :])
    ci = lax.rem(lax.axis_index("ctx"), GROUP)
    f = lax.axis_index("fsdp")

    def of_place(c):
        k = ci ^ c
        found = pieces[0]
        for j in range(1, GROUP):
            found = jnp.where(k == j, pieces[j], found)
        return found

    width_own = own.shape[1]
    units = of_place(f)
    parts = unit_ref.shape[2] // width_own
    for l in range(depth):
        for j in range(parts):
            row = l * parts + j
            unit_ref[l, :, j * width_own : (j + 1) * width_own] = units[row : row + 1, :]
    head_own = heads_ref.shape[3]
    heads = heads_ref.shape[2] // GROUP
    for c in range(GROUP):
        found = of_place(c)
        for l in range(depth):
            for j in range(2):
                for h in range(heads):
                    first = ((2 * l + j) * heads + h) * head_dim
                    row, lane = 4 + first // width_own, first % width_own
                    value = found[row : row + 1, lane : lane + head_own]
                    for a in range(1, head_dim // head_own):
                        start = lane + a * head_own
                        value = jnp.where(
                            f == a, found[row : row + 1, start : start + head_own], value
                        )
                    heads_ref[l, j, c * heads + h : c * heads + h + 1, :] = value


def place_rows_kernel(own, other, out_hbm, sems):
    rows = own.shape[0]
    start = pl.multiple_of(lax.axis_index("tp") * rows, rows)
    copies = start_copies(
        [
            (own, out_hbm.at[0, pl.ds(start, rows), :]),
            (other, out_hbm.at[0, pl.ds(pl.multiple_of(rows - start, rows), rows), :]),
        ],
        sems,
    )
    for copy in copies:
        copy.wait()


def per_device(
    inputs, lengths, cotangent, norm_gains, shifts, qv_bias, fc1_bias, w_qkv, w_out, w_fc1, w_fc2
):
    depth = w_qkv.shape[0]
    width_own = w_qkv.shape[2]
    fsdp = lax.axis_size("fsdp")
    tp = lax.axis_size("tp")
    ctx = lax.axis_size("ctx")
    outer = ctx // GROUP
    rows = inputs.shape[1] // tp
    half = rows * CHIPS
    all_rows = 2 * half
    head_own = qv_bias.shape[3]
    head_dim = head_own * fsdp
    heads = qv_bias.shape[2] // GROUP
    feats = heads * head_dim
    hidden = w_fc1.shape[2] // GROUP
    width = width_own * fsdp
    t = lax.axis_index("tp")
    f = lax.axis_index("fsdp")
    ci = lax.axis_index("ctx") % GROUP
    tile = half // 2
    attn_limit = 12 if outer == 1 else 48

    def swap_core(value):
        return lax.ppermute(value, "ctx", [(i, i ^ 1) for i in range(ctx)])

    def swap_x(value):
        return lax.ppermute(value, "ctx", [(i, i ^ 2) for i in range(ctx)])

    def swap_y(value):
        return lax.ppermute(value, "tp", [(i, i ^ 1) for i in range(tp)])

    def swap_xy(value):
        pairs = [
            (i * tp + k, (i ^ 2) * tp + (k ^ 1)) for i in range(ctx) for k in range(tp)
        ]
        return lax.ppermute(value, ("ctx", "tp"), pairs)

    def shift_z(value, d):
        return lax.ppermute(value, "fsdp", [(i, (i + d) % fsdp) for i in range(fsdp)])

    outer_groups = [[o * GROUP + i for o in range(outer)] for i in range(GROUP)]

    def gather_rows(own):
        near = (own, swap_xy(own), swap_x(own), swap_y(own))
        return near, tuple(swap_core(chunk) for chunk in near)

    def settle(value, *after):
        return kernel_call(
            settle_kernel, [(value.shape, value.dtype)], value, name="settle", after=after
        )[0]

    def reduce_rows(*pairs, after=()):
        count = len(pairs)
        *owns, xy, x, y = kernel_call(
            functools.partial(core_sum_kernel, count),
            [((rows, width), f32)] * count + [((count * rows, width), bf16)] * 3,
            *[v for near, far in pairs for v in (near, swap_core(far))],
            name="core_sum",
            after=after,
        )
        peers = (swap_xy(xy), swap_x(x), swap_y(y))
        return [(own, *peers) for own in owns]

    def pack_attn(l, after):
        return kernel_call(
            functools.partial(pack_attn_kernel, l, feats),
            [((width_own, 4 * feats), bf16), TOKEN],
            Far(w_qkv),
            Far(w_out),
            name="pack_attn",
            after=after,
            scratch=[
                pltpu.VMEM((3, width_own, feats), bf16),
                pltpu.VMEM((feats, width_own), bf16),
                DMA((2,)),
            ],
        )

    def pack_mlp(l, after):
        return kernel_call(
            functools.partial(pack_mlp_kernel, l, hidden),
            [((width_own, 2 * hidden), bf16), TOKEN],
            Far(w_fc1),
            Far(w_fc2),
            name="pack_mlp",
            after=after,
            scratch=[
                pltpu.VMEM((width_own, hidden), bf16),
                pltpu.VMEM((hidden, width_own), bf16),
                DMA((2,)),
            ],
        )

    attn_w = []
    mlp_w = []
    token = None
    for l in range(depth):
        own, token = pack_attn(l, () if token is None else (token,))
        attn_w.append((lax.all_gather(own, "fsdp", axis=0, tiled=True),))
        own, token = pack_mlp(l, (token,))
        mlp_w.append(lax.all_gather(own, "fsdp", axis=0, tiled=True))
        if l == 0:
            pack_token = token

    qv_own = lax.dynamic_slice_in_dim(qv_bias, ci * heads, heads, axis=2)
    vec_rows = depth * 6
    c1_rows = depth * fc1_bias.shape[2] // width_own
    qv_own = qv_own.reshape(1, -1)
    small_own = jnp.concatenate(
        [
            norm_gains.reshape(-1, width_own),
            shifts.reshape(-1, width_own),
            fc1_bias.reshape(-1, width_own),
            jnp.pad(qv_own, ((0, 0), (0, width_own - qv_own.shape[1]))),
        ],
        axis=0,
    )
    shifted = [small_own] + [shift_z(small_own, d) for d in range(1, fsdp)]

    def shard(a):
        picked = shifted[0]
        for d in range(1, fsdp):
            picked = jnp.where((f - d) % fsdp == a, shifted[d], picked)
        return picked.astype(f32)

    small = [shard(a) for a in range(fsdp)]
    vecs = jnp.concatenate([s[:vec_rows] for s in small], axis=1)
    fc1_all = shard(ci)[vec_rows : vec_rows + c1_rows].reshape(depth, 1, hidden)
    qv_all = jnp.stack(
        [s[vec_rows + c1_rows, : qv_own.shape[1]].reshape(depth, 2, heads, head_own) for s in small],
        axis=3,
    ).reshape(depth, 2, feats)

    def gain_row(l, i):
        return 2 * l + i

    def shift_row(l, i):
        return 2 * depth + 4 * l + i

    key_rows = outer * all_rows
    row_f32 = ((rows, width), f32)
    row_bf16 = ((rows, width), bf16)
    upstream, upstream_b, usable, mask = kernel_call(
        functools.partial(prep_upstream_kernel, tp, outer),
        [saved((rows, width), f32), row_bf16, ((1, key_rows), f32), ((rows, 128), f32)],
        Scalars(lengths),
        Far(cotangent),
        name="prep_upstream",
        after=(pack_token,),
        scratch=[pltpu.VMEM((rows, width), f32), pltpu.VMEM((rows, width), f32), DMA((2,))],
    )
    near, far = gather_rows(upstream_b)
    half_x = pltpu.VMEM((half, width), bf16)
    *upstream_rows, upstream_token = kernel_call(
        keep_rows_kernel,
        [saved((half, width), bf16)] * 2 + [TOKEN],
        *near,
        *far,
        name="keep_rows",
        scratch=[half_x, half_x, DMA((2,))],
    )
    upstream_chunks = [(Far(x),) for x in upstream_rows]
    stream, first = kernel_call(
        functools.partial(prep_first_kernel, depth),
        [row_f32, row_bf16],
        Far(inputs),
        vecs,
        name="prep_first",
        scratch=[DMA((1,))],
    )
    first_chunks = gather_rows(first)

    partial_out = ((half, width), bf16)
    saved_all = []
    for l in range(depth):
        qkv = []
        first_x = []
        for side in (0, 1):
            qkv_half, x_half = kernel_call(
                functools.partial(qkv_kernel, feats, len(attn_w[l])),
                [((half, 3 * feats), bf16), ((half, width), bf16)],
                *first_chunks[side],
                *attn_w[l],
                qv_all[l],
                name="qkv",
                after=(upstream_token,) if l == 0 and side == 0 else (),
            )
            qkv.append(qkv_half)
            first_x.append(x_half)
        if outer > 1:
            pairs = jnp.concatenate([part[:, feats:] for part in qkv], axis=0)
            pairs = lax.all_gather(
                pairs, "ctx", axis=0, tiled=True, axis_index_groups=outer_groups
            )
            key_parts = (pairs,)
        else:
            key_parts = tuple(qkv)
        attn = [None, None]
        for side in (1, 0):
            kept = (first_x[side], qkv[side]) + ((stream,) if side == 1 else ())
            attn[side] = kernel_call(
                functools.partial(
                    attn_kernel, feats, heads, len(attn_w[l]), len(key_parts), len(kept), tile
                ),
                [partial_out, saved((half, feats), bf16), saved((half, feats), f32)]
                + [saved(k.shape, k.dtype) for k in kept],
                qkv[side],
                *key_parts,
                *attn_w[l],
                usable,
                *kept,
                name="attn",
                limit=attn_limit,
                scratch=[
                    pltpu.VMEM((key_rows, feats), bf16),
                    pltpu.VMEM((key_rows, feats), bf16),
                    pltpu.VMEM((half, feats), bf16),
                    pltpu.VMEM((half, feats), f32),
                    DMA((len(kept) + 2,)),
                ],
            )
        (sums,) = reduce_rows((attn[0][0], attn[1][0]))
        middle, second = kernel_call(
            functools.partial(sum_norm_kernel, shift_row(l, 2), gain_row(l, 1), shift_row(l, 1)),
            [row_f32, row_bf16],
            *sums,
            Far(attn[1][5]),
            vecs,
            name="sum_norm",
            scratch=[pltpu.VMEM((rows, width), f32), DMA((1,))],
        )
        second_chunks = gather_rows(second)
        mlp = [None, None]
        for side in (1, 0):
            kept = (middle,) if side == 1 else ()
            saves = l + 1 < depth
            shapes = [
                ((half, width), bf16),
                ((half, hidden), bf16),
                ((2, half, hidden // 2), f32),
            ]
            mlp[side] = kernel_call(
                functools.partial(mlp_kernel, hidden, len(kept), saves),
                [partial_out]
                + [saved(*shape) if saves else shape for shape in shapes]
                + [saved(k.shape, k.dtype) for k in kept],
                *second_chunks[side],
                mlp_w[l],
                fc1_all[l],
                *kept,
                name="mlp",
                scratch=[pltpu.VMEM(*shape) for shape in shapes if saves]
                + [DMA((4 + len(kept),))],
            )
            if saves:
                mlp[side] = [mlp[side][0], *[Far(v) for v in mlp[side][1:4]], *mlp[side][4:]]
        saved_all.append((attn, pairs if outer > 1 else None, mlp))
        if l + 1 < depth:
            (sums,) = reduce_rows((mlp[0][0], mlp[1][0]))
            stream, first = kernel_call(
                functools.partial(
                    sum_norm_kernel, shift_row(l, 3), gain_row(l + 1, 0), shift_row(l + 1, 0)
                ),
                [row_f32, row_bf16],
                *sums,
                Far(mlp[1][4]),
                vecs,
                name="sum_norm",
                scratch=[pltpu.VMEM((rows, width), f32), DMA((1,))],
            )
            first_chunks = gather_rows(first)

    def scatter_grads(grad):
        part = lax.psum_scatter(grad, "fsdp", scatter_dimension=0, tiled=True)
        if outer > 1:
            part = lax.psum(part, "ctx", axis_index_groups=outer_groups)
        return part

    row_sums = [None] * depth
    unit_sums = [None] * depth
    head_sums = [None] * depth
    mlp_parts = [None] * depth
    attn_parts = [None] * depth
    for l in reversed(range(depth)):
        attn, pairs, mlp = saved_all[l]
        back = [None, None]
        for side in (1, 0):
            back[side] = kernel_call(
                functools.partial(mlp_back_kernel, hidden, len(upstream_chunks[side])),
                [
                    partial_out,
                    ((half, hidden), bf16),
                    saved((1, hidden), f32),
                    ((half, width), bf16),
                ],
                *upstream_chunks[side],
                mlp_w[l],
                mlp[side][3],
                name="mlp_back",
                scratch=[
                    pltpu.VMEM((2, half, hidden // 2), f32),
                    pltpu.VMEM((1, hidden), f32),
                    DMA((3,)),
                ],
            )
        pairs_now = [(back[0][0], back[1][0])]
        if l + 1 == depth:
            pairs_now.append((mlp[0][0], mlp[1][0]))
        sums, *output_sums = reduce_rows(*pairs_now)
        if l + 1 == depth:
            outputs_own, output_token = kernel_call(
                functools.partial(sum_out_kernel, shift_row(l, 3)),
                [saved((rows, width), f32), TOKEN],
                *output_sums[0],
                Far(mlp[1][4]),
                vecs,
                mask,
                name="sum_out",
                scratch=[pltpu.VMEM((rows, width), f32)] * 2 + [DMA((2,))],
            )
            after = (output_token,)
        else:
            after = ()
        unit_sums[l] = (back[0][2], back[1][2])
        grad_middle, middle_b, sums_two = kernel_call(
            functools.partial(norm_back_two_kernel, gain_row(l, 1)),
            [row_f32, row_bf16, ((4, width), f32)],
            *sums,
            Far(mlp[1][4]),
            Far(upstream),
            vecs,
            name="norm_back_two",
            scratch=[pltpu.VMEM((rows, width), f32)] * 2 + [DMA((2,))],
        )
        mlp_grad, middle_b, sums_two, grad_middle = kernel_call(
            functools.partial(mlp_grad_kernel, hidden),
            [
                saved((width, 2 * hidden), bf16),
                row_bf16,
                saved((4, width), f32),
                saved((rows, width), f32),
            ],
            mlp[0][1],
            mlp[1][1],
            mlp[0][2],
            mlp[1][2],
            back[0][3],
            back[1][3],
            back[0][1],
            back[1][1],
            middle_b,
            sums_two,
            grad_middle,
            name="mlp_grad",
            after=after,
            scratch=[
                pltpu.VMEM((all_rows, width), bf16),
                pltpu.VMEM((all_rows, hidden), bf16),
                pltpu.VMEM((all_rows, width), bf16),
                pltpu.VMEM((all_rows, hidden), bf16),
                pltpu.VMEM((width, hidden), bf16),
                pltpu.VMEM((width, hidden), bf16),
                DMA((8,)),
            ],
            limit=16,
        )
        mlp_parts[l] = scatter_grads(mlp_grad)
        if l + 1 < depth:
            middle_b = settle(middle_b, Far(mlp_parts[l + 1]))
        middle_chunks = gather_rows(middle_b)
        grad_q = [None, None]
        middle_x = [None, None]
        carried = ()
        for side in (0, 1):
            key_parts = (pairs,) if outer > 1 else (attn[0][4], attn[1][4])
            middle_x[side], grad_q[side], *carried = kernel_call(
                functools.partial(
                    attn_back_kernel,
                    feats,
                    heads,
                    len(attn_w[l]),
                    len(key_parts),
                    tile,
                    len(carried) > 0,
                ),
                [
                    ((half, width), bf16),
                    ((half, feats), f32),
                    ((key_rows, feats), f32),
                    ((key_rows, feats), f32),
                ],
                *middle_chunks[side],
                *attn_w[l],
                usable,
                Far(attn[side][4]),
                Far(attn[side][1]),
                Far(attn[side][2]),
                *[Far(part) for part in key_parts],
                *carried,
                name="attn_back",
                scratch=[
                    pltpu.VMEM((key_rows, 2 * feats), bf16),
                    pltpu.VMEM((half, feats), bf16),
                    pltpu.VMEM((half, feats), bf16),
                    pltpu.VMEM((half, feats), f32),
                    pltpu.VMEM((half, feats), bf16),
                    DMA((3 + len(key_parts),)),
                ],
                limit=attn_limit,
            )
        grad_k, grad_v = carried
        if outer > 1:
            grad_k, grad_v = (
                lax.psum_scatter(
                    v, "ctx", scatter_dimension=0, tiled=True, axis_index_groups=outer_groups
                )
                for v in (grad_k, grad_v)
            )

        def project(side, after):
            return kernel_call(
                functools.partial(project_kernel, feats, side * half, len(attn_w[l])),
                [partial_out],
                grad_q[side],
                grad_k,
                grad_v,
                *attn_w[l],
                name="project",
                after=after,
                scratch=[pltpu.VMEM((half, 3 * feats), bf16)],
            )[0]

        far_part = project(1, ())
        near_part = project(0, ())
        (sums,) = reduce_rows((near_part, far_part))
        body = functools.partial(norm_back_one_kernel, gain_row(l, 0))
        if l > 0:
            masked = ()
            body = lambda *refs, body=body: body(*refs[:7], None, *refs[7:])
        else:
            masked = (mask,)
        upstream, upstream_b, sums_one = kernel_call(
            body,
            [row_f32, row_bf16, ((2, width), f32)],
            *sums,
            Far(attn[1][5]),
            Far(grad_middle),
            vecs,
            *masked,
            name="norm_back_one",
            scratch=[pltpu.VMEM((rows, width), f32)] * 2 + [DMA((2,))],
        )
        lines = ()
        if l == 0:
            terms = [sums_two, *unit_sums[0]]
            for k in range(1, depth):
                terms += [*row_sums[k], *unit_sums[k], head_sums[k]]
            packed = kernel_call(
                functools.partial(vector_pack_kernel, depth),
                [((6 * depth + 2, width), f32)],
                sums_one,
                *grad_q,
                grad_v,
                *[Far(v) for v in terms],
                name="vector_pack",
                scratch=[pltpu.VMEM(v.shape, f32) for v in terms] + [DMA((len(terms),))],
            )[0]
            if outer > 1:
                packed = lax.psum(packed, "ctx", axis_index_groups=outer_groups)
            lines = kernel_call(
                functools.partial(vector_lines_kernel, depth, width_own),
                [((fsdp, 32, 2 * width_own), bf16)],
                packed,
                name="vector_lines",
            )
        count = 1 if l > 0 else fsdp
        shapes = [((width, 3 * feats), bf16), ((width, feats), bf16)]
        if l == 0:
            shapes = [((fsdp, width_own + 32, 4 * feats), bf16)]
        *attn_grads, head_sums[l], upstream_b, sums_one, upstream = kernel_call(
            functools.partial(attn_grad_kernel, feats, count),
            [saved((width if l > 0 else width_own + 32, 4 * feats), bf16)] * count
            + [
                saved((2, feats), f32),
                row_bf16,
                saved((2, width), f32),
                saved((rows, width), f32),
            ],
            Far(attn[0][3]),
            Far(attn[1][3]),
            Far(attn[0][1]),
            Far(attn[1][1]),
            *middle_x,
            *grad_q,
            grad_k,
            grad_v,
            upstream_b,
            sums_one,
            upstream,
            *(lines or (sums_one,)),
            name="attn_grad",
            scratch=[
                pltpu.VMEM((all_rows, width), bf16),
                pltpu.VMEM((all_rows, feats), bf16),
                pltpu.VMEM((all_rows, width), bf16),
                pltpu.VMEM((all_rows, 3 * feats), bf16),
                pltpu.VMEM((2, feats), f32),
            ]
            + [pltpu.VMEM(*shape) for shape in shapes]
            + [DMA((9 + count,))],
        )
        if l > 0:
            attn_parts[l] = scatter_grads(attn_grads[0])
            upstream_chunks = gather_rows(upstream_b)
        row_sums[l] = (sums_one, sums_two)

    sources = [mlp_parts[0]]
    for l in range(1, depth):
        sources += [mlp_parts[l], attn_parts[l]]
    blocks = 3 * depth - 1
    (stacked,) = kernel_call(
        functools.partial(fetch_kernel, len(sources)),
        [((blocks * width_own, hidden), bf16)],
        *[Far(v) for v in sources],
        name="fetch",
        after=(upstream_b,),
        scratch=[DMA((blocks,))],
    )
    own_term, *other_terms = attn_grads
    other_terms = [shift_z(term, d + 1) for d, term in enumerate(other_terms)]
    crossed = swap_x(stacked)
    others = (swap_y(upstream), swap_y(outputs_own))
    part, mine, pair = kernel_call(
        functools.partial(shard_sum_kernel, depth),
        [
            ((width_own, 4 * feats), bf16),
            ((24, width_own), f32),
            ((2 * blocks * width_own, hidden), bf16),
        ],
        Far(own_term),
        stacked,
        crossed,
        *other_terms,
        name="shard_sum",
        after=others,
        scratch=[pltpu.VMEM(own_term.shape, bf16), DMA((3,))],
    )
    if outer > 1:
        part = lax.psum(part, "ctx", axis_index_groups=outer_groups)
    part_crossed = swap_x(part)
    pieces = [
        *(part, swap_core(part), part_crossed, swap_core(part_crossed)),
        *(pair, swap_core(pair)),
    ]
    mine = kernel_call(
        functools.partial(vector_plane_kernel, depth),
        [((32, width_own), f32)],
        mine,
        swap_xy(mine),
        swap_x(mine),
        swap_y(mine),
        name="vector_plane",
        after=(part_crossed,),
    )[0]
    grad_gains, grad_shifts, grad_fc1_bias, grad_qv_bias = kernel_call(
        functools.partial(vector_place_kernel, depth, head_dim),
        [
            (norm_gains.shape, f32),
            (shifts.shape, f32),
            (fc1_bias.shape, f32),
            (qv_bias.shape, f32),
        ],
        mine,
        swap_core(mine),
        name="vector_place",
    )
    grad_inputs, outputs = (
        kernel_call(
            place_rows_kernel,
            [saved(inputs.shape, f32)],
            own,
            other,
            name="place_rows",
            scratch=[DMA((2,))],
        )[0]
        for own, other in zip((upstream, outputs_own), others)
    )
    placed = kernel_call(
        functools.partial(place_kernel, depth, hidden, feats),
        [saved(v.shape, f32) for v in (w_qkv, w_out, w_fc1, w_fc2)],
        *pieces,
        name="place",
        limit=24,
        scratch=[
            pltpu.VMEM((depth, GROUP, width_own, hidden), f32),
            pltpu.VMEM((depth, GROUP, hidden, width_own), f32),
            pltpu.VMEM((depth, GROUP, 3, width_own, feats), f32),
            pltpu.VMEM((depth, GROUP, feats, width_own), f32),
            DMA((16 * depth,)),
        ],
    )
    return (
        outputs,
        grad_inputs,
        grad_gains,
        grad_shifts,
        grad_qv_bias,
        grad_fc1_bias,
        *placed,
    )


def solution(mesh):
    rows = P("fsdp", "ctx", None)
    params = (
        P(None, None, "fsdp"),
        P(None, None, "fsdp"),
        P(None, None, "tp", "fsdp"),
        P(None, "tp", "fsdp"),
        P(None, None, "fsdp", "tp"),
        P(None, "tp", "fsdp"),
        P(None, "fsdp", "tp"),
        P(None, "tp", "fsdp"),
    )
    return jax.shard_map(
        per_device,
        mesh=mesh,
        in_specs=(rows, P("fsdp", None), rows) + params,
        out_specs=(rows, rows) + params,
        check_vma=False,
    )
```

```python
import functools
import math

import jax
import jax.numpy as jnp
from jax import lax
from jax.experimental import pallas as pl
from jax.experimental.pallas import tpu as pltpu
from jax.sharding import PartitionSpec as P

NORM_EPSILON = 1e-06
MASK_FILL = -1e30
ROOT_HALF = 0.7071067811865476
INV_ROOT_TAU = 0.3989422804014327
GROUP = 4
ORDER = (0, 5, 4, 1, 2, 7, 6, 3)
CHIPS = 4

bf16 = jnp.bfloat16
f32 = jnp.float32
VMEM = pl.BlockSpec(memory_space=pltpu.VMEM)
SMEM = pl.BlockSpec(memory_space=pltpu.SMEM)
HBM = pl.BlockSpec(memory_space=pltpu.HBM)
DMA = pltpu.SemaphoreType.DMA
TOKEN = ((8, 128), f32)


def dot(a, b):
    return lax.dot_general(a, b, (((1,), (0,)), ((), ())), preferred_element_type=f32)


def dot_nt(a, b):
    return lax.dot_general(a, b, (((1,), (1,)), ((), ())), preferred_element_type=f32)


def dot_tn(a, b):
    return lax.dot_general(a, b, (((0,), (0,)), ((), ())), preferred_element_type=f32)


class Far:
    def __init__(self, value):
        self.value = value


class Scalars:
    def __init__(self, value):
        self.value = value


def saved(shape, dtype):
    return pltpu.HBM(shape, dtype)


def kernel_call(body, outs, *args, name, limit=12, scratch=(), after=(), aliases=None, us=0):
    values, specs = [], []
    for arg in (*args, *after):
        if isinstance(arg, Far):
            values.append(pltpu.with_memory_space_constraint(arg.value, pltpu.HBM))
            specs.append(HBM)
        elif isinstance(arg, Scalars):
            values.append(arg.value)
            specs.append(SMEM)
        else:
            values.append(arg)
            specs.append(VMEM)
    first, last = len(args), len(args) + len(after)

    def run(*refs):
        body(*refs[:first], *refs[last:])

    out_shape, out_specs = [], []
    for out in outs:
        if isinstance(out, tuple):
            out_shape.append(jax.ShapeDtypeStruct(*out))
            out_specs.append(VMEM)
        else:
            out_shape.append(out)
            out_specs.append(HBM)
    return pl.pallas_call(
        run,
        out_shape=out_shape,
        in_specs=specs,
        out_specs=out_specs,
        scratch_shapes=list(scratch),
        input_output_aliases=aliases or {},
        compiler_params=pltpu.CompilerParams(vmem_limit_bytes=limit << 20),
        cost_estimate=pl.CostEstimate(flops=us * 10**9, bytes_accessed=0, transcendentals=0),
        name=name,
    )(*values)


def start_copies(pairs, sems):
    copies = [
        pltpu.make_async_copy(source, target, sems.at[k])
        for k, (source, target) in enumerate(pairs)
    ]
    for copy in copies:
        copy.start()
    return copies


def row_mean(value):
    return jnp.mean(value, axis=-1, keepdims=True)


def normalize(values):
    center = values - row_mean(values)
    inverse = lax.rsqrt(row_mean(center * center) + NORM_EPSILON)
    return center * inverse, inverse


def lanes_of(head, head_dim, width):
    lane = lax.broadcasted_iota(jnp.int32, (1, width), 1)
    return (lane >= head * head_dim) & (lane < (head + 1) * head_dim)


def assemble(chunks, target):
    rows = chunks[0].shape[0]
    for k, chunk in enumerate(chunks):
        target[k * rows : (k + 1) * rows, :] = chunk[...]


def only(flag, value):
    return jnp.where(flag, value, jnp.zeros_like(value))


def shards(weights):
    if len(weights) == 1:
        rows = weights[0].shape[0]
        return [(pl.ds(0, rows), weights[0])]
    count = len(weights)
    rows = weights[0].shape[0]
    f = lax.axis_index("fsdp")
    found = []
    for d, ref in enumerate(weights):
        place = lax.rem(f + (count - d), count)
        found.append((pl.ds(pl.multiple_of(place * rows, rows), rows), ref))
    return found


def pack_attn_kernel(layer, feats, qkv_hbm, out_hbm, packed_ref, token, qkv, out, sems):
    ci = lax.rem(lax.axis_index("ctx"), GROUP)
    span = pl.ds(pl.multiple_of(ci * feats, feats), feats)
    copies = start_copies(
        [(qkv_hbm.at[layer, :, :, span], qkv), (out_hbm.at[layer, span, :], out)], sems
    )
    copies[0].wait()
    for k in range(3):
        packed_ref[:, k * feats : (k + 1) * feats] = qkv[k]
    copies[1].wait()
    packed_ref[:, 3 * feats :] = out[...].T
    token[...] = jnp.zeros_like(token)


def pack_first_kernel(feats, qkv_hbm, out_hbm, gains, shifts, units, heads_ref,
                      packed_ref, token, qkv, out, sems):
    width_own = qkv.shape[1]
    weights = packed_ref.at[pl.ds(0, width_own), :]
    pack_attn_kernel(0, feats, qkv_hbm, out_hbm, weights, token, qkv, out, sems)
    packed_ref[width_own:, :] = jnp.zeros_like(packed_ref[width_own:, :])
    depth = gains.shape[0]
    ci = lax.rem(lax.axis_index("ctx"), GROUP)
    lines = [gains[l].astype(f32) for l in range(depth)]
    lines += [shifts[l].astype(f32) for l in range(depth)]
    for l in range(depth):
        for first in range(0, units.shape[2], width_own):
            lines.append(units[l, :, first : first + width_own].astype(f32))
    lines = jnp.concatenate(lines, axis=0)
    count = lines.shape[0]
    packed_ref[width_own : width_own + count, :width_own] = lines.astype(bf16)
    heads = heads_ref.shape[2] // GROUP
    values = []
    for l in range(depth):
        for j in range(2):
            rows = heads_ref[l, j].astype(f32)
            for h in range(heads):
                value = rows[h : h + 1, :]
                for c in range(1, GROUP):
                    value = jnp.where(ci == c, rows[c * heads + h : c * heads + h + 1, :], value)
                values.append(value)
    values = jnp.concatenate(values, axis=1)
    packed_ref[width_own + count : width_own + count + 1, : values.shape[1]] = values.astype(bf16)


def unpack_first_kernel(feats, head_dim, *refs):
    *chunks, weights_ref, vecs_ref, units_ref, heads_ref = refs
    fsdp = len(chunks)
    width_own = weights_ref.shape[0] // fsdp
    f = lax.axis_index("fsdp")
    ci = lax.rem(lax.axis_index("ctx"), GROUP)
    for d, chunk in enumerate(chunks):
        place = lax.rem(f + (fsdp - d), fsdp)
        span = pl.ds(pl.multiple_of(place * width_own, width_own), width_own)
        weights_ref[span, :] = chunk[:width_own, :]
    below = [chunk[width_own:, :].astype(f32) for chunk in chunks]
    shard = []
    for a in range(fsdp):
        found = below[0]
        for d in range(1, fsdp):
            found = jnp.where(lax.rem(f + (fsdp - d), fsdp) == a, below[d], found)
        shard.append(found)
    vec_rows = vecs_ref.shape[0]
    for a in range(fsdp):
        vecs_ref[:, a * width_own : (a + 1) * width_own] = shard[a][:vec_rows, :width_own]
    mine = shard[0]
    for a in range(1, fsdp):
        mine = jnp.where(ci == a, shard[a], mine)
    depth = units_ref.shape[0]
    parts = units_ref.shape[2] // width_own
    for l in range(depth):
        for k in range(parts):
            row = vec_rows + l * parts + k
            units_ref[l, :, k * width_own : (k + 1) * width_own] = mine[row : row + 1, :width_own]
    row = vec_rows + depth * parts
    head_own = head_dim // fsdp
    heads = feats // head_dim
    for l in range(depth):
        for j in range(2):
            pieces = []
            for h in range(heads):
                first = ((2 * l + j) * heads + h) * head_own
                for a in range(fsdp):
                    pieces.append(shard[a][row : row + 1, first : first + head_own])
            heads_ref[l, j : j + 1, :] = jnp.concatenate(pieces, axis=1)


def pack_mlp_kernel(layer, hidden, fc1_hbm, fc2_hbm, packed_ref, token, fc1, fc2, sems):
    ci = lax.rem(lax.axis_index("ctx"), GROUP)
    span = pl.ds(pl.multiple_of(ci * hidden, hidden), hidden)
    copies = start_copies(
        [(fc1_hbm.at[layer, :, span], fc1), (fc2_hbm.at[layer, span, :], fc2)], sems
    )
    copies[0].wait()
    packed_ref[:, :hidden] = fc1[...]
    copies[1].wait()
    packed_ref[:, hidden:] = fc2[...].T
    token[...] = jnp.zeros_like(token)


def prep_upstream_kernel(tp, outer, lengths, cotangent_hbm,
                         upstream_hbm, upstream_b_ref, usable_ref, mask_ref,
                         rows_in, upstream_ref, sems):
    rows = rows_in.shape[0]
    c = lax.axis_index("ctx")
    t = lax.axis_index("tp")
    place = lax.rem(c, GROUP) * tp + t
    start = pl.multiple_of(t * rows, rows)
    copies = start_copies(
        [(cotangent_hbm.at[0, pl.ds(start, rows), :], rows_in)], sems.at[pl.ds(0, 1)]
    )
    lane = lax.broadcasted_iota(jnp.int32, usable_ref.shape, 1)
    limit = jnp.zeros(usable_ref.shape, jnp.int32)
    for o in range(outer):
        for k, d in enumerate(ORDER):
            source = place ^ d
            first_lane = (o * len(ORDER) + k) * rows
            count = lengths[0, o * GROUP + lax.div(source, tp)] - lax.rem(source, tp) * rows
            limit = jnp.where(lane >= first_lane, first_lane + jnp.clip(count, 0, rows), limit)
    usable_ref[...] = jnp.where(lane < limit, 1.0, 0.0)
    row = lax.broadcasted_iota(jnp.int32, mask_ref.shape, 0)
    mask = jnp.where(row + start < lengths[0, c], 1.0, 0.0)
    mask_ref[...] = mask
    copies[0].wait()
    upstream = rows_in[...] * mask[:, 0:1]
    upstream_ref[...] = upstream
    sent = start_copies([(upstream_ref, upstream_hbm)], sems.at[pl.ds(1, 1)])
    upstream_b_ref[...] = upstream.astype(bf16)
    sent[0].wait()


def prep_first_kernel(inputs_hbm, stream_ref, first_ref, sems):
    rows = stream_ref.shape[0]
    start = pl.multiple_of(lax.axis_index("tp") * rows, rows)
    copies = start_copies([(inputs_hbm.at[0, pl.ds(start, rows), :], stream_ref)], sems)
    copies[0].wait()
    first_ref[...] = normalize(stream_ref[...])[0].astype(bf16)


def keep_rows_kernel(*refs):
    chunks, (near_hbm, far_hbm, token, near, far, sems) = refs[:8], refs[8:]
    assemble(chunks[:4], near)
    assemble(chunks[4:], far)
    for copy in start_copies([(near, near_hbm), (far, far_hbm)], sems):
        copy.wait()
    token[...] = jnp.zeros_like(token)


def qkv_kernel(feats, weight_count, shift_row, *refs):
    c0, c1, c2, c3, *rest = refs
    weights = rest[:weight_count]
    if shift_row is None:
        bias, qkv_ref, x = rest[weight_count:]
        assemble((c0, c1, c2, c3), x)
    else:
        bias, vecs, qkv_ref, x = rest[weight_count:]
        rows = c0.shape[0]
        gain, shift = vecs[0:1, :], vecs[shift_row : shift_row + 1, :]
        for k, chunk in enumerate((c0, c1, c2, c3)):
            value = chunk[...].astype(f32) * gain + shift
            x[k * rows : (k + 1) * rows, :] = value.astype(bf16)
    qkv = sum(dot(x[:, span], w[:, : 3 * feats]) for span, w in shards(weights))
    qkv_ref[:, :feats] = (qkv[:, :feats] + bias[0:1, :]).astype(bf16)
    qkv_ref[:, feats : 2 * feats] = qkv[:, feats : 2 * feats].astype(bf16)
    qkv_ref[:, 2 * feats :] = (qkv[:, 2 * feats :] + bias[1:2, :]).astype(bf16)


def attn_kernel(feats, heads, weight_count, part_count, keep_count, tile, *refs):
    q_ref, *rest = refs
    parts = rest[:part_count]
    weights = rest[part_count : part_count + weight_count]
    rest = rest[part_count + weight_count :]
    usable, *rest = rest
    kept, rest = rest[:keep_count], rest[keep_count:]
    partial_ref, attended_hbm, norm_hbm, *rest = rest
    kept_hbm, rest = rest[:keep_count], rest[keep_count:]
    keys, values, attended_ref, norm_ref, sems = rest
    head_dim = feats // heads
    scale = 1.0 / math.sqrt(head_dim)
    copies = start_copies(list(zip(kept, kept_hbm)), sems)
    first = 0
    for part in parts:
        rows, width = part.shape
        keys[first : first + rows, :] = part[:, width - 2 * feats : width - feats]
        values[first : first + rows, :] = part[:, width - feats :]
        first += rows
    keep = usable[...] > 0.5
    rows = q_ref.shape[0]
    for first in range(0, rows, tile):
        span = slice(first, first + tile)
        q = q_ref[span, :feats]
        attended = None
        for h in range(heads):
            own = lanes_of(h, head_dim, feats)
            scores = dot_nt(only(own, q), keys[...]) * scale
            scores = jnp.where(keep, scores, MASK_FILL)
            highest = jnp.max(scores, axis=-1, keepdims=True)
            raised = jnp.exp(scores - highest)
            total = jnp.sum(raised, axis=-1, keepdims=True)
            soft = (raised * (1.0 / total)).astype(bf16)
            result = dot(soft, values[...])
            log_norm = jnp.broadcast_to(highest + jnp.log(total), (tile, feats))
            if attended is None:
                attended, norms = result, log_norm
            else:
                attended = jnp.where(own, result, attended)
                norms = jnp.where(own, log_norm, norms)
        attended_ref[span, :] = attended.astype(bf16)
        norm_ref[span, :] = norms
    copies += start_copies(
        [(attended_ref, attended_hbm), (norm_ref, norm_hbm)],
        sems.at[pl.ds(keep_count, 2)],
    )
    for span, w in shards(weights):
        partial_ref[:, span] = dot_nt(attended_ref[...], w[:, 3 * feats :]).astype(bf16)
    for copy in copies:
        copy.wait()


def core_sum_kernel(count, *refs):
    pairs, owns = refs[: 2 * count], refs[2 * count : 3 * count]
    peers = refs[3 * count :]
    rows = owns[0].shape[0]
    for j in range(count):
        near, far = pairs[2 * j], pairs[2 * j + 1]
        for k in range(1 + len(peers)):
            span = slice(k * rows, (k + 1) * rows)
            total = near[span, :].astype(f32) + far[span, :].astype(f32)
            if k == 0:
                owns[j][...] = total
            else:
                peers[k - 1][j * rows : (j + 1) * rows, :] = total.astype(bf16)


def total_of(own, xy, x, y, part=0):
    rows = own.shape[0]
    span = slice(part * rows, (part + 1) * rows)
    return (
        own[...] + y[span, :].astype(f32) + x[span, :].astype(f32) + xy[span, :].astype(f32)
    )


def sum_norm_kernel(bias_row, gain_row, shift_row, own, xy, x, y, residual_hbm, vecs,
                    stream_ref, normed_ref, residual, sems):
    copies = start_copies([(residual_hbm, residual)], sems)
    total = total_of(own, xy, x, y) + vecs[bias_row : bias_row + 1, :]
    copies[0].wait()
    stream = residual[...] + total
    stream_ref[...] = stream
    normed, _ = normalize(stream)
    gain = vecs[gain_row : gain_row + 1, :]
    normed_ref[...] = (normed * gain + vecs[shift_row : shift_row + 1, :]).astype(bf16)


def sum_out_kernel(bias_row, own, xy, x, y, residual_hbm, vecs, mask, out_hbm, token,
                   residual, out_ref, sems):
    copies = start_copies([(residual_hbm, residual)], sems.at[pl.ds(0, 1)])
    total = total_of(own, xy, x, y, 1) + vecs[bias_row : bias_row + 1, :]
    copies[0].wait()
    out_ref[...] = (residual[...] + total) * mask[:, 0:1]
    token[...] = jnp.zeros_like(token)
    for copy in start_copies([(out_ref, out_hbm)], sems.at[pl.ds(1, 1)]):
        copy.wait()


def mlp_kernel(hidden, keep_count, saves, c0, c1, c2, c3, w, bias, *refs):
    kept, rest = refs[:keep_count], refs[keep_count:]
    partial_ref, x_out, act_out, slope_out, *rest = rest
    kept_hbm, rest = rest[:keep_count], rest[keep_count:]
    if saves:
        x, act_ref, slope_ref, sems = rest
    else:
        x, act_ref, slope_ref = x_out, act_out, slope_out
        (sems,) = rest
    copies = start_copies(list(zip(kept, kept_hbm)), sems)
    assemble((c0, c1, c2, c3), x)
    if saves:
        copies += start_copies([(x, x_out)], sems.at[pl.ds(keep_count, 1)])
    block = hidden // 2
    for k in range(2):
        span = slice(k * block, (k + 1) * block)
        pre = dot(x[...], w[:, span]) + bias[:, span]
        cdf = 0.5 * (1.0 + lax.erf(pre * ROOT_HALF))
        density = jnp.exp(-0.5 * pre * pre) * INV_ROOT_TAU
        slope_ref[k] = cdf + pre * density
        act_ref[:, span] = (pre * cdf).astype(bf16)
        if saves:
            copies += start_copies(
                [(slope_ref.at[k], slope_out.at[k])], sems.at[pl.ds(1 + keep_count + k, 1)]
            )
    if saves:
        copies += start_copies([(act_ref, act_out)], sems.at[pl.ds(3 + keep_count, 1)])
    partial_ref[...] = dot_nt(act_ref[...], w[:, hidden:]).astype(bf16)
    for copy in copies:
        copy.wait()


def mlp_back_kernel(hidden, chunk_count, *refs):
    chunks, (w, slope_hbm, *rest) = refs[:chunk_count], refs[chunk_count:]
    partial_ref, grad_ref, sum_hbm, x, slope, sum_ref, sems = rest
    copies = start_copies([(slope_hbm, slope)], sems)
    if chunk_count == 1:
        copies += start_copies([(chunks[0], x)], sems.at[pl.ds(1, 1)])
        copies[1].wait()
    else:
        assemble(chunks, x)
    grad = dot(x[...], w[:, hidden:])
    copies[0].wait()
    block = hidden // 2
    for k in range(2):
        span = slice(k * block, (k + 1) * block)
        part = grad[:, span] * slope[k]
        grad_ref[:, span] = part.astype(bf16)
        sum_ref[:, span] = jnp.sum(part, axis=0, keepdims=True)
    sent = start_copies([(sum_ref, sum_hbm)], sems.at[pl.ds(2, 1)])
    partial_ref[...] = dot_nt(grad_ref[...], w[:, :hidden]).astype(bf16)
    sent[0].wait()


def mlp_grad_kernel(hidden, second_near, second_far, act_near, act_far, up_near, up_far,
                    grad_near, grad_far, passed, sums, middle, out_hbm, passed_ref, sums_hbm,
                    middle_hbm, second, act, up, grad, out_one, out_two, sems):
    rows = up_near.shape[0]
    sent = start_copies([(sums, sums_hbm), (middle, middle_hbm)], sems.at[pl.ds(6, 2)])
    near, far = pl.ds(0, rows), pl.ds(rows, rows)
    copies = start_copies(
        [
            (act_near, act.at[near]),
            (act_far, act.at[far]),
            (second_near, second.at[near]),
            (second_far, second.at[far]),
        ],
        sems,
    )
    passed_ref[...] = passed[...]
    up[:rows, :] = up_near[...]
    up[rows:, :] = up_far[...]
    grad[:rows, :] = grad_near[...]
    grad[rows:, :] = grad_far[...]
    for copy in copies[:2]:
        copy.wait()
    out_two[...] = dot_tn(up[...], act[...]).astype(bf16)
    sent += start_copies(
        [(out_two, out_hbm.at[:, pl.ds(hidden, hidden)])], sems.at[pl.ds(4, 1)]
    )
    for copy in copies[2:]:
        copy.wait()
    out_one[...] = dot_tn(second[...], grad[...]).astype(bf16)
    sent += start_copies([(out_one, out_hbm.at[:, pl.ds(0, hidden)])], sems.at[pl.ds(5, 1)])
    for copy in sent:
        copy.wait()


def norm_back(upstream, values, gain):
    normed, inverse = normalize(values)
    scaled = upstream * gain
    back = inverse * (scaled - row_mean(scaled) - normed * row_mean(scaled * normed))
    gain_grad = jnp.sum(upstream * normed, axis=0, keepdims=True)
    return back, gain_grad, jnp.sum(upstream, axis=0, keepdims=True)


def norm_back_two_kernel(gain_row, own, xy, x, y, values_hbm, upstream_hbm, vecs,
                         grad_ref, grad_b_ref, sums_ref, values, upstream, sems):
    copies = start_copies([(values_hbm, values), (upstream_hbm, upstream)], sems)
    total = total_of(own, xy, x, y)
    for copy in copies:
        copy.wait()
    up = upstream[...]
    back, gain_grad, shift_grad = norm_back(
        total, values[...], vecs[gain_row : gain_row + 1, :]
    )
    grad = up + back
    grad_ref[...] = grad
    grad_b_ref[...] = grad.astype(bf16)
    sums_ref[0:1, :] = gain_grad
    sums_ref[1:2, :] = shift_grad
    sums_ref[2:3, :] = jnp.sum(grad, axis=0, keepdims=True)
    sums_ref[3:4, :] = jnp.sum(up, axis=0, keepdims=True)


def norm_back_one_kernel(gain_row, own, xy, x, y, values_hbm, upstream_hbm, vecs, mask,
                         grad_ref, grad_b_ref, sums_ref, values, upstream, sems):
    copies = start_copies([(values_hbm, values), (upstream_hbm, upstream)], sems)
    total = total_of(own, xy, x, y)
    for copy in copies:
        copy.wait()
    back, gain_grad, shift_grad = norm_back(
        total, values[...], vecs[gain_row : gain_row + 1, :]
    )
    grad = upstream[...] + back
    if mask is not None:
        grad = grad * mask[:, 0:1]
    grad_ref[...] = grad
    grad_b_ref[...] = grad.astype(bf16)
    sums_ref[0:1, :] = gain_grad
    sums_ref[1:2, :] = shift_grad


def attn_back_kernel(feats, heads, weight_count, part_count, tile, carried, *refs):
    c0, c1, c2, c3, *rest = refs
    weights, rest = rest[:weight_count], rest[weight_count:]
    usable, q_hbm, attended_hbm, norm_hbm, *rest = rest
    parts, rest = rest[:part_count], rest[part_count:]
    if carried:
        keys_before, values_before, *rest = rest
    x, grad_q, grad_k, grad_v, pairs, q_ref, attended, norms, grad_att, sems = rest
    head_dim = feats // heads
    scale = 1.0 / math.sqrt(head_dim)
    moves = [(q_hbm.at[:, pl.ds(0, feats)], q_ref), (attended_hbm, attended), (norm_hbm, norms)]
    first = 0
    for part in parts:
        rows, width = part.shape
        moves.append(
            (part.at[:, pl.ds(width - 2 * feats, 2 * feats)], pairs.at[pl.ds(first, rows)])
        )
        first += rows
    copies = start_copies(moves, sems)
    assemble((c0, c1, c2, c3), x)
    grad_att[...] = sum(
        dot(x[:, span], w[:, 3 * feats :]) for span, w in shards(weights)
    ).astype(bf16)
    keep = usable[...] > 0.5
    rows = q_ref.shape[0]
    if carried:
        sum_k, sum_v = keys_before[...], values_before[...]
    else:
        sum_k = jnp.zeros(grad_k.shape, f32)
        sum_v = jnp.zeros(grad_v.shape, f32)
    for copy in copies:
        copy.wait()
    keys, values = pairs[:, :feats], pairs[:, feats:]
    for first in range(0, rows, tile):
        span = slice(first, first + tile)
        q = q_ref[span, :]
        ga = grad_att[span, :]
        products = ga.astype(f32) * attended[span, :].astype(f32)
        gq = None
        for h in range(heads):
            own = lanes_of(h, head_dim, feats)
            q_h = only(own, q)
            ga_h = only(own, ga)
            row_dots = jnp.sum(only(own, products), axis=-1, keepdims=True)
            scores = dot_nt(q_h, keys) * scale
            scores = jnp.where(keep, scores, MASK_FILL)
            soft = jnp.exp(scores - norms[span, h * head_dim : h * head_dim + 1])
            grad_soft = dot_nt(ga_h, values)
            grad_scores = (soft * (grad_soft - row_dots)).astype(bf16)
            part = dot(grad_scores, keys)
            gq = part if gq is None else jnp.where(own, part, gq)
            sum_k = sum_k + dot_tn(grad_scores, q_h) * scale
            sum_v = sum_v + dot_tn(soft.astype(bf16), ga_h)
        grad_q[span, :] = gq * scale
    grad_k[...] = sum_k
    grad_v[...] = sum_v


def project_kernel(feats, first, weight_count, gq, gk, gv, *refs):
    weights, (partial_ref, packed) = refs[:weight_count], refs[weight_count:]
    rows = gq.shape[0]
    span = slice(first, first + rows)
    packed[:, :feats] = gq[...].astype(bf16)
    packed[:, feats : 2 * feats] = gk[span, :].astype(bf16)
    packed[:, 2 * feats :] = gv[span, :].astype(bf16)
    for columns, w in shards(weights):
        partial_ref[:, columns] = dot_nt(packed[...], w[:, : 3 * feats]).astype(bf16)


def attn_grad_kernel(feats, count, first_near, first_far, att_near, att_far, up_near, up_far,
                     gq_near, gq_far, gk, gv, passed, sums, stream, lines, *refs):
    outs, rest = refs[:count], refs[count:]
    heads_hbm, passed_ref, sums_hbm, stream_hbm, *rest = rest
    first, att, up, packed, sums_ref, *staged, sems = rest
    rows = up_near.shape[0]
    sent = start_copies([(sums, sums_hbm), (stream, stream_hbm)], sems.at[pl.ds(6, 2)])
    near, far = pl.ds(0, rows), pl.ds(rows, rows)
    copies = start_copies(
        [
            (att_near, att.at[near]),
            (att_far, att.at[far]),
            (first_near, first.at[near]),
            (first_far, first.at[far]),
        ],
        sems,
    )
    passed_ref[...] = passed[...]
    up[:rows, :] = up_near[...]
    up[rows:, :] = up_far[...]
    packed[:rows, :feats] = gq_near[...].astype(bf16)
    packed[rows:, :feats] = gq_far[...].astype(bf16)
    packed[:, feats : 2 * feats] = gk[...].astype(bf16)
    packed[:, 2 * feats :] = gv[...].astype(bf16)
    sums_ref[0:1, :] = jnp.sum(gq_near[...], axis=0, keepdims=True) + jnp.sum(
        gq_far[...], axis=0, keepdims=True
    )
    sums_ref[1:2, :] = jnp.sum(gv[...], axis=0, keepdims=True)
    sent += start_copies([(sums_ref, heads_hbm)], sems.at[pl.ds(8, 1)])
    if count == 1:
        out_one, out_two = staged
        for copy in copies[:2]:
            copy.wait()
        out_two[...] = dot_tn(up[...], att[...]).astype(bf16)
        sent += start_copies(
            [(out_two, outs[0].at[:, pl.ds(3 * feats, feats)])], sems.at[pl.ds(4, 1)]
        )
        for copy in copies[2:]:
            copy.wait()
        out_one[...] = dot_tn(first[...], packed[...]).astype(bf16)
        sent += start_copies(
            [(out_one, outs[0].at[:, pl.ds(0, 3 * feats)])], sems.at[pl.ds(5, 1)]
        )
        for copy in sent:
            copy.wait()
        return
    (stage,) = staged
    for copy in copies:
        copy.wait()
    below = lines.shape[1]
    width_own = outs[0].shape[0] - below
    for d in reversed(range(count)):
        place = lax.rem(lax.axis_index("fsdp") + d, count)
        span = pl.ds(pl.multiple_of(place * width_own, width_own), width_own)
        stage[d, :width_own, : 3 * feats] = dot_tn(first[:, span], packed[...]).astype(bf16)
        stage[d, :width_own, 3 * feats :] = dot_tn(up[:, span], att[...]).astype(bf16)
        stage[d, width_own:, :] = lines[d]
        sent += start_copies([(stage.at[d], outs[d])], sems.at[pl.ds(9 + d, 1)])
    for copy in sent:
        copy.wait()


def settle_kernel(passed, *refs):
    passed_ref = refs[-1]
    passed_ref[...] = passed[...]


def fetch_kernel(count, *refs):
    sources, (target, sems) = refs[:count], refs[count:]
    columns = target.shape[1]
    moves = []
    row = 0
    for source in sources:
        rows = source.shape[0]
        for first in range(0, source.shape[1], columns):
            moves.append(
                (source.at[:, pl.ds(first, columns)], target.at[pl.ds(row, rows), :])
            )
            row += rows
    for copy in start_copies(moves, sems):
        copy.wait()


def shard_sum_kernel(depth, own_hbm, stacked, crossed, *refs):
    *others, part_ref, mine_ref, pair_ref, own, sems = refs
    count = stacked.shape[0]
    first, *copies = start_copies(
        [
            (own_hbm, own),
            (stacked, pair_ref.at[pl.ds(0, count), :]),
            (crossed, pair_ref.at[pl.ds(count, count), :]),
        ],
        sems,
    )
    first.wait()
    rows, width = part_ref.shape[0], mine_ref.shape[1]
    terms = [ref[...].astype(f32) for ref in (own, *others)]
    total = terms[0]
    for term in terms[1:]:
        total = total + term
    part_ref[...] = total[:rows, :].astype(bf16)
    lines = total[rows:, :width] + total[rows:, width:]
    mine_ref[: 6 * depth, :] = lines[: 6 * depth, :]
    for k in range(mine_ref.shape[0] - 16):
        mine_ref[16 + k : 17 + k, :] = lines[6 * depth + k : 6 * depth + k + 1, :]
    for copy in copies:
        copy.wait()


def place_kernel(depth, hidden, feats, *refs):
    alone, pairs, rest = refs[:2], refs[2:4], refs[4:]

    def half_of(pair, k):
        count = pair[k % 2].shape[0] // 2
        return pair[k % 2].at[pl.ds(k // 2 * count, count), :]

    slices = [(half_of(alone, k), half_of(pairs, k)) for k in range(GROUP)]
    qkv_hbm, out_hbm, fc1_hbm, fc2_hbm, fc1, fc2, qkv, out, sems = rest
    ci = lax.rem(lax.axis_index("ctx"), GROUP)
    rows = fc1.shape[2]
    copies = []

    def send(source, target):
        copies.extend(start_copies([(source, target)], sems.at[pl.ds(len(copies), 1)]))

    for l in range(depth):
        for k in range(GROUP):
            _, stacked = slices[k]
            first = 0 if l == 0 else (3 * l - 1) * rows
            span = pl.ds(pl.multiple_of((ci ^ k) * hidden, hidden), hidden)
            fc1[l, k] = stacked[first : first + rows, :].astype(f32)
            send(fc1.at[l, k], fc1_hbm.at[l, :, span])
            fc2[l, k] = stacked[first + rows : first + 2 * rows, :].T.astype(f32)
            send(fc2.at[l, k], fc2_hbm.at[l, span, :])
    for l in reversed(range(depth)):
        for k in range(GROUP):
            last, stacked = slices[k]
            piece = last if l == 0 else stacked.at[pl.ds((3 * l + 1) * rows, rows), :]
            span = pl.ds(pl.multiple_of((ci ^ k) * feats, feats), feats)
            for j in range(3):
                qkv[l, k, j] = piece[:, j * feats : (j + 1) * feats].astype(f32)
            send(qkv.at[l, k], qkv_hbm.at[l, :, :, span])
            out[l, k] = piece[:, 3 * feats :].T.astype(f32)
            send(out.at[l, k], out_hbm.at[l, span, :])
    for copy in copies:
        copy.wait()


def vector_pack_kernel(depth, one_now, gq_near, gq_far, gv, *refs):
    count = 5 * depth - 2
    out_ref, *found, sems = refs[count:]
    copies = start_copies(list(zip(refs[:count], found)), sems)
    out_ref[...] = jnp.zeros_like(out_ref)
    feats = gv.shape[1]
    head_now = [
        jnp.sum(gq_near[...], axis=0, keepdims=True) + jnp.sum(gq_far[...], axis=0, keepdims=True),
        jnp.sum(gv[...], axis=0, keepdims=True),
    ]
    for copy in copies:
        copy.wait()
    for l in range(depth):
        if l == 0:
            one, (two, unit_near, unit_far) = one_now, found[:3]
            heads = head_now
        else:
            one, two, unit_near, unit_far, head = found[5 * l - 2 : 5 * l + 3]
            heads = [head[0:1, :], head[1:2, :]]
        out_ref[6 * l : 6 * l + 1, :] = one[0:1, :]
        out_ref[6 * l + 1 : 6 * l + 2, :] = two[0:1, :]
        out_ref[6 * l + 2 : 6 * l + 3, :] = one[1:2, :]
        out_ref[6 * l + 3 : 6 * l + 6, :] = two[1:4, :]
        units = unit_near.shape[1]
        row = 6 * depth
        out_ref[row : row + 1, l * units : (l + 1) * units] = unit_near[...] + unit_far[...]
        for j in range(2):
            start = (2 * l + j) * feats
            out_ref[row + 1 : row + 2, start : start + feats] = heads[j]


def vector_lines_kernel(depth, width_own, packed, lines_ref):
    count = lines_ref.shape[0]
    f = lax.axis_index("fsdp")
    total = packed[...]
    high = total.astype(bf16).astype(f32)
    low = total - high
    lines_ref[...] = jnp.zeros_like(lines_ref)
    last = 6 * depth
    for k, value in enumerate((high, low)):
        lanes = slice(k * width_own, (k + 1) * width_own)
        columns = [value[:, a * width_own : (a + 1) * width_own] for a in range(count)]
        for d in range(count):
            mine = columns[0]
            for a in range(1, count):
                mine = jnp.where(lax.rem(f + d, count) == a, columns[a], mine)
            rows = [mine[:last, :]]
            for r in range(2):
                for a in range(count):
                    rows.append(columns[a][last + r : last + r + 1, :])
            rows.append(jnp.zeros((lines_ref.shape[1] - last - 2 * count, width_own), f32))
            lines_ref[d, :, lanes] = jnp.concatenate(rows, axis=0).astype(bf16)


def vector_plane_kernel(depth, own, xy, x, y, part, part_x, out_ref, pair_ref):
    last = 6 * depth
    rows = part.shape[0]
    pair_ref[:rows, :] = part[...]
    pair_ref[rows:, :] = part_x[...]
    out_ref[:last, :] = own[:last, :] + xy[:last, :] + x[:last, :] + y[:last, :]
    out_ref[16:24, :] = own[16:24, :]
    out_ref[24:32, :] = x[16:24, :]


def vector_place_kernel(depth, head_dim, own, far, gains_ref, shifts_ref, unit_ref, heads_ref):
    total = own[: 6 * depth, :] + far[: 6 * depth, :]
    for l in range(depth):
        gains_ref[l] = total[6 * l : 6 * l + 2, :]
        shifts_ref[l] = total[6 * l + 2 : 6 * l + 6, :]
    pieces = (own[16:24, :], far[16:24, :], own[24:32, :], far[24:32, :])
    ci = lax.rem(lax.axis_index("ctx"), GROUP)
    f = lax.axis_index("fsdp")

    def of_place(c):
        k = ci ^ c
        found = pieces[0]
        for j in range(1, GROUP):
            found = jnp.where(k == j, pieces[j], found)
        return found

    width_own = own.shape[1]
    units = of_place(f)
    parts = unit_ref.shape[2] // width_own
    for l in range(depth):
        for j in range(parts):
            row = l * parts + j
            unit_ref[l, :, j * width_own : (j + 1) * width_own] = units[row : row + 1, :]
    head_own = heads_ref.shape[3]
    heads = heads_ref.shape[2] // GROUP
    for c in range(GROUP):
        found = of_place(c)
        for l in range(depth):
            for j in range(2):
                for h in range(heads):
                    first = ((2 * l + j) * heads + h) * head_dim
                    row, lane = 4 + first // width_own, first % width_own
                    value = found[row : row + 1, lane : lane + head_own]
                    for a in range(1, head_dim // head_own):
                        start = lane + a * head_own
                        value = jnp.where(
                            f == a, found[row : row + 1, start : start + head_own], value
                        )
                    heads_ref[l, j, c * heads + h : c * heads + h + 1, :] = value


def place_rows_kernel(own, other, out_hbm, sems):
    rows = own.shape[0]
    start = pl.multiple_of(lax.axis_index("tp") * rows, rows)
    copies = start_copies(
        [
            (own, out_hbm.at[0, pl.ds(start, rows), :]),
            (other, out_hbm.at[0, pl.ds(pl.multiple_of(rows - start, rows), rows), :]),
        ],
        sems,
    )
    for copy in copies:
        copy.wait()


def per_device(
    inputs, lengths, cotangent, norm_gains, shifts, qv_bias, fc1_bias, w_qkv, w_out, w_fc1, w_fc2
):
    depth = w_qkv.shape[0]
    width_own = w_qkv.shape[2]
    fsdp = lax.axis_size("fsdp")
    tp = lax.axis_size("tp")
    ctx = lax.axis_size("ctx")
    outer = ctx // GROUP
    rows = inputs.shape[1] // tp
    half = rows * CHIPS
    all_rows = 2 * half
    head_own = qv_bias.shape[3]
    head_dim = head_own * fsdp
    heads = qv_bias.shape[2] // GROUP
    feats = heads * head_dim
    hidden = w_fc1.shape[2] // GROUP
    width = width_own * fsdp
    t = lax.axis_index("tp")
    f = lax.axis_index("fsdp")
    ci = lax.axis_index("ctx") % GROUP
    tile = half // 2
    attn_limit = 12 if outer == 1 else 48

    def swap_core(value):
        return lax.ppermute(value, "ctx", [(i, i ^ 1) for i in range(ctx)])

    def swap_x(value):
        return lax.ppermute(value, "ctx", [(i, i ^ 2) for i in range(ctx)])

    def swap_y(value):
        return lax.ppermute(value, "tp", [(i, i ^ 1) for i in range(tp)])

    def swap_xy(value):
        pairs = [
            (i * tp + k, (i ^ 2) * tp + (k ^ 1)) for i in range(ctx) for k in range(tp)
        ]
        return lax.ppermute(value, ("ctx", "tp"), pairs)

    def shift_z(value, d):
        return lax.ppermute(value, "fsdp", [(i, (i + d) % fsdp) for i in range(fsdp)])

    outer_groups = [[o * GROUP + i for o in range(outer)] for i in range(GROUP)]

    def gather_rows(own):
        near = (own, swap_xy(own), swap_x(own), swap_y(own))
        return near, tuple(swap_core(chunk) for chunk in near)

    def settle(value, *after):
        return kernel_call(
            settle_kernel, [(value.shape, value.dtype)], value, name="settle", after=after
        )[0]

    def reduce_rows(*pairs, after=()):
        count = len(pairs)
        *owns, xy, x, y = kernel_call(
            functools.partial(core_sum_kernel, count),
            [((rows, width), f32)] * count + [((count * rows, width), bf16)] * 3,
            *[v for near, far in pairs for v in (near, swap_core(far))],
            name="core_sum",
            after=after,
        )
        peers = (swap_xy(xy), swap_x(x), swap_y(y))
        return [(own, *peers) for own in owns]

    def pack_attn(l, after):
        return kernel_call(
            functools.partial(pack_attn_kernel, l, feats),
            [((width_own, 4 * feats), bf16), TOKEN],
            Far(w_qkv),
            Far(w_out),
            name="pack_attn",
            after=after,
            scratch=[
                pltpu.VMEM((3, width_own, feats), bf16),
                pltpu.VMEM((feats, width_own), bf16),
                DMA((2,)),
            ],
        )

    def pack_mlp(l, after):
        return kernel_call(
            functools.partial(pack_mlp_kernel, l, hidden),
            [((width_own, 2 * hidden), bf16), TOKEN],
            Far(w_fc1),
            Far(w_fc2),
            name="pack_mlp",
            after=after,
            scratch=[
                pltpu.VMEM((width_own, hidden), bf16),
                pltpu.VMEM((hidden, width_own), bf16),
                DMA((2,)),
            ],
        )

    first_own, token = kernel_call(
        functools.partial(pack_first_kernel, feats),
        [((width_own + 32, 4 * feats), bf16), TOKEN],
        Far(w_qkv),
        Far(w_out),
        norm_gains,
        shifts,
        fc1_bias,
        qv_bias,
        name="pack_first",
        scratch=[
            pltpu.VMEM((3, width_own, feats), bf16),
            pltpu.VMEM((feats, width_own), bf16),
            DMA((2,)),
        ],
    )
    first_shards = [first_own] + [shift_z(first_own, d) for d in range(1, fsdp)]
    attn_w = [None] * depth
    mlp_w = [None] * depth
    for l in range(depth):
        if l > 0:
            own, token = pack_attn(l, (token,))
            attn_w[l] = (lax.all_gather(own, "fsdp", axis=0, tiled=True),)
        own, token = pack_mlp(l, (token,))
        mlp_w[l] = lax.all_gather(own, "fsdp", axis=0, tiled=True)
        if l == 0:
            pack_token = token
    first_w, vecs, fc1_all, qv_all = kernel_call(
        functools.partial(unpack_first_kernel, feats, head_dim),
        [
            ((width, 4 * feats), bf16),
            ((6 * depth, width), f32),
            ((depth, 1, hidden), f32),
            ((depth, 2, feats), f32),
        ],
        *first_shards,
        name="unpack_first",
    )
    attn_w[0] = (first_w,)

    def gain_row(l, i):
        return 2 * l + i

    def shift_row(l, i):
        return 2 * depth + 4 * l + i

    key_rows = outer * all_rows
    row_f32 = ((rows, width), f32)
    row_bf16 = ((rows, width), bf16)
    upstream, upstream_b, usable, mask = kernel_call(
        functools.partial(prep_upstream_kernel, tp, outer),
        [saved((rows, width), f32), row_bf16, ((1, key_rows), f32), ((rows, 128), f32)],
        Scalars(lengths),
        Far(cotangent),
        name="prep_upstream",
        after=(pack_token,),
        scratch=[pltpu.VMEM((rows, width), f32), pltpu.VMEM((rows, width), f32), DMA((2,))],
    )
    near, far = gather_rows(upstream_b)
    half_x = pltpu.VMEM((half, width), bf16)
    *upstream_rows, upstream_token = kernel_call(
        keep_rows_kernel,
        [saved((half, width), bf16)] * 2 + [TOKEN],
        *near,
        *far,
        name="keep_rows",
        scratch=[half_x, half_x, DMA((2,))],
    )
    upstream_chunks = [(Far(x),) for x in upstream_rows]
    stream, first = kernel_call(
        prep_first_kernel,
        [row_f32, row_bf16],
        Far(inputs),
        name="prep_first",
        after=(pack_token,),
        scratch=[DMA((1,))],
    )
    first_chunks = gather_rows(first)

    partial_out = ((half, width), bf16)
    saved_all = []
    for l in range(depth):
        qkv = []
        first_x = []
        for side in (0, 1):
            qkv_half, x_half = kernel_call(
                functools.partial(
                    qkv_kernel, feats, len(attn_w[l]), shift_row(0, 0) if l == 0 else None
                ),
                [((half, 3 * feats), bf16), ((half, width), bf16)],
                *first_chunks[side],
                *attn_w[l],
                qv_all[l],
                *((vecs,) if l == 0 else ()),
                name="qkv",
                after=(upstream_token,) if l == 0 and side == 0 else (),
            )
            qkv.append(qkv_half)
            first_x.append(x_half)
        if outer > 1:
            pairs = jnp.concatenate([part[:, feats:] for part in qkv], axis=0)
            pairs = lax.all_gather(
                pairs, "ctx", axis=0, tiled=True, axis_index_groups=outer_groups
            )
            key_parts = (pairs,)
        else:
            key_parts = tuple(qkv)
        attn = [None, None]
        for side in (1, 0):
            kept = (first_x[side], qkv[side]) + ((stream,) if side == 1 else ())
            if l == 0 and side == 1:
                kept += attn_w[0]
            attn[side] = kernel_call(
                functools.partial(
                    attn_kernel, feats, heads, len(attn_w[l]), len(key_parts), len(kept), tile
                ),
                [partial_out, saved((half, feats), bf16), saved((half, feats), f32)]
                + [saved(k.shape, k.dtype) for k in kept],
                qkv[side],
                *key_parts,
                *attn_w[l],
                usable,
                *kept,
                name="attn",
                limit=attn_limit,
                scratch=[
                    pltpu.VMEM((key_rows, feats), bf16),
                    pltpu.VMEM((key_rows, feats), bf16),
                    pltpu.VMEM((half, feats), bf16),
                    pltpu.VMEM((half, feats), f32),
                    DMA((len(kept) + 2,)),
                ],
            )
        (sums,) = reduce_rows((attn[0][0], attn[1][0]))
        middle, second = kernel_call(
            functools.partial(sum_norm_kernel, shift_row(l, 2), gain_row(l, 1), shift_row(l, 1)),
            [row_f32, row_bf16],
            *sums,
            Far(attn[1][5]),
            vecs,
            name="sum_norm",
            scratch=[pltpu.VMEM((rows, width), f32), DMA((1,))],
        )
        second_chunks = gather_rows(second)
        mlp = [None, None]
        for side in (1, 0):
            kept = (middle,) if side == 1 else ()
            saves = l + 1 < depth
            shapes = [
                ((half, width), bf16),
                ((half, hidden), bf16),
                ((2, half, hidden // 2), f32),
            ]
            mlp[side] = kernel_call(
                functools.partial(mlp_kernel, hidden, len(kept), saves),
                [partial_out]
                + [saved(*shape) if saves else shape for shape in shapes]
                + [saved(k.shape, k.dtype) for k in kept],
                *second_chunks[side],
                mlp_w[l],
                fc1_all[l],
                *kept,
                name="mlp",
                scratch=[pltpu.VMEM(*shape) for shape in shapes if saves]
                + [DMA((4 + len(kept),))],
            )
            if saves:
                mlp[side] = [mlp[side][0], *[Far(v) for v in mlp[side][1:4]], *mlp[side][4:]]
        saved_all.append((attn, pairs if outer > 1 else None, mlp))
        if l + 1 < depth:
            (sums,) = reduce_rows((mlp[0][0], mlp[1][0]))
            stream, first = kernel_call(
                functools.partial(
                    sum_norm_kernel, shift_row(l, 3), gain_row(l + 1, 0), shift_row(l + 1, 0)
                ),
                [row_f32, row_bf16],
                *sums,
                Far(mlp[1][4]),
                vecs,
                name="sum_norm",
                scratch=[pltpu.VMEM((rows, width), f32), DMA((1,))],
            )
            first_chunks = gather_rows(first)

    def scatter_grads(grad):
        part = lax.psum_scatter(grad, "fsdp", scatter_dimension=0, tiled=True)
        if outer > 1:
            part = lax.psum(part, "ctx", axis_index_groups=outer_groups)
        return part

    row_sums = [None] * depth
    unit_sums = [None] * depth
    head_sums = [None] * depth
    mlp_parts = [None] * depth
    attn_parts = [None] * depth
    for l in reversed(range(depth)):
        attn, pairs, mlp = saved_all[l]
        if l == 0:
            attn_w[0] = (attn[1][6],)
        back = [None, None]
        for side in (1, 0):
            back[side] = kernel_call(
                functools.partial(mlp_back_kernel, hidden, len(upstream_chunks[side])),
                [
                    partial_out,
                    ((half, hidden), bf16),
                    saved((1, hidden), f32),
                    ((half, width), bf16),
                ],
                *upstream_chunks[side],
                mlp_w[l],
                mlp[side][3],
                name="mlp_back",
                scratch=[
                    pltpu.VMEM((2, half, hidden // 2), f32),
                    pltpu.VMEM((1, hidden), f32),
                    DMA((3,)),
                ],
            )
        pairs_now = [(back[0][0], back[1][0])]
        if l + 1 == depth:
            pairs_now.append((mlp[0][0], mlp[1][0]))
        sums, *output_sums = reduce_rows(*pairs_now)
        if l + 1 == depth:
            outputs_own, output_token = kernel_call(
                functools.partial(sum_out_kernel, shift_row(l, 3)),
                [saved((rows, width), f32), TOKEN],
                *output_sums[0],
                Far(mlp[1][4]),
                vecs,
                mask,
                name="sum_out",
                scratch=[pltpu.VMEM((rows, width), f32)] * 2 + [DMA((2,))],
            )
            after = (output_token,)
        else:
            after = ()
        unit_sums[l] = (back[0][2], back[1][2])
        grad_middle, middle_b, sums_two = kernel_call(
            functools.partial(norm_back_two_kernel, gain_row(l, 1)),
            [row_f32, row_bf16, ((4, width), f32)],
            *sums,
            Far(mlp[1][4]),
            Far(upstream),
            vecs,
            name="norm_back_two",
            scratch=[pltpu.VMEM((rows, width), f32)] * 2 + [DMA((2,))],
        )
        mlp_grad, middle_b, sums_two, grad_middle = kernel_call(
            functools.partial(mlp_grad_kernel, hidden),
            [
                saved((width, 2 * hidden), bf16),
                row_bf16,
                saved((4, width), f32),
                saved((rows, width), f32),
            ],
            mlp[0][1],
            mlp[1][1],
            mlp[0][2],
            mlp[1][2],
            back[0][3],
            back[1][3],
            back[0][1],
            back[1][1],
            middle_b,
            sums_two,
            grad_middle,
            name="mlp_grad",
            after=after,
            scratch=[
                pltpu.VMEM((all_rows, width), bf16),
                pltpu.VMEM((all_rows, hidden), bf16),
                pltpu.VMEM((all_rows, width), bf16),
                pltpu.VMEM((all_rows, hidden), bf16),
                pltpu.VMEM((width, hidden), bf16),
                pltpu.VMEM((width, hidden), bf16),
                DMA((8,)),
            ],
            limit=16,
        )
        mlp_parts[l] = scatter_grads(mlp_grad)
        if l + 1 < depth:
            middle_b = settle(middle_b, Far(mlp_parts[l + 1]))
        middle_chunks = gather_rows(middle_b)
        grad_q = [None, None]
        middle_x = [None, None]
        carried = ()
        for side in (0, 1):
            key_parts = (pairs,) if outer > 1 else (attn[0][4], attn[1][4])
            middle_x[side], grad_q[side], *carried = kernel_call(
                functools.partial(
                    attn_back_kernel,
                    feats,
                    heads,
                    len(attn_w[l]),
                    len(key_parts),
                    tile,
                    len(carried) > 0,
                ),
                [
                    ((half, width), bf16),
                    ((half, feats), f32),
                    ((key_rows, feats), f32),
                    ((key_rows, feats), f32),
                ],
                *middle_chunks[side],
                *attn_w[l],
                usable,
                Far(attn[side][4]),
                Far(attn[side][1]),
                Far(attn[side][2]),
                *[Far(part) for part in key_parts],
                *carried,
                name="attn_back",
                scratch=[
                    pltpu.VMEM((key_rows, 2 * feats), bf16),
                    pltpu.VMEM((half, feats), bf16),
                    pltpu.VMEM((half, feats), bf16),
                    pltpu.VMEM((half, feats), f32),
                    pltpu.VMEM((half, feats), bf16),
                    DMA((3 + len(key_parts),)),
                ],
                limit=attn_limit,
            )
        grad_k, grad_v = carried
        if outer > 1:
            grad_k, grad_v = (
                lax.psum_scatter(
                    v, "ctx", scatter_dimension=0, tiled=True, axis_index_groups=outer_groups
                )
                for v in (grad_k, grad_v)
            )

        def project(side, after):
            return kernel_call(
                functools.partial(project_kernel, feats, side * half, len(attn_w[l])),
                [partial_out],
                grad_q[side],
                grad_k,
                grad_v,
                *attn_w[l],
                name="project",
                after=after,
                scratch=[pltpu.VMEM((half, 3 * feats), bf16)],
            )[0]

        far_part = project(1, ())
        near_part = project(0, ())
        (sums,) = reduce_rows((near_part, far_part))
        body = functools.partial(norm_back_one_kernel, gain_row(l, 0))
        if l > 0:
            masked = ()
            body = lambda *refs, body=body: body(*refs[:7], None, *refs[7:])
        else:
            masked = (mask,)
        upstream, upstream_b, sums_one = kernel_call(
            body,
            [row_f32, row_bf16, ((2, width), f32)],
            *sums,
            Far(attn[1][5]),
            Far(grad_middle),
            vecs,
            *masked,
            name="norm_back_one",
            scratch=[pltpu.VMEM((rows, width), f32)] * 2 + [DMA((2,))],
        )
        lines = ()
        if l == 0:
            terms = [sums_two, *unit_sums[0]]
            for k in range(1, depth):
                terms += [*row_sums[k], *unit_sums[k], head_sums[k]]
            packed = kernel_call(
                functools.partial(vector_pack_kernel, depth),
                [((6 * depth + 2, width), f32)],
                sums_one,
                *grad_q,
                grad_v,
                *[Far(v) for v in terms],
                name="vector_pack",
                scratch=[pltpu.VMEM(v.shape, f32) for v in terms] + [DMA((len(terms),))],
            )[0]
            if outer > 1:
                packed = lax.psum(packed, "ctx", axis_index_groups=outer_groups)
            lines = kernel_call(
                functools.partial(vector_lines_kernel, depth, width_own),
                [((fsdp, 32, 2 * width_own), bf16)],
                packed,
                name="vector_lines",
            )
        count = 1 if l > 0 else fsdp
        shapes = [((width, 3 * feats), bf16), ((width, feats), bf16)]
        if l == 0:
            shapes = [((fsdp, width_own + 32, 4 * feats), bf16)]
        *attn_grads, head_sums[l], upstream_b, sums_one, upstream = kernel_call(
            functools.partial(attn_grad_kernel, feats, count),
            [saved((width if l > 0 else width_own + 32, 4 * feats), bf16)] * count
            + [
                saved((2, feats), f32),
                row_bf16,
                saved((2, width), f32),
                saved((rows, width), f32),
            ],
            Far(attn[0][3]),
            Far(attn[1][3]),
            Far(attn[0][1]),
            Far(attn[1][1]),
            *middle_x,
            *grad_q,
            grad_k,
            grad_v,
            upstream_b,
            sums_one,
            upstream,
            *(lines or (sums_one,)),
            name="attn_grad",
            scratch=[
                pltpu.VMEM((all_rows, width), bf16),
                pltpu.VMEM((all_rows, feats), bf16),
                pltpu.VMEM((all_rows, width), bf16),
                pltpu.VMEM((all_rows, 3 * feats), bf16),
                pltpu.VMEM((2, feats), f32),
            ]
            + [pltpu.VMEM(*shape) for shape in shapes]
            + [DMA((9 + count,))],
        )
        if l > 0:
            attn_parts[l] = scatter_grads(attn_grads[0])
            upstream_chunks = gather_rows(upstream_b)
        row_sums[l] = (sums_one, sums_two)

    sources = [mlp_parts[0]]
    for l in range(1, depth):
        sources += [mlp_parts[l], attn_parts[l]]
    blocks = 3 * depth - 1
    (stacked,) = kernel_call(
        functools.partial(fetch_kernel, len(sources)),
        [((blocks * width_own, hidden), bf16)],
        *[Far(v) for v in sources],
        name="fetch",
        after=(upstream_b,),
        scratch=[DMA((blocks,))],
    )
    own_term, *other_terms = attn_grads
    other_terms = [shift_z(term, d + 1) for d, term in enumerate(other_terms)]
    crossed = swap_x(stacked)
    others = (swap_y(upstream), swap_y(outputs_own))
    part, mine, pair = kernel_call(
        functools.partial(shard_sum_kernel, depth),
        [
            ((width_own, 4 * feats), bf16),
            ((24, width_own), f32),
            ((2 * blocks * width_own, hidden), bf16),
        ],
        Far(own_term),
        stacked,
        crossed,
        *other_terms,
        name="shard_sum",
        after=others,
        scratch=[pltpu.VMEM(own_term.shape, bf16), DMA((3,))],
    )
    if outer > 1:
        part = lax.psum(part, "ctx", axis_index_groups=outer_groups)
    mine, last_pair = kernel_call(
        functools.partial(vector_plane_kernel, depth),
        [((32, width_own), f32), ((2 * width_own, 4 * feats), bf16)],
        mine,
        swap_xy(mine),
        swap_x(mine),
        swap_y(mine),
        part,
        swap_x(part),
        name="vector_plane",
    )
    pieces = [last_pair, swap_core(last_pair), pair, swap_core(pair)]
    grad_gains, grad_shifts, grad_fc1_bias, grad_qv_bias = kernel_call(
        functools.partial(vector_place_kernel, depth, head_dim),
        [
            (norm_gains.shape, f32),
            (shifts.shape, f32),
            (fc1_bias.shape, f32),
            (qv_bias.shape, f32),
        ],
        mine,
        swap_core(mine),
        name="vector_place",
    )
    grad_inputs, outputs = (
        kernel_call(
            place_rows_kernel,
            [saved(inputs.shape, f32)],
            own,
            other,
            name="place_rows",
            scratch=[DMA((2,))],
        )[0]
        for own, other in zip((upstream, outputs_own), others)
    )
    placed = kernel_call(
        functools.partial(place_kernel, depth, hidden, feats),
        [saved(v.shape, f32) for v in (w_qkv, w_out, w_fc1, w_fc2)],
        *pieces,
        name="place",
        limit=24,
        scratch=[
            pltpu.VMEM((depth, GROUP, width_own, hidden), f32),
            pltpu.VMEM((depth, GROUP, hidden, width_own), f32),
            pltpu.VMEM((depth, GROUP, 3, width_own, feats), f32),
            pltpu.VMEM((depth, GROUP, feats, width_own), f32),
            DMA((16 * depth,)),
        ],
    )
    return (
        outputs,
        grad_inputs,
        grad_gains,
        grad_shifts,
        grad_qv_bias,
        grad_fc1_bias,
        *placed,
    )


def solution(mesh):
    rows = P("fsdp", "ctx", None)
    params = (
        P(None, None, "fsdp"),
        P(None, None, "fsdp"),
        P(None, None, "tp", "fsdp"),
        P(None, "tp", "fsdp"),
        P(None, None, "fsdp", "tp"),
        P(None, "tp", "fsdp"),
        P(None, "fsdp", "tp"),
        P(None, "tp", "fsdp"),
    )
    return jax.shard_map(
        per_device,
        mesh=mesh,
        in_specs=(rows, P("fsdp", None), rows) + params,
        out_specs=(rows, rows) + params,
        check_vma=False,
    )
```

```python
import functools
import math

import jax
import jax.numpy as jnp
from jax import lax
from jax.experimental import pallas as pl
from jax.experimental.pallas import tpu as pltpu
from jax.sharding import PartitionSpec as P

NORM_EPSILON = 1e-06
MASK_FILL = -1e30
ROOT_HALF = 0.7071067811865476
INV_ROOT_TAU = 0.3989422804014327
GROUP = 4
ORDER = (0, 5, 4, 1, 2, 7, 6, 3)
CHIPS = 4

bf16 = jnp.bfloat16
f32 = jnp.float32
VMEM = pl.BlockSpec(memory_space=pltpu.VMEM)
SMEM = pl.BlockSpec(memory_space=pltpu.SMEM)
HBM = pl.BlockSpec(memory_space=pltpu.HBM)
DMA = pltpu.SemaphoreType.DMA
TOKEN = ((8, 128), f32)


def dot(a, b):
    return lax.dot_general(a, b, (((1,), (0,)), ((), ())), preferred_element_type=f32)


def dot_nt(a, b):
    return lax.dot_general(a, b, (((1,), (1,)), ((), ())), preferred_element_type=f32)


def dot_tn(a, b):
    return lax.dot_general(a, b, (((0,), (0,)), ((), ())), preferred_element_type=f32)


class Far:
    def __init__(self, value):
        self.value = value


class Scalars:
    def __init__(self, value):
        self.value = value


def saved(shape, dtype):
    return pltpu.HBM(shape, dtype)


def kernel_call(body, outs, *args, name, limit=12, scratch=(), after=(), aliases=None, us=0):
    values, specs = [], []
    for arg in (*args, *after):
        if isinstance(arg, Far):
            values.append(pltpu.with_memory_space_constraint(arg.value, pltpu.HBM))
            specs.append(HBM)
        elif isinstance(arg, Scalars):
            values.append(arg.value)
            specs.append(SMEM)
        else:
            values.append(arg)
            specs.append(VMEM)
    first, last = len(args), len(args) + len(after)

    def run(*refs):
        body(*refs[:first], *refs[last:])

    out_shape, out_specs = [], []
    for out in outs:
        if isinstance(out, tuple):
            out_shape.append(jax.ShapeDtypeStruct(*out))
            out_specs.append(VMEM)
        else:
            out_shape.append(out)
            out_specs.append(HBM)
    return pl.pallas_call(
        run,
        out_shape=out_shape,
        in_specs=specs,
        out_specs=out_specs,
        scratch_shapes=list(scratch),
        input_output_aliases=aliases or {},
        compiler_params=pltpu.CompilerParams(vmem_limit_bytes=limit << 20),
        cost_estimate=pl.CostEstimate(flops=us * 10**9, bytes_accessed=0, transcendentals=0),
        name=name,
    )(*values)


def start_copies(pairs, sems):
    copies = [
        pltpu.make_async_copy(source, target, sems.at[k])
        for k, (source, target) in enumerate(pairs)
    ]
    for copy in copies:
        copy.start()
    return copies


def row_mean(value):
    return jnp.mean(value, axis=-1, keepdims=True)


def normalize(values):
    center = values - row_mean(values)
    inverse = lax.rsqrt(row_mean(center * center) + NORM_EPSILON)
    return center * inverse, inverse


def lanes_of(head, head_dim, width):
    lane = lax.broadcasted_iota(jnp.int32, (1, width), 1)
    return (lane >= head * head_dim) & (lane < (head + 1) * head_dim)


def assemble(chunks, target):
    rows = chunks[0].shape[0]
    for k, chunk in enumerate(chunks):
        target[k * rows : (k + 1) * rows, :] = chunk[...]


def only(flag, value):
    return jnp.where(flag, value, jnp.zeros_like(value))


def shards(weights):
    if len(weights) == 1:
        rows = weights[0].shape[0]
        return [(pl.ds(0, rows), weights[0])]
    count = len(weights)
    rows = weights[0].shape[0]
    f = lax.axis_index("fsdp")
    found = []
    for d, ref in enumerate(weights):
        place = lax.rem(f + (count - d), count)
        found.append((pl.ds(pl.multiple_of(place * rows, rows), rows), ref))
    return found


def pack_attn_kernel(layer, feats, qkv_hbm, out_hbm, packed_ref, token, qkv, out, sems):
    ci = lax.rem(lax.axis_index("ctx"), GROUP)
    span = pl.ds(pl.multiple_of(ci * feats, feats), feats)
    copies = start_copies(
        [(qkv_hbm.at[layer, :, :, span], qkv), (out_hbm.at[layer, span, :], out)], sems
    )
    copies[0].wait()
    for k in range(3):
        packed_ref[:, k * feats : (k + 1) * feats] = qkv[k]
    copies[1].wait()
    packed_ref[:, 3 * feats :] = out[...].T
    token[...] = jnp.zeros_like(token)


def pack_mlp_kernel(layer, hidden, fc1_hbm, fc2_hbm, packed_ref, token, fc1, fc2, sems):
    ci = lax.rem(lax.axis_index("ctx"), GROUP)
    span = pl.ds(pl.multiple_of(ci * hidden, hidden), hidden)
    copies = start_copies(
        [(fc1_hbm.at[layer, :, span], fc1), (fc2_hbm.at[layer, span, :], fc2)], sems
    )
    copies[0].wait()
    packed_ref[:, :hidden] = fc1[...]
    copies[1].wait()
    packed_ref[:, hidden:] = fc2[...].T
    token[...] = jnp.zeros_like(token)


def prep_upstream_kernel(tp, outer, lengths, cotangent_hbm,
                         upstream_hbm, upstream_b_ref, usable_ref, mask_ref,
                         rows_in, upstream_ref, sems):
    rows = rows_in.shape[0]
    c = lax.axis_index("ctx")
    t = lax.axis_index("tp")
    place = lax.rem(c, GROUP) * tp + t
    start = pl.multiple_of(t * rows, rows)
    copies = start_copies(
        [(cotangent_hbm.at[0, pl.ds(start, rows), :], rows_in)], sems.at[pl.ds(0, 1)]
    )
    lane = lax.broadcasted_iota(jnp.int32, usable_ref.shape, 1)
    limit = jnp.zeros(usable_ref.shape, jnp.int32)
    for o in range(outer):
        for k, d in enumerate(ORDER):
            source = place ^ d
            first_lane = (o * len(ORDER) + k) * rows
            count = lengths[0, o * GROUP + lax.div(source, tp)] - lax.rem(source, tp) * rows
            limit = jnp.where(lane >= first_lane, first_lane + jnp.clip(count, 0, rows), limit)
    usable_ref[...] = jnp.where(lane < limit, 1.0, 0.0)
    row = lax.broadcasted_iota(jnp.int32, mask_ref.shape, 0)
    mask = jnp.where(row + start < lengths[0, c], 1.0, 0.0)
    mask_ref[...] = mask
    copies[0].wait()
    upstream = rows_in[...] * mask[:, 0:1]
    upstream_ref[...] = upstream
    sent = start_copies([(upstream_ref, upstream_hbm)], sems.at[pl.ds(1, 1)])
    upstream_b_ref[...] = upstream.astype(bf16)
    sent[0].wait()


def prep_first_kernel(depth, inputs_hbm, vecs, stream_ref, first_ref, sems):
    rows = stream_ref.shape[0]
    start = pl.multiple_of(lax.axis_index("tp") * rows, rows)
    copies = start_copies([(inputs_hbm.at[0, pl.ds(start, rows), :], stream_ref)], sems)
    copies[0].wait()
    normed, _ = normalize(stream_ref[...])
    shift = vecs[2 * depth : 2 * depth + 1, :]
    first_ref[...] = (normed * vecs[0:1, :] + shift).astype(bf16)


def keep_rows_kernel(*refs):
    chunks, (near_hbm, far_hbm, token, near, far, sems) = refs[:8], refs[8:]
    assemble(chunks[:4], near)
    assemble(chunks[4:], far)
    for copy in start_copies([(near, near_hbm), (far, far_hbm)], sems):
        copy.wait()
    token[...] = jnp.zeros_like(token)


def qkv_kernel(feats, weight_count, *refs):
    c0, c1, c2, c3, *rest = refs
    weights = rest[:weight_count]
    bias, qkv_ref, x = rest[weight_count:]
    assemble((c0, c1, c2, c3), x)
    qkv = sum(dot(x[:, span], w[:, : 3 * feats]) for span, w in shards(weights))
    qkv_ref[:, :feats] = (qkv[:, :feats] + bias[0:1, :]).astype(bf16)
    qkv_ref[:, feats : 2 * feats] = qkv[:, feats : 2 * feats].astype(bf16)
    qkv_ref[:, 2 * feats :] = (qkv[:, 2 * feats :] + bias[1:2, :]).astype(bf16)


def attn_kernel(feats, heads, weight_count, part_count, keep_count, tile, *refs):
    q_ref, *rest = refs
    parts = rest[:part_count]
    weights = rest[part_count : part_count + weight_count]
    rest = rest[part_count + weight_count :]
    usable, *rest = rest
    kept, rest = rest[:keep_count], rest[keep_count:]
    partial_ref, attended_hbm, norm_hbm, *rest = rest
    kept_hbm, rest = rest[:keep_count], rest[keep_count:]
    keys, values, attended_ref, norm_ref, sems = rest
    head_dim = feats // heads
    scale = 1.0 / math.sqrt(head_dim)
    copies = start_copies(list(zip(kept, kept_hbm)), sems)
    first = 0
    for part in parts:
        rows, width = part.shape
        keys[first : first + rows, :] = part[:, width - 2 * feats : width - feats]
        values[first : first + rows, :] = part[:, width - feats :]
        first += rows
    keep = usable[...] > 0.5
    rows = q_ref.shape[0]
    for first in range(0, rows, tile):
        span = slice(first, first + tile)
        q = q_ref[span, :feats]
        attended = None
        for h in range(heads):
            own = lanes_of(h, head_dim, feats)
            scores = dot_nt(only(own, q), keys[...]) * scale
            scores = jnp.where(keep, scores, MASK_FILL)
            highest = jnp.max(scores, axis=-1, keepdims=True)
            raised = jnp.exp(scores - highest)
            total = jnp.sum(raised, axis=-1, keepdims=True)
            soft = (raised * (1.0 / total)).astype(bf16)
            result = dot(soft, values[...])
            log_norm = jnp.broadcast_to(highest + jnp.log(total), (tile, feats))
            if attended is None:
                attended, norms = result, log_norm
            else:
                attended = jnp.where(own, result, attended)
                norms = jnp.where(own, log_norm, norms)
        attended_ref[span, :] = attended.astype(bf16)
        norm_ref[span, :] = norms
    copies += start_copies(
        [(attended_ref, attended_hbm), (norm_ref, norm_hbm)],
        sems.at[pl.ds(keep_count, 2)],
    )
    for span, w in shards(weights):
        partial_ref[:, span] = dot_nt(attended_ref[...], w[:, 3 * feats :]).astype(bf16)
    for copy in copies:
        copy.wait()


def core_sum_kernel(count, *refs):
    pairs, owns = refs[: 2 * count], refs[2 * count : 3 * count]
    peers = refs[3 * count :]
    rows = owns[0].shape[0]
    for j in range(count):
        near, far = pairs[2 * j], pairs[2 * j + 1]
        for k in range(1 + len(peers)):
            span = slice(k * rows, (k + 1) * rows)
            total = near[span, :].astype(f32) + far[span, :].astype(f32)
            if k == 0:
                owns[j][...] = total
            else:
                peers[k - 1][j * rows : (j + 1) * rows, :] = total.astype(bf16)


def total_of(own, xy, x, y, part=0):
    rows = own.shape[0]
    span = slice(part * rows, (part + 1) * rows)
    return (
        own[...] + y[span, :].astype(f32) + x[span, :].astype(f32) + xy[span, :].astype(f32)
    )


def sum_norm_kernel(bias_row, gain_row, shift_row, own, xy, x, y, residual_hbm, vecs,
                    stream_ref, normed_ref, residual, sems):
    copies = start_copies([(residual_hbm, residual)], sems)
    total = total_of(own, xy, x, y) + vecs[bias_row : bias_row + 1, :]
    copies[0].wait()
    stream = residual[...] + total
    stream_ref[...] = stream
    normed, _ = normalize(stream)
    gain = vecs[gain_row : gain_row + 1, :]
    normed_ref[...] = (normed * gain + vecs[shift_row : shift_row + 1, :]).astype(bf16)


def sum_out_kernel(bias_row, own, xy, x, y, residual_hbm, vecs, mask, out_hbm, token,
                   residual, out_ref, sems):
    copies = start_copies([(residual_hbm, residual)], sems.at[pl.ds(0, 1)])
    total = total_of(own, xy, x, y, 1) + vecs[bias_row : bias_row + 1, :]
    copies[0].wait()
    out_ref[...] = (residual[...] + total) * mask[:, 0:1]
    token[...] = jnp.zeros_like(token)
    for copy in start_copies([(out_ref, out_hbm)], sems.at[pl.ds(1, 1)]):
        copy.wait()


def mlp_kernel(hidden, keep_count, saves, c0, c1, c2, c3, w, bias, *refs):
    kept, rest = refs[:keep_count], refs[keep_count:]
    partial_ref, x_out, act_out, slope_out, *rest = rest
    kept_hbm, rest = rest[:keep_count], rest[keep_count:]
    if saves:
        x, act_ref, slope_ref, sems = rest
    else:
        x, act_ref, slope_ref = x_out, act_out, slope_out
        (sems,) = rest
    copies = start_copies(list(zip(kept, kept_hbm)), sems)
    assemble((c0, c1, c2, c3), x)
    if saves:
        copies += start_copies([(x, x_out)], sems.at[pl.ds(keep_count, 1)])
    block = hidden // 2
    for k in range(2):
        span = slice(k * block, (k + 1) * block)
        pre = dot(x[...], w[:, span]) + bias[:, span]
        cdf = 0.5 * (1.0 + lax.erf(pre * ROOT_HALF))
        density = jnp.exp(-0.5 * pre * pre) * INV_ROOT_TAU
        slope_ref[k] = cdf + pre * density
        act_ref[:, span] = (pre * cdf).astype(bf16)
        if saves:
            copies += start_copies(
                [(slope_ref.at[k], slope_out.at[k])], sems.at[pl.ds(1 + keep_count + k, 1)]
            )
    if saves:
        copies += start_copies([(act_ref, act_out)], sems.at[pl.ds(3 + keep_count, 1)])
    partial_ref[...] = dot_nt(act_ref[...], w[:, hidden:]).astype(bf16)
    for copy in copies:
        copy.wait()


def mlp_back_kernel(hidden, chunk_count, *refs):
    chunks, (w, slope, *rest) = refs[:chunk_count], refs[chunk_count:]
    partial_ref, grad_ref, sum_hbm, x, sum_ref, sems = rest
    assemble(chunks, x)
    grad = dot(x[...], w[:, hidden:])
    block = hidden // 2
    for k in range(2):
        span = slice(k * block, (k + 1) * block)
        part = grad[:, span] * slope[k]
        grad_ref[:, span] = part.astype(bf16)
        sum_ref[:, span] = jnp.sum(part, axis=0, keepdims=True)
    sent = start_copies([(sum_ref, sum_hbm)], sems)
    partial_ref[...] = dot_nt(grad_ref[...], w[:, :hidden]).astype(bf16)
    sent[0].wait()


def mlp_grad_kernel(hidden, second_near, second_far, act_near, act_far, up_near, up_far,
                    grad_near, grad_far, passed, sums, middle, out_hbm, passed_ref, sums_hbm,
                    middle_hbm, second, act, up, grad, out_one, out_two, sems):
    rows = up_near.shape[0]
    sent = start_copies([(sums, sums_hbm), (middle, middle_hbm)], sems.at[pl.ds(6, 2)])
    near, far = pl.ds(0, rows), pl.ds(rows, rows)
    copies = start_copies(
        [
            (act_near, act.at[near]),
            (act_far, act.at[far]),
            (second_near, second.at[near]),
            (second_far, second.at[far]),
        ],
        sems,
    )
    passed_ref[...] = passed[...]
    up[:rows, :] = up_near[...]
    up[rows:, :] = up_far[...]
    grad[:rows, :] = grad_near[...]
    grad[rows:, :] = grad_far[...]
    for copy in copies[:2]:
        copy.wait()
    out_two[...] = dot_tn(up[...], act[...]).astype(bf16)
    sent += start_copies(
        [(out_two, out_hbm.at[:, pl.ds(hidden, hidden)])], sems.at[pl.ds(4, 1)]
    )
    for copy in copies[2:]:
        copy.wait()
    out_one[...] = dot_tn(second[...], grad[...]).astype(bf16)
    sent += start_copies([(out_one, out_hbm.at[:, pl.ds(0, hidden)])], sems.at[pl.ds(5, 1)])
    for copy in sent:
        copy.wait()


def norm_back(upstream, values, gain):
    normed, inverse = normalize(values)
    scaled = upstream * gain
    back = inverse * (scaled - row_mean(scaled) - normed * row_mean(scaled * normed))
    gain_grad = jnp.sum(upstream * normed, axis=0, keepdims=True)
    return back, gain_grad, jnp.sum(upstream, axis=0, keepdims=True)


def norm_back_two_kernel(gain_row, own, xy, x, y, values_hbm, upstream_hbm, vecs,
                         grad_ref, grad_b_ref, sums_ref, values, upstream, sems):
    copies = start_copies([(values_hbm, values), (upstream_hbm, upstream)], sems)
    total = total_of(own, xy, x, y)
    for copy in copies:
        copy.wait()
    up = upstream[...]
    back, gain_grad, shift_grad = norm_back(
        total, values[...], vecs[gain_row : gain_row + 1, :]
    )
    grad = up + back
    grad_ref[...] = grad
    grad_b_ref[...] = grad.astype(bf16)
    sums_ref[0:1, :] = gain_grad
    sums_ref[1:2, :] = shift_grad
    sums_ref[2:3, :] = jnp.sum(grad, axis=0, keepdims=True)
    sums_ref[3:4, :] = jnp.sum(up, axis=0, keepdims=True)


def norm_back_one_kernel(gain_row, own, xy, x, y, values_hbm, upstream_hbm, vecs, mask,
                         grad_ref, grad_b_ref, sums_ref, values, upstream, sems):
    copies = start_copies([(values_hbm, values), (upstream_hbm, upstream)], sems)
    total = total_of(own, xy, x, y)
    for copy in copies:
        copy.wait()
    back, gain_grad, shift_grad = norm_back(
        total, values[...], vecs[gain_row : gain_row + 1, :]
    )
    grad = upstream[...] + back
    if mask is not None:
        grad = grad * mask[:, 0:1]
    grad_ref[...] = grad
    grad_b_ref[...] = grad.astype(bf16)
    sums_ref[0:1, :] = gain_grad
    sums_ref[1:2, :] = shift_grad


def attn_back_kernel(feats, heads, weight_count, part_count, tile, carried, *refs):
    c0, c1, c2, c3, *rest = refs
    weights, rest = rest[:weight_count], rest[weight_count:]
    usable, qkv, attended, norms, *rest = rest
    parts, rest = rest[:part_count], rest[part_count:]
    if carried:
        keys_before, values_before, *rest = rest
    x, grad_q, grad_k, grad_v, pairs, grad_att = rest
    head_dim = feats // heads
    scale = 1.0 / math.sqrt(head_dim)
    first = 0
    for part in parts:
        rows, width = part.shape
        pairs[first : first + rows, :] = part[:, width - 2 * feats :]
        first += rows
    assemble((c0, c1, c2, c3), x)
    grad_att[...] = sum(
        dot(x[:, span], w[:, 3 * feats :]) for span, w in shards(weights)
    ).astype(bf16)
    keep = usable[...] > 0.5
    rows = qkv.shape[0]
    if carried:
        sum_k, sum_v = keys_before[...], values_before[...]
    else:
        sum_k = jnp.zeros(grad_k.shape, f32)
        sum_v = jnp.zeros(grad_v.shape, f32)
    keys, values = pairs[:, :feats], pairs[:, feats:]
    for first in range(0, rows, tile):
        span = slice(first, first + tile)
        q = qkv[span, :feats]
        ga = grad_att[span, :]
        products = ga.astype(f32) * attended[span, :].astype(f32)
        gq = None
        for h in range(heads):
            own = lanes_of(h, head_dim, feats)
            q_h = only(own, q)
            ga_h = only(own, ga)
            row_dots = jnp.sum(only(own, products), axis=-1, keepdims=True)
            scores = dot_nt(q_h, keys) * scale
            scores = jnp.where(keep, scores, MASK_FILL)
            soft = jnp.exp(scores - norms[span, h * head_dim : h * head_dim + 1])
            grad_soft = dot_nt(ga_h, values)
            grad_scores = (soft * (grad_soft - row_dots)).astype(bf16)
            part = dot(grad_scores, keys)
            gq = part if gq is None else jnp.where(own, part, gq)
            sum_k = sum_k + dot_tn(grad_scores, q_h) * scale
            sum_v = sum_v + dot_tn(soft.astype(bf16), ga_h)
        grad_q[span, :] = gq * scale
    grad_k[...] = sum_k
    grad_v[...] = sum_v


def project_kernel(feats, first, weight_count, gq, gk, gv, *refs):
    weights, (partial_ref, packed) = refs[:weight_count], refs[weight_count:]
    rows = gq.shape[0]
    span = slice(first, first + rows)
    packed[:, :feats] = gq[...].astype(bf16)
    packed[:, feats : 2 * feats] = gk[span, :].astype(bf16)
    packed[:, 2 * feats :] = gv[span, :].astype(bf16)
    for columns, w in shards(weights):
        partial_ref[:, columns] = dot_nt(packed[...], w[:, : 3 * feats]).astype(bf16)


def attn_grad_kernel(feats, count, first_near, first_far, att_near, att_far, up_near, up_far,
                     gq_near, gq_far, gk, gv, passed, sums, stream, lines, *refs):
    outs, rest = refs[:count], refs[count:]
    heads_hbm, passed_ref, sums_hbm, stream_hbm, *rest = rest
    first, att, up, packed, sums_ref, *staged, sems = rest
    rows = up_near.shape[0]
    sent = start_copies([(sums, sums_hbm), (stream, stream_hbm)], sems.at[pl.ds(6, 2)])
    near, far = pl.ds(0, rows), pl.ds(rows, rows)
    copies = start_copies(
        [
            (att_near, att.at[near]),
            (att_far, att.at[far]),
            (first_near, first.at[near]),
            (first_far, first.at[far]),
        ],
        sems,
    )
    passed_ref[...] = passed[...]
    up[:rows, :] = up_near[...]
    up[rows:, :] = up_far[...]
    packed[:rows, :feats] = gq_near[...].astype(bf16)
    packed[rows:, :feats] = gq_far[...].astype(bf16)
    packed[:, feats : 2 * feats] = gk[...].astype(bf16)
    packed[:, 2 * feats :] = gv[...].astype(bf16)
    sums_ref[0:1, :] = jnp.sum(gq_near[...], axis=0, keepdims=True) + jnp.sum(
        gq_far[...], axis=0, keepdims=True
    )
    sums_ref[1:2, :] = jnp.sum(gv[...], axis=0, keepdims=True)
    sent += start_copies([(sums_ref, heads_hbm)], sems.at[pl.ds(8, 1)])
    if count == 1:
        out_one, out_two = staged
        for copy in copies[:2]:
            copy.wait()
        out_two[...] = dot_tn(up[...], att[...]).astype(bf16)
        sent += start_copies(
            [(out_two, outs[0].at[:, pl.ds(3 * feats, feats)])], sems.at[pl.ds(4, 1)]
        )
        for copy in copies[2:]:
            copy.wait()
        out_one[...] = dot_tn(first[...], packed[...]).astype(bf16)
        sent += start_copies(
            [(out_one, outs[0].at[:, pl.ds(0, 3 * feats)])], sems.at[pl.ds(5, 1)]
        )
        for copy in sent:
            copy.wait()
        return
    (stage,) = staged
    for copy in copies:
        copy.wait()
    below = lines.shape[1]
    width_own = outs[0].shape[0] - below
    for d in reversed(range(count)):
        place = lax.rem(lax.axis_index("fsdp") + d, count)
        span = pl.ds(pl.multiple_of(place * width_own, width_own), width_own)
        stage[d, :width_own, : 3 * feats] = dot_tn(first[:, span], packed[...]).astype(bf16)
        stage[d, :width_own, 3 * feats :] = dot_tn(up[:, span], att[...]).astype(bf16)
        stage[d, width_own:, :] = lines[d]
        sent += start_copies([(stage.at[d], outs[d])], sems.at[pl.ds(9 + d, 1)])
    for copy in sent:
        copy.wait()


def settle_kernel(passed, *refs):
    passed_ref = refs[-1]
    passed_ref[...] = passed[...]


def fetch_kernel(count, *refs):
    sources, (target, sems) = refs[:count], refs[count:]
    columns = target.shape[1]
    moves = []
    row = 0
    for source in sources:
        rows = source.shape[0]
        for first in range(0, source.shape[1], columns):
            moves.append(
                (source.at[:, pl.ds(first, columns)], target.at[pl.ds(row, rows), :])
            )
            row += rows
    for copy in start_copies(moves, sems):
        copy.wait()


def shard_sum_kernel(depth, own_hbm, stacked, crossed, *refs):
    *others, part_ref, mine_ref, pair_ref, own, sems = refs
    count = stacked.shape[0]
    first, *copies = start_copies(
        [
            (own_hbm, own),
            (stacked, pair_ref.at[pl.ds(0, count), :]),
            (crossed, pair_ref.at[pl.ds(count, count), :]),
        ],
        sems,
    )
    first.wait()
    rows, width = part_ref.shape[0], mine_ref.shape[1]
    terms = [ref[...].astype(f32) for ref in (own, *others)]
    total = terms[0]
    for term in terms[1:]:
        total = total + term
    part_ref[...] = total[:rows, :].astype(bf16)
    lines = total[rows:, :width] + total[rows:, width:]
    mine_ref[: 6 * depth, :] = lines[: 6 * depth, :]
    for k in range(mine_ref.shape[0] - 16):
        mine_ref[16 + k : 17 + k, :] = lines[6 * depth + k : 6 * depth + k + 1, :]
    for copy in copies:
        copy.wait()


def place_kernel(depth, hidden, feats, *refs):
    alone, pairs, rest = refs[:2], refs[2:4], refs[4:]

    def half_of(pair, k):
        count = pair[k % 2].shape[0] // 2
        return pair[k % 2].at[pl.ds(k // 2 * count, count), :]

    slices = [(half_of(alone, k), half_of(pairs, k)) for k in range(GROUP)]
    qkv_hbm, out_hbm, fc1_hbm, fc2_hbm, fc1, fc2, qkv, out, sems = rest
    ci = lax.rem(lax.axis_index("ctx"), GROUP)
    rows = fc1.shape[2]
    copies = []

    def send(source, target):
        copies.extend(start_copies([(source, target)], sems.at[pl.ds(len(copies), 1)]))

    for l in range(depth):
        for k in range(GROUP):
            _, stacked = slices[k]
            first = 0 if l == 0 else (3 * l - 1) * rows
            span = pl.ds(pl.multiple_of((ci ^ k) * hidden, hidden), hidden)
            fc1[l, k] = stacked[first : first + rows, :].astype(f32)
            send(fc1.at[l, k], fc1_hbm.at[l, :, span])
            fc2[l, k] = stacked[first + rows : first + 2 * rows, :].T.astype(f32)
            send(fc2.at[l, k], fc2_hbm.at[l, span, :])
    for l in reversed(range(depth)):
        for k in range(GROUP):
            last, stacked = slices[k]
            piece = last if l == 0 else stacked.at[pl.ds((3 * l + 1) * rows, rows), :]
            span = pl.ds(pl.multiple_of((ci ^ k) * feats, feats), feats)
            for j in range(3):
                qkv[l, k, j] = piece[:, j * feats : (j + 1) * feats].astype(f32)
            send(qkv.at[l, k], qkv_hbm.at[l, :, :, span])
            out[l, k] = piece[:, 3 * feats :].T.astype(f32)
            send(out.at[l, k], out_hbm.at[l, span, :])
    for copy in copies:
        copy.wait()


def vector_pack_kernel(depth, one_now, gq_near, gq_far, gv, *refs):
    count = 5 * depth - 2
    out_ref, *found, sems = refs[count:]
    copies = start_copies(list(zip(refs[:count], found)), sems)
    out_ref[...] = jnp.zeros_like(out_ref)
    feats = gv.shape[1]
    head_now = [
        jnp.sum(gq_near[...], axis=0, keepdims=True) + jnp.sum(gq_far[...], axis=0, keepdims=True),
        jnp.sum(gv[...], axis=0, keepdims=True),
    ]
    for copy in copies:
        copy.wait()
    for l in range(depth):
        if l == 0:
            one, (two, unit_near, unit_far) = one_now, found[:3]
            heads = head_now
        else:
            one, two, unit_near, unit_far, head = found[5 * l - 2 : 5 * l + 3]
            heads = [head[0:1, :], head[1:2, :]]
        out_ref[6 * l : 6 * l + 1, :] = one[0:1, :]
        out_ref[6 * l + 1 : 6 * l + 2, :] = two[0:1, :]
        out_ref[6 * l + 2 : 6 * l + 3, :] = one[1:2, :]
        out_ref[6 * l + 3 : 6 * l + 6, :] = two[1:4, :]
        units = unit_near.shape[1]
        row = 6 * depth
        out_ref[row : row + 1, l * units : (l + 1) * units] = unit_near[...] + unit_far[...]
        for j in range(2):
            start = (2 * l + j) * feats
            out_ref[row + 1 : row + 2, start : start + feats] = heads[j]


def vector_lines_kernel(depth, width_own, packed, lines_ref):
    count = lines_ref.shape[0]
    f = lax.axis_index("fsdp")
    total = packed[...]
    high = total.astype(bf16).astype(f32)
    low = total - high
    lines_ref[...] = jnp.zeros_like(lines_ref)
    last = 6 * depth
    for k, value in enumerate((high, low)):
        lanes = slice(k * width_own, (k + 1) * width_own)
        columns = [value[:, a * width_own : (a + 1) * width_own] for a in range(count)]
        for d in range(count):
            mine = columns[0]
            for a in range(1, count):
                mine = jnp.where(lax.rem(f + d, count) == a, columns[a], mine)
            rows = [mine[:last, :]]
            for r in range(2):
                for a in range(count):
                    rows.append(columns[a][last + r : last + r + 1, :])
            rows.append(jnp.zeros((lines_ref.shape[1] - last - 2 * count, width_own), f32))
            lines_ref[d, :, lanes] = jnp.concatenate(rows, axis=0).astype(bf16)


def vector_plane_kernel(depth, own, xy, x, y, part, part_x, out_ref, pair_ref):
    last = 6 * depth
    rows = part.shape[0]
    pair_ref[:rows, :] = part[...]
    pair_ref[rows:, :] = part_x[...]
    out_ref[:last, :] = own[:last, :] + xy[:last, :] + x[:last, :] + y[:last, :]
    out_ref[16:24, :] = own[16:24, :]
    out_ref[24:32, :] = x[16:24, :]


def vector_place_kernel(depth, head_dim, own, far, gains_ref, shifts_ref, unit_ref, heads_ref):
    total = own[: 6 * depth, :] + far[: 6 * depth, :]
    for l in range(depth):
        gains_ref[l] = total[6 * l : 6 * l + 2, :]
        shifts_ref[l] = total[6 * l + 2 : 6 * l + 6, :]
    pieces = (own[16:24, :], far[16:24, :], own[24:32, :], far[24:32, :])
    ci = lax.rem(lax.axis_index("ctx"), GROUP)
    f = lax.axis_index("fsdp")

    def of_place(c):
        k = ci ^ c
        found = pieces[0]
        for j in range(1, GROUP):
            found = jnp.where(k == j, pieces[j], found)
        return found

    width_own = own.shape[1]
    units = of_place(f)
    parts = unit_ref.shape[2] // width_own
    for l in range(depth):
        for j in range(parts):
            row = l * parts + j
            unit_ref[l, :, j * width_own : (j + 1) * width_own] = units[row : row + 1, :]
    head_own = heads_ref.shape[3]
    heads = heads_ref.shape[2] // GROUP
    for c in range(GROUP):
        found = of_place(c)
        for l in range(depth):
            for j in range(2):
                for h in range(heads):
                    first = ((2 * l + j) * heads + h) * head_dim
                    row, lane = 4 + first // width_own, first % width_own
                    value = found[row : row + 1, lane : lane + head_own]
                    for a in range(1, head_dim // head_own):
                        start = lane + a * head_own
                        value = jnp.where(
                            f == a, found[row : row + 1, start : start + head_own], value
                        )
                    heads_ref[l, j, c * heads + h : c * heads + h + 1, :] = value


def place_rows_kernel(own, other, out_hbm, sems):
    rows = own.shape[0]
    start = pl.multiple_of(lax.axis_index("tp") * rows, rows)
    copies = start_copies(
        [
            (own, out_hbm.at[0, pl.ds(start, rows), :]),
            (other, out_hbm.at[0, pl.ds(pl.multiple_of(rows - start, rows), rows), :]),
        ],
        sems,
    )
    for copy in copies:
        copy.wait()


def per_device(
    inputs, lengths, cotangent, norm_gains, shifts, qv_bias, fc1_bias, w_qkv, w_out, w_fc1, w_fc2
):
    depth = w_qkv.shape[0]
    width_own = w_qkv.shape[2]
    fsdp = lax.axis_size("fsdp")
    tp = lax.axis_size("tp")
    ctx = lax.axis_size("ctx")
    outer = ctx // GROUP
    rows = inputs.shape[1] // tp
    half = rows * CHIPS
    all_rows = 2 * half
    head_own = qv_bias.shape[3]
    head_dim = head_own * fsdp
    heads = qv_bias.shape[2] // GROUP
    feats = heads * head_dim
    hidden = w_fc1.shape[2] // GROUP
    width = width_own * fsdp
    t = lax.axis_index("tp")
    f = lax.axis_index("fsdp")
    ci = lax.axis_index("ctx") % GROUP
    tile = half // 2
    attn_limit = 12 if outer == 1 else 48

    def swap_core(value):
        return lax.ppermute(value, "ctx", [(i, i ^ 1) for i in range(ctx)])

    def swap_x(value):
        return lax.ppermute(value, "ctx", [(i, i ^ 2) for i in range(ctx)])

    def swap_y(value):
        return lax.ppermute(value, "tp", [(i, i ^ 1) for i in range(tp)])

    def swap_xy(value):
        pairs = [
            (i * tp + k, (i ^ 2) * tp + (k ^ 1)) for i in range(ctx) for k in range(tp)
        ]
        return lax.ppermute(value, ("ctx", "tp"), pairs)

    def shift_z(value, d):
        return lax.ppermute(value, "fsdp", [(i, (i + d) % fsdp) for i in range(fsdp)])

    outer_groups = [[o * GROUP + i for o in range(outer)] for i in range(GROUP)]

    def gather_rows(own):
        near = (own, swap_xy(own), swap_x(own), swap_y(own))
        return near, tuple(swap_core(chunk) for chunk in near)

    def settle(value, *after):
        return kernel_call(
            settle_kernel, [(value.shape, value.dtype)], value, name="settle", after=after
        )[0]

    def reduce_rows(*pairs, after=()):
        count = len(pairs)
        *owns, xy, x, y = kernel_call(
            functools.partial(core_sum_kernel, count),
            [((rows, width), f32)] * count + [((count * rows, width), bf16)] * 3,
            *[v for near, far in pairs for v in (near, swap_core(far))],
            name="core_sum",
            after=after,
        )
        peers = (swap_xy(xy), swap_x(x), swap_y(y))
        return [(own, *peers) for own in owns]

    def pack_attn(l, after):
        return kernel_call(
            functools.partial(pack_attn_kernel, l, feats),
            [((width_own, 4 * feats), bf16), TOKEN],
            Far(w_qkv),
            Far(w_out),
            name="pack_attn",
            after=after,
            scratch=[
                pltpu.VMEM((3, width_own, feats), bf16),
                pltpu.VMEM((feats, width_own), bf16),
                DMA((2,)),
            ],
        )

    def pack_mlp(l, after):
        return kernel_call(
            functools.partial(pack_mlp_kernel, l, hidden),
            [((width_own, 2 * hidden), bf16), TOKEN],
            Far(w_fc1),
            Far(w_fc2),
            name="pack_mlp",
            after=after,
            scratch=[
                pltpu.VMEM((width_own, hidden), bf16),
                pltpu.VMEM((hidden, width_own), bf16),
                DMA((2,)),
            ],
        )

    attn_w = []
    mlp_w = []
    token = None
    for l in range(depth):
        own, token = pack_attn(l, () if token is None else (token,))
        attn_w.append((lax.all_gather(own, "fsdp", axis=0, tiled=True),))
        own, token = pack_mlp(l, (token,))
        mlp_w.append(lax.all_gather(own, "fsdp", axis=0, tiled=True))
        if l == 0:
            pack_token = token

    qv_own = lax.dynamic_slice_in_dim(qv_bias, ci * heads, heads, axis=2)
    vec_rows = depth * 6
    c1_rows = depth * fc1_bias.shape[2] // width_own
    qv_own = qv_own.reshape(1, -1)
    small_own = jnp.concatenate(
        [
            norm_gains.reshape(-1, width_own),
            shifts.reshape(-1, width_own),
            fc1_bias.reshape(-1, width_own),
            jnp.pad(qv_own, ((0, 0), (0, width_own - qv_own.shape[1]))),
        ],
        axis=0,
    )
    shifted = [small_own] + [shift_z(small_own, d) for d in range(1, fsdp)]

    def shard(a):
        picked = shifted[0]
        for d in range(1, fsdp):
            picked = jnp.where((f - d) % fsdp == a, shifted[d], picked)
        return picked.astype(f32)

    small = [shard(a) for a in range(fsdp)]
    vecs = jnp.concatenate([s[:vec_rows] for s in small], axis=1)
    fc1_all = shard(ci)[vec_rows : vec_rows + c1_rows].reshape(depth, 1, hidden)
    qv_all = jnp.stack(
        [s[vec_rows + c1_rows, : qv_own.shape[1]].reshape(depth, 2, heads, head_own) for s in small],
        axis=3,
    ).reshape(depth, 2, feats)

    def gain_row(l, i):
        return 2 * l + i

    def shift_row(l, i):
        return 2 * depth + 4 * l + i

    key_rows = outer * all_rows
    row_f32 = ((rows, width), f32)
    row_bf16 = ((rows, width), bf16)
    upstream, upstream_b, usable, mask = kernel_call(
        functools.partial(prep_upstream_kernel, tp, outer),
        [saved((rows, width), f32), row_bf16, ((1, key_rows), f32), ((rows, 128), f32)],
        Scalars(lengths),
        Far(cotangent),
        name="prep_upstream",
        after=(pack_token,),
        scratch=[pltpu.VMEM((rows, width), f32), pltpu.VMEM((rows, width), f32), DMA((2,))],
    )
    near, far = gather_rows(upstream_b)
    half_x = pltpu.VMEM((half, width), bf16)
    *upstream_rows, upstream_token = kernel_call(
        keep_rows_kernel,
        [saved((half, width), bf16)] * 2 + [TOKEN],
        *near,
        *far,
        name="keep_rows",
        scratch=[half_x, half_x, DMA((2,))],
    )
    upstream_chunks = [(x,) for x in upstream_rows]
    stream, first = kernel_call(
        functools.partial(prep_first_kernel, depth),
        [row_f32, row_bf16],
        Far(inputs),
        vecs,
        name="prep_first",
        scratch=[DMA((1,))],
    )
    first_chunks = gather_rows(first)

    partial_out = ((half, width), bf16)
    saved_all = []
    for l in range(depth):
        qkv = []
        first_x = []
        for side in (0, 1):
            qkv_half, x_half = kernel_call(
                functools.partial(qkv_kernel, feats, len(attn_w[l])),
                [((half, 3 * feats), bf16), ((half, width), bf16)],
                *first_chunks[side],
                *attn_w[l],
                qv_all[l],
                name="qkv",
                after=(upstream_token,) if l == 0 and side == 0 else (),
            )
            qkv.append(qkv_half)
            first_x.append(x_half)
        if outer > 1:
            pairs = jnp.concatenate([part[:, feats:] for part in qkv], axis=0)
            pairs = lax.all_gather(
                pairs, "ctx", axis=0, tiled=True, axis_index_groups=outer_groups
            )
            key_parts = (pairs,)
        else:
            key_parts = tuple(qkv)
        attn = [None, None]
        for side in (1, 0):
            kept = (first_x[side], qkv[side]) + ((stream,) if side == 1 else ())
            attn[side] = kernel_call(
                functools.partial(
                    attn_kernel, feats, heads, len(attn_w[l]), len(key_parts), len(kept), tile
                ),
                [partial_out, saved((half, feats), bf16), saved((half, feats), f32)]
                + [saved(k.shape, k.dtype) for k in kept],
                qkv[side],
                *key_parts,
                *attn_w[l],
                usable,
                *kept,
                name="attn",
                limit=attn_limit,
                scratch=[
                    pltpu.VMEM((key_rows, feats), bf16),
                    pltpu.VMEM((key_rows, feats), bf16),
                    pltpu.VMEM((half, feats), bf16),
                    pltpu.VMEM((half, feats), f32),
                    DMA((len(kept) + 2,)),
                ],
            )
        (sums,) = reduce_rows((attn[0][0], attn[1][0]))
        middle, second = kernel_call(
            functools.partial(sum_norm_kernel, shift_row(l, 2), gain_row(l, 1), shift_row(l, 1)),
            [row_f32, row_bf16],
            *sums,
            Far(attn[1][5]),
            vecs,
            name="sum_norm",
            scratch=[pltpu.VMEM((rows, width), f32), DMA((1,))],
        )
        second_chunks = gather_rows(second)
        mlp = [None, None]
        for side in (1, 0):
            kept = (middle,) if side == 1 else ()
            saves = l + 1 < depth
            shapes = [
                ((half, width), bf16),
                ((half, hidden), bf16),
                ((2, half, hidden // 2), f32),
            ]
            mlp[side] = kernel_call(
                functools.partial(mlp_kernel, hidden, len(kept), saves),
                [partial_out]
                + [saved(*shape) if saves else shape for shape in shapes]
                + [saved(k.shape, k.dtype) for k in kept],
                *second_chunks[side],
                mlp_w[l],
                fc1_all[l],
                *kept,
                name="mlp",
                scratch=[pltpu.VMEM(*shape) for shape in shapes if saves]
                + [DMA((4 + len(kept),))],
            )
        saved_all.append((attn, pairs if outer > 1 else None, mlp))
        if l + 1 < depth:
            (sums,) = reduce_rows((mlp[0][0], mlp[1][0]))
            stream, first = kernel_call(
                functools.partial(
                    sum_norm_kernel, shift_row(l, 3), gain_row(l + 1, 0), shift_row(l + 1, 0)
                ),
                [row_f32, row_bf16],
                *sums,
                Far(mlp[1][4]),
                vecs,
                name="sum_norm",
                scratch=[pltpu.VMEM((rows, width), f32), DMA((1,))],
            )
            first_chunks = gather_rows(first)

    def scatter_grads(grad):
        part = lax.psum_scatter(grad, "fsdp", scatter_dimension=0, tiled=True)
        if outer > 1:
            part = lax.psum(part, "ctx", axis_index_groups=outer_groups)
        return part

    row_sums = [None] * depth
    unit_sums = [None] * depth
    head_sums = [None] * depth
    mlp_parts = [None] * depth
    attn_parts = [None] * depth
    for l in reversed(range(depth)):
        attn, pairs, mlp = saved_all[l]
        back = [None, None]
        for side in (1, 0):
            back[side] = kernel_call(
                functools.partial(mlp_back_kernel, hidden, len(upstream_chunks[side])),
                [
                    partial_out,
                    ((half, hidden), bf16),
                    saved((1, hidden), f32),
                    ((half, width), bf16),
                ],
                *upstream_chunks[side],
                mlp_w[l],
                mlp[side][3],
                name="mlp_back",
                scratch=[pltpu.VMEM((1, hidden), f32), DMA((1,))],
            )
        pairs_now = [(back[0][0], back[1][0])]
        if l + 1 == depth:
            pairs_now.append((mlp[0][0], mlp[1][0]))
        sums, *output_sums = reduce_rows(*pairs_now)
        if l + 1 == depth:
            outputs_own, output_token = kernel_call(
                functools.partial(sum_out_kernel, shift_row(l, 3)),
                [saved((rows, width), f32), TOKEN],
                *output_sums[0],
                Far(mlp[1][4]),
                vecs,
                mask,
                name="sum_out",
                scratch=[pltpu.VMEM((rows, width), f32)] * 2 + [DMA((2,))],
            )
            after = (output_token,)
        else:
            after = ()
        unit_sums[l] = (back[0][2], back[1][2])
        grad_middle, middle_b, sums_two = kernel_call(
            functools.partial(norm_back_two_kernel, gain_row(l, 1)),
            [row_f32, row_bf16, ((4, width), f32)],
            *sums,
            Far(mlp[1][4]),
            Far(upstream),
            vecs,
            name="norm_back_two",
            scratch=[pltpu.VMEM((rows, width), f32)] * 2 + [DMA((2,))],
        )
        mlp_grad, middle_b, sums_two, grad_middle = kernel_call(
            functools.partial(mlp_grad_kernel, hidden),
            [
                saved((width, 2 * hidden), bf16),
                row_bf16,
                saved((4, width), f32),
                saved((rows, width), f32),
            ],
            mlp[0][1],
            mlp[1][1],
            mlp[0][2],
            mlp[1][2],
            back[0][3],
            back[1][3],
            back[0][1],
            back[1][1],
            middle_b,
            sums_two,
            grad_middle,
            name="mlp_grad",
            after=after,
            scratch=[
                pltpu.VMEM((all_rows, width), bf16),
                pltpu.VMEM((all_rows, hidden), bf16),
                pltpu.VMEM((all_rows, width), bf16),
                pltpu.VMEM((all_rows, hidden), bf16),
                pltpu.VMEM((width, hidden), bf16),
                pltpu.VMEM((width, hidden), bf16),
                DMA((8,)),
            ],
            limit=16,
        )
        mlp_parts[l] = scatter_grads(mlp_grad)
        if l + 1 < depth:
            middle_b = settle(middle_b, Far(mlp_parts[l + 1]))
        middle_chunks = gather_rows(middle_b)
        grad_q = [None, None]
        middle_x = [None, None]
        carried = ()
        for side in (0, 1):
            key_parts = (pairs,) if outer > 1 else (attn[0][4], attn[1][4])
            middle_x[side], grad_q[side], *carried = kernel_call(
                functools.partial(
                    attn_back_kernel,
                    feats,
                    heads,
                    len(attn_w[l]),
                    len(key_parts),
                    tile,
                    len(carried) > 0,
                ),
                [
                    ((half, width), bf16),
                    ((half, feats), f32),
                    ((key_rows, feats), f32),
                    ((key_rows, feats), f32),
                ],
                *middle_chunks[side],
                *attn_w[l],
                usable,
                attn[side][4],
                attn[side][1],
                attn[side][2],
                *key_parts,
                *carried,
                name="attn_back",
                scratch=[
                    pltpu.VMEM((key_rows, 2 * feats), bf16),
                    pltpu.VMEM((half, feats), bf16),
                ],
                limit=attn_limit,
            )
        grad_k, grad_v = carried
        if outer > 1:
            grad_k, grad_v = (
                lax.psum_scatter(
                    v, "ctx", scatter_dimension=0, tiled=True, axis_index_groups=outer_groups
                )
                for v in (grad_k, grad_v)
            )

        def project(side, after):
            return kernel_call(
                functools.partial(project_kernel, feats, side * half, len(attn_w[l])),
                [partial_out],
                grad_q[side],
                grad_k,
                grad_v,
                *attn_w[l],
                name="project",
                after=after,
                scratch=[pltpu.VMEM((half, 3 * feats), bf16)],
            )[0]

        far_part = project(1, ())
        near_part = project(0, ())
        (sums,) = reduce_rows((near_part, far_part))
        body = functools.partial(norm_back_one_kernel, gain_row(l, 0))
        if l > 0:
            masked = ()
            body = lambda *refs, body=body: body(*refs[:7], None, *refs[7:])
        else:
            masked = (mask,)
        upstream, upstream_b, sums_one = kernel_call(
            body,
            [row_f32, row_bf16, ((2, width), f32)],
            *sums,
            Far(attn[1][5]),
            Far(grad_middle),
            vecs,
            *masked,
            name="norm_back_one",
            scratch=[pltpu.VMEM((rows, width), f32)] * 2 + [DMA((2,))],
        )
        lines = ()
        if l == 0:
            terms = [sums_two, *unit_sums[0]]
            for k in range(1, depth):
                terms += [*row_sums[k], *unit_sums[k], head_sums[k]]
            packed = kernel_call(
                functools.partial(vector_pack_kernel, depth),
                [((6 * depth + 2, width), f32)],
                sums_one,
                *grad_q,
                grad_v,
                *[Far(v) for v in terms],
                name="vector_pack",
                scratch=[pltpu.VMEM(v.shape, f32) for v in terms] + [DMA((len(terms),))],
            )[0]
            if outer > 1:
                packed = lax.psum(packed, "ctx", axis_index_groups=outer_groups)
            lines = kernel_call(
                functools.partial(vector_lines_kernel, depth, width_own),
                [((fsdp, 32, 2 * width_own), bf16)],
                packed,
                name="vector_lines",
            )
        count = 1 if l > 0 else fsdp
        shapes = [((width, 3 * feats), bf16), ((width, feats), bf16)]
        if l == 0:
            shapes = [((fsdp, width_own + 32, 4 * feats), bf16)]
        *attn_grads, head_sums[l], upstream_b, sums_one, upstream = kernel_call(
            functools.partial(attn_grad_kernel, feats, count),
            [saved((width if l > 0 else width_own + 32, 4 * feats), bf16)] * count
            + [
                saved((2, feats), f32),
                row_bf16,
                saved((2, width), f32),
                saved((rows, width), f32),
            ],
            Far(attn[0][3]),
            Far(attn[1][3]),
            Far(attn[0][1]),
            Far(attn[1][1]),
            *middle_x,
            *grad_q,
            grad_k,
            grad_v,
            upstream_b,
            sums_one,
            upstream,
            *(lines or (sums_one,)),
            name="attn_grad",
            scratch=[
                pltpu.VMEM((all_rows, width), bf16),
                pltpu.VMEM((all_rows, feats), bf16),
                pltpu.VMEM((all_rows, width), bf16),
                pltpu.VMEM((all_rows, 3 * feats), bf16),
                pltpu.VMEM((2, feats), f32),
            ]
            + [pltpu.VMEM(*shape) for shape in shapes]
            + [DMA((9 + count,))],
        )
        if l > 0:
            attn_parts[l] = scatter_grads(attn_grads[0])
            upstream_chunks = gather_rows(upstream_b)
        row_sums[l] = (sums_one, sums_two)

    sources = [mlp_parts[0]]
    for l in range(1, depth):
        sources += [mlp_parts[l], attn_parts[l]]
    blocks = 3 * depth - 1
    (stacked,) = kernel_call(
        functools.partial(fetch_kernel, len(sources)),
        [((blocks * width_own, hidden), bf16)],
        *[Far(v) for v in sources],
        name="fetch",
        after=(upstream_b,),
        scratch=[DMA((blocks,))],
    )
    own_term, *other_terms = attn_grads
    other_terms = [shift_z(term, d + 1) for d, term in enumerate(other_terms)]
    crossed = swap_x(stacked)
    others = (swap_y(upstream), swap_y(outputs_own))
    part, mine, pair = kernel_call(
        functools.partial(shard_sum_kernel, depth),
        [
            ((width_own, 4 * feats), bf16),
            ((24, width_own), f32),
            ((2 * blocks * width_own, hidden), bf16),
        ],
        Far(own_term),
        stacked,
        crossed,
        *other_terms,
        name="shard_sum",
        after=others,
        scratch=[pltpu.VMEM(own_term.shape, bf16), DMA((3,))],
    )
    if outer > 1:
        part = lax.psum(part, "ctx", axis_index_groups=outer_groups)
    mine, last_pair = kernel_call(
        functools.partial(vector_plane_kernel, depth),
        [((32, width_own), f32), ((2 * width_own, 4 * feats), bf16)],
        mine,
        swap_xy(mine),
        swap_x(mine),
        swap_y(mine),
        part,
        swap_x(part),
        name="vector_plane",
    )
    pieces = [last_pair, swap_core(last_pair), pair, swap_core(pair)]
    grad_gains, grad_shifts, grad_fc1_bias, grad_qv_bias = kernel_call(
        functools.partial(vector_place_kernel, depth, head_dim),
        [
            (norm_gains.shape, f32),
            (shifts.shape, f32),
            (fc1_bias.shape, f32),
            (qv_bias.shape, f32),
        ],
        mine,
        swap_core(mine),
        name="vector_place",
    )
    grad_inputs, outputs = (
        kernel_call(
            place_rows_kernel,
            [saved(inputs.shape, f32)],
            own,
            other,
            name="place_rows",
            scratch=[DMA((2,))],
        )[0]
        for own, other in zip((upstream, outputs_own), others)
    )
    placed = kernel_call(
        functools.partial(place_kernel, depth, hidden, feats),
        [saved(v.shape, f32) for v in (w_qkv, w_out, w_fc1, w_fc2)],
        *pieces,
        name="place",
        limit=24,
        scratch=[
            pltpu.VMEM((depth, GROUP, width_own, hidden), f32),
            pltpu.VMEM((depth, GROUP, hidden, width_own), f32),
            pltpu.VMEM((depth, GROUP, 3, width_own, feats), f32),
            pltpu.VMEM((depth, GROUP, feats, width_own), f32),
            DMA((16 * depth,)),
        ],
    )
    return (
        outputs,
        grad_inputs,
        grad_gains,
        grad_shifts,
        grad_qv_bias,
        grad_fc1_bias,
        *placed,
    )


def solution(mesh):
    rows = P("fsdp", "ctx", None)
    params = (
        P(None, None, "fsdp"),
        P(None, None, "fsdp"),
        P(None, None, "tp", "fsdp"),
        P(None, "tp", "fsdp"),
        P(None, None, "fsdp", "tp"),
        P(None, "tp", "fsdp"),
        P(None, "fsdp", "tp"),
        P(None, "tp", "fsdp"),
    )
    return jax.shard_map(
        per_device,
        mesh=mesh,
        in_specs=(rows, P("fsdp", None), rows) + params,
        out_specs=(rows, rows) + params,
        check_vma=False,
    )
```

```python
import functools
import math

import jax
import jax.numpy as jnp
from jax import lax
from jax.experimental import pallas as pl
from jax.experimental.pallas import tpu as pltpu
from jax.sharding import PartitionSpec as P

NORM_EPSILON = 1e-06
MASK_FILL = -1e30
ROOT_HALF = 0.7071067811865476
INV_ROOT_TAU = 0.3989422804014327
GROUP = 4
ORDER = (0, 5, 4, 1, 2, 7, 6, 3)
CHIPS = 4

bf16 = jnp.bfloat16
f32 = jnp.float32
VMEM = pl.BlockSpec(memory_space=pltpu.VMEM)
SMEM = pl.BlockSpec(memory_space=pltpu.SMEM)
HBM = pl.BlockSpec(memory_space=pltpu.HBM)
DMA = pltpu.SemaphoreType.DMA
TOKEN = ((8, 128), f32)


def dot(a, b):
    return lax.dot_general(a, b, (((1,), (0,)), ((), ())), preferred_element_type=f32)


def dot_nt(a, b):
    return lax.dot_general(a, b, (((1,), (1,)), ((), ())), preferred_element_type=f32)


def dot_tn(a, b):
    return lax.dot_general(a, b, (((0,), (0,)), ((), ())), preferred_element_type=f32)


class Far:
    def __init__(self, value):
        self.value = value


class Scalars:
    def __init__(self, value):
        self.value = value


def saved(shape, dtype):
    return pltpu.HBM(shape, dtype)


def kernel_call(body, outs, *args, name, limit=12, scratch=(), after=(), aliases=None, us=0):
    values, specs = [], []
    for arg in (*args, *after):
        if isinstance(arg, Far):
            values.append(pltpu.with_memory_space_constraint(arg.value, pltpu.HBM))
            specs.append(HBM)
        elif isinstance(arg, Scalars):
            values.append(arg.value)
            specs.append(SMEM)
        else:
            values.append(arg)
            specs.append(VMEM)
    first, last = len(args), len(args) + len(after)

    def run(*refs):
        body(*refs[:first], *refs[last:])

    out_shape, out_specs = [], []
    for out in outs:
        if isinstance(out, tuple):
            out_shape.append(jax.ShapeDtypeStruct(*out))
            out_specs.append(VMEM)
        else:
            out_shape.append(out)
            out_specs.append(HBM)
    return pl.pallas_call(
        run,
        out_shape=out_shape,
        in_specs=specs,
        out_specs=out_specs,
        scratch_shapes=list(scratch),
        input_output_aliases=aliases or {},
        compiler_params=pltpu.CompilerParams(vmem_limit_bytes=limit << 20),
        cost_estimate=pl.CostEstimate(flops=us * 10**9, bytes_accessed=0, transcendentals=0),
        name=name,
    )(*values)


def start_copies(pairs, sems):
    copies = [
        pltpu.make_async_copy(source, target, sems.at[k])
        for k, (source, target) in enumerate(pairs)
    ]
    for copy in copies:
        copy.start()
    return copies


def row_mean(value):
    return jnp.mean(value, axis=-1, keepdims=True)


def normalize(values):
    center = values - row_mean(values)
    inverse = lax.rsqrt(row_mean(center * center) + NORM_EPSILON)
    return center * inverse, inverse


def lanes_of(head, head_dim, width):
    lane = lax.broadcasted_iota(jnp.int32, (1, width), 1)
    return (lane >= head * head_dim) & (lane < (head + 1) * head_dim)


def assemble(chunks, target):
    rows = chunks[0].shape[0]
    for k, chunk in enumerate(chunks):
        target[k * rows : (k + 1) * rows, :] = chunk[...]


def only(flag, value):
    return jnp.where(flag, value, jnp.zeros_like(value))


def shards(weights):
    if len(weights) == 1:
        rows = weights[0].shape[0]
        return [(pl.ds(0, rows), weights[0])]
    count = len(weights)
    rows = weights[0].shape[0]
    f = lax.axis_index("fsdp")
    found = []
    for d, ref in enumerate(weights):
        place = lax.rem(f + (count - d), count)
        found.append((pl.ds(pl.multiple_of(place * rows, rows), rows), ref))
    return found


def pack_attn_kernel(layer, feats, qkv_hbm, out_hbm, packed_ref, token, qkv, out, sems):
    ci = lax.rem(lax.axis_index("ctx"), GROUP)
    span = pl.ds(pl.multiple_of(ci * feats, feats), feats)
    copies = start_copies(
        [(qkv_hbm.at[layer, :, :, span], qkv), (out_hbm.at[layer, span, :], out)], sems
    )
    copies[0].wait()
    for k in range(3):
        packed_ref[:, k * feats : (k + 1) * feats] = qkv[k]
    copies[1].wait()
    packed_ref[:, 3 * feats :] = out[...].T
    token[...] = jnp.zeros_like(token)


def pack_mlp_kernel(layer, hidden, fc1_hbm, fc2_hbm, packed_ref, token, fc1, fc2, sems):
    ci = lax.rem(lax.axis_index("ctx"), GROUP)
    span = pl.ds(pl.multiple_of(ci * hidden, hidden), hidden)
    copies = start_copies(
        [(fc1_hbm.at[layer, :, span], fc1), (fc2_hbm.at[layer, span, :], fc2)], sems
    )
    copies[0].wait()
    packed_ref[:, :hidden] = fc1[...]
    copies[1].wait()
    packed_ref[:, hidden:] = fc2[...].T
    token[...] = jnp.zeros_like(token)


def prep_upstream_kernel(tp, outer, lengths, cotangent_hbm,
                         upstream_hbm, upstream_b_ref, usable_ref, mask_ref,
                         rows_in, upstream_ref, sems):
    rows = rows_in.shape[0]
    c = lax.axis_index("ctx")
    t = lax.axis_index("tp")
    place = lax.rem(c, GROUP) * tp + t
    start = pl.multiple_of(t * rows, rows)
    copies = start_copies(
        [(cotangent_hbm.at[0, pl.ds(start, rows), :], rows_in)], sems.at[pl.ds(0, 1)]
    )
    lane = lax.broadcasted_iota(jnp.int32, usable_ref.shape, 1)
    limit = jnp.zeros(usable_ref.shape, jnp.int32)
    for o in range(outer):
        for k, d in enumerate(ORDER):
            source = place ^ d
            first_lane = (o * len(ORDER) + k) * rows
            count = lengths[0, o * GROUP + lax.div(source, tp)] - lax.rem(source, tp) * rows
            limit = jnp.where(lane >= first_lane, first_lane + jnp.clip(count, 0, rows), limit)
    usable_ref[...] = jnp.where(lane < limit, 1.0, 0.0)
    row = lax.broadcasted_iota(jnp.int32, mask_ref.shape, 0)
    mask = jnp.where(row + start < lengths[0, c], 1.0, 0.0)
    mask_ref[...] = mask
    copies[0].wait()
    upstream = rows_in[...] * mask[:, 0:1]
    upstream_ref[...] = upstream
    sent = start_copies([(upstream_ref, upstream_hbm)], sems.at[pl.ds(1, 1)])
    upstream_b_ref[...] = upstream.astype(bf16)
    sent[0].wait()


def prep_first_kernel(depth, inputs_hbm, vecs, stream_ref, first_ref, sems):
    rows = stream_ref.shape[0]
    start = pl.multiple_of(lax.axis_index("tp") * rows, rows)
    copies = start_copies([(inputs_hbm.at[0, pl.ds(start, rows), :], stream_ref)], sems)
    copies[0].wait()
    normed, _ = normalize(stream_ref[...])
    shift = vecs[2 * depth : 2 * depth + 1, :]
    first_ref[...] = (normed * vecs[0:1, :] + shift).astype(bf16)


def keep_rows_kernel(*refs):
    chunks, (near_hbm, far_hbm, token, near, far, sems) = refs[:8], refs[8:]
    assemble(chunks[:4], near)
    assemble(chunks[4:], far)
    for copy in start_copies([(near, near_hbm), (far, far_hbm)], sems):
        copy.wait()
    token[...] = jnp.zeros_like(token)


def qkv_kernel(feats, weight_count, *refs):
    c0, c1, c2, c3, *rest = refs
    weights = rest[:weight_count]
    bias, qkv_ref, x = rest[weight_count:]
    assemble((c0, c1, c2, c3), x)
    qkv = sum(dot(x[:, span], w[:, : 3 * feats]) for span, w in shards(weights))
    qkv_ref[:, :feats] = (qkv[:, :feats] + bias[0:1, :]).astype(bf16)
    qkv_ref[:, feats : 2 * feats] = qkv[:, feats : 2 * feats].astype(bf16)
    qkv_ref[:, 2 * feats :] = (qkv[:, 2 * feats :] + bias[1:2, :]).astype(bf16)


def attn_kernel(feats, heads, weight_count, part_count, keep_count, tile, *refs):
    q_ref, *rest = refs
    parts = rest[:part_count]
    weights = rest[part_count : part_count + weight_count]
    rest = rest[part_count + weight_count :]
    usable, *rest = rest
    kept, rest = rest[:keep_count], rest[keep_count:]
    partial_ref, attended_hbm, norm_hbm, *rest = rest
    kept_hbm, rest = rest[:keep_count], rest[keep_count:]
    keys, values, attended_ref, norm_ref, sems = rest
    head_dim = feats // heads
    scale = 1.0 / math.sqrt(head_dim)
    copies = start_copies(list(zip(kept, kept_hbm)), sems)
    first = 0
    for part in parts:
        rows, width = part.shape
        keys[first : first + rows, :] = part[:, width - 2 * feats : width - feats]
        values[first : first + rows, :] = part[:, width - feats :]
        first += rows
    keep = usable[...] > 0.5
    rows = q_ref.shape[0]
    for first in range(0, rows, tile):
        span = slice(first, first + tile)
        q = q_ref[span, :feats]
        attended = None
        for h in range(heads):
            own = lanes_of(h, head_dim, feats)
            scores = dot_nt(only(own, q), keys[...]) * scale
            scores = jnp.where(keep, scores, MASK_FILL)
            highest = jnp.max(scores, axis=-1, keepdims=True)
            raised = jnp.exp(scores - highest)
            total = jnp.sum(raised, axis=-1, keepdims=True)
            soft = (raised * (1.0 / total)).astype(bf16)
            result = dot(soft, values[...])
            log_norm = jnp.broadcast_to(highest + jnp.log(total), (tile, feats))
            if attended is None:
                attended, norms = result, log_norm
            else:
                attended = jnp.where(own, result, attended)
                norms = jnp.where(own, log_norm, norms)
        attended_ref[span, :] = attended.astype(bf16)
        norm_ref[span, :] = norms
    copies += start_copies(
        [(attended_ref, attended_hbm), (norm_ref, norm_hbm)],
        sems.at[pl.ds(keep_count, 2)],
    )
    for span, w in shards(weights):
        partial_ref[:, span] = dot_nt(attended_ref[...], w[:, 3 * feats :]).astype(bf16)
    for copy in copies:
        copy.wait()


def core_sum_kernel(count, *refs):
    pairs, owns = refs[: 2 * count], refs[2 * count : 3 * count]
    peers = refs[3 * count :]
    rows = owns[0].shape[0]
    for j in range(count):
        near, far = pairs[2 * j], pairs[2 * j + 1]
        for k in range(1 + len(peers)):
            span = slice(k * rows, (k + 1) * rows)
            total = near[span, :].astype(f32) + far[span, :].astype(f32)
            if k == 0:
                owns[j][...] = total
            else:
                peers[k - 1][j * rows : (j + 1) * rows, :] = total.astype(bf16)


def total_of(own, xy, x, y, part=0):
    rows = own.shape[0]
    span = slice(part * rows, (part + 1) * rows)
    return (
        own[...] + y[span, :].astype(f32) + x[span, :].astype(f32) + xy[span, :].astype(f32)
    )


def sum_norm_kernel(bias_row, gain_row, shift_row, own, xy, x, y, residual_hbm, vecs,
                    stream_ref, normed_ref, residual, sems):
    copies = start_copies([(residual_hbm, residual)], sems)
    total = total_of(own, xy, x, y) + vecs[bias_row : bias_row + 1, :]
    copies[0].wait()
    stream = residual[...] + total
    stream_ref[...] = stream
    normed, _ = normalize(stream)
    gain = vecs[gain_row : gain_row + 1, :]
    normed_ref[...] = (normed * gain + vecs[shift_row : shift_row + 1, :]).astype(bf16)


def sum_out_kernel(bias_row, own, xy, x, y, residual_hbm, vecs, mask, out_hbm, token,
                   residual, out_ref, sems):
    copies = start_copies([(residual_hbm, residual)], sems.at[pl.ds(0, 1)])
    total = total_of(own, xy, x, y, 1) + vecs[bias_row : bias_row + 1, :]
    copies[0].wait()
    out_ref[...] = (residual[...] + total) * mask[:, 0:1]
    token[...] = jnp.zeros_like(token)
    for copy in start_copies([(out_ref, out_hbm)], sems.at[pl.ds(1, 1)]):
        copy.wait()


def mlp_kernel(hidden, keep_count, saves, loads, c0, c1, c2, c3, w, bias, *refs):
    kept, rest = refs[:keep_count], refs[keep_count:]
    partial_ref, x_out, act_out, slope_out, *rest = rest
    kept_hbm, rest = rest[:keep_count], rest[keep_count:]
    loaded = []
    if loads:
        *rest, w_ref, w_sems = rest
        spans = (pl.ds(0, hidden), pl.ds(hidden, hidden))
        loaded = start_copies([(w.at[:, c], w_ref.at[:, c]) for c in spans], w_sems)
        w = w_ref
    if saves:
        x, act_ref, slope_ref, sems = rest
    else:
        x, act_ref, slope_ref = x_out, act_out, slope_out
        (sems,) = rest
    copies = start_copies(list(zip(kept, kept_hbm)), sems)
    assemble((c0, c1, c2, c3), x)
    if saves:
        copies += start_copies([(x, x_out)], sems.at[pl.ds(keep_count, 1)])
    block = hidden // 2
    if loads:
        loaded[0].wait()
    for k in range(2):
        span = slice(k * block, (k + 1) * block)
        pre = dot(x[...], w[:, span]) + bias[:, span]
        cdf = 0.5 * (1.0 + lax.erf(pre * ROOT_HALF))
        density = jnp.exp(-0.5 * pre * pre) * INV_ROOT_TAU
        slope_ref[k] = cdf + pre * density
        act_ref[:, span] = (pre * cdf).astype(bf16)
        if saves:
            copies += start_copies(
                [(slope_ref.at[k], slope_out.at[k])], sems.at[pl.ds(1 + keep_count + k, 1)]
            )
    if saves:
        copies += start_copies([(act_ref, act_out)], sems.at[pl.ds(3 + keep_count, 1)])
    if loads:
        loaded[1].wait()
    partial_ref[...] = dot_nt(act_ref[...], w[:, hidden:]).astype(bf16)
    for copy in copies:
        copy.wait()


def mlp_back_kernel(hidden, chunk_count, *refs):
    chunks, (w, slope, *rest) = refs[:chunk_count], refs[chunk_count:]
    partial_ref, grad_ref, sum_hbm, x, sum_ref, sems = rest
    assemble(chunks, x)
    grad = dot(x[...], w[:, hidden:])
    block = hidden // 2
    for k in range(2):
        span = slice(k * block, (k + 1) * block)
        part = grad[:, span] * slope[k]
        grad_ref[:, span] = part.astype(bf16)
        sum_ref[:, span] = jnp.sum(part, axis=0, keepdims=True)
    sent = start_copies([(sum_ref, sum_hbm)], sems)
    partial_ref[...] = dot_nt(grad_ref[...], w[:, :hidden]).astype(bf16)
    sent[0].wait()


def mlp_grad_kernel(hidden, second_near, second_far, act_near, act_far, up_near, up_far,
                    grad_near, grad_far, out_hbm, token, out_one, out_two, sems):
    token[...] = jnp.zeros_like(token)
    total = dot_tn(up_near[...], act_near[...]) + dot_tn(up_far[...], act_far[...])
    out_two[...] = total.astype(bf16)
    sent = start_copies(
        [(out_two, out_hbm.at[:, pl.ds(hidden, hidden)])], sems.at[pl.ds(0, 1)]
    )
    total = dot_tn(second_near[...], grad_near[...]) + dot_tn(second_far[...], grad_far[...])
    out_one[...] = total.astype(bf16)
    sent += start_copies([(out_one, out_hbm.at[:, pl.ds(0, hidden)])], sems.at[pl.ds(1, 1)])
    for copy in sent:
        copy.wait()


def norm_back(upstream, values, gain):
    normed, inverse = normalize(values)
    scaled = upstream * gain
    back = inverse * (scaled - row_mean(scaled) - normed * row_mean(scaled * normed))
    gain_grad = jnp.sum(upstream * normed, axis=0, keepdims=True)
    return back, gain_grad, jnp.sum(upstream, axis=0, keepdims=True)


def norm_back_two_kernel(gain_row, own, xy, x, y, values_hbm, upstream_hbm, vecs,
                         grad_ref, grad_b_ref, sums_ref, values, upstream, sems):
    copies = start_copies([(values_hbm, values), (upstream_hbm, upstream)], sems)
    total = total_of(own, xy, x, y)
    for copy in copies:
        copy.wait()
    up = upstream[...]
    back, gain_grad, shift_grad = norm_back(
        total, values[...], vecs[gain_row : gain_row + 1, :]
    )
    grad = up + back
    grad_ref[...] = grad
    grad_b_ref[...] = grad.astype(bf16)
    sums_ref[0:1, :] = gain_grad
    sums_ref[1:2, :] = shift_grad
    sums_ref[2:3, :] = jnp.sum(grad, axis=0, keepdims=True)
    sums_ref[3:4, :] = jnp.sum(up, axis=0, keepdims=True)


def norm_back_one_kernel(gain_row, own, xy, x, y, values_hbm, upstream_hbm, vecs, mask,
                         grad_ref, grad_b_ref, sums_ref, values, upstream, sems):
    copies = start_copies([(values_hbm, values), (upstream_hbm, upstream)], sems)
    total = total_of(own, xy, x, y)
    for copy in copies:
        copy.wait()
    back, gain_grad, shift_grad = norm_back(
        total, values[...], vecs[gain_row : gain_row + 1, :]
    )
    grad = upstream[...] + back
    if mask is not None:
        grad = grad * mask[:, 0:1]
    grad_ref[...] = grad
    grad_b_ref[...] = grad.astype(bf16)
    sums_ref[0:1, :] = gain_grad
    sums_ref[1:2, :] = shift_grad


def attn_back_kernel(feats, heads, weight_count, part_count, tile, carried, *refs):
    c0, c1, c2, c3, *rest = refs
    weights, rest = rest[:weight_count], rest[weight_count:]
    usable, qkv, attended, norms, *rest = rest
    parts, rest = rest[:part_count], rest[part_count:]
    if carried:
        keys_before, values_before, *rest = rest
    x, grad_q, grad_k, grad_v, pairs, grad_att = rest
    head_dim = feats // heads
    scale = 1.0 / math.sqrt(head_dim)
    first = 0
    for part in parts:
        rows, width = part.shape
        pairs[first : first + rows, :] = part[:, width - 2 * feats :]
        first += rows
    assemble((c0, c1, c2, c3), x)
    grad_att[...] = sum(
        dot(x[:, span], w[:, 3 * feats :]) for span, w in shards(weights)
    ).astype(bf16)
    keep = usable[...] > 0.5
    rows = qkv.shape[0]
    if carried:
        sum_k, sum_v = keys_before[...], values_before[...]
    else:
        sum_k = jnp.zeros(grad_k.shape, f32)
        sum_v = jnp.zeros(grad_v.shape, f32)
    keys, values = pairs[:, :feats], pairs[:, feats:]
    for first in range(0, rows, tile):
        span = slice(first, first + tile)
        q = qkv[span, :feats]
        ga = grad_att[span, :]
        products = ga.astype(f32) * attended[span, :].astype(f32)
        gq = None
        for h in range(heads):
            own = lanes_of(h, head_dim, feats)
            q_h = only(own, q)
            ga_h = only(own, ga)
            row_dots = jnp.sum(only(own, products), axis=-1, keepdims=True)
            scores = dot_nt(q_h, keys) * scale
            scores = jnp.where(keep, scores, MASK_FILL)
            soft = jnp.exp(scores - norms[span, h * head_dim : h * head_dim + 1])
            grad_soft = dot_nt(ga_h, values)
            grad_scores = (soft * (grad_soft - row_dots)).astype(bf16)
            part = dot(grad_scores, keys)
            gq = part if gq is None else jnp.where(own, part, gq)
            sum_k = sum_k + dot_tn(grad_scores, q_h) * scale
            sum_v = sum_v + dot_tn(soft.astype(bf16), ga_h)
        grad_q[span, :] = gq * scale
    grad_k[...] = sum_k
    grad_v[...] = sum_v


def project_kernel(feats, first, weight_count, gq, gk, gv, *refs):
    weights, (partial_ref, packed) = refs[:weight_count], refs[weight_count:]
    rows = gq.shape[0]
    span = slice(first, first + rows)
    packed[:, :feats] = gq[...].astype(bf16)
    packed[:, feats : 2 * feats] = gk[span, :].astype(bf16)
    packed[:, 2 * feats :] = gv[span, :].astype(bf16)
    for columns, w in shards(weights):
        partial_ref[:, columns] = dot_nt(packed[...], w[:, : 3 * feats]).astype(bf16)


def attn_grad_kernel(feats, count, keep_count, first_near, first_far, att_near, att_far,
                     up_near, up_far, gq_near, gq_far, gk, gv, passed, lines, *refs):
    kept, refs = refs[:keep_count], refs[keep_count:]
    outs, refs = refs[:count], refs[count:]
    heads_hbm, passed_ref, *refs = refs
    kept_hbm, (packed, sums_ref, *staged, sems) = refs[:keep_count], refs[keep_count:]
    rows = up_near.shape[0]
    used = count + 2
    sent = start_copies(list(zip(kept, kept_hbm)), sems.at[pl.ds(used, keep_count)])
    passed_ref[...] = passed[...]
    packed[:rows, :feats] = gq_near[...].astype(bf16)
    packed[rows:, :feats] = gq_far[...].astype(bf16)
    packed[:, feats : 2 * feats] = gk[...].astype(bf16)
    packed[:, 2 * feats :] = gv[...].astype(bf16)
    sums_ref[0:1, :] = jnp.sum(gq_near[...], axis=0, keepdims=True) + jnp.sum(
        gq_far[...], axis=0, keepdims=True
    )
    sums_ref[1:2, :] = jnp.sum(gv[...], axis=0, keepdims=True)
    sent += start_copies([(sums_ref, heads_hbm)], sems.at[pl.ds(0, 1)])

    def out_part(span):
        return dot_tn(up_near[:, span], att_near[...]) + dot_tn(up_far[:, span], att_far[...])

    def qkv_part(span):
        return dot_tn(first_near[:, span], packed[:rows, :]) + dot_tn(
            first_far[:, span], packed[rows:, :]
        )

    if count == 1:
        out_one, out_two = staged
        whole = slice(None)
        out_two[...] = out_part(whole).astype(bf16)
        sent += start_copies(
            [(out_two, outs[0].at[:, pl.ds(3 * feats, feats)])], sems.at[pl.ds(1, 1)]
        )
        out_one[...] = qkv_part(whole).astype(bf16)
        sent += start_copies(
            [(out_one, outs[0].at[:, pl.ds(0, 3 * feats)])], sems.at[pl.ds(2, 1)]
        )
    else:
        (stage,) = staged
        below = lines.shape[1]
        width_own = outs[0].shape[0] - below
        for d in reversed(range(count)):
            place = lax.rem(lax.axis_index("fsdp") + d, count)
            span = pl.ds(pl.multiple_of(place * width_own, width_own), width_own)
            stage[d, :width_own, : 3 * feats] = qkv_part(span).astype(bf16)
            stage[d, :width_own, 3 * feats :] = out_part(span).astype(bf16)
            stage[d, width_own:, :] = lines[d]
            sent += start_copies([(stage.at[d], outs[d])], sems.at[pl.ds(1 + d, 1)])
    for copy in sent:
        copy.wait()


def settle_kernel(keep_count, after_count, passed, *refs):
    kept, refs = refs[:keep_count], refs[keep_count + after_count :]
    passed_ref, *kept_hbm, sems = refs
    copies = start_copies(list(zip(kept, kept_hbm)), sems)
    passed_ref[...] = passed[...]
    for copy in copies:
        copy.wait()


def fetch_kernel(count, *refs):
    sources, (target, sems) = refs[:count], refs[count:]
    columns = target.shape[1]
    moves = []
    row = 0
    for source in sources:
        rows = source.shape[0]
        for first in range(0, source.shape[1], columns):
            moves.append(
                (source.at[:, pl.ds(first, columns)], target.at[pl.ds(row, rows), :])
            )
            row += rows
    for copy in start_copies(moves, sems):
        copy.wait()


def shard_sum_kernel(depth, own_hbm, stacked, crossed, *refs):
    *others, part_ref, mine_ref, pair_ref, own, sems = refs
    count = stacked.shape[0]
    first, *copies = start_copies(
        [
            (own_hbm, own),
            (stacked, pair_ref.at[pl.ds(0, count), :]),
            (crossed, pair_ref.at[pl.ds(count, count), :]),
        ],
        sems,
    )
    first.wait()
    rows, width = part_ref.shape[0], mine_ref.shape[1]
    terms = [ref[...].astype(f32) for ref in (own, *others)]
    total = terms[0]
    for term in terms[1:]:
        total = total + term
    part_ref[...] = total[:rows, :].astype(bf16)
    lines = total[rows:, :width] + total[rows:, width:]
    mine_ref[: 6 * depth, :] = lines[: 6 * depth, :]
    for k in range(mine_ref.shape[0] - 16):
        mine_ref[16 + k : 17 + k, :] = lines[6 * depth + k : 6 * depth + k + 1, :]
    for copy in copies:
        copy.wait()


def place_kernel(depth, hidden, feats, *refs):
    alone, pairs, rest = refs[:2], refs[2:4], refs[4:]

    def half_of(pair, k):
        count = pair[k % 2].shape[0] // 2
        return pair[k % 2].at[pl.ds(k // 2 * count, count), :]

    slices = [(half_of(alone, k), half_of(pairs, k)) for k in range(GROUP)]
    qkv_hbm, out_hbm, fc1_hbm, fc2_hbm, fc1, fc2, qkv, out, sems = rest
    ci = lax.rem(lax.axis_index("ctx"), GROUP)
    rows = fc1.shape[2]
    copies = []

    def send(source, target):
        copies.extend(start_copies([(source, target)], sems.at[pl.ds(len(copies), 1)]))

    for l in range(depth):
        for k in range(GROUP):
            _, stacked = slices[k]
            first = 0 if l == 0 else (3 * l - 1) * rows
            span = pl.ds(pl.multiple_of((ci ^ k) * hidden, hidden), hidden)
            fc1[l, k] = stacked[first : first + rows, :].astype(f32)
            send(fc1.at[l, k], fc1_hbm.at[l, :, span])
            fc2[l, k] = stacked[first + rows : first + 2 * rows, :].T.astype(f32)
            send(fc2.at[l, k], fc2_hbm.at[l, span, :])
    for l in reversed(range(depth)):
        for k in range(GROUP):
            last, stacked = slices[k]
            piece = last if l == 0 else stacked.at[pl.ds((3 * l + 1) * rows, rows), :]
            span = pl.ds(pl.multiple_of((ci ^ k) * feats, feats), feats)
            for j in range(3):
                qkv[l, k, j] = piece[:, j * feats : (j + 1) * feats].astype(f32)
            send(qkv.at[l, k], qkv_hbm.at[l, :, :, span])
            out[l, k] = piece[:, 3 * feats :].T.astype(f32)
            send(out.at[l, k], out_hbm.at[l, span, :])
    for copy in copies:
        copy.wait()


def vector_pack_kernel(depth, one_now, gq_near, gq_far, gv, *refs):
    count = 5 * depth - 2
    out_ref, *found, sems = refs[count:]
    copies = start_copies(list(zip(refs[:count], found)), sems)
    out_ref[...] = jnp.zeros_like(out_ref)
    feats = gv.shape[1]
    head_now = [
        jnp.sum(gq_near[...], axis=0, keepdims=True) + jnp.sum(gq_far[...], axis=0, keepdims=True),
        jnp.sum(gv[...], axis=0, keepdims=True),
    ]
    for copy in copies:
        copy.wait()
    for l in range(depth):
        if l == 0:
            one, (two, unit_near, unit_far) = one_now, found[:3]
            heads = head_now
        else:
            one, two, unit_near, unit_far, head = found[5 * l - 2 : 5 * l + 3]
            heads = [head[0:1, :], head[1:2, :]]
        out_ref[6 * l : 6 * l + 1, :] = one[0:1, :]
        out_ref[6 * l + 1 : 6 * l + 2, :] = two[0:1, :]
        out_ref[6 * l + 2 : 6 * l + 3, :] = one[1:2, :]
        out_ref[6 * l + 3 : 6 * l + 6, :] = two[1:4, :]
        units = unit_near.shape[1]
        row = 6 * depth
        out_ref[row : row + 1, l * units : (l + 1) * units] = unit_near[...] + unit_far[...]
        for j in range(2):
            start = (2 * l + j) * feats
            out_ref[row + 1 : row + 2, start : start + feats] = heads[j]


def vector_lines_kernel(depth, width_own, packed, lines_ref):
    count = lines_ref.shape[0]
    f = lax.axis_index("fsdp")
    total = packed[...]
    high = total.astype(bf16).astype(f32)
    low = total - high
    lines_ref[...] = jnp.zeros_like(lines_ref)
    last = 6 * depth
    for k, value in enumerate((high, low)):
        lanes = slice(k * width_own, (k + 1) * width_own)
        columns = [value[:, a * width_own : (a + 1) * width_own] for a in range(count)]
        for d in range(count):
            mine = columns[0]
            for a in range(1, count):
                mine = jnp.where(lax.rem(f + d, count) == a, columns[a], mine)
            rows = [mine[:last, :]]
            for r in range(2):
                for a in range(count):
                    rows.append(columns[a][last + r : last + r + 1, :])
            rows.append(jnp.zeros((lines_ref.shape[1] - last - 2 * count, width_own), f32))
            lines_ref[d, :, lanes] = jnp.concatenate(rows, axis=0).astype(bf16)


def vector_plane_kernel(depth, own, xy, x, y, part, part_x, out_ref, pair_ref):
    last = 6 * depth
    rows = part.shape[0]
    pair_ref[:rows, :] = part[...]
    pair_ref[rows:, :] = part_x[...]
    out_ref[:last, :] = own[:last, :] + xy[:last, :] + x[:last, :] + y[:last, :]
    out_ref[16:24, :] = own[16:24, :]
    out_ref[24:32, :] = x[16:24, :]


def vector_place_kernel(depth, head_dim, own, far, gains_ref, shifts_ref, unit_ref, heads_ref):
    total = own[: 6 * depth, :] + far[: 6 * depth, :]
    for l in range(depth):
        gains_ref[l] = total[6 * l : 6 * l + 2, :]
        shifts_ref[l] = total[6 * l + 2 : 6 * l + 6, :]
    pieces = (own[16:24, :], far[16:24, :], own[24:32, :], far[24:32, :])
    ci = lax.rem(lax.axis_index("ctx"), GROUP)
    f = lax.axis_index("fsdp")

    def of_place(c):
        k = ci ^ c
        found = pieces[0]
        for j in range(1, GROUP):
            found = jnp.where(k == j, pieces[j], found)
        return found

    width_own = own.shape[1]
    units = of_place(f)
    parts = unit_ref.shape[2] // width_own
    for l in range(depth):
        for j in range(parts):
            row = l * parts + j
            unit_ref[l, :, j * width_own : (j + 1) * width_own] = units[row : row + 1, :]
    head_own = heads_ref.shape[3]
    heads = heads_ref.shape[2] // GROUP
    for c in range(GROUP):
        found = of_place(c)
        for l in range(depth):
            for j in range(2):
                for h in range(heads):
                    first = ((2 * l + j) * heads + h) * head_dim
                    row, lane = 4 + first // width_own, first % width_own
                    value = found[row : row + 1, lane : lane + head_own]
                    for a in range(1, head_dim // head_own):
                        start = lane + a * head_own
                        value = jnp.where(
                            f == a, found[row : row + 1, start : start + head_own], value
                        )
                    heads_ref[l, j, c * heads + h : c * heads + h + 1, :] = value


def place_rows_kernel(own, other, out_hbm, sems):
    rows = own.shape[0]
    start = pl.multiple_of(lax.axis_index("tp") * rows, rows)
    copies = start_copies(
        [
            (own, out_hbm.at[0, pl.ds(start, rows), :]),
            (other, out_hbm.at[0, pl.ds(pl.multiple_of(rows - start, rows), rows), :]),
        ],
        sems,
    )
    for copy in copies:
        copy.wait()


def per_device(
    inputs, lengths, cotangent, norm_gains, shifts, qv_bias, fc1_bias, w_qkv, w_out, w_fc1, w_fc2
):
    depth = w_qkv.shape[0]
    width_own = w_qkv.shape[2]
    fsdp = lax.axis_size("fsdp")
    tp = lax.axis_size("tp")
    ctx = lax.axis_size("ctx")
    outer = ctx // GROUP
    rows = inputs.shape[1] // tp
    half = rows * CHIPS
    all_rows = 2 * half
    head_own = qv_bias.shape[3]
    head_dim = head_own * fsdp
    heads = qv_bias.shape[2] // GROUP
    feats = heads * head_dim
    hidden = w_fc1.shape[2] // GROUP
    width = width_own * fsdp
    t = lax.axis_index("tp")
    f = lax.axis_index("fsdp")
    ci = lax.axis_index("ctx") % GROUP
    tile = half // 2
    attn_limit = 12 if outer == 1 else 48

    def swap_core(value):
        return lax.ppermute(value, "ctx", [(i, i ^ 1) for i in range(ctx)])

    def swap_x(value):
        return lax.ppermute(value, "ctx", [(i, i ^ 2) for i in range(ctx)])

    def swap_y(value):
        return lax.ppermute(value, "tp", [(i, i ^ 1) for i in range(tp)])

    def swap_xy(value):
        pairs = [
            (i * tp + k, (i ^ 2) * tp + (k ^ 1)) for i in range(ctx) for k in range(tp)
        ]
        return lax.ppermute(value, ("ctx", "tp"), pairs)

    def shift_z(value, d):
        return lax.ppermute(value, "fsdp", [(i, (i + d) % fsdp) for i in range(fsdp)])

    outer_groups = [[o * GROUP + i for o in range(outer)] for i in range(GROUP)]

    def gather_rows(own):
        near = (own, swap_xy(own), swap_x(own), swap_y(own))
        return near, tuple(swap_core(chunk) for chunk in near)

    def settle(value, there, *kept):
        return kernel_call(
            functools.partial(settle_kernel, len(kept), 1),
            [(value.shape, value.dtype)] + [saved(k.shape, k.dtype) for k in kept],
            value,
            *kept,
            Far(there),
            name="settle",
            scratch=[DMA((max(1, len(kept)),))],
        )

    def reduce_rows(*pairs, after=()):
        count = len(pairs)
        *owns, xy, x, y = kernel_call(
            functools.partial(core_sum_kernel, count),
            [((rows, width), f32)] * count + [((count * rows, width), bf16)] * 3,
            *[v for near, far in pairs for v in (near, swap_core(far))],
            name="core_sum",
            after=after,
        )
        peers = (swap_xy(xy), swap_x(x), swap_y(y))
        return [(own, *peers) for own in owns]

    def pack_attn(l, after):
        return kernel_call(
            functools.partial(pack_attn_kernel, l, feats),
            [((width_own, 4 * feats), bf16), TOKEN],
            Far(w_qkv),
            Far(w_out),
            name="pack_attn",
            after=after,
            scratch=[
                pltpu.VMEM((3, width_own, feats), bf16),
                pltpu.VMEM((feats, width_own), bf16),
                DMA((2,)),
            ],
        )

    def pack_mlp(l, after):
        return kernel_call(
            functools.partial(pack_mlp_kernel, l, hidden),
            [((width_own, 2 * hidden), bf16), TOKEN],
            Far(w_fc1),
            Far(w_fc2),
            name="pack_mlp",
            after=after,
            scratch=[
                pltpu.VMEM((width_own, hidden), bf16),
                pltpu.VMEM((hidden, width_own), bf16),
                DMA((2,)),
            ],
        )

    attn_w = []
    mlp_w = []
    token = None
    for l in range(depth):
        own, token = pack_attn(l, () if token is None else (token,))
        attn_w.append((lax.all_gather(own, "fsdp", axis=0, tiled=True),))
        own, token = pack_mlp(l, (token,))
        mlp_w.append(lax.all_gather(own, "fsdp", axis=0, tiled=True))
        if l == 0:
            pack_token = token

    qv_own = lax.dynamic_slice_in_dim(qv_bias, ci * heads, heads, axis=2)
    vec_rows = depth * 6
    c1_rows = depth * fc1_bias.shape[2] // width_own
    qv_own = qv_own.reshape(1, -1)
    small_own = jnp.concatenate(
        [
            norm_gains.reshape(-1, width_own),
            shifts.reshape(-1, width_own),
            fc1_bias.reshape(-1, width_own),
            jnp.pad(qv_own, ((0, 0), (0, width_own - qv_own.shape[1]))),
        ],
        axis=0,
    )
    shifted = [small_own] + [shift_z(small_own, d) for d in range(1, fsdp)]

    def shard(a):
        picked = shifted[0]
        for d in range(1, fsdp):
            picked = jnp.where((f - d) % fsdp == a, shifted[d], picked)
        return picked.astype(f32)

    small = [shard(a) for a in range(fsdp)]
    vecs = jnp.concatenate([s[:vec_rows] for s in small], axis=1)
    fc1_all = shard(ci)[vec_rows : vec_rows + c1_rows].reshape(depth, 1, hidden)
    qv_all = jnp.stack(
        [s[vec_rows + c1_rows, : qv_own.shape[1]].reshape(depth, 2, heads, head_own) for s in small],
        axis=3,
    ).reshape(depth, 2, feats)

    def gain_row(l, i):
        return 2 * l + i

    def shift_row(l, i):
        return 2 * depth + 4 * l + i

    key_rows = outer * all_rows
    row_f32 = ((rows, width), f32)
    row_bf16 = ((rows, width), bf16)
    upstream, upstream_b, usable, mask = kernel_call(
        functools.partial(prep_upstream_kernel, tp, outer),
        [saved((rows, width), f32), row_bf16, ((1, key_rows), f32), ((rows, 128), f32)],
        Scalars(lengths),
        Far(cotangent),
        name="prep_upstream",
        after=(pack_token,),
        scratch=[pltpu.VMEM((rows, width), f32), pltpu.VMEM((rows, width), f32), DMA((2,))],
    )
    near, far = gather_rows(upstream_b)
    half_x = pltpu.VMEM((half, width), bf16)
    *upstream_rows, upstream_token = kernel_call(
        keep_rows_kernel,
        [saved((half, width), bf16)] * 2 + [TOKEN],
        *near,
        *far,
        name="keep_rows",
        scratch=[half_x, half_x, DMA((2,))],
    )
    upstream_chunks = [(x,) for x in upstream_rows]
    stream, first = kernel_call(
        functools.partial(prep_first_kernel, depth),
        [row_f32, row_bf16],
        Far(inputs),
        vecs,
        name="prep_first",
        scratch=[DMA((1,))],
    )
    first_chunks = gather_rows(first)

    partial_out = ((half, width), bf16)
    saved_all = []
    for l in range(depth):
        qkv = []
        first_x = []
        for side in (0, 1):
            qkv_half, x_half = kernel_call(
                functools.partial(qkv_kernel, feats, len(attn_w[l])),
                [((half, 3 * feats), bf16), ((half, width), bf16)],
                *first_chunks[side],
                *attn_w[l],
                qv_all[l],
                name="qkv",
                after=(upstream_token,) if l == 0 and side == 0 else (),
            )
            qkv.append(qkv_half)
            first_x.append(x_half)
        if outer > 1:
            pairs = jnp.concatenate([part[:, feats:] for part in qkv], axis=0)
            pairs = lax.all_gather(
                pairs, "ctx", axis=0, tiled=True, axis_index_groups=outer_groups
            )
            key_parts = (pairs,)
        else:
            key_parts = tuple(qkv)
        attn = [None, None]
        for side in (1, 0):
            kept = (first_x[side], qkv[side]) + ((stream,) if side == 1 else ())
            attn[side] = kernel_call(
                functools.partial(
                    attn_kernel, feats, heads, len(attn_w[l]), len(key_parts), len(kept), tile
                ),
                [partial_out, saved((half, feats), bf16), saved((half, feats), f32)]
                + [saved(k.shape, k.dtype) for k in kept],
                qkv[side],
                *key_parts,
                *attn_w[l],
                usable,
                *kept,
                name="attn",
                limit=attn_limit,
                scratch=[
                    pltpu.VMEM((key_rows, feats), bf16),
                    pltpu.VMEM((key_rows, feats), bf16),
                    pltpu.VMEM((half, feats), bf16),
                    pltpu.VMEM((half, feats), f32),
                    DMA((len(kept) + 2,)),
                ],
            )
        (sums,) = reduce_rows((attn[0][0], attn[1][0]))
        middle, second = kernel_call(
            functools.partial(sum_norm_kernel, shift_row(l, 2), gain_row(l, 1), shift_row(l, 1)),
            [row_f32, row_bf16],
            *sums,
            Far(attn[1][5]),
            vecs,
            name="sum_norm",
            scratch=[pltpu.VMEM((rows, width), f32), DMA((1,))],
        )
        second_chunks = gather_rows(second)
        mlp = [None, None]
        for side in (1, 0):
            kept = (middle,) if side == 1 else ()
            saves = l + 1 < depth
            loads = not saves and side == 1
            shapes = [
                ((half, width), bf16),
                ((half, hidden), bf16),
                ((2, half, hidden // 2), f32),
            ]
            mlp[side] = kernel_call(
                functools.partial(mlp_kernel, hidden, len(kept), saves, loads),
                [partial_out]
                + [saved(*shape) if saves else shape for shape in shapes]
                + [saved(k.shape, k.dtype) for k in kept],
                *second_chunks[side],
                Far(mlp_w[l]) if loads else mlp_w[l],
                fc1_all[l],
                *kept,
                name="mlp",
                scratch=[pltpu.VMEM(*shape) for shape in shapes if saves]
                + [DMA((4 + len(kept),))]
                + ([pltpu.VMEM((width, 2 * hidden), bf16), DMA((2,))] if loads else []),
            )
        saved_all.append((attn, pairs if outer > 1 else None, mlp))
        if l + 1 < depth:
            (sums,) = reduce_rows((mlp[0][0], mlp[1][0]))
            stream, first = kernel_call(
                functools.partial(
                    sum_norm_kernel, shift_row(l, 3), gain_row(l + 1, 0), shift_row(l + 1, 0)
                ),
                [row_f32, row_bf16],
                *sums,
                Far(mlp[1][4]),
                vecs,
                name="sum_norm",
                scratch=[pltpu.VMEM((rows, width), f32), DMA((1,))],
            )
            first_chunks = gather_rows(first)

    def scatter_grads(grad):
        part = lax.psum_scatter(grad, "fsdp", scatter_dimension=0, tiled=True)
        if outer > 1:
            part = lax.psum(part, "ctx", axis_index_groups=outer_groups)
        return part

    row_sums = [None] * depth
    unit_sums = [None] * depth
    head_sums = [None] * depth
    mlp_parts = [None] * depth
    attn_parts = [None] * depth
    for l in reversed(range(depth)):
        attn, pairs, mlp = saved_all[l]
        back = [None, None]
        for side in (1, 0):
            back[side] = kernel_call(
                functools.partial(mlp_back_kernel, hidden, len(upstream_chunks[side])),
                [
                    partial_out,
                    ((half, hidden), bf16),
                    saved((1, hidden), f32),
                    ((half, width), bf16),
                ],
                *upstream_chunks[side],
                mlp_w[l],
                mlp[side][3],
                name="mlp_back",
                scratch=[pltpu.VMEM((1, hidden), f32), DMA((1,))],
            )
        mlp_grad, token = kernel_call(
            functools.partial(mlp_grad_kernel, hidden),
            [saved((width, 2 * hidden), bf16), TOKEN],
            mlp[0][1],
            mlp[1][1],
            mlp[0][2],
            mlp[1][2],
            back[0][3],
            back[1][3],
            back[0][1],
            back[1][1],
            name="mlp_grad",
            scratch=[
                pltpu.VMEM((width, hidden), bf16),
                pltpu.VMEM((width, hidden), bf16),
                DMA((2,)),
            ],
        )
        mlp_parts[l] = scatter_grads(mlp_grad)
        pairs_now = [(back[0][0], back[1][0])]
        if l + 1 == depth:
            pairs_now.append((mlp[0][0], mlp[1][0]))
        sums, *output_sums = reduce_rows(*pairs_now, after=(token,))
        if l + 1 == depth:
            outputs_own, output_token = kernel_call(
                functools.partial(sum_out_kernel, shift_row(l, 3)),
                [saved((rows, width), f32), TOKEN],
                *output_sums[0],
                Far(mlp[1][4]),
                vecs,
                mask,
                name="sum_out",
                scratch=[pltpu.VMEM((rows, width), f32)] * 2 + [DMA((2,))],
            )
            after = (output_token,)
        else:
            after = ()
        unit_sums[l] = (back[0][2], back[1][2])
        grad_middle, middle_b, sums_two = kernel_call(
            functools.partial(norm_back_two_kernel, gain_row(l, 1)),
            [row_f32, row_bf16, ((4, width), f32)],
            *sums,
            Far(mlp[1][4]),
            Far(upstream),
            vecs,
            name="norm_back_two",
            after=after,
            scratch=[pltpu.VMEM((rows, width), f32)] * 2 + [DMA((2,))],
        )
        if l + 1 < depth:
            middle_b, sums_two, grad_middle = settle(
                middle_b, attn_parts[l + 1], sums_two, grad_middle
            )
        middle_chunks = gather_rows(middle_b)
        grad_q = [None, None]
        middle_x = [None, None]
        carried = ()
        for side in (0, 1):
            key_parts = (pairs,) if outer > 1 else (attn[0][4], attn[1][4])
            middle_x[side], grad_q[side], *carried = kernel_call(
                functools.partial(
                    attn_back_kernel,
                    feats,
                    heads,
                    len(attn_w[l]),
                    len(key_parts),
                    tile,
                    len(carried) > 0,
                ),
                [
                    ((half, width), bf16),
                    ((half, feats), f32),
                    ((key_rows, feats), f32),
                    ((key_rows, feats), f32),
                ],
                *middle_chunks[side],
                *attn_w[l],
                usable,
                attn[side][4],
                attn[side][1],
                attn[side][2],
                *key_parts,
                *carried,
                name="attn_back",
                scratch=[
                    pltpu.VMEM((key_rows, 2 * feats), bf16),
                    pltpu.VMEM((half, feats), bf16),
                ],
                limit=attn_limit,
            )
        grad_k, grad_v = carried
        if outer > 1:
            grad_k, grad_v = (
                lax.psum_scatter(
                    v, "ctx", scatter_dimension=0, tiled=True, axis_index_groups=outer_groups
                )
                for v in (grad_k, grad_v)
            )

        def project(side, after):
            return kernel_call(
                functools.partial(project_kernel, feats, side * half, len(attn_w[l])),
                [partial_out],
                grad_q[side],
                grad_k,
                grad_v,
                *attn_w[l],
                name="project",
                after=after,
                scratch=[pltpu.VMEM((half, 3 * feats), bf16)],
            )[0]

        far_part = project(1, ())
        near_part = project(0, ())
        (sums,) = reduce_rows((near_part, far_part))
        body = functools.partial(norm_back_one_kernel, gain_row(l, 0))
        if l > 0:
            masked = ()
            body = lambda *refs, body=body: body(*refs[:7], None, *refs[7:])
        else:
            masked = (mask,)
        upstream, upstream_b, sums_one = kernel_call(
            body,
            [row_f32, row_bf16, ((2, width), f32)],
            *sums,
            Far(attn[1][5]),
            Far(grad_middle) if l + 1 < depth else grad_middle,
            vecs,
            *masked,
            name="norm_back_one",
            scratch=[pltpu.VMEM((rows, width), f32)] * 2 + [DMA((2,))],
        )
        lines = ()
        if l == 0:
            terms = [sums_two, *unit_sums[0]]
            for k in range(1, depth):
                terms += [*row_sums[k], *unit_sums[k], head_sums[k]]
            packed = kernel_call(
                functools.partial(vector_pack_kernel, depth),
                [((6 * depth + 2, width), f32)],
                sums_one,
                *grad_q,
                grad_v,
                *[Far(v) for v in terms],
                name="vector_pack",
                scratch=[pltpu.VMEM(v.shape, f32) for v in terms] + [DMA((len(terms),))],
            )[0]
            if outer > 1:
                packed = lax.psum(packed, "ctx", axis_index_groups=outer_groups)
            lines = kernel_call(
                functools.partial(vector_lines_kernel, depth, width_own),
                [((fsdp, 32, 2 * width_own), bf16)],
                packed,
                name="vector_lines",
            )
        count = 1 if l > 0 else fsdp
        shapes = [((width, 3 * feats), bf16), ((width, feats), bf16)]
        if l == 0:
            shapes = [((fsdp, width_own + 32, 4 * feats), bf16)]
        kept = [sums_one, upstream] + ([sums_two] if l + 1 == depth else [])
        *attn_grads, head_sums[l], upstream_b, sums_one, upstream, sums_kept = [
            *kernel_call(
                functools.partial(attn_grad_kernel, feats, count, len(kept)),
                [saved((width if l > 0 else width_own + 32, 4 * feats), bf16)] * count
                + [saved((2, feats), f32), row_bf16]
                + [saved(k.shape, k.dtype) for k in kept],
                attn[0][3],
                attn[1][3],
                attn[0][1],
                attn[1][1],
                *middle_x,
                *grad_q,
                grad_k,
                grad_v,
                upstream_b,
                *(lines or (sums_one,)),
                *kept,
                name="attn_grad",
                scratch=[
                    pltpu.VMEM((all_rows, 3 * feats), bf16),
                    pltpu.VMEM((2, feats), f32),
                ]
                + [pltpu.VMEM(*shape) for shape in shapes]
                + [DMA((count + 2 + len(kept),))],
            ),
            sums_two,
        ][: count + 5]
        if l + 1 == depth:
            sums_two = sums_kept
        if l > 0:
            attn_parts[l] = scatter_grads(attn_grads[0])
            (upstream_b,) = settle(upstream_b, mlp_parts[l])
            upstream_chunks = gather_rows(upstream_b)
        row_sums[l] = (sums_one, sums_two)

    sources = [mlp_parts[0]]
    for l in range(1, depth):
        sources += [mlp_parts[l], attn_parts[l]]
    blocks = 3 * depth - 1
    (stacked,) = kernel_call(
        functools.partial(fetch_kernel, len(sources)),
        [((blocks * width_own, hidden), bf16)],
        *[Far(v) for v in sources],
        name="fetch",
        after=(upstream_b,),
        scratch=[DMA((blocks,))],
    )
    own_term, *other_terms = attn_grads
    other_terms = [shift_z(term, d + 1) for d, term in enumerate(other_terms)]
    crossed = swap_x(stacked)
    others = (swap_y(upstream), swap_y(outputs_own))
    part, mine, pair = kernel_call(
        functools.partial(shard_sum_kernel, depth),
        [
            ((width_own, 4 * feats), bf16),
            ((24, width_own), f32),
            ((2 * blocks * width_own, hidden), bf16),
        ],
        Far(own_term),
        stacked,
        crossed,
        *other_terms,
        name="shard_sum",
        after=others,
        scratch=[pltpu.VMEM(own_term.shape, bf16), DMA((3,))],
    )
    if outer > 1:
        part = lax.psum(part, "ctx", axis_index_groups=outer_groups)
    mine, last_pair = kernel_call(
        functools.partial(vector_plane_kernel, depth),
        [((32, width_own), f32), ((2 * width_own, 4 * feats), bf16)],
        mine,
        swap_xy(mine),
        swap_x(mine),
        swap_y(mine),
        part,
        swap_x(part),
        name="vector_plane",
    )
    pieces = [last_pair, swap_core(last_pair), pair, swap_core(pair)]
    grad_gains, grad_shifts, grad_fc1_bias, grad_qv_bias = kernel_call(
        functools.partial(vector_place_kernel, depth, head_dim),
        [
            (norm_gains.shape, f32),
            (shifts.shape, f32),
            (fc1_bias.shape, f32),
            (qv_bias.shape, f32),
        ],
        mine,
        swap_core(mine),
        name="vector_place",
    )
    grad_inputs, outputs = (
        kernel_call(
            place_rows_kernel,
            [saved(inputs.shape, f32)],
            own,
            other,
            name="place_rows",
            scratch=[DMA((2,))],
        )[0]
        for own, other in zip((upstream, outputs_own), others)
    )
    placed = kernel_call(
        functools.partial(place_kernel, depth, hidden, feats),
        [saved(v.shape, f32) for v in (w_qkv, w_out, w_fc1, w_fc2)],
        *pieces,
        name="place",
        limit=24,
        scratch=[
            pltpu.VMEM((depth, GROUP, width_own, hidden), f32),
            pltpu.VMEM((depth, GROUP, hidden, width_own), f32),
            pltpu.VMEM((depth, GROUP, 3, width_own, feats), f32),
            pltpu.VMEM((depth, GROUP, feats, width_own), f32),
            DMA((16 * depth,)),
        ],
    )
    return (
        outputs,
        grad_inputs,
        grad_gains,
        grad_shifts,
        grad_qv_bias,
        grad_fc1_bias,
        *placed,
    )


def solution(mesh):
    rows = P("fsdp", "ctx", None)
    params = (
        P(None, None, "fsdp"),
        P(None, None, "fsdp"),
        P(None, None, "tp", "fsdp"),
        P(None, "tp", "fsdp"),
        P(None, None, "fsdp", "tp"),
        P(None, "tp", "fsdp"),
        P(None, "fsdp", "tp"),
        P(None, "tp", "fsdp"),
    )
    return jax.shard_map(
        per_device,
        mesh=mesh,
        in_specs=(rows, P("fsdp", None), rows) + params,
        out_specs=(rows, rows) + params,
        check_vma=False,
    )
```

```python
import functools
import math

import jax
import jax.numpy as jnp
from jax import lax
from jax.experimental import pallas as pl
from jax.experimental.pallas import tpu as pltpu
from jax.sharding import PartitionSpec as P

NORM_EPSILON = 1e-06
MASK_FILL = -1e30
ROOT_HALF = 0.7071067811865476
INV_ROOT_TAU = 0.3989422804014327
GROUP = 4
ORDER = (0, 5, 4, 1, 2, 7, 6, 3)
CHIPS = 4

bf16 = jnp.bfloat16
f32 = jnp.float32
VMEM = pl.BlockSpec(memory_space=pltpu.VMEM)
SMEM = pl.BlockSpec(memory_space=pltpu.SMEM)
HBM = pl.BlockSpec(memory_space=pltpu.HBM)
DMA = pltpu.SemaphoreType.DMA
TOKEN = ((8, 128), f32)


def dot(a, b):
    return lax.dot_general(a, b, (((1,), (0,)), ((), ())), preferred_element_type=f32)


def dot_nt(a, b):
    return lax.dot_general(a, b, (((1,), (1,)), ((), ())), preferred_element_type=f32)


def dot_tn(a, b):
    return lax.dot_general(a, b, (((0,), (0,)), ((), ())), preferred_element_type=f32)


class Far:
    def __init__(self, value):
        self.value = value


class Scalars:
    def __init__(self, value):
        self.value = value


def saved(shape, dtype):
    return pltpu.HBM(shape, dtype)


def kernel_call(body, outs, *args, name, limit=12, scratch=(), after=(), aliases=None, us=0):
    values, specs = [], []
    for arg in (*args, *after):
        if isinstance(arg, Far):
            values.append(pltpu.with_memory_space_constraint(arg.value, pltpu.HBM))
            specs.append(HBM)
        elif isinstance(arg, Scalars):
            values.append(arg.value)
            specs.append(SMEM)
        else:
            values.append(arg)
            specs.append(VMEM)
    first, last = len(args), len(args) + len(after)

    def run(*refs):
        body(*refs[:first], *refs[last:])

    out_shape, out_specs = [], []
    for out in outs:
        if isinstance(out, tuple):
            out_shape.append(jax.ShapeDtypeStruct(*out))
            out_specs.append(VMEM)
        else:
            out_shape.append(out)
            out_specs.append(HBM)
    return pl.pallas_call(
        run,
        out_shape=out_shape,
        in_specs=specs,
        out_specs=out_specs,
        scratch_shapes=list(scratch),
        input_output_aliases=aliases or {},
        compiler_params=pltpu.CompilerParams(vmem_limit_bytes=limit << 20),
        cost_estimate=pl.CostEstimate(flops=us * 10**9, bytes_accessed=0, transcendentals=0),
        name=name,
    )(*values)


def start_copies(pairs, sems):
    copies = [
        pltpu.make_async_copy(source, target, sems.at[k])
        for k, (source, target) in enumerate(pairs)
    ]
    for copy in copies:
        copy.start()
    return copies


def row_mean(value):
    return jnp.mean(value, axis=-1, keepdims=True)


def normalize(values):
    center = values - row_mean(values)
    inverse = lax.rsqrt(row_mean(center * center) + NORM_EPSILON)
    return center * inverse, inverse


def lanes_of(head, head_dim, width):
    lane = lax.broadcasted_iota(jnp.int32, (1, width), 1)
    return (lane >= head * head_dim) & (lane < (head + 1) * head_dim)


def assemble(chunks, target):
    rows = chunks[0].shape[0]
    for k, chunk in enumerate(chunks):
        target[k * rows : (k + 1) * rows, :] = chunk[...]


def only(flag, value):
    return jnp.where(flag, value, jnp.zeros_like(value))


def shards(weights):
    if len(weights) == 1:
        rows = weights[0].shape[0]
        return [(pl.ds(0, rows), weights[0])]
    count = len(weights)
    rows = weights[0].shape[0]
    f = lax.axis_index("fsdp")
    found = []
    for d, ref in enumerate(weights):
        place = lax.rem(f + (count - d), count)
        found.append((pl.ds(pl.multiple_of(place * rows, rows), rows), ref))
    return found


def pack_attn_kernel(layer, feats, qkv_hbm, out_hbm, packed_ref, token, qkv, out, sems):
    ci = lax.rem(lax.axis_index("ctx"), GROUP)
    span = pl.ds(pl.multiple_of(ci * feats, feats), feats)
    copies = start_copies(
        [(qkv_hbm.at[layer, :, :, span], qkv), (out_hbm.at[layer, span, :], out)], sems
    )
    copies[0].wait()
    for k in range(3):
        packed_ref[:, k * feats : (k + 1) * feats] = qkv[k]
    copies[1].wait()
    packed_ref[:, 3 * feats :] = out[...].T
    token[...] = jnp.zeros_like(token)


def pack_mlp_kernel(layer, hidden, fc1_hbm, fc2_hbm, packed_ref, token, fc1, fc2, sems):
    ci = lax.rem(lax.axis_index("ctx"), GROUP)
    span = pl.ds(pl.multiple_of(ci * hidden, hidden), hidden)
    copies = start_copies(
        [(fc1_hbm.at[layer, :, span], fc1), (fc2_hbm.at[layer, span, :], fc2)], sems
    )
    copies[0].wait()
    packed_ref[:, :hidden] = fc1[...]
    copies[1].wait()
    packed_ref[:, hidden:] = fc2[...].T
    token[...] = jnp.zeros_like(token)


def prep_upstream_kernel(tp, outer, lengths, cotangent_hbm,
                         upstream_hbm, upstream_b_ref, usable_ref, mask_ref,
                         rows_in, upstream_ref, sems):
    rows = rows_in.shape[0]
    c = lax.axis_index("ctx")
    t = lax.axis_index("tp")
    place = lax.rem(c, GROUP) * tp + t
    start = pl.multiple_of(t * rows, rows)
    copies = start_copies(
        [(cotangent_hbm.at[0, pl.ds(start, rows), :], rows_in)], sems.at[pl.ds(0, 1)]
    )
    lane = lax.broadcasted_iota(jnp.int32, usable_ref.shape, 1)
    limit = jnp.zeros(usable_ref.shape, jnp.int32)
    for o in range(outer):
        for k, d in enumerate(ORDER):
            source = place ^ d
            first_lane = (o * len(ORDER) + k) * rows
            count = lengths[0, o * GROUP + lax.div(source, tp)] - lax.rem(source, tp) * rows
            limit = jnp.where(lane >= first_lane, first_lane + jnp.clip(count, 0, rows), limit)
    usable_ref[...] = jnp.where(lane < limit, 1.0, 0.0)
    row = lax.broadcasted_iota(jnp.int32, mask_ref.shape, 0)
    mask = jnp.where(row + start < lengths[0, c], 1.0, 0.0)
    mask_ref[...] = mask
    copies[0].wait()
    upstream = rows_in[...] * mask[:, 0:1]
    upstream_ref[...] = upstream
    sent = start_copies([(upstream_ref, upstream_hbm)], sems.at[pl.ds(1, 1)])
    upstream_b_ref[...] = upstream.astype(bf16)
    sent[0].wait()


def prep_first_kernel(depth, inputs_hbm, vecs, stream_ref, first_ref, sems):
    rows = stream_ref.shape[0]
    start = pl.multiple_of(lax.axis_index("tp") * rows, rows)
    copies = start_copies([(inputs_hbm.at[0, pl.ds(start, rows), :], stream_ref)], sems)
    copies[0].wait()
    normed, _ = normalize(stream_ref[...])
    shift = vecs[2 * depth : 2 * depth + 1, :]
    first_ref[...] = (normed * vecs[0:1, :] + shift).astype(bf16)


def keep_rows_kernel(*refs):
    chunks, (near_hbm, far_hbm, token, near, far, sems) = refs[:8], refs[8:]
    assemble(chunks[:4], near)
    assemble(chunks[4:], far)
    for copy in start_copies([(near, near_hbm), (far, far_hbm)], sems):
        copy.wait()
    token[...] = jnp.zeros_like(token)


def qkv_kernel(feats, weight_count, *refs):
    c0, c1, c2, c3, *rest = refs
    weights = rest[:weight_count]
    bias, qkv_ref, x = rest[weight_count:]
    assemble((c0, c1, c2, c3), x)
    qkv = sum(dot(x[:, span], w[:, : 3 * feats]) for span, w in shards(weights))
    qkv_ref[:, :feats] = (qkv[:, :feats] + bias[0:1, :]).astype(bf16)
    qkv_ref[:, feats : 2 * feats] = qkv[:, feats : 2 * feats].astype(bf16)
    qkv_ref[:, 2 * feats :] = (qkv[:, 2 * feats :] + bias[1:2, :]).astype(bf16)


def attn_kernel(feats, heads, weight_count, part_count, keep_count, tile, *refs):
    q_ref, *rest = refs
    parts = rest[:part_count]
    weights = rest[part_count : part_count + weight_count]
    rest = rest[part_count + weight_count :]
    usable, *rest = rest
    kept, rest = rest[:keep_count], rest[keep_count:]
    partial_ref, attended_hbm, norm_hbm, *rest = rest
    kept_hbm, rest = rest[:keep_count], rest[keep_count:]
    keys, values, attended_ref, norm_ref, sems = rest
    head_dim = feats // heads
    scale = 1.0 / math.sqrt(head_dim)
    copies = start_copies(list(zip(kept, kept_hbm)), sems)
    first = 0
    for part in parts:
        rows, width = part.shape
        keys[first : first + rows, :] = part[:, width - 2 * feats : width - feats]
        values[first : first + rows, :] = part[:, width - feats :]
        first += rows
    keep = usable[...] > 0.5
    rows = q_ref.shape[0]
    for first in range(0, rows, tile):
        span = slice(first, first + tile)
        q = q_ref[span, :feats]
        attended = None
        for h in range(heads):
            own = lanes_of(h, head_dim, feats)
            scores = dot_nt(only(own, q), keys[...]) * scale
            scores = jnp.where(keep, scores, MASK_FILL)
            highest = jnp.max(scores, axis=-1, keepdims=True)
            raised = jnp.exp(scores - highest)
            total = jnp.sum(raised, axis=-1, keepdims=True)
            soft = (raised * (1.0 / total)).astype(bf16)
            result = dot(soft, values[...])
            log_norm = jnp.broadcast_to(highest + jnp.log(total), (tile, feats))
            if attended is None:
                attended, norms = result, log_norm
            else:
                attended = jnp.where(own, result, attended)
                norms = jnp.where(own, log_norm, norms)
        attended_ref[span, :] = attended.astype(bf16)
        norm_ref[span, :] = norms
    copies += start_copies(
        [(attended_ref, attended_hbm), (norm_ref, norm_hbm)],
        sems.at[pl.ds(keep_count, 2)],
    )
    for span, w in shards(weights):
        partial_ref[:, span] = dot_nt(attended_ref[...], w[:, 3 * feats :]).astype(bf16)
    for copy in copies:
        copy.wait()


def core_sum_kernel(count, *refs):
    pairs, owns = refs[: 2 * count], refs[2 * count : 3 * count]
    peers = refs[3 * count :]
    rows = owns[0].shape[0]
    for j in range(count):
        near, far = pairs[2 * j], pairs[2 * j + 1]
        for k in range(1 + len(peers)):
            span = slice(k * rows, (k + 1) * rows)
            total = near[span, :].astype(f32) + far[span, :].astype(f32)
            if k == 0:
                owns[j][...] = total
            else:
                peers[k - 1][j * rows : (j + 1) * rows, :] = total.astype(bf16)


def total_of(own, xy, x, y, part=0):
    rows = own.shape[0]
    span = slice(part * rows, (part + 1) * rows)
    return (
        own[...] + y[span, :].astype(f32) + x[span, :].astype(f32) + xy[span, :].astype(f32)
    )


def sum_norm_kernel(bias_row, gain_row, shift_row, own, xy, x, y, residual_hbm, vecs,
                    stream_ref, normed_ref, residual, sems):
    copies = start_copies([(residual_hbm, residual)], sems)
    total = total_of(own, xy, x, y) + vecs[bias_row : bias_row + 1, :]
    copies[0].wait()
    stream = residual[...] + total
    stream_ref[...] = stream
    normed, _ = normalize(stream)
    gain = vecs[gain_row : gain_row + 1, :]
    normed_ref[...] = (normed * gain + vecs[shift_row : shift_row + 1, :]).astype(bf16)


def sum_out_kernel(bias_row, own, xy, x, y, residual_hbm, vecs, mask, out_hbm, token,
                   residual, out_ref, sems):
    copies = start_copies([(residual_hbm, residual)], sems.at[pl.ds(0, 1)])
    total = total_of(own, xy, x, y, 1) + vecs[bias_row : bias_row + 1, :]
    copies[0].wait()
    out_ref[...] = (residual[...] + total) * mask[:, 0:1]
    token[...] = jnp.zeros_like(token)
    for copy in start_copies([(out_ref, out_hbm)], sems.at[pl.ds(1, 1)]):
        copy.wait()


def mlp_kernel(hidden, keep_count, saves, load_count, c0, c1, c2, c3, w, bias, *refs):
    kept, rest = refs[:keep_count], refs[keep_count:]
    sources, rest = rest[: max(0, load_count - 1)], rest[max(0, load_count - 1) :]
    partial_ref, x_out, act_out, slope_out, *rest = rest
    kept_hbm, rest = rest[:keep_count], rest[keep_count:]
    loaded = []
    if load_count:
        w_ref, *targets = rest[:load_count]
        *rest, load_sems = rest[load_count:]
        spans = (pl.ds(0, hidden), pl.ds(hidden, hidden))
        loaded = start_copies(
            [(w.at[:, c], w_ref.at[:, c]) for c in spans] + list(zip(sources, targets)), load_sems
        )
        w = w_ref
    if saves:
        x, act_ref, slope_ref, sems = rest
    else:
        x, act_ref, slope_ref = x_out, act_out, slope_out
        (sems,) = rest
    copies = start_copies(list(zip(kept, kept_hbm)), sems)
    assemble((c0, c1, c2, c3), x)
    if saves:
        copies += start_copies([(x, x_out)], sems.at[pl.ds(keep_count, 1)])
    block = hidden // 2
    if load_count:
        loaded[0].wait()
    for k in range(2):
        span = slice(k * block, (k + 1) * block)
        pre = dot(x[...], w[:, span]) + bias[:, span]
        cdf = 0.5 * (1.0 + lax.erf(pre * ROOT_HALF))
        density = jnp.exp(-0.5 * pre * pre) * INV_ROOT_TAU
        slope_ref[k] = cdf + pre * density
        act_ref[:, span] = (pre * cdf).astype(bf16)
        if saves:
            copies += start_copies(
                [(slope_ref.at[k], slope_out.at[k])], sems.at[pl.ds(1 + keep_count + k, 1)]
            )
    if saves:
        copies += start_copies([(act_ref, act_out)], sems.at[pl.ds(3 + keep_count, 1)])
    if load_count:
        loaded[1].wait()
    partial_ref[...] = dot_nt(act_ref[...], w[:, hidden:]).astype(bf16)
    for copy in copies + loaded[2:]:
        copy.wait()


def mlp_back_kernel(hidden, chunk_count, *refs):
    chunks, (w, slope, *rest) = refs[:chunk_count], refs[chunk_count:]
    partial_ref, grad_ref, sum_hbm, x, sum_ref, sems = rest
    assemble(chunks, x)
    grad = dot(x[...], w[:, hidden:])
    block = hidden // 2
    for k in range(2):
        span = slice(k * block, (k + 1) * block)
        part = grad[:, span] * slope[k]
        grad_ref[:, span] = part.astype(bf16)
        sum_ref[:, span] = jnp.sum(part, axis=0, keepdims=True)
    sent = start_copies([(sum_ref, sum_hbm)], sems)
    partial_ref[...] = dot_nt(grad_ref[...], w[:, :hidden]).astype(bf16)
    sent[0].wait()


def mlp_grad_kernel(hidden, keep_count, second_near, second_far, act_near, act_far,
                    up_near, up_far, grad_near, grad_far, passed, *refs):
    kept, refs = refs[:keep_count], refs[keep_count:]
    out_hbm, passed_ref, *refs = refs
    kept_hbm, (out_one, out_two, sems) = refs[:keep_count], refs[keep_count:]
    sent = start_copies(list(zip(kept, kept_hbm)), sems.at[pl.ds(2, keep_count)]) if kept else []
    passed_ref[...] = passed[...]
    total = dot_tn(up_near[...], act_near[...]) + dot_tn(up_far[...], act_far[...])
    out_two[...] = total.astype(bf16)
    sent += start_copies(
        [(out_two, out_hbm.at[:, pl.ds(hidden, hidden)])], sems.at[pl.ds(0, 1)]
    )
    total = dot_tn(second_near[...], grad_near[...]) + dot_tn(second_far[...], grad_far[...])
    out_one[...] = total.astype(bf16)
    sent += start_copies([(out_one, out_hbm.at[:, pl.ds(0, hidden)])], sems.at[pl.ds(1, 1)])
    for copy in sent:
        copy.wait()


def norm_back(upstream, values, gain):
    normed, inverse = normalize(values)
    scaled = upstream * gain
    back = inverse * (scaled - row_mean(scaled) - normed * row_mean(scaled * normed))
    gain_grad = jnp.sum(upstream * normed, axis=0, keepdims=True)
    return back, gain_grad, jnp.sum(upstream, axis=0, keepdims=True)


def norm_back_two_kernel(gain_row, own, xy, x, y, values_hbm, upstream_hbm, vecs,
                         grad_ref, grad_b_ref, sums_ref, values, upstream, sems):
    copies = start_copies([(values_hbm, values), (upstream_hbm, upstream)], sems)
    total = total_of(own, xy, x, y)
    for copy in copies:
        copy.wait()
    up = upstream[...]
    back, gain_grad, shift_grad = norm_back(
        total, values[...], vecs[gain_row : gain_row + 1, :]
    )
    grad = up + back
    grad_ref[...] = grad
    grad_b_ref[...] = grad.astype(bf16)
    sums_ref[0:1, :] = gain_grad
    sums_ref[1:2, :] = shift_grad
    sums_ref[2:3, :] = jnp.sum(grad, axis=0, keepdims=True)
    sums_ref[3:4, :] = jnp.sum(up, axis=0, keepdims=True)


def norm_back_one_kernel(gain_row, own, xy, x, y, values_hbm, upstream_hbm, vecs, mask,
                         grad_ref, grad_b_ref, sums_ref, values, upstream, sems):
    copies = start_copies([(values_hbm, values), (upstream_hbm, upstream)], sems)
    total = total_of(own, xy, x, y)
    for copy in copies:
        copy.wait()
    back, gain_grad, shift_grad = norm_back(
        total, values[...], vecs[gain_row : gain_row + 1, :]
    )
    grad = upstream[...] + back
    if mask is not None:
        grad = grad * mask[:, 0:1]
    grad_ref[...] = grad
    grad_b_ref[...] = grad.astype(bf16)
    sums_ref[0:1, :] = gain_grad
    sums_ref[1:2, :] = shift_grad


def attn_back_kernel(feats, heads, weight_count, part_count, tile, carried, *refs):
    c0, c1, c2, c3, *rest = refs
    weights, rest = rest[:weight_count], rest[weight_count:]
    usable, qkv, attended, norms, *rest = rest
    parts, rest = rest[:part_count], rest[part_count:]
    if carried:
        keys_before, values_before, *rest = rest
    x, grad_q, grad_k, grad_v, pairs, grad_att = rest
    head_dim = feats // heads
    scale = 1.0 / math.sqrt(head_dim)
    first = 0
    for part in parts:
        rows, width = part.shape
        pairs[first : first + rows, :] = part[:, width - 2 * feats :]
        first += rows
    assemble((c0, c1, c2, c3), x)
    grad_att[...] = sum(
        dot(x[:, span], w[:, 3 * feats :]) for span, w in shards(weights)
    ).astype(bf16)
    keep = usable[...] > 0.5
    rows = qkv.shape[0]
    if carried:
        sum_k, sum_v = keys_before[...], values_before[...]
    else:
        sum_k = jnp.zeros(grad_k.shape, f32)
        sum_v = jnp.zeros(grad_v.shape, f32)
    keys, values = pairs[:, :feats], pairs[:, feats:]
    for first in range(0, rows, tile):
        span = slice(first, first + tile)
        q = qkv[span, :feats]
        ga = grad_att[span, :]
        products = ga.astype(f32) * attended[span, :].astype(f32)
        gq = None
        for h in range(heads):
            own = lanes_of(h, head_dim, feats)
            q_h = only(own, q)
            ga_h = only(own, ga)
            row_dots = jnp.sum(only(own, products), axis=-1, keepdims=True)
            scores = dot_nt(q_h, keys) * scale
            scores = jnp.where(keep, scores, MASK_FILL)
            soft = jnp.exp(scores - norms[span, h * head_dim : h * head_dim + 1])
            grad_soft = dot_nt(ga_h, values)
            grad_scores = (soft * (grad_soft - row_dots)).astype(bf16)
            part = dot(grad_scores, keys)
            gq = part if gq is None else jnp.where(own, part, gq)
            sum_k = sum_k + dot_tn(grad_scores, q_h) * scale
            sum_v = sum_v + dot_tn(soft.astype(bf16), ga_h)
        grad_q[span, :] = gq * scale
    grad_k[...] = sum_k
    grad_v[...] = sum_v


def project_kernel(feats, first, weight_count, gq, gk, gv, *refs):
    weights, (partial_ref, packed) = refs[:weight_count], refs[weight_count:]
    rows = gq.shape[0]
    span = slice(first, first + rows)
    packed[:, :feats] = gq[...].astype(bf16)
    packed[:, feats : 2 * feats] = gk[span, :].astype(bf16)
    packed[:, 2 * feats :] = gv[span, :].astype(bf16)
    for columns, w in shards(weights):
        partial_ref[:, columns] = dot_nt(packed[...], w[:, : 3 * feats]).astype(bf16)


def attn_grad_kernel(feats, count, keep_count, first_near, first_far, att_near, att_far,
                     up_near, up_far, gq_near, gq_far, gk, gv, passed, lines, *refs):
    kept, refs = refs[:keep_count], refs[keep_count:]
    outs, refs = refs[:count], refs[count:]
    heads_hbm, passed_ref, *refs = refs
    kept_hbm, (packed, sums_ref, *staged, sems) = refs[:keep_count], refs[keep_count:]
    rows = up_near.shape[0]
    used = count + 2
    sent = start_copies(list(zip(kept, kept_hbm)), sems.at[pl.ds(used, keep_count)])
    passed_ref[...] = passed[...]
    packed[:rows, :feats] = gq_near[...].astype(bf16)
    packed[rows:, :feats] = gq_far[...].astype(bf16)
    packed[:, feats : 2 * feats] = gk[...].astype(bf16)
    packed[:, 2 * feats :] = gv[...].astype(bf16)
    sums_ref[0:1, :] = jnp.sum(gq_near[...], axis=0, keepdims=True) + jnp.sum(
        gq_far[...], axis=0, keepdims=True
    )
    sums_ref[1:2, :] = jnp.sum(gv[...], axis=0, keepdims=True)
    sent += start_copies([(sums_ref, heads_hbm)], sems.at[pl.ds(0, 1)])

    def out_part(span):
        return dot_tn(up_near[:, span], att_near[...]) + dot_tn(up_far[:, span], att_far[...])

    def qkv_part(span):
        return dot_tn(first_near[:, span], packed[:rows, :]) + dot_tn(
            first_far[:, span], packed[rows:, :]
        )

    if count == 1:
        out_one, out_two = staged
        whole = slice(None)
        out_two[...] = out_part(whole).astype(bf16)
        sent += start_copies(
            [(out_two, outs[0].at[:, pl.ds(3 * feats, feats)])], sems.at[pl.ds(1, 1)]
        )
        out_one[...] = qkv_part(whole).astype(bf16)
        sent += start_copies(
            [(out_one, outs[0].at[:, pl.ds(0, 3 * feats)])], sems.at[pl.ds(2, 1)]
        )
    else:
        (stage,) = staged
        below = lines.shape[1]
        width_own = outs[0].shape[0] - below
        for d in reversed(range(count)):
            place = lax.rem(lax.axis_index("fsdp") + d, count)
            span = pl.ds(pl.multiple_of(place * width_own, width_own), width_own)
            stage[d, :width_own, : 3 * feats] = qkv_part(span).astype(bf16)
            stage[d, :width_own, 3 * feats :] = out_part(span).astype(bf16)
            stage[d, width_own:, :] = lines[d]
            sent += start_copies([(stage.at[d], outs[d])], sems.at[pl.ds(1 + d, 1)])
    for copy in sent:
        copy.wait()


def settle_kernel(keep_count, passed, there, through, *refs):
    kept, (passed_ref, _, *kept_hbm, sems) = refs[:keep_count], refs[keep_count:]
    copies = start_copies(list(zip(kept, kept_hbm)), sems)
    passed_ref[...] = passed[...]
    for copy in copies:
        copy.wait()


def fetch_kernel(count, *refs):
    sources, (target, sems) = refs[:count], refs[count:]
    columns = target.shape[1]
    moves = []
    row = 0
    for source in sources:
        rows = source.shape[0]
        for first in range(0, source.shape[1], columns):
            moves.append(
                (source.at[:, pl.ds(first, columns)], target.at[pl.ds(row, rows), :])
            )
            row += rows
    for copy in start_copies(moves, sems):
        copy.wait()


def shard_sum_kernel(depth, stacked, crossed, *refs):
    below, refs = refs[: depth - 1], refs[depth - 1 :]
    *sources, part_ref, mine_ref, pair_ref, found, sems = refs
    count = stacked.shape[0]
    rows, width = part_ref.shape[0] // depth, mine_ref.shape[1]
    loads = start_copies([(v, found.at[k]) for k, v in enumerate(sources)], sems)
    copies = start_copies(
        [
            (stacked, pair_ref.at[pl.ds(0, count), :]),
            (crossed, pair_ref.at[pl.ds(count, count), :]),
        ]
        + [(part, part_ref.at[pl.ds((1 + k) * rows, rows), :]) for k, part in enumerate(below)],
        sems.at[pl.ds(len(sources), 1 + depth)],
    )
    for load in loads:
        load.wait()
    total = found[0].astype(f32)
    for k in range(1, len(sources)):
        total = total + found[k].astype(f32)
    part_ref[:rows, :] = total[:rows, :].astype(bf16)
    lines = total[rows:, :width] + total[rows:, width:]
    mine_ref[: 6 * depth, :] = lines[: 6 * depth, :]
    for k in range(mine_ref.shape[0] - 16):
        mine_ref[16 + k : 17 + k, :] = lines[6 * depth + k : 6 * depth + k + 1, :]
    for copy in copies:
        copy.wait()


def place_kernel(depth, hidden, feats, *refs):
    alone, pairs, rest = refs[:2], refs[2:4], refs[4:]

    def half_of(pair, k):
        count = pair[k % 2].shape[0] // 2
        return pair[k % 2].at[pl.ds(k // 2 * count, count), :]

    slices = [(half_of(alone, k), half_of(pairs, k)) for k in range(GROUP)]
    qkv_hbm, out_hbm, fc1_hbm, fc2_hbm, fc1, fc2, qkv, out, sems = rest
    ci = lax.rem(lax.axis_index("ctx"), GROUP)
    rows = fc1.shape[2]
    copies = []

    def send(source, target):
        copies.extend(start_copies([(source, target)], sems.at[pl.ds(len(copies), 1)]))

    for l in range(depth):
        for k in range(GROUP):
            _, stacked = slices[k]
            first = 2 * l * rows
            span = pl.ds(pl.multiple_of((ci ^ k) * hidden, hidden), hidden)
            fc1[l, k] = stacked[first : first + rows, :].astype(f32)
            send(fc1.at[l, k], fc1_hbm.at[l, :, span])
            fc2[l, k] = stacked[first + rows : first + 2 * rows, :].T.astype(f32)
            send(fc2.at[l, k], fc2_hbm.at[l, span, :])
    for l in reversed(range(depth)):
        for k in range(GROUP):
            piece = slices[k][0].at[pl.ds(l * rows, rows), :]
            span = pl.ds(pl.multiple_of((ci ^ k) * feats, feats), feats)
            for j in range(3):
                qkv[l, k, j] = piece[:, j * feats : (j + 1) * feats].astype(f32)
            send(qkv.at[l, k], qkv_hbm.at[l, :, :, span])
            out[l, k] = piece[:, 3 * feats :].T.astype(f32)
            send(out.at[l, k], out_hbm.at[l, span, :])
    for copy in copies:
        copy.wait()


def vector_pack_kernel(depth, one_now, gq_near, gq_far, gv, *refs):
    count = 5 * depth - 2
    out_ref, *found, sems = refs[count:]
    copies = start_copies(list(zip(refs[:count], found)), sems)
    out_ref[...] = jnp.zeros_like(out_ref)
    feats = gv.shape[1]
    head_now = [
        jnp.sum(gq_near[...], axis=0, keepdims=True) + jnp.sum(gq_far[...], axis=0, keepdims=True),
        jnp.sum(gv[...], axis=0, keepdims=True),
    ]
    for copy in copies:
        copy.wait()
    for l in range(depth):
        if l == 0:
            one, (two, unit_near, unit_far) = one_now, found[:3]
            heads = head_now
        else:
            one, two, unit_near, unit_far, head = found[5 * l - 2 : 5 * l + 3]
            heads = [head[0:1, :], head[1:2, :]]
        out_ref[6 * l : 6 * l + 1, :] = one[0:1, :]
        out_ref[6 * l + 1 : 6 * l + 2, :] = two[0:1, :]
        out_ref[6 * l + 2 : 6 * l + 3, :] = one[1:2, :]
        out_ref[6 * l + 3 : 6 * l + 6, :] = two[1:4, :]
        units = unit_near.shape[1]
        row = 6 * depth
        out_ref[row : row + 1, l * units : (l + 1) * units] = unit_near[...] + unit_far[...]
        for j in range(2):
            start = (2 * l + j) * feats
            out_ref[row + 1 : row + 2, start : start + feats] = heads[j]


def vector_lines_kernel(depth, width_own, packed, lines_ref):
    count = lines_ref.shape[0]
    f = lax.axis_index("fsdp")
    total = packed[...]
    high = total.astype(bf16).astype(f32)
    low = total - high
    lines_ref[...] = jnp.zeros_like(lines_ref)
    last = 6 * depth
    for k, value in enumerate((high, low)):
        lanes = slice(k * width_own, (k + 1) * width_own)
        columns = [value[:, a * width_own : (a + 1) * width_own] for a in range(count)]
        for d in range(count):
            mine = columns[0]
            for a in range(1, count):
                mine = jnp.where(lax.rem(f + d, count) == a, columns[a], mine)
            rows = [mine[:last, :]]
            for r in range(2):
                for a in range(count):
                    rows.append(columns[a][last + r : last + r + 1, :])
            rows.append(jnp.zeros((lines_ref.shape[1] - last - 2 * count, width_own), f32))
            lines_ref[d, :, lanes] = jnp.concatenate(rows, axis=0).astype(bf16)


def vector_plane_kernel(depth, own, xy, x, y, part, part_x, out_ref, pair_ref):
    last = 6 * depth
    rows = part.shape[0]
    pair_ref[:rows, :] = part[...]
    pair_ref[rows:, :] = part_x[...]
    out_ref[:last, :] = own[:last, :] + xy[:last, :] + x[:last, :] + y[:last, :]
    out_ref[16:24, :] = own[16:24, :]
    out_ref[24:32, :] = x[16:24, :]


def vector_place_kernel(depth, head_dim, own, far, gains_ref, shifts_ref, unit_ref, heads_ref):
    total = own[: 6 * depth, :] + far[: 6 * depth, :]
    for l in range(depth):
        gains_ref[l] = total[6 * l : 6 * l + 2, :]
        shifts_ref[l] = total[6 * l + 2 : 6 * l + 6, :]
    pieces = (own[16:24, :], far[16:24, :], own[24:32, :], far[24:32, :])
    ci = lax.rem(lax.axis_index("ctx"), GROUP)
    f = lax.axis_index("fsdp")

    def of_place(c):
        k = ci ^ c
        found = pieces[0]
        for j in range(1, GROUP):
            found = jnp.where(k == j, pieces[j], found)
        return found

    width_own = own.shape[1]
    units = of_place(f)
    parts = unit_ref.shape[2] // width_own
    for l in range(depth):
        for j in range(parts):
            row = l * parts + j
            unit_ref[l, :, j * width_own : (j + 1) * width_own] = units[row : row + 1, :]
    head_own = heads_ref.shape[3]
    heads = heads_ref.shape[2] // GROUP
    for c in range(GROUP):
        found = of_place(c)
        for l in range(depth):
            for j in range(2):
                for h in range(heads):
                    first = ((2 * l + j) * heads + h) * head_dim
                    row, lane = 4 + first // width_own, first % width_own
                    value = found[row : row + 1, lane : lane + head_own]
                    for a in range(1, head_dim // head_own):
                        start = lane + a * head_own
                        value = jnp.where(
                            f == a, found[row : row + 1, start : start + head_own], value
                        )
                    heads_ref[l, j, c * heads + h : c * heads + h + 1, :] = value


def place_rows_kernel(own, other, out_hbm, sems):
    rows = own.shape[0]
    start = pl.multiple_of(lax.axis_index("tp") * rows, rows)
    copies = start_copies(
        [
            (own, out_hbm.at[0, pl.ds(start, rows), :]),
            (other, out_hbm.at[0, pl.ds(pl.multiple_of(rows - start, rows), rows), :]),
        ],
        sems,
    )
    for copy in copies:
        copy.wait()


def per_device(
    inputs, lengths, cotangent, norm_gains, shifts, qv_bias, fc1_bias, w_qkv, w_out, w_fc1, w_fc2
):
    depth = w_qkv.shape[0]
    width_own = w_qkv.shape[2]
    fsdp = lax.axis_size("fsdp")
    tp = lax.axis_size("tp")
    ctx = lax.axis_size("ctx")
    outer = ctx // GROUP
    rows = inputs.shape[1] // tp
    half = rows * CHIPS
    all_rows = 2 * half
    head_own = qv_bias.shape[3]
    head_dim = head_own * fsdp
    heads = qv_bias.shape[2] // GROUP
    feats = heads * head_dim
    hidden = w_fc1.shape[2] // GROUP
    width = width_own * fsdp
    t = lax.axis_index("tp")
    f = lax.axis_index("fsdp")
    ci = lax.axis_index("ctx") % GROUP
    tile = half // 2
    attn_limit = 12 if outer == 1 else 48

    def swap_core(value):
        return lax.ppermute(value, "ctx", [(i, i ^ 1) for i in range(ctx)])

    def swap_x(value):
        return lax.ppermute(value, "ctx", [(i, i ^ 2) for i in range(ctx)])

    def swap_y(value):
        return lax.ppermute(value, "tp", [(i, i ^ 1) for i in range(tp)])

    def swap_xy(value):
        pairs = [
            (i * tp + k, (i ^ 2) * tp + (k ^ 1)) for i in range(ctx) for k in range(tp)
        ]
        return lax.ppermute(value, ("ctx", "tp"), pairs)

    def shift_z(value, d):
        return lax.ppermute(value, "fsdp", [(i, (i + d) % fsdp) for i in range(fsdp)])

    outer_groups = [[o * GROUP + i for o in range(outer)] for i in range(GROUP)]

    def gather_rows(own):
        near = (own, swap_xy(own), swap_x(own), swap_y(own))
        return near, tuple(swap_core(chunk) for chunk in near)

    def settle(value, there, through, *kept):
        return kernel_call(
            functools.partial(settle_kernel, len(kept)),
            [(value.shape, value.dtype), saved(through.shape, through.dtype)]
            + [saved(k.shape, k.dtype) for k in kept],
            value,
            Far(there),
            Far(through),
            *kept,
            name="settle",
            scratch=[DMA((len(kept),))],
            aliases={2: 1},
        )

    def reduce_rows(*pairs, after=()):
        count = len(pairs)
        *owns, xy, x, y = kernel_call(
            functools.partial(core_sum_kernel, count),
            [((rows, width), f32)] * count + [((count * rows, width), bf16)] * 3,
            *[v for near, far in pairs for v in (near, swap_core(far))],
            name="core_sum",
            after=after,
        )
        peers = (swap_xy(xy), swap_x(x), swap_y(y))
        return [(own, *peers) for own in owns]

    def pack_attn(l, after):
        return kernel_call(
            functools.partial(pack_attn_kernel, l, feats),
            [((width_own, 4 * feats), bf16), TOKEN],
            Far(w_qkv),
            Far(w_out),
            name="pack_attn",
            after=after,
            scratch=[
                pltpu.VMEM((3, width_own, feats), bf16),
                pltpu.VMEM((feats, width_own), bf16),
                DMA((2,)),
            ],
        )

    def pack_mlp(l, after):
        return kernel_call(
            functools.partial(pack_mlp_kernel, l, hidden),
            [((width_own, 2 * hidden), bf16), TOKEN],
            Far(w_fc1),
            Far(w_fc2),
            name="pack_mlp",
            after=after,
            scratch=[
                pltpu.VMEM((width_own, hidden), bf16),
                pltpu.VMEM((hidden, width_own), bf16),
                DMA((2,)),
            ],
        )

    attn_w = []
    mlp_w = []
    token = None
    for l in range(depth):
        own, token = pack_attn(l, () if token is None else (token,))
        attn_w.append((lax.all_gather(own, "fsdp", axis=0, tiled=True),))
        own, token = pack_mlp(l, (token,))
        mlp_w.append(lax.all_gather(own, "fsdp", axis=0, tiled=True))
        if l == 0:
            pack_token = token

    qv_own = lax.dynamic_slice_in_dim(qv_bias, ci * heads, heads, axis=2)
    vec_rows = depth * 6
    c1_rows = depth * fc1_bias.shape[2] // width_own
    qv_own = qv_own.reshape(1, -1)
    small_own = jnp.concatenate(
        [
            norm_gains.reshape(-1, width_own),
            shifts.reshape(-1, width_own),
            fc1_bias.reshape(-1, width_own),
            jnp.pad(qv_own, ((0, 0), (0, width_own - qv_own.shape[1]))),
        ],
        axis=0,
    )
    shifted = [small_own] + [shift_z(small_own, d) for d in range(1, fsdp)]

    def shard(a):
        picked = shifted[0]
        for d in range(1, fsdp):
            picked = jnp.where((f - d) % fsdp == a, shifted[d], picked)
        return picked.astype(f32)

    small = [shard(a) for a in range(fsdp)]
    vecs = jnp.concatenate([s[:vec_rows] for s in small], axis=1)
    fc1_all = shard(ci)[vec_rows : vec_rows + c1_rows].reshape(depth, 1, hidden)
    qv_all = jnp.stack(
        [s[vec_rows + c1_rows, : qv_own.shape[1]].reshape(depth, 2, heads, head_own) for s in small],
        axis=3,
    ).reshape(depth, 2, feats)

    def gain_row(l, i):
        return 2 * l + i

    def shift_row(l, i):
        return 2 * depth + 4 * l + i

    key_rows = outer * all_rows
    row_f32 = ((rows, width), f32)
    row_bf16 = ((rows, width), bf16)
    upstream, upstream_b, usable, mask = kernel_call(
        functools.partial(prep_upstream_kernel, tp, outer),
        [saved((rows, width), f32), row_bf16, ((1, key_rows), f32), ((rows, 128), f32)],
        Scalars(lengths),
        Far(cotangent),
        name="prep_upstream",
        after=(pack_token,),
        scratch=[pltpu.VMEM((rows, width), f32), pltpu.VMEM((rows, width), f32), DMA((2,))],
    )
    near, far = gather_rows(upstream_b)
    half_x = pltpu.VMEM((half, width), bf16)
    *upstream_rows, upstream_token = kernel_call(
        keep_rows_kernel,
        [saved((half, width), bf16)] * 2 + [TOKEN],
        *near,
        *far,
        name="keep_rows",
        scratch=[half_x, half_x, DMA((2,))],
    )
    stream, first = kernel_call(
        functools.partial(prep_first_kernel, depth),
        [row_f32, row_bf16],
        Far(inputs),
        vecs,
        name="prep_first",
        scratch=[DMA((1,))],
    )
    first_chunks = gather_rows(first)

    partial_out = ((half, width), bf16)
    saved_all = []
    for l in range(depth):
        qkv = []
        first_x = []
        for side in (0, 1):
            qkv_half, x_half = kernel_call(
                functools.partial(qkv_kernel, feats, len(attn_w[l])),
                [((half, 3 * feats), bf16), ((half, width), bf16)],
                *first_chunks[side],
                *attn_w[l],
                qv_all[l],
                name="qkv",
                after=(upstream_token,) if l == 0 and side == 0 else (),
            )
            qkv.append(qkv_half)
            first_x.append(x_half)
        if outer > 1:
            pairs = jnp.concatenate([part[:, feats:] for part in qkv], axis=0)
            pairs = lax.all_gather(
                pairs, "ctx", axis=0, tiled=True, axis_index_groups=outer_groups
            )
            key_parts = (pairs,)
        else:
            key_parts = tuple(qkv)
        attn = [None, None]
        for side in (1, 0):
            kept = (first_x[side], qkv[side]) + ((stream,) if side == 1 else ())
            attn[side] = kernel_call(
                functools.partial(
                    attn_kernel, feats, heads, len(attn_w[l]), len(key_parts), len(kept), tile
                ),
                [partial_out, saved((half, feats), bf16), saved((half, feats), f32)]
                + [saved(k.shape, k.dtype) for k in kept],
                qkv[side],
                *key_parts,
                *attn_w[l],
                usable,
                *kept,
                name="attn",
                limit=attn_limit,
                scratch=[
                    pltpu.VMEM((key_rows, feats), bf16),
                    pltpu.VMEM((key_rows, feats), bf16),
                    pltpu.VMEM((half, feats), bf16),
                    pltpu.VMEM((half, feats), f32),
                    DMA((len(kept) + 2,)),
                ],
            )
        (sums,) = reduce_rows((attn[0][0], attn[1][0]))
        middle, second = kernel_call(
            functools.partial(sum_norm_kernel, shift_row(l, 2), gain_row(l, 1), shift_row(l, 1)),
            [row_f32, row_bf16],
            *sums,
            Far(attn[1][5]),
            vecs,
            name="sum_norm",
            scratch=[pltpu.VMEM((rows, width), f32), DMA((1,))],
        )
        second_chunks = gather_rows(second)
        mlp = [None, None]
        for side in (1, 0):
            kept = (middle,) if side == 1 else ()
            saves = l + 1 < depth
            loads = (mlp_w[l], *upstream_rows) if not saves and side == 1 else ()
            shapes = [
                ((half, width), bf16),
                ((half, hidden), bf16),
                ((2, half, hidden // 2), f32),
            ]
            mlp[side] = kernel_call(
                functools.partial(mlp_kernel, hidden, len(kept), saves, len(loads)),
                [partial_out]
                + [saved(*shape) if saves else shape for shape in shapes]
                + [saved(k.shape, k.dtype) for k in kept]
                + [(v.shape, v.dtype) for v in loads],
                *second_chunks[side],
                Far(mlp_w[l]) if loads else mlp_w[l],
                fc1_all[l],
                *kept,
                *[Far(v) for v in loads[1:]],
                name="mlp",
                scratch=[pltpu.VMEM(*shape) for shape in shapes if saves]
                + [DMA((4 + len(kept),))]
                + [DMA((len(loads) + 1,)) for _ in loads[:1]],
            )
            if loads:
                *mlp[side], mlp_w[l], near, far = mlp[side]
                upstream_chunks = [(near,), (far,)]
        saved_all.append((attn, pairs if outer > 1 else None, mlp))
        if l + 1 < depth:
            (sums,) = reduce_rows((mlp[0][0], mlp[1][0]))
            stream, first = kernel_call(
                functools.partial(
                    sum_norm_kernel, shift_row(l, 3), gain_row(l + 1, 0), shift_row(l + 1, 0)
                ),
                [row_f32, row_bf16],
                *sums,
                Far(mlp[1][4]),
                vecs,
                name="sum_norm",
                scratch=[pltpu.VMEM((rows, width), f32), DMA((1,))],
            )
            first_chunks = gather_rows(first)

    def scatter_grads(grad):
        part = lax.psum_scatter(grad, "fsdp", scatter_dimension=0, tiled=True)
        if outer > 1:
            part = lax.psum(part, "ctx", axis_index_groups=outer_groups)
        return part

    row_sums = [None] * depth
    unit_sums = [None] * depth
    head_sums = [None] * depth
    mlp_parts = [None] * depth
    attn_parts = [None] * depth
    for l in reversed(range(depth)):
        attn, pairs, mlp = saved_all[l]
        back = [None, None]
        for side in (1, 0):
            back[side] = kernel_call(
                functools.partial(mlp_back_kernel, hidden, len(upstream_chunks[side])),
                [
                    partial_out,
                    ((half, hidden), bf16),
                    saved((1, hidden), f32),
                    ((half, width), bf16),
                ],
                *upstream_chunks[side],
                mlp_w[l],
                mlp[side][3],
                name="mlp_back",
                scratch=[pltpu.VMEM((1, hidden), f32), DMA((1,))],
            )
        def weight_grad(passed, *kept):
            return kernel_call(
                functools.partial(mlp_grad_kernel, hidden, len(kept)),
                [saved((width, 2 * hidden), bf16), (passed.shape, passed.dtype)]
                + [saved(k.shape, k.dtype) for k in kept],
                mlp[0][1],
                mlp[1][1],
                mlp[0][2],
                mlp[1][2],
                back[0][3],
                back[1][3],
                back[0][1],
                back[1][1],
                passed,
                *kept,
                name="mlp_grad",
                scratch=[
                    pltpu.VMEM((width, hidden), bf16),
                    pltpu.VMEM((width, hidden), bf16),
                    DMA((2 + len(kept),)),
                ],
            )

        token = ()
        if l + 1 < depth:
            mlp_grad, *token = weight_grad(upstream_b)
            mlp_parts[l] = scatter_grads(mlp_grad)
        pairs_now = [(back[0][0], back[1][0])]
        if l + 1 == depth:
            pairs_now.append((mlp[0][0], mlp[1][0]))
        sums, *output_sums = reduce_rows(*pairs_now, after=token)
        if l + 1 == depth:
            outputs_own, output_token = kernel_call(
                functools.partial(sum_out_kernel, shift_row(l, 3)),
                [saved((rows, width), f32), TOKEN],
                *output_sums[0],
                Far(mlp[1][4]),
                vecs,
                mask,
                name="sum_out",
                scratch=[pltpu.VMEM((rows, width), f32)] * 2 + [DMA((2,))],
            )
            after = (output_token,)
        else:
            after = ()
        unit_sums[l] = (back[0][2], back[1][2])
        grad_middle, middle_b, sums_two = kernel_call(
            functools.partial(norm_back_two_kernel, gain_row(l, 1)),
            [row_f32, row_bf16, ((4, width), f32)],
            *sums,
            Far(mlp[1][4]),
            Far(upstream),
            vecs,
            name="norm_back_two",
            after=after,
            scratch=[pltpu.VMEM((rows, width), f32)] * 2 + [DMA((2,))],
        )
        if l + 1 < depth:
            middle_b, through, sums_two, grad_middle = settle(
                middle_b, mlp_parts[l + 1], attn_later, sums_two, grad_middle
            )
            attn_parts[l + 1] = scatter_grads(through)
        else:
            mlp_grad, middle_b, sums_two, grad_middle = weight_grad(
                middle_b, sums_two, grad_middle
            )
            mlp_parts[l] = scatter_grads(mlp_grad)
        middle_chunks = gather_rows(middle_b)
        grad_q = [None, None]
        middle_x = [None, None]
        carried = ()
        for side in (0, 1):
            key_parts = (pairs,) if outer > 1 else (attn[0][4], attn[1][4])
            middle_x[side], grad_q[side], *carried = kernel_call(
                functools.partial(
                    attn_back_kernel,
                    feats,
                    heads,
                    len(attn_w[l]),
                    len(key_parts),
                    tile,
                    len(carried) > 0,
                ),
                [
                    ((half, width), bf16),
                    ((half, feats), f32),
                    ((key_rows, feats), f32),
                    ((key_rows, feats), f32),
                ],
                *middle_chunks[side],
                *attn_w[l],
                usable,
                attn[side][4],
                attn[side][1],
                attn[side][2],
                *key_parts,
                *carried,
                name="attn_back",
                scratch=[
                    pltpu.VMEM((key_rows, 2 * feats), bf16),
                    pltpu.VMEM((half, feats), bf16),
                ],
                limit=attn_limit,
            )
        grad_k, grad_v = carried
        if outer > 1:
            grad_k, grad_v = (
                lax.psum_scatter(
                    v, "ctx", scatter_dimension=0, tiled=True, axis_index_groups=outer_groups
                )
                for v in (grad_k, grad_v)
            )

        def project(side, after):
            return kernel_call(
                functools.partial(project_kernel, feats, side * half, len(attn_w[l])),
                [partial_out],
                grad_q[side],
                grad_k,
                grad_v,
                *attn_w[l],
                name="project",
                after=after,
                scratch=[pltpu.VMEM((half, 3 * feats), bf16)],
            )[0]

        far_part = project(1, ())
        near_part = project(0, ())
        (sums,) = reduce_rows((near_part, far_part))
        body = functools.partial(norm_back_one_kernel, gain_row(l, 0))
        if l > 0:
            masked = ()
            body = lambda *refs, body=body: body(*refs[:7], None, *refs[7:])
        else:
            masked = (mask,)
        upstream, upstream_b, sums_one = kernel_call(
            body,
            [row_f32, row_bf16, ((2, width), f32)],
            *sums,
            Far(attn[1][5]),
            Far(grad_middle),
            vecs,
            *masked,
            name="norm_back_one",
            scratch=[pltpu.VMEM((rows, width), f32)] * 2 + [DMA((2,))],
        )
        lines = ()
        if l == 0:
            terms = [sums_two, *unit_sums[0]]
            for k in range(1, depth):
                terms += [*row_sums[k], *unit_sums[k], head_sums[k]]
            packed = kernel_call(
                functools.partial(vector_pack_kernel, depth),
                [((6 * depth + 2, width), f32)],
                sums_one,
                *grad_q,
                grad_v,
                *[Far(v) for v in terms],
                name="vector_pack",
                scratch=[pltpu.VMEM(v.shape, f32) for v in terms] + [DMA((len(terms),))],
            )[0]
            if outer > 1:
                packed = lax.psum(packed, "ctx", axis_index_groups=outer_groups)
            lines = kernel_call(
                functools.partial(vector_lines_kernel, depth, width_own),
                [((fsdp, 32, 2 * width_own), bf16)],
                packed,
                name="vector_lines",
            )
        count = 1 if l > 0 else fsdp
        shapes = [((width, 3 * feats), bf16), ((width, feats), bf16)]
        if l == 0:
            shapes = [((fsdp, width_own + 32, 4 * feats), bf16)]
        kept = [sums_one, upstream]
        *attn_grads, head_sums[l], upstream_b, sums_one, upstream = kernel_call(
            functools.partial(attn_grad_kernel, feats, count, len(kept)),
            [saved((width if l > 0 else width_own + 32, 4 * feats), bf16)] * count
            + [saved((2, feats), f32), row_bf16]
            + [saved(k.shape, k.dtype) for k in kept],
            attn[0][3],
            attn[1][3],
            attn[0][1],
            attn[1][1],
            *middle_x,
            *grad_q,
            grad_k,
            grad_v,
            upstream_b,
            *(lines or (sums_one,)),
            *kept,
            name="attn_grad",
            scratch=[
                pltpu.VMEM((all_rows, 3 * feats), bf16),
                pltpu.VMEM((2, feats), f32),
            ]
            + [pltpu.VMEM(*shape) for shape in shapes]
            + [DMA((count + 2 + len(kept),))],
        )
        if l > 0:
            attn_later = attn_grads[0]
            upstream_chunks = gather_rows(upstream_b)
        row_sums[l] = (sums_one, sums_two)

    sources = mlp_parts
    blocks = 2 * depth
    (stacked,) = kernel_call(
        functools.partial(fetch_kernel, len(sources)),
        [((blocks * width_own, hidden), bf16)],
        *[Far(v) for v in sources],
        name="fetch",
        after=(upstream_b,),
        scratch=[DMA((blocks,))],
    )
    own_term, *other_terms = attn_grads
    other_terms = [shift_z(term, d + 1) for d, term in enumerate(other_terms)]
    crossed = swap_x(stacked)
    others = (swap_y(upstream), swap_y(outputs_own))
    part, mine, pair = kernel_call(
        functools.partial(shard_sum_kernel, depth),
        [
            ((depth * width_own, 4 * feats), bf16),
            ((24, width_own), f32),
            ((2 * blocks * width_own, hidden), bf16),
        ],
        stacked,
        crossed,
        *[Far(v) for v in (*attn_parts[1:], own_term, *other_terms)],
        name="shard_sum",
        after=others,
        scratch=[
            pltpu.VMEM((fsdp, *own_term.shape), bf16),
            DMA((fsdp + 1 + depth,)),
        ],
    )
    if outer > 1:
        part = lax.psum(part, "ctx", axis_index_groups=outer_groups)
    mine, last_pair = kernel_call(
        functools.partial(vector_plane_kernel, depth),
        [((32, width_own), f32), ((2 * depth * width_own, 4 * feats), bf16)],
        mine,
        swap_xy(mine),
        swap_x(mine),
        swap_y(mine),
        part,
        swap_x(part),
        name="vector_plane",
    )
    pieces = [last_pair, swap_core(last_pair), pair, swap_core(pair)]
    grad_gains, grad_shifts, grad_fc1_bias, grad_qv_bias = kernel_call(
        functools.partial(vector_place_kernel, depth, head_dim),
        [
            (norm_gains.shape, f32),
            (shifts.shape, f32),
            (fc1_bias.shape, f32),
            (qv_bias.shape, f32),
        ],
        mine,
        swap_core(mine),
        name="vector_place",
    )
    grad_inputs, outputs = (
        kernel_call(
            place_rows_kernel,
            [saved(inputs.shape, f32)],
            own,
            other,
            name="place_rows",
            scratch=[DMA((2,))],
        )[0]
        for own, other in zip((upstream, outputs_own), others)
    )
    placed = kernel_call(
        functools.partial(place_kernel, depth, hidden, feats),
        [saved(v.shape, f32) for v in (w_qkv, w_out, w_fc1, w_fc2)],
        *pieces,
        name="place",
        limit=24,
        scratch=[
            pltpu.VMEM((depth, GROUP, width_own, hidden), f32),
            pltpu.VMEM((depth, GROUP, hidden, width_own), f32),
            pltpu.VMEM((depth, GROUP, 3, width_own, feats), f32),
            pltpu.VMEM((depth, GROUP, feats, width_own), f32),
            DMA((16 * depth,)),
        ],
    )
    return (
        outputs,
        grad_inputs,
        grad_gains,
        grad_shifts,
        grad_qv_bias,
        grad_fc1_bias,
        *placed,
    )


def solution(mesh):
    rows = P("fsdp", "ctx", None)
    params = (
        P(None, None, "fsdp"),
        P(None, None, "fsdp"),
        P(None, None, "tp", "fsdp"),
        P(None, "tp", "fsdp"),
        P(None, None, "fsdp", "tp"),
        P(None, "tp", "fsdp"),
        P(None, "fsdp", "tp"),
        P(None, "tp", "fsdp"),
    )
    return jax.shard_map(
        per_device,
        mesh=mesh,
        in_specs=(rows, P("fsdp", None), rows) + params,
        out_specs=(rows, rows) + params,
        check_vma=False,
    )
```

```python
import functools
import math

import jax
import jax.numpy as jnp
from jax import lax
from jax.experimental import pallas as pl
from jax.experimental.pallas import tpu as pltpu
from jax.sharding import PartitionSpec as P

NORM_EPSILON = 1e-06
MASK_FILL = -1e30
ROOT_HALF = 0.7071067811865476
INV_ROOT_TAU = 0.3989422804014327
GROUP = 4
ORDER = (0, 5, 4, 1, 2, 7, 6, 3)
CHIPS = 4

bf16 = jnp.bfloat16
f32 = jnp.float32
VMEM = pl.BlockSpec(memory_space=pltpu.VMEM)
SMEM = pl.BlockSpec(memory_space=pltpu.SMEM)
HBM = pl.BlockSpec(memory_space=pltpu.HBM)
DMA = pltpu.SemaphoreType.DMA
TOKEN = ((8, 128), f32)


def dot(a, b):
    return lax.dot_general(a, b, (((1,), (0,)), ((), ())), preferred_element_type=f32)


def dot_nt(a, b):
    return lax.dot_general(a, b, (((1,), (1,)), ((), ())), preferred_element_type=f32)


def dot_tn(a, b):
    return lax.dot_general(a, b, (((0,), (0,)), ((), ())), preferred_element_type=f32)


class Far:
    def __init__(self, value):
        self.value = value


class Scalars:
    def __init__(self, value):
        self.value = value


def saved(shape, dtype):
    return pltpu.HBM(shape, dtype)


def kernel_call(body, outs, *args, name, limit=12, scratch=(), after=(), aliases=None, us=0):
    values, specs = [], []
    for arg in (*args, *after):
        if isinstance(arg, Far):
            values.append(pltpu.with_memory_space_constraint(arg.value, pltpu.HBM))
            specs.append(HBM)
        elif isinstance(arg, Scalars):
            values.append(arg.value)
            specs.append(SMEM)
        else:
            values.append(arg)
            specs.append(VMEM)
    first, last = len(args), len(args) + len(after)

    def run(*refs):
        body(*refs[:first], *refs[last:])

    out_shape, out_specs = [], []
    for out in outs:
        if isinstance(out, tuple):
            out_shape.append(jax.ShapeDtypeStruct(*out))
            out_specs.append(VMEM)
        else:
            out_shape.append(out)
            out_specs.append(HBM)
    return pl.pallas_call(
        run,
        out_shape=out_shape,
        in_specs=specs,
        out_specs=out_specs,
        scratch_shapes=list(scratch),
        input_output_aliases=aliases or {},
        compiler_params=pltpu.CompilerParams(vmem_limit_bytes=limit << 20),
        cost_estimate=pl.CostEstimate(flops=us * 10**9, bytes_accessed=0, transcendentals=0),
        name=name,
    )(*values)


def start_copies(pairs, sems):
    copies = [
        pltpu.make_async_copy(source, target, sems.at[k])
        for k, (source, target) in enumerate(pairs)
    ]
    for copy in copies:
        copy.start()
    return copies


def row_mean(value):
    return jnp.mean(value, axis=-1, keepdims=True)


def normalize(values):
    center = values - row_mean(values)
    inverse = lax.rsqrt(row_mean(center * center) + NORM_EPSILON)
    return center * inverse, inverse


def lanes_of(head, head_dim, width):
    lane = lax.broadcasted_iota(jnp.int32, (1, width), 1)
    return (lane >= head * head_dim) & (lane < (head + 1) * head_dim)


def assemble(chunks, target):
    rows = chunks[0].shape[0]
    for k, chunk in enumerate(chunks):
        target[k * rows : (k + 1) * rows, :] = chunk[...]


def only(flag, value):
    return jnp.where(flag, value, jnp.zeros_like(value))


def shards(weights):
    if len(weights) == 1:
        rows = weights[0].shape[0]
        return [(pl.ds(0, rows), weights[0])]
    count = len(weights)
    rows = weights[0].shape[0]
    f = lax.axis_index("fsdp")
    found = []
    for d, ref in enumerate(weights):
        place = lax.rem(f + (count - d), count)
        found.append((pl.ds(pl.multiple_of(place * rows, rows), rows), ref))
    return found


def pack_attn_kernel(layer, feats, qkv_hbm, out_hbm, packed_ref, token, qkv, out, sems):
    ci = lax.rem(lax.axis_index("ctx"), GROUP)
    span = pl.ds(pl.multiple_of(ci * feats, feats), feats)
    copies = start_copies(
        [(qkv_hbm.at[layer, :, :, span], qkv), (out_hbm.at[layer, span, :], out)], sems
    )
    copies[0].wait()
    for k in range(3):
        packed_ref[:, k * feats : (k + 1) * feats] = qkv[k]
    copies[1].wait()
    packed_ref[:, 3 * feats :] = out[...].T
    token[...] = jnp.zeros_like(token)


def pack_mlp_kernel(layer, hidden, fc1_hbm, fc2_hbm, packed_ref, token, fc1, fc2, sems):
    ci = lax.rem(lax.axis_index("ctx"), GROUP)
    span = pl.ds(pl.multiple_of(ci * hidden, hidden), hidden)
    copies = start_copies(
        [(fc1_hbm.at[layer, :, span], fc1), (fc2_hbm.at[layer, span, :], fc2)], sems
    )
    copies[0].wait()
    packed_ref[:, :hidden] = fc1[...]
    copies[1].wait()
    packed_ref[:, hidden:] = fc2[...].T
    token[...] = jnp.zeros_like(token)


def prep_upstream_kernel(tp, outer, lengths, cotangent_hbm,
                         upstream_hbm, upstream_b_ref, usable_ref, mask_ref,
                         rows_in, upstream_ref, sems):
    rows = rows_in.shape[0]
    c = lax.axis_index("ctx")
    t = lax.axis_index("tp")
    place = lax.rem(c, GROUP) * tp + t
    start = pl.multiple_of(t * rows, rows)
    copies = start_copies(
        [(cotangent_hbm.at[0, pl.ds(start, rows), :], rows_in)], sems.at[pl.ds(0, 1)]
    )
    lane = lax.broadcasted_iota(jnp.int32, usable_ref.shape, 1)
    limit = jnp.zeros(usable_ref.shape, jnp.int32)
    for o in range(outer):
        for k, d in enumerate(ORDER):
            source = place ^ d
            first_lane = (o * len(ORDER) + k) * rows
            count = lengths[0, o * GROUP + lax.div(source, tp)] - lax.rem(source, tp) * rows
            limit = jnp.where(lane >= first_lane, first_lane + jnp.clip(count, 0, rows), limit)
    usable_ref[...] = jnp.where(lane < limit, 1.0, 0.0)
    row = lax.broadcasted_iota(jnp.int32, mask_ref.shape, 0)
    mask = jnp.where(row + start < lengths[0, c], 1.0, 0.0)
    mask_ref[...] = mask
    copies[0].wait()
    upstream = rows_in[...] * mask[:, 0:1]
    upstream_ref[...] = upstream
    sent = start_copies([(upstream_ref, upstream_hbm)], sems.at[pl.ds(1, 1)])
    upstream_b_ref[...] = upstream.astype(bf16)
    sent[0].wait()


def prep_first_kernel(depth, inputs_hbm, vecs, stream_ref, first_ref, sems):
    rows = stream_ref.shape[0]
    start = pl.multiple_of(lax.axis_index("tp") * rows, rows)
    copies = start_copies([(inputs_hbm.at[0, pl.ds(start, rows), :], stream_ref)], sems)
    copies[0].wait()
    normed, _ = normalize(stream_ref[...])
    shift = vecs[2 * depth : 2 * depth + 1, :]
    first_ref[...] = (normed * vecs[0:1, :] + shift).astype(bf16)


def keep_rows_kernel(*refs):
    chunks, (near_hbm, far_hbm, token, near, far, sems) = refs[:8], refs[8:]
    assemble(chunks[:4], near)
    assemble(chunks[4:], far)
    for copy in start_copies([(near, near_hbm), (far, far_hbm)], sems):
        copy.wait()
    token[...] = jnp.zeros_like(token)


def qkv_kernel(feats, weight_count, *refs):
    c0, c1, c2, c3, *rest = refs
    weights = rest[:weight_count]
    bias, qkv_ref, x = rest[weight_count:]
    assemble((c0, c1, c2, c3), x)
    qkv = sum(dot(x[:, span], w[:, : 3 * feats]) for span, w in shards(weights))
    qkv_ref[:, :feats] = (qkv[:, :feats] + bias[0:1, :]).astype(bf16)
    qkv_ref[:, feats : 2 * feats] = qkv[:, feats : 2 * feats].astype(bf16)
    qkv_ref[:, 2 * feats :] = (qkv[:, 2 * feats :] + bias[1:2, :]).astype(bf16)


def attn_kernel(feats, heads, weight_count, part_count, keep_count, tile, *refs):
    q_ref, *rest = refs
    parts = rest[:part_count]
    weights = rest[part_count : part_count + weight_count]
    rest = rest[part_count + weight_count :]
    usable, *rest = rest
    kept, rest = rest[:keep_count], rest[keep_count:]
    partial_ref, attended_hbm, norm_hbm, *rest = rest
    kept_hbm, rest = rest[:keep_count], rest[keep_count:]
    keys, values, attended_ref, norm_ref, sems = rest
    head_dim = feats // heads
    scale = 1.0 / math.sqrt(head_dim)
    copies = start_copies(list(zip(kept, kept_hbm)), sems)
    first = 0
    for part in parts:
        rows, width = part.shape
        keys[first : first + rows, :] = part[:, width - 2 * feats : width - feats]
        values[first : first + rows, :] = part[:, width - feats :]
        first += rows
    keep = usable[...] > 0.5
    rows = q_ref.shape[0]
    for first in range(0, rows, tile):
        span = slice(first, first + tile)
        q = q_ref[span, :feats]
        attended = None
        for h in range(heads):
            own = lanes_of(h, head_dim, feats)
            scores = dot_nt(only(own, q), keys[...]) * scale
            scores = jnp.where(keep, scores, MASK_FILL)
            highest = jnp.max(scores, axis=-1, keepdims=True)
            raised = jnp.exp(scores - highest)
            total = jnp.sum(raised, axis=-1, keepdims=True)
            soft = (raised * (1.0 / total)).astype(bf16)
            result = dot(soft, values[...])
            log_norm = jnp.broadcast_to(highest + jnp.log(total), (tile, feats))
            if attended is None:
                attended, norms = result, log_norm
            else:
                attended = jnp.where(own, result, attended)
                norms = jnp.where(own, log_norm, norms)
        attended_ref[span, :] = attended.astype(bf16)
        norm_ref[span, :] = norms
    copies += start_copies(
        [(attended_ref, attended_hbm), (norm_ref, norm_hbm)],
        sems.at[pl.ds(keep_count, 2)],
    )
    for span, w in shards(weights):
        partial_ref[:, span] = dot_nt(attended_ref[...], w[:, 3 * feats :]).astype(bf16)
    for copy in copies:
        copy.wait()


def core_sum_kernel(count, *refs):
    pairs, owns = refs[: 2 * count], refs[2 * count : 3 * count]
    peers = refs[3 * count :]
    rows = owns[0].shape[0]
    for j in range(count):
        near, far = pairs[2 * j], pairs[2 * j + 1]
        for k in range(1 + len(peers)):
            span = slice(k * rows, (k + 1) * rows)
            total = near[span, :].astype(f32) + far[span, :].astype(f32)
            if k == 0:
                owns[j][...] = total
            else:
                peers[k - 1][j * rows : (j + 1) * rows, :] = total.astype(bf16)


def total_of(own, xy, x, y, part=0):
    rows = own.shape[0]
    span = slice(part * rows, (part + 1) * rows)
    return (
        own[...] + y[span, :].astype(f32) + x[span, :].astype(f32) + xy[span, :].astype(f32)
    )


def sum_norm_kernel(bias_row, gain_row, shift_row, own, xy, x, y, residual_hbm, vecs,
                    stream_ref, normed_ref, residual, sems):
    copies = start_copies([(residual_hbm, residual)], sems)
    total = total_of(own, xy, x, y) + vecs[bias_row : bias_row + 1, :]
    copies[0].wait()
    stream = residual[...] + total
    stream_ref[...] = stream
    normed, _ = normalize(stream)
    gain = vecs[gain_row : gain_row + 1, :]
    normed_ref[...] = (normed * gain + vecs[shift_row : shift_row + 1, :]).astype(bf16)


def sum_out_kernel(bias_row, own, xy, x, y, residual_hbm, vecs, mask, out_hbm, token,
                   residual, out_ref, sems):
    copies = start_copies([(residual_hbm, residual)], sems.at[pl.ds(0, 1)])
    total = total_of(own, xy, x, y, 1) + vecs[bias_row : bias_row + 1, :]
    copies[0].wait()
    out_ref[...] = (residual[...] + total) * mask[:, 0:1]
    token[...] = jnp.zeros_like(token)
    for copy in start_copies([(out_ref, out_hbm)], sems.at[pl.ds(1, 1)]):
        copy.wait()


def mlp_kernel(hidden, keep_count, saves, load_count, c0, c1, c2, c3, w, bias, *refs):
    kept, rest = refs[:keep_count], refs[keep_count:]
    sources, rest = rest[: max(0, load_count - 1)], rest[max(0, load_count - 1) :]
    partial_ref, x_out, act_out, slope_out, *rest = rest
    kept_hbm, rest = rest[:keep_count], rest[keep_count:]
    loaded = []
    if load_count:
        w_ref, *targets = rest[:load_count]
        *rest, load_sems = rest[load_count:]
        spans = (pl.ds(0, hidden), pl.ds(hidden, hidden))
        loaded = start_copies(
            [(w.at[:, c], w_ref.at[:, c]) for c in spans] + list(zip(sources, targets)), load_sems
        )
        w = w_ref
    if saves:
        x, act_ref, slope_ref, sems = rest
    else:
        x, act_ref, slope_ref = x_out, act_out, slope_out
        (sems,) = rest
    copies = start_copies(list(zip(kept, kept_hbm)), sems)
    assemble((c0, c1, c2, c3), x)
    if saves:
        copies += start_copies([(x, x_out)], sems.at[pl.ds(keep_count, 1)])
    block = hidden // 2
    if load_count:
        loaded[0].wait()
    for k in range(2):
        span = slice(k * block, (k + 1) * block)
        pre = dot(x[...], w[:, span]) + bias[:, span]
        cdf = 0.5 * (1.0 + lax.erf(pre * ROOT_HALF))
        density = jnp.exp(-0.5 * pre * pre) * INV_ROOT_TAU
        slope_ref[k] = cdf + pre * density
        act_ref[:, span] = (pre * cdf).astype(bf16)
        if saves:
            copies += start_copies(
                [(slope_ref.at[k], slope_out.at[k])], sems.at[pl.ds(1 + keep_count + k, 1)]
            )
    if saves:
        copies += start_copies([(act_ref, act_out)], sems.at[pl.ds(3 + keep_count, 1)])
    if load_count:
        loaded[1].wait()
    partial_ref[...] = dot_nt(act_ref[...], w[:, hidden:]).astype(bf16)
    for copy in copies + loaded[2:]:
        copy.wait()


def mlp_back_kernel(hidden, chunk_count, *refs):
    chunks, (w, slope, *rest) = refs[:chunk_count], refs[chunk_count:]
    partial_ref, grad_ref, sum_hbm, x, sum_ref, sems = rest
    assemble(chunks, x)
    grad = dot(x[...], w[:, hidden:])
    block = hidden // 2
    for k in range(2):
        span = slice(k * block, (k + 1) * block)
        part = grad[:, span] * slope[k]
        grad_ref[:, span] = part.astype(bf16)
        sum_ref[:, span] = jnp.sum(part, axis=0, keepdims=True)
    sent = start_copies([(sum_ref, sum_hbm)], sems)
    partial_ref[...] = dot_nt(grad_ref[...], w[:, :hidden]).astype(bf16)
    sent[0].wait()


def mlp_grad_kernel(hidden, keep_count, second_near, second_far, act_near, act_far,
                    up_near, up_far, grad_near, grad_far, *refs):
    kept, refs = refs[:keep_count], refs[keep_count:]
    out_hbm, *refs = refs
    kept_hbm, (out_one, out_two, sems) = refs[:keep_count], refs[keep_count:]
    sent = start_copies(list(zip(kept, kept_hbm)), sems.at[pl.ds(2, keep_count)])
    total = dot_tn(up_near[...], act_near[...]) + dot_tn(up_far[...], act_far[...])
    out_two[...] = total.astype(bf16)
    sent += start_copies(
        [(out_two, out_hbm.at[:, pl.ds(hidden, hidden)])], sems.at[pl.ds(0, 1)]
    )
    total = dot_tn(second_near[...], grad_near[...]) + dot_tn(second_far[...], grad_far[...])
    out_one[...] = total.astype(bf16)
    sent += start_copies([(out_one, out_hbm.at[:, pl.ds(0, hidden)])], sems.at[pl.ds(1, 1)])
    for copy in sent:
        copy.wait()


def norm_back(upstream, values, gain):
    normed, inverse = normalize(values)
    scaled = upstream * gain
    back = inverse * (scaled - row_mean(scaled) - normed * row_mean(scaled * normed))
    gain_grad = jnp.sum(upstream * normed, axis=0, keepdims=True)
    return back, gain_grad, jnp.sum(upstream, axis=0, keepdims=True)


def norm_back_two_kernel(gain_row, own, xy, x, y, values_hbm, upstream_hbm, vecs,
                         grad_ref, grad_b_ref, sums_ref, values, upstream, sems):
    copies = start_copies([(values_hbm, values), (upstream_hbm, upstream)], sems)
    total = total_of(own, xy, x, y)
    for copy in copies:
        copy.wait()
    up = upstream[...]
    back, gain_grad, shift_grad = norm_back(
        total, values[...], vecs[gain_row : gain_row + 1, :]
    )
    grad = up + back
    grad_ref[...] = grad
    grad_b_ref[...] = grad.astype(bf16)
    sums_ref[0:1, :] = gain_grad
    sums_ref[1:2, :] = shift_grad
    sums_ref[2:3, :] = jnp.sum(grad, axis=0, keepdims=True)
    sums_ref[3:4, :] = jnp.sum(up, axis=0, keepdims=True)


def norm_back_one_kernel(gain_row, own, xy, x, y, values_hbm, upstream_hbm, vecs, mask,
                         grad_ref, grad_b_ref, sums_ref, values, upstream, sems):
    copies = start_copies([(values_hbm, values), (upstream_hbm, upstream)], sems)
    total = total_of(own, xy, x, y)
    for copy in copies:
        copy.wait()
    back, gain_grad, shift_grad = norm_back(
        total, values[...], vecs[gain_row : gain_row + 1, :]
    )
    grad = upstream[...] + back
    if mask is not None:
        grad = grad * mask[:, 0:1]
    grad_ref[...] = grad
    grad_b_ref[...] = grad.astype(bf16)
    sums_ref[0:1, :] = gain_grad
    sums_ref[1:2, :] = shift_grad


def attn_back_kernel(feats, heads, weight_count, part_count, tile, carried, *refs):
    c0, c1, c2, c3, *rest = refs
    weights, rest = rest[:weight_count], rest[weight_count:]
    usable, qkv, attended, norms, *rest = rest
    parts, rest = rest[:part_count], rest[part_count:]
    if carried:
        keys_before, values_before, *rest = rest
    x, grad_q, grad_k, grad_v, pairs, grad_att = rest
    head_dim = feats // heads
    scale = 1.0 / math.sqrt(head_dim)
    first = 0
    for part in parts:
        rows, width = part.shape
        pairs[first : first + rows, :] = part[:, width - 2 * feats :]
        first += rows
    assemble((c0, c1, c2, c3), x)
    grad_att[...] = sum(
        dot(x[:, span], w[:, 3 * feats :]) for span, w in shards(weights)
    ).astype(bf16)
    keep = usable[...] > 0.5
    rows = qkv.shape[0]
    if carried:
        sum_k, sum_v = keys_before[...], values_before[...]
    else:
        sum_k = jnp.zeros(grad_k.shape, f32)
        sum_v = jnp.zeros(grad_v.shape, f32)
    keys, values = pairs[:, :feats], pairs[:, feats:]
    for first in range(0, rows, tile):
        span = slice(first, first + tile)
        q = qkv[span, :feats]
        ga = grad_att[span, :]
        products = ga.astype(f32) * attended[span, :].astype(f32)
        gq = None
        for h in range(heads):
            own = lanes_of(h, head_dim, feats)
            q_h = only(own, q)
            ga_h = only(own, ga)
            row_dots = jnp.sum(only(own, products), axis=-1, keepdims=True)
            scores = dot_nt(q_h, keys) * scale
            scores = jnp.where(keep, scores, MASK_FILL)
            soft = jnp.exp(scores - norms[span, h * head_dim : h * head_dim + 1])
            grad_soft = dot_nt(ga_h, values)
            grad_scores = (soft * (grad_soft - row_dots)).astype(bf16)
            part = dot(grad_scores, keys)
            gq = part if gq is None else jnp.where(own, part, gq)
            sum_k = sum_k + dot_tn(grad_scores, q_h) * scale
            sum_v = sum_v + dot_tn(soft.astype(bf16), ga_h)
        grad_q[span, :] = gq * scale
    grad_k[...] = sum_k
    grad_v[...] = sum_v


def project_kernel(feats, first, weight_count, gq, gk, gv, *refs):
    weights, (partial_ref, packed) = refs[:weight_count], refs[weight_count:]
    rows = gq.shape[0]
    span = slice(first, first + rows)
    packed[:, :feats] = gq[...].astype(bf16)
    packed[:, feats : 2 * feats] = gk[span, :].astype(bf16)
    packed[:, 2 * feats :] = gv[span, :].astype(bf16)
    for columns, w in shards(weights):
        partial_ref[:, columns] = dot_nt(packed[...], w[:, : 3 * feats]).astype(bf16)


def attn_grad_kernel(feats, count, keep_count, first_near, first_far, att_near, att_far,
                     up_near, up_far, gq_near, gq_far, gk, gv, passed, lines, *refs):
    kept, refs = refs[:keep_count], refs[keep_count:]
    outs, refs = refs[:count], refs[count:]
    heads_hbm, passed_ref, *refs = refs
    kept_hbm, (packed, sums_ref, *staged, sems) = refs[:keep_count], refs[keep_count:]
    rows = up_near.shape[0]
    used = count + 2
    sent = start_copies(list(zip(kept, kept_hbm)), sems.at[pl.ds(used, keep_count)])
    passed_ref[...] = passed[...]
    packed[:rows, :feats] = gq_near[...].astype(bf16)
    packed[rows:, :feats] = gq_far[...].astype(bf16)
    packed[:, feats : 2 * feats] = gk[...].astype(bf16)
    packed[:, 2 * feats :] = gv[...].astype(bf16)
    sums_ref[0:1, :] = jnp.sum(gq_near[...], axis=0, keepdims=True) + jnp.sum(
        gq_far[...], axis=0, keepdims=True
    )
    sums_ref[1:2, :] = jnp.sum(gv[...], axis=0, keepdims=True)
    sent += start_copies([(sums_ref, heads_hbm)], sems.at[pl.ds(0, 1)])

    def out_part(span):
        return dot_tn(up_near[:, span], att_near[...]) + dot_tn(up_far[:, span], att_far[...])

    def qkv_part(span):
        return dot_tn(first_near[:, span], packed[:rows, :]) + dot_tn(
            first_far[:, span], packed[rows:, :]
        )

    if count == 1:
        out_one, out_two = staged
        whole = slice(None)
        out_two[...] = out_part(whole).astype(bf16)
        sent += start_copies(
            [(out_two, outs[0].at[:, pl.ds(3 * feats, feats)])], sems.at[pl.ds(1, 1)]
        )
        out_one[...] = qkv_part(whole).astype(bf16)
        sent += start_copies(
            [(out_one, outs[0].at[:, pl.ds(0, 3 * feats)])], sems.at[pl.ds(2, 1)]
        )
    else:
        (stage,) = staged
        below = lines.shape[1]
        width_own = outs[0].shape[0] - below
        for d in reversed(range(count)):
            place = lax.rem(lax.axis_index("fsdp") + d, count)
            span = pl.ds(pl.multiple_of(place * width_own, width_own), width_own)
            stage[d, :width_own, : 3 * feats] = qkv_part(span).astype(bf16)
            stage[d, :width_own, 3 * feats :] = out_part(span).astype(bf16)
            stage[d, width_own:, :] = lines[d]
            sent += start_copies([(stage.at[d], outs[d])], sems.at[pl.ds(1 + d, 1)])
    for copy in sent:
        copy.wait()


def settle_kernel(keep_count, after_count, passed, *refs):
    kept, refs = refs[:keep_count], refs[keep_count + after_count :]
    passed_ref, *kept_hbm, sems = refs
    copies = start_copies(list(zip(kept, kept_hbm)), sems)
    passed_ref[...] = passed[...]
    for copy in copies:
        copy.wait()


def fetch_kernel(count, *refs):
    sources, (target, sems) = refs[:count], refs[count:]
    columns = target.shape[1]
    moves = []
    row = 0
    for source in sources:
        rows = source.shape[0]
        for first in range(0, source.shape[1], columns):
            moves.append(
                (source.at[:, pl.ds(first, columns)], target.at[pl.ds(row, rows), :])
            )
            row += rows
    for copy in start_copies(moves, sems):
        copy.wait()


def shard_sum_kernel(depth, own_hbm, stacked, crossed, *refs):
    *others, part_ref, mine_ref, pair_ref, own, sems = refs
    count = stacked.shape[0]
    first, *copies = start_copies(
        [
            (own_hbm, own),
            (stacked, pair_ref.at[pl.ds(0, count), :]),
            (crossed, pair_ref.at[pl.ds(count, count), :]),
        ],
        sems,
    )
    first.wait()
    rows, width = part_ref.shape[0], mine_ref.shape[1]
    terms = [ref[...].astype(f32) for ref in (own, *others)]
    total = terms[0]
    for term in terms[1:]:
        total = total + term
    part_ref[...] = total[:rows, :].astype(bf16)
    lines = total[rows:, :width] + total[rows:, width:]
    mine_ref[: 6 * depth, :] = lines[: 6 * depth, :]
    for k in range(mine_ref.shape[0] - 16):
        mine_ref[16 + k : 17 + k, :] = lines[6 * depth + k : 6 * depth + k + 1, :]
    for copy in copies:
        copy.wait()


def place_kernel(depth, hidden, feats, *refs):
    alone, pairs, rest = refs[:2], refs[2:4], refs[4:]

    def half_of(pair, k):
        count = pair[k % 2].shape[0] // 2
        return pair[k % 2].at[pl.ds(k // 2 * count, count), :]

    slices = [(half_of(alone, k), half_of(pairs, k)) for k in range(GROUP)]
    qkv_hbm, out_hbm, fc1_hbm, fc2_hbm, fc1, fc2, qkv, out, sems = rest
    ci = lax.rem(lax.axis_index("ctx"), GROUP)
    rows = fc1.shape[2]
    copies = []

    def send(source, target):
        copies.extend(start_copies([(source, target)], sems.at[pl.ds(len(copies), 1)]))

    for l in range(depth):
        for k in range(GROUP):
            _, stacked = slices[k]
            first = 0 if l == 0 else (3 * l - 1) * rows
            span = pl.ds(pl.multiple_of((ci ^ k) * hidden, hidden), hidden)
            fc1[l, k] = stacked[first : first + rows, :].astype(f32)
            send(fc1.at[l, k], fc1_hbm.at[l, :, span])
            fc2[l, k] = stacked[first + rows : first + 2 * rows, :].T.astype(f32)
            send(fc2.at[l, k], fc2_hbm.at[l, span, :])
    for l in reversed(range(depth)):
        for k in range(GROUP):
            last, stacked = slices[k]
            piece = last if l == 0 else stacked.at[pl.ds((3 * l + 1) * rows, rows), :]
            span = pl.ds(pl.multiple_of((ci ^ k) * feats, feats), feats)
            for j in range(3):
                qkv[l, k, j] = piece[:, j * feats : (j + 1) * feats].astype(f32)
            send(qkv.at[l, k], qkv_hbm.at[l, :, :, span])
            out[l, k] = piece[:, 3 * feats :].T.astype(f32)
            send(out.at[l, k], out_hbm.at[l, span, :])
    for copy in copies:
        copy.wait()


def vector_pack_kernel(depth, one_now, gq_near, gq_far, gv, *refs):
    count = 5 * depth - 2
    out_ref, *found, sems = refs[count:]
    copies = start_copies(list(zip(refs[:count], found)), sems)
    out_ref[...] = jnp.zeros_like(out_ref)
    feats = gv.shape[1]
    head_now = [
        jnp.sum(gq_near[...], axis=0, keepdims=True) + jnp.sum(gq_far[...], axis=0, keepdims=True),
        jnp.sum(gv[...], axis=0, keepdims=True),
    ]
    for copy in copies:
        copy.wait()
    for l in range(depth):
        if l == 0:
            one, (two, unit_near, unit_far) = one_now, found[:3]
            heads = head_now
        else:
            one, two, unit_near, unit_far, head = found[5 * l - 2 : 5 * l + 3]
            heads = [head[0:1, :], head[1:2, :]]
        out_ref[6 * l : 6 * l + 1, :] = one[0:1, :]
        out_ref[6 * l + 1 : 6 * l + 2, :] = two[0:1, :]
        out_ref[6 * l + 2 : 6 * l + 3, :] = one[1:2, :]
        out_ref[6 * l + 3 : 6 * l + 6, :] = two[1:4, :]
        units = unit_near.shape[1]
        row = 6 * depth
        out_ref[row : row + 1, l * units : (l + 1) * units] = unit_near[...] + unit_far[...]
        for j in range(2):
            start = (2 * l + j) * feats
            out_ref[row + 1 : row + 2, start : start + feats] = heads[j]


def vector_lines_kernel(depth, width_own, packed, lines_ref):
    count = lines_ref.shape[0]
    f = lax.axis_index("fsdp")
    total = packed[...]
    high = total.astype(bf16).astype(f32)
    low = total - high
    lines_ref[...] = jnp.zeros_like(lines_ref)
    last = 6 * depth
    for k, value in enumerate((high, low)):
        lanes = slice(k * width_own, (k + 1) * width_own)
        columns = [value[:, a * width_own : (a + 1) * width_own] for a in range(count)]
        for d in range(count):
            mine = columns[0]
            for a in range(1, count):
                mine = jnp.where(lax.rem(f + d, count) == a, columns[a], mine)
            rows = [mine[:last, :]]
            for r in range(2):
                for a in range(count):
                    rows.append(columns[a][last + r : last + r + 1, :])
            rows.append(jnp.zeros((lines_ref.shape[1] - last - 2 * count, width_own), f32))
            lines_ref[d, :, lanes] = jnp.concatenate(rows, axis=0).astype(bf16)


def vector_plane_kernel(depth, own, xy, x, y, part, part_x, out_ref, pair_ref):
    last = 6 * depth
    rows = part.shape[0]
    pair_ref[:rows, :] = part[...]
    pair_ref[rows:, :] = part_x[...]
    out_ref[:last, :] = own[:last, :] + xy[:last, :] + x[:last, :] + y[:last, :]
    out_ref[16:24, :] = own[16:24, :]
    out_ref[24:32, :] = x[16:24, :]


def vector_place_kernel(depth, head_dim, own, far, gains_ref, shifts_ref, unit_ref, heads_ref):
    total = own[: 6 * depth, :] + far[: 6 * depth, :]
    for l in range(depth):
        gains_ref[l] = total[6 * l : 6 * l + 2, :]
        shifts_ref[l] = total[6 * l + 2 : 6 * l + 6, :]
    pieces = (own[16:24, :], far[16:24, :], own[24:32, :], far[24:32, :])
    ci = lax.rem(lax.axis_index("ctx"), GROUP)
    f = lax.axis_index("fsdp")

    def of_place(c):
        k = ci ^ c
        found = pieces[0]
        for j in range(1, GROUP):
            found = jnp.where(k == j, pieces[j], found)
        return found

    width_own = own.shape[1]
    units = of_place(f)
    parts = unit_ref.shape[2] // width_own
    for l in range(depth):
        for j in range(parts):
            row = l * parts + j
            unit_ref[l, :, j * width_own : (j + 1) * width_own] = units[row : row + 1, :]
    head_own = heads_ref.shape[3]
    heads = heads_ref.shape[2] // GROUP
    for c in range(GROUP):
        found = of_place(c)
        for l in range(depth):
            for j in range(2):
                for h in range(heads):
                    first = ((2 * l + j) * heads + h) * head_dim
                    row, lane = 4 + first // width_own, first % width_own
                    value = found[row : row + 1, lane : lane + head_own]
                    for a in range(1, head_dim // head_own):
                        start = lane + a * head_own
                        value = jnp.where(
                            f == a, found[row : row + 1, start : start + head_own], value
                        )
                    heads_ref[l, j, c * heads + h : c * heads + h + 1, :] = value


def place_rows_kernel(own, other, out_hbm, sems):
    rows = own.shape[0]
    start = pl.multiple_of(lax.axis_index("tp") * rows, rows)
    copies = start_copies(
        [
            (own, out_hbm.at[0, pl.ds(start, rows), :]),
            (other, out_hbm.at[0, pl.ds(pl.multiple_of(rows - start, rows), rows), :]),
        ],
        sems,
    )
    for copy in copies:
        copy.wait()


def per_device(
    inputs, lengths, cotangent, norm_gains, shifts, qv_bias, fc1_bias, w_qkv, w_out, w_fc1, w_fc2
):
    depth = w_qkv.shape[0]
    width_own = w_qkv.shape[2]
    fsdp = lax.axis_size("fsdp")
    tp = lax.axis_size("tp")
    ctx = lax.axis_size("ctx")
    outer = ctx // GROUP
    rows = inputs.shape[1] // tp
    half = rows * CHIPS
    all_rows = 2 * half
    head_own = qv_bias.shape[3]
    head_dim = head_own * fsdp
    heads = qv_bias.shape[2] // GROUP
    feats = heads * head_dim
    hidden = w_fc1.shape[2] // GROUP
    width = width_own * fsdp
    t = lax.axis_index("tp")
    f = lax.axis_index("fsdp")
    ci = lax.axis_index("ctx") % GROUP
    tile = half // 2
    attn_limit = 12 if outer == 1 else 48

    def swap_core(value):
        return lax.ppermute(value, "ctx", [(i, i ^ 1) for i in range(ctx)])

    def swap_x(value):
        return lax.ppermute(value, "ctx", [(i, i ^ 2) for i in range(ctx)])

    def swap_y(value):
        return lax.ppermute(value, "tp", [(i, i ^ 1) for i in range(tp)])

    def swap_xy(value):
        pairs = [
            (i * tp + k, (i ^ 2) * tp + (k ^ 1)) for i in range(ctx) for k in range(tp)
        ]
        return lax.ppermute(value, ("ctx", "tp"), pairs)

    def shift_z(value, d):
        return lax.ppermute(value, "fsdp", [(i, (i + d) % fsdp) for i in range(fsdp)])

    outer_groups = [[o * GROUP + i for o in range(outer)] for i in range(GROUP)]

    def gather_rows(own):
        near = (own, swap_xy(own), swap_x(own), swap_y(own))
        return near, tuple(swap_core(chunk) for chunk in near)

    def settle(value, there, *kept):
        return kernel_call(
            functools.partial(settle_kernel, len(kept), 1),
            [(value.shape, value.dtype)] + [saved(k.shape, k.dtype) for k in kept],
            value,
            *kept,
            Far(there),
            name="settle",
            scratch=[DMA((max(1, len(kept)),))],
        )

    def reduce_rows(*pairs, after=()):
        count = len(pairs)
        *owns, xy, x, y = kernel_call(
            functools.partial(core_sum_kernel, count),
            [((rows, width), f32)] * count + [((count * rows, width), bf16)] * 3,
            *[v for near, far in pairs for v in (near, swap_core(far))],
            name="core_sum",
            after=after,
        )
        peers = (swap_xy(xy), swap_x(x), swap_y(y))
        return [(own, *peers) for own in owns]

    def pack_attn(l, after):
        return kernel_call(
            functools.partial(pack_attn_kernel, l, feats),
            [((width_own, 4 * feats), bf16), TOKEN],
            Far(w_qkv),
            Far(w_out),
            name="pack_attn",
            after=after,
            scratch=[
                pltpu.VMEM((3, width_own, feats), bf16),
                pltpu.VMEM((feats, width_own), bf16),
                DMA((2,)),
            ],
        )

    def pack_mlp(l, after):
        return kernel_call(
            functools.partial(pack_mlp_kernel, l, hidden),
            [((width_own, 2 * hidden), bf16), TOKEN],
            Far(w_fc1),
            Far(w_fc2),
            name="pack_mlp",
            after=after,
            scratch=[
                pltpu.VMEM((width_own, hidden), bf16),
                pltpu.VMEM((hidden, width_own), bf16),
                DMA((2,)),
            ],
        )

    attn_w = []
    mlp_w = []
    token = None
    for l in range(depth):
        own, token = pack_attn(l, () if token is None else (token,))
        attn_w.append((lax.all_gather(own, "fsdp", axis=0, tiled=True),))
        own, token = pack_mlp(l, (token,))
        mlp_w.append(lax.all_gather(own, "fsdp", axis=0, tiled=True))
        if l == 0:
            pack_token = token

    qv_own = lax.dynamic_slice_in_dim(qv_bias, ci * heads, heads, axis=2)
    vec_rows = depth * 6
    c1_rows = depth * fc1_bias.shape[2] // width_own
    qv_own = qv_own.reshape(1, -1)
    small_own = jnp.concatenate(
        [
            norm_gains.reshape(-1, width_own),
            shifts.reshape(-1, width_own),
            fc1_bias.reshape(-1, width_own),
            jnp.pad(qv_own, ((0, 0), (0, width_own - qv_own.shape[1]))),
        ],
        axis=0,
    )
    shifted = [small_own] + [shift_z(small_own, d) for d in range(1, fsdp)]

    def shard(a):
        picked = shifted[0]
        for d in range(1, fsdp):
            picked = jnp.where((f - d) % fsdp == a, shifted[d], picked)
        return picked.astype(f32)

    small = [shard(a) for a in range(fsdp)]
    vecs = jnp.concatenate([s[:vec_rows] for s in small], axis=1)
    fc1_all = shard(ci)[vec_rows : vec_rows + c1_rows].reshape(depth, 1, hidden)
    qv_all = jnp.stack(
        [s[vec_rows + c1_rows, : qv_own.shape[1]].reshape(depth, 2, heads, head_own) for s in small],
        axis=3,
    ).reshape(depth, 2, feats)

    def gain_row(l, i):
        return 2 * l + i

    def shift_row(l, i):
        return 2 * depth + 4 * l + i

    key_rows = outer * all_rows
    row_f32 = ((rows, width), f32)
    row_bf16 = ((rows, width), bf16)
    upstream, upstream_b, usable, mask = kernel_call(
        functools.partial(prep_upstream_kernel, tp, outer),
        [saved((rows, width), f32), row_bf16, ((1, key_rows), f32), ((rows, 128), f32)],
        Scalars(lengths),
        Far(cotangent),
        name="prep_upstream",
        after=(pack_token,),
        scratch=[pltpu.VMEM((rows, width), f32), pltpu.VMEM((rows, width), f32), DMA((2,))],
    )
    near, far = gather_rows(upstream_b)
    half_x = pltpu.VMEM((half, width), bf16)
    *upstream_rows, upstream_token = kernel_call(
        keep_rows_kernel,
        [saved((half, width), bf16)] * 2 + [TOKEN],
        *near,
        *far,
        name="keep_rows",
        scratch=[half_x, half_x, DMA((2,))],
    )
    stream, first = kernel_call(
        functools.partial(prep_first_kernel, depth),
        [row_f32, row_bf16],
        Far(inputs),
        vecs,
        name="prep_first",
        scratch=[DMA((1,))],
    )
    first_chunks = gather_rows(first)

    partial_out = ((half, width), bf16)
    saved_all = []
    for l in range(depth):
        qkv = []
        first_x = []
        for side in (0, 1):
            qkv_half, x_half = kernel_call(
                functools.partial(qkv_kernel, feats, len(attn_w[l])),
                [((half, 3 * feats), bf16), ((half, width), bf16)],
                *first_chunks[side],
                *attn_w[l],
                qv_all[l],
                name="qkv",
                after=(upstream_token,) if l == 0 and side == 0 else (),
            )
            qkv.append(qkv_half)
            first_x.append(x_half)
        if outer > 1:
            pairs = jnp.concatenate([part[:, feats:] for part in qkv], axis=0)
            pairs = lax.all_gather(
                pairs, "ctx", axis=0, tiled=True, axis_index_groups=outer_groups
            )
            key_parts = (pairs,)
        else:
            key_parts = tuple(qkv)
        attn = [None, None]
        for side in (1, 0):
            kept = (first_x[side], qkv[side]) + ((stream,) if side == 1 else ())
            attn[side] = kernel_call(
                functools.partial(
                    attn_kernel, feats, heads, len(attn_w[l]), len(key_parts), len(kept), tile
                ),
                [partial_out, saved((half, feats), bf16), saved((half, feats), f32)]
                + [saved(k.shape, k.dtype) for k in kept],
                qkv[side],
                *key_parts,
                *attn_w[l],
                usable,
                *kept,
                name="attn",
                limit=attn_limit,
                scratch=[
                    pltpu.VMEM((key_rows, feats), bf16),
                    pltpu.VMEM((key_rows, feats), bf16),
                    pltpu.VMEM((half, feats), bf16),
                    pltpu.VMEM((half, feats), f32),
                    DMA((len(kept) + 2,)),
                ],
            )
        (sums,) = reduce_rows((attn[0][0], attn[1][0]))
        middle, second = kernel_call(
            functools.partial(sum_norm_kernel, shift_row(l, 2), gain_row(l, 1), shift_row(l, 1)),
            [row_f32, row_bf16],
            *sums,
            Far(attn[1][5]),
            vecs,
            name="sum_norm",
            scratch=[pltpu.VMEM((rows, width), f32), DMA((1,))],
        )
        second_chunks = gather_rows(second)
        mlp = [None, None]
        for side in (1, 0):
            kept = (middle,) if side == 1 else ()
            saves = l + 1 < depth
            loads = (mlp_w[l], *upstream_rows) if not saves and side == 1 else ()
            shapes = [
                ((half, width), bf16),
                ((half, hidden), bf16),
                ((2, half, hidden // 2), f32),
            ]
            mlp[side] = kernel_call(
                functools.partial(mlp_kernel, hidden, len(kept), saves, len(loads)),
                [partial_out]
                + [saved(*shape) if saves else shape for shape in shapes]
                + [saved(k.shape, k.dtype) for k in kept]
                + [(v.shape, v.dtype) for v in loads],
                *second_chunks[side],
                Far(mlp_w[l]) if loads else mlp_w[l],
                fc1_all[l],
                *kept,
                *[Far(v) for v in loads[1:]],
                name="mlp",
                scratch=[pltpu.VMEM(*shape) for shape in shapes if saves]
                + [DMA((4 + len(kept),))]
                + [DMA((len(loads) + 1,)) for _ in loads[:1]],
            )
            if loads:
                *mlp[side], mlp_w[l], near, far = mlp[side]
                upstream_chunks = [(near,), (far,)]
        saved_all.append((attn, pairs if outer > 1 else None, mlp))
        if l + 1 < depth:
            (sums,) = reduce_rows((mlp[0][0], mlp[1][0]))
            stream, first = kernel_call(
                functools.partial(
                    sum_norm_kernel, shift_row(l, 3), gain_row(l + 1, 0), shift_row(l + 1, 0)
                ),
                [row_f32, row_bf16],
                *sums,
                Far(mlp[1][4]),
                vecs,
                name="sum_norm",
                scratch=[pltpu.VMEM((rows, width), f32), DMA((1,))],
            )
            first_chunks = gather_rows(first)

    def scatter_grads(grad):
        part = lax.psum_scatter(grad, "fsdp", scatter_dimension=0, tiled=True)
        if outer > 1:
            part = lax.psum(part, "ctx", axis_index_groups=outer_groups)
        return part

    row_sums = [None] * depth
    unit_sums = [None] * depth
    head_sums = [None] * depth
    mlp_parts = [None] * depth
    attn_parts = [None] * depth
    for l in reversed(range(depth)):
        attn, pairs, mlp = saved_all[l]
        back = [None, None]
        for side in (1, 0):
            back[side] = kernel_call(
                functools.partial(mlp_back_kernel, hidden, len(upstream_chunks[side])),
                [
                    partial_out,
                    ((half, hidden), bf16),
                    saved((1, hidden), f32),
                    ((half, width), bf16),
                ],
                *upstream_chunks[side],
                mlp_w[l],
                mlp[side][3],
                name="mlp_back",
                scratch=[pltpu.VMEM((1, hidden), f32), DMA((1,))],
            )
        kept = [back[0][0], back[1][0]]
        if l + 1 == depth:
            kept += [mlp[0][0], mlp[1][0]]
        mlp_grad, *kept = kernel_call(
            functools.partial(mlp_grad_kernel, hidden, len(kept)),
            [saved((width, 2 * hidden), bf16)] + [saved(k.shape, k.dtype) for k in kept],
            mlp[0][1],
            mlp[1][1],
            mlp[0][2],
            mlp[1][2],
            back[0][3],
            back[1][3],
            back[0][1],
            back[1][1],
            *kept,
            name="mlp_grad",
            scratch=[
                pltpu.VMEM((width, hidden), bf16),
                pltpu.VMEM((width, hidden), bf16),
                DMA((2 + len(kept),)),
            ],
        )
        mlp_parts[l] = scatter_grads(mlp_grad)
        sums, *output_sums = reduce_rows(*zip(kept[0::2], kept[1::2]))
        if l + 1 == depth:
            outputs_own, output_token = kernel_call(
                functools.partial(sum_out_kernel, shift_row(l, 3)),
                [saved((rows, width), f32), TOKEN],
                *output_sums[0],
                Far(mlp[1][4]),
                vecs,
                mask,
                name="sum_out",
                scratch=[pltpu.VMEM((rows, width), f32)] * 2 + [DMA((2,))],
            )
            after = (output_token,)
        else:
            after = ()
        unit_sums[l] = (back[0][2], back[1][2])
        grad_middle, middle_b, sums_two = kernel_call(
            functools.partial(norm_back_two_kernel, gain_row(l, 1)),
            [row_f32, row_bf16, ((4, width), f32)],
            *sums,
            Far(mlp[1][4]),
            Far(upstream),
            vecs,
            name="norm_back_two",
            after=after,
            scratch=[pltpu.VMEM((rows, width), f32)] * 2 + [DMA((2,))],
        )
        if l + 1 < depth:
            middle_b, sums_two, grad_middle = settle(
                middle_b, attn_parts[l + 1], sums_two, grad_middle
            )
        middle_chunks = gather_rows(middle_b)
        grad_q = [None, None]
        middle_x = [None, None]
        carried = ()
        for side in (0, 1):
            key_parts = (pairs,) if outer > 1 else (attn[0][4], attn[1][4])
            middle_x[side], grad_q[side], *carried = kernel_call(
                functools.partial(
                    attn_back_kernel,
                    feats,
                    heads,
                    len(attn_w[l]),
                    len(key_parts),
                    tile,
                    len(carried) > 0,
                ),
                [
                    ((half, width), bf16),
                    ((half, feats), f32),
                    ((key_rows, feats), f32),
                    ((key_rows, feats), f32),
                ],
                *middle_chunks[side],
                *attn_w[l],
                usable,
                attn[side][4],
                attn[side][1],
                attn[side][2],
                *key_parts,
                *carried,
                name="attn_back",
                scratch=[
                    pltpu.VMEM((key_rows, 2 * feats), bf16),
                    pltpu.VMEM((half, feats), bf16),
                ],
                limit=attn_limit,
            )
        grad_k, grad_v = carried
        if outer > 1:
            grad_k, grad_v = (
                lax.psum_scatter(
                    v, "ctx", scatter_dimension=0, tiled=True, axis_index_groups=outer_groups
                )
                for v in (grad_k, grad_v)
            )

        def project(side, after):
            return kernel_call(
                functools.partial(project_kernel, feats, side * half, len(attn_w[l])),
                [partial_out],
                grad_q[side],
                grad_k,
                grad_v,
                *attn_w[l],
                name="project",
                after=after,
                scratch=[pltpu.VMEM((half, 3 * feats), bf16)],
            )[0]

        far_part = project(1, ())
        near_part = project(0, ())
        (sums,) = reduce_rows((near_part, far_part))
        body = functools.partial(norm_back_one_kernel, gain_row(l, 0))
        if l > 0:
            masked = ()
            body = lambda *refs, body=body: body(*refs[:7], None, *refs[7:])
        else:
            masked = (mask,)
        upstream, upstream_b, sums_one = kernel_call(
            body,
            [row_f32, row_bf16, ((2, width), f32)],
            *sums,
            Far(attn[1][5]),
            Far(grad_middle) if l + 1 < depth else grad_middle,
            vecs,
            *masked,
            name="norm_back_one",
            scratch=[pltpu.VMEM((rows, width), f32)] * 2 + [DMA((2,))],
        )
        lines = ()
        if l == 0:
            terms = [sums_two, *unit_sums[0]]
            for k in range(1, depth):
                terms += [*row_sums[k], *unit_sums[k], head_sums[k]]
            packed = kernel_call(
                functools.partial(vector_pack_kernel, depth),
                [((6 * depth + 2, width), f32)],
                sums_one,
                *grad_q,
                grad_v,
                *[Far(v) for v in terms],
                name="vector_pack",
                scratch=[pltpu.VMEM(v.shape, f32) for v in terms] + [DMA((len(terms),))],
            )[0]
            if outer > 1:
                packed = lax.psum(packed, "ctx", axis_index_groups=outer_groups)
            lines = kernel_call(
                functools.partial(vector_lines_kernel, depth, width_own),
                [((fsdp, 32, 2 * width_own), bf16)],
                packed,
                name="vector_lines",
            )
        count = 1 if l > 0 else fsdp
        shapes = [((width, 3 * feats), bf16), ((width, feats), bf16)]
        if l == 0:
            shapes = [((fsdp, width_own + 32, 4 * feats), bf16)]
        kept = [sums_one, upstream] + ([sums_two] if l + 1 == depth else [])
        *attn_grads, head_sums[l], upstream_b, sums_one, upstream, sums_kept = [
            *kernel_call(
                functools.partial(attn_grad_kernel, feats, count, len(kept)),
                [saved((width if l > 0 else width_own + 32, 4 * feats), bf16)] * count
                + [saved((2, feats), f32), row_bf16]
                + [saved(k.shape, k.dtype) for k in kept],
                attn[0][3],
                attn[1][3],
                attn[0][1],
                attn[1][1],
                *middle_x,
                *grad_q,
                grad_k,
                grad_v,
                upstream_b,
                *(lines or (sums_one,)),
                *kept,
                name="attn_grad",
                scratch=[
                    pltpu.VMEM((all_rows, 3 * feats), bf16),
                    pltpu.VMEM((2, feats), f32),
                ]
                + [pltpu.VMEM(*shape) for shape in shapes]
                + [DMA((count + 2 + len(kept),))],
            ),
            sums_two,
        ][: count + 5]
        if l + 1 == depth:
            sums_two = sums_kept
        if l > 0:
            attn_parts[l] = scatter_grads(attn_grads[0])
            (upstream_b,) = settle(upstream_b, mlp_parts[l])
            upstream_chunks = gather_rows(upstream_b)
        row_sums[l] = (sums_one, sums_two)

    sources = [mlp_parts[0]]
    for l in range(1, depth):
        sources += [mlp_parts[l], attn_parts[l]]
    blocks = 3 * depth - 1
    (stacked,) = kernel_call(
        functools.partial(fetch_kernel, len(sources)),
        [((blocks * width_own, hidden), bf16)],
        *[Far(v) for v in sources],
        name="fetch",
        after=(upstream_b,),
        scratch=[DMA((blocks,))],
    )
    own_term, *other_terms = attn_grads
    other_terms = [shift_z(term, d + 1) for d, term in enumerate(other_terms)]
    crossed = swap_x(stacked)
    others = (swap_y(upstream), swap_y(outputs_own))
    part, mine, pair = kernel_call(
        functools.partial(shard_sum_kernel, depth),
        [
            ((width_own, 4 * feats), bf16),
            ((24, width_own), f32),
            ((2 * blocks * width_own, hidden), bf16),
        ],
        Far(own_term),
        stacked,
        crossed,
        *other_terms,
        name="shard_sum",
        after=others,
        scratch=[pltpu.VMEM(own_term.shape, bf16), DMA((3,))],
    )
    if outer > 1:
        part = lax.psum(part, "ctx", axis_index_groups=outer_groups)
    mine, last_pair = kernel_call(
        functools.partial(vector_plane_kernel, depth),
        [((32, width_own), f32), ((2 * width_own, 4 * feats), bf16)],
        mine,
        swap_xy(mine),
        swap_x(mine),
        swap_y(mine),
        part,
        swap_x(part),
        name="vector_plane",
    )
    pieces = [last_pair, swap_core(last_pair), pair, swap_core(pair)]
    grad_gains, grad_shifts, grad_fc1_bias, grad_qv_bias = kernel_call(
        functools.partial(vector_place_kernel, depth, head_dim),
        [
            (norm_gains.shape, f32),
            (shifts.shape, f32),
            (fc1_bias.shape, f32),
            (qv_bias.shape, f32),
        ],
        mine,
        swap_core(mine),
        name="vector_place",
    )
    grad_inputs, outputs = (
        kernel_call(
            place_rows_kernel,
            [saved(inputs.shape, f32)],
            own,
            other,
            name="place_rows",
            scratch=[DMA((2,))],
        )[0]
        for own, other in zip((upstream, outputs_own), others)
    )
    placed = kernel_call(
        functools.partial(place_kernel, depth, hidden, feats),
        [saved(v.shape, f32) for v in (w_qkv, w_out, w_fc1, w_fc2)],
        *pieces,
        name="place",
        limit=24,
        scratch=[
            pltpu.VMEM((depth, GROUP, width_own, hidden), f32),
            pltpu.VMEM((depth, GROUP, hidden, width_own), f32),
            pltpu.VMEM((depth, GROUP, 3, width_own, feats), f32),
            pltpu.VMEM((depth, GROUP, feats, width_own), f32),
            DMA((16 * depth,)),
        ],
    )
    return (
        outputs,
        grad_inputs,
        grad_gains,
        grad_shifts,
        grad_qv_bias,
        grad_fc1_bias,
        *placed,
    )


def solution(mesh):
    rows = P("fsdp", "ctx", None)
    params = (
        P(None, None, "fsdp"),
        P(None, None, "fsdp"),
        P(None, None, "tp", "fsdp"),
        P(None, "tp", "fsdp"),
        P(None, None, "fsdp", "tp"),
        P(None, "tp", "fsdp"),
        P(None, "fsdp", "tp"),
        P(None, "tp", "fsdp"),
    )
    return jax.shard_map(
        per_device,
        mesh=mesh,
        in_specs=(rows, P("fsdp", None), rows) + params,
        out_specs=(rows, rows) + params,
        check_vma=False,
    )
```

```python
import functools
import math

import jax
import jax.numpy as jnp
from jax import lax
from jax.experimental import pallas as pl
from jax.experimental.pallas import tpu as pltpu
from jax.sharding import PartitionSpec as P

NORM_EPSILON = 1e-06
MASK_FILL = -1e30
ROOT_HALF = 0.7071067811865476
INV_ROOT_TAU = 0.3989422804014327
GROUP = 4
ORDER = (0, 5, 4, 1, 2, 7, 6, 3)
CHIPS = 4

bf16 = jnp.bfloat16
f32 = jnp.float32
VMEM = pl.BlockSpec(memory_space=pltpu.VMEM)
SMEM = pl.BlockSpec(memory_space=pltpu.SMEM)
HBM = pl.BlockSpec(memory_space=pltpu.HBM)
DMA = pltpu.SemaphoreType.DMA
TOKEN = ((8, 128), f32)


def dot(a, b):
    return lax.dot_general(a, b, (((1,), (0,)), ((), ())), preferred_element_type=f32)


def dot_nt(a, b):
    return lax.dot_general(a, b, (((1,), (1,)), ((), ())), preferred_element_type=f32)


def dot_tn(a, b):
    return lax.dot_general(a, b, (((0,), (0,)), ((), ())), preferred_element_type=f32)


class Far:
    def __init__(self, value):
        self.value = value


class Anywhere:
    def __init__(self, value):
        self.value = value


class Scalars:
    def __init__(self, value):
        self.value = value


def saved(shape, dtype):
    return pltpu.HBM(shape, dtype)


def kernel_call(body, outs, *args, name, limit=12, scratch=(), after=(), aliases=None, us=0):
    values, specs = [], []
    for arg in (*args, *after):
        if isinstance(arg, Far):
            values.append(pltpu.with_memory_space_constraint(arg.value, pltpu.HBM))
            specs.append(HBM)
        elif isinstance(arg, Anywhere):
            values.append(arg.value)
            specs.append(pl.BlockSpec(memory_space=pl.ANY))
        elif isinstance(arg, Scalars):
            values.append(arg.value)
            specs.append(SMEM)
        else:
            values.append(arg)
            specs.append(VMEM)
    first, last = len(args), len(args) + len(after)

    def run(*refs):
        body(*refs[:first], *refs[last:])

    out_shape, out_specs = [], []
    for out in outs:
        if isinstance(out, tuple):
            out_shape.append(jax.ShapeDtypeStruct(*out))
            out_specs.append(VMEM)
        else:
            out_shape.append(out)
            out_specs.append(HBM)
    return pl.pallas_call(
        run,
        out_shape=out_shape,
        in_specs=specs,
        out_specs=out_specs,
        scratch_shapes=list(scratch),
        input_output_aliases=aliases or {},
        compiler_params=pltpu.CompilerParams(vmem_limit_bytes=limit << 20),
        cost_estimate=pl.CostEstimate(flops=us * 10**9, bytes_accessed=0, transcendentals=0),
        name=name,
    )(*values)


def start_copies(pairs, sems):
    copies = [
        pltpu.make_async_copy(source, target, sems.at[k])
        for k, (source, target) in enumerate(pairs)
    ]
    for copy in copies:
        copy.start()
    return copies


def row_mean(value):
    return jnp.mean(value, axis=-1, keepdims=True)


def normalize(values):
    center = values - row_mean(values)
    inverse = lax.rsqrt(row_mean(center * center) + NORM_EPSILON)
    return center * inverse, inverse


def lanes_of(head, head_dim, width):
    lane = lax.broadcasted_iota(jnp.int32, (1, width), 1)
    return (lane >= head * head_dim) & (lane < (head + 1) * head_dim)


def assemble(chunks, target):
    rows = chunks[0].shape[0]
    for k, chunk in enumerate(chunks):
        target[k * rows : (k + 1) * rows, :] = chunk[...]


def only(flag, value):
    return jnp.where(flag, value, jnp.zeros_like(value))


def shards(weights):
    if len(weights) == 1:
        rows = weights[0].shape[0]
        return [(pl.ds(0, rows), weights[0])]
    count = len(weights)
    rows = weights[0].shape[0]
    f = lax.axis_index("fsdp")
    found = []
    for d, ref in enumerate(weights):
        place = lax.rem(f + (count - d), count)
        found.append((pl.ds(pl.multiple_of(place * rows, rows), rows), ref))
    return found


def pack_attn_kernel(layer, feats, qkv_hbm, out_hbm, packed_ref, token, qkv, out, sems):
    ci = lax.rem(lax.axis_index("ctx"), GROUP)
    span = pl.ds(pl.multiple_of(ci * feats, feats), feats)
    copies = start_copies(
        [(qkv_hbm.at[layer, :, :, span], qkv), (out_hbm.at[layer, span, :], out)], sems
    )
    copies[0].wait()
    for k in range(3):
        packed_ref[:, k * feats : (k + 1) * feats] = qkv[k]
    copies[1].wait()
    packed_ref[:, 3 * feats :] = out[...].T
    token[...] = jnp.zeros_like(token)


def pack_mlp_kernel(layer, hidden, fc1_hbm, fc2_hbm, packed_ref, token, fc1, fc2, sems):
    ci = lax.rem(lax.axis_index("ctx"), GROUP)
    span = pl.ds(pl.multiple_of(ci * hidden, hidden), hidden)
    copies = start_copies(
        [(fc1_hbm.at[layer, :, span], fc1), (fc2_hbm.at[layer, span, :], fc2)], sems
    )
    copies[0].wait()
    packed_ref[:, :hidden] = fc1[...]
    copies[1].wait()
    packed_ref[:, hidden:] = fc2[...].T
    token[...] = jnp.zeros_like(token)


def prep_upstream_kernel(tp, outer, lengths, cotangent_hbm,
                         upstream_hbm, upstream_b_ref, usable_ref, mask_ref,
                         rows_in, upstream_ref, sems):
    rows = rows_in.shape[0]
    c = lax.axis_index("ctx")
    t = lax.axis_index("tp")
    place = lax.rem(c, GROUP) * tp + t
    start = pl.multiple_of(t * rows, rows)
    copies = start_copies(
        [(cotangent_hbm.at[0, pl.ds(start, rows), :], rows_in)], sems.at[pl.ds(0, 1)]
    )
    lane = lax.broadcasted_iota(jnp.int32, usable_ref.shape, 1)
    limit = jnp.zeros(usable_ref.shape, jnp.int32)
    for o in range(outer):
        for k, d in enumerate(ORDER):
            source = place ^ d
            first_lane = (o * len(ORDER) + k) * rows
            count = lengths[0, o * GROUP + lax.div(source, tp)] - lax.rem(source, tp) * rows
            limit = jnp.where(lane >= first_lane, first_lane + jnp.clip(count, 0, rows), limit)
    usable_ref[...] = jnp.where(lane < limit, 1.0, 0.0)
    row = lax.broadcasted_iota(jnp.int32, mask_ref.shape, 0)
    mask = jnp.where(row + start < lengths[0, c], 1.0, 0.0)
    mask_ref[...] = mask
    copies[0].wait()
    upstream = rows_in[...] * mask[:, 0:1]
    upstream_ref[...] = upstream
    sent = start_copies([(upstream_ref, upstream_hbm)], sems.at[pl.ds(1, 1)])
    upstream_b_ref[...] = upstream.astype(bf16)
    sent[0].wait()


def prep_first_kernel(depth, inputs_hbm, vecs, stream_ref, first_ref, sems):
    rows = stream_ref.shape[0]
    start = pl.multiple_of(lax.axis_index("tp") * rows, rows)
    copies = start_copies([(inputs_hbm.at[0, pl.ds(start, rows), :], stream_ref)], sems)
    copies[0].wait()
    normed, _ = normalize(stream_ref[...])
    shift = vecs[2 * depth : 2 * depth + 1, :]
    first_ref[...] = (normed * vecs[0:1, :] + shift).astype(bf16)


def keep_rows_kernel(*refs):
    chunks, (near_hbm, far_hbm, token, near, far, sems) = refs[:8], refs[8:]
    assemble(chunks[:4], near)
    assemble(chunks[4:], far)
    for copy in start_copies([(near, near_hbm), (far, far_hbm)], sems):
        copy.wait()
    token[...] = jnp.zeros_like(token)


def qkv_kernel(feats, weight_count, *refs):
    c0, c1, c2, c3, *rest = refs
    weights = rest[:weight_count]
    bias, qkv_ref, x = rest[weight_count:]
    assemble((c0, c1, c2, c3), x)
    qkv = sum(dot(x[:, span], w[:, : 3 * feats]) for span, w in shards(weights))
    qkv_ref[:, :feats] = (qkv[:, :feats] + bias[0:1, :]).astype(bf16)
    qkv_ref[:, feats : 2 * feats] = qkv[:, feats : 2 * feats].astype(bf16)
    qkv_ref[:, 2 * feats :] = (qkv[:, 2 * feats :] + bias[1:2, :]).astype(bf16)


def attn_kernel(feats, heads, weight_count, part_count, keep_count, tile, *refs):
    q_ref, *rest = refs
    parts = rest[:part_count]
    weights = rest[part_count : part_count + weight_count]
    rest = rest[part_count + weight_count :]
    usable, *rest = rest
    kept, rest = rest[:keep_count], rest[keep_count:]
    partial_ref, attended_hbm, norm_hbm, *rest = rest
    kept_hbm, rest = rest[:keep_count], rest[keep_count:]
    keys, values, attended_ref, norm_ref, sems = rest
    head_dim = feats // heads
    scale = 1.0 / math.sqrt(head_dim)
    copies = start_copies(list(zip(kept, kept_hbm)), sems)
    first = 0
    for part in parts:
        rows, width = part.shape
        keys[first : first + rows, :] = part[:, width - 2 * feats : width - feats]
        values[first : first + rows, :] = part[:, width - feats :]
        first += rows
    keep = usable[...] > 0.5
    rows = q_ref.shape[0]
    for first in range(0, rows, tile):
        span = slice(first, first + tile)
        q = q_ref[span, :feats]
        attended = None
        for h in range(heads):
            own = lanes_of(h, head_dim, feats)
            scores = dot_nt(only(own, q), keys[...]) * scale
            scores = jnp.where(keep, scores, MASK_FILL)
            highest = jnp.max(scores, axis=-1, keepdims=True)
            raised = jnp.exp(scores - highest)
            total = jnp.sum(raised, axis=-1, keepdims=True)
            soft = (raised * (1.0 / total)).astype(bf16)
            result = dot(soft, values[...])
            log_norm = jnp.broadcast_to(highest + jnp.log(total), (tile, feats))
            if attended is None:
                attended, norms = result, log_norm
            else:
                attended = jnp.where(own, result, attended)
                norms = jnp.where(own, log_norm, norms)
        attended_ref[span, :] = attended.astype(bf16)
        norm_ref[span, :] = norms
    copies += start_copies(
        [(attended_ref, attended_hbm), (norm_ref, norm_hbm)],
        sems.at[pl.ds(keep_count, 2)],
    )
    for span, w in shards(weights):
        partial_ref[:, span] = dot_nt(attended_ref[...], w[:, 3 * feats :]).astype(bf16)
    for copy in copies:
        copy.wait()


def core_sum_kernel(count, *refs):
    pairs, owns = refs[: 2 * count], refs[2 * count : 3 * count]
    peers = refs[3 * count :]
    rows = owns[0].shape[0]
    for j in range(count):
        near, far = pairs[2 * j], pairs[2 * j + 1]
        for k in range(1 + len(peers)):
            span = slice(k * rows, (k + 1) * rows)
            total = near[span, :].astype(f32) + far[span, :].astype(f32)
            if k == 0:
                owns[j][...] = total
            else:
                peers[k - 1][j * rows : (j + 1) * rows, :] = total.astype(bf16)


def total_of(own, xy, x, y, part=0):
    rows = own.shape[0]
    span = slice(part * rows, (part + 1) * rows)
    return (
        own[...] + y[span, :].astype(f32) + x[span, :].astype(f32) + xy[span, :].astype(f32)
    )


def sum_norm_kernel(bias_row, gain_row, shift_row, own, xy, x, y, residual_hbm, vecs,
                    stream_ref, normed_ref, residual, sems):
    copies = start_copies([(residual_hbm, residual)], sems)
    total = total_of(own, xy, x, y) + vecs[bias_row : bias_row + 1, :]
    copies[0].wait()
    stream = residual[...] + total
    stream_ref[...] = stream
    normed, _ = normalize(stream)
    gain = vecs[gain_row : gain_row + 1, :]
    normed_ref[...] = (normed * gain + vecs[shift_row : shift_row + 1, :]).astype(bf16)


def sum_out_kernel(bias_row, own, xy, x, y, residual_hbm, vecs, mask, out_hbm, token,
                   residual, out_ref, sems):
    copies = start_copies([(residual_hbm, residual)], sems.at[pl.ds(0, 1)])
    total = total_of(own, xy, x, y, 1) + vecs[bias_row : bias_row + 1, :]
    copies[0].wait()
    out_ref[...] = (residual[...] + total) * mask[:, 0:1]
    token[...] = jnp.zeros_like(token)
    for copy in start_copies([(out_ref, out_hbm)], sems.at[pl.ds(1, 1)]):
        copy.wait()


def mlp_kernel(hidden, keep_count, saves, load_count, c0, c1, c2, c3, w, bias, *refs):
    kept, rest = refs[:keep_count], refs[keep_count:]
    sources, rest = rest[: max(0, load_count - 1)], rest[max(0, load_count - 1) :]
    partial_ref, x_out, act_out, slope_out, *rest = rest
    kept_hbm, rest = rest[:keep_count], rest[keep_count:]
    loaded = []
    if load_count:
        w_ref, *targets = rest[:load_count]
        *rest, load_sems, chunk_sems = rest[load_count:]
        rows = c0.shape[0]
        chunks = start_copies(
            [(c, x_out.at[pl.ds(k * rows, rows), :]) for k, c in enumerate((c0, c1, c2, c3))],
            chunk_sems,
        )
        spans = (pl.ds(0, hidden), pl.ds(hidden, hidden))
        loaded = start_copies(
            [(w.at[:, c], w_ref.at[:, c]) for c in spans] + list(zip(sources, targets)), load_sems
        )
        w = w_ref
    if saves:
        x, act_ref, slope_ref, sems = rest
    else:
        x, act_ref, slope_ref = x_out, act_out, slope_out
        (sems,) = rest
    copies = start_copies(list(zip(kept, kept_hbm)), sems)
    if load_count:
        for chunk in chunks:
            chunk.wait()
    else:
        assemble((c0, c1, c2, c3), x)
    if saves:
        copies += start_copies([(x, x_out)], sems.at[pl.ds(keep_count, 1)])
    block = hidden // 2
    if load_count:
        loaded[0].wait()
    for k in range(2):
        span = slice(k * block, (k + 1) * block)
        pre = dot(x[...], w[:, span]) + bias[:, span]
        cdf = 0.5 * (1.0 + lax.erf(pre * ROOT_HALF))
        density = jnp.exp(-0.5 * pre * pre) * INV_ROOT_TAU
        slope_ref[k] = cdf + pre * density
        act_ref[:, span] = (pre * cdf).astype(bf16)
        if saves:
            copies += start_copies(
                [(slope_ref.at[k], slope_out.at[k])], sems.at[pl.ds(1 + keep_count + k, 1)]
            )
    if saves:
        copies += start_copies([(act_ref, act_out)], sems.at[pl.ds(3 + keep_count, 1)])
    if load_count:
        loaded[1].wait()
    partial_ref[...] = dot_nt(act_ref[...], w[:, hidden:]).astype(bf16)
    for copy in copies + loaded[2:]:
        copy.wait()


def mlp_back_kernel(hidden, chunk_count, *refs):
    chunks, (w, slope, *rest) = refs[:chunk_count], refs[chunk_count:]
    partial_ref, grad_ref, sum_hbm, x, sum_ref, sems = rest
    assemble(chunks, x)
    grad = dot(x[...], w[:, hidden:])
    block = hidden // 2
    for k in range(2):
        span = slice(k * block, (k + 1) * block)
        part = grad[:, span] * slope[k]
        grad_ref[:, span] = part.astype(bf16)
        sum_ref[:, span] = jnp.sum(part, axis=0, keepdims=True)
    sent = start_copies([(sum_ref, sum_hbm)], sems)
    partial_ref[...] = dot_nt(grad_ref[...], w[:, :hidden]).astype(bf16)
    sent[0].wait()


def mlp_grad_kernel(hidden, keep_count, second_near, second_far, act_near, act_far,
                    up_near, up_far, grad_near, grad_far, *refs):
    kept, refs = refs[:keep_count], refs[keep_count:]
    out_hbm, *refs = refs
    kept_hbm, (out_one, out_two, sems) = refs[:keep_count], refs[keep_count:]
    sent = start_copies(list(zip(kept, kept_hbm)), sems.at[pl.ds(2, keep_count)])
    total = dot_tn(up_near[...], act_near[...]) + dot_tn(up_far[...], act_far[...])
    out_two[...] = total.astype(bf16)
    sent += start_copies(
        [(out_two, out_hbm.at[:, pl.ds(hidden, hidden)])], sems.at[pl.ds(0, 1)]
    )
    total = dot_tn(second_near[...], grad_near[...]) + dot_tn(second_far[...], grad_far[...])
    out_one[...] = total.astype(bf16)
    sent += start_copies([(out_one, out_hbm.at[:, pl.ds(0, hidden)])], sems.at[pl.ds(1, 1)])
    for copy in sent:
        copy.wait()


def norm_back(upstream, values, gain):
    normed, inverse = normalize(values)
    scaled = upstream * gain
    back = inverse * (scaled - row_mean(scaled) - normed * row_mean(scaled * normed))
    gain_grad = jnp.sum(upstream * normed, axis=0, keepdims=True)
    return back, gain_grad, jnp.sum(upstream, axis=0, keepdims=True)


def norm_back_two_kernel(gain_row, own, xy, x, y, values, upstream, vecs,
                         grad_ref, grad_b_ref, sums_ref):
    total = total_of(own, xy, x, y)
    up = upstream[...]
    back, gain_grad, shift_grad = norm_back(
        total, values[...], vecs[gain_row : gain_row + 1, :]
    )
    grad = up + back
    grad_ref[...] = grad
    grad_b_ref[...] = grad.astype(bf16)
    sums_ref[0:1, :] = gain_grad
    sums_ref[1:2, :] = shift_grad
    sums_ref[2:3, :] = jnp.sum(grad, axis=0, keepdims=True)
    sums_ref[3:4, :] = jnp.sum(up, axis=0, keepdims=True)


def norm_back_one_kernel(gain_row, own, xy, x, y, values, upstream, vecs, mask,
                         grad_ref, grad_b_ref, sums_ref):
    total = total_of(own, xy, x, y)
    back, gain_grad, shift_grad = norm_back(
        total, values[...], vecs[gain_row : gain_row + 1, :]
    )
    grad = upstream[...] + back
    if mask is not None:
        grad = grad * mask[:, 0:1]
    grad_ref[...] = grad
    grad_b_ref[...] = grad.astype(bf16)
    sums_ref[0:1, :] = gain_grad
    sums_ref[1:2, :] = shift_grad


def attn_back_kernel(feats, heads, weight_count, part_count, tile, carried, *refs):
    c0, c1, c2, c3, *rest = refs
    weights, rest = rest[:weight_count], rest[weight_count:]
    usable, qkv, attended, norms, *rest = rest
    parts, rest = rest[:part_count], rest[part_count:]
    if carried:
        keys_before, values_before, *rest = rest
    x, grad_q, grad_k, grad_v, pairs, grad_att = rest
    head_dim = feats // heads
    scale = 1.0 / math.sqrt(head_dim)
    first = 0
    for part in parts:
        rows, width = part.shape
        pairs[first : first + rows, :] = part[:, width - 2 * feats :]
        first += rows
    assemble((c0, c1, c2, c3), x)
    grad_att[...] = sum(
        dot(x[:, span], w[:, 3 * feats :]) for span, w in shards(weights)
    ).astype(bf16)
    keep = usable[...] > 0.5
    rows = qkv.shape[0]
    if carried:
        sum_k, sum_v = keys_before[...], values_before[...]
    else:
        sum_k = jnp.zeros(grad_k.shape, f32)
        sum_v = jnp.zeros(grad_v.shape, f32)
    keys, values = pairs[:, :feats], pairs[:, feats:]
    for first in range(0, rows, tile):
        span = slice(first, first + tile)
        q = qkv[span, :feats]
        ga = grad_att[span, :]
        products = ga.astype(f32) * attended[span, :].astype(f32)
        gq = None
        for h in range(heads):
            own = lanes_of(h, head_dim, feats)
            q_h = only(own, q)
            ga_h = only(own, ga)
            row_dots = jnp.sum(only(own, products), axis=-1, keepdims=True)
            scores = dot_nt(q_h, keys) * scale
            scores = jnp.where(keep, scores, MASK_FILL)
            soft = jnp.exp(scores - norms[span, h * head_dim : h * head_dim + 1])
            grad_soft = dot_nt(ga_h, values)
            grad_scores = (soft * (grad_soft - row_dots)).astype(bf16)
            part = dot(grad_scores, keys)
            gq = part if gq is None else jnp.where(own, part, gq)
            sum_k = sum_k + dot_tn(grad_scores, q_h) * scale
            sum_v = sum_v + dot_tn(soft.astype(bf16), ga_h)
        grad_q[span, :] = gq * scale
    grad_k[...] = sum_k
    grad_v[...] = sum_v


def project_kernel(feats, first, weight_count, gq, gk, gv, *refs):
    weights, (partial_ref, packed) = refs[:weight_count], refs[weight_count:]
    rows = gq.shape[0]
    span = slice(first, first + rows)
    packed[:, :feats] = gq[...].astype(bf16)
    packed[:, feats : 2 * feats] = gk[span, :].astype(bf16)
    packed[:, 2 * feats :] = gv[span, :].astype(bf16)
    for columns, w in shards(weights):
        partial_ref[:, columns] = dot_nt(packed[...], w[:, : 3 * feats]).astype(bf16)


def attn_grad_kernel(feats, count, keep_count, first_near, first_far, att_near, att_far,
                     up_near, up_far, gq_near, gq_far, gk, gv, passed, lines, *refs):
    kept, refs = refs[:keep_count], refs[keep_count:]
    outs, refs = refs[:count], refs[count:]
    heads_hbm, passed_ref, *refs = refs
    kept_hbm, (packed, sums_ref, *staged, sems) = refs[:keep_count], refs[keep_count:]
    rows = up_near.shape[0]
    used = count + 2
    sent = start_copies(list(zip(kept, kept_hbm)), sems.at[pl.ds(used, keep_count)])
    passed_ref[...] = passed[...]
    packed[:rows, :feats] = gq_near[...].astype(bf16)
    packed[rows:, :feats] = gq_far[...].astype(bf16)
    packed[:, feats : 2 * feats] = gk[...].astype(bf16)
    packed[:, 2 * feats :] = gv[...].astype(bf16)
    sums_ref[0:1, :] = jnp.sum(gq_near[...], axis=0, keepdims=True) + jnp.sum(
        gq_far[...], axis=0, keepdims=True
    )
    sums_ref[1:2, :] = jnp.sum(gv[...], axis=0, keepdims=True)
    sent += start_copies([(sums_ref, heads_hbm)], sems.at[pl.ds(0, 1)])

    def out_part(span):
        return dot_tn(up_near[:, span], att_near[...]) + dot_tn(up_far[:, span], att_far[...])

    def qkv_part(span):
        return dot_tn(first_near[:, span], packed[:rows, :]) + dot_tn(
            first_far[:, span], packed[rows:, :]
        )

    if count == 1:
        out_one, out_two = staged
        whole = slice(None)
        out_two[...] = out_part(whole).astype(bf16)
        sent += start_copies(
            [(out_two, outs[0].at[:, pl.ds(3 * feats, feats)])], sems.at[pl.ds(1, 1)]
        )
        out_one[...] = qkv_part(whole).astype(bf16)
        sent += start_copies(
            [(out_one, outs[0].at[:, pl.ds(0, 3 * feats)])], sems.at[pl.ds(2, 1)]
        )
    else:
        (stage,) = staged
        below = lines.shape[1]
        width_own = outs[0].shape[0] - below
        for d in reversed(range(count)):
            place = lax.rem(lax.axis_index("fsdp") + d, count)
            span = pl.ds(pl.multiple_of(place * width_own, width_own), width_own)
            stage[d, :width_own, : 3 * feats] = qkv_part(span).astype(bf16)
            stage[d, :width_own, 3 * feats :] = out_part(span).astype(bf16)
            stage[d, width_own:, :] = lines[d]
            sent += start_copies([(stage.at[d], outs[d])], sems.at[pl.ds(1 + d, 1)])
    for copy in sent:
        copy.wait()


def settle_kernel(keep_count, after_count, passed, *refs):
    kept, refs = refs[:keep_count], refs[keep_count + after_count :]
    passed_ref, *kept_hbm, sems = refs
    copies = start_copies(list(zip(kept, kept_hbm)), sems)
    passed_ref[...] = passed[...]
    for copy in copies:
        copy.wait()


def fetch_kernel(count, *refs):
    sources, (target, sems) = refs[:count], refs[count:]
    columns = target.shape[1]
    moves = []
    row = 0
    for source in sources:
        rows = source.shape[0]
        for first in range(0, source.shape[1], columns):
            moves.append(
                (source.at[:, pl.ds(first, columns)], target.at[pl.ds(row, rows), :])
            )
            row += rows
    for copy in start_copies(moves, sems):
        copy.wait()


def shard_sum_kernel(depth, own_hbm, stacked, crossed, *refs):
    *others, part_ref, mine_ref, pair_ref, own, sems = refs
    count = stacked.shape[0]
    first, *copies = start_copies(
        [
            (own_hbm, own),
            (stacked, pair_ref.at[pl.ds(0, count), :]),
            (crossed, pair_ref.at[pl.ds(count, count), :]),
        ],
        sems,
    )
    first.wait()
    rows, width = part_ref.shape[0], mine_ref.shape[1]
    terms = [ref[...].astype(f32) for ref in (own, *others)]
    total = terms[0]
    for term in terms[1:]:
        total = total + term
    part_ref[...] = total[:rows, :].astype(bf16)
    lines = total[rows:, :width] + total[rows:, width:]
    mine_ref[: 6 * depth, :] = lines[: 6 * depth, :]
    for k in range(mine_ref.shape[0] - 16):
        mine_ref[16 + k : 17 + k, :] = lines[6 * depth + k : 6 * depth + k + 1, :]
    for copy in copies:
        copy.wait()


def place_kernel(depth, hidden, feats, *refs):
    alone, pairs, rest = refs[:2], refs[2:4], refs[4:]

    def half_of(pair, k):
        count = pair[k % 2].shape[0] // 2
        return pair[k % 2].at[pl.ds(k // 2 * count, count), :]

    slices = [(half_of(alone, k), half_of(pairs, k)) for k in range(GROUP)]
    qkv_hbm, out_hbm, fc1_hbm, fc2_hbm, fc1, fc2, qkv, out, sems = rest
    ci = lax.rem(lax.axis_index("ctx"), GROUP)
    rows = fc1.shape[2]
    copies = []

    def send(source, target):
        copies.extend(start_copies([(source, target)], sems.at[pl.ds(len(copies), 1)]))

    for l in range(depth):
        for k in range(GROUP):
            _, stacked = slices[k]
            first = 0 if l == 0 else (3 * l - 1) * rows
            span = pl.ds(pl.multiple_of((ci ^ k) * hidden, hidden), hidden)
            fc1[l, k] = stacked[first : first + rows, :].astype(f32)
            send(fc1.at[l, k], fc1_hbm.at[l, :, span])
            fc2[l, k] = stacked[first + rows : first + 2 * rows, :].T.astype(f32)
            send(fc2.at[l, k], fc2_hbm.at[l, span, :])
    for l in reversed(range(depth)):
        for k in range(GROUP):
            last, stacked = slices[k]
            piece = last if l == 0 else stacked.at[pl.ds((3 * l + 1) * rows, rows), :]
            span = pl.ds(pl.multiple_of((ci ^ k) * feats, feats), feats)
            for j in range(3):
                qkv[l, k, j] = piece[:, j * feats : (j + 1) * feats].astype(f32)
            send(qkv.at[l, k], qkv_hbm.at[l, :, :, span])
            out[l, k] = piece[:, 3 * feats :].T.astype(f32)
            send(out.at[l, k], out_hbm.at[l, span, :])
    for copy in copies:
        copy.wait()


def vector_pack_kernel(depth, one_now, gq_near, gq_far, gv, *refs):
    count = 5 * depth - 2
    out_ref, *found, sems = refs[count:]
    copies = start_copies(list(zip(refs[:count], found)), sems)
    out_ref[...] = jnp.zeros_like(out_ref)
    feats = gv.shape[1]
    head_now = [
        jnp.sum(gq_near[...], axis=0, keepdims=True) + jnp.sum(gq_far[...], axis=0, keepdims=True),
        jnp.sum(gv[...], axis=0, keepdims=True),
    ]
    for copy in copies:
        copy.wait()
    for l in range(depth):
        if l == 0:
            one, (two, unit_near, unit_far) = one_now, found[:3]
            heads = head_now
        else:
            one, two, unit_near, unit_far, head = found[5 * l - 2 : 5 * l + 3]
            heads = [head[0:1, :], head[1:2, :]]
        out_ref[6 * l : 6 * l + 1, :] = one[0:1, :]
        out_ref[6 * l + 1 : 6 * l + 2, :] = two[0:1, :]
        out_ref[6 * l + 2 : 6 * l + 3, :] = one[1:2, :]
        out_ref[6 * l + 3 : 6 * l + 6, :] = two[1:4, :]
        units = unit_near.shape[1]
        row = 6 * depth
        out_ref[row : row + 1, l * units : (l + 1) * units] = unit_near[...] + unit_far[...]
        for j in range(2):
            start = (2 * l + j) * feats
            out_ref[row + 1 : row + 2, start : start + feats] = heads[j]


def vector_lines_kernel(depth, width_own, packed, lines_ref):
    count = lines_ref.shape[0]
    f = lax.axis_index("fsdp")
    total = packed[...]
    high = total.astype(bf16).astype(f32)
    low = total - high
    lines_ref[...] = jnp.zeros_like(lines_ref)
    last = 6 * depth
    for k, value in enumerate((high, low)):
        lanes = slice(k * width_own, (k + 1) * width_own)
        columns = [value[:, a * width_own : (a + 1) * width_own] for a in range(count)]
        for d in range(count):
            mine = columns[0]
            for a in range(1, count):
                mine = jnp.where(lax.rem(f + d, count) == a, columns[a], mine)
            rows = [mine[:last, :]]
            for r in range(2):
                for a in range(count):
                    rows.append(columns[a][last + r : last + r + 1, :])
            rows.append(jnp.zeros((lines_ref.shape[1] - last - 2 * count, width_own), f32))
            lines_ref[d, :, lanes] = jnp.concatenate(rows, axis=0).astype(bf16)


def vector_plane_kernel(depth, own, xy, x, y, part, part_x, out_ref, pair_ref):
    last = 6 * depth
    rows = part.shape[0]
    pair_ref[:rows, :] = part[...]
    pair_ref[rows:, :] = part_x[...]
    out_ref[:last, :] = own[:last, :] + xy[:last, :] + x[:last, :] + y[:last, :]
    out_ref[16:24, :] = own[16:24, :]
    out_ref[24:32, :] = x[16:24, :]


def vector_place_kernel(depth, head_dim, own, far, gains_ref, shifts_ref, unit_ref, heads_ref):
    total = own[: 6 * depth, :] + far[: 6 * depth, :]
    for l in range(depth):
        gains_ref[l] = total[6 * l : 6 * l + 2, :]
        shifts_ref[l] = total[6 * l + 2 : 6 * l + 6, :]
    pieces = (own[16:24, :], far[16:24, :], own[24:32, :], far[24:32, :])
    ci = lax.rem(lax.axis_index("ctx"), GROUP)
    f = lax.axis_index("fsdp")

    def of_place(c):
        k = ci ^ c
        found = pieces[0]
        for j in range(1, GROUP):
            found = jnp.where(k == j, pieces[j], found)
        return found

    width_own = own.shape[1]
    units = of_place(f)
    parts = unit_ref.shape[2] // width_own
    for l in range(depth):
        for j in range(parts):
            row = l * parts + j
            unit_ref[l, :, j * width_own : (j + 1) * width_own] = units[row : row + 1, :]
    head_own = heads_ref.shape[3]
    heads = heads_ref.shape[2] // GROUP
    for c in range(GROUP):
        found = of_place(c)
        for l in range(depth):
            for j in range(2):
                for h in range(heads):
                    first = ((2 * l + j) * heads + h) * head_dim
                    row, lane = 4 + first // width_own, first % width_own
                    value = found[row : row + 1, lane : lane + head_own]
                    for a in range(1, head_dim // head_own):
                        start = lane + a * head_own
                        value = jnp.where(
                            f == a, found[row : row + 1, start : start + head_own], value
                        )
                    heads_ref[l, j, c * heads + h : c * heads + h + 1, :] = value


def place_rows_kernel(own, other, out_hbm, sems):
    rows = own.shape[0]
    start = pl.multiple_of(lax.axis_index("tp") * rows, rows)
    copies = start_copies(
        [
            (own, out_hbm.at[0, pl.ds(start, rows), :]),
            (other, out_hbm.at[0, pl.ds(pl.multiple_of(rows - start, rows), rows), :]),
        ],
        sems,
    )
    for copy in copies:
        copy.wait()


def per_device(
    inputs, lengths, cotangent, norm_gains, shifts, qv_bias, fc1_bias, w_qkv, w_out, w_fc1, w_fc2
):
    depth = w_qkv.shape[0]
    width_own = w_qkv.shape[2]
    fsdp = lax.axis_size("fsdp")
    tp = lax.axis_size("tp")
    ctx = lax.axis_size("ctx")
    outer = ctx // GROUP
    rows = inputs.shape[1] // tp
    half = rows * CHIPS
    all_rows = 2 * half
    head_own = qv_bias.shape[3]
    head_dim = head_own * fsdp
    heads = qv_bias.shape[2] // GROUP
    feats = heads * head_dim
    hidden = w_fc1.shape[2] // GROUP
    width = width_own * fsdp
    t = lax.axis_index("tp")
    f = lax.axis_index("fsdp")
    ci = lax.axis_index("ctx") % GROUP
    tile = half // 2
    attn_limit = 12 if outer == 1 else 48

    def swap_core(value):
        return lax.ppermute(value, "ctx", [(i, i ^ 1) for i in range(ctx)])

    def swap_x(value):
        return lax.ppermute(value, "ctx", [(i, i ^ 2) for i in range(ctx)])

    def swap_y(value):
        return lax.ppermute(value, "tp", [(i, i ^ 1) for i in range(tp)])

    def swap_xy(value):
        pairs = [
            (i * tp + k, (i ^ 2) * tp + (k ^ 1)) for i in range(ctx) for k in range(tp)
        ]
        return lax.ppermute(value, ("ctx", "tp"), pairs)

    def shift_z(value, d):
        return lax.ppermute(value, "fsdp", [(i, (i + d) % fsdp) for i in range(fsdp)])

    outer_groups = [[o * GROUP + i for o in range(outer)] for i in range(GROUP)]

    def gather_rows(own):
        near = (own, swap_xy(own), swap_x(own), swap_y(own))
        return near, tuple(swap_core(chunk) for chunk in near)

    def settle(value, there, *kept):
        return kernel_call(
            functools.partial(settle_kernel, len(kept), 1),
            [(value.shape, value.dtype)] + [saved(k.shape, k.dtype) for k in kept],
            value,
            *kept,
            Far(there),
            name="settle",
            scratch=[DMA((max(1, len(kept)),))],
        )

    def reduce_rows(*pairs, after=()):
        count = len(pairs)
        *owns, xy, x, y = kernel_call(
            functools.partial(core_sum_kernel, count),
            [((rows, width), f32)] * count + [((count * rows, width), bf16)] * 3,
            *[v for near, far in pairs for v in (near, swap_core(far))],
            name="core_sum",
            after=after,
        )
        peers = (swap_xy(xy), swap_x(x), swap_y(y))
        return [(own, *peers) for own in owns]

    def pack_attn(l, after):
        return kernel_call(
            functools.partial(pack_attn_kernel, l, feats),
            [((width_own, 4 * feats), bf16), TOKEN],
            Far(w_qkv),
            Far(w_out),
            name="pack_attn",
            after=after,
            scratch=[
                pltpu.VMEM((3, width_own, feats), bf16),
                pltpu.VMEM((feats, width_own), bf16),
                DMA((2,)),
            ],
        )

    def pack_mlp(l, after):
        return kernel_call(
            functools.partial(pack_mlp_kernel, l, hidden),
            [((width_own, 2 * hidden), bf16), TOKEN],
            Far(w_fc1),
            Far(w_fc2),
            name="pack_mlp",
            after=after,
            scratch=[
                pltpu.VMEM((width_own, hidden), bf16),
                pltpu.VMEM((hidden, width_own), bf16),
                DMA((2,)),
            ],
        )

    attn_w = []
    mlp_w = []
    token = None
    for l in range(depth):
        own, token = pack_attn(l, () if token is None else (token,))
        attn_w.append((lax.all_gather(own, "fsdp", axis=0, tiled=True),))
        own, token = pack_mlp(l, (token,))
        mlp_w.append(lax.all_gather(own, "fsdp", axis=0, tiled=True))
        if l == 0:
            pack_token = token

    qv_own = lax.dynamic_slice_in_dim(qv_bias, ci * heads, heads, axis=2)
    vec_rows = depth * 6
    c1_rows = depth * fc1_bias.shape[2] // width_own
    qv_own = qv_own.reshape(1, -1)
    small_own = jnp.concatenate(
        [
            norm_gains.reshape(-1, width_own),
            shifts.reshape(-1, width_own),
            fc1_bias.reshape(-1, width_own),
            jnp.pad(qv_own, ((0, 0), (0, width_own - qv_own.shape[1]))),
        ],
        axis=0,
    )
    shifted = [small_own] + [shift_z(small_own, d) for d in range(1, fsdp)]

    def shard(a):
        picked = shifted[0]
        for d in range(1, fsdp):
            picked = jnp.where((f - d) % fsdp == a, shifted[d], picked)
        return picked.astype(f32)

    small = [shard(a) for a in range(fsdp)]
    vecs = jnp.concatenate([s[:vec_rows] for s in small], axis=1)
    fc1_all = shard(ci)[vec_rows : vec_rows + c1_rows].reshape(depth, 1, hidden)
    qv_all = jnp.stack(
        [s[vec_rows + c1_rows, : qv_own.shape[1]].reshape(depth, 2, heads, head_own) for s in small],
        axis=3,
    ).reshape(depth, 2, feats)

    def gain_row(l, i):
        return 2 * l + i

    def shift_row(l, i):
        return 2 * depth + 4 * l + i

    key_rows = outer * all_rows
    row_f32 = ((rows, width), f32)
    row_bf16 = ((rows, width), bf16)
    upstream, upstream_b, usable, mask = kernel_call(
        functools.partial(prep_upstream_kernel, tp, outer),
        [saved((rows, width), f32), row_bf16, ((1, key_rows), f32), ((rows, 128), f32)],
        Scalars(lengths),
        Far(cotangent),
        name="prep_upstream",
        after=(pack_token,),
        scratch=[pltpu.VMEM((rows, width), f32), pltpu.VMEM((rows, width), f32), DMA((2,))],
    )
    near, far = gather_rows(upstream_b)
    half_x = pltpu.VMEM((half, width), bf16)
    *upstream_rows, upstream_token = kernel_call(
        keep_rows_kernel,
        [saved((half, width), bf16)] * 2 + [TOKEN],
        *near,
        *far,
        name="keep_rows",
        scratch=[half_x, half_x, DMA((2,))],
    )
    stream, first = kernel_call(
        functools.partial(prep_first_kernel, depth),
        [row_f32, row_bf16],
        Far(inputs),
        vecs,
        name="prep_first",
        scratch=[DMA((1,))],
    )
    first_chunks = gather_rows(first)

    partial_out = ((half, width), bf16)
    saved_all = []
    for l in range(depth):
        qkv = []
        first_x = []
        for side in (0, 1):
            qkv_half, x_half = kernel_call(
                functools.partial(qkv_kernel, feats, len(attn_w[l])),
                [((half, 3 * feats), bf16), ((half, width), bf16)],
                *first_chunks[side],
                *attn_w[l],
                qv_all[l],
                name="qkv",
                after=(upstream_token,) if l == 0 and side == 0 else (),
            )
            qkv.append(qkv_half)
            first_x.append(x_half)
        if outer > 1:
            pairs = jnp.concatenate([part[:, feats:] for part in qkv], axis=0)
            pairs = lax.all_gather(
                pairs, "ctx", axis=0, tiled=True, axis_index_groups=outer_groups
            )
            key_parts = (pairs,)
        else:
            key_parts = tuple(qkv)
        attn = [None, None]
        for side in (1, 0):
            kept = (first_x[side], qkv[side]) + ((stream,) if side == 1 else ())
            attn[side] = kernel_call(
                functools.partial(
                    attn_kernel, feats, heads, len(attn_w[l]), len(key_parts), len(kept), tile
                ),
                [partial_out, saved((half, feats), bf16), saved((half, feats), f32)]
                + [saved(k.shape, k.dtype) for k in kept],
                qkv[side],
                *key_parts,
                *attn_w[l],
                usable,
                *kept,
                name="attn",
                limit=attn_limit,
                scratch=[
                    pltpu.VMEM((key_rows, feats), bf16),
                    pltpu.VMEM((key_rows, feats), bf16),
                    pltpu.VMEM((half, feats), bf16),
                    pltpu.VMEM((half, feats), f32),
                    DMA((len(kept) + 2,)),
                ],
            )
        (sums,) = reduce_rows((attn[0][0], attn[1][0]))
        middle, second = kernel_call(
            functools.partial(sum_norm_kernel, shift_row(l, 2), gain_row(l, 1), shift_row(l, 1)),
            [row_f32, row_bf16],
            *sums,
            Far(attn[1][5]),
            vecs,
            name="sum_norm",
            scratch=[pltpu.VMEM((rows, width), f32), DMA((1,))],
        )
        second_chunks = gather_rows(second)
        mlp = [None, None]
        for side in (1, 0):
            kept = (middle,) if side == 1 else ()
            saves = l + 1 < depth
            loads = (mlp_w[l], *upstream_rows) if not saves and side == 1 else ()
            shapes = [
                ((half, width), bf16),
                ((half, hidden), bf16),
                ((2, half, hidden // 2), f32),
            ]
            mlp[side] = kernel_call(
                functools.partial(mlp_kernel, hidden, len(kept), saves, len(loads)),
                [partial_out]
                + [saved(*shape) if saves else shape for shape in shapes]
                + [saved(k.shape, k.dtype) for k in kept]
                + [(v.shape, v.dtype) for v in loads],
                *[Anywhere(c) if loads else c for c in second_chunks[side]],
                Far(mlp_w[l]) if loads else mlp_w[l],
                fc1_all[l],
                *kept,
                *[Far(v) for v in loads[1:]],
                name="mlp",
                scratch=[pltpu.VMEM(*shape) for shape in shapes if saves]
                + [DMA((4 + len(kept),))]
                + ([DMA((len(loads) + 1,)), DMA((CHIPS,))] if loads else []),
            )
            if loads:
                *mlp[side], mlp_w[l], near, far = mlp[side]
                upstream_chunks = [(near,), (far,)]
        saved_all.append((attn, pairs if outer > 1 else None, mlp))
        if l + 1 < depth:
            (sums,) = reduce_rows((mlp[0][0], mlp[1][0]))
            stream, first = kernel_call(
                functools.partial(
                    sum_norm_kernel, shift_row(l, 3), gain_row(l + 1, 0), shift_row(l + 1, 0)
                ),
                [row_f32, row_bf16],
                *sums,
                Far(mlp[1][4]),
                vecs,
                name="sum_norm",
                scratch=[pltpu.VMEM((rows, width), f32), DMA((1,))],
            )
            first_chunks = gather_rows(first)

    def scatter_grads(grad):
        part = lax.psum_scatter(grad, "fsdp", scatter_dimension=0, tiled=True)
        if outer > 1:
            part = lax.psum(part, "ctx", axis_index_groups=outer_groups)
        return part

    row_sums = [None] * depth
    unit_sums = [None] * depth
    head_sums = [None] * depth
    mlp_parts = [None] * depth
    attn_parts = [None] * depth
    for l in reversed(range(depth)):
        attn, pairs, mlp = saved_all[l]
        back = [None, None]
        for side in (1, 0):
            back[side] = kernel_call(
                functools.partial(mlp_back_kernel, hidden, len(upstream_chunks[side])),
                [
                    partial_out,
                    ((half, hidden), bf16),
                    saved((1, hidden), f32),
                    ((half, width), bf16),
                ],
                *upstream_chunks[side],
                mlp_w[l],
                mlp[side][3],
                name="mlp_back",
                scratch=[pltpu.VMEM((1, hidden), f32), DMA((1,))],
            )
        kept = [back[0][0], back[1][0]]
        if l + 1 == depth:
            kept += [mlp[0][0], mlp[1][0]]
        mlp_grad, *kept = kernel_call(
            functools.partial(mlp_grad_kernel, hidden, len(kept)),
            [saved((width, 2 * hidden), bf16)] + [saved(k.shape, k.dtype) for k in kept],
            mlp[0][1],
            mlp[1][1],
            mlp[0][2],
            mlp[1][2],
            back[0][3],
            back[1][3],
            back[0][1],
            back[1][1],
            *kept,
            name="mlp_grad",
            scratch=[
                pltpu.VMEM((width, hidden), bf16),
                pltpu.VMEM((width, hidden), bf16),
                DMA((2 + len(kept),)),
            ],
        )
        mlp_parts[l] = scatter_grads(mlp_grad)
        sums, *output_sums = reduce_rows(*zip(kept[0::2], kept[1::2]))
        if l + 1 == depth:
            outputs_own, output_token = kernel_call(
                functools.partial(sum_out_kernel, shift_row(l, 3)),
                [saved((rows, width), f32), TOKEN],
                *output_sums[0],
                Far(mlp[1][4]),
                vecs,
                mask,
                name="sum_out",
                scratch=[pltpu.VMEM((rows, width), f32)] * 2 + [DMA((2,))],
            )
            after = (output_token,)
        else:
            after = ()
        unit_sums[l] = (back[0][2], back[1][2])
        grad_middle, middle_b, sums_two = kernel_call(
            functools.partial(norm_back_two_kernel, gain_row(l, 1)),
            [row_f32, row_bf16, ((4, width), f32)],
            *sums,
            mlp[1][4],
            upstream,
            vecs,
            name="norm_back_two",
            after=after,
        )
        if l + 1 < depth:
            middle_b, sums_two, grad_middle = settle(
                middle_b, attn_parts[l + 1], sums_two, grad_middle
            )
        middle_chunks = gather_rows(middle_b)
        grad_q = [None, None]
        middle_x = [None, None]
        carried = ()
        for side in (0, 1):
            key_parts = (pairs,) if outer > 1 else (attn[0][4], attn[1][4])
            middle_x[side], grad_q[side], *carried = kernel_call(
                functools.partial(
                    attn_back_kernel,
                    feats,
                    heads,
                    len(attn_w[l]),
                    len(key_parts),
                    tile,
                    len(carried) > 0,
                ),
                [
                    ((half, width), bf16),
                    ((half, feats), f32),
                    ((key_rows, feats), f32),
                    ((key_rows, feats), f32),
                ],
                *middle_chunks[side],
                *attn_w[l],
                usable,
                attn[side][4],
                attn[side][1],
                attn[side][2],
                *key_parts,
                *carried,
                name="attn_back",
                scratch=[
                    pltpu.VMEM((key_rows, 2 * feats), bf16),
                    pltpu.VMEM((half, feats), bf16),
                ],
                limit=attn_limit,
            )
        grad_k, grad_v = carried
        if outer > 1:
            grad_k, grad_v = (
                lax.psum_scatter(
                    v, "ctx", scatter_dimension=0, tiled=True, axis_index_groups=outer_groups
                )
                for v in (grad_k, grad_v)
            )

        def project(side, after):
            return kernel_call(
                functools.partial(project_kernel, feats, side * half, len(attn_w[l])),
                [partial_out],
                grad_q[side],
                grad_k,
                grad_v,
                *attn_w[l],
                name="project",
                after=after,
                scratch=[pltpu.VMEM((half, 3 * feats), bf16)],
            )[0]

        far_part = project(1, ())
        near_part = project(0, ())
        (sums,) = reduce_rows((near_part, far_part))
        body = functools.partial(norm_back_one_kernel, gain_row(l, 0))
        if l > 0:
            masked = ()
            body = lambda *refs, body=body: body(*refs[:7], None, *refs[7:])
        else:
            masked = (mask,)
        upstream, upstream_b, sums_one = kernel_call(
            body,
            [row_f32, row_bf16, ((2, width), f32)],
            *sums,
            attn[1][5],
            grad_middle,
            vecs,
            *masked,
            name="norm_back_one",
        )
        lines = ()
        if l == 0:
            terms = [sums_two, *unit_sums[0]]
            for k in range(1, depth):
                terms += [*row_sums[k], *unit_sums[k], head_sums[k]]
            packed = kernel_call(
                functools.partial(vector_pack_kernel, depth),
                [((6 * depth + 2, width), f32)],
                sums_one,
                *grad_q,
                grad_v,
                *[Far(v) for v in terms],
                name="vector_pack",
                scratch=[pltpu.VMEM(v.shape, f32) for v in terms] + [DMA((len(terms),))],
            )[0]
            if outer > 1:
                packed = lax.psum(packed, "ctx", axis_index_groups=outer_groups)
            lines = kernel_call(
                functools.partial(vector_lines_kernel, depth, width_own),
                [((fsdp, 32, 2 * width_own), bf16)],
                packed,
                name="vector_lines",
            )
        count = 1 if l > 0 else fsdp
        shapes = [((width, 3 * feats), bf16), ((width, feats), bf16)]
        if l == 0:
            shapes = [((fsdp, width_own + 32, 4 * feats), bf16)]
        kept = [sums_one, upstream] + ([sums_two] if l + 1 == depth else [])
        *attn_grads, head_sums[l], upstream_b, sums_one, upstream, sums_kept = [
            *kernel_call(
                functools.partial(attn_grad_kernel, feats, count, len(kept)),
                [saved((width if l > 0 else width_own + 32, 4 * feats), bf16)] * count
                + [saved((2, feats), f32), row_bf16]
                + [saved(k.shape, k.dtype) for k in kept],
                attn[0][3],
                attn[1][3],
                attn[0][1],
                attn[1][1],
                *middle_x,
                *grad_q,
                grad_k,
                grad_v,
                upstream_b,
                *(lines or (sums_one,)),
                *kept,
                name="attn_grad",
                scratch=[
                    pltpu.VMEM((all_rows, 3 * feats), bf16),
                    pltpu.VMEM((2, feats), f32),
                ]
                + [pltpu.VMEM(*shape) for shape in shapes]
                + [DMA((count + 2 + len(kept),))],
            ),
            sums_two,
        ][: count + 5]
        if l + 1 == depth:
            sums_two = sums_kept
        if l > 0:
            attn_parts[l] = scatter_grads(attn_grads[0])
            (upstream_b,) = settle(upstream_b, mlp_parts[l])
            upstream_chunks = gather_rows(upstream_b)
        row_sums[l] = (sums_one, sums_two)

    sources = [mlp_parts[0]]
    for l in range(1, depth):
        sources += [mlp_parts[l], attn_parts[l]]
    blocks = 3 * depth - 1
    (stacked,) = kernel_call(
        functools.partial(fetch_kernel, len(sources)),
        [((blocks * width_own, hidden), bf16)],
        *[Far(v) for v in sources],
        name="fetch",
        after=(upstream_b,),
        scratch=[DMA((blocks,))],
    )
    own_term, *other_terms = attn_grads
    other_terms = [shift_z(term, d + 1) for d, term in enumerate(other_terms)]
    crossed = swap_x(stacked)
    others = (swap_y(upstream), swap_y(outputs_own))
    part, mine, pair = kernel_call(
        functools.partial(shard_sum_kernel, depth),
        [
            ((width_own, 4 * feats), bf16),
            ((24, width_own), f32),
            ((2 * blocks * width_own, hidden), bf16),
        ],
        Far(own_term),
        stacked,
        crossed,
        *other_terms,
        name="shard_sum",
        after=others,
        scratch=[pltpu.VMEM(own_term.shape, bf16), DMA((3,))],
    )
    if outer > 1:
        part = lax.psum(part, "ctx", axis_index_groups=outer_groups)
    mine, last_pair = kernel_call(
        functools.partial(vector_plane_kernel, depth),
        [((32, width_own), f32), ((2 * width_own, 4 * feats), bf16)],
        mine,
        swap_xy(mine),
        swap_x(mine),
        swap_y(mine),
        part,
        swap_x(part),
        name="vector_plane",
    )
    pieces = [last_pair, swap_core(last_pair), pair, swap_core(pair)]
    grad_gains, grad_shifts, grad_fc1_bias, grad_qv_bias = kernel_call(
        functools.partial(vector_place_kernel, depth, head_dim),
        [
            (norm_gains.shape, f32),
            (shifts.shape, f32),
            (fc1_bias.shape, f32),
            (qv_bias.shape, f32),
        ],
        mine,
        swap_core(mine),
        name="vector_place",
    )
    grad_inputs, outputs = (
        kernel_call(
            place_rows_kernel,
            [saved(inputs.shape, f32)],
            own,
            other,
            name="place_rows",
            scratch=[DMA((2,))],
        )[0]
        for own, other in zip((upstream, outputs_own), others)
    )
    placed = kernel_call(
        functools.partial(place_kernel, depth, hidden, feats),
        [saved(v.shape, f32) for v in (w_qkv, w_out, w_fc1, w_fc2)],
        *pieces,
        name="place",
        limit=24,
        scratch=[
            pltpu.VMEM((depth, GROUP, width_own, hidden), f32),
            pltpu.VMEM((depth, GROUP, hidden, width_own), f32),
            pltpu.VMEM((depth, GROUP, 3, width_own, feats), f32),
            pltpu.VMEM((depth, GROUP, feats, width_own), f32),
            DMA((16 * depth,)),
        ],
    )
    return (
        outputs,
        grad_inputs,
        grad_gains,
        grad_shifts,
        grad_qv_bias,
        grad_fc1_bias,
        *placed,
    )


def solution(mesh):
    rows = P("fsdp", "ctx", None)
    params = (
        P(None, None, "fsdp"),
        P(None, None, "fsdp"),
        P(None, None, "tp", "fsdp"),
        P(None, "tp", "fsdp"),
        P(None, None, "fsdp", "tp"),
        P(None, "tp", "fsdp"),
        P(None, "fsdp", "tp"),
        P(None, "tp", "fsdp"),
    )
    return jax.shard_map(
        per_device,
        mesh=mesh,
        in_specs=(rows, P("fsdp", None), rows) + params,
        out_specs=(rows, rows) + params,
        check_vma=False,
    )
```

```python
import functools
import math

import jax
import jax.numpy as jnp
from jax import lax
from jax.experimental import pallas as pl
from jax.experimental.pallas import tpu as pltpu
from jax.sharding import PartitionSpec as P

NORM_EPSILON = 1e-06
MASK_FILL = -1e30
ROOT_HALF = 0.7071067811865476
INV_ROOT_TAU = 0.3989422804014327
GROUP = 4
ORDER = (0, 5, 4, 1, 2, 7, 6, 3)
CHIPS = 4

bf16 = jnp.bfloat16
f32 = jnp.float32
VMEM = pl.BlockSpec(memory_space=pltpu.VMEM)
SMEM = pl.BlockSpec(memory_space=pltpu.SMEM)
HBM = pl.BlockSpec(memory_space=pltpu.HBM)
DMA = pltpu.SemaphoreType.DMA
TOKEN = ((8, 128), f32)


def dot(a, b):
    return lax.dot_general(a, b, (((1,), (0,)), ((), ())), preferred_element_type=f32)


def dot_nt(a, b):
    return lax.dot_general(a, b, (((1,), (1,)), ((), ())), preferred_element_type=f32)


def dot_tn(a, b):
    return lax.dot_general(a, b, (((0,), (0,)), ((), ())), preferred_element_type=f32)


class Far:
    def __init__(self, value):
        self.value = value


class Anywhere:
    def __init__(self, value):
        self.value = value


class Scalars:
    def __init__(self, value):
        self.value = value


def saved(shape, dtype):
    return pltpu.HBM(shape, dtype)


def kernel_call(body, outs, *args, name, limit=12, scratch=(), after=(), aliases=None, us=0):
    values, specs = [], []
    for arg in (*args, *after):
        if isinstance(arg, Far):
            values.append(pltpu.with_memory_space_constraint(arg.value, pltpu.HBM))
            specs.append(HBM)
        elif isinstance(arg, Anywhere):
            values.append(arg.value)
            specs.append(pl.BlockSpec(memory_space=pl.ANY))
        elif isinstance(arg, Scalars):
            values.append(arg.value)
            specs.append(SMEM)
        else:
            values.append(arg)
            specs.append(VMEM)
    first, last = len(args), len(args) + len(after)

    def run(*refs):
        body(*refs[:first], *refs[last:])

    out_shape, out_specs = [], []
    for out in outs:
        if isinstance(out, tuple):
            out_shape.append(jax.ShapeDtypeStruct(*out))
            out_specs.append(VMEM)
        else:
            out_shape.append(out)
            out_specs.append(HBM)
    return pl.pallas_call(
        run,
        out_shape=out_shape,
        in_specs=specs,
        out_specs=out_specs,
        scratch_shapes=list(scratch),
        input_output_aliases=aliases or {},
        compiler_params=pltpu.CompilerParams(vmem_limit_bytes=limit << 20),
        cost_estimate=pl.CostEstimate(flops=us * 10**9, bytes_accessed=0, transcendentals=0),
        name=name,
    )(*values)


def start_copies(pairs, sems):
    copies = [
        pltpu.make_async_copy(source, target, sems.at[k])
        for k, (source, target) in enumerate(pairs)
    ]
    for copy in copies:
        copy.start()
    return copies


def row_mean(value):
    return jnp.mean(value, axis=-1, keepdims=True)


def normalize(values):
    center = values - row_mean(values)
    inverse = lax.rsqrt(row_mean(center * center) + NORM_EPSILON)
    return center * inverse, inverse


def lanes_of(head, head_dim, width):
    lane = lax.broadcasted_iota(jnp.int32, (1, width), 1)
    return (lane >= head * head_dim) & (lane < (head + 1) * head_dim)


def assemble(chunks, target):
    rows = chunks[0].shape[0]
    for k, chunk in enumerate(chunks):
        target[k * rows : (k + 1) * rows, :] = chunk[...]


def only(flag, value):
    return jnp.where(flag, value, jnp.zeros_like(value))


def shards(weights):
    if len(weights) == 1:
        rows = weights[0].shape[0]
        return [(pl.ds(0, rows), weights[0])]
    count = len(weights)
    rows = weights[0].shape[0]
    f = lax.axis_index("fsdp")
    found = []
    for d, ref in enumerate(weights):
        place = lax.rem(f + (count - d), count)
        found.append((pl.ds(pl.multiple_of(place * rows, rows), rows), ref))
    return found


def pack_attn_kernel(layer, feats, qkv_hbm, out_hbm, packed_ref, token, qkv, out, sems):
    ci = lax.rem(lax.axis_index("ctx"), GROUP)
    span = pl.ds(pl.multiple_of(ci * feats, feats), feats)
    copies = start_copies(
        [(qkv_hbm.at[layer, :, :, span], qkv), (out_hbm.at[layer, span, :], out)], sems
    )
    copies[0].wait()
    for k in range(3):
        packed_ref[:, k * feats : (k + 1) * feats] = qkv[k]
    copies[1].wait()
    packed_ref[:, 3 * feats :] = out[...].T
    token[...] = jnp.zeros_like(token)


def pack_mlp_kernel(layer, hidden, fc1_hbm, fc2_hbm, packed_ref, token, fc1, fc2, sems):
    ci = lax.rem(lax.axis_index("ctx"), GROUP)
    span = pl.ds(pl.multiple_of(ci * hidden, hidden), hidden)
    copies = start_copies(
        [(fc1_hbm.at[layer, :, span], fc1), (fc2_hbm.at[layer, span, :], fc2)], sems
    )
    copies[0].wait()
    packed_ref[:, :hidden] = fc1[...]
    copies[1].wait()
    packed_ref[:, hidden:] = fc2[...].T
    token[...] = jnp.zeros_like(token)


def prep_upstream_kernel(tp, outer, lengths, cotangent_hbm,
                         upstream_hbm, upstream_b_ref, usable_ref, mask_ref,
                         rows_in, upstream_ref, sems):
    rows = rows_in.shape[0]
    c = lax.axis_index("ctx")
    t = lax.axis_index("tp")
    place = lax.rem(c, GROUP) * tp + t
    start = pl.multiple_of(t * rows, rows)
    copies = start_copies(
        [(cotangent_hbm.at[0, pl.ds(start, rows), :], rows_in)], sems.at[pl.ds(0, 1)]
    )
    lane = lax.broadcasted_iota(jnp.int32, usable_ref.shape, 1)
    limit = jnp.zeros(usable_ref.shape, jnp.int32)
    for o in range(outer):
        for k, d in enumerate(ORDER):
            source = place ^ d
            first_lane = (o * len(ORDER) + k) * rows
            count = lengths[0, o * GROUP + lax.div(source, tp)] - lax.rem(source, tp) * rows
            limit = jnp.where(lane >= first_lane, first_lane + jnp.clip(count, 0, rows), limit)
    usable_ref[...] = jnp.where(lane < limit, 1.0, 0.0)
    row = lax.broadcasted_iota(jnp.int32, mask_ref.shape, 0)
    mask = jnp.where(row + start < lengths[0, c], 1.0, 0.0)
    mask_ref[...] = mask
    copies[0].wait()
    upstream = rows_in[...] * mask[:, 0:1]
    upstream_ref[...] = upstream
    sent = start_copies([(upstream_ref, upstream_hbm)], sems.at[pl.ds(1, 1)])
    upstream_b_ref[...] = upstream.astype(bf16)
    sent[0].wait()


def prep_first_kernel(depth, inputs_hbm, vecs, stream_ref, first_ref, sems):
    rows = stream_ref.shape[0]
    start = pl.multiple_of(lax.axis_index("tp") * rows, rows)
    copies = start_copies([(inputs_hbm.at[0, pl.ds(start, rows), :], stream_ref)], sems)
    copies[0].wait()
    normed, _ = normalize(stream_ref[...])
    shift = vecs[2 * depth : 2 * depth + 1, :]
    first_ref[...] = (normed * vecs[0:1, :] + shift).astype(bf16)


def keep_rows_kernel(*refs):
    chunks, (near_hbm, far_hbm, token, near, far, sems) = refs[:8], refs[8:]
    assemble(chunks[:4], near)
    assemble(chunks[4:], far)
    for copy in start_copies([(near, near_hbm), (far, far_hbm)], sems):
        copy.wait()
    token[...] = jnp.zeros_like(token)


def qkv_kernel(feats, weight_count, *refs):
    c0, c1, c2, c3, *rest = refs
    weights = rest[:weight_count]
    bias, qkv_ref, x = rest[weight_count:]
    assemble((c0, c1, c2, c3), x)
    qkv = sum(dot(x[:, span], w[:, : 3 * feats]) for span, w in shards(weights))
    qkv_ref[:, :feats] = (qkv[:, :feats] + bias[0:1, :]).astype(bf16)
    qkv_ref[:, feats : 2 * feats] = qkv[:, feats : 2 * feats].astype(bf16)
    qkv_ref[:, 2 * feats :] = (qkv[:, 2 * feats :] + bias[1:2, :]).astype(bf16)


def attn_kernel(feats, heads, weight_count, part_count, keep_count, tile, *refs):
    q_ref, *rest = refs
    parts = rest[:part_count]
    weights = rest[part_count : part_count + weight_count]
    rest = rest[part_count + weight_count :]
    usable, *rest = rest
    kept, rest = rest[:keep_count], rest[keep_count:]
    partial_ref, attended_hbm, norm_hbm, *rest = rest
    kept_hbm, rest = rest[:keep_count], rest[keep_count:]
    keys, values, attended_ref, norm_ref, sems = rest
    head_dim = feats // heads
    scale = 1.0 / math.sqrt(head_dim)
    copies = start_copies(list(zip(kept, kept_hbm)), sems)
    first = 0
    for part in parts:
        rows, width = part.shape
        keys[first : first + rows, :] = part[:, width - 2 * feats : width - feats]
        values[first : first + rows, :] = part[:, width - feats :]
        first += rows
    keep = usable[...] > 0.5
    rows = q_ref.shape[0]
    for first in range(0, rows, tile):
        span = slice(first, first + tile)
        q = q_ref[span, :feats]
        attended = None
        for h in range(heads):
            own = lanes_of(h, head_dim, feats)
            scores = dot_nt(only(own, q), keys[...]) * scale
            scores = jnp.where(keep, scores, MASK_FILL)
            highest = jnp.max(scores, axis=-1, keepdims=True)
            raised = jnp.exp(scores - highest)
            total = jnp.sum(raised, axis=-1, keepdims=True)
            soft = (raised * (1.0 / total)).astype(bf16)
            result = dot(soft, values[...])
            log_norm = jnp.broadcast_to(highest + jnp.log(total), (tile, feats))
            if attended is None:
                attended, norms = result, log_norm
            else:
                attended = jnp.where(own, result, attended)
                norms = jnp.where(own, log_norm, norms)
        attended_ref[span, :] = attended.astype(bf16)
        norm_ref[span, :] = norms
    copies += start_copies(
        [(attended_ref, attended_hbm), (norm_ref, norm_hbm)],
        sems.at[pl.ds(keep_count, 2)],
    )
    for span, w in shards(weights):
        partial_ref[:, span] = dot_nt(attended_ref[...], w[:, 3 * feats :]).astype(bf16)
    for copy in copies:
        copy.wait()


def core_sum_kernel(count, *refs):
    pairs, owns = refs[: 2 * count], refs[2 * count : 3 * count]
    peers = refs[3 * count :]
    rows = owns[0].shape[0]
    for j in range(count):
        near, far = pairs[2 * j], pairs[2 * j + 1]
        for k in range(1 + len(peers)):
            span = slice(k * rows, (k + 1) * rows)
            total = near[span, :].astype(f32) + far[span, :].astype(f32)
            if k == 0:
                owns[j][...] = total
            else:
                peers[k - 1][j * rows : (j + 1) * rows, :] = total.astype(bf16)


def total_of(own, xy, x, y, part=0):
    rows = own.shape[0]
    span = slice(part * rows, (part + 1) * rows)
    return (
        own[...] + y[span, :].astype(f32) + x[span, :].astype(f32) + xy[span, :].astype(f32)
    )


def sum_norm_kernel(bias_row, gain_row, shift_row, own, xy, x, y, residual_hbm, vecs,
                    stream_ref, normed_ref, residual, sems):
    copies = start_copies([(residual_hbm, residual)], sems)
    total = total_of(own, xy, x, y) + vecs[bias_row : bias_row + 1, :]
    copies[0].wait()
    stream = residual[...] + total
    stream_ref[...] = stream
    normed, _ = normalize(stream)
    gain = vecs[gain_row : gain_row + 1, :]
    normed_ref[...] = (normed * gain + vecs[shift_row : shift_row + 1, :]).astype(bf16)


def sum_out_kernel(bias_row, own, xy, x, y, residual_hbm, vecs, mask, out_hbm, token,
                   residual, out_ref, sems):
    copies = start_copies([(residual_hbm, residual)], sems.at[pl.ds(0, 1)])
    total = total_of(own, xy, x, y, 1) + vecs[bias_row : bias_row + 1, :]
    copies[0].wait()
    out_ref[...] = (residual[...] + total) * mask[:, 0:1]
    token[...] = jnp.zeros_like(token)
    for copy in start_copies([(out_ref, out_hbm)], sems.at[pl.ds(1, 1)]):
        copy.wait()


def mlp_kernel(hidden, keep_count, saves, load_count, c0, c1, c2, c3, w, bias, *refs):
    kept, rest = refs[:keep_count], refs[keep_count:]
    sources, rest = rest[: max(0, load_count - 1)], rest[max(0, load_count - 1) :]
    partial_ref, x_out, act_out, slope_out, *rest = rest
    kept_hbm, rest = rest[:keep_count], rest[keep_count:]
    loaded = []
    if load_count:
        w_ref, *targets = rest[:load_count]
        *rest, load_sems, chunk_sems = rest[load_count:]
        rows = c0.shape[0]
        chunks = start_copies(
            [(c, x_out.at[pl.ds(k * rows, rows), :]) for k, c in enumerate((c0, c1, c2, c3))],
            chunk_sems,
        )
        spans = (pl.ds(0, hidden), pl.ds(hidden, hidden))
        loaded = start_copies(
            [(w.at[:, c], w_ref.at[:, c]) for c in spans] + list(zip(sources, targets)), load_sems
        )
        w = w_ref
    if saves:
        x, act_ref, slope_ref, sems = rest
    else:
        x, act_ref, slope_ref = x_out, act_out, slope_out
        (sems,) = rest
    copies = start_copies(list(zip(kept, kept_hbm)), sems)
    if load_count:
        for chunk in chunks:
            chunk.wait()
    else:
        assemble((c0, c1, c2, c3), x)
    if saves:
        copies += start_copies([(x, x_out)], sems.at[pl.ds(keep_count, 1)])
    block = hidden // 2
    if load_count:
        loaded[0].wait()
    for k in range(2):
        span = slice(k * block, (k + 1) * block)
        pre = dot(x[...], w[:, span]) + bias[:, span]
        cdf = 0.5 * (1.0 + lax.erf(pre * ROOT_HALF))
        density = jnp.exp(-0.5 * pre * pre) * INV_ROOT_TAU
        slope_ref[k] = cdf + pre * density
        act_ref[:, span] = (pre * cdf).astype(bf16)
        if saves:
            copies += start_copies(
                [(slope_ref.at[k], slope_out.at[k])], sems.at[pl.ds(1 + keep_count + k, 1)]
            )
    if saves:
        copies += start_copies([(act_ref, act_out)], sems.at[pl.ds(3 + keep_count, 1)])
    if load_count:
        loaded[1].wait()
    partial_ref[...] = dot_nt(act_ref[...], w[:, hidden:]).astype(bf16)
    for copy in copies + loaded[2:]:
        copy.wait()


def mlp_back_kernel(hidden, chunk_count, *refs):
    chunks, (w, slope, *rest) = refs[:chunk_count], refs[chunk_count:]
    partial_ref, grad_ref, sum_hbm, x, sum_ref, sems = rest
    assemble(chunks, x)
    grad = dot(x[...], w[:, hidden:])
    block = hidden // 2
    for k in range(2):
        span = slice(k * block, (k + 1) * block)
        part = grad[:, span] * slope[k]
        grad_ref[:, span] = part.astype(bf16)
        sum_ref[:, span] = jnp.sum(part, axis=0, keepdims=True)
    sent = start_copies([(sum_ref, sum_hbm)], sems)
    partial_ref[...] = dot_nt(grad_ref[...], w[:, :hidden]).astype(bf16)
    sent[0].wait()


def mlp_grad_kernel(hidden, keep_count, second_near, second_far, act_near, act_far,
                    up_near, up_far, grad_near, grad_far, *refs):
    kept, refs = refs[:keep_count], refs[keep_count:]
    out_hbm, *refs = refs
    kept_hbm, (out_one, out_two, sems) = refs[:keep_count], refs[keep_count:]
    sent = start_copies(list(zip(kept, kept_hbm)), sems.at[pl.ds(2, keep_count)])
    total = dot_tn(up_near[...], act_near[...]) + dot_tn(up_far[...], act_far[...])
    out_two[...] = total.astype(bf16)
    sent += start_copies(
        [(out_two, out_hbm.at[:, pl.ds(hidden, hidden)])], sems.at[pl.ds(0, 1)]
    )
    total = dot_tn(second_near[...], grad_near[...]) + dot_tn(second_far[...], grad_far[...])
    out_one[...] = total.astype(bf16)
    sent += start_copies([(out_one, out_hbm.at[:, pl.ds(0, hidden)])], sems.at[pl.ds(1, 1)])
    for copy in sent:
        copy.wait()


def norm_back(upstream, values, gain):
    normed, inverse = normalize(values)
    scaled = upstream * gain
    back = inverse * (scaled - row_mean(scaled) - normed * row_mean(scaled * normed))
    gain_grad = jnp.sum(upstream * normed, axis=0, keepdims=True)
    return back, gain_grad, jnp.sum(upstream, axis=0, keepdims=True)


def norm_back_two_kernel(gain_row, own, xy, x, y, values, upstream, vecs,
                         grad_ref, grad_b_ref, sums_ref):
    total = total_of(own, xy, x, y)
    up = upstream[...]
    back, gain_grad, shift_grad = norm_back(
        total, values[...], vecs[gain_row : gain_row + 1, :]
    )
    grad = up + back
    grad_ref[...] = grad
    grad_b_ref[...] = grad.astype(bf16)
    sums_ref[0:1, :] = gain_grad
    sums_ref[1:2, :] = shift_grad
    sums_ref[2:3, :] = jnp.sum(grad, axis=0, keepdims=True)
    sums_ref[3:4, :] = jnp.sum(up, axis=0, keepdims=True)


def norm_back_one_kernel(gain_row, own, xy, x, y, values, upstream, vecs, mask,
                         grad_ref, grad_b_ref, sums_ref):
    total = total_of(own, xy, x, y)
    back, gain_grad, shift_grad = norm_back(
        total, values[...], vecs[gain_row : gain_row + 1, :]
    )
    grad = upstream[...] + back
    if mask is not None:
        grad = grad * mask[:, 0:1]
    grad_ref[...] = grad
    grad_b_ref[...] = grad.astype(bf16)
    sums_ref[0:1, :] = gain_grad
    sums_ref[1:2, :] = shift_grad


def attn_back_kernel(feats, heads, weight_count, part_count, tile, carried, *refs):
    c0, c1, c2, c3, *rest = refs
    weights, rest = rest[:weight_count], rest[weight_count:]
    usable, qkv, attended, norms, *rest = rest
    parts, rest = rest[:part_count], rest[part_count:]
    if carried:
        keys_before, values_before, *rest = rest
    x, grad_q, grad_k, grad_v, pairs, grad_att = rest
    head_dim = feats // heads
    scale = 1.0 / math.sqrt(head_dim)
    first = 0
    for part in parts:
        rows, width = part.shape
        pairs[first : first + rows, :] = part[:, width - 2 * feats :]
        first += rows
    assemble((c0, c1, c2, c3), x)
    grad_att[...] = sum(
        dot(x[:, span], w[:, 3 * feats :]) for span, w in shards(weights)
    ).astype(bf16)
    keep = usable[...] > 0.5
    rows = qkv.shape[0]
    if carried:
        sum_k, sum_v = keys_before[...], values_before[...]
    else:
        sum_k = jnp.zeros(grad_k.shape, f32)
        sum_v = jnp.zeros(grad_v.shape, f32)
    keys, values = pairs[:, :feats], pairs[:, feats:]
    for first in range(0, rows, tile):
        span = slice(first, first + tile)
        q = qkv[span, :feats]
        ga = grad_att[span, :]
        products = ga.astype(f32) * attended[span, :].astype(f32)
        gq = None
        for h in range(heads):
            own = lanes_of(h, head_dim, feats)
            q_h = only(own, q)
            ga_h = only(own, ga)
            row_dots = jnp.sum(only(own, products), axis=-1, keepdims=True)
            scores = dot_nt(q_h, keys) * scale
            scores = jnp.where(keep, scores, MASK_FILL)
            soft = jnp.exp(scores - norms[span, h * head_dim : h * head_dim + 1])
            grad_soft = dot_nt(ga_h, values)
            grad_scores = (soft * (grad_soft - row_dots)).astype(bf16)
            part = dot(grad_scores, keys)
            gq = part if gq is None else jnp.where(own, part, gq)
            sum_k = sum_k + dot_tn(grad_scores, q_h) * scale
            sum_v = sum_v + dot_tn(soft.astype(bf16), ga_h)
        grad_q[span, :] = gq * scale
    grad_k[...] = sum_k
    grad_v[...] = sum_v


def project_kernel(feats, first, weight_count, gq, gk, gv, *refs):
    weights, (partial_ref, packed) = refs[:weight_count], refs[weight_count:]
    rows = gq.shape[0]
    span = slice(first, first + rows)
    packed[:, :feats] = gq[...].astype(bf16)
    packed[:, feats : 2 * feats] = gk[span, :].astype(bf16)
    packed[:, 2 * feats :] = gv[span, :].astype(bf16)
    for columns, w in shards(weights):
        partial_ref[:, columns] = dot_nt(packed[...], w[:, : 3 * feats]).astype(bf16)


def attn_grad_kernel(feats, count, keep_count, first_near, first_far, att_near, att_far,
                     up_near, up_far, gq_near, gq_far, gk, gv, passed, lines, *refs):
    kept, refs = refs[:keep_count], refs[keep_count:]
    outs, refs = refs[:count], refs[count:]
    heads_hbm, passed_ref, *refs = refs
    kept_hbm, (packed, sums_ref, *staged, sems) = refs[:keep_count], refs[keep_count:]
    rows = up_near.shape[0]
    used = count + 2
    sent = start_copies(list(zip(kept, kept_hbm)), sems.at[pl.ds(used, keep_count)])
    passed_ref[...] = passed[...]
    packed[:rows, :feats] = gq_near[...].astype(bf16)
    packed[rows:, :feats] = gq_far[...].astype(bf16)
    packed[:, feats : 2 * feats] = gk[...].astype(bf16)
    packed[:, 2 * feats :] = gv[...].astype(bf16)
    sums_ref[0:1, :] = jnp.sum(gq_near[...], axis=0, keepdims=True) + jnp.sum(
        gq_far[...], axis=0, keepdims=True
    )
    sums_ref[1:2, :] = jnp.sum(gv[...], axis=0, keepdims=True)
    sent += start_copies([(sums_ref, heads_hbm)], sems.at[pl.ds(0, 1)])

    def out_part(span):
        return dot_tn(up_near[:, span], att_near[...]) + dot_tn(up_far[:, span], att_far[...])

    def qkv_part(span):
        return dot_tn(first_near[:, span], packed[:rows, :]) + dot_tn(
            first_far[:, span], packed[rows:, :]
        )

    if count == 1:
        out_one, out_two = staged
        whole = slice(None)
        out_two[...] = out_part(whole).astype(bf16)
        sent += start_copies(
            [(out_two, outs[0].at[:, pl.ds(3 * feats, feats)])], sems.at[pl.ds(1, 1)]
        )
        out_one[...] = qkv_part(whole).astype(bf16)
        sent += start_copies(
            [(out_one, outs[0].at[:, pl.ds(0, 3 * feats)])], sems.at[pl.ds(2, 1)]
        )
    else:
        (stage,) = staged
        below = lines.shape[1]
        width_own = outs[0].shape[0] - below
        for d in reversed(range(count)):
            place = lax.rem(lax.axis_index("fsdp") + d, count)
            span = pl.ds(pl.multiple_of(place * width_own, width_own), width_own)
            stage[d, :width_own, : 3 * feats] = qkv_part(span).astype(bf16)
            stage[d, :width_own, 3 * feats :] = out_part(span).astype(bf16)
            stage[d, width_own:, :] = lines[d]
            sent += start_copies([(stage.at[d], outs[d])], sems.at[pl.ds(1 + d, 1)])
    for copy in sent:
        copy.wait()


def settle_kernel(keep_count, after_count, passed, *refs):
    kept, refs = refs[:keep_count], refs[keep_count + after_count :]
    passed_ref, *kept_hbm, sems = refs
    copies = start_copies(list(zip(kept, kept_hbm)), sems)
    passed_ref[...] = passed[...]
    for copy in copies:
        copy.wait()


def fetch_kernel(count, *refs):
    sources, (target, sems) = refs[:count], refs[count:]
    columns = target.shape[1]
    moves = []
    row = 0
    for source in sources:
        rows = source.shape[0]
        for first in range(0, source.shape[1], columns):
            moves.append(
                (source.at[:, pl.ds(first, columns)], target.at[pl.ds(row, rows), :])
            )
            row += rows
    for copy in start_copies(moves, sems):
        copy.wait()


def shard_sum_kernel(depth, own_hbm, stacked, crossed, *refs):
    *others, part_ref, mine_ref, pair_ref, own, sems = refs
    count = stacked.shape[0]
    first, *copies = start_copies(
        [
            (own_hbm, own),
            (stacked, pair_ref.at[pl.ds(0, count), :]),
            (crossed, pair_ref.at[pl.ds(count, count), :]),
        ],
        sems,
    )
    first.wait()
    rows, width = part_ref.shape[0], mine_ref.shape[1]
    terms = [ref[...].astype(f32) for ref in (own, *others)]
    total = terms[0]
    for term in terms[1:]:
        total = total + term
    part_ref[...] = total[:rows, :].astype(bf16)
    lines = total[rows:, :width] + total[rows:, width:]
    mine_ref[: 6 * depth, :] = lines[: 6 * depth, :]
    for k in range(mine_ref.shape[0] - 16):
        mine_ref[16 + k : 17 + k, :] = lines[6 * depth + k : 6 * depth + k + 1, :]
    for copy in copies:
        copy.wait()


def place_kernel(depth, hidden, feats, here, sibling, *refs):
    qkv_hbm, out_hbm, fc1_hbm, fc2_hbm, token, fc1, fc2, qkv, out, sems = refs
    token[...] = jnp.zeros_like(token)
    ci = lax.rem(lax.axis_index("ctx"), GROUP)
    rows = fc1.shape[2]
    count = here.shape[0] // 2
    copies = []

    def send(source, target):
        copies.extend(start_copies([(source, target)], sems.at[pl.ds(len(copies), 1)]))

    for k in range(GROUP):
        stacked = (here, sibling)[k % 2].at[pl.ds(k // 2 * count, count), :]
        wide = pl.ds(pl.multiple_of((ci ^ k) * hidden, hidden), hidden)
        narrow = pl.ds(pl.multiple_of((ci ^ k) * feats, feats), feats)
        for l in range(depth):
            first = 0 if l == 0 else (3 * l - 1) * rows
            fc1[l, k] = stacked[first : first + rows, :].astype(f32)
            send(fc1.at[l, k], fc1_hbm.at[l, :, wide])
            fc2[l, k] = stacked[first + rows : first + 2 * rows, :].T.astype(f32)
            send(fc2.at[l, k], fc2_hbm.at[l, wide, :])
            if l > 0:
                piece = stacked.at[pl.ds(first + 2 * rows, rows), :]
                for j in range(3):
                    qkv[l - 1, k, j] = piece[:, j * feats : (j + 1) * feats].astype(f32)
                send(qkv.at[l - 1, k], qkv_hbm.at[l, :, :, narrow])
                out[l - 1, k] = piece[:, 3 * feats :].T.astype(f32)
                send(out.at[l - 1, k], out_hbm.at[l, narrow, :])
    for copy in copies:
        copy.wait()


def place_last_kernel(feats, here, sibling, qkv_in, out_in, qkv_hbm, out_hbm, qkv, out, sems):
    ci = lax.rem(lax.axis_index("ctx"), GROUP)
    rows = here.shape[0] // 2
    copies = []
    for k in range(GROUP):
        piece = (here, sibling)[k % 2].at[pl.ds(k // 2 * rows, rows), :]
        span = pl.ds(pl.multiple_of((ci ^ k) * feats, feats), feats)
        for j in range(3):
            qkv[k, j] = piece[:, j * feats : (j + 1) * feats].astype(f32)
        copies += start_copies(
            [(qkv.at[k], qkv_hbm.at[0, :, :, span])], sems.at[pl.ds(2 * k, 1)]
        )
        out[k] = piece[:, 3 * feats :].T.astype(f32)
        copies += start_copies(
            [(out.at[k], out_hbm.at[0, span, :])], sems.at[pl.ds(2 * k + 1, 1)]
        )
    for copy in copies:
        copy.wait()


def vector_pack_kernel(depth, one_now, gq_near, gq_far, gv, *refs):
    count = 5 * depth - 2
    out_ref, *found, sems = refs[count:]
    copies = start_copies(list(zip(refs[:count], found)), sems)
    out_ref[...] = jnp.zeros_like(out_ref)
    feats = gv.shape[1]
    head_now = [
        jnp.sum(gq_near[...], axis=0, keepdims=True) + jnp.sum(gq_far[...], axis=0, keepdims=True),
        jnp.sum(gv[...], axis=0, keepdims=True),
    ]
    for copy in copies:
        copy.wait()
    for l in range(depth):
        if l == 0:
            one, (two, unit_near, unit_far) = one_now, found[:3]
            heads = head_now
        else:
            one, two, unit_near, unit_far, head = found[5 * l - 2 : 5 * l + 3]
            heads = [head[0:1, :], head[1:2, :]]
        out_ref[6 * l : 6 * l + 1, :] = one[0:1, :]
        out_ref[6 * l + 1 : 6 * l + 2, :] = two[0:1, :]
        out_ref[6 * l + 2 : 6 * l + 3, :] = one[1:2, :]
        out_ref[6 * l + 3 : 6 * l + 6, :] = two[1:4, :]
        units = unit_near.shape[1]
        row = 6 * depth
        out_ref[row : row + 1, l * units : (l + 1) * units] = unit_near[...] + unit_far[...]
        for j in range(2):
            start = (2 * l + j) * feats
            out_ref[row + 1 : row + 2, start : start + feats] = heads[j]


def vector_lines_kernel(depth, width_own, packed, lines_ref):
    count = lines_ref.shape[0]
    f = lax.axis_index("fsdp")
    total = packed[...]
    high = total.astype(bf16).astype(f32)
    low = total - high
    lines_ref[...] = jnp.zeros_like(lines_ref)
    last = 6 * depth
    for k, value in enumerate((high, low)):
        lanes = slice(k * width_own, (k + 1) * width_own)
        columns = [value[:, a * width_own : (a + 1) * width_own] for a in range(count)]
        for d in range(count):
            mine = columns[0]
            for a in range(1, count):
                mine = jnp.where(lax.rem(f + d, count) == a, columns[a], mine)
            rows = [mine[:last, :]]
            for r in range(2):
                for a in range(count):
                    rows.append(columns[a][last + r : last + r + 1, :])
            rows.append(jnp.zeros((lines_ref.shape[1] - last - 2 * count, width_own), f32))
            lines_ref[d, :, lanes] = jnp.concatenate(rows, axis=0).astype(bf16)


def vector_plane_kernel(depth, own, xy, x, y, part, part_x, out_ref, pair_ref):
    last = 6 * depth
    rows = part.shape[0]
    pair_ref[:rows, :] = part[...]
    pair_ref[rows:, :] = part_x[...]
    out_ref[:last, :] = own[:last, :] + xy[:last, :] + x[:last, :] + y[:last, :]
    out_ref[16:24, :] = own[16:24, :]
    out_ref[24:32, :] = x[16:24, :]


def vector_place_kernel(depth, head_dim, own, far, gains_ref, shifts_ref, unit_ref, heads_ref):
    total = own[: 6 * depth, :] + far[: 6 * depth, :]
    for l in range(depth):
        gains_ref[l] = total[6 * l : 6 * l + 2, :]
        shifts_ref[l] = total[6 * l + 2 : 6 * l + 6, :]
    pieces = (own[16:24, :], far[16:24, :], own[24:32, :], far[24:32, :])
    ci = lax.rem(lax.axis_index("ctx"), GROUP)
    f = lax.axis_index("fsdp")

    def of_place(c):
        k = ci ^ c
        found = pieces[0]
        for j in range(1, GROUP):
            found = jnp.where(k == j, pieces[j], found)
        return found

    width_own = own.shape[1]
    units = of_place(f)
    parts = unit_ref.shape[2] // width_own
    for l in range(depth):
        for j in range(parts):
            row = l * parts + j
            unit_ref[l, :, j * width_own : (j + 1) * width_own] = units[row : row + 1, :]
    head_own = heads_ref.shape[3]
    heads = heads_ref.shape[2] // GROUP
    for c in range(GROUP):
        found = of_place(c)
        for l in range(depth):
            for j in range(2):
                for h in range(heads):
                    first = ((2 * l + j) * heads + h) * head_dim
                    row, lane = 4 + first // width_own, first % width_own
                    value = found[row : row + 1, lane : lane + head_own]
                    for a in range(1, head_dim // head_own):
                        start = lane + a * head_own
                        value = jnp.where(
                            f == a, found[row : row + 1, start : start + head_own], value
                        )
                    heads_ref[l, j, c * heads + h : c * heads + h + 1, :] = value


def place_rows_kernel(own, other, out_hbm, sems):
    rows = own.shape[0]
    start = pl.multiple_of(lax.axis_index("tp") * rows, rows)
    copies = start_copies(
        [
            (own, out_hbm.at[0, pl.ds(start, rows), :]),
            (other, out_hbm.at[0, pl.ds(pl.multiple_of(rows - start, rows), rows), :]),
        ],
        sems,
    )
    for copy in copies:
        copy.wait()


def per_device(
    inputs, lengths, cotangent, norm_gains, shifts, qv_bias, fc1_bias, w_qkv, w_out, w_fc1, w_fc2
):
    depth = w_qkv.shape[0]
    width_own = w_qkv.shape[2]
    fsdp = lax.axis_size("fsdp")
    tp = lax.axis_size("tp")
    ctx = lax.axis_size("ctx")
    outer = ctx // GROUP
    rows = inputs.shape[1] // tp
    half = rows * CHIPS
    all_rows = 2 * half
    head_own = qv_bias.shape[3]
    head_dim = head_own * fsdp
    heads = qv_bias.shape[2] // GROUP
    feats = heads * head_dim
    hidden = w_fc1.shape[2] // GROUP
    width = width_own * fsdp
    t = lax.axis_index("tp")
    f = lax.axis_index("fsdp")
    ci = lax.axis_index("ctx") % GROUP
    tile = half // 2
    attn_limit = 12 if outer == 1 else 48

    def swap_core(value):
        return lax.ppermute(value, "ctx", [(i, i ^ 1) for i in range(ctx)])

    def swap_x(value):
        return lax.ppermute(value, "ctx", [(i, i ^ 2) for i in range(ctx)])

    def swap_y(value):
        return lax.ppermute(value, "tp", [(i, i ^ 1) for i in range(tp)])

    def swap_xy(value):
        pairs = [
            (i * tp + k, (i ^ 2) * tp + (k ^ 1)) for i in range(ctx) for k in range(tp)
        ]
        return lax.ppermute(value, ("ctx", "tp"), pairs)

    def shift_z(value, d):
        return lax.ppermute(value, "fsdp", [(i, (i + d) % fsdp) for i in range(fsdp)])

    outer_groups = [[o * GROUP + i for o in range(outer)] for i in range(GROUP)]

    def gather_rows(own):
        near = (own, swap_xy(own), swap_x(own), swap_y(own))
        return near, tuple(swap_core(chunk) for chunk in near)

    def settle(value, there, *kept):
        return kernel_call(
            functools.partial(settle_kernel, len(kept), 1),
            [(value.shape, value.dtype)] + [saved(k.shape, k.dtype) for k in kept],
            value,
            *kept,
            Far(there),
            name="settle",
            scratch=[DMA((max(1, len(kept)),))],
        )

    def reduce_rows(*pairs, after=()):
        count = len(pairs)
        *owns, xy, x, y = kernel_call(
            functools.partial(core_sum_kernel, count),
            [((rows, width), f32)] * count + [((count * rows, width), bf16)] * 3,
            *[v for near, far in pairs for v in (near, swap_core(far))],
            name="core_sum",
            after=after,
        )
        peers = (swap_xy(xy), swap_x(x), swap_y(y))
        return [(own, *peers) for own in owns]

    def pack_attn(l, after):
        return kernel_call(
            functools.partial(pack_attn_kernel, l, feats),
            [((width_own, 4 * feats), bf16), TOKEN],
            Far(w_qkv),
            Far(w_out),
            name="pack_attn",
            after=after,
            scratch=[
                pltpu.VMEM((3, width_own, feats), bf16),
                pltpu.VMEM((feats, width_own), bf16),
                DMA((2,)),
            ],
        )

    def pack_mlp(l, after):
        return kernel_call(
            functools.partial(pack_mlp_kernel, l, hidden),
            [((width_own, 2 * hidden), bf16), TOKEN],
            Far(w_fc1),
            Far(w_fc2),
            name="pack_mlp",
            after=after,
            scratch=[
                pltpu.VMEM((width_own, hidden), bf16),
                pltpu.VMEM((hidden, width_own), bf16),
                DMA((2,)),
            ],
        )

    attn_w = []
    mlp_w = []
    token = None
    for l in range(depth):
        own, token = pack_attn(l, () if token is None else (token,))
        attn_w.append((lax.all_gather(own, "fsdp", axis=0, tiled=True),))
        own, token = pack_mlp(l, (token,))
        mlp_w.append(lax.all_gather(own, "fsdp", axis=0, tiled=True))
        if l == 0:
            pack_token = token

    qv_own = lax.dynamic_slice_in_dim(qv_bias, ci * heads, heads, axis=2)
    vec_rows = depth * 6
    c1_rows = depth * fc1_bias.shape[2] // width_own
    qv_own = qv_own.reshape(1, -1)
    small_own = jnp.concatenate(
        [
            norm_gains.reshape(-1, width_own),
            shifts.reshape(-1, width_own),
            fc1_bias.reshape(-1, width_own),
            jnp.pad(qv_own, ((0, 0), (0, width_own - qv_own.shape[1]))),
        ],
        axis=0,
    )
    shifted = [small_own] + [shift_z(small_own, d) for d in range(1, fsdp)]

    def shard(a):
        picked = shifted[0]
        for d in range(1, fsdp):
            picked = jnp.where((f - d) % fsdp == a, shifted[d], picked)
        return picked.astype(f32)

    small = [shard(a) for a in range(fsdp)]
    vecs = jnp.concatenate([s[:vec_rows] for s in small], axis=1)
    fc1_all = shard(ci)[vec_rows : vec_rows + c1_rows].reshape(depth, 1, hidden)
    qv_all = jnp.stack(
        [s[vec_rows + c1_rows, : qv_own.shape[1]].reshape(depth, 2, heads, head_own) for s in small],
        axis=3,
    ).reshape(depth, 2, feats)

    def gain_row(l, i):
        return 2 * l + i

    def shift_row(l, i):
        return 2 * depth + 4 * l + i

    key_rows = outer * all_rows
    row_f32 = ((rows, width), f32)
    row_bf16 = ((rows, width), bf16)
    upstream, upstream_b, usable, mask = kernel_call(
        functools.partial(prep_upstream_kernel, tp, outer),
        [saved((rows, width), f32), row_bf16, ((1, key_rows), f32), ((rows, 128), f32)],
        Scalars(lengths),
        Far(cotangent),
        name="prep_upstream",
        after=(pack_token,),
        scratch=[pltpu.VMEM((rows, width), f32), pltpu.VMEM((rows, width), f32), DMA((2,))],
    )
    near, far = gather_rows(upstream_b)
    half_x = pltpu.VMEM((half, width), bf16)
    *upstream_rows, upstream_token = kernel_call(
        keep_rows_kernel,
        [saved((half, width), bf16)] * 2 + [TOKEN],
        *near,
        *far,
        name="keep_rows",
        scratch=[half_x, half_x, DMA((2,))],
    )
    stream, first = kernel_call(
        functools.partial(prep_first_kernel, depth),
        [row_f32, row_bf16],
        Far(inputs),
        vecs,
        name="prep_first",
        scratch=[DMA((1,))],
    )
    first_chunks = gather_rows(first)

    partial_out = ((half, width), bf16)
    saved_all = []
    for l in range(depth):
        qkv = []
        first_x = []
        for side in (0, 1):
            qkv_half, x_half = kernel_call(
                functools.partial(qkv_kernel, feats, len(attn_w[l])),
                [((half, 3 * feats), bf16), ((half, width), bf16)],
                *first_chunks[side],
                *attn_w[l],
                qv_all[l],
                name="qkv",
                after=(upstream_token,) if l == 0 and side == 0 else (),
            )
            qkv.append(qkv_half)
            first_x.append(x_half)
        if outer > 1:
            pairs = jnp.concatenate([part[:, feats:] for part in qkv], axis=0)
            pairs = lax.all_gather(
                pairs, "ctx", axis=0, tiled=True, axis_index_groups=outer_groups
            )
            key_parts = (pairs,)
        else:
            key_parts = tuple(qkv)
        attn = [None, None]
        for side in (1, 0):
            kept = (first_x[side], qkv[side]) + ((stream,) if side == 1 else ())
            attn[side] = kernel_call(
                functools.partial(
                    attn_kernel, feats, heads, len(attn_w[l]), len(key_parts), len(kept), tile
                ),
                [partial_out, saved((half, feats), bf16), saved((half, feats), f32)]
                + [saved(k.shape, k.dtype) for k in kept],
                qkv[side],
                *key_parts,
                *attn_w[l],
                usable,
                *kept,
                name="attn",
                limit=attn_limit,
                scratch=[
                    pltpu.VMEM((key_rows, feats), bf16),
                    pltpu.VMEM((key_rows, feats), bf16),
                    pltpu.VMEM((half, feats), bf16),
                    pltpu.VMEM((half, feats), f32),
                    DMA((len(kept) + 2,)),
                ],
            )
        (sums,) = reduce_rows((attn[0][0], attn[1][0]))
        middle, second = kernel_call(
            functools.partial(sum_norm_kernel, shift_row(l, 2), gain_row(l, 1), shift_row(l, 1)),
            [row_f32, row_bf16],
            *sums,
            Far(attn[1][5]),
            vecs,
            name="sum_norm",
            scratch=[pltpu.VMEM((rows, width), f32), DMA((1,))],
        )
        second_chunks = gather_rows(second)
        mlp = [None, None]
        for side in (1, 0):
            kept = (middle,) if side == 1 else ()
            saves = l + 1 < depth
            loads = (mlp_w[l], *upstream_rows) if not saves and side == 1 else ()
            shapes = [
                ((half, width), bf16),
                ((half, hidden), bf16),
                ((2, half, hidden // 2), f32),
            ]
            mlp[side] = kernel_call(
                functools.partial(mlp_kernel, hidden, len(kept), saves, len(loads)),
                [partial_out]
                + [saved(*shape) if saves else shape for shape in shapes]
                + [saved(k.shape, k.dtype) for k in kept]
                + [(v.shape, v.dtype) for v in loads],
                *[Anywhere(c) if loads else c for c in second_chunks[side]],
                Far(mlp_w[l]) if loads else mlp_w[l],
                fc1_all[l],
                *kept,
                *[Far(v) for v in loads[1:]],
                name="mlp",
                scratch=[pltpu.VMEM(*shape) for shape in shapes if saves]
                + [DMA((4 + len(kept),))]
                + ([DMA((len(loads) + 1,)), DMA((CHIPS,))] if loads else []),
            )
            if loads:
                *mlp[side], mlp_w[l], near, far = mlp[side]
                upstream_chunks = [(near,), (far,)]
        saved_all.append((attn, pairs if outer > 1 else None, mlp))
        if l + 1 < depth:
            (sums,) = reduce_rows((mlp[0][0], mlp[1][0]))
            stream, first = kernel_call(
                functools.partial(
                    sum_norm_kernel, shift_row(l, 3), gain_row(l + 1, 0), shift_row(l + 1, 0)
                ),
                [row_f32, row_bf16],
                *sums,
                Far(mlp[1][4]),
                vecs,
                name="sum_norm",
                scratch=[pltpu.VMEM((rows, width), f32), DMA((1,))],
            )
            first_chunks = gather_rows(first)

    def scatter_grads(grad):
        part = lax.psum_scatter(grad, "fsdp", scatter_dimension=0, tiled=True)
        if outer > 1:
            part = lax.psum(part, "ctx", axis_index_groups=outer_groups)
        return part

    row_sums = [None] * depth
    unit_sums = [None] * depth
    head_sums = [None] * depth
    mlp_parts = [None] * depth
    attn_parts = [None] * depth
    for l in reversed(range(depth)):
        attn, pairs, mlp = saved_all[l]
        back = [None, None]
        for side in (1, 0):
            back[side] = kernel_call(
                functools.partial(mlp_back_kernel, hidden, len(upstream_chunks[side])),
                [
                    partial_out,
                    ((half, hidden), bf16),
                    saved((1, hidden), f32),
                    ((half, width), bf16),
                ],
                *upstream_chunks[side],
                mlp_w[l],
                mlp[side][3],
                name="mlp_back",
                scratch=[pltpu.VMEM((1, hidden), f32), DMA((1,))],
            )
        kept = [back[0][0], back[1][0]]
        if l + 1 == depth:
            kept += [mlp[0][0], mlp[1][0]]
        mlp_grad, *kept = kernel_call(
            functools.partial(mlp_grad_kernel, hidden, len(kept)),
            [saved((width, 2 * hidden), bf16)] + [saved(k.shape, k.dtype) for k in kept],
            mlp[0][1],
            mlp[1][1],
            mlp[0][2],
            mlp[1][2],
            back[0][3],
            back[1][3],
            back[0][1],
            back[1][1],
            *kept,
            name="mlp_grad",
            scratch=[
                pltpu.VMEM((width, hidden), bf16),
                pltpu.VMEM((width, hidden), bf16),
                DMA((2 + len(kept),)),
            ],
        )
        mlp_parts[l] = scatter_grads(mlp_grad)
        sums, *output_sums = reduce_rows(*zip(kept[0::2], kept[1::2]))
        if l + 1 == depth:
            outputs_own, output_token = kernel_call(
                functools.partial(sum_out_kernel, shift_row(l, 3)),
                [saved((rows, width), f32), TOKEN],
                *output_sums[0],
                Far(mlp[1][4]),
                vecs,
                mask,
                name="sum_out",
                scratch=[pltpu.VMEM((rows, width), f32)] * 2 + [DMA((2,))],
            )
            after = (output_token,)
        else:
            after = ()
        unit_sums[l] = (back[0][2], back[1][2])
        grad_middle, middle_b, sums_two = kernel_call(
            functools.partial(norm_back_two_kernel, gain_row(l, 1)),
            [row_f32, row_bf16, ((4, width), f32)],
            *sums,
            mlp[1][4],
            upstream,
            vecs,
            name="norm_back_two",
            after=after,
        )
        if l + 1 < depth:
            middle_b, sums_two, grad_middle = settle(
                middle_b, attn_parts[l + 1], sums_two, grad_middle
            )
        middle_chunks = gather_rows(middle_b)
        grad_q = [None, None]
        middle_x = [None, None]
        carried = ()
        for side in (0, 1):
            key_parts = (pairs,) if outer > 1 else (attn[0][4], attn[1][4])
            middle_x[side], grad_q[side], *carried = kernel_call(
                functools.partial(
                    attn_back_kernel,
                    feats,
                    heads,
                    len(attn_w[l]),
                    len(key_parts),
                    tile,
                    len(carried) > 0,
                ),
                [
                    ((half, width), bf16),
                    ((half, feats), f32),
                    ((key_rows, feats), f32),
                    ((key_rows, feats), f32),
                ],
                *middle_chunks[side],
                *attn_w[l],
                usable,
                attn[side][4],
                attn[side][1],
                attn[side][2],
                *key_parts,
                *carried,
                name="attn_back",
                scratch=[
                    pltpu.VMEM((key_rows, 2 * feats), bf16),
                    pltpu.VMEM((half, feats), bf16),
                ],
                limit=attn_limit,
            )
        grad_k, grad_v = carried
        if outer > 1:
            grad_k, grad_v = (
                lax.psum_scatter(
                    v, "ctx", scatter_dimension=0, tiled=True, axis_index_groups=outer_groups
                )
                for v in (grad_k, grad_v)
            )

        def project(side, after):
            return kernel_call(
                functools.partial(project_kernel, feats, side * half, len(attn_w[l])),
                [partial_out],
                grad_q[side],
                grad_k,
                grad_v,
                *attn_w[l],
                name="project",
                after=after,
                scratch=[pltpu.VMEM((half, 3 * feats), bf16)],
            )[0]

        far_part = project(1, ())
        near_part = project(0, ())
        (sums,) = reduce_rows((near_part, far_part))
        body = functools.partial(norm_back_one_kernel, gain_row(l, 0))
        if l > 0:
            masked = ()
            body = lambda *refs, body=body: body(*refs[:7], None, *refs[7:])
        else:
            masked = (mask,)
        upstream, upstream_b, sums_one = kernel_call(
            body,
            [row_f32, row_bf16, ((2, width), f32)],
            *sums,
            attn[1][5],
            grad_middle,
            vecs,
            *masked,
            name="norm_back_one",
        )
        lines = ()
        if l == 0:
            terms = [sums_two, *unit_sums[0]]
            for k in range(1, depth):
                terms += [*row_sums[k], *unit_sums[k], head_sums[k]]
            packed = kernel_call(
                functools.partial(vector_pack_kernel, depth),
                [((6 * depth + 2, width), f32)],
                sums_one,
                *grad_q,
                grad_v,
                *[Far(v) for v in terms],
                name="vector_pack",
                scratch=[pltpu.VMEM(v.shape, f32) for v in terms] + [DMA((len(terms),))],
            )[0]
            if outer > 1:
                packed = lax.psum(packed, "ctx", axis_index_groups=outer_groups)
            lines = kernel_call(
                functools.partial(vector_lines_kernel, depth, width_own),
                [((fsdp, 32, 2 * width_own), bf16)],
                packed,
                name="vector_lines",
            )
        count = 1 if l > 0 else fsdp
        shapes = [((width, 3 * feats), bf16), ((width, feats), bf16)]
        if l == 0:
            shapes = [((fsdp, width_own + 32, 4 * feats), bf16)]
        kept = [sums_one, upstream] + ([sums_two] if l + 1 == depth else [])
        *attn_grads, head_sums[l], upstream_b, sums_one, upstream, sums_kept = [
            *kernel_call(
                functools.partial(attn_grad_kernel, feats, count, len(kept)),
                [saved((width if l > 0 else width_own + 32, 4 * feats), bf16)] * count
                + [saved((2, feats), f32), row_bf16]
                + [saved(k.shape, k.dtype) for k in kept],
                attn[0][3],
                attn[1][3],
                attn[0][1],
                attn[1][1],
                *middle_x,
                *grad_q,
                grad_k,
                grad_v,
                upstream_b,
                *(lines or (sums_one,)),
                *kept,
                name="attn_grad",
                scratch=[
                    pltpu.VMEM((all_rows, 3 * feats), bf16),
                    pltpu.VMEM((2, feats), f32),
                ]
                + [pltpu.VMEM(*shape) for shape in shapes]
                + [DMA((count + 2 + len(kept),))],
            ),
            sums_two,
        ][: count + 5]
        if l + 1 == depth:
            sums_two = sums_kept
        if l > 0:
            attn_parts[l] = scatter_grads(attn_grads[0])
            (upstream_b,) = settle(upstream_b, mlp_parts[l])
            upstream_chunks = gather_rows(upstream_b)
        row_sums[l] = (sums_one, sums_two)

    sources = [mlp_parts[0]]
    for l in range(1, depth):
        sources += [mlp_parts[l], attn_parts[l]]
    blocks = 3 * depth - 1
    (stacked,) = kernel_call(
        functools.partial(fetch_kernel, len(sources)),
        [((blocks * width_own, hidden), bf16)],
        *[Far(v) for v in sources],
        name="fetch",
        after=(upstream_b,),
        scratch=[DMA((blocks,))],
    )
    own_term, *other_terms = attn_grads
    other_terms = [shift_z(term, d + 1) for d, term in enumerate(other_terms)]
    crossed = swap_x(stacked)
    others = (swap_y(upstream), swap_y(outputs_own))
    part, mine, pair = kernel_call(
        functools.partial(shard_sum_kernel, depth),
        [
            ((width_own, 4 * feats), bf16),
            ((24, width_own), f32),
            ((2 * blocks * width_own, hidden), bf16),
        ],
        Far(own_term),
        stacked,
        crossed,
        *other_terms,
        name="shard_sum",
        after=others,
        scratch=[pltpu.VMEM(own_term.shape, bf16), DMA((3,))],
    )
    if outer > 1:
        part = lax.psum(part, "ctx", axis_index_groups=outer_groups)
    *placed, place_token = kernel_call(
        functools.partial(place_kernel, depth, hidden, feats),
        [saved(v.shape, f32) for v in (w_qkv, w_out, w_fc1, w_fc2)] + [TOKEN],
        pair,
        swap_core(pair),
        name="place",
        limit=24,
        scratch=[
            pltpu.VMEM((depth, GROUP, width_own, hidden), f32),
            pltpu.VMEM((depth, GROUP, hidden, width_own), f32),
            pltpu.VMEM((depth - 1, GROUP, 3, width_own, feats), f32),
            pltpu.VMEM((depth - 1, GROUP, feats, width_own), f32),
            DMA((16 * depth,)),
        ],
    )
    mine, last_pair = kernel_call(
        functools.partial(vector_plane_kernel, depth),
        [((32, width_own), f32), ((2 * width_own, 4 * feats), bf16)],
        mine,
        swap_xy(mine),
        swap_x(mine),
        swap_y(mine),
        part,
        swap_x(part),
        name="vector_plane",
        after=(place_token,),
    )
    grad_gains, grad_shifts, grad_fc1_bias, grad_qv_bias = kernel_call(
        functools.partial(vector_place_kernel, depth, head_dim),
        [
            (norm_gains.shape, f32),
            (shifts.shape, f32),
            (fc1_bias.shape, f32),
            (qv_bias.shape, f32),
        ],
        mine,
        swap_core(mine),
        name="vector_place",
    )
    grad_inputs, outputs = (
        kernel_call(
            place_rows_kernel,
            [saved(inputs.shape, f32)],
            own,
            other,
            name="place_rows",
            scratch=[DMA((2,))],
        )[0]
        for own, other in zip((upstream, outputs_own), others)
    )
    placed[:2] = kernel_call(
        functools.partial(place_last_kernel, feats),
        [saved(v.shape, f32) for v in (w_qkv, w_out)],
        last_pair,
        swap_core(last_pair),
        Far(placed[0]),
        Far(placed[1]),
        name="place_last",
        scratch=[
            pltpu.VMEM((GROUP, 3, width_own, feats), f32),
            pltpu.VMEM((GROUP, feats, width_own), f32),
            DMA((2 * GROUP,)),
        ],
        aliases={2: 0, 3: 1},
    )
    return (
        outputs,
        grad_inputs,
        grad_gains,
        grad_shifts,
        grad_qv_bias,
        grad_fc1_bias,
        *placed,
    )


def solution(mesh):
    rows = P("fsdp", "ctx", None)
    params = (
        P(None, None, "fsdp"),
        P(None, None, "fsdp"),
        P(None, None, "tp", "fsdp"),
        P(None, "tp", "fsdp"),
        P(None, None, "fsdp", "tp"),
        P(None, "tp", "fsdp"),
        P(None, "fsdp", "tp"),
        P(None, "tp", "fsdp"),
    )
    return jax.shard_map(
        per_device,
        mesh=mesh,
        in_specs=(rows, P("fsdp", None), rows) + params,
        out_specs=(rows, rows) + params,
        check_vma=False,
    )
```

```python
import functools
import math

import jax
import jax.numpy as jnp
from jax import lax
from jax.experimental import pallas as pl
from jax.experimental.pallas import tpu as pltpu
from jax.sharding import PartitionSpec as P

NORM_EPSILON = 1e-06
MASK_FILL = -1e30
ROOT_HALF = 0.7071067811865476
INV_ROOT_TAU = 0.3989422804014327
GROUP = 4
ORDER = (0, 5, 4, 1, 2, 7, 6, 3)
CHIPS = 4

bf16 = jnp.bfloat16
f32 = jnp.float32
VMEM = pl.BlockSpec(memory_space=pltpu.VMEM)
SMEM = pl.BlockSpec(memory_space=pltpu.SMEM)
HBM = pl.BlockSpec(memory_space=pltpu.HBM)
DMA = pltpu.SemaphoreType.DMA
TOKEN = ((8, 128), f32)


def dot(a, b):
    return lax.dot_general(a, b, (((1,), (0,)), ((), ())), preferred_element_type=f32)


def dot_nt(a, b):
    return lax.dot_general(a, b, (((1,), (1,)), ((), ())), preferred_element_type=f32)


def dot_tn(a, b):
    return lax.dot_general(a, b, (((0,), (0,)), ((), ())), preferred_element_type=f32)


class Far:
    def __init__(self, value):
        self.value = value


class Anywhere:
    def __init__(self, value):
        self.value = value


class Scalars:
    def __init__(self, value):
        self.value = value


def saved(shape, dtype):
    return pltpu.HBM(shape, dtype)


def kernel_call(body, outs, *args, name, limit=12, scratch=(), after=(), aliases=None, us=0):
    values, specs = [], []
    for arg in (*args, *after):
        if isinstance(arg, Far):
            values.append(pltpu.with_memory_space_constraint(arg.value, pltpu.HBM))
            specs.append(HBM)
        elif isinstance(arg, Anywhere):
            values.append(arg.value)
            specs.append(pl.BlockSpec(memory_space=pl.ANY))
        elif isinstance(arg, Scalars):
            values.append(arg.value)
            specs.append(SMEM)
        else:
            values.append(arg)
            specs.append(VMEM)
    first, last = len(args), len(args) + len(after)

    def run(*refs):
        body(*refs[:first], *refs[last:])

    out_shape, out_specs = [], []
    for out in outs:
        if isinstance(out, tuple):
            out_shape.append(jax.ShapeDtypeStruct(*out))
            out_specs.append(VMEM)
        else:
            out_shape.append(out)
            out_specs.append(HBM)
    return pl.pallas_call(
        run,
        out_shape=out_shape,
        in_specs=specs,
        out_specs=out_specs,
        scratch_shapes=list(scratch),
        input_output_aliases=aliases or {},
        compiler_params=pltpu.CompilerParams(vmem_limit_bytes=limit << 20),
        cost_estimate=pl.CostEstimate(flops=us * 10**9, bytes_accessed=0, transcendentals=0),
        name=name,
    )(*values)


def start_copies(pairs, sems):
    copies = [
        pltpu.make_async_copy(source, target, sems.at[k])
        for k, (source, target) in enumerate(pairs)
    ]
    for copy in copies:
        copy.start()
    return copies


def row_mean(value):
    return jnp.mean(value, axis=-1, keepdims=True)


def normalize(values):
    center = values - row_mean(values)
    inverse = lax.rsqrt(row_mean(center * center) + NORM_EPSILON)
    return center * inverse, inverse


def lanes_of(head, head_dim, width):
    lane = lax.broadcasted_iota(jnp.int32, (1, width), 1)
    return (lane >= head * head_dim) & (lane < (head + 1) * head_dim)


def assemble(chunks, target):
    rows = chunks[0].shape[0]
    for k, chunk in enumerate(chunks):
        target[k * rows : (k + 1) * rows, :] = chunk[...]


def only(flag, value):
    return jnp.where(flag, value, jnp.zeros_like(value))


def shards(weights):
    if len(weights) == 1:
        rows = weights[0].shape[0]
        return [(pl.ds(0, rows), weights[0])]
    count = len(weights)
    rows = weights[0].shape[0]
    f = lax.axis_index("fsdp")
    found = []
    for d, ref in enumerate(weights):
        place = lax.rem(f + (count - d), count)
        found.append((pl.ds(pl.multiple_of(place * rows, rows), rows), ref))
    return found


def pack_attn_kernel(layer, feats, qkv_hbm, out_hbm, packed_ref, token, qkv, out, sems):
    ci = lax.rem(lax.axis_index("ctx"), GROUP)
    span = pl.ds(pl.multiple_of(ci * feats, feats), feats)
    copies = start_copies(
        [(qkv_hbm.at[layer, :, :, span], qkv), (out_hbm.at[layer, span, :], out)], sems
    )
    copies[0].wait()
    for k in range(3):
        packed_ref[:, k * feats : (k + 1) * feats] = qkv[k]
    copies[1].wait()
    packed_ref[:, 3 * feats :] = out[...].T
    token[...] = jnp.zeros_like(token)


def pack_mlp_kernel(layer, hidden, fc1_hbm, fc2_hbm, packed_ref, token, fc1, fc2, sems):
    ci = lax.rem(lax.axis_index("ctx"), GROUP)
    span = pl.ds(pl.multiple_of(ci * hidden, hidden), hidden)
    copies = start_copies(
        [(fc1_hbm.at[layer, :, span], fc1), (fc2_hbm.at[layer, span, :], fc2)], sems
    )
    copies[0].wait()
    packed_ref[:, :hidden] = fc1[...]
    copies[1].wait()
    packed_ref[:, hidden:] = fc2[...].T
    token[...] = jnp.zeros_like(token)


def prep_upstream_kernel(tp, outer, lengths, cotangent_hbm,
                         upstream_hbm, upstream_b_ref, usable_ref, mask_ref,
                         rows_in, upstream_ref, sems):
    rows = rows_in.shape[0]
    c = lax.axis_index("ctx")
    t = lax.axis_index("tp")
    place = lax.rem(c, GROUP) * tp + t
    start = pl.multiple_of(t * rows, rows)
    copies = start_copies(
        [(cotangent_hbm.at[0, pl.ds(start, rows), :], rows_in)], sems.at[pl.ds(0, 1)]
    )
    lane = lax.broadcasted_iota(jnp.int32, usable_ref.shape, 1)
    limit = jnp.zeros(usable_ref.shape, jnp.int32)
    for o in range(outer):
        for k, d in enumerate(ORDER):
            source = place ^ d
            first_lane = (o * len(ORDER) + k) * rows
            count = lengths[0, o * GROUP + lax.div(source, tp)] - lax.rem(source, tp) * rows
            limit = jnp.where(lane >= first_lane, first_lane + jnp.clip(count, 0, rows), limit)
    usable_ref[...] = jnp.where(lane < limit, 1.0, 0.0)
    row = lax.broadcasted_iota(jnp.int32, mask_ref.shape, 0)
    mask = jnp.where(row + start < lengths[0, c], 1.0, 0.0)
    mask_ref[...] = mask
    copies[0].wait()
    upstream = rows_in[...] * mask[:, 0:1]
    upstream_ref[...] = upstream
    sent = start_copies([(upstream_ref, upstream_hbm)], sems.at[pl.ds(1, 1)])
    upstream_b_ref[...] = upstream.astype(bf16)
    sent[0].wait()


def prep_first_kernel(depth, inputs_hbm, vecs, stream_ref, first_ref, sems):
    rows = stream_ref.shape[0]
    start = pl.multiple_of(lax.axis_index("tp") * rows, rows)
    copies = start_copies([(inputs_hbm.at[0, pl.ds(start, rows), :], stream_ref)], sems)
    copies[0].wait()
    normed, _ = normalize(stream_ref[...])
    shift = vecs[2 * depth : 2 * depth + 1, :]
    first_ref[...] = (normed * vecs[0:1, :] + shift).astype(bf16)


def keep_rows_kernel(*refs):
    chunks, (near_hbm, far_hbm, token, near, far, sems) = refs[:8], refs[8:]
    assemble(chunks[:4], near)
    assemble(chunks[4:], far)
    for copy in start_copies([(near, near_hbm), (far, far_hbm)], sems):
        copy.wait()
    token[...] = jnp.zeros_like(token)


def qkv_kernel(feats, weight_count, *refs):
    c0, c1, c2, c3, *rest = refs
    weights = rest[:weight_count]
    bias, qkv_ref, x = rest[weight_count:]
    assemble((c0, c1, c2, c3), x)
    qkv = sum(dot(x[:, span], w[:, : 3 * feats]) for span, w in shards(weights))
    qkv_ref[:, :feats] = (qkv[:, :feats] + bias[0:1, :]).astype(bf16)
    qkv_ref[:, feats : 2 * feats] = qkv[:, feats : 2 * feats].astype(bf16)
    qkv_ref[:, 2 * feats :] = (qkv[:, 2 * feats :] + bias[1:2, :]).astype(bf16)


def attn_kernel(feats, heads, weight_count, part_count, keep_count, tile, *refs):
    q_ref, *rest = refs
    parts = rest[:part_count]
    weights = rest[part_count : part_count + weight_count]
    rest = rest[part_count + weight_count :]
    usable, *rest = rest
    kept, rest = rest[:keep_count], rest[keep_count:]
    partial_ref, attended_hbm, norm_hbm, *rest = rest
    kept_hbm, rest = rest[:keep_count], rest[keep_count:]
    keys, values, attended_ref, norm_ref, sems = rest
    head_dim = feats // heads
    scale = 1.0 / math.sqrt(head_dim)
    copies = start_copies(list(zip(kept, kept_hbm)), sems)
    first = 0
    for part in parts:
        rows, width = part.shape
        keys[first : first + rows, :] = part[:, width - 2 * feats : width - feats]
        values[first : first + rows, :] = part[:, width - feats :]
        first += rows
    keep = usable[...] > 0.5
    rows = q_ref.shape[0]
    for first in range(0, rows, tile):
        span = slice(first, first + tile)
        q = q_ref[span, :feats]
        attended = None
        for h in range(heads):
            own = lanes_of(h, head_dim, feats)
            scores = dot_nt(only(own, q), keys[...]) * scale
            scores = jnp.where(keep, scores, MASK_FILL)
            highest = jnp.max(scores, axis=-1, keepdims=True)
            raised = jnp.exp(scores - highest)
            total = jnp.sum(raised, axis=-1, keepdims=True)
            soft = (raised * (1.0 / total)).astype(bf16)
            result = dot(soft, values[...])
            log_norm = jnp.broadcast_to(highest + jnp.log(total), (tile, feats))
            if attended is None:
                attended, norms = result, log_norm
            else:
                attended = jnp.where(own, result, attended)
                norms = jnp.where(own, log_norm, norms)
        attended_ref[span, :] = attended.astype(bf16)
        norm_ref[span, :] = norms
    copies += start_copies(
        [(attended_ref, attended_hbm), (norm_ref, norm_hbm)],
        sems.at[pl.ds(keep_count, 2)],
    )
    for span, w in shards(weights):
        partial_ref[:, span] = dot_nt(attended_ref[...], w[:, 3 * feats :]).astype(bf16)
    for copy in copies:
        copy.wait()


def core_sum_kernel(count, *refs):
    pairs, owns = refs[: 2 * count], refs[2 * count : 3 * count]
    peers = refs[3 * count :]
    rows = owns[0].shape[0]
    for j in range(count):
        near, far = pairs[2 * j], pairs[2 * j + 1]
        for k in range(1 + len(peers)):
            span = slice(k * rows, (k + 1) * rows)
            total = near[span, :].astype(f32) + far[span, :].astype(f32)
            if k == 0:
                owns[j][...] = total
            else:
                peers[k - 1][j * rows : (j + 1) * rows, :] = total.astype(bf16)


def total_of(own, xy, x, y, part=0):
    rows = own.shape[0]
    span = slice(part * rows, (part + 1) * rows)
    return (
        own[...] + y[span, :].astype(f32) + x[span, :].astype(f32) + xy[span, :].astype(f32)
    )


def sum_norm_kernel(bias_row, gain_row, shift_row, own, xy, x, y, residual_hbm, vecs,
                    stream_ref, normed_ref, residual, sems):
    copies = start_copies([(residual_hbm, residual)], sems)
    total = total_of(own, xy, x, y) + vecs[bias_row : bias_row + 1, :]
    copies[0].wait()
    stream = residual[...] + total
    stream_ref[...] = stream
    normed, _ = normalize(stream)
    gain = vecs[gain_row : gain_row + 1, :]
    normed_ref[...] = (normed * gain + vecs[shift_row : shift_row + 1, :]).astype(bf16)


def sum_out_kernel(bias_row, own, xy, x, y, residual_hbm, vecs, mask, out_hbm, token,
                   residual, out_ref, sems):
    copies = start_copies([(residual_hbm, residual)], sems.at[pl.ds(0, 1)])
    total = total_of(own, xy, x, y, 1) + vecs[bias_row : bias_row + 1, :]
    copies[0].wait()
    out_ref[...] = (residual[...] + total) * mask[:, 0:1]
    token[...] = jnp.zeros_like(token)
    for copy in start_copies([(out_ref, out_hbm)], sems.at[pl.ds(1, 1)]):
        copy.wait()


def mlp_kernel(hidden, keep_count, saves, load_w, load_count, c0, c1, c2, c3, w, bias, *refs):
    kept, rest = refs[:keep_count], refs[keep_count:]
    sources, rest = rest[:load_count], rest[load_count:]
    partial_ref, x_out, act_out, slope_out, *rest = rest
    kept_hbm, rest = rest[:keep_count], rest[keep_count:]
    targets, rest = rest[:load_count], rest[load_count:]
    loaded = []
    if load_w:
        w_ref, *rest, w_sems, chunk_sems = rest
        rows = c0.shape[0]
        chunks = start_copies(
            [(c, x_out.at[pl.ds(k * rows, rows), :]) for k, c in enumerate((c0, c1, c2, c3))],
            chunk_sems,
        )
        spans = (pl.ds(0, hidden), pl.ds(hidden, hidden))
        loaded = start_copies([(w.at[:, c], w_ref.at[:, c]) for c in spans], w_sems)
        w = w_ref
    if load_count:
        *rest, load_sems = rest
        fetched = start_copies(list(zip(sources, targets)), load_sems)
    else:
        fetched = []
    if saves:
        x, act_ref, slope_ref, sems = rest
    else:
        x, act_ref, slope_ref = x_out, act_out, slope_out
        (sems,) = rest
    copies = start_copies(list(zip(kept, kept_hbm)), sems)
    if load_w:
        for chunk in chunks:
            chunk.wait()
    else:
        assemble((c0, c1, c2, c3), x)
    if saves:
        copies += start_copies([(x, x_out)], sems.at[pl.ds(keep_count, 1)])
    block = hidden // 2
    if load_w:
        loaded[0].wait()
    for k in range(2):
        span = slice(k * block, (k + 1) * block)
        pre = dot(x[...], w[:, span]) + bias[:, span]
        cdf = 0.5 * (1.0 + lax.erf(pre * ROOT_HALF))
        density = jnp.exp(-0.5 * pre * pre) * INV_ROOT_TAU
        slope_ref[k] = cdf + pre * density
        act_ref[:, span] = (pre * cdf).astype(bf16)
        if saves:
            copies += start_copies(
                [(slope_ref.at[k], slope_out.at[k])], sems.at[pl.ds(1 + keep_count + k, 1)]
            )
    if saves:
        copies += start_copies([(act_ref, act_out)], sems.at[pl.ds(3 + keep_count, 1)])
    if load_w:
        loaded[1].wait()
    partial_ref[...] = dot_nt(act_ref[...], w[:, hidden:]).astype(bf16)
    for copy in copies + fetched:
        copy.wait()


def mlp_back_kernel(hidden, chunk_count, *refs):
    chunks, (w, slope, *rest) = refs[:chunk_count], refs[chunk_count:]
    partial_ref, grad_ref, sum_hbm, x, sum_ref, sems = rest
    assemble(chunks, x)
    grad = dot(x[...], w[:, hidden:])
    block = hidden // 2
    for k in range(2):
        span = slice(k * block, (k + 1) * block)
        part = grad[:, span] * slope[k]
        grad_ref[:, span] = part.astype(bf16)
        sum_ref[:, span] = jnp.sum(part, axis=0, keepdims=True)
    sent = start_copies([(sum_ref, sum_hbm)], sems)
    partial_ref[...] = dot_nt(grad_ref[...], w[:, :hidden]).astype(bf16)
    sent[0].wait()


def mlp_grad_kernel(hidden, keep_count, second_near, second_far, act_near, act_far,
                    up_near, up_far, grad_near, grad_far, *refs):
    kept, refs = refs[:keep_count], refs[keep_count:]
    out_hbm, *refs = refs
    kept_hbm, (out_one, out_two, sems) = refs[:keep_count], refs[keep_count:]
    sent = start_copies(list(zip(kept, kept_hbm)), sems.at[pl.ds(2, keep_count)])
    total = dot_tn(up_near[...], act_near[...]) + dot_tn(up_far[...], act_far[...])
    out_two[...] = total.astype(bf16)
    sent += start_copies(
        [(out_two, out_hbm.at[:, pl.ds(hidden, hidden)])], sems.at[pl.ds(0, 1)]
    )
    total = dot_tn(second_near[...], grad_near[...]) + dot_tn(second_far[...], grad_far[...])
    out_one[...] = total.astype(bf16)
    sent += start_copies([(out_one, out_hbm.at[:, pl.ds(0, hidden)])], sems.at[pl.ds(1, 1)])
    for copy in sent:
        copy.wait()


def norm_back(upstream, values, gain):
    normed, inverse = normalize(values)
    scaled = upstream * gain
    back = inverse * (scaled - row_mean(scaled) - normed * row_mean(scaled * normed))
    gain_grad = jnp.sum(upstream * normed, axis=0, keepdims=True)
    return back, gain_grad, jnp.sum(upstream, axis=0, keepdims=True)


def norm_back_two_kernel(gain_row, own, xy, x, y, values, upstream, vecs,
                         grad_ref, grad_b_ref, sums_ref):
    total = total_of(own, xy, x, y)
    up = upstream[...]
    back, gain_grad, shift_grad = norm_back(
        total, values[...], vecs[gain_row : gain_row + 1, :]
    )
    grad = up + back
    grad_ref[...] = grad
    grad_b_ref[...] = grad.astype(bf16)
    sums_ref[0:1, :] = gain_grad
    sums_ref[1:2, :] = shift_grad
    sums_ref[2:3, :] = jnp.sum(grad, axis=0, keepdims=True)
    sums_ref[3:4, :] = jnp.sum(up, axis=0, keepdims=True)


def norm_back_one_kernel(gain_row, own, xy, x, y, values, upstream, vecs, mask,
                         grad_ref, grad_b_ref, sums_ref):
    total = total_of(own, xy, x, y)
    back, gain_grad, shift_grad = norm_back(
        total, values[...], vecs[gain_row : gain_row + 1, :]
    )
    grad = upstream[...] + back
    if mask is not None:
        grad = grad * mask[:, 0:1]
    grad_ref[...] = grad
    grad_b_ref[...] = grad.astype(bf16)
    sums_ref[0:1, :] = gain_grad
    sums_ref[1:2, :] = shift_grad


def attn_back_kernel(feats, heads, weight_count, part_count, tile, carried, *refs):
    c0, c1, c2, c3, *rest = refs
    weights, rest = rest[:weight_count], rest[weight_count:]
    usable, qkv, attended, norms, *rest = rest
    parts, rest = rest[:part_count], rest[part_count:]
    if carried:
        keys_before, values_before, *rest = rest
    x, grad_q, grad_k, grad_v, pairs, grad_att = rest
    head_dim = feats // heads
    scale = 1.0 / math.sqrt(head_dim)
    first = 0
    for part in parts:
        rows, width = part.shape
        pairs[first : first + rows, :] = part[:, width - 2 * feats :]
        first += rows
    assemble((c0, c1, c2, c3), x)
    grad_att[...] = sum(
        dot(x[:, span], w[:, 3 * feats :]) for span, w in shards(weights)
    ).astype(bf16)
    keep = usable[...] > 0.5
    rows = qkv.shape[0]
    if carried:
        sum_k, sum_v = keys_before[...], values_before[...]
    else:
        sum_k = jnp.zeros(grad_k.shape, f32)
        sum_v = jnp.zeros(grad_v.shape, f32)
    keys, values = pairs[:, :feats], pairs[:, feats:]
    for first in range(0, rows, tile):
        span = slice(first, first + tile)
        q = qkv[span, :feats]
        ga = grad_att[span, :]
        products = ga.astype(f32) * attended[span, :].astype(f32)
        gq = None
        for h in range(heads):
            own = lanes_of(h, head_dim, feats)
            q_h = only(own, q)
            ga_h = only(own, ga)
            row_dots = jnp.sum(only(own, products), axis=-1, keepdims=True)
            scores = dot_nt(q_h, keys) * scale
            scores = jnp.where(keep, scores, MASK_FILL)
            soft = jnp.exp(scores - norms[span, h * head_dim : h * head_dim + 1])
            grad_soft = dot_nt(ga_h, values)
            grad_scores = (soft * (grad_soft - row_dots)).astype(bf16)
            part = dot(grad_scores, keys)
            gq = part if gq is None else jnp.where(own, part, gq)
            sum_k = sum_k + dot_tn(grad_scores, q_h) * scale
            sum_v = sum_v + dot_tn(soft.astype(bf16), ga_h)
        grad_q[span, :] = gq * scale
    grad_k[...] = sum_k
    grad_v[...] = sum_v


def project_kernel(feats, first, weight_count, gq, gk, gv, *refs):
    weights, (partial_ref, packed) = refs[:weight_count], refs[weight_count:]
    rows = gq.shape[0]
    span = slice(first, first + rows)
    packed[:, :feats] = gq[...].astype(bf16)
    packed[:, feats : 2 * feats] = gk[span, :].astype(bf16)
    packed[:, 2 * feats :] = gv[span, :].astype(bf16)
    for columns, w in shards(weights):
        partial_ref[:, columns] = dot_nt(packed[...], w[:, : 3 * feats]).astype(bf16)


def attn_grad_kernel(feats, count, keep_count, first_near, first_far, att_near, att_far,
                     up_near, up_far, gq_near, gq_far, gk, gv, passed, lines, *refs):
    kept, refs = refs[:keep_count], refs[keep_count:]
    outs, refs = refs[:count], refs[count:]
    heads_hbm, passed_ref, *refs = refs
    kept_hbm, (packed, sums_ref, *staged, sems) = refs[:keep_count], refs[keep_count:]
    rows = up_near.shape[0]
    used = count + 2
    sent = start_copies(list(zip(kept, kept_hbm)), sems.at[pl.ds(used, keep_count)])
    passed_ref[...] = passed[...]
    packed[:rows, :feats] = gq_near[...].astype(bf16)
    packed[rows:, :feats] = gq_far[...].astype(bf16)
    packed[:, feats : 2 * feats] = gk[...].astype(bf16)
    packed[:, 2 * feats :] = gv[...].astype(bf16)
    sums_ref[0:1, :] = jnp.sum(gq_near[...], axis=0, keepdims=True) + jnp.sum(
        gq_far[...], axis=0, keepdims=True
    )
    sums_ref[1:2, :] = jnp.sum(gv[...], axis=0, keepdims=True)
    sent += start_copies([(sums_ref, heads_hbm)], sems.at[pl.ds(0, 1)])

    def out_part(span):
        return dot_tn(up_near[:, span], att_near[...]) + dot_tn(up_far[:, span], att_far[...])

    def qkv_part(span):
        return dot_tn(first_near[:, span], packed[:rows, :]) + dot_tn(
            first_far[:, span], packed[rows:, :]
        )

    if count == 1:
        out_one, out_two = staged
        whole = slice(None)
        out_two[...] = out_part(whole).astype(bf16)
        sent += start_copies(
            [(out_two, outs[0].at[:, pl.ds(3 * feats, feats)])], sems.at[pl.ds(1, 1)]
        )
        out_one[...] = qkv_part(whole).astype(bf16)
        sent += start_copies(
            [(out_one, outs[0].at[:, pl.ds(0, 3 * feats)])], sems.at[pl.ds(2, 1)]
        )
    else:
        (stage,) = staged
        below = lines.shape[1]
        width_own = outs[0].shape[0] - below
        for d in reversed(range(count)):
            place = lax.rem(lax.axis_index("fsdp") + d, count)
            span = pl.ds(pl.multiple_of(place * width_own, width_own), width_own)
            stage[d, :width_own, : 3 * feats] = qkv_part(span).astype(bf16)
            stage[d, :width_own, 3 * feats :] = out_part(span).astype(bf16)
            stage[d, width_own:, :] = lines[d]
            sent += start_copies([(stage.at[d], outs[d])], sems.at[pl.ds(1 + d, 1)])
    for copy in sent:
        copy.wait()


def settle_kernel(keep_count, after_count, passed, *refs):
    kept, refs = refs[:keep_count], refs[keep_count + after_count :]
    passed_ref, *kept_hbm, sems = refs
    copies = start_copies(list(zip(kept, kept_hbm)), sems)
    passed_ref[...] = passed[...]
    for copy in copies:
        copy.wait()


def fetch_kernel(count, *refs):
    sources, (target, sems) = refs[:count], refs[count:]
    columns = target.shape[1]
    moves = []
    row = 0
    for source in sources:
        rows = source.shape[0]
        for first in range(0, source.shape[1], columns):
            moves.append(
                (source.at[:, pl.ds(first, columns)], target.at[pl.ds(row, rows), :])
            )
            row += rows
    for copy in start_copies(moves, sems):
        copy.wait()


def shard_sum_kernel(depth, own_hbm, stacked, crossed, *refs):
    *others, part_ref, mine_ref, pair_ref, own, sems = refs
    count = stacked.shape[0]
    first, *copies = start_copies(
        [
            (own_hbm, own),
            (stacked, pair_ref.at[pl.ds(0, count), :]),
            (crossed, pair_ref.at[pl.ds(count, count), :]),
        ],
        sems,
    )
    first.wait()
    rows, width = part_ref.shape[0], mine_ref.shape[1]
    terms = [ref[...].astype(f32) for ref in (own, *others)]
    total = terms[0]
    for term in terms[1:]:
        total = total + term
    part_ref[...] = total[:rows, :].astype(bf16)
    lines = total[rows:, :width] + total[rows:, width:]
    mine_ref[: 6 * depth, :] = lines[: 6 * depth, :]
    for k in range(mine_ref.shape[0] - 16):
        mine_ref[16 + k : 17 + k, :] = lines[6 * depth + k : 6 * depth + k + 1, :]
    for copy in copies:
        copy.wait()


def place_kernel(depth, hidden, feats, here, sibling, *refs):
    qkv_hbm, out_hbm, fc1_hbm, fc2_hbm, token, fc1, fc2, qkv, out, sems = refs
    token[...] = jnp.zeros_like(token)
    ci = lax.rem(lax.axis_index("ctx"), GROUP)
    rows = fc1.shape[2]
    count = here.shape[0] // 2
    copies = []

    def send(source, target):
        copies.extend(start_copies([(source, target)], sems.at[pl.ds(len(copies), 1)]))

    for k in range(GROUP):
        stacked = (here, sibling)[k % 2].at[pl.ds(k // 2 * count, count), :]
        wide = pl.ds(pl.multiple_of((ci ^ k) * hidden, hidden), hidden)
        narrow = pl.ds(pl.multiple_of((ci ^ k) * feats, feats), feats)
        for l in range(depth):
            first = 0 if l == 0 else (3 * l - 1) * rows
            fc1[l, k] = stacked[first : first + rows, :].astype(f32)
            send(fc1.at[l, k], fc1_hbm.at[l, :, wide])
            fc2[l, k] = stacked[first + rows : first + 2 * rows, :].T.astype(f32)
            send(fc2.at[l, k], fc2_hbm.at[l, wide, :])
            if l > 0:
                piece = stacked.at[pl.ds(first + 2 * rows, rows), :]
                for j in range(3):
                    qkv[l - 1, k, j] = piece[:, j * feats : (j + 1) * feats].astype(f32)
                send(qkv.at[l - 1, k], qkv_hbm.at[l, :, :, narrow])
                out[l - 1, k] = piece[:, 3 * feats :].T.astype(f32)
                send(out.at[l - 1, k], out_hbm.at[l, narrow, :])
    for copy in copies:
        copy.wait()


def place_last_kernel(feats, here, sibling, qkv_in, out_in, qkv_hbm, out_hbm, qkv, out, sems):
    ci = lax.rem(lax.axis_index("ctx"), GROUP)
    rows = here.shape[0] // 2
    copies = []
    for k in range(GROUP):
        piece = (here, sibling)[k % 2].at[pl.ds(k // 2 * rows, rows), :]
        span = pl.ds(pl.multiple_of((ci ^ k) * feats, feats), feats)
        for j in range(3):
            qkv[k, j] = piece[:, j * feats : (j + 1) * feats].astype(f32)
        copies += start_copies(
            [(qkv.at[k], qkv_hbm.at[0, :, :, span])], sems.at[pl.ds(2 * k, 1)]
        )
        out[k] = piece[:, 3 * feats :].T.astype(f32)
        copies += start_copies(
            [(out.at[k], out_hbm.at[0, span, :])], sems.at[pl.ds(2 * k + 1, 1)]
        )
    for copy in copies:
        copy.wait()


def vector_pack_kernel(depth, one_now, gq_near, gq_far, gv, *refs):
    count = 5 * depth - 2
    out_ref, *found, sems = refs[count:]
    copies = start_copies(list(zip(refs[:count], found)), sems)
    out_ref[...] = jnp.zeros_like(out_ref)
    feats = gv.shape[1]
    head_now = [
        jnp.sum(gq_near[...], axis=0, keepdims=True) + jnp.sum(gq_far[...], axis=0, keepdims=True),
        jnp.sum(gv[...], axis=0, keepdims=True),
    ]
    for copy in copies:
        copy.wait()
    for l in range(depth):
        if l == 0:
            one, (two, unit_near, unit_far) = one_now, found[:3]
            heads = head_now
        else:
            one, two, unit_near, unit_far, head = found[5 * l - 2 : 5 * l + 3]
            heads = [head[0:1, :], head[1:2, :]]
        out_ref[6 * l : 6 * l + 1, :] = one[0:1, :]
        out_ref[6 * l + 1 : 6 * l + 2, :] = two[0:1, :]
        out_ref[6 * l + 2 : 6 * l + 3, :] = one[1:2, :]
        out_ref[6 * l + 3 : 6 * l + 6, :] = two[1:4, :]
        units = unit_near.shape[1]
        row = 6 * depth
        out_ref[row : row + 1, l * units : (l + 1) * units] = unit_near[...] + unit_far[...]
        for j in range(2):
            start = (2 * l + j) * feats
            out_ref[row + 1 : row + 2, start : start + feats] = heads[j]


def vector_lines_kernel(depth, width_own, packed, lines_ref):
    count = lines_ref.shape[0]
    f = lax.axis_index("fsdp")
    total = packed[...]
    high = total.astype(bf16).astype(f32)
    low = total - high
    lines_ref[...] = jnp.zeros_like(lines_ref)
    last = 6 * depth
    for k, value in enumerate((high, low)):
        lanes = slice(k * width_own, (k + 1) * width_own)
        columns = [value[:, a * width_own : (a + 1) * width_own] for a in range(count)]
        for d in range(count):
            mine = columns[0]
            for a in range(1, count):
                mine = jnp.where(lax.rem(f + d, count) == a, columns[a], mine)
            rows = [mine[:last, :]]
            for r in range(2):
                for a in range(count):
                    rows.append(columns[a][last + r : last + r + 1, :])
            rows.append(jnp.zeros((lines_ref.shape[1] - last - 2 * count, width_own), f32))
            lines_ref[d, :, lanes] = jnp.concatenate(rows, axis=0).astype(bf16)


def vector_plane_kernel(depth, own, xy, x, y, part, part_x, out_ref, pair_ref):
    last = 6 * depth
    rows = part.shape[0]
    pair_ref[:rows, :] = part[...]
    pair_ref[rows:, :] = part_x[...]
    out_ref[:last, :] = own[:last, :] + xy[:last, :] + x[:last, :] + y[:last, :]
    out_ref[16:24, :] = own[16:24, :]
    out_ref[24:32, :] = x[16:24, :]


def vector_place_kernel(depth, head_dim, own, far, gains_ref, shifts_ref, unit_ref, heads_ref):
    total = own[: 6 * depth, :] + far[: 6 * depth, :]
    for l in range(depth):
        gains_ref[l] = total[6 * l : 6 * l + 2, :]
        shifts_ref[l] = total[6 * l + 2 : 6 * l + 6, :]
    pieces = (own[16:24, :], far[16:24, :], own[24:32, :], far[24:32, :])
    ci = lax.rem(lax.axis_index("ctx"), GROUP)
    f = lax.axis_index("fsdp")

    def of_place(c):
        k = ci ^ c
        found = pieces[0]
        for j in range(1, GROUP):
            found = jnp.where(k == j, pieces[j], found)
        return found

    width_own = own.shape[1]
    units = of_place(f)
    parts = unit_ref.shape[2] // width_own
    for l in range(depth):
        for j in range(parts):
            row = l * parts + j
            unit_ref[l, :, j * width_own : (j + 1) * width_own] = units[row : row + 1, :]
    head_own = heads_ref.shape[3]
    heads = heads_ref.shape[2] // GROUP
    for c in range(GROUP):
        found = of_place(c)
        for l in range(depth):
            for j in range(2):
                for h in range(heads):
                    first = ((2 * l + j) * heads + h) * head_dim
                    row, lane = 4 + first // width_own, first % width_own
                    value = found[row : row + 1, lane : lane + head_own]
                    for a in range(1, head_dim // head_own):
                        start = lane + a * head_own
                        value = jnp.where(
                            f == a, found[row : row + 1, start : start + head_own], value
                        )
                    heads_ref[l, j, c * heads + h : c * heads + h + 1, :] = value


def place_rows_kernel(own, other, out_hbm, sems):
    rows = own.shape[0]
    start = pl.multiple_of(lax.axis_index("tp") * rows, rows)
    copies = start_copies(
        [
            (own, out_hbm.at[0, pl.ds(start, rows), :]),
            (other, out_hbm.at[0, pl.ds(pl.multiple_of(rows - start, rows), rows), :]),
        ],
        sems,
    )
    for copy in copies:
        copy.wait()


def per_device(
    inputs, lengths, cotangent, norm_gains, shifts, qv_bias, fc1_bias, w_qkv, w_out, w_fc1, w_fc2
):
    depth = w_qkv.shape[0]
    width_own = w_qkv.shape[2]
    fsdp = lax.axis_size("fsdp")
    tp = lax.axis_size("tp")
    ctx = lax.axis_size("ctx")
    outer = ctx // GROUP
    rows = inputs.shape[1] // tp
    half = rows * CHIPS
    all_rows = 2 * half
    head_own = qv_bias.shape[3]
    head_dim = head_own * fsdp
    heads = qv_bias.shape[2] // GROUP
    feats = heads * head_dim
    hidden = w_fc1.shape[2] // GROUP
    width = width_own * fsdp
    t = lax.axis_index("tp")
    f = lax.axis_index("fsdp")
    ci = lax.axis_index("ctx") % GROUP
    tile = half // 2
    attn_limit = 12 if outer == 1 else 48

    def swap_core(value):
        return lax.ppermute(value, "ctx", [(i, i ^ 1) for i in range(ctx)])

    def swap_x(value):
        return lax.ppermute(value, "ctx", [(i, i ^ 2) for i in range(ctx)])

    def swap_y(value):
        return lax.ppermute(value, "tp", [(i, i ^ 1) for i in range(tp)])

    def swap_xy(value):
        pairs = [
            (i * tp + k, (i ^ 2) * tp + (k ^ 1)) for i in range(ctx) for k in range(tp)
        ]
        return lax.ppermute(value, ("ctx", "tp"), pairs)

    def shift_z(value, d):
        return lax.ppermute(value, "fsdp", [(i, (i + d) % fsdp) for i in range(fsdp)])

    outer_groups = [[o * GROUP + i for o in range(outer)] for i in range(GROUP)]

    def gather_rows(own):
        near = (own, swap_xy(own), swap_x(own), swap_y(own))
        return near, tuple(swap_core(chunk) for chunk in near)

    def settle(value, there, *kept):
        return kernel_call(
            functools.partial(settle_kernel, len(kept), 1),
            [(value.shape, value.dtype)] + [saved(k.shape, k.dtype) for k in kept],
            value,
            *kept,
            Far(there),
            name="settle",
            scratch=[DMA((max(1, len(kept)),))],
        )

    def reduce_rows(*pairs, after=()):
        count = len(pairs)
        *owns, xy, x, y = kernel_call(
            functools.partial(core_sum_kernel, count),
            [((rows, width), f32)] * count + [((count * rows, width), bf16)] * 3,
            *[v for near, far in pairs for v in (near, swap_core(far))],
            name="core_sum",
            after=after,
        )
        peers = (swap_xy(xy), swap_x(x), swap_y(y))
        return [(own, *peers) for own in owns]

    def pack_attn(l, after):
        return kernel_call(
            functools.partial(pack_attn_kernel, l, feats),
            [((width_own, 4 * feats), bf16), TOKEN],
            Far(w_qkv),
            Far(w_out),
            name="pack_attn",
            after=after,
            scratch=[
                pltpu.VMEM((3, width_own, feats), bf16),
                pltpu.VMEM((feats, width_own), bf16),
                DMA((2,)),
            ],
        )

    def pack_mlp(l, after):
        return kernel_call(
            functools.partial(pack_mlp_kernel, l, hidden),
            [((width_own, 2 * hidden), bf16), TOKEN],
            Far(w_fc1),
            Far(w_fc2),
            name="pack_mlp",
            after=after,
            scratch=[
                pltpu.VMEM((width_own, hidden), bf16),
                pltpu.VMEM((hidden, width_own), bf16),
                DMA((2,)),
            ],
        )

    attn_w = []
    mlp_w = []
    token = None
    for l in range(depth):
        own, token = pack_attn(l, () if token is None else (token,))
        attn_w.append((lax.all_gather(own, "fsdp", axis=0, tiled=True),))
        own, token = pack_mlp(l, (token,))
        mlp_w.append(lax.all_gather(own, "fsdp", axis=0, tiled=True))
        if l == 0:
            pack_token = token

    qv_own = lax.dynamic_slice_in_dim(qv_bias, ci * heads, heads, axis=2)
    vec_rows = depth * 6
    c1_rows = depth * fc1_bias.shape[2] // width_own
    qv_own = qv_own.reshape(1, -1)
    small_own = jnp.concatenate(
        [
            norm_gains.reshape(-1, width_own),
            shifts.reshape(-1, width_own),
            fc1_bias.reshape(-1, width_own),
            jnp.pad(qv_own, ((0, 0), (0, width_own - qv_own.shape[1]))),
        ],
        axis=0,
    )
    shifted = [small_own] + [shift_z(small_own, d) for d in range(1, fsdp)]

    def shard(a):
        picked = shifted[0]
        for d in range(1, fsdp):
            picked = jnp.where((f - d) % fsdp == a, shifted[d], picked)
        return picked.astype(f32)

    small = [shard(a) for a in range(fsdp)]
    vecs = jnp.concatenate([s[:vec_rows] for s in small], axis=1)
    fc1_all = shard(ci)[vec_rows : vec_rows + c1_rows].reshape(depth, 1, hidden)
    qv_all = jnp.stack(
        [s[vec_rows + c1_rows, : qv_own.shape[1]].reshape(depth, 2, heads, head_own) for s in small],
        axis=3,
    ).reshape(depth, 2, feats)

    def gain_row(l, i):
        return 2 * l + i

    def shift_row(l, i):
        return 2 * depth + 4 * l + i

    key_rows = outer * all_rows
    row_f32 = ((rows, width), f32)
    row_bf16 = ((rows, width), bf16)
    upstream, upstream_b, usable, mask = kernel_call(
        functools.partial(prep_upstream_kernel, tp, outer),
        [saved((rows, width), f32), row_bf16, ((1, key_rows), f32), ((rows, 128), f32)],
        Scalars(lengths),
        Far(cotangent),
        name="prep_upstream",
        after=(pack_token,),
        scratch=[pltpu.VMEM((rows, width), f32), pltpu.VMEM((rows, width), f32), DMA((2,))],
    )
    near, far = gather_rows(upstream_b)
    half_x = pltpu.VMEM((half, width), bf16)
    *upstream_rows, upstream_token = kernel_call(
        keep_rows_kernel,
        [saved((half, width), bf16)] * 2 + [TOKEN],
        *near,
        *far,
        name="keep_rows",
        scratch=[half_x, half_x, DMA((2,))],
    )
    stream, first = kernel_call(
        functools.partial(prep_first_kernel, depth),
        [row_f32, row_bf16],
        Far(inputs),
        vecs,
        name="prep_first",
        scratch=[DMA((1,))],
    )
    first_chunks = gather_rows(first)

    partial_out = ((half, width), bf16)
    saved_all = []
    for l in range(depth):
        qkv = []
        first_x = []
        for side in (0, 1):
            qkv_half, x_half = kernel_call(
                functools.partial(qkv_kernel, feats, len(attn_w[l])),
                [((half, 3 * feats), bf16), ((half, width), bf16)],
                *first_chunks[side],
                *attn_w[l],
                qv_all[l],
                name="qkv",
                after=(upstream_token,) if l == 0 and side == 0 else (),
            )
            qkv.append(qkv_half)
            first_x.append(x_half)
        if outer > 1:
            pairs = jnp.concatenate([part[:, feats:] for part in qkv], axis=0)
            pairs = lax.all_gather(
                pairs, "ctx", axis=0, tiled=True, axis_index_groups=outer_groups
            )
            key_parts = (pairs,)
        else:
            key_parts = tuple(qkv)
        attn = [None, None]
        for side in (1, 0):
            kept = (first_x[side], qkv[side]) + ((stream,) if side == 1 else ())
            attn[side] = kernel_call(
                functools.partial(
                    attn_kernel, feats, heads, len(attn_w[l]), len(key_parts), len(kept), tile
                ),
                [partial_out, saved((half, feats), bf16), saved((half, feats), f32)]
                + [saved(k.shape, k.dtype) for k in kept],
                qkv[side],
                *key_parts,
                *attn_w[l],
                usable,
                *kept,
                name="attn",
                limit=attn_limit,
                scratch=[
                    pltpu.VMEM((key_rows, feats), bf16),
                    pltpu.VMEM((key_rows, feats), bf16),
                    pltpu.VMEM((half, feats), bf16),
                    pltpu.VMEM((half, feats), f32),
                    DMA((len(kept) + 2,)),
                ],
            )
        (sums,) = reduce_rows((attn[0][0], attn[1][0]))
        middle, second = kernel_call(
            functools.partial(sum_norm_kernel, shift_row(l, 2), gain_row(l, 1), shift_row(l, 1)),
            [row_f32, row_bf16],
            *sums,
            Far(attn[1][5]),
            vecs,
            name="sum_norm",
            scratch=[pltpu.VMEM((rows, width), f32), DMA((1,))],
        )
        second_chunks = gather_rows(second)
        mlp = [None, None]
        for side in (1, 0):
            kept = (middle,) if side == 1 else ()
            saves = l + 1 < depth
            load_w = not saves and side == 1
            loads = tuple(upstream_rows) if not saves and side == 0 else ()
            shapes = [
                ((half, width), bf16),
                ((half, hidden), bf16),
                ((2, half, hidden // 2), f32),
            ]
            mlp[side] = kernel_call(
                functools.partial(mlp_kernel, hidden, len(kept), saves, load_w, len(loads)),
                [partial_out]
                + [saved(*shape) if saves else shape for shape in shapes]
                + [saved(k.shape, k.dtype) for k in kept]
                + [(v.shape, v.dtype) for v in loads]
                + ([(mlp_w[l].shape, bf16)] if load_w else []),
                *[Anywhere(c) if load_w else c for c in second_chunks[side]],
                Far(mlp_w[l]) if load_w else mlp_w[l],
                fc1_all[l],
                *kept,
                *[Far(v) for v in loads],
                name="mlp",
                scratch=[pltpu.VMEM(*shape) for shape in shapes if saves]
                + [DMA((4 + len(kept),))]
                + ([DMA((2,)), DMA((CHIPS,))] if load_w else [])
                + [DMA((len(loads),)) for _ in loads[:1]],
            )
            if load_w:
                *mlp[side], mlp_w[l] = mlp[side]
            if loads:
                *mlp[side], near, far = mlp[side]
                upstream_chunks = [(near,), (far,)]
        saved_all.append((attn, pairs if outer > 1 else None, mlp))
        if l + 1 < depth:
            (sums,) = reduce_rows((mlp[0][0], mlp[1][0]))
            stream, first = kernel_call(
                functools.partial(
                    sum_norm_kernel, shift_row(l, 3), gain_row(l + 1, 0), shift_row(l + 1, 0)
                ),
                [row_f32, row_bf16],
                *sums,
                Far(mlp[1][4]),
                vecs,
                name="sum_norm",
                scratch=[pltpu.VMEM((rows, width), f32), DMA((1,))],
            )
            first_chunks = gather_rows(first)

    def scatter_grads(grad):
        part = lax.psum_scatter(grad, "fsdp", scatter_dimension=0, tiled=True)
        if outer > 1:
            part = lax.psum(part, "ctx", axis_index_groups=outer_groups)
        return part

    row_sums = [None] * depth
    unit_sums = [None] * depth
    head_sums = [None] * depth
    mlp_parts = [None] * depth
    attn_parts = [None] * depth
    for l in reversed(range(depth)):
        attn, pairs, mlp = saved_all[l]
        back = [None, None]
        for side in (1, 0):
            back[side] = kernel_call(
                functools.partial(mlp_back_kernel, hidden, len(upstream_chunks[side])),
                [
                    partial_out,
                    ((half, hidden), bf16),
                    saved((1, hidden), f32),
                    ((half, width), bf16),
                ],
                *upstream_chunks[side],
                mlp_w[l],
                mlp[side][3],
                name="mlp_back",
                scratch=[pltpu.VMEM((1, hidden), f32), DMA((1,))],
            )
        kept = [back[0][0], back[1][0]]
        if l + 1 == depth:
            kept += [mlp[0][0], mlp[1][0]]
        mlp_grad, *kept = kernel_call(
            functools.partial(mlp_grad_kernel, hidden, len(kept)),
            [saved((width, 2 * hidden), bf16)] + [saved(k.shape, k.dtype) for k in kept],
            mlp[0][1],
            mlp[1][1],
            mlp[0][2],
            mlp[1][2],
            back[0][3],
            back[1][3],
            back[0][1],
            back[1][1],
            *kept,
            name="mlp_grad",
            scratch=[
                pltpu.VMEM((width, hidden), bf16),
                pltpu.VMEM((width, hidden), bf16),
                DMA((2 + len(kept),)),
            ],
        )
        mlp_parts[l] = scatter_grads(mlp_grad)
        (sums,) = reduce_rows(tuple(kept[:2]))
        if l + 1 == depth:
            output_pair = tuple(kept[2:])
        unit_sums[l] = (back[0][2], back[1][2])
        grad_middle, middle_b, sums_two = kernel_call(
            functools.partial(norm_back_two_kernel, gain_row(l, 1)),
            [row_f32, row_bf16, ((4, width), f32)],
            *sums,
            mlp[1][4],
            upstream,
            vecs,
            name="norm_back_two",
        )
        if l + 1 < depth:
            middle_b, sums_two, grad_middle = settle(
                middle_b, attn_parts[l + 1], sums_two, grad_middle
            )
        middle_chunks = gather_rows(middle_b)
        grad_q = [None, None]
        middle_x = [None, None]
        carried = ()
        for side in (0, 1):
            key_parts = (pairs,) if outer > 1 else (attn[0][4], attn[1][4])
            middle_x[side], grad_q[side], *carried = kernel_call(
                functools.partial(
                    attn_back_kernel,
                    feats,
                    heads,
                    len(attn_w[l]),
                    len(key_parts),
                    tile,
                    len(carried) > 0,
                ),
                [
                    ((half, width), bf16),
                    ((half, feats), f32),
                    ((key_rows, feats), f32),
                    ((key_rows, feats), f32),
                ],
                *middle_chunks[side],
                *attn_w[l],
                usable,
                attn[side][4],
                attn[side][1],
                attn[side][2],
                *key_parts,
                *carried,
                name="attn_back",
                scratch=[
                    pltpu.VMEM((key_rows, 2 * feats), bf16),
                    pltpu.VMEM((half, feats), bf16),
                ],
                limit=attn_limit,
            )
        grad_k, grad_v = carried
        if outer > 1:
            grad_k, grad_v = (
                lax.psum_scatter(
                    v, "ctx", scatter_dimension=0, tiled=True, axis_index_groups=outer_groups
                )
                for v in (grad_k, grad_v)
            )

        def project(side, after):
            return kernel_call(
                functools.partial(project_kernel, feats, side * half, len(attn_w[l])),
                [partial_out],
                grad_q[side],
                grad_k,
                grad_v,
                *attn_w[l],
                name="project",
                after=after,
                scratch=[pltpu.VMEM((half, 3 * feats), bf16)],
            )[0]

        far_part = project(1, ())
        near_part = project(0, ())
        pairs_now = [(near_part, far_part)]
        if l == 0:
            pairs_now.append(output_pair)
        sums, *output_sums = reduce_rows(*pairs_now)
        body = functools.partial(norm_back_one_kernel, gain_row(l, 0))
        if l > 0:
            masked = ()
            body = lambda *refs, body=body: body(*refs[:7], None, *refs[7:])
        else:
            masked = (mask,)
        upstream, upstream_b, sums_one = kernel_call(
            body,
            [row_f32, row_bf16, ((2, width), f32)],
            *sums,
            attn[1][5],
            grad_middle,
            vecs,
            *masked,
            name="norm_back_one",
        )
        lines = ()
        if l == 0:
            terms = [sums_two, *unit_sums[0]]
            for k in range(1, depth):
                terms += [*row_sums[k], *unit_sums[k], head_sums[k]]
            packed = kernel_call(
                functools.partial(vector_pack_kernel, depth),
                [((6 * depth + 2, width), f32)],
                sums_one,
                *grad_q,
                grad_v,
                *[Far(v) for v in terms],
                name="vector_pack",
                scratch=[pltpu.VMEM(v.shape, f32) for v in terms] + [DMA((len(terms),))],
            )[0]
            if outer > 1:
                packed = lax.psum(packed, "ctx", axis_index_groups=outer_groups)
            lines = kernel_call(
                functools.partial(vector_lines_kernel, depth, width_own),
                [((fsdp, 32, 2 * width_own), bf16)],
                packed,
                name="vector_lines",
            )
        count = 1 if l > 0 else fsdp
        shapes = [((width, 3 * feats), bf16), ((width, feats), bf16)]
        if l == 0:
            shapes = [((fsdp, width_own + 32, 4 * feats), bf16)]
        kept = [sums_one, upstream] + ([sums_two] if l + 1 == depth else [])
        *attn_grads, head_sums[l], upstream_b, sums_one, upstream, sums_kept = [
            *kernel_call(
                functools.partial(attn_grad_kernel, feats, count, len(kept)),
                [saved((width if l > 0 else width_own + 32, 4 * feats), bf16)] * count
                + [saved((2, feats), f32), row_bf16]
                + [saved(k.shape, k.dtype) for k in kept],
                attn[0][3],
                attn[1][3],
                attn[0][1],
                attn[1][1],
                *middle_x,
                *grad_q,
                grad_k,
                grad_v,
                upstream_b,
                *(lines or (sums_one,)),
                *kept,
                name="attn_grad",
                scratch=[
                    pltpu.VMEM((all_rows, 3 * feats), bf16),
                    pltpu.VMEM((2, feats), f32),
                ]
                + [pltpu.VMEM(*shape) for shape in shapes]
                + [DMA((count + 2 + len(kept),))],
            ),
            sums_two,
        ][: count + 5]
        if l + 1 == depth:
            sums_two = sums_kept
        if l > 0:
            attn_parts[l] = scatter_grads(attn_grads[0])
            (upstream_b,) = settle(upstream_b, mlp_parts[l])
            upstream_chunks = gather_rows(upstream_b)
        row_sums[l] = (sums_one, sums_two)

    sources = [mlp_parts[0]]
    for l in range(1, depth):
        sources += [mlp_parts[l], attn_parts[l]]
    blocks = 3 * depth - 1
    (stacked,) = kernel_call(
        functools.partial(fetch_kernel, len(sources)),
        [((blocks * width_own, hidden), bf16)],
        *[Far(v) for v in sources],
        name="fetch",
        after=(upstream_b,),
        scratch=[DMA((blocks,))],
    )
    outputs_own, _ = kernel_call(
        functools.partial(sum_out_kernel, shift_row(depth - 1, 3)),
        [saved((rows, width), f32), TOKEN],
        *output_sums[0],
        Far(saved_all[depth - 1][2][1][4]),
        vecs,
        mask,
        name="sum_out",
        scratch=[pltpu.VMEM((rows, width), f32)] * 2 + [DMA((2,))],
    )
    own_term, *other_terms = attn_grads
    other_terms = [shift_z(term, d + 1) for d, term in enumerate(other_terms)]
    crossed = swap_x(stacked)
    others = (swap_y(upstream), swap_y(outputs_own))
    part, mine, pair = kernel_call(
        functools.partial(shard_sum_kernel, depth),
        [
            ((width_own, 4 * feats), bf16),
            ((24, width_own), f32),
            ((2 * blocks * width_own, hidden), bf16),
        ],
        Far(own_term),
        stacked,
        crossed,
        *other_terms,
        name="shard_sum",
        after=others,
        scratch=[pltpu.VMEM(own_term.shape, bf16), DMA((3,))],
    )
    if outer > 1:
        part = lax.psum(part, "ctx", axis_index_groups=outer_groups)
    *placed, place_token = kernel_call(
        functools.partial(place_kernel, depth, hidden, feats),
        [saved(v.shape, f32) for v in (w_qkv, w_out, w_fc1, w_fc2)] + [TOKEN],
        pair,
        swap_core(pair),
        name="place",
        limit=24,
        scratch=[
            pltpu.VMEM((depth, GROUP, width_own, hidden), f32),
            pltpu.VMEM((depth, GROUP, hidden, width_own), f32),
            pltpu.VMEM((depth - 1, GROUP, 3, width_own, feats), f32),
            pltpu.VMEM((depth - 1, GROUP, feats, width_own), f32),
            DMA((16 * depth,)),
        ],
    )
    mine, last_pair = kernel_call(
        functools.partial(vector_plane_kernel, depth),
        [((32, width_own), f32), ((2 * width_own, 4 * feats), bf16)],
        mine,
        swap_xy(mine),
        swap_x(mine),
        swap_y(mine),
        part,
        swap_x(part),
        name="vector_plane",
        after=(place_token,),
    )
    grad_gains, grad_shifts, grad_fc1_bias, grad_qv_bias = kernel_call(
        functools.partial(vector_place_kernel, depth, head_dim),
        [
            (norm_gains.shape, f32),
            (shifts.shape, f32),
            (fc1_bias.shape, f32),
            (qv_bias.shape, f32),
        ],
        mine,
        swap_core(mine),
        name="vector_place",
    )
    grad_inputs, outputs = (
        kernel_call(
            place_rows_kernel,
            [saved(inputs.shape, f32)],
            own,
            other,
            name="place_rows",
            scratch=[DMA((2,))],
        )[0]
        for own, other in zip((upstream, outputs_own), others)
    )
    placed[:2] = kernel_call(
        functools.partial(place_last_kernel, feats),
        [saved(v.shape, f32) for v in (w_qkv, w_out)],
        last_pair,
        swap_core(last_pair),
        Far(placed[0]),
        Far(placed[1]),
        name="place_last",
        scratch=[
            pltpu.VMEM((GROUP, 3, width_own, feats), f32),
            pltpu.VMEM((GROUP, feats, width_own), f32),
            DMA((2 * GROUP,)),
        ],
        aliases={2: 0, 3: 1},
    )
    return (
        outputs,
        grad_inputs,
        grad_gains,
        grad_shifts,
        grad_qv_bias,
        grad_fc1_bias,
        *placed,
    )


def solution(mesh):
    rows = P("fsdp", "ctx", None)
    params = (
        P(None, None, "fsdp"),
        P(None, None, "fsdp"),
        P(None, None, "tp", "fsdp"),
        P(None, "tp", "fsdp"),
        P(None, None, "fsdp", "tp"),
        P(None, "tp", "fsdp"),
        P(None, "fsdp", "tp"),
        P(None, "tp", "fsdp"),
    )
    return jax.shard_map(
        per_device,
        mesh=mesh,
        in_specs=(rows, P("fsdp", None), rows) + params,
        out_specs=(rows, rows) + params,
        check_vma=False,
    )
```

```python
import functools
import math

import jax
import jax.numpy as jnp
from jax import lax
from jax.experimental import pallas as pl
from jax.experimental.pallas import tpu as pltpu
from jax.sharding import PartitionSpec as P

NORM_EPSILON = 1e-06
MASK_FILL = -1e30
ROOT_HALF = 0.7071067811865476
INV_ROOT_TAU = 0.3989422804014327
GROUP = 4
ORDER = (0, 5, 4, 1, 2, 7, 6, 3)
CHIPS = 4

bf16 = jnp.bfloat16
f32 = jnp.float32
VMEM = pl.BlockSpec(memory_space=pltpu.VMEM)
SMEM = pl.BlockSpec(memory_space=pltpu.SMEM)
HBM = pl.BlockSpec(memory_space=pltpu.HBM)
DMA = pltpu.SemaphoreType.DMA
TOKEN = ((8, 128), f32)


def dot(a, b):
    return lax.dot_general(a, b, (((1,), (0,)), ((), ())), preferred_element_type=f32)


def dot_nt(a, b):
    return lax.dot_general(a, b, (((1,), (1,)), ((), ())), preferred_element_type=f32)


def dot_tn(a, b):
    return lax.dot_general(a, b, (((0,), (0,)), ((), ())), preferred_element_type=f32)


class Far:
    def __init__(self, value):
        self.value = value


class Anywhere:
    def __init__(self, value):
        self.value = value


class Scalars:
    def __init__(self, value):
        self.value = value


def saved(shape, dtype):
    return pltpu.HBM(shape, dtype)


def kernel_call(body, outs, *args, name, limit=12, scratch=(), after=(), aliases=None, us=0):
    values, specs = [], []
    for arg in (*args, *after):
        if isinstance(arg, Far):
            values.append(pltpu.with_memory_space_constraint(arg.value, pltpu.HBM))
            specs.append(HBM)
        elif isinstance(arg, Anywhere):
            values.append(arg.value)
            specs.append(pl.BlockSpec(memory_space=pl.ANY))
        elif isinstance(arg, Scalars):
            values.append(arg.value)
            specs.append(SMEM)
        else:
            values.append(arg)
            specs.append(VMEM)
    first, last = len(args), len(args) + len(after)

    def run(*refs):
        body(*refs[:first], *refs[last:])

    out_shape, out_specs = [], []
    for out in outs:
        if isinstance(out, tuple):
            out_shape.append(jax.ShapeDtypeStruct(*out))
            out_specs.append(VMEM)
        else:
            out_shape.append(out)
            out_specs.append(HBM)
    return pl.pallas_call(
        run,
        out_shape=out_shape,
        in_specs=specs,
        out_specs=out_specs,
        scratch_shapes=list(scratch),
        input_output_aliases=aliases or {},
        compiler_params=pltpu.CompilerParams(vmem_limit_bytes=limit << 20),
        cost_estimate=pl.CostEstimate(flops=us * 10**9, bytes_accessed=0, transcendentals=0),
        name=name,
    )(*values)


def start_copies(pairs, sems):
    copies = [
        pltpu.make_async_copy(source, target, sems.at[k])
        for k, (source, target) in enumerate(pairs)
    ]
    for copy in copies:
        copy.start()
    return copies


def row_mean(value):
    return jnp.mean(value, axis=-1, keepdims=True)


def normalize(values):
    center = values - row_mean(values)
    inverse = lax.rsqrt(row_mean(center * center) + NORM_EPSILON)
    return center * inverse, inverse


def lanes_of(head, head_dim, width):
    lane = lax.broadcasted_iota(jnp.int32, (1, width), 1)
    return (lane >= head * head_dim) & (lane < (head + 1) * head_dim)


def assemble(chunks, target):
    rows = chunks[0].shape[0]
    for k, chunk in enumerate(chunks):
        target[k * rows : (k + 1) * rows, :] = chunk[...]


def only(flag, value):
    return jnp.where(flag, value, jnp.zeros_like(value))


def shards(weights):
    if len(weights) == 1:
        rows = weights[0].shape[0]
        return [(pl.ds(0, rows), weights[0])]
    count = len(weights)
    rows = weights[0].shape[0]
    f = lax.axis_index("fsdp")
    found = []
    for d, ref in enumerate(weights):
        place = lax.rem(f + (count - d), count)
        found.append((pl.ds(pl.multiple_of(place * rows, rows), rows), ref))
    return found


def pack_attn_kernel(layer, feats, qkv_hbm, out_hbm, packed_ref, token, qkv, out, sems):
    ci = lax.rem(lax.axis_index("ctx"), GROUP)
    span = pl.ds(pl.multiple_of(ci * feats, feats), feats)
    copies = start_copies(
        [(qkv_hbm.at[layer, :, :, span], qkv), (out_hbm.at[layer, span, :], out)], sems
    )
    copies[0].wait()
    for k in range(3):
        packed_ref[:, k * feats : (k + 1) * feats] = qkv[k]
    copies[1].wait()
    packed_ref[:, 3 * feats :] = out[...].T
    token[...] = jnp.zeros_like(token)


def pack_mlp_kernel(layer, hidden, fc1_hbm, fc2_hbm, packed_ref, token, fc1, fc2, sems):
    ci = lax.rem(lax.axis_index("ctx"), GROUP)
    span = pl.ds(pl.multiple_of(ci * hidden, hidden), hidden)
    copies = start_copies(
        [(fc1_hbm.at[layer, :, span], fc1), (fc2_hbm.at[layer, span, :], fc2)], sems
    )
    copies[0].wait()
    packed_ref[:, :hidden] = fc1[...]
    copies[1].wait()
    packed_ref[:, hidden:] = fc2[...].T
    token[...] = jnp.zeros_like(token)


def prep_upstream_kernel(tp, outer, lengths, cotangent_hbm,
                         upstream_hbm, upstream_b_ref, usable_ref, mask_ref,
                         rows_in, upstream_ref, sems):
    rows = rows_in.shape[0]
    c = lax.axis_index("ctx")
    t = lax.axis_index("tp")
    place = lax.rem(c, GROUP) * tp + t
    start = pl.multiple_of(t * rows, rows)
    copies = start_copies(
        [(cotangent_hbm.at[0, pl.ds(start, rows), :], rows_in)], sems.at[pl.ds(0, 1)]
    )
    lane = lax.broadcasted_iota(jnp.int32, usable_ref.shape, 1)
    limit = jnp.zeros(usable_ref.shape, jnp.int32)
    for o in range(outer):
        for k, d in enumerate(ORDER):
            source = place ^ d
            first_lane = (o * len(ORDER) + k) * rows
            count = lengths[0, o * GROUP + lax.div(source, tp)] - lax.rem(source, tp) * rows
            limit = jnp.where(lane >= first_lane, first_lane + jnp.clip(count, 0, rows), limit)
    usable_ref[...] = jnp.where(lane < limit, 1.0, 0.0)
    row = lax.broadcasted_iota(jnp.int32, mask_ref.shape, 0)
    mask = jnp.where(row + start < lengths[0, c], 1.0, 0.0)
    mask_ref[...] = mask
    copies[0].wait()
    upstream = rows_in[...] * mask[:, 0:1]
    upstream_ref[...] = upstream
    sent = start_copies([(upstream_ref, upstream_hbm)], sems.at[pl.ds(1, 1)])
    upstream_b_ref[...] = upstream.astype(bf16)
    sent[0].wait()


def prep_first_kernel(depth, inputs_hbm, vecs, stream_ref, first_ref, sems):
    rows = stream_ref.shape[0]
    start = pl.multiple_of(lax.axis_index("tp") * rows, rows)
    copies = start_copies([(inputs_hbm.at[0, pl.ds(start, rows), :], stream_ref)], sems)
    copies[0].wait()
    normed, _ = normalize(stream_ref[...])
    shift = vecs[2 * depth : 2 * depth + 1, :]
    first_ref[...] = (normed * vecs[0:1, :] + shift).astype(bf16)


def keep_rows_kernel(*refs):
    chunks, (near_hbm, far_hbm, token, near, far, sems) = refs[:8], refs[8:]
    assemble(chunks[:4], near)
    assemble(chunks[4:], far)
    for copy in start_copies([(near, near_hbm), (far, far_hbm)], sems):
        copy.wait()
    token[...] = jnp.zeros_like(token)


def qkv_kernel(feats, weight_count, *refs):
    c0, c1, c2, c3, *rest = refs
    weights = rest[:weight_count]
    bias, qkv_ref, x = rest[weight_count:]
    assemble((c0, c1, c2, c3), x)
    qkv = sum(dot(x[:, span], w[:, : 3 * feats]) for span, w in shards(weights))
    qkv_ref[:, :feats] = (qkv[:, :feats] + bias[0:1, :]).astype(bf16)
    qkv_ref[:, feats : 2 * feats] = qkv[:, feats : 2 * feats].astype(bf16)
    qkv_ref[:, 2 * feats :] = (qkv[:, 2 * feats :] + bias[1:2, :]).astype(bf16)


def attn_kernel(feats, heads, weight_count, part_count, keep_count, tile, *refs):
    q_ref, *rest = refs
    parts = rest[:part_count]
    weights = rest[part_count : part_count + weight_count]
    rest = rest[part_count + weight_count :]
    usable, *rest = rest
    kept, rest = rest[:keep_count], rest[keep_count:]
    partial_ref, attended_hbm, norm_hbm, *rest = rest
    kept_hbm, rest = rest[:keep_count], rest[keep_count:]
    keys, values, attended_ref, norm_ref, sems = rest
    head_dim = feats // heads
    scale = 1.0 / math.sqrt(head_dim)
    copies = start_copies(list(zip(kept, kept_hbm)), sems)
    first = 0
    for part in parts:
        rows, width = part.shape
        keys[first : first + rows, :] = part[:, width - 2 * feats : width - feats]
        values[first : first + rows, :] = part[:, width - feats :]
        first += rows
    keep = usable[...] > 0.5
    rows = q_ref.shape[0]
    for first in range(0, rows, tile):
        span = slice(first, first + tile)
        q = q_ref[span, :feats]
        attended = None
        for h in range(heads):
            own = lanes_of(h, head_dim, feats)
            scores = dot_nt(only(own, q), keys[...]) * scale
            scores = jnp.where(keep, scores, MASK_FILL)
            highest = jnp.max(scores, axis=-1, keepdims=True)
            raised = jnp.exp(scores - highest)
            total = jnp.sum(raised, axis=-1, keepdims=True)
            soft = (raised * (1.0 / total)).astype(bf16)
            result = dot(soft, values[...])
            log_norm = jnp.broadcast_to(highest + jnp.log(total), (tile, feats))
            if attended is None:
                attended, norms = result, log_norm
            else:
                attended = jnp.where(own, result, attended)
                norms = jnp.where(own, log_norm, norms)
        attended_ref[span, :] = attended.astype(bf16)
        norm_ref[span, :] = norms
    copies += start_copies(
        [(attended_ref, attended_hbm), (norm_ref, norm_hbm)],
        sems.at[pl.ds(keep_count, 2)],
    )
    for span, w in shards(weights):
        partial_ref[:, span] = dot_nt(attended_ref[...], w[:, 3 * feats :]).astype(bf16)
    for copy in copies:
        copy.wait()


def core_sum_kernel(count, *refs):
    pairs, owns = refs[: 2 * count], refs[2 * count : 3 * count]
    peers = refs[3 * count :]
    rows = owns[0].shape[0]
    for j in range(count):
        near, far = pairs[2 * j], pairs[2 * j + 1]
        for k in range(1 + len(peers)):
            span = slice(k * rows, (k + 1) * rows)
            total = near[span, :].astype(f32) + far[span, :].astype(f32)
            if k == 0:
                owns[j][...] = total
            else:
                peers[k - 1][j * rows : (j + 1) * rows, :] = total.astype(bf16)


def total_of(own, xy, x, y, part=0):
    rows = own.shape[0]
    span = slice(part * rows, (part + 1) * rows)
    return (
        own[...] + y[span, :].astype(f32) + x[span, :].astype(f32) + xy[span, :].astype(f32)
    )


def sum_norm_kernel(bias_row, gain_row, shift_row, own, xy, x, y, residual_hbm, vecs,
                    stream_ref, normed_ref, residual, sems):
    copies = start_copies([(residual_hbm, residual)], sems)
    total = total_of(own, xy, x, y) + vecs[bias_row : bias_row + 1, :]
    copies[0].wait()
    stream = residual[...] + total
    stream_ref[...] = stream
    normed, _ = normalize(stream)
    gain = vecs[gain_row : gain_row + 1, :]
    normed_ref[...] = (normed * gain + vecs[shift_row : shift_row + 1, :]).astype(bf16)


def sum_out_kernel(bias_row, own, xy, x, y, residual_hbm, vecs, mask, out_hbm, token,
                   residual, out_ref, sems):
    copies = start_copies([(residual_hbm, residual)], sems.at[pl.ds(0, 1)])
    total = total_of(own, xy, x, y, 1) + vecs[bias_row : bias_row + 1, :]
    copies[0].wait()
    out_ref[...] = (residual[...] + total) * mask[:, 0:1]
    token[...] = jnp.zeros_like(token)
    for copy in start_copies([(out_ref, out_hbm)], sems.at[pl.ds(1, 1)]):
        copy.wait()


def mlp_kernel(hidden, keep_count, saves, load_w, load_count, c0, c1, c2, c3, w, bias, *refs):
    kept, rest = refs[:keep_count], refs[keep_count:]
    sources, rest = rest[:load_count], rest[load_count:]
    partial_ref, x_out, act_out, slope_out, *rest = rest
    kept_hbm, rest = rest[:keep_count], rest[keep_count:]
    targets, rest = rest[:load_count], rest[load_count:]
    loaded = []
    if load_w:
        w_ref, *rest, w_sems, chunk_sems = rest
        rows = c0.shape[0]
        chunks = start_copies(
            [(c, x_out.at[pl.ds(k * rows, rows), :]) for k, c in enumerate((c0, c1, c2, c3))],
            chunk_sems,
        )
        spans = (pl.ds(0, hidden), pl.ds(hidden, hidden))
        loaded = start_copies([(w.at[:, c], w_ref.at[:, c]) for c in spans], w_sems)
        w = w_ref
    if load_count:
        *rest, load_sems = rest
        fetched = start_copies(list(zip(sources, targets)), load_sems)
    else:
        fetched = []
    if saves:
        x, act_ref, slope_ref, sems = rest
    else:
        x, act_ref, slope_ref = x_out, act_out, slope_out
        (sems,) = rest
    copies = start_copies(list(zip(kept, kept_hbm)), sems)
    if load_w:
        for chunk in chunks:
            chunk.wait()
    else:
        assemble((c0, c1, c2, c3), x)
    if saves:
        copies += start_copies([(x, x_out)], sems.at[pl.ds(keep_count, 1)])
    block = hidden // 2
    if load_w:
        loaded[0].wait()
    for k in range(2):
        span = slice(k * block, (k + 1) * block)
        pre = dot(x[...], w[:, span]) + bias[:, span]
        cdf = 0.5 * (1.0 + lax.erf(pre * ROOT_HALF))
        density = jnp.exp(-0.5 * pre * pre) * INV_ROOT_TAU
        slope_ref[k] = cdf + pre * density
        act_ref[:, span] = (pre * cdf).astype(bf16)
        if saves:
            copies += start_copies(
                [(slope_ref.at[k], slope_out.at[k])], sems.at[pl.ds(1 + keep_count + k, 1)]
            )
    if saves:
        copies += start_copies([(act_ref, act_out)], sems.at[pl.ds(3 + keep_count, 1)])
    if load_w:
        loaded[1].wait()
    partial_ref[...] = dot_nt(act_ref[...], w[:, hidden:]).astype(bf16)
    for copy in copies + fetched:
        copy.wait()


def mlp_back_kernel(hidden, chunk_count, fetches, *refs):
    chunks, (w, slope, *rest) = refs[:chunk_count], refs[chunk_count:]
    if fetches:
        *rest, slope_ref, slope_sem = rest
        fetched = start_copies([(slope, slope_ref)], slope_sem)
        slope = slope_ref
    partial_ref, grad_ref, sum_hbm, x, sum_ref, sems = rest
    assemble(chunks, x)
    grad = dot(x[...], w[:, hidden:])
    if fetches:
        fetched[0].wait()
    block = hidden // 2
    for k in range(2):
        span = slice(k * block, (k + 1) * block)
        part = grad[:, span] * slope[k]
        grad_ref[:, span] = part.astype(bf16)
        sum_ref[:, span] = jnp.sum(part, axis=0, keepdims=True)
    sent = start_copies([(sum_ref, sum_hbm)], sems)
    partial_ref[...] = dot_nt(grad_ref[...], w[:, :hidden]).astype(bf16)
    sent[0].wait()


def mlp_grad_kernel(hidden, keep_count, second_near, second_far, act_near, act_far,
                    up_near, up_far, grad_near, grad_far, *refs):
    kept, refs = refs[:keep_count], refs[keep_count:]
    out_hbm, *refs = refs
    kept_hbm, (out_one, out_two, sems) = refs[:keep_count], refs[keep_count:]
    sent = start_copies(list(zip(kept, kept_hbm)), sems.at[pl.ds(2, keep_count)])
    total = dot_tn(up_near[...], act_near[...]) + dot_tn(up_far[...], act_far[...])
    out_two[...] = total.astype(bf16)
    sent += start_copies(
        [(out_two, out_hbm.at[:, pl.ds(hidden, hidden)])], sems.at[pl.ds(0, 1)]
    )
    total = dot_tn(second_near[...], grad_near[...]) + dot_tn(second_far[...], grad_far[...])
    out_one[...] = total.astype(bf16)
    sent += start_copies([(out_one, out_hbm.at[:, pl.ds(0, hidden)])], sems.at[pl.ds(1, 1)])
    for copy in sent:
        copy.wait()


def norm_back(upstream, values, gain):
    normed, inverse = normalize(values)
    scaled = upstream * gain
    back = inverse * (scaled - row_mean(scaled) - normed * row_mean(scaled * normed))
    gain_grad = jnp.sum(upstream * normed, axis=0, keepdims=True)
    return back, gain_grad, jnp.sum(upstream, axis=0, keepdims=True)


def norm_back_two_kernel(gain_row, own, xy, x, y, values, upstream, vecs,
                         grad_ref, grad_b_ref, sums_ref):
    total = total_of(own, xy, x, y)
    up = upstream[...]
    back, gain_grad, shift_grad = norm_back(
        total, values[...], vecs[gain_row : gain_row + 1, :]
    )
    grad = up + back
    grad_ref[...] = grad
    grad_b_ref[...] = grad.astype(bf16)
    sums_ref[0:1, :] = gain_grad
    sums_ref[1:2, :] = shift_grad
    sums_ref[2:3, :] = jnp.sum(grad, axis=0, keepdims=True)
    sums_ref[3:4, :] = jnp.sum(up, axis=0, keepdims=True)


def norm_back_one_kernel(gain_row, own, xy, x, y, values, upstream, vecs, mask,
                         grad_ref, grad_b_ref, sums_ref):
    total = total_of(own, xy, x, y)
    back, gain_grad, shift_grad = norm_back(
        total, values[...], vecs[gain_row : gain_row + 1, :]
    )
    grad = upstream[...] + back
    if mask is not None:
        grad = grad * mask[:, 0:1]
    grad_ref[...] = grad
    grad_b_ref[...] = grad.astype(bf16)
    sums_ref[0:1, :] = gain_grad
    sums_ref[1:2, :] = shift_grad


def attn_back_kernel(feats, heads, weight_count, part_count, tile, carried, *refs):
    c0, c1, c2, c3, *rest = refs
    weights, rest = rest[:weight_count], rest[weight_count:]
    usable, qkv, attended, norms, *rest = rest
    parts, rest = rest[:part_count], rest[part_count:]
    if carried:
        keys_before, values_before, *rest = rest
    x, grad_q, grad_k, grad_v, pairs, grad_att = rest
    head_dim = feats // heads
    scale = 1.0 / math.sqrt(head_dim)
    first = 0
    for part in parts:
        rows, width = part.shape
        pairs[first : first + rows, :] = part[:, width - 2 * feats :]
        first += rows
    assemble((c0, c1, c2, c3), x)
    grad_att[...] = sum(
        dot(x[:, span], w[:, 3 * feats :]) for span, w in shards(weights)
    ).astype(bf16)
    keep = usable[...] > 0.5
    rows = qkv.shape[0]
    if carried:
        sum_k, sum_v = keys_before[...], values_before[...]
    else:
        sum_k = jnp.zeros(grad_k.shape, f32)
        sum_v = jnp.zeros(grad_v.shape, f32)
    keys, values = pairs[:, :feats], pairs[:, feats:]
    for first in range(0, rows, tile):
        span = slice(first, first + tile)
        q = qkv[span, :feats]
        ga = grad_att[span, :]
        products = ga.astype(f32) * attended[span, :].astype(f32)
        gq = None
        for h in range(heads):
            own = lanes_of(h, head_dim, feats)
            q_h = only(own, q)
            ga_h = only(own, ga)
            row_dots = jnp.sum(only(own, products), axis=-1, keepdims=True)
            scores = dot_nt(q_h, keys) * scale
            scores = jnp.where(keep, scores, MASK_FILL)
            soft = jnp.exp(scores - norms[span, h * head_dim : h * head_dim + 1])
            grad_soft = dot_nt(ga_h, values)
            grad_scores = (soft * (grad_soft - row_dots)).astype(bf16)
            part = dot(grad_scores, keys)
            gq = part if gq is None else jnp.where(own, part, gq)
            sum_k = sum_k + dot_tn(grad_scores, q_h) * scale
            sum_v = sum_v + dot_tn(soft.astype(bf16), ga_h)
        grad_q[span, :] = gq * scale
    grad_k[...] = sum_k
    grad_v[...] = sum_v


def project_kernel(feats, first, weight_count, gq, gk, gv, *refs):
    weights, (partial_ref, packed) = refs[:weight_count], refs[weight_count:]
    rows = gq.shape[0]
    span = slice(first, first + rows)
    packed[:, :feats] = gq[...].astype(bf16)
    packed[:, feats : 2 * feats] = gk[span, :].astype(bf16)
    packed[:, 2 * feats :] = gv[span, :].astype(bf16)
    for columns, w in shards(weights):
        partial_ref[:, columns] = dot_nt(packed[...], w[:, : 3 * feats]).astype(bf16)


def attn_grad_kernel(feats, count, keep_count, first_near, first_far, att_near, att_far,
                     up_near, up_far, gq_near, gq_far, gk, gv, passed, lines, *refs):
    kept, refs = refs[:keep_count], refs[keep_count:]
    outs, refs = refs[:count], refs[count:]
    heads_hbm, passed_ref, *refs = refs
    kept_hbm, (packed, sums_ref, *staged, sems) = refs[:keep_count], refs[keep_count:]
    rows = up_near.shape[0]
    used = count + 2
    sent = start_copies(
        [(passed, passed_ref), *zip(kept, kept_hbm)], sems.at[pl.ds(used, 1 + keep_count)]
    )
    packed[:rows, :feats] = gq_near[...].astype(bf16)
    packed[rows:, :feats] = gq_far[...].astype(bf16)
    packed[:, feats : 2 * feats] = gk[...].astype(bf16)
    packed[:, 2 * feats :] = gv[...].astype(bf16)
    sums_ref[0:1, :] = jnp.sum(gq_near[...], axis=0, keepdims=True) + jnp.sum(
        gq_far[...], axis=0, keepdims=True
    )
    sums_ref[1:2, :] = jnp.sum(gv[...], axis=0, keepdims=True)
    sent += start_copies([(sums_ref, heads_hbm)], sems.at[pl.ds(0, 1)])

    def out_part(span):
        return dot_tn(up_near[:, span], att_near[...]) + dot_tn(up_far[:, span], att_far[...])

    def qkv_part(span):
        return dot_tn(first_near[:, span], packed[:rows, :]) + dot_tn(
            first_far[:, span], packed[rows:, :]
        )

    if count == 1:
        out_one, out_two = staged
        whole = slice(None)
        out_two[...] = out_part(whole).astype(bf16)
        sent += start_copies(
            [(out_two, outs[0].at[:, pl.ds(3 * feats, feats)])], sems.at[pl.ds(1, 1)]
        )
        out_one[...] = qkv_part(whole).astype(bf16)
        sent += start_copies(
            [(out_one, outs[0].at[:, pl.ds(0, 3 * feats)])], sems.at[pl.ds(2, 1)]
        )
    else:
        (stage,) = staged
        below = lines.shape[1]
        width_own = outs[0].shape[0] - below
        for d in reversed(range(count)):
            place = lax.rem(lax.axis_index("fsdp") + d, count)
            span = pl.ds(pl.multiple_of(place * width_own, width_own), width_own)
            stage[d, :width_own, : 3 * feats] = qkv_part(span).astype(bf16)
            stage[d, :width_own, 3 * feats :] = out_part(span).astype(bf16)
            stage[d, width_own:, :] = lines[d]
            sent += start_copies([(stage.at[d], outs[d])], sems.at[pl.ds(1 + d, 1)])
    for copy in sent:
        copy.wait()


def settle_kernel(keep_count, after_count, passed, *refs):
    kept, refs = refs[:keep_count], refs[keep_count + after_count :]
    passed_ref, *kept_hbm, sems = refs
    for copy in start_copies([(passed, passed_ref), *zip(kept, kept_hbm)], sems):
        copy.wait()


def fetch_kernel(count, *refs):
    sources, (target, sems) = refs[:count], refs[count:]
    columns = target.shape[1]
    moves = []
    row = 0
    for source in sources:
        rows = source.shape[0]
        for first in range(0, source.shape[1], columns):
            moves.append(
                (source.at[:, pl.ds(first, columns)], target.at[pl.ds(row, rows), :])
            )
            row += rows
    for copy in start_copies(moves, sems):
        copy.wait()


def shard_sum_kernel(depth, own_hbm, stacked, crossed, *refs):
    *others, part_ref, mine_ref, pair_ref, own, sems = refs
    count = stacked.shape[0]
    first, *copies = start_copies(
        [
            (own_hbm, own),
            (stacked, pair_ref.at[pl.ds(0, count), :]),
            (crossed, pair_ref.at[pl.ds(count, count), :]),
        ],
        sems,
    )
    first.wait()
    rows, width = part_ref.shape[0], mine_ref.shape[1]
    terms = [ref[...].astype(f32) for ref in (own, *others)]
    total = terms[0]
    for term in terms[1:]:
        total = total + term
    part_ref[...] = total[:rows, :].astype(bf16)
    lines = total[rows:, :width] + total[rows:, width:]
    mine_ref[: 6 * depth, :] = lines[: 6 * depth, :]
    for k in range(mine_ref.shape[0] - 16):
        mine_ref[16 + k : 17 + k, :] = lines[6 * depth + k : 6 * depth + k + 1, :]
    for copy in copies:
        copy.wait()


def place_kernel(depth, hidden, feats, here, sibling, *refs):
    qkv_hbm, out_hbm, fc1_hbm, fc2_hbm, token, fc1, fc2, qkv, out, sems = refs
    token[...] = jnp.zeros_like(token)
    ci = lax.rem(lax.axis_index("ctx"), GROUP)
    rows = fc1.shape[2]
    count = here.shape[0] // 2
    copies = []

    def send(source, target):
        copies.extend(start_copies([(source, target)], sems.at[pl.ds(len(copies), 1)]))

    for k in range(GROUP):
        stacked = (here, sibling)[k % 2].at[pl.ds(k // 2 * count, count), :]
        wide = pl.ds(pl.multiple_of((ci ^ k) * hidden, hidden), hidden)
        narrow = pl.ds(pl.multiple_of((ci ^ k) * feats, feats), feats)
        for l in range(depth):
            first = 0 if l == 0 else (3 * l - 1) * rows
            fc1[l, k] = stacked[first : first + rows, :].astype(f32)
            send(fc1.at[l, k], fc1_hbm.at[l, :, wide])
            fc2[l, k] = stacked[first + rows : first + 2 * rows, :].T.astype(f32)
            send(fc2.at[l, k], fc2_hbm.at[l, wide, :])
            if l > 0:
                piece = stacked.at[pl.ds(first + 2 * rows, rows), :]
                for j in range(3):
                    qkv[l - 1, k, j] = piece[:, j * feats : (j + 1) * feats].astype(f32)
                send(qkv.at[l - 1, k], qkv_hbm.at[l, :, :, narrow])
                out[l - 1, k] = piece[:, 3 * feats :].T.astype(f32)
                send(out.at[l - 1, k], out_hbm.at[l, narrow, :])
    for copy in copies:
        copy.wait()


def place_last_kernel(feats, vectors, here, sibling, qkv_in, out_in, mine, far, *refs):
    qkv_hbm, out_hbm, *vector_refs, qkv, out, sems = refs
    ci = lax.rem(lax.axis_index("ctx"), GROUP)
    rows = here.shape[0] // 2
    copies = []
    for k in range(GROUP):
        piece = (here, sibling)[k % 2].at[pl.ds(k // 2 * rows, rows), :]
        span = pl.ds(pl.multiple_of((ci ^ k) * feats, feats), feats)
        for j in range(3):
            qkv[k, j] = piece[:, j * feats : (j + 1) * feats].astype(f32)
        copies += start_copies(
            [(qkv.at[k], qkv_hbm.at[0, :, :, span])], sems.at[pl.ds(2 * k, 1)]
        )
        out[k] = piece[:, 3 * feats :].T.astype(f32)
        copies += start_copies(
            [(out.at[k], out_hbm.at[0, span, :])], sems.at[pl.ds(2 * k + 1, 1)]
        )
    vectors(mine, far, *vector_refs)
    for copy in copies:
        copy.wait()


def vector_pack_kernel(depth, one_now, gq_near, gq_far, gv, *refs):
    count = 5 * depth - 2
    out_ref, *found, sems = refs[count:]
    copies = start_copies(list(zip(refs[:count], found)), sems)
    out_ref[...] = jnp.zeros_like(out_ref)
    feats = gv.shape[1]
    head_now = [
        jnp.sum(gq_near[...], axis=0, keepdims=True) + jnp.sum(gq_far[...], axis=0, keepdims=True),
        jnp.sum(gv[...], axis=0, keepdims=True),
    ]
    for copy in copies:
        copy.wait()
    for l in range(depth):
        if l == 0:
            one, (two, unit_near, unit_far) = one_now, found[:3]
            heads = head_now
        else:
            one, two, unit_near, unit_far, head = found[5 * l - 2 : 5 * l + 3]
            heads = [head[0:1, :], head[1:2, :]]
        out_ref[6 * l : 6 * l + 1, :] = one[0:1, :]
        out_ref[6 * l + 1 : 6 * l + 2, :] = two[0:1, :]
        out_ref[6 * l + 2 : 6 * l + 3, :] = one[1:2, :]
        out_ref[6 * l + 3 : 6 * l + 6, :] = two[1:4, :]
        units = unit_near.shape[1]
        row = 6 * depth
        out_ref[row : row + 1, l * units : (l + 1) * units] = unit_near[...] + unit_far[...]
        for j in range(2):
            start = (2 * l + j) * feats
            out_ref[row + 1 : row + 2, start : start + feats] = heads[j]


def vector_lines_kernel(depth, width_own, packed, lines_ref):
    count = lines_ref.shape[0]
    f = lax.axis_index("fsdp")
    total = packed[...]
    high = total.astype(bf16).astype(f32)
    low = total - high
    lines_ref[...] = jnp.zeros_like(lines_ref)
    last = 6 * depth
    for k, value in enumerate((high, low)):
        lanes = slice(k * width_own, (k + 1) * width_own)
        columns = [value[:, a * width_own : (a + 1) * width_own] for a in range(count)]
        for d in range(count):
            mine = columns[0]
            for a in range(1, count):
                mine = jnp.where(lax.rem(f + d, count) == a, columns[a], mine)
            rows = [mine[:last, :]]
            for r in range(2):
                for a in range(count):
                    rows.append(columns[a][last + r : last + r + 1, :])
            rows.append(jnp.zeros((lines_ref.shape[1] - last - 2 * count, width_own), f32))
            lines_ref[d, :, lanes] = jnp.concatenate(rows, axis=0).astype(bf16)


def vector_plane_kernel(depth, own, xy, x, y, part, part_x, out_ref, pair_ref):
    last = 6 * depth
    rows = part.shape[0]
    pair_ref[:rows, :] = part[...]
    pair_ref[rows:, :] = part_x[...]
    out_ref[:last, :] = own[:last, :] + xy[:last, :] + x[:last, :] + y[:last, :]
    out_ref[16:24, :] = own[16:24, :]
    out_ref[24:32, :] = x[16:24, :]


def vector_place_kernel(depth, head_dim, own, far, gains_ref, shifts_ref, unit_ref, heads_ref):
    total = own[: 6 * depth, :] + far[: 6 * depth, :]
    for l in range(depth):
        gains_ref[l] = total[6 * l : 6 * l + 2, :]
        shifts_ref[l] = total[6 * l + 2 : 6 * l + 6, :]
    pieces = (own[16:24, :], far[16:24, :], own[24:32, :], far[24:32, :])
    ci = lax.rem(lax.axis_index("ctx"), GROUP)
    f = lax.axis_index("fsdp")

    def of_place(c):
        k = ci ^ c
        found = pieces[0]
        for j in range(1, GROUP):
            found = jnp.where(k == j, pieces[j], found)
        return found

    width_own = own.shape[1]
    units = of_place(f)
    parts = unit_ref.shape[2] // width_own
    for l in range(depth):
        for j in range(parts):
            row = l * parts + j
            unit_ref[l, :, j * width_own : (j + 1) * width_own] = units[row : row + 1, :]
    head_own = heads_ref.shape[3]
    heads = heads_ref.shape[2] // GROUP
    for c in range(GROUP):
        found = of_place(c)
        for l in range(depth):
            for j in range(2):
                for h in range(heads):
                    first = ((2 * l + j) * heads + h) * head_dim
                    row, lane = 4 + first // width_own, first % width_own
                    value = found[row : row + 1, lane : lane + head_own]
                    for a in range(1, head_dim // head_own):
                        start = lane + a * head_own
                        value = jnp.where(
                            f == a, found[row : row + 1, start : start + head_own], value
                        )
                    heads_ref[l, j, c * heads + h : c * heads + h + 1, :] = value


def place_rows_kernel(count, *refs):
    terms, outs, sems = refs[: 2 * count], refs[2 * count : 3 * count], refs[-1]
    rows = terms[0].shape[0]
    start = pl.multiple_of(lax.axis_index("tp") * rows, rows)
    places = (pl.ds(start, rows), pl.ds(pl.multiple_of(rows - start, rows), rows))
    moves = [
        (terms[2 * k + j], out.at[0, places[j], :]) for k, out in enumerate(outs) for j in range(2)
    ]
    for copy in start_copies(moves, sems):
        copy.wait()


def per_device(
    inputs, lengths, cotangent, norm_gains, shifts, qv_bias, fc1_bias, w_qkv, w_out, w_fc1, w_fc2
):
    depth = w_qkv.shape[0]
    width_own = w_qkv.shape[2]
    fsdp = lax.axis_size("fsdp")
    tp = lax.axis_size("tp")
    ctx = lax.axis_size("ctx")
    outer = ctx // GROUP
    rows = inputs.shape[1] // tp
    half = rows * CHIPS
    all_rows = 2 * half
    head_own = qv_bias.shape[3]
    head_dim = head_own * fsdp
    heads = qv_bias.shape[2] // GROUP
    feats = heads * head_dim
    hidden = w_fc1.shape[2] // GROUP
    width = width_own * fsdp
    t = lax.axis_index("tp")
    f = lax.axis_index("fsdp")
    ci = lax.axis_index("ctx") % GROUP
    tile = half // 2
    attn_limit = 12 if outer == 1 else 48

    def swap_core(value):
        return lax.ppermute(value, "ctx", [(i, i ^ 1) for i in range(ctx)])

    def swap_x(value):
        return lax.ppermute(value, "ctx", [(i, i ^ 2) for i in range(ctx)])

    def swap_y(value):
        return lax.ppermute(value, "tp", [(i, i ^ 1) for i in range(tp)])

    def swap_xy(value):
        pairs = [
            (i * tp + k, (i ^ 2) * tp + (k ^ 1)) for i in range(ctx) for k in range(tp)
        ]
        return lax.ppermute(value, ("ctx", "tp"), pairs)

    def shift_z(value, d):
        return lax.ppermute(value, "fsdp", [(i, (i + d) % fsdp) for i in range(fsdp)])

    outer_groups = [[o * GROUP + i for o in range(outer)] for i in range(GROUP)]

    def gather_rows(own):
        near = (own, swap_xy(own), swap_x(own), swap_y(own))
        return near, tuple(swap_core(chunk) for chunk in near)

    def settle(value, there, *kept):
        shape = value.value if isinstance(value, Far) else value
        return kernel_call(
            functools.partial(settle_kernel, len(kept), 1),
            [(shape.shape, shape.dtype)] + [saved(k.shape, k.dtype) for k in kept],
            value,
            *kept,
            Far(there),
            name="settle",
            scratch=[DMA((1 + len(kept),))],
        )

    def reduce_rows(*pairs, after=()):
        count = len(pairs)
        *owns, xy, x, y = kernel_call(
            functools.partial(core_sum_kernel, count),
            [((rows, width), f32)] * count + [((count * rows, width), bf16)] * 3,
            *[v for near, far in pairs for v in (near, swap_core(far))],
            name="core_sum",
            after=after,
        )
        peers = (swap_xy(xy), swap_x(x), swap_y(y))
        return [(own, *peers) for own in owns]

    def pack_attn(l, after):
        return kernel_call(
            functools.partial(pack_attn_kernel, l, feats),
            [((width_own, 4 * feats), bf16), TOKEN],
            Far(w_qkv),
            Far(w_out),
            name="pack_attn",
            after=after,
            scratch=[
                pltpu.VMEM((3, width_own, feats), bf16),
                pltpu.VMEM((feats, width_own), bf16),
                DMA((2,)),
            ],
        )

    def pack_mlp(l, after):
        return kernel_call(
            functools.partial(pack_mlp_kernel, l, hidden),
            [((width_own, 2 * hidden), bf16), TOKEN],
            Far(w_fc1),
            Far(w_fc2),
            name="pack_mlp",
            after=after,
            scratch=[
                pltpu.VMEM((width_own, hidden), bf16),
                pltpu.VMEM((hidden, width_own), bf16),
                DMA((2,)),
            ],
        )

    attn_w = []
    mlp_w = []
    token = None
    for l in range(depth):
        own, token = pack_attn(l, () if token is None else (token,))
        attn_w.append((lax.all_gather(own, "fsdp", axis=0, tiled=True),))
        own, token = pack_mlp(l, (token,))
        mlp_w.append(lax.all_gather(own, "fsdp", axis=0, tiled=True))
        if l == 0:
            pack_token = token

    qv_own = lax.dynamic_slice_in_dim(qv_bias, ci * heads, heads, axis=2)
    vec_rows = depth * 6
    c1_rows = depth * fc1_bias.shape[2] // width_own
    qv_own = qv_own.reshape(1, -1)
    small_own = jnp.concatenate(
        [
            norm_gains.reshape(-1, width_own),
            shifts.reshape(-1, width_own),
            fc1_bias.reshape(-1, width_own),
            jnp.pad(qv_own, ((0, 0), (0, width_own - qv_own.shape[1]))),
        ],
        axis=0,
    )
    shifted = [small_own] + [shift_z(small_own, d) for d in range(1, fsdp)]

    def shard(a):
        picked = shifted[0]
        for d in range(1, fsdp):
            picked = jnp.where((f - d) % fsdp == a, shifted[d], picked)
        return picked.astype(f32)

    small = [shard(a) for a in range(fsdp)]
    vecs = jnp.concatenate([s[:vec_rows] for s in small], axis=1)
    fc1_all = shard(ci)[vec_rows : vec_rows + c1_rows].reshape(depth, 1, hidden)
    qv_all = jnp.stack(
        [s[vec_rows + c1_rows, : qv_own.shape[1]].reshape(depth, 2, heads, head_own) for s in small],
        axis=3,
    ).reshape(depth, 2, feats)

    def gain_row(l, i):
        return 2 * l + i

    def shift_row(l, i):
        return 2 * depth + 4 * l + i

    key_rows = outer * all_rows
    row_f32 = ((rows, width), f32)
    row_bf16 = ((rows, width), bf16)
    upstream, upstream_b, usable, mask = kernel_call(
        functools.partial(prep_upstream_kernel, tp, outer),
        [saved((rows, width), f32), row_bf16, ((1, key_rows), f32), ((rows, 128), f32)],
        Scalars(lengths),
        Far(cotangent),
        name="prep_upstream",
        after=(pack_token,),
        scratch=[pltpu.VMEM((rows, width), f32), pltpu.VMEM((rows, width), f32), DMA((2,))],
    )
    near, far = gather_rows(upstream_b)
    half_x = pltpu.VMEM((half, width), bf16)
    *upstream_rows, upstream_token = kernel_call(
        keep_rows_kernel,
        [saved((half, width), bf16)] * 2 + [TOKEN],
        *near,
        *far,
        name="keep_rows",
        scratch=[half_x, half_x, DMA((2,))],
    )
    stream, first = kernel_call(
        functools.partial(prep_first_kernel, depth),
        [row_f32, row_bf16],
        Far(inputs),
        vecs,
        name="prep_first",
        scratch=[DMA((1,))],
    )
    first_chunks = gather_rows(first)

    partial_out = ((half, width), bf16)
    saved_all = []
    for l in range(depth):
        qkv = []
        first_x = []
        for side in (0, 1):
            qkv_half, x_half = kernel_call(
                functools.partial(qkv_kernel, feats, len(attn_w[l])),
                [((half, 3 * feats), bf16), ((half, width), bf16)],
                *first_chunks[side],
                *attn_w[l],
                qv_all[l],
                name="qkv",
                after=(upstream_token,) if l == 0 and side == 0 else (),
            )
            qkv.append(qkv_half)
            first_x.append(x_half)
        if outer > 1:
            pairs = jnp.concatenate([part[:, feats:] for part in qkv], axis=0)
            pairs = lax.all_gather(
                pairs, "ctx", axis=0, tiled=True, axis_index_groups=outer_groups
            )
            key_parts = (pairs,)
        else:
            key_parts = tuple(qkv)
        attn = [None, None]
        for side in (1, 0):
            kept = (first_x[side], qkv[side]) + ((stream,) if side == 1 else ())
            attn[side] = kernel_call(
                functools.partial(
                    attn_kernel, feats, heads, len(attn_w[l]), len(key_parts), len(kept), tile
                ),
                [partial_out, saved((half, feats), bf16), saved((half, feats), f32)]
                + [saved(k.shape, k.dtype) for k in kept],
                qkv[side],
                *key_parts,
                *attn_w[l],
                usable,
                *kept,
                name="attn",
                limit=attn_limit,
                scratch=[
                    pltpu.VMEM((key_rows, feats), bf16),
                    pltpu.VMEM((key_rows, feats), bf16),
                    pltpu.VMEM((half, feats), bf16),
                    pltpu.VMEM((half, feats), f32),
                    DMA((len(kept) + 2,)),
                ],
            )
        (sums,) = reduce_rows((attn[0][0], attn[1][0]))
        middle, second = kernel_call(
            functools.partial(sum_norm_kernel, shift_row(l, 2), gain_row(l, 1), shift_row(l, 1)),
            [row_f32, row_bf16],
            *sums,
            Far(attn[1][5]),
            vecs,
            name="sum_norm",
            scratch=[pltpu.VMEM((rows, width), f32), DMA((1,))],
        )
        second_chunks = gather_rows(second)
        mlp = [None, None]
        for side in (1, 0):
            kept = (middle,) if side == 1 else ()
            saves = l + 1 < depth
            load_w = not saves and side == 1
            loads = tuple(upstream_rows) if not saves and side == 0 else ()
            shapes = [
                ((half, width), bf16),
                ((half, hidden), bf16),
                ((2, half, hidden // 2), f32),
            ]
            mlp[side] = kernel_call(
                functools.partial(mlp_kernel, hidden, len(kept), saves, load_w, len(loads)),
                [partial_out]
                + [saved(*shape) if saves else shape for shape in shapes]
                + [saved(k.shape, k.dtype) for k in kept]
                + [(v.shape, v.dtype) for v in loads]
                + ([(mlp_w[l].shape, bf16)] if load_w else []),
                *[Anywhere(c) if load_w else c for c in second_chunks[side]],
                Far(mlp_w[l]) if load_w else mlp_w[l],
                fc1_all[l],
                *kept,
                *[Far(v) for v in loads],
                name="mlp",
                scratch=[pltpu.VMEM(*shape) for shape in shapes if saves]
                + [DMA((4 + len(kept),))]
                + ([DMA((2,)), DMA((CHIPS,))] if load_w else [])
                + [DMA((len(loads),)) for _ in loads[:1]],
            )
            if load_w:
                *mlp[side], mlp_w[l] = mlp[side]
            if loads:
                *mlp[side], near, far = mlp[side]
                upstream_chunks = [(near,), (far,)]
        saved_all.append((attn, pairs if outer > 1 else None, mlp))
        if l + 1 < depth:
            (sums,) = reduce_rows((mlp[0][0], mlp[1][0]))
            stream, first = kernel_call(
                functools.partial(
                    sum_norm_kernel, shift_row(l, 3), gain_row(l + 1, 0), shift_row(l + 1, 0)
                ),
                [row_f32, row_bf16],
                *sums,
                Far(mlp[1][4]),
                vecs,
                name="sum_norm",
                scratch=[pltpu.VMEM((rows, width), f32), DMA((1,))],
            )
            first_chunks = gather_rows(first)

    def scatter_grads(grad):
        part = lax.psum_scatter(grad, "fsdp", scatter_dimension=0, tiled=True)
        if outer > 1:
            part = lax.psum(part, "ctx", axis_index_groups=outer_groups)
        return part

    row_sums = [None] * depth
    unit_sums = [None] * depth
    head_sums = [None] * depth
    mlp_parts = [None] * depth
    attn_parts = [None] * depth
    for l in reversed(range(depth)):
        attn, pairs, mlp = saved_all[l]
        back = [None, None]
        for side in (1, 0):
            fetches = l + 1 < depth and side == 0
            back[side] = kernel_call(
                functools.partial(mlp_back_kernel, hidden, len(upstream_chunks[side]), fetches),
                [
                    partial_out,
                    ((half, hidden), bf16),
                    saved((1, hidden), f32),
                    ((half, width), bf16),
                ],
                *upstream_chunks[side],
                mlp_w[l],
                Far(mlp[side][3]) if fetches else mlp[side][3],
                name="mlp_back",
                scratch=[pltpu.VMEM((1, hidden), f32), DMA((1,))]
                + ([pltpu.VMEM(mlp[side][3].shape, f32), DMA((1,))] if fetches else []),
            )
        kept = [back[0][0], back[1][0]]
        if l + 1 == depth:
            kept += [mlp[0][0], mlp[1][0]]
        mlp_grad, *kept = kernel_call(
            functools.partial(mlp_grad_kernel, hidden, len(kept)),
            [saved((width, 2 * hidden), bf16)] + [saved(k.shape, k.dtype) for k in kept],
            mlp[0][1],
            mlp[1][1],
            mlp[0][2],
            mlp[1][2],
            back[0][3],
            back[1][3],
            back[0][1],
            back[1][1],
            *kept,
            name="mlp_grad",
            scratch=[
                pltpu.VMEM((width, hidden), bf16),
                pltpu.VMEM((width, hidden), bf16),
                DMA((2 + len(kept),)),
            ],
        )
        mlp_parts[l] = scatter_grads(mlp_grad)
        (sums,) = reduce_rows(tuple(kept[:2]))
        if l + 1 == depth:
            output_pair = tuple(kept[2:])
        unit_sums[l] = (back[0][2], back[1][2])
        grad_middle, middle_b, sums_two = kernel_call(
            functools.partial(norm_back_two_kernel, gain_row(l, 1)),
            [row_f32, row_bf16, ((4, width), f32)],
            *sums,
            mlp[1][4],
            upstream,
            vecs,
            name="norm_back_two",
        )
        if l + 1 < depth:
            middle_b, sums_two, grad_middle = settle(
                middle_b, attn_parts[l + 1], sums_two, grad_middle
            )
        middle_chunks = gather_rows(middle_b)
        grad_q = [None, None]
        middle_x = [None, None]
        carried = ()
        for side in (0, 1):
            key_parts = (pairs,) if outer > 1 else (attn[0][4], attn[1][4])
            middle_x[side], grad_q[side], *carried = kernel_call(
                functools.partial(
                    attn_back_kernel,
                    feats,
                    heads,
                    len(attn_w[l]),
                    len(key_parts),
                    tile,
                    len(carried) > 0,
                ),
                [
                    ((half, width), bf16),
                    ((half, feats), f32),
                    ((key_rows, feats), f32),
                    ((key_rows, feats), f32),
                ],
                *middle_chunks[side],
                *attn_w[l],
                usable,
                attn[side][4],
                attn[side][1],
                attn[side][2],
                *key_parts,
                *carried,
                name="attn_back",
                scratch=[
                    pltpu.VMEM((key_rows, 2 * feats), bf16),
                    pltpu.VMEM((half, feats), bf16),
                ],
                limit=attn_limit,
            )
        grad_k, grad_v = carried
        if outer > 1:
            grad_k, grad_v = (
                lax.psum_scatter(
                    v, "ctx", scatter_dimension=0, tiled=True, axis_index_groups=outer_groups
                )
                for v in (grad_k, grad_v)
            )

        def project(side, after):
            return kernel_call(
                functools.partial(project_kernel, feats, side * half, len(attn_w[l])),
                [partial_out],
                grad_q[side],
                grad_k,
                grad_v,
                *attn_w[l],
                name="project",
                after=after,
                scratch=[pltpu.VMEM((half, 3 * feats), bf16)],
            )[0]

        far_part = project(1, ())
        near_part = project(0, ())
        pairs_now = [(near_part, far_part)]
        if l == 0:
            pairs_now.append(output_pair)
        sums, *output_sums = reduce_rows(*pairs_now)
        body = functools.partial(norm_back_one_kernel, gain_row(l, 0))
        if l > 0:
            masked = ()
            body = lambda *refs, body=body: body(*refs[:7], None, *refs[7:])
        else:
            masked = (mask,)
        upstream, upstream_b, sums_one = kernel_call(
            body,
            [row_f32, row_bf16, ((2, width), f32)],
            *sums,
            attn[1][5],
            grad_middle,
            vecs,
            *masked,
            name="norm_back_one",
        )
        lines = ()
        if l == 0:
            terms = [sums_two, *unit_sums[0]]
            for k in range(1, depth):
                terms += [*row_sums[k], *unit_sums[k], head_sums[k]]
            packed = kernel_call(
                functools.partial(vector_pack_kernel, depth),
                [((6 * depth + 2, width), f32)],
                sums_one,
                *grad_q,
                grad_v,
                *[Far(v) for v in terms],
                name="vector_pack",
                scratch=[pltpu.VMEM(v.shape, f32) for v in terms] + [DMA((len(terms),))],
            )[0]
            if outer > 1:
                packed = lax.psum(packed, "ctx", axis_index_groups=outer_groups)
            lines = kernel_call(
                functools.partial(vector_lines_kernel, depth, width_own),
                [((fsdp, 32, 2 * width_own), bf16)],
                packed,
                name="vector_lines",
            )
        count = 1 if l > 0 else fsdp
        shapes = [((width, 3 * feats), bf16), ((width, feats), bf16)]
        if l == 0:
            shapes = [((fsdp, width_own + 32, 4 * feats), bf16)]
        kept = [sums_one, upstream] + ([sums_two] if l + 1 == depth else [])
        *attn_grads, head_sums[l], upstream_b, sums_one, upstream, sums_kept = [
            *kernel_call(
                functools.partial(attn_grad_kernel, feats, count, len(kept)),
                [saved((width if l > 0 else width_own + 32, 4 * feats), bf16)] * count
                + [saved((2, feats), f32), saved(*row_bf16) if l > 0 else row_bf16]
                + [saved(k.shape, k.dtype) for k in kept],
                attn[0][3],
                attn[1][3],
                attn[0][1],
                attn[1][1],
                *middle_x,
                *grad_q,
                grad_k,
                grad_v,
                upstream_b,
                *(lines or (sums_one,)),
                *kept,
                name="attn_grad",
                scratch=[
                    pltpu.VMEM((all_rows, 3 * feats), bf16),
                    pltpu.VMEM((2, feats), f32),
                ]
                + [pltpu.VMEM(*shape) for shape in shapes]
                + [DMA((count + 3 + len(kept),))],
            ),
            sums_two,
        ][: count + 5]
        if l + 1 == depth:
            sums_two = sums_kept
        if l > 0:
            attn_parts[l] = scatter_grads(attn_grads[0])
            (upstream_b,) = settle(Far(upstream_b), mlp_parts[l])
            upstream_chunks = gather_rows(upstream_b)
        row_sums[l] = (sums_one, sums_two)

    sources = [mlp_parts[0]]
    for l in range(1, depth):
        sources += [mlp_parts[l], attn_parts[l]]
    blocks = 3 * depth - 1
    (stacked,) = kernel_call(
        functools.partial(fetch_kernel, len(sources)),
        [((blocks * width_own, hidden), bf16)],
        *[Far(v) for v in sources],
        name="fetch",
        after=(upstream_b,),
        scratch=[DMA((blocks,))],
    )
    outputs_own, _ = kernel_call(
        functools.partial(sum_out_kernel, shift_row(depth - 1, 3)),
        [saved((rows, width), f32), TOKEN],
        *output_sums[0],
        Far(saved_all[depth - 1][2][1][4]),
        vecs,
        mask,
        name="sum_out",
        scratch=[pltpu.VMEM((rows, width), f32)] * 2 + [DMA((2,))],
    )
    own_term, *other_terms = attn_grads
    other_terms = [shift_z(term, d + 1) for d, term in enumerate(other_terms)]
    crossed = swap_x(stacked)
    others = (swap_y(upstream), swap_y(outputs_own))
    part, mine, pair = kernel_call(
        functools.partial(shard_sum_kernel, depth),
        [
            ((width_own, 4 * feats), bf16),
            ((24, width_own), f32),
            ((2 * blocks * width_own, hidden), bf16),
        ],
        Far(own_term),
        stacked,
        crossed,
        *other_terms,
        name="shard_sum",
        after=others,
        scratch=[pltpu.VMEM(own_term.shape, bf16), DMA((3,))],
    )
    if outer > 1:
        part = lax.psum(part, "ctx", axis_index_groups=outer_groups)
    *placed, place_token = kernel_call(
        functools.partial(place_kernel, depth, hidden, feats),
        [saved(v.shape, f32) for v in (w_qkv, w_out, w_fc1, w_fc2)] + [TOKEN],
        pair,
        swap_core(pair),
        name="place",
        limit=24,
        scratch=[
            pltpu.VMEM((depth, GROUP, width_own, hidden), f32),
            pltpu.VMEM((depth, GROUP, hidden, width_own), f32),
            pltpu.VMEM((depth - 1, GROUP, 3, width_own, feats), f32),
            pltpu.VMEM((depth - 1, GROUP, feats, width_own), f32),
            DMA((16 * depth,)),
        ],
    )
    mine, last_pair = kernel_call(
        functools.partial(vector_plane_kernel, depth),
        [((32, width_own), f32), ((2 * width_own, 4 * feats), bf16)],
        mine,
        swap_xy(mine),
        swap_x(mine),
        swap_y(mine),
        part,
        swap_x(part),
        name="vector_plane",
        after=(place_token,),
    )
    grad_inputs, outputs = kernel_call(
        functools.partial(place_rows_kernel, 2),
        [saved(inputs.shape, f32)] * 2,
        *(upstream, others[0], outputs_own, others[1]),
        name="place_rows",
        scratch=[DMA((4,))],
    )
    *placed[:2], grad_gains, grad_shifts, grad_fc1_bias, grad_qv_bias = kernel_call(
        functools.partial(
            place_last_kernel, feats, functools.partial(vector_place_kernel, depth, head_dim)
        ),
        [saved(v.shape, f32) for v in (w_qkv, w_out)]
        + [(v.shape, f32) for v in (norm_gains, shifts, fc1_bias, qv_bias)],
        last_pair,
        swap_core(last_pair),
        Far(placed[0]),
        Far(placed[1]),
        mine,
        swap_core(mine),
        name="place_last",
        scratch=[
            pltpu.VMEM((GROUP, 3, width_own, feats), f32),
            pltpu.VMEM((GROUP, feats, width_own), f32),
            DMA((2 * GROUP,)),
        ],
        aliases={2: 0, 3: 1},
    )
    return (
        outputs,
        grad_inputs,
        grad_gains,
        grad_shifts,
        grad_qv_bias,
        grad_fc1_bias,
        *placed,
    )


def solution(mesh):
    rows = P("fsdp", "ctx", None)
    params = (
        P(None, None, "fsdp"),
        P(None, None, "fsdp"),
        P(None, None, "tp", "fsdp"),
        P(None, "tp", "fsdp"),
        P(None, None, "fsdp", "tp"),
        P(None, "tp", "fsdp"),
        P(None, "fsdp", "tp"),
        P(None, "tp", "fsdp"),
    )
    return jax.shard_map(
        per_device,
        mesh=mesh,
        in_specs=(rows, P("fsdp", None), rows) + params,
        out_specs=(rows, rows) + params,
        check_vma=False,
    )
```

```python
import functools
import math

import jax
import jax.numpy as jnp
from jax import lax
from jax.experimental import pallas as pl
from jax.experimental.pallas import tpu as pltpu
from jax.sharding import PartitionSpec as P

NORM_EPSILON = 1e-06
MASK_FILL = -1e30
ROOT_HALF = 0.7071067811865476
INV_ROOT_TAU = 0.3989422804014327
GROUP = 4
ORDER = (0, 5, 4, 1, 2, 7, 6, 3)
CHIPS = 4

bf16 = jnp.bfloat16
f32 = jnp.float32
VMEM = pl.BlockSpec(memory_space=pltpu.VMEM)
SMEM = pl.BlockSpec(memory_space=pltpu.SMEM)
HBM = pl.BlockSpec(memory_space=pltpu.HBM)
DMA = pltpu.SemaphoreType.DMA
TOKEN = ((8, 128), f32)


def dot(a, b):
    return lax.dot_general(a, b, (((1,), (0,)), ((), ())), preferred_element_type=f32)


def dot_nt(a, b):
    return lax.dot_general(a, b, (((1,), (1,)), ((), ())), preferred_element_type=f32)


def dot_tn(a, b):
    return lax.dot_general(a, b, (((0,), (0,)), ((), ())), preferred_element_type=f32)


class Far:
    def __init__(self, value):
        self.value = value


class Anywhere:
    def __init__(self, value):
        self.value = value


class Scalars:
    def __init__(self, value):
        self.value = value


def saved(shape, dtype):
    return pltpu.HBM(shape, dtype)


def kernel_call(body, outs, *args, name, limit=12, scratch=(), after=(), aliases=None, us=0):
    values, specs = [], []
    for arg in (*args, *after):
        if isinstance(arg, Far):
            values.append(pltpu.with_memory_space_constraint(arg.value, pltpu.HBM))
            specs.append(HBM)
        elif isinstance(arg, Anywhere):
            values.append(arg.value)
            specs.append(pl.BlockSpec(memory_space=pl.ANY))
        elif isinstance(arg, Scalars):
            values.append(arg.value)
            specs.append(SMEM)
        else:
            values.append(arg)
            specs.append(VMEM)
    first, last = len(args), len(args) + len(after)

    def run(*refs):
        body(*refs[:first], *refs[last:])

    out_shape, out_specs = [], []
    for out in outs:
        if isinstance(out, tuple):
            out_shape.append(jax.ShapeDtypeStruct(*out))
            out_specs.append(VMEM)
        else:
            out_shape.append(out)
            out_specs.append(HBM)
    return pl.pallas_call(
        run,
        out_shape=out_shape,
        in_specs=specs,
        out_specs=out_specs,
        scratch_shapes=list(scratch),
        input_output_aliases=aliases or {},
        compiler_params=pltpu.CompilerParams(vmem_limit_bytes=limit << 20),
        cost_estimate=pl.CostEstimate(flops=us * 10**9, bytes_accessed=0, transcendentals=0),
        name=name,
    )(*values)


def start_copies(pairs, sems):
    copies = [
        pltpu.make_async_copy(source, target, sems.at[k])
        for k, (source, target) in enumerate(pairs)
    ]
    for copy in copies:
        copy.start()
    return copies


def row_mean(value):
    return jnp.mean(value, axis=-1, keepdims=True)


def normalize(values):
    center = values - row_mean(values)
    inverse = lax.rsqrt(row_mean(center * center) + NORM_EPSILON)
    return center * inverse, inverse


def lanes_of(head, head_dim, width):
    lane = lax.broadcasted_iota(jnp.int32, (1, width), 1)
    return (lane >= head * head_dim) & (lane < (head + 1) * head_dim)


def assemble(chunks, target):
    rows = chunks[0].shape[0]
    for k, chunk in enumerate(chunks):
        target[k * rows : (k + 1) * rows, :] = chunk[...]


def only(flag, value):
    return jnp.where(flag, value, jnp.zeros_like(value))


def shards(weights):
    if len(weights) == 1:
        rows = weights[0].shape[0]
        return [(pl.ds(0, rows), weights[0])]
    count = len(weights)
    rows = weights[0].shape[0]
    f = lax.axis_index("fsdp")
    found = []
    for d, ref in enumerate(weights):
        place = lax.rem(f + (count - d), count)
        found.append((pl.ds(pl.multiple_of(place * rows, rows), rows), ref))
    return found


def pack_attn_kernel(layer, feats, qkv_hbm, out_hbm, packed_ref, token, qkv, out, sems):
    ci = lax.rem(lax.axis_index("ctx"), GROUP)
    span = pl.ds(pl.multiple_of(ci * feats, feats), feats)
    copies = start_copies(
        [(qkv_hbm.at[layer, :, :, span], qkv), (out_hbm.at[layer, span, :], out)], sems
    )
    copies[0].wait()
    for k in range(3):
        packed_ref[:, k * feats : (k + 1) * feats] = qkv[k]
    copies[1].wait()
    packed_ref[:, 3 * feats :] = out[...].T
    token[...] = jnp.zeros_like(token)


def pack_mlp_kernel(layer, hidden, fc1_hbm, fc2_hbm, packed_ref, token, fc1, fc2, sems):
    ci = lax.rem(lax.axis_index("ctx"), GROUP)
    span = pl.ds(pl.multiple_of(ci * hidden, hidden), hidden)
    copies = start_copies(
        [(fc1_hbm.at[layer, :, span], fc1), (fc2_hbm.at[layer, span, :], fc2)], sems
    )
    copies[0].wait()
    packed_ref[:, :hidden] = fc1[...]
    copies[1].wait()
    packed_ref[:, hidden:] = fc2[...].T
    token[...] = jnp.zeros_like(token)


def prep_upstream_kernel(tp, outer, lengths, cotangent_hbm,
                         upstream_hbm, upstream_b_ref, usable_ref, mask_ref,
                         rows_in, upstream_ref, sems):
    rows = rows_in.shape[0]
    c = lax.axis_index("ctx")
    t = lax.axis_index("tp")
    place = lax.rem(c, GROUP) * tp + t
    start = pl.multiple_of(t * rows, rows)
    copies = start_copies(
        [(cotangent_hbm.at[0, pl.ds(start, rows), :], rows_in)], sems.at[pl.ds(0, 1)]
    )
    lane = lax.broadcasted_iota(jnp.int32, usable_ref.shape, 1)
    limit = jnp.zeros(usable_ref.shape, jnp.int32)
    for o in range(outer):
        for k, d in enumerate(ORDER):
            source = place ^ d
            first_lane = (o * len(ORDER) + k) * rows
            count = lengths[0, o * GROUP + lax.div(source, tp)] - lax.rem(source, tp) * rows
            limit = jnp.where(lane >= first_lane, first_lane + jnp.clip(count, 0, rows), limit)
    usable_ref[...] = jnp.where(lane < limit, 1.0, 0.0)
    row = lax.broadcasted_iota(jnp.int32, mask_ref.shape, 0)
    mask = jnp.where(row + start < lengths[0, c], 1.0, 0.0)
    mask_ref[...] = mask
    copies[0].wait()
    upstream = rows_in[...] * mask[:, 0:1]
    upstream_ref[...] = upstream
    sent = start_copies([(upstream_ref, upstream_hbm)], sems.at[pl.ds(1, 1)])
    upstream_b_ref[...] = upstream.astype(bf16)
    sent[0].wait()


def prep_first_kernel(depth, inputs_hbm, vecs, stream_ref, first_ref, sems):
    rows = stream_ref.shape[0]
    start = pl.multiple_of(lax.axis_index("tp") * rows, rows)
    copies = start_copies([(inputs_hbm.at[0, pl.ds(start, rows), :], stream_ref)], sems)
    copies[0].wait()
    normed, _ = normalize(stream_ref[...])
    shift = vecs[2 * depth : 2 * depth + 1, :]
    first_ref[...] = (normed * vecs[0:1, :] + shift).astype(bf16)


def keep_rows_kernel(*refs):
    chunks, (near_hbm, far_hbm, token, near, far, sems) = refs[:8], refs[8:]
    assemble(chunks[:4], near)
    assemble(chunks[4:], far)
    for copy in start_copies([(near, near_hbm), (far, far_hbm)], sems):
        copy.wait()
    token[...] = jnp.zeros_like(token)


def qkv_kernel(feats, weight_count, *refs):
    c0, c1, c2, c3, *rest = refs
    weights = rest[:weight_count]
    bias, qkv_ref, x = rest[weight_count:]
    assemble((c0, c1, c2, c3), x)
    qkv = sum(dot(x[:, span], w[:, : 3 * feats]) for span, w in shards(weights))
    qkv_ref[:, :feats] = (qkv[:, :feats] + bias[0:1, :]).astype(bf16)
    qkv_ref[:, feats : 2 * feats] = qkv[:, feats : 2 * feats].astype(bf16)
    qkv_ref[:, 2 * feats :] = (qkv[:, 2 * feats :] + bias[1:2, :]).astype(bf16)


def attn_kernel(feats, heads, weight_count, part_count, keep_count, tile, *refs):
    q_ref, *rest = refs
    parts = rest[:part_count]
    weights = rest[part_count : part_count + weight_count]
    rest = rest[part_count + weight_count :]
    usable, *rest = rest
    kept, rest = rest[:keep_count], rest[keep_count:]
    partial_ref, attended_hbm, norm_hbm, *rest = rest
    kept_hbm, rest = rest[:keep_count], rest[keep_count:]
    keys, values, attended_ref, norm_ref, sems = rest
    head_dim = feats // heads
    scale = 1.0 / math.sqrt(head_dim)
    copies = start_copies(list(zip(kept, kept_hbm)), sems)
    first = 0
    for part in parts:
        rows, width = part.shape
        keys[first : first + rows, :] = part[:, width - 2 * feats : width - feats]
        values[first : first + rows, :] = part[:, width - feats :]
        first += rows
    keep = usable[...] > 0.5
    rows = q_ref.shape[0]
    for first in range(0, rows, tile):
        span = slice(first, first + tile)
        q = q_ref[span, :feats]
        attended = None
        for h in range(heads):
            own = lanes_of(h, head_dim, feats)
            scores = dot_nt(only(own, q), keys[...]) * scale
            scores = jnp.where(keep, scores, MASK_FILL)
            highest = jnp.max(scores, axis=-1, keepdims=True)
            raised = jnp.exp(scores - highest)
            total = jnp.sum(raised, axis=-1, keepdims=True)
            soft = (raised * (1.0 / total)).astype(bf16)
            result = dot(soft, values[...])
            log_norm = jnp.broadcast_to(highest + jnp.log(total), (tile, feats))
            if attended is None:
                attended, norms = result, log_norm
            else:
                attended = jnp.where(own, result, attended)
                norms = jnp.where(own, log_norm, norms)
        attended_ref[span, :] = attended.astype(bf16)
        norm_ref[span, :] = norms
    copies += start_copies(
        [(attended_ref, attended_hbm), (norm_ref, norm_hbm)],
        sems.at[pl.ds(keep_count, 2)],
    )
    for span, w in shards(weights):
        partial_ref[:, span] = dot_nt(attended_ref[...], w[:, 3 * feats :]).astype(bf16)
    for copy in copies:
        copy.wait()


def core_sum_kernel(count, *refs):
    pairs, owns = refs[: 2 * count], refs[2 * count : 3 * count]
    peers = refs[3 * count :]
    rows = owns[0].shape[0]
    for j in range(count):
        near, far = pairs[2 * j], pairs[2 * j + 1]
        for k in range(1 + len(peers)):
            span = slice(k * rows, (k + 1) * rows)
            total = near[span, :].astype(f32) + far[span, :].astype(f32)
            if k == 0:
                owns[j][...] = total
            else:
                peers[k - 1][j * rows : (j + 1) * rows, :] = total.astype(bf16)


def total_of(own, xy, x, y, part=0):
    rows = own.shape[0]
    span = slice(part * rows, (part + 1) * rows)
    return (
        own[...] + y[span, :].astype(f32) + x[span, :].astype(f32) + xy[span, :].astype(f32)
    )


def sum_norm_kernel(bias_row, gain_row, shift_row, own, xy, x, y, residual_hbm, vecs,
                    stream_ref, normed_ref, residual, sems):
    copies = start_copies([(residual_hbm, residual)], sems)
    total = total_of(own, xy, x, y) + vecs[bias_row : bias_row + 1, :]
    copies[0].wait()
    stream = residual[...] + total
    stream_ref[...] = stream
    normed, _ = normalize(stream)
    gain = vecs[gain_row : gain_row + 1, :]
    normed_ref[...] = (normed * gain + vecs[shift_row : shift_row + 1, :]).astype(bf16)


def sum_out_kernel(bias_row, own, xy, x, y, residual_hbm, vecs, mask, out_hbm, token,
                   residual, out_ref, sems):
    copies = start_copies([(residual_hbm, residual)], sems.at[pl.ds(0, 1)])
    total = total_of(own, xy, x, y, 1) + vecs[bias_row : bias_row + 1, :]
    copies[0].wait()
    out_ref[...] = (residual[...] + total) * mask[:, 0:1]
    token[...] = jnp.zeros_like(token)
    for copy in start_copies([(out_ref, out_hbm)], sems.at[pl.ds(1, 1)]):
        copy.wait()


def mlp_kernel(hidden, keep_count, saves, load_w, load_count, c0, c1, c2, c3, w, bias, *refs):
    kept, rest = refs[:keep_count], refs[keep_count:]
    sources, rest = rest[:load_count], rest[load_count:]
    partial_ref, x_out, act_out, slope_out, *rest = rest
    kept_hbm, rest = rest[:keep_count], rest[keep_count:]
    targets, rest = rest[:load_count], rest[load_count:]
    loaded = []
    if load_w:
        w_ref, *rest, w_sems, chunk_sems = rest
        rows = c0.shape[0]
        chunks = start_copies(
            [(c, x_out.at[pl.ds(k * rows, rows), :]) for k, c in enumerate((c0, c1, c2, c3))],
            chunk_sems,
        )
        spans = (pl.ds(0, hidden), pl.ds(hidden, hidden))
        loaded = start_copies([(w.at[:, c], w_ref.at[:, c]) for c in spans], w_sems)
        w = w_ref
    if load_count:
        *rest, load_sems = rest
        fetched = start_copies(list(zip(sources, targets)), load_sems)
    else:
        fetched = []
    if saves:
        x, act_ref, slope_ref, sems = rest
    else:
        x, act_ref, slope_ref = x_out, act_out, slope_out
        (sems,) = rest
    copies = start_copies(list(zip(kept, kept_hbm)), sems)
    if load_w:
        for chunk in chunks:
            chunk.wait()
    else:
        assemble((c0, c1, c2, c3), x)
    if saves:
        copies += start_copies([(x, x_out)], sems.at[pl.ds(keep_count, 1)])
    block = hidden // 2
    if load_w:
        loaded[0].wait()
    for k in range(2):
        span = slice(k * block, (k + 1) * block)
        pre = dot(x[...], w[:, span]) + bias[:, span]
        cdf = 0.5 * (1.0 + lax.erf(pre * ROOT_HALF))
        density = jnp.exp(-0.5 * pre * pre) * INV_ROOT_TAU
        slope_ref[k] = cdf + pre * density
        act_ref[:, span] = (pre * cdf).astype(bf16)
        if saves:
            copies += start_copies(
                [(slope_ref.at[k], slope_out.at[k])], sems.at[pl.ds(1 + keep_count + k, 1)]
            )
    if saves:
        copies += start_copies([(act_ref, act_out)], sems.at[pl.ds(3 + keep_count, 1)])
    if load_w:
        loaded[1].wait()
    partial_ref[...] = dot_nt(act_ref[...], w[:, hidden:]).astype(bf16)
    for copy in copies + fetched:
        copy.wait()


def mlp_back_kernel(hidden, chunk_count, fetches, *refs):
    chunks, (w, slope, *rest) = refs[:chunk_count], refs[chunk_count:]
    if fetches:
        *rest, slope_ref, slope_sem = rest
        fetched = start_copies([(slope, slope_ref)], slope_sem)
        slope = slope_ref
    partial_ref, grad_ref, sum_hbm, x, sum_ref, sems = rest
    assemble(chunks, x)
    grad = dot(x[...], w[:, hidden:])
    if fetches:
        fetched[0].wait()
    block = hidden // 2
    for k in range(2):
        span = slice(k * block, (k + 1) * block)
        part = grad[:, span] * slope[k]
        grad_ref[:, span] = part.astype(bf16)
        sum_ref[:, span] = jnp.sum(part, axis=0, keepdims=True)
    sent = start_copies([(sum_ref, sum_hbm)], sems)
    partial_ref[...] = dot_nt(grad_ref[...], w[:, :hidden]).astype(bf16)
    sent[0].wait()


def mlp_grad_kernel(hidden, keep_count, second_near, second_far, act_near, act_far,
                    up_near, up_far, grad_near, grad_far, *refs):
    kept, refs = refs[:keep_count], refs[keep_count:]
    out_hbm, *refs = refs
    kept_hbm, (out_one, out_two, sems) = refs[:keep_count], refs[keep_count:]
    sent = start_copies(list(zip(kept, kept_hbm)), sems.at[pl.ds(2, keep_count)])
    total = dot_tn(up_near[...], act_near[...]) + dot_tn(up_far[...], act_far[...])
    out_two[...] = total.astype(bf16)
    sent += start_copies(
        [(out_two, out_hbm.at[:, pl.ds(hidden, hidden)])], sems.at[pl.ds(0, 1)]
    )
    total = dot_tn(second_near[...], grad_near[...]) + dot_tn(second_far[...], grad_far[...])
    out_one[...] = total.astype(bf16)
    sent += start_copies([(out_one, out_hbm.at[:, pl.ds(0, hidden)])], sems.at[pl.ds(1, 1)])
    for copy in sent:
        copy.wait()


def norm_back(upstream, values, gain):
    normed, inverse = normalize(values)
    scaled = upstream * gain
    back = inverse * (scaled - row_mean(scaled) - normed * row_mean(scaled * normed))
    gain_grad = jnp.sum(upstream * normed, axis=0, keepdims=True)
    return back, gain_grad, jnp.sum(upstream, axis=0, keepdims=True)


def norm_back_two_kernel(gain_row, own, xy, x, y, values, upstream, vecs,
                         grad_ref, grad_b_ref, sums_ref):
    total = total_of(own, xy, x, y)
    up = upstream[...]
    back, gain_grad, shift_grad = norm_back(
        total, values[...], vecs[gain_row : gain_row + 1, :]
    )
    grad = up + back
    grad_ref[...] = grad
    grad_b_ref[...] = grad.astype(bf16)
    sums_ref[0:1, :] = gain_grad
    sums_ref[1:2, :] = shift_grad
    sums_ref[2:3, :] = jnp.sum(grad, axis=0, keepdims=True)
    sums_ref[3:4, :] = jnp.sum(up, axis=0, keepdims=True)


def norm_back_one_kernel(gain_row, own, xy, x, y, values, upstream, vecs, mask,
                         grad_ref, grad_b_ref, sums_ref):
    total = total_of(own, xy, x, y)
    back, gain_grad, shift_grad = norm_back(
        total, values[...], vecs[gain_row : gain_row + 1, :]
    )
    grad = upstream[...] + back
    if mask is not None:
        grad = grad * mask[:, 0:1]
    grad_ref[...] = grad
    grad_b_ref[...] = grad.astype(bf16)
    sums_ref[0:1, :] = gain_grad
    sums_ref[1:2, :] = shift_grad


def attn_back_kernel(feats, heads, weight_count, part_count, tile, carried, *refs):
    c0, c1, c2, c3, *rest = refs
    weights, rest = rest[:weight_count], rest[weight_count:]
    usable, qkv, attended, norms, *rest = rest
    parts, rest = rest[:part_count], rest[part_count:]
    if carried:
        keys_before, values_before, *rest = rest
    x, grad_q, grad_k, grad_v, pairs, grad_att = rest
    head_dim = feats // heads
    scale = 1.0 / math.sqrt(head_dim)
    first = 0
    for part in parts:
        rows, width = part.shape
        pairs[first : first + rows, :] = part[:, width - 2 * feats :]
        first += rows
    assemble((c0, c1, c2, c3), x)
    grad_att[...] = sum(
        dot(x[:, span], w[:, 3 * feats :]) for span, w in shards(weights)
    ).astype(bf16)
    keep = usable[...] > 0.5
    rows = qkv.shape[0]
    if carried:
        sum_k, sum_v = keys_before[...], values_before[...]
    else:
        sum_k = jnp.zeros(grad_k.shape, f32)
        sum_v = jnp.zeros(grad_v.shape, f32)
    keys, values = pairs[:, :feats], pairs[:, feats:]
    for first in range(0, rows, tile):
        span = slice(first, first + tile)
        q = qkv[span, :feats]
        ga = grad_att[span, :]
        products = ga.astype(f32) * attended[span, :].astype(f32)
        gq = None
        for h in range(heads):
            own = lanes_of(h, head_dim, feats)
            q_h = only(own, q)
            ga_h = only(own, ga)
            row_dots = jnp.sum(only(own, products), axis=-1, keepdims=True)
            scores = dot_nt(q_h, keys) * scale
            scores = jnp.where(keep, scores, MASK_FILL)
            soft = jnp.exp(scores - norms[span, h * head_dim : h * head_dim + 1])
            grad_soft = dot_nt(ga_h, values)
            grad_scores = (soft * (grad_soft - row_dots)).astype(bf16)
            part = dot(grad_scores, keys)
            gq = part if gq is None else jnp.where(own, part, gq)
            sum_k = sum_k + dot_tn(grad_scores, q_h) * scale
            sum_v = sum_v + dot_tn(soft.astype(bf16), ga_h)
        grad_q[span, :] = gq * scale
    grad_k[...] = sum_k
    grad_v[...] = sum_v


def project_kernel(feats, first, weight_count, gq, gk, gv, *refs):
    weights, (partial_ref, packed) = refs[:weight_count], refs[weight_count:]
    rows = gq.shape[0]
    span = slice(first, first + rows)
    packed[:, :feats] = gq[...].astype(bf16)
    packed[:, feats : 2 * feats] = gk[span, :].astype(bf16)
    packed[:, 2 * feats :] = gv[span, :].astype(bf16)
    for columns, w in shards(weights):
        partial_ref[:, columns] = dot_nt(packed[...], w[:, : 3 * feats]).astype(bf16)


def attn_grad_kernel(feats, count, keep_count, first_near, first_far, att_near, att_far,
                     up_near, up_far, gq_near, gq_far, gk, gv, passed, lines, *refs):
    kept, refs = refs[:keep_count], refs[keep_count:]
    outs, refs = refs[:count], refs[count:]
    heads_hbm, passed_ref, *refs = refs
    kept_hbm, (packed, sums_ref, *staged, sems) = refs[:keep_count], refs[keep_count:]
    rows = up_near.shape[0]
    used = count + 2
    sent = start_copies(
        [(passed, passed_ref), *zip(kept, kept_hbm)], sems.at[pl.ds(used, 1 + keep_count)]
    )
    packed[:rows, :feats] = gq_near[...].astype(bf16)
    packed[rows:, :feats] = gq_far[...].astype(bf16)
    packed[:, feats : 2 * feats] = gk[...].astype(bf16)
    packed[:, 2 * feats :] = gv[...].astype(bf16)
    sums_ref[0:1, :] = jnp.sum(gq_near[...], axis=0, keepdims=True) + jnp.sum(
        gq_far[...], axis=0, keepdims=True
    )
    sums_ref[1:2, :] = jnp.sum(gv[...], axis=0, keepdims=True)
    sent += start_copies([(sums_ref, heads_hbm)], sems.at[pl.ds(0, 1)])

    def out_part(span):
        return dot_tn(up_near[:, span], att_near[...]) + dot_tn(up_far[:, span], att_far[...])

    def qkv_part(span):
        return dot_tn(first_near[:, span], packed[:rows, :]) + dot_tn(
            first_far[:, span], packed[rows:, :]
        )

    if count == 1:
        out_one, out_two = staged
        whole = slice(None)
        out_two[...] = out_part(whole).astype(bf16)
        sent += start_copies(
            [(out_two, outs[0].at[:, pl.ds(3 * feats, feats)])], sems.at[pl.ds(1, 1)]
        )
        out_one[...] = qkv_part(whole).astype(bf16)
        sent += start_copies(
            [(out_one, outs[0].at[:, pl.ds(0, 3 * feats)])], sems.at[pl.ds(2, 1)]
        )
    else:
        (stage,) = staged
        below = lines.shape[1]
        width_own = outs[0].shape[0] - below
        for d in reversed(range(count)):
            place = lax.rem(lax.axis_index("fsdp") + d, count)
            span = pl.ds(pl.multiple_of(place * width_own, width_own), width_own)
            stage[d, :width_own, : 3 * feats] = qkv_part(span).astype(bf16)
            stage[d, :width_own, 3 * feats :] = out_part(span).astype(bf16)
            stage[d, width_own:, :] = lines[d]
            sent += start_copies([(stage.at[d], outs[d])], sems.at[pl.ds(1 + d, 1)])
    for copy in sent:
        copy.wait()


def settle_kernel(keep_count, after_count, passed, *refs):
    kept, refs = refs[:keep_count], refs[keep_count + after_count :]
    passed_ref, *kept_hbm, sems = refs
    for copy in start_copies([(passed, passed_ref), *zip(kept, kept_hbm)], sems):
        copy.wait()


def fetch_kernel(count, *refs):
    sources, (target, sems) = refs[:count], refs[count:]
    columns = target.shape[1]
    moves = []
    row = 0
    for source in sources:
        rows = source.shape[0]
        for first in range(0, source.shape[1], columns):
            moves.append(
                (source.at[:, pl.ds(first, columns)], target.at[pl.ds(row, rows), :])
            )
            row += rows
    for copy in start_copies(moves, sems):
        copy.wait()


def shard_sum_kernel(depth, own_hbm, mine_a, mine_b, cross_a, cross_b, *refs):
    *others, part_ref, mine_ref, pair_ref, own, sems = refs
    moves = [(own_hbm, own)]
    row = 0
    for source in (mine_a, mine_b, cross_a, cross_b):
        count = source.shape[0]
        moves.append((source, pair_ref.at[pl.ds(row, count), :]))
        row += count
    first, *copies = start_copies(moves, sems)
    first.wait()
    rows, width = part_ref.shape[0], mine_ref.shape[1]
    terms = [ref[...].astype(f32) for ref in (own, *others)]
    total = terms[0]
    for term in terms[1:]:
        total = total + term
    part_ref[...] = total[:rows, :].astype(bf16)
    lines = total[rows:, :width] + total[rows:, width:]
    mine_ref[: 6 * depth, :] = lines[: 6 * depth, :]
    for k in range(mine_ref.shape[0] - 16):
        mine_ref[16 + k : 17 + k, :] = lines[6 * depth + k : 6 * depth + k + 1, :]
    for copy in copies:
        copy.wait()


def place_kernel(depth, hidden, feats, here, sibling, *refs):
    qkv_hbm, out_hbm, fc1_hbm, fc2_hbm, token, fc1, fc2, qkv, out, sems = refs
    token[...] = jnp.zeros_like(token)
    ci = lax.rem(lax.axis_index("ctx"), GROUP)
    rows = fc1.shape[2]
    count = here.shape[0] // 2
    copies = []

    def send(source, target):
        copies.extend(start_copies([(source, target)], sems.at[pl.ds(len(copies), 1)]))

    for k in range(GROUP):
        stacked = (here, sibling)[k % 2].at[pl.ds(k // 2 * count, count), :]
        wide = pl.ds(pl.multiple_of((ci ^ k) * hidden, hidden), hidden)
        narrow = pl.ds(pl.multiple_of((ci ^ k) * feats, feats), feats)
        for l in range(depth):
            first = 0 if l == 0 else (3 * l - 1) * rows
            fc1[l, k] = stacked[first : first + rows, :].astype(f32)
            send(fc1.at[l, k], fc1_hbm.at[l, :, wide])
            fc2[l, k] = stacked[first + rows : first + 2 * rows, :].T.astype(f32)
            send(fc2.at[l, k], fc2_hbm.at[l, wide, :])
            if l > 0:
                piece = stacked.at[pl.ds(first + 2 * rows, rows), :]
                for j in range(3):
                    qkv[l - 1, k, j] = piece[:, j * feats : (j + 1) * feats].astype(f32)
                send(qkv.at[l - 1, k], qkv_hbm.at[l, :, :, narrow])
                out[l - 1, k] = piece[:, 3 * feats :].T.astype(f32)
                send(out.at[l - 1, k], out_hbm.at[l, narrow, :])
    for copy in copies:
        copy.wait()


def place_last_kernel(feats, vectors, here, sibling, qkv_in, out_in, mine, far, *refs):
    qkv_hbm, out_hbm, *vector_refs, qkv, out, sems = refs
    ci = lax.rem(lax.axis_index("ctx"), GROUP)
    rows = here.shape[0] // 2
    copies = []
    for k in range(GROUP):
        piece = (here, sibling)[k % 2].at[pl.ds(k // 2 * rows, rows), :]
        span = pl.ds(pl.multiple_of((ci ^ k) * feats, feats), feats)
        for j in range(3):
            qkv[k, j] = piece[:, j * feats : (j + 1) * feats].astype(f32)
        copies += start_copies(
            [(qkv.at[k], qkv_hbm.at[0, :, :, span])], sems.at[pl.ds(2 * k, 1)]
        )
        out[k] = piece[:, 3 * feats :].T.astype(f32)
        copies += start_copies(
            [(out.at[k], out_hbm.at[0, span, :])], sems.at[pl.ds(2 * k + 1, 1)]
        )
    vectors(mine, far, *vector_refs)
    for copy in copies:
        copy.wait()


def vector_pack_kernel(depth, one_now, gq_near, gq_far, gv, *refs):
    count = 5 * depth - 2
    out_ref, *found, sems = refs[count:]
    copies = start_copies(list(zip(refs[:count], found)), sems)
    out_ref[...] = jnp.zeros_like(out_ref)
    feats = gv.shape[1]
    head_now = [
        jnp.sum(gq_near[...], axis=0, keepdims=True) + jnp.sum(gq_far[...], axis=0, keepdims=True),
        jnp.sum(gv[...], axis=0, keepdims=True),
    ]
    for copy in copies:
        copy.wait()
    for l in range(depth):
        if l == 0:
            one, (two, unit_near, unit_far) = one_now, found[:3]
            heads = head_now
        else:
            one, two, unit_near, unit_far, head = found[5 * l - 2 : 5 * l + 3]
            heads = [head[0:1, :], head[1:2, :]]
        out_ref[6 * l : 6 * l + 1, :] = one[0:1, :]
        out_ref[6 * l + 1 : 6 * l + 2, :] = two[0:1, :]
        out_ref[6 * l + 2 : 6 * l + 3, :] = one[1:2, :]
        out_ref[6 * l + 3 : 6 * l + 6, :] = two[1:4, :]
        units = unit_near.shape[1]
        row = 6 * depth
        out_ref[row : row + 1, l * units : (l + 1) * units] = unit_near[...] + unit_far[...]
        for j in range(2):
            start = (2 * l + j) * feats
            out_ref[row + 1 : row + 2, start : start + feats] = heads[j]


def vector_lines_kernel(depth, width_own, packed, lines_ref):
    count = lines_ref.shape[0]
    f = lax.axis_index("fsdp")
    total = packed[...]
    high = total.astype(bf16).astype(f32)
    low = total - high
    lines_ref[...] = jnp.zeros_like(lines_ref)
    last = 6 * depth
    for k, value in enumerate((high, low)):
        lanes = slice(k * width_own, (k + 1) * width_own)
        columns = [value[:, a * width_own : (a + 1) * width_own] for a in range(count)]
        for d in range(count):
            mine = columns[0]
            for a in range(1, count):
                mine = jnp.where(lax.rem(f + d, count) == a, columns[a], mine)
            rows = [mine[:last, :]]
            for r in range(2):
                for a in range(count):
                    rows.append(columns[a][last + r : last + r + 1, :])
            rows.append(jnp.zeros((lines_ref.shape[1] - last - 2 * count, width_own), f32))
            lines_ref[d, :, lanes] = jnp.concatenate(rows, axis=0).astype(bf16)


def vector_plane_kernel(depth, own, xy, x, y, part, part_x, out_ref, pair_ref):
    last = 6 * depth
    rows = part.shape[0]
    pair_ref[:rows, :] = part[...]
    pair_ref[rows:, :] = part_x[...]
    out_ref[:last, :] = own[:last, :] + xy[:last, :] + x[:last, :] + y[:last, :]
    out_ref[16:24, :] = own[16:24, :]
    out_ref[24:32, :] = x[16:24, :]


def vector_place_kernel(depth, head_dim, own, far, gains_ref, shifts_ref, unit_ref, heads_ref):
    total = own[: 6 * depth, :] + far[: 6 * depth, :]
    for l in range(depth):
        gains_ref[l] = total[6 * l : 6 * l + 2, :]
        shifts_ref[l] = total[6 * l + 2 : 6 * l + 6, :]
    pieces = (own[16:24, :], far[16:24, :], own[24:32, :], far[24:32, :])
    ci = lax.rem(lax.axis_index("ctx"), GROUP)
    f = lax.axis_index("fsdp")

    def of_place(c):
        k = ci ^ c
        found = pieces[0]
        for j in range(1, GROUP):
            found = jnp.where(k == j, pieces[j], found)
        return found

    width_own = own.shape[1]
    units = of_place(f)
    parts = unit_ref.shape[2] // width_own
    for l in range(depth):
        for j in range(parts):
            row = l * parts + j
            unit_ref[l, :, j * width_own : (j + 1) * width_own] = units[row : row + 1, :]
    head_own = heads_ref.shape[3]
    heads = heads_ref.shape[2] // GROUP
    for c in range(GROUP):
        found = of_place(c)
        for l in range(depth):
            for j in range(2):
                for h in range(heads):
                    first = ((2 * l + j) * heads + h) * head_dim
                    row, lane = 4 + first // width_own, first % width_own
                    value = found[row : row + 1, lane : lane + head_own]
                    for a in range(1, head_dim // head_own):
                        start = lane + a * head_own
                        value = jnp.where(
                            f == a, found[row : row + 1, start : start + head_own], value
                        )
                    heads_ref[l, j, c * heads + h : c * heads + h + 1, :] = value


def place_rows_kernel(count, *refs):
    terms, outs, sems = refs[: 2 * count], refs[2 * count : 3 * count], refs[-1]
    rows = terms[0].shape[0]
    start = pl.multiple_of(lax.axis_index("tp") * rows, rows)
    places = (pl.ds(start, rows), pl.ds(pl.multiple_of(rows - start, rows), rows))
    moves = [
        (terms[2 * k + j], out.at[0, places[j], :]) for k, out in enumerate(outs) for j in range(2)
    ]
    for copy in start_copies(moves, sems):
        copy.wait()


def per_device(
    inputs, lengths, cotangent, norm_gains, shifts, qv_bias, fc1_bias, w_qkv, w_out, w_fc1, w_fc2
):
    depth = w_qkv.shape[0]
    width_own = w_qkv.shape[2]
    fsdp = lax.axis_size("fsdp")
    tp = lax.axis_size("tp")
    ctx = lax.axis_size("ctx")
    outer = ctx // GROUP
    rows = inputs.shape[1] // tp
    half = rows * CHIPS
    all_rows = 2 * half
    head_own = qv_bias.shape[3]
    head_dim = head_own * fsdp
    heads = qv_bias.shape[2] // GROUP
    feats = heads * head_dim
    hidden = w_fc1.shape[2] // GROUP
    width = width_own * fsdp
    t = lax.axis_index("tp")
    f = lax.axis_index("fsdp")
    ci = lax.axis_index("ctx") % GROUP
    tile = half // 2
    attn_limit = 12 if outer == 1 else 48

    def swap_core(value):
        return lax.ppermute(value, "ctx", [(i, i ^ 1) for i in range(ctx)])

    def swap_x(value):
        return lax.ppermute(value, "ctx", [(i, i ^ 2) for i in range(ctx)])

    def swap_y(value):
        return lax.ppermute(value, "tp", [(i, i ^ 1) for i in range(tp)])

    def swap_xy(value):
        pairs = [
            (i * tp + k, (i ^ 2) * tp + (k ^ 1)) for i in range(ctx) for k in range(tp)
        ]
        return lax.ppermute(value, ("ctx", "tp"), pairs)

    def shift_z(value, d):
        return lax.ppermute(value, "fsdp", [(i, (i + d) % fsdp) for i in range(fsdp)])

    outer_groups = [[o * GROUP + i for o in range(outer)] for i in range(GROUP)]

    def gather_rows(own):
        near = (own, swap_xy(own), swap_x(own), swap_y(own))
        return near, tuple(swap_core(chunk) for chunk in near)

    def settle(value, there, *kept):
        shape = value.value if isinstance(value, Far) else value
        return kernel_call(
            functools.partial(settle_kernel, len(kept), 1),
            [(shape.shape, shape.dtype)] + [saved(k.shape, k.dtype) for k in kept],
            value,
            *kept,
            Far(there),
            name="settle",
            scratch=[DMA((1 + len(kept),))],
        )

    def reduce_rows(*pairs, after=()):
        count = len(pairs)
        *owns, xy, x, y = kernel_call(
            functools.partial(core_sum_kernel, count),
            [((rows, width), f32)] * count + [((count * rows, width), bf16)] * 3,
            *[v for near, far in pairs for v in (near, swap_core(far))],
            name="core_sum",
            after=after,
        )
        peers = (swap_xy(xy), swap_x(x), swap_y(y))
        return [(own, *peers) for own in owns]

    def pack_attn(l, after):
        return kernel_call(
            functools.partial(pack_attn_kernel, l, feats),
            [((width_own, 4 * feats), bf16), TOKEN],
            Far(w_qkv),
            Far(w_out),
            name="pack_attn",
            after=after,
            scratch=[
                pltpu.VMEM((3, width_own, feats), bf16),
                pltpu.VMEM((feats, width_own), bf16),
                DMA((2,)),
            ],
        )

    def pack_mlp(l, after):
        return kernel_call(
            functools.partial(pack_mlp_kernel, l, hidden),
            [((width_own, 2 * hidden), bf16), TOKEN],
            Far(w_fc1),
            Far(w_fc2),
            name="pack_mlp",
            after=after,
            scratch=[
                pltpu.VMEM((width_own, hidden), bf16),
                pltpu.VMEM((hidden, width_own), bf16),
                DMA((2,)),
            ],
        )

    attn_w = []
    mlp_w = []
    token = None
    for l in range(depth):
        own, token = pack_attn(l, () if token is None else (token,))
        attn_w.append((lax.all_gather(own, "fsdp", axis=0, tiled=True),))
        own, token = pack_mlp(l, (token,))
        mlp_w.append(lax.all_gather(own, "fsdp", axis=0, tiled=True))
        if l == 0:
            pack_token = token

    qv_own = lax.dynamic_slice_in_dim(qv_bias, ci * heads, heads, axis=2)
    vec_rows = depth * 6
    c1_rows = depth * fc1_bias.shape[2] // width_own
    qv_own = qv_own.reshape(1, -1)
    small_own = jnp.concatenate(
        [
            norm_gains.reshape(-1, width_own),
            shifts.reshape(-1, width_own),
            fc1_bias.reshape(-1, width_own),
            jnp.pad(qv_own, ((0, 0), (0, width_own - qv_own.shape[1]))),
        ],
        axis=0,
    )
    shifted = [small_own] + [shift_z(small_own, d) for d in range(1, fsdp)]

    def shard(a):
        picked = shifted[0]
        for d in range(1, fsdp):
            picked = jnp.where((f - d) % fsdp == a, shifted[d], picked)
        return picked.astype(f32)

    small = [shard(a) for a in range(fsdp)]
    vecs = jnp.concatenate([s[:vec_rows] for s in small], axis=1)
    fc1_all = shard(ci)[vec_rows : vec_rows + c1_rows].reshape(depth, 1, hidden)
    qv_all = jnp.stack(
        [s[vec_rows + c1_rows, : qv_own.shape[1]].reshape(depth, 2, heads, head_own) for s in small],
        axis=3,
    ).reshape(depth, 2, feats)

    def gain_row(l, i):
        return 2 * l + i

    def shift_row(l, i):
        return 2 * depth + 4 * l + i

    key_rows = outer * all_rows
    row_f32 = ((rows, width), f32)
    row_bf16 = ((rows, width), bf16)
    upstream, upstream_b, usable, mask = kernel_call(
        functools.partial(prep_upstream_kernel, tp, outer),
        [saved((rows, width), f32), row_bf16, ((1, key_rows), f32), ((rows, 128), f32)],
        Scalars(lengths),
        Far(cotangent),
        name="prep_upstream",
        after=(pack_token,),
        scratch=[pltpu.VMEM((rows, width), f32), pltpu.VMEM((rows, width), f32), DMA((2,))],
    )
    near, far = gather_rows(upstream_b)
    half_x = pltpu.VMEM((half, width), bf16)
    *upstream_rows, upstream_token = kernel_call(
        keep_rows_kernel,
        [saved((half, width), bf16)] * 2 + [TOKEN],
        *near,
        *far,
        name="keep_rows",
        scratch=[half_x, half_x, DMA((2,))],
    )
    stream, first = kernel_call(
        functools.partial(prep_first_kernel, depth),
        [row_f32, row_bf16],
        Far(inputs),
        vecs,
        name="prep_first",
        scratch=[DMA((1,))],
    )
    first_chunks = gather_rows(first)

    partial_out = ((half, width), bf16)
    saved_all = []
    for l in range(depth):
        qkv = []
        first_x = []
        for side in (0, 1):
            qkv_half, x_half = kernel_call(
                functools.partial(qkv_kernel, feats, len(attn_w[l])),
                [((half, 3 * feats), bf16), ((half, width), bf16)],
                *first_chunks[side],
                *attn_w[l],
                qv_all[l],
                name="qkv",
                after=(upstream_token,) if l == 0 and side == 0 else (),
            )
            qkv.append(qkv_half)
            first_x.append(x_half)
        if outer > 1:
            pairs = jnp.concatenate([part[:, feats:] for part in qkv], axis=0)
            pairs = lax.all_gather(
                pairs, "ctx", axis=0, tiled=True, axis_index_groups=outer_groups
            )
            key_parts = (pairs,)
        else:
            key_parts = tuple(qkv)
        attn = [None, None]
        for side in (1, 0):
            kept = (first_x[side], qkv[side]) + ((stream,) if side == 1 else ())
            attn[side] = kernel_call(
                functools.partial(
                    attn_kernel, feats, heads, len(attn_w[l]), len(key_parts), len(kept), tile
                ),
                [partial_out, saved((half, feats), bf16), saved((half, feats), f32)]
                + [saved(k.shape, k.dtype) for k in kept],
                qkv[side],
                *key_parts,
                *attn_w[l],
                usable,
                *kept,
                name="attn",
                limit=attn_limit,
                scratch=[
                    pltpu.VMEM((key_rows, feats), bf16),
                    pltpu.VMEM((key_rows, feats), bf16),
                    pltpu.VMEM((half, feats), bf16),
                    pltpu.VMEM((half, feats), f32),
                    DMA((len(kept) + 2,)),
                ],
            )
        (sums,) = reduce_rows((attn[0][0], attn[1][0]))
        middle, second = kernel_call(
            functools.partial(sum_norm_kernel, shift_row(l, 2), gain_row(l, 1), shift_row(l, 1)),
            [row_f32, row_bf16],
            *sums,
            Far(attn[1][5]),
            vecs,
            name="sum_norm",
            scratch=[pltpu.VMEM((rows, width), f32), DMA((1,))],
        )
        second_chunks = gather_rows(second)
        mlp = [None, None]
        for side in (1, 0):
            kept = (middle,) if side == 1 else ()
            saves = l + 1 < depth
            load_w = not saves and side == 1
            loads = tuple(upstream_rows) if not saves and side == 0 else ()
            shapes = [
                ((half, width), bf16),
                ((half, hidden), bf16),
                ((2, half, hidden // 2), f32),
            ]
            mlp[side] = kernel_call(
                functools.partial(mlp_kernel, hidden, len(kept), saves, load_w, len(loads)),
                [partial_out]
                + [saved(*shape) if saves else shape for shape in shapes]
                + [saved(k.shape, k.dtype) for k in kept]
                + [(v.shape, v.dtype) for v in loads]
                + ([(mlp_w[l].shape, bf16)] if load_w else []),
                *[Anywhere(c) if load_w else c for c in second_chunks[side]],
                Far(mlp_w[l]) if load_w else mlp_w[l],
                fc1_all[l],
                *kept,
                *[Far(v) for v in loads],
                name="mlp",
                scratch=[pltpu.VMEM(*shape) for shape in shapes if saves]
                + [DMA((4 + len(kept),))]
                + ([DMA((2,)), DMA((CHIPS,))] if load_w else [])
                + [DMA((len(loads),)) for _ in loads[:1]],
            )
            if load_w:
                *mlp[side], mlp_w[l] = mlp[side]
            if loads:
                *mlp[side], near, far = mlp[side]
                upstream_chunks = [(near,), (far,)]
        saved_all.append((attn, pairs if outer > 1 else None, mlp))
        if l + 1 < depth:
            (sums,) = reduce_rows((mlp[0][0], mlp[1][0]))
            stream, first = kernel_call(
                functools.partial(
                    sum_norm_kernel, shift_row(l, 3), gain_row(l + 1, 0), shift_row(l + 1, 0)
                ),
                [row_f32, row_bf16],
                *sums,
                Far(mlp[1][4]),
                vecs,
                name="sum_norm",
                scratch=[pltpu.VMEM((rows, width), f32), DMA((1,))],
            )
            first_chunks = gather_rows(first)

    def scatter_grads(grad):
        part = lax.psum_scatter(grad, "fsdp", scatter_dimension=0, tiled=True)
        if outer > 1:
            part = lax.psum(part, "ctx", axis_index_groups=outer_groups)
        return part

    row_sums = [None] * depth
    unit_sums = [None] * depth
    head_sums = [None] * depth
    mlp_parts = [None] * depth
    attn_parts = [None] * depth
    for l in reversed(range(depth)):
        attn, pairs, mlp = saved_all[l]
        back = [None, None]
        for side in (1, 0):
            fetches = l + 1 < depth and side == 0
            back[side] = kernel_call(
                functools.partial(mlp_back_kernel, hidden, len(upstream_chunks[side]), fetches),
                [
                    partial_out,
                    ((half, hidden), bf16),
                    saved((1, hidden), f32),
                    ((half, width), bf16),
                ],
                *upstream_chunks[side],
                mlp_w[l],
                Far(mlp[side][3]) if fetches else mlp[side][3],
                name="mlp_back",
                scratch=[pltpu.VMEM((1, hidden), f32), DMA((1,))]
                + ([pltpu.VMEM(mlp[side][3].shape, f32), DMA((1,))] if fetches else []),
            )
        kept = [back[0][0], back[1][0]]
        if l + 1 == depth:
            kept += [mlp[0][0], mlp[1][0]]
        mlp_grad, *kept = kernel_call(
            functools.partial(mlp_grad_kernel, hidden, len(kept)),
            [saved((width, 2 * hidden), bf16)] + [saved(k.shape, k.dtype) for k in kept],
            mlp[0][1],
            mlp[1][1],
            mlp[0][2],
            mlp[1][2],
            back[0][3],
            back[1][3],
            back[0][1],
            back[1][1],
            *kept,
            name="mlp_grad",
            scratch=[
                pltpu.VMEM((width, hidden), bf16),
                pltpu.VMEM((width, hidden), bf16),
                DMA((2 + len(kept),)),
            ],
        )
        mlp_parts[l] = scatter_grads(mlp_grad)
        (sums,) = reduce_rows(tuple(kept[:2]))
        if l + 1 == depth:
            output_pair = tuple(kept[2:])
        unit_sums[l] = (back[0][2], back[1][2])
        grad_middle, middle_b, sums_two = kernel_call(
            functools.partial(norm_back_two_kernel, gain_row(l, 1)),
            [row_f32, row_bf16, ((4, width), f32)],
            *sums,
            mlp[1][4],
            upstream,
            vecs,
            name="norm_back_two",
        )
        if l + 1 < depth:
            middle_b, sums_two, grad_middle = settle(
                middle_b, attn_parts[l + 1], sums_two, grad_middle
            )
        middle_chunks = gather_rows(middle_b)
        grad_q = [None, None]
        middle_x = [None, None]
        carried = ()
        for side in (0, 1):
            key_parts = (pairs,) if outer > 1 else (attn[0][4], attn[1][4])
            middle_x[side], grad_q[side], *carried = kernel_call(
                functools.partial(
                    attn_back_kernel,
                    feats,
                    heads,
                    len(attn_w[l]),
                    len(key_parts),
                    tile,
                    len(carried) > 0,
                ),
                [
                    ((half, width), bf16),
                    ((half, feats), f32),
                    ((key_rows, feats), f32),
                    ((key_rows, feats), f32),
                ],
                *middle_chunks[side],
                *attn_w[l],
                usable,
                attn[side][4],
                attn[side][1],
                attn[side][2],
                *key_parts,
                *carried,
                name="attn_back",
                scratch=[
                    pltpu.VMEM((key_rows, 2 * feats), bf16),
                    pltpu.VMEM((half, feats), bf16),
                ],
                limit=attn_limit,
            )
        grad_k, grad_v = carried
        if outer > 1:
            grad_k, grad_v = (
                lax.psum_scatter(
                    v, "ctx", scatter_dimension=0, tiled=True, axis_index_groups=outer_groups
                )
                for v in (grad_k, grad_v)
            )

        def project(side, after):
            return kernel_call(
                functools.partial(project_kernel, feats, side * half, len(attn_w[l])),
                [partial_out],
                grad_q[side],
                grad_k,
                grad_v,
                *attn_w[l],
                name="project",
                after=after,
                scratch=[pltpu.VMEM((half, 3 * feats), bf16)],
            )[0]

        far_part = project(1, ())
        near_part = project(0, ())
        pairs_now = [(near_part, far_part)]
        if l == 0:
            pairs_now.append(output_pair)
        sums, *output_sums = reduce_rows(*pairs_now)
        body = functools.partial(norm_back_one_kernel, gain_row(l, 0))
        if l > 0:
            masked = ()
            body = lambda *refs, body=body: body(*refs[:7], None, *refs[7:])
        else:
            masked = (mask,)
        upstream, upstream_b, sums_one = kernel_call(
            body,
            [row_f32, row_bf16, ((2, width), f32)],
            *sums,
            attn[1][5],
            grad_middle,
            vecs,
            *masked,
            name="norm_back_one",
        )
        lines = ()
        if l == 0:
            terms = [sums_two, *unit_sums[0]]
            for k in range(1, depth):
                terms += [*row_sums[k], *unit_sums[k], head_sums[k]]
            packed = kernel_call(
                functools.partial(vector_pack_kernel, depth),
                [((6 * depth + 2, width), f32)],
                sums_one,
                *grad_q,
                grad_v,
                *[Far(v) for v in terms],
                name="vector_pack",
                scratch=[pltpu.VMEM(v.shape, f32) for v in terms] + [DMA((len(terms),))],
            )[0]
            if outer > 1:
                packed = lax.psum(packed, "ctx", axis_index_groups=outer_groups)
            lines = kernel_call(
                functools.partial(vector_lines_kernel, depth, width_own),
                [((fsdp, 32, 2 * width_own), bf16)],
                packed,
                name="vector_lines",
            )
        count = 1 if l > 0 else fsdp
        shapes = [((width, 3 * feats), bf16), ((width, feats), bf16)]
        if l == 0:
            shapes = [((fsdp, width_own + 32, 4 * feats), bf16)]
        sums_now = sums_one
        kept = [sums_one, upstream] + ([sums_two] if l + 1 == depth else [])
        *attn_grads, head_sums[l], upstream_b, sums_one, upstream, sums_kept = [
            *kernel_call(
                functools.partial(attn_grad_kernel, feats, count, len(kept)),
                [saved((width if l > 0 else width_own + 32, 4 * feats), bf16)] * count
                + [saved((2, feats), f32), saved(*row_bf16) if l > 0 else row_bf16]
                + [saved(k.shape, k.dtype) for k in kept],
                attn[0][3],
                attn[1][3],
                attn[0][1],
                attn[1][1],
                *middle_x,
                *grad_q,
                grad_k,
                grad_v,
                upstream_b,
                *(lines or (sums_one,)),
                *kept,
                name="attn_grad",
                scratch=[
                    pltpu.VMEM((all_rows, 3 * feats), bf16),
                    pltpu.VMEM((2, feats), f32),
                ]
                + [pltpu.VMEM(*shape) for shape in shapes]
                + [DMA((count + 3 + len(kept),))],
            ),
            sums_two,
        ][: count + 5]
        if l + 1 == depth:
            sums_two = sums_kept
        if l > 0:
            attn_parts[l] = scatter_grads(attn_grads[0])
            (upstream_b,) = settle(Far(upstream_b), mlp_parts[l])
            upstream_chunks = gather_rows(upstream_b)
        row_sums[l] = (sums_one, sums_two)

    blocks = 3 * depth - 1

    def fetch(sources, after):
        count = sum(v.shape[1] // hidden for v in sources)
        return kernel_call(
            functools.partial(fetch_kernel, len(sources)),
            [((count * width_own, hidden), bf16)],
            *[Far(v) for v in sources],
            name="fetch",
            after=after,
            scratch=[DMA((count,))],
        )[0]

    upper = [v for l in range(1, depth) for v in (mlp_parts[l], attn_parts[l])]
    stacked = (fetch(mlp_parts[:1], (upstream_b,)), fetch(upper, (sums_now,)))
    crossed = [swap_x(v) for v in stacked]
    own_term, *other_terms = attn_grads
    other_terms = [shift_z(term, d + 1) for d, term in enumerate(other_terms)]
    inputs_other = swap_y(upstream)
    outputs_own, output_token = kernel_call(
        functools.partial(sum_out_kernel, shift_row(depth - 1, 3)),
        [saved((rows, width), f32), TOKEN],
        *output_sums[0],
        Far(saved_all[depth - 1][2][1][4]),
        vecs,
        mask,
        name="sum_out",
        after=(Anywhere(inputs_other),),
        scratch=[pltpu.VMEM((rows, width), f32)] * 2 + [DMA((2,))],
    )
    part, mine, pair = kernel_call(
        functools.partial(shard_sum_kernel, depth),
        [
            ((width_own, 4 * feats), bf16),
            ((24, width_own), f32),
            ((2 * blocks * width_own, hidden), bf16),
        ],
        Far(own_term),
        *[Anywhere(v) for v in (*stacked, *crossed)],
        *other_terms,
        name="shard_sum",
        after=(output_token,),
        scratch=[pltpu.VMEM(own_term.shape, bf16), DMA((5,))],
    )
    others = (inputs_other, swap_y(outputs_own))
    if outer > 1:
        part = lax.psum(part, "ctx", axis_index_groups=outer_groups)
    *placed, place_token = kernel_call(
        functools.partial(place_kernel, depth, hidden, feats),
        [saved(v.shape, f32) for v in (w_qkv, w_out, w_fc1, w_fc2)] + [TOKEN],
        pair,
        swap_core(pair),
        name="place",
        limit=24,
        scratch=[
            pltpu.VMEM((depth, GROUP, width_own, hidden), f32),
            pltpu.VMEM((depth, GROUP, hidden, width_own), f32),
            pltpu.VMEM((depth - 1, GROUP, 3, width_own, feats), f32),
            pltpu.VMEM((depth - 1, GROUP, feats, width_own), f32),
            DMA((16 * depth,)),
        ],
    )
    mine, last_pair = kernel_call(
        functools.partial(vector_plane_kernel, depth),
        [((32, width_own), f32), ((2 * width_own, 4 * feats), bf16)],
        mine,
        swap_xy(mine),
        swap_x(mine),
        swap_y(mine),
        part,
        swap_x(part),
        name="vector_plane",
        after=(place_token, Anywhere(others[1])),
    )
    grad_inputs, outputs = kernel_call(
        functools.partial(place_rows_kernel, 2),
        [saved(inputs.shape, f32)] * 2,
        *(upstream, others[0], outputs_own, others[1]),
        name="place_rows",
        scratch=[DMA((4,))],
    )
    *placed[:2], grad_gains, grad_shifts, grad_fc1_bias, grad_qv_bias = kernel_call(
        functools.partial(
            place_last_kernel, feats, functools.partial(vector_place_kernel, depth, head_dim)
        ),
        [saved(v.shape, f32) for v in (w_qkv, w_out)]
        + [(v.shape, f32) for v in (norm_gains, shifts, fc1_bias, qv_bias)],
        last_pair,
        swap_core(last_pair),
        Far(placed[0]),
        Far(placed[1]),
        mine,
        swap_core(mine),
        name="place_last",
        scratch=[
            pltpu.VMEM((GROUP, 3, width_own, feats), f32),
            pltpu.VMEM((GROUP, feats, width_own), f32),
            DMA((2 * GROUP,)),
        ],
        aliases={2: 0, 3: 1},
    )
    return (
        outputs,
        grad_inputs,
        grad_gains,
        grad_shifts,
        grad_qv_bias,
        grad_fc1_bias,
        *placed,
    )


def solution(mesh):
    rows = P("fsdp", "ctx", None)
    params = (
        P(None, None, "fsdp"),
        P(None, None, "fsdp"),
        P(None, None, "tp", "fsdp"),
        P(None, "tp", "fsdp"),
        P(None, None, "fsdp", "tp"),
        P(None, "tp", "fsdp"),
        P(None, "fsdp", "tp"),
        P(None, "tp", "fsdp"),
    )
    return jax.shard_map(
        per_device,
        mesh=mesh,
        in_specs=(rows, P("fsdp", None), rows) + params,
        out_specs=(rows, rows) + params,
        check_vma=False,
    )
```

```python
import functools
import math

import jax
import jax.numpy as jnp
from jax import lax
from jax.experimental import pallas as pl
from jax.experimental.pallas import tpu as pltpu
from jax.sharding import PartitionSpec as P

NORM_EPSILON = 1e-06
MASK_FILL = -1e30
ROOT_HALF = 0.7071067811865476
INV_ROOT_TAU = 0.3989422804014327
GROUP = 4
ORDER = (0, 5, 4, 1, 2, 7, 6, 3)
CHIPS = 4

bf16 = jnp.bfloat16
f32 = jnp.float32
VMEM = pl.BlockSpec(memory_space=pltpu.VMEM)
SMEM = pl.BlockSpec(memory_space=pltpu.SMEM)
HBM = pl.BlockSpec(memory_space=pltpu.HBM)
DMA = pltpu.SemaphoreType.DMA
TOKEN = ((8, 128), f32)


def dot(a, b):
    return lax.dot_general(a, b, (((1,), (0,)), ((), ())), preferred_element_type=f32)


def dot_nt(a, b):
    return lax.dot_general(a, b, (((1,), (1,)), ((), ())), preferred_element_type=f32)


def dot_tn(a, b):
    return lax.dot_general(a, b, (((0,), (0,)), ((), ())), preferred_element_type=f32)


class Far:
    def __init__(self, value):
        self.value = value


class Anywhere:
    def __init__(self, value):
        self.value = value


class Scalars:
    def __init__(self, value):
        self.value = value


def saved(shape, dtype):
    return pltpu.HBM(shape, dtype)


def kernel_call(body, outs, *args, name, limit=12, scratch=(), after=(), aliases=None, us=0):
    values, specs = [], []
    for arg in (*args, *after):
        if isinstance(arg, Far):
            values.append(pltpu.with_memory_space_constraint(arg.value, pltpu.HBM))
            specs.append(HBM)
        elif isinstance(arg, Anywhere):
            values.append(arg.value)
            specs.append(pl.BlockSpec(memory_space=pl.ANY))
        elif isinstance(arg, Scalars):
            values.append(arg.value)
            specs.append(SMEM)
        else:
            values.append(arg)
            specs.append(VMEM)
    first, last = len(args), len(args) + len(after)

    def run(*refs):
        body(*refs[:first], *refs[last:])

    out_shape, out_specs = [], []
    for out in outs:
        if isinstance(out, tuple):
            out_shape.append(jax.ShapeDtypeStruct(*out))
            out_specs.append(VMEM)
        else:
            out_shape.append(out)
            out_specs.append(HBM)
    return pl.pallas_call(
        run,
        out_shape=out_shape,
        in_specs=specs,
        out_specs=out_specs,
        scratch_shapes=list(scratch),
        input_output_aliases=aliases or {},
        compiler_params=pltpu.CompilerParams(vmem_limit_bytes=limit << 20),
        cost_estimate=pl.CostEstimate(flops=us * 10**9, bytes_accessed=0, transcendentals=0),
        name=name,
    )(*values)


def start_copies(pairs, sems):
    copies = [
        pltpu.make_async_copy(source, target, sems.at[k])
        for k, (source, target) in enumerate(pairs)
    ]
    for copy in copies:
        copy.start()
    return copies


def row_mean(value):
    return jnp.mean(value, axis=-1, keepdims=True)


def normalize(values):
    center = values - row_mean(values)
    inverse = lax.rsqrt(row_mean(center * center) + NORM_EPSILON)
    return center * inverse, inverse


def lanes_of(head, head_dim, width):
    lane = lax.broadcasted_iota(jnp.int32, (1, width), 1)
    return (lane >= head * head_dim) & (lane < (head + 1) * head_dim)


def assemble(chunks, target):
    rows = chunks[0].shape[0]
    for k, chunk in enumerate(chunks):
        target[k * rows : (k + 1) * rows, :] = chunk[...]


def only(flag, value):
    return jnp.where(flag, value, jnp.zeros_like(value))


def shards(weights):
    if len(weights) == 1:
        rows = weights[0].shape[0]
        return [(pl.ds(0, rows), weights[0])]
    count = len(weights)
    rows = weights[0].shape[0]
    f = lax.axis_index("fsdp")
    found = []
    for d, ref in enumerate(weights):
        place = lax.rem(f + (count - d), count)
        found.append((pl.ds(pl.multiple_of(place * rows, rows), rows), ref))
    return found


def pack_attn_kernel(layer, feats, qkv_hbm, out_hbm, packed_ref, token, qkv, out, sems):
    ci = lax.rem(lax.axis_index("ctx"), GROUP)
    span = pl.ds(pl.multiple_of(ci * feats, feats), feats)
    copies = start_copies(
        [(qkv_hbm.at[layer, :, :, span], qkv), (out_hbm.at[layer, span, :], out)], sems
    )
    copies[0].wait()
    for k in range(3):
        packed_ref[:, k * feats : (k + 1) * feats] = qkv[k]
    copies[1].wait()
    packed_ref[:, 3 * feats :] = out[...].T
    token[...] = jnp.zeros_like(token)


def pack_mlp_kernel(layer, hidden, fc1_hbm, fc2_hbm, packed_ref, token, fc1, fc2, sems):
    ci = lax.rem(lax.axis_index("ctx"), GROUP)
    span = pl.ds(pl.multiple_of(ci * hidden, hidden), hidden)
    copies = start_copies(
        [(fc1_hbm.at[layer, :, span], fc1), (fc2_hbm.at[layer, span, :], fc2)], sems
    )
    copies[0].wait()
    packed_ref[:, :hidden] = fc1[...]
    copies[1].wait()
    packed_ref[:, hidden:] = fc2[...].T
    token[...] = jnp.zeros_like(token)


def prep_upstream_kernel(tp, outer, lengths, cotangent_hbm,
                         upstream_hbm, upstream_b_ref, usable_ref, mask_ref,
                         rows_in, upstream_ref, sems):
    rows = rows_in.shape[0]
    c = lax.axis_index("ctx")
    t = lax.axis_index("tp")
    place = lax.rem(c, GROUP) * tp + t
    start = pl.multiple_of(t * rows, rows)
    copies = start_copies(
        [(cotangent_hbm.at[0, pl.ds(start, rows), :], rows_in)], sems.at[pl.ds(0, 1)]
    )
    lane = lax.broadcasted_iota(jnp.int32, usable_ref.shape, 1)
    limit = jnp.zeros(usable_ref.shape, jnp.int32)
    for o in range(outer):
        for k, d in enumerate(ORDER):
            source = place ^ d
            first_lane = (o * len(ORDER) + k) * rows
            count = lengths[0, o * GROUP + lax.div(source, tp)] - lax.rem(source, tp) * rows
            limit = jnp.where(lane >= first_lane, first_lane + jnp.clip(count, 0, rows), limit)
    usable_ref[...] = jnp.where(lane < limit, 1.0, 0.0)
    row = lax.broadcasted_iota(jnp.int32, mask_ref.shape, 0)
    mask = jnp.where(row + start < lengths[0, c], 1.0, 0.0)
    mask_ref[...] = mask
    copies[0].wait()
    upstream = rows_in[...] * mask[:, 0:1]
    upstream_ref[...] = upstream
    sent = start_copies([(upstream_ref, upstream_hbm)], sems.at[pl.ds(1, 1)])
    upstream_b_ref[...] = upstream.astype(bf16)
    sent[0].wait()


def prep_first_kernel(depth, inputs_hbm, vecs, stream_ref, first_ref, sems):
    rows = stream_ref.shape[0]
    start = pl.multiple_of(lax.axis_index("tp") * rows, rows)
    copies = start_copies([(inputs_hbm.at[0, pl.ds(start, rows), :], stream_ref)], sems)
    copies[0].wait()
    normed, _ = normalize(stream_ref[...])
    shift = vecs[2 * depth : 2 * depth + 1, :]
    first_ref[...] = (normed * vecs[0:1, :] + shift).astype(bf16)


def keep_rows_kernel(*refs):
    chunks, (near_hbm, far_hbm, token, near, far, sems) = refs[:8], refs[8:]
    assemble(chunks[:4], near)
    assemble(chunks[4:], far)
    for copy in start_copies([(near, near_hbm), (far, far_hbm)], sems):
        copy.wait()
    token[...] = jnp.zeros_like(token)


def qkv_kernel(feats, weight_count, *refs):
    c0, c1, c2, c3, *rest = refs
    weights = rest[:weight_count]
    bias, qkv_ref, x = rest[weight_count:]
    assemble((c0, c1, c2, c3), x)
    qkv = sum(dot(x[:, span], w[:, : 3 * feats]) for span, w in shards(weights))
    qkv_ref[:, :feats] = (qkv[:, :feats] + bias[0:1, :]).astype(bf16)
    qkv_ref[:, feats : 2 * feats] = qkv[:, feats : 2 * feats].astype(bf16)
    qkv_ref[:, 2 * feats :] = (qkv[:, 2 * feats :] + bias[1:2, :]).astype(bf16)


def attn_kernel(feats, heads, weight_count, part_count, keep_count, tile, *refs):
    q_ref, *rest = refs
    parts = rest[:part_count]
    weights = rest[part_count : part_count + weight_count]
    rest = rest[part_count + weight_count :]
    usable, *rest = rest
    kept, rest = rest[:keep_count], rest[keep_count:]
    partial_ref, attended_hbm, norm_hbm, *rest = rest
    kept_hbm, rest = rest[:keep_count], rest[keep_count:]
    keys, values, attended_ref, norm_ref, sems = rest
    head_dim = feats // heads
    scale = 1.0 / math.sqrt(head_dim)
    copies = start_copies(list(zip(kept, kept_hbm)), sems)
    first = 0
    for part in parts:
        rows, width = part.shape
        keys[first : first + rows, :] = part[:, width - 2 * feats : width - feats]
        values[first : first + rows, :] = part[:, width - feats :]
        first += rows
    keep = usable[...] > 0.5
    rows = q_ref.shape[0]
    for first in range(0, rows, tile):
        span = slice(first, first + tile)
        q = q_ref[span, :feats]
        attended = None
        for h in range(heads):
            own = lanes_of(h, head_dim, feats)
            scores = dot_nt(only(own, q), keys[...]) * scale
            scores = jnp.where(keep, scores, MASK_FILL)
            highest = jnp.max(scores, axis=-1, keepdims=True)
            raised = jnp.exp(scores - highest)
            total = jnp.sum(raised, axis=-1, keepdims=True)
            soft = (raised * (1.0 / total)).astype(bf16)
            result = dot(soft, values[...])
            log_norm = jnp.broadcast_to(highest + jnp.log(total), (tile, feats))
            if attended is None:
                attended, norms = result, log_norm
            else:
                attended = jnp.where(own, result, attended)
                norms = jnp.where(own, log_norm, norms)
        attended_ref[span, :] = attended.astype(bf16)
        norm_ref[span, :] = norms
    copies += start_copies(
        [(attended_ref, attended_hbm), (norm_ref, norm_hbm)],
        sems.at[pl.ds(keep_count, 2)],
    )
    for span, w in shards(weights):
        partial_ref[:, span] = dot_nt(attended_ref[...], w[:, 3 * feats :]).astype(bf16)
    for copy in copies:
        copy.wait()


def core_sum_kernel(count, *refs):
    pairs, owns = refs[: 2 * count], refs[2 * count : 3 * count]
    peers = refs[3 * count :]
    rows = owns[0].shape[0]
    for j in range(count):
        near, far = pairs[2 * j], pairs[2 * j + 1]
        for k in range(1 + len(peers)):
            span = slice(k * rows, (k + 1) * rows)
            total = near[span, :].astype(f32) + far[span, :].astype(f32)
            if k == 0:
                owns[j][...] = total
            else:
                peers[k - 1][j * rows : (j + 1) * rows, :] = total.astype(bf16)


def total_of(own, xy, x, y, part=0):
    rows = own.shape[0]
    span = slice(part * rows, (part + 1) * rows)
    return (
        own[...] + y[span, :].astype(f32) + x[span, :].astype(f32) + xy[span, :].astype(f32)
    )


def sum_norm_kernel(bias_row, gain_row, shift_row, own, xy, x, y, residual_hbm, vecs,
                    stream_ref, normed_ref, residual, sems):
    copies = start_copies([(residual_hbm, residual)], sems)
    total = total_of(own, xy, x, y) + vecs[bias_row : bias_row + 1, :]
    copies[0].wait()
    stream = residual[...] + total
    stream_ref[...] = stream
    normed, _ = normalize(stream)
    gain = vecs[gain_row : gain_row + 1, :]
    normed_ref[...] = (normed * gain + vecs[shift_row : shift_row + 1, :]).astype(bf16)


def sum_out_kernel(bias_row, own, xy, x, y, residual_hbm, vecs, mask, out_hbm, token,
                   residual, out_ref, sems):
    copies = start_copies([(residual_hbm, residual)], sems.at[pl.ds(0, 1)])
    total = total_of(own, xy, x, y, 1) + vecs[bias_row : bias_row + 1, :]
    copies[0].wait()
    out_ref[...] = (residual[...] + total) * mask[:, 0:1]
    token[...] = jnp.zeros_like(token)
    for copy in start_copies([(out_ref, out_hbm)], sems.at[pl.ds(1, 1)]):
        copy.wait()


def mlp_kernel(hidden, keep_count, saves, load_w, load_count, c0, c1, c2, c3, w, bias, *refs):
    kept, rest = refs[:keep_count], refs[keep_count:]
    sources, rest = rest[:load_count], rest[load_count:]
    partial_ref, x_out, act_out, slope_out, *rest = rest
    kept_hbm, rest = rest[:keep_count], rest[keep_count:]
    targets, rest = rest[:load_count], rest[load_count:]
    loaded = []
    if load_w:
        w_ref, *rest, w_sems, chunk_sems = rest
        rows = c0.shape[0]
        chunks = start_copies(
            [(c, x_out.at[pl.ds(k * rows, rows), :]) for k, c in enumerate((c0, c1, c2, c3))],
            chunk_sems,
        )
        spans = (pl.ds(0, hidden), pl.ds(hidden, hidden))
        loaded = start_copies([(w.at[:, c], w_ref.at[:, c]) for c in spans], w_sems)
        w = w_ref
    if load_count:
        *rest, load_sems = rest
        fetched = start_copies(list(zip(sources, targets)), load_sems)
    else:
        fetched = []
    if saves:
        x, act_ref, slope_ref, sems = rest
    else:
        x, act_ref, slope_ref = x_out, act_out, slope_out
        (sems,) = rest
    copies = start_copies(list(zip(kept, kept_hbm)), sems)
    if load_w:
        for chunk in chunks:
            chunk.wait()
    else:
        assemble((c0, c1, c2, c3), x)
    if saves:
        copies += start_copies([(x, x_out)], sems.at[pl.ds(keep_count, 1)])
    block = hidden // 2
    if load_w:
        loaded[0].wait()
    for k in range(2):
        span = slice(k * block, (k + 1) * block)
        pre = dot(x[...], w[:, span]) + bias[:, span]
        cdf = 0.5 * (1.0 + lax.erf(pre * ROOT_HALF))
        density = jnp.exp(-0.5 * pre * pre) * INV_ROOT_TAU
        slope_ref[k] = cdf + pre * density
        act_ref[:, span] = (pre * cdf).astype(bf16)
        if saves:
            copies += start_copies(
                [(slope_ref.at[k], slope_out.at[k])], sems.at[pl.ds(1 + keep_count + k, 1)]
            )
    if saves:
        copies += start_copies([(act_ref, act_out)], sems.at[pl.ds(3 + keep_count, 1)])
    if load_w:
        loaded[1].wait()
    partial_ref[...] = dot_nt(act_ref[...], w[:, hidden:]).astype(bf16)
    for copy in copies + fetched:
        copy.wait()


def mlp_back_kernel(hidden, chunk_count, fetches, *refs):
    chunks, (w, slope, *rest) = refs[:chunk_count], refs[chunk_count:]
    if fetches:
        *rest, slope_ref, slope_sem = rest
        fetched = start_copies([(slope, slope_ref)], slope_sem)
        slope = slope_ref
    partial_ref, grad_ref, sum_hbm, x, sum_ref, sems = rest
    assemble(chunks, x)
    grad = dot(x[...], w[:, hidden:])
    if fetches:
        fetched[0].wait()
    block = hidden // 2
    for k in range(2):
        span = slice(k * block, (k + 1) * block)
        part = grad[:, span] * slope[k]
        grad_ref[:, span] = part.astype(bf16)
        sum_ref[:, span] = jnp.sum(part, axis=0, keepdims=True)
    sent = start_copies([(sum_ref, sum_hbm)], sems)
    partial_ref[...] = dot_nt(grad_ref[...], w[:, :hidden]).astype(bf16)
    sent[0].wait()


def mlp_grad_kernel(hidden, keep_count, second_near, second_far, act_near, act_far,
                    up_near, up_far, grad_near, grad_far, *refs):
    kept, refs = refs[:keep_count], refs[keep_count:]
    out_hbm, *refs = refs
    kept_hbm, (out_one, out_two, sems) = refs[:keep_count], refs[keep_count:]
    sent = start_copies(list(zip(kept, kept_hbm)), sems.at[pl.ds(2, keep_count)])
    total = dot_tn(up_near[...], act_near[...]) + dot_tn(up_far[...], act_far[...])
    out_two[...] = total.astype(bf16)
    sent += start_copies(
        [(out_two, out_hbm.at[:, pl.ds(hidden, hidden)])], sems.at[pl.ds(0, 1)]
    )
    total = dot_tn(second_near[...], grad_near[...]) + dot_tn(second_far[...], grad_far[...])
    out_one[...] = total.astype(bf16)
    sent += start_copies([(out_one, out_hbm.at[:, pl.ds(0, hidden)])], sems.at[pl.ds(1, 1)])
    for copy in sent:
        copy.wait()


def norm_back(upstream, values, gain):
    normed, inverse = normalize(values)
    scaled = upstream * gain
    back = inverse * (scaled - row_mean(scaled) - normed * row_mean(scaled * normed))
    gain_grad = jnp.sum(upstream * normed, axis=0, keepdims=True)
    return back, gain_grad, jnp.sum(upstream, axis=0, keepdims=True)


def norm_back_two_kernel(gain_row, own, xy, x, y, values, upstream, vecs,
                         grad_ref, grad_b_ref, sums_ref):
    total = total_of(own, xy, x, y)
    up = upstream[...]
    back, gain_grad, shift_grad = norm_back(
        total, values[...], vecs[gain_row : gain_row + 1, :]
    )
    grad = up + back
    grad_ref[...] = grad
    grad_b_ref[...] = grad.astype(bf16)
    sums_ref[0:1, :] = gain_grad
    sums_ref[1:2, :] = shift_grad
    sums_ref[2:3, :] = jnp.sum(grad, axis=0, keepdims=True)
    sums_ref[3:4, :] = jnp.sum(up, axis=0, keepdims=True)


def norm_back_one_kernel(gain_row, own, xy, x, y, values, upstream, vecs, mask,
                         grad_ref, grad_b_ref, sums_ref):
    total = total_of(own, xy, x, y)
    back, gain_grad, shift_grad = norm_back(
        total, values[...], vecs[gain_row : gain_row + 1, :]
    )
    grad = upstream[...] + back
    if mask is not None:
        grad = grad * mask[:, 0:1]
    grad_ref[...] = grad
    grad_b_ref[...] = grad.astype(bf16)
    sums_ref[0:1, :] = gain_grad
    sums_ref[1:2, :] = shift_grad


def attn_back_kernel(feats, heads, weight_count, part_count, tile, carried, *refs):
    c0, c1, c2, c3, *rest = refs
    weights, rest = rest[:weight_count], rest[weight_count:]
    usable, qkv, attended, norms, *rest = rest
    parts, rest = rest[:part_count], rest[part_count:]
    if carried:
        keys_before, values_before, *rest = rest
    x, grad_q, grad_k, grad_v, pairs, grad_att = rest
    head_dim = feats // heads
    scale = 1.0 / math.sqrt(head_dim)
    first = 0
    for part in parts:
        rows, width = part.shape
        pairs[first : first + rows, :] = part[:, width - 2 * feats :]
        first += rows
    assemble((c0, c1, c2, c3), x)
    grad_att[...] = sum(
        dot(x[:, span], w[:, 3 * feats :]) for span, w in shards(weights)
    ).astype(bf16)
    keep = usable[...] > 0.5
    rows = qkv.shape[0]
    if carried:
        sum_k, sum_v = keys_before[...], values_before[...]
    else:
        sum_k = jnp.zeros(grad_k.shape, f32)
        sum_v = jnp.zeros(grad_v.shape, f32)
    keys, values = pairs[:, :feats], pairs[:, feats:]
    for first in range(0, rows, tile):
        span = slice(first, first + tile)
        q = qkv[span, :feats]
        ga = grad_att[span, :]
        products = ga.astype(f32) * attended[span, :].astype(f32)
        gq = None
        for h in range(heads):
            own = lanes_of(h, head_dim, feats)
            q_h = only(own, q)
            ga_h = only(own, ga)
            row_dots = jnp.sum(only(own, products), axis=-1, keepdims=True)
            scores = dot_nt(q_h, keys) * scale
            scores = jnp.where(keep, scores, MASK_FILL)
            soft = jnp.exp(scores - norms[span, h * head_dim : h * head_dim + 1])
            grad_soft = dot_nt(ga_h, values)
            grad_scores = (soft * (grad_soft - row_dots)).astype(bf16)
            part = dot(grad_scores, keys)
            gq = part if gq is None else jnp.where(own, part, gq)
            sum_k = sum_k + dot_tn(grad_scores, q_h) * scale
            sum_v = sum_v + dot_tn(soft.astype(bf16), ga_h)
        grad_q[span, :] = gq * scale
    grad_k[...] = sum_k
    grad_v[...] = sum_v


def project_kernel(feats, first, weight_count, gq, gk, gv, *refs):
    weights, (partial_ref, packed) = refs[:weight_count], refs[weight_count:]
    rows = gq.shape[0]
    span = slice(first, first + rows)
    packed[:, :feats] = gq[...].astype(bf16)
    packed[:, feats : 2 * feats] = gk[span, :].astype(bf16)
    packed[:, 2 * feats :] = gv[span, :].astype(bf16)
    for columns, w in shards(weights):
        partial_ref[:, columns] = dot_nt(packed[...], w[:, : 3 * feats]).astype(bf16)


def attn_grad_kernel(feats, count, keep_count, first_near, first_far, att_near, att_far,
                     up_near, up_far, gq_near, gq_far, gk, gv, passed, lines, *refs):
    kept, refs = refs[:keep_count], refs[keep_count:]
    outs, refs = refs[:count], refs[count:]
    heads_hbm, passed_ref, *refs = refs
    kept_hbm, (packed, sums_ref, *staged, sems) = refs[:keep_count], refs[keep_count:]
    rows = up_near.shape[0]
    used = count + 2
    sent = start_copies(
        [(passed, passed_ref), *zip(kept, kept_hbm)], sems.at[pl.ds(used, 1 + keep_count)]
    )
    packed[:rows, :feats] = gq_near[...].astype(bf16)
    packed[rows:, :feats] = gq_far[...].astype(bf16)
    packed[:, feats : 2 * feats] = gk[...].astype(bf16)
    packed[:, 2 * feats :] = gv[...].astype(bf16)
    sums_ref[0:1, :] = jnp.sum(gq_near[...], axis=0, keepdims=True) + jnp.sum(
        gq_far[...], axis=0, keepdims=True
    )
    sums_ref[1:2, :] = jnp.sum(gv[...], axis=0, keepdims=True)
    sent += start_copies([(sums_ref, heads_hbm)], sems.at[pl.ds(0, 1)])

    def out_part(span):
        return dot_tn(up_near[:, span], att_near[...]) + dot_tn(up_far[:, span], att_far[...])

    def qkv_part(span):
        return dot_tn(first_near[:, span], packed[:rows, :]) + dot_tn(
            first_far[:, span], packed[rows:, :]
        )

    if count == 1:
        out_one, out_two = staged
        whole = slice(None)
        out_two[...] = out_part(whole).astype(bf16)
        sent += start_copies(
            [(out_two, outs[0].at[:, pl.ds(3 * feats, feats)])], sems.at[pl.ds(1, 1)]
        )
        out_one[...] = qkv_part(whole).astype(bf16)
        sent += start_copies(
            [(out_one, outs[0].at[:, pl.ds(0, 3 * feats)])], sems.at[pl.ds(2, 1)]
        )
    else:
        (stage,) = staged
        below = lines.shape[1]
        width_own = outs[0].shape[0] - below
        for d in reversed(range(count)):
            place = lax.rem(lax.axis_index("fsdp") + d, count)
            span = pl.ds(pl.multiple_of(place * width_own, width_own), width_own)
            stage[d, :width_own, : 3 * feats] = qkv_part(span).astype(bf16)
            stage[d, :width_own, 3 * feats :] = out_part(span).astype(bf16)
            stage[d, width_own:, :] = lines[d]
            sent += start_copies([(stage.at[d], outs[d])], sems.at[pl.ds(1 + d, 1)])
    for copy in sent:
        copy.wait()


def settle_kernel(keep_count, after_count, passed, *refs):
    kept, refs = refs[:keep_count], refs[keep_count + after_count :]
    passed_ref, *kept_hbm, sems = refs
    for copy in start_copies([(passed, passed_ref), *zip(kept, kept_hbm)], sems):
        copy.wait()


def fetch_kernel(count, *refs):
    sources, (target, sems) = refs[:count], refs[count:]
    columns = target.shape[1]
    moves = []
    row = 0
    for source in sources:
        rows = source.shape[0]
        for first in range(0, source.shape[1], columns):
            moves.append(
                (source.at[:, pl.ds(first, columns)], target.at[pl.ds(row, rows), :])
            )
            row += rows
    for copy in start_copies(moves, sems):
        copy.wait()


def shard_sum_kernel(depth, own_hbm, mine_a, mine_b, cross_a, cross_b, *refs):
    *others, part_ref, mine_ref, pair_ref, own, sems = refs
    moves = [(own_hbm, own)]
    row = 0
    for source in (mine_a, mine_b, cross_a, cross_b):
        count = source.shape[0]
        moves.append((source, pair_ref.at[pl.ds(row, count), :]))
        row += count
    first, *copies = start_copies(moves, sems)
    first.wait()
    rows, width = part_ref.shape[0], mine_ref.shape[1]
    terms = [ref[...].astype(f32) for ref in (own, *others)]
    total = terms[0]
    for term in terms[1:]:
        total = total + term
    part_ref[...] = total[:rows, :].astype(bf16)
    lines = total[rows:, :width] + total[rows:, width:]
    mine_ref[: 6 * depth, :] = lines[: 6 * depth, :]
    for k in range(mine_ref.shape[0] - 16):
        mine_ref[16 + k : 17 + k, :] = lines[6 * depth + k : 6 * depth + k + 1, :]
    for copy in copies:
        copy.wait()


def place_kernel(depth, hidden, feats, here, sibling, *refs):
    qkv_hbm, out_hbm, fc1_hbm, fc2_hbm, token, fc1, fc2, qkv, out, sems = refs
    token[...] = jnp.zeros_like(token)
    ci = lax.rem(lax.axis_index("ctx"), GROUP)
    rows = fc1.shape[2]
    count = here.shape[0] // 2
    copies = []

    def send(source, target):
        copies.extend(start_copies([(source, target)], sems.at[pl.ds(len(copies), 1)]))

    for k in range(GROUP):
        stacked = (here, sibling)[k % 2].at[pl.ds(k // 2 * count, count), :]
        wide = pl.ds(pl.multiple_of((ci ^ k) * hidden, hidden), hidden)
        narrow = pl.ds(pl.multiple_of((ci ^ k) * feats, feats), feats)
        for l in range(depth):
            first = 0 if l == 0 else (3 * l - 1) * rows
            fc1[l, k] = stacked[first : first + rows, :].astype(f32)
            send(fc1.at[l, k], fc1_hbm.at[l, :, wide])
            fc2[l, k] = stacked[first + rows : first + 2 * rows, :].T.astype(f32)
            send(fc2.at[l, k], fc2_hbm.at[l, wide, :])
            if l > 0:
                piece = stacked.at[pl.ds(first + 2 * rows, rows), :]
                for j in range(3):
                    qkv[l - 1, k, j] = piece[:, j * feats : (j + 1) * feats].astype(f32)
                send(qkv.at[l - 1, k], qkv_hbm.at[l, :, :, narrow])
                out[l - 1, k] = piece[:, 3 * feats :].T.astype(f32)
                send(out.at[l - 1, k], out_hbm.at[l, narrow, :])
    for copy in copies:
        copy.wait()


def place_last_kernel(feats, vectors, here, sibling, qkv_in, out_in, mine, far, *refs):
    qkv_hbm, out_hbm, *vector_refs, qkv, out, sems = refs
    ci = lax.rem(lax.axis_index("ctx"), GROUP)
    rows = here.shape[0] // 2
    copies = []
    for k in range(GROUP):
        piece = (here, sibling)[k % 2].at[pl.ds(k // 2 * rows, rows), :]
        span = pl.ds(pl.multiple_of((ci ^ k) * feats, feats), feats)
        for j in range(3):
            qkv[k, j] = piece[:, j * feats : (j + 1) * feats].astype(f32)
        copies += start_copies(
            [(qkv.at[k], qkv_hbm.at[0, :, :, span])], sems.at[pl.ds(2 * k, 1)]
        )
        out[k] = piece[:, 3 * feats :].T.astype(f32)
        copies += start_copies(
            [(out.at[k], out_hbm.at[0, span, :])], sems.at[pl.ds(2 * k + 1, 1)]
        )
    vectors(mine, far, *vector_refs)
    for copy in copies:
        copy.wait()


def vector_pack_kernel(depth, one_now, gq_near, gq_far, gv, *refs):
    count = 5 * depth - 2
    out_ref, *found, sems = refs[count:]
    copies = start_copies(list(zip(refs[:count], found)), sems)
    out_ref[...] = jnp.zeros_like(out_ref)
    feats = gv.shape[1]
    head_now = [
        jnp.sum(gq_near[...], axis=0, keepdims=True) + jnp.sum(gq_far[...], axis=0, keepdims=True),
        jnp.sum(gv[...], axis=0, keepdims=True),
    ]
    for copy in copies:
        copy.wait()
    for l in range(depth):
        if l == 0:
            one, (two, unit_near, unit_far) = one_now, found[:3]
            heads = head_now
        else:
            one, two, unit_near, unit_far, head = found[5 * l - 2 : 5 * l + 3]
            heads = [head[0:1, :], head[1:2, :]]
        out_ref[6 * l : 6 * l + 1, :] = one[0:1, :]
        out_ref[6 * l + 1 : 6 * l + 2, :] = two[0:1, :]
        out_ref[6 * l + 2 : 6 * l + 3, :] = one[1:2, :]
        out_ref[6 * l + 3 : 6 * l + 6, :] = two[1:4, :]
        units = unit_near.shape[1]
        row = 6 * depth
        out_ref[row : row + 1, l * units : (l + 1) * units] = unit_near[...] + unit_far[...]
        for j in range(2):
            start = (2 * l + j) * feats
            out_ref[row + 1 : row + 2, start : start + feats] = heads[j]


def vector_lines_kernel(depth, width_own, packed, lines_ref):
    count = lines_ref.shape[0]
    f = lax.axis_index("fsdp")
    total = packed[...]
    high = total.astype(bf16).astype(f32)
    low = total - high
    lines_ref[...] = jnp.zeros_like(lines_ref)
    last = 6 * depth
    for k, value in enumerate((high, low)):
        lanes = slice(k * width_own, (k + 1) * width_own)
        columns = [value[:, a * width_own : (a + 1) * width_own] for a in range(count)]
        for d in range(count):
            mine = columns[0]
            for a in range(1, count):
                mine = jnp.where(lax.rem(f + d, count) == a, columns[a], mine)
            rows = [mine[:last, :]]
            for r in range(2):
                for a in range(count):
                    rows.append(columns[a][last + r : last + r + 1, :])
            rows.append(jnp.zeros((lines_ref.shape[1] - last - 2 * count, width_own), f32))
            lines_ref[d, :, lanes] = jnp.concatenate(rows, axis=0).astype(bf16)


def vector_plane_kernel(depth, own, xy, x, y, part, part_x, out_ref, pair_ref):
    last = 6 * depth
    rows = part.shape[0]
    pair_ref[:rows, :] = part[...]
    pair_ref[rows:, :] = part_x[...]
    out_ref[:last, :] = own[:last, :] + xy[:last, :] + x[:last, :] + y[:last, :]
    out_ref[16:24, :] = own[16:24, :]
    out_ref[24:32, :] = x[16:24, :]


def vector_place_kernel(depth, head_dim, own, far, gains_ref, shifts_ref, unit_ref, heads_ref):
    total = own[: 6 * depth, :] + far[: 6 * depth, :]
    for l in range(depth):
        gains_ref[l] = total[6 * l : 6 * l + 2, :]
        shifts_ref[l] = total[6 * l + 2 : 6 * l + 6, :]
    pieces = (own[16:24, :], far[16:24, :], own[24:32, :], far[24:32, :])
    ci = lax.rem(lax.axis_index("ctx"), GROUP)
    f = lax.axis_index("fsdp")

    def of_place(c):
        k = ci ^ c
        found = pieces[0]
        for j in range(1, GROUP):
            found = jnp.where(k == j, pieces[j], found)
        return found

    width_own = own.shape[1]
    units = of_place(f)
    parts = unit_ref.shape[2] // width_own
    for l in range(depth):
        for j in range(parts):
            row = l * parts + j
            unit_ref[l, :, j * width_own : (j + 1) * width_own] = units[row : row + 1, :]
    head_own = heads_ref.shape[3]
    heads = heads_ref.shape[2] // GROUP
    for c in range(GROUP):
        found = of_place(c)
        for l in range(depth):
            for j in range(2):
                for h in range(heads):
                    first = ((2 * l + j) * heads + h) * head_dim
                    row, lane = 4 + first // width_own, first % width_own
                    value = found[row : row + 1, lane : lane + head_own]
                    for a in range(1, head_dim // head_own):
                        start = lane + a * head_own
                        value = jnp.where(
                            f == a, found[row : row + 1, start : start + head_own], value
                        )
                    heads_ref[l, j, c * heads + h : c * heads + h + 1, :] = value


def place_rows_kernel(count, *refs):
    terms, outs, sems = refs[: 2 * count], refs[2 * count : 3 * count], refs[-1]
    rows = terms[0].shape[0]
    start = pl.multiple_of(lax.axis_index("tp") * rows, rows)
    places = (pl.ds(start, rows), pl.ds(pl.multiple_of(rows - start, rows), rows))
    moves = [
        (terms[2 * k + j], out.at[0, places[j], :]) for k, out in enumerate(outs) for j in range(2)
    ]
    for copy in start_copies(moves, sems):
        copy.wait()


def per_device(
    inputs, lengths, cotangent, norm_gains, shifts, qv_bias, fc1_bias, w_qkv, w_out, w_fc1, w_fc2
):
    depth = w_qkv.shape[0]
    width_own = w_qkv.shape[2]
    fsdp = lax.axis_size("fsdp")
    tp = lax.axis_size("tp")
    ctx = lax.axis_size("ctx")
    outer = ctx // GROUP
    rows = inputs.shape[1] // tp
    half = rows * CHIPS
    all_rows = 2 * half
    head_own = qv_bias.shape[3]
    head_dim = head_own * fsdp
    heads = qv_bias.shape[2] // GROUP
    feats = heads * head_dim
    hidden = w_fc1.shape[2] // GROUP
    width = width_own * fsdp
    t = lax.axis_index("tp")
    f = lax.axis_index("fsdp")
    ci = lax.axis_index("ctx") % GROUP
    tile = half // 2
    attn_limit = 12 if outer == 1 else 48

    def swap_core(value):
        return lax.ppermute(value, "ctx", [(i, i ^ 1) for i in range(ctx)])

    def swap_x(value):
        return lax.ppermute(value, "ctx", [(i, i ^ 2) for i in range(ctx)])

    def swap_y(value):
        return lax.ppermute(value, "tp", [(i, i ^ 1) for i in range(tp)])

    def swap_xy(value):
        pairs = [
            (i * tp + k, (i ^ 2) * tp + (k ^ 1)) for i in range(ctx) for k in range(tp)
        ]
        return lax.ppermute(value, ("ctx", "tp"), pairs)

    def shift_z(value, d):
        return lax.ppermute(value, "fsdp", [(i, (i + d) % fsdp) for i in range(fsdp)])

    outer_groups = [[o * GROUP + i for o in range(outer)] for i in range(GROUP)]

    def gather_rows(own):
        near = (own, swap_xy(own), swap_x(own), swap_y(own))
        return near, tuple(swap_core(chunk) for chunk in near)

    def settle(value, there, *kept):
        shape = value.value if isinstance(value, Far) else value
        return kernel_call(
            functools.partial(settle_kernel, len(kept), 1),
            [(shape.shape, shape.dtype)] + [saved(k.shape, k.dtype) for k in kept],
            value,
            *kept,
            Far(there),
            name="settle",
            scratch=[DMA((1 + len(kept),))],
        )

    def reduce_rows(*pairs, after=()):
        count = len(pairs)
        *owns, xy, x, y = kernel_call(
            functools.partial(core_sum_kernel, count),
            [((rows, width), f32)] * count + [((count * rows, width), bf16)] * 3,
            *[v for near, far in pairs for v in (near, swap_core(far))],
            name="core_sum",
            after=after,
        )
        peers = (swap_xy(xy), swap_x(x), swap_y(y))
        return [(own, *peers) for own in owns]

    def pack_attn(l, after):
        return kernel_call(
            functools.partial(pack_attn_kernel, l, feats),
            [((width_own, 4 * feats), bf16), TOKEN],
            Far(w_qkv),
            Far(w_out),
            name="pack_attn",
            after=after,
            scratch=[
                pltpu.VMEM((3, width_own, feats), bf16),
                pltpu.VMEM((feats, width_own), bf16),
                DMA((2,)),
            ],
        )

    def pack_mlp(l, after):
        return kernel_call(
            functools.partial(pack_mlp_kernel, l, hidden),
            [((width_own, 2 * hidden), bf16), TOKEN],
            Far(w_fc1),
            Far(w_fc2),
            name="pack_mlp",
            after=after,
            scratch=[
                pltpu.VMEM((width_own, hidden), bf16),
                pltpu.VMEM((hidden, width_own), bf16),
                DMA((2,)),
            ],
        )

    attn_w = []
    mlp_w = []
    token = None
    for l in range(depth):
        own, token = pack_attn(l, () if token is None else (token,))
        attn_w.append((lax.all_gather(own, "fsdp", axis=0, tiled=True),))
        own, token = pack_mlp(l, (token,))
        mlp_w.append(lax.all_gather(own, "fsdp", axis=0, tiled=True))
        if l == 0:
            pack_token = token

    qv_own = lax.dynamic_slice_in_dim(qv_bias, ci * heads, heads, axis=2)
    vec_rows = depth * 6
    c1_rows = depth * fc1_bias.shape[2] // width_own
    qv_own = qv_own.reshape(1, -1)
    small_own = jnp.concatenate(
        [
            norm_gains.reshape(-1, width_own),
            shifts.reshape(-1, width_own),
            fc1_bias.reshape(-1, width_own),
            jnp.pad(qv_own, ((0, 0), (0, width_own - qv_own.shape[1]))),
        ],
        axis=0,
    )
    shifted = [small_own] + [shift_z(small_own, d) for d in range(1, fsdp)]

    def shard(a):
        picked = shifted[0]
        for d in range(1, fsdp):
            picked = jnp.where((f - d) % fsdp == a, shifted[d], picked)
        return picked.astype(f32)

    small = [shard(a) for a in range(fsdp)]
    vecs = jnp.concatenate([s[:vec_rows] for s in small], axis=1)
    fc1_all = shard(ci)[vec_rows : vec_rows + c1_rows].reshape(depth, 1, hidden)
    qv_all = jnp.stack(
        [s[vec_rows + c1_rows, : qv_own.shape[1]].reshape(depth, 2, heads, head_own) for s in small],
        axis=3,
    ).reshape(depth, 2, feats)

    def gain_row(l, i):
        return 2 * l + i

    def shift_row(l, i):
        return 2 * depth + 4 * l + i

    key_rows = outer * all_rows
    row_f32 = ((rows, width), f32)
    row_bf16 = ((rows, width), bf16)
    upstream, upstream_b, usable, mask = kernel_call(
        functools.partial(prep_upstream_kernel, tp, outer),
        [saved((rows, width), f32), row_bf16, ((1, key_rows), f32), ((rows, 128), f32)],
        Scalars(lengths),
        Far(cotangent),
        name="prep_upstream",
        after=(pack_token,),
        scratch=[pltpu.VMEM((rows, width), f32), pltpu.VMEM((rows, width), f32), DMA((2,))],
    )
    near, far = gather_rows(upstream_b)
    half_x = pltpu.VMEM((half, width), bf16)
    *upstream_rows, upstream_token = kernel_call(
        keep_rows_kernel,
        [saved((half, width), bf16)] * 2 + [TOKEN],
        *near,
        *far,
        name="keep_rows",
        scratch=[half_x, half_x, DMA((2,))],
    )
    stream, first = kernel_call(
        functools.partial(prep_first_kernel, depth),
        [row_f32, row_bf16],
        Far(inputs),
        vecs,
        name="prep_first",
        scratch=[DMA((1,))],
    )
    first_chunks = gather_rows(first)

    partial_out = ((half, width), bf16)
    saved_all = []
    for l in range(depth):
        qkv = []
        first_x = []
        for side in (0, 1):
            qkv_half, x_half = kernel_call(
                functools.partial(qkv_kernel, feats, len(attn_w[l])),
                [((half, 3 * feats), bf16), ((half, width), bf16)],
                *first_chunks[side],
                *attn_w[l],
                qv_all[l],
                name="qkv",
                after=(upstream_token,) if l == 0 and side == 0 else (),
            )
            qkv.append(qkv_half)
            first_x.append(x_half)
        if outer > 1:
            pairs = jnp.concatenate([part[:, feats:] for part in qkv], axis=0)
            pairs = lax.all_gather(
                pairs, "ctx", axis=0, tiled=True, axis_index_groups=outer_groups
            )
            key_parts = (pairs,)
        else:
            key_parts = tuple(qkv)
        attn = [None, None]
        for side in (1, 0):
            kept = (first_x[side], qkv[side]) + ((stream,) if side == 1 else ())
            attn[side] = kernel_call(
                functools.partial(
                    attn_kernel, feats, heads, len(attn_w[l]), len(key_parts), len(kept), tile
                ),
                [partial_out, saved((half, feats), bf16), saved((half, feats), f32)]
                + [saved(k.shape, k.dtype) for k in kept],
                qkv[side],
                *key_parts,
                *attn_w[l],
                usable,
                *kept,
                name="attn",
                limit=attn_limit,
                scratch=[
                    pltpu.VMEM((key_rows, feats), bf16),
                    pltpu.VMEM((key_rows, feats), bf16),
                    pltpu.VMEM((half, feats), bf16),
                    pltpu.VMEM((half, feats), f32),
                    DMA((len(kept) + 2,)),
                ],
            )
        (sums,) = reduce_rows((attn[0][0], attn[1][0]))
        middle, second = kernel_call(
            functools.partial(sum_norm_kernel, shift_row(l, 2), gain_row(l, 1), shift_row(l, 1)),
            [row_f32, row_bf16],
            *sums,
            Far(attn[1][5]),
            vecs,
            name="sum_norm",
            scratch=[pltpu.VMEM((rows, width), f32), DMA((1,))],
        )
        second_chunks = gather_rows(second)
        mlp = [None, None]
        for side in (1, 0):
            kept = (middle,) if side == 1 else ()
            saves = l + 1 < depth
            load_w = not saves and side == 1
            loads = tuple(upstream_rows) if not saves and side == 0 else ()
            shapes = [
                ((half, width), bf16),
                ((half, hidden), bf16),
                ((2, half, hidden // 2), f32),
            ]
            mlp[side] = kernel_call(
                functools.partial(mlp_kernel, hidden, len(kept), saves, load_w, len(loads)),
                [partial_out]
                + [saved(*shape) if saves else shape for shape in shapes]
                + [saved(k.shape, k.dtype) for k in kept]
                + [(v.shape, v.dtype) for v in loads]
                + ([(mlp_w[l].shape, bf16)] if load_w else []),
                *[Anywhere(c) if load_w else c for c in second_chunks[side]],
                Far(mlp_w[l]) if load_w else mlp_w[l],
                fc1_all[l],
                *kept,
                *[Far(v) for v in loads],
                name="mlp",
                scratch=[pltpu.VMEM(*shape) for shape in shapes if saves]
                + [DMA((4 + len(kept),))]
                + ([DMA((2,)), DMA((CHIPS,))] if load_w else [])
                + [DMA((len(loads),)) for _ in loads[:1]],
            )
            if load_w:
                *mlp[side], mlp_w[l] = mlp[side]
            if loads:
                *mlp[side], near, far = mlp[side]
                upstream_chunks = [(near,), (far,)]
        saved_all.append((attn, pairs if outer > 1 else None, mlp))
        if l + 1 < depth:
            (sums,) = reduce_rows((mlp[0][0], mlp[1][0]))
            stream, first = kernel_call(
                functools.partial(
                    sum_norm_kernel, shift_row(l, 3), gain_row(l + 1, 0), shift_row(l + 1, 0)
                ),
                [row_f32, row_bf16],
                *sums,
                Far(mlp[1][4]),
                vecs,
                name="sum_norm",
                scratch=[pltpu.VMEM((rows, width), f32), DMA((1,))],
            )
            first_chunks = gather_rows(first)

    def scatter_grads(grad):
        part = lax.psum_scatter(grad, "fsdp", scatter_dimension=0, tiled=True)
        if outer > 1:
            part = lax.psum(part, "ctx", axis_index_groups=outer_groups)
        return part

    row_sums = [None] * depth
    unit_sums = [None] * depth
    head_sums = [None] * depth
    mlp_parts = [None] * depth
    attn_parts = [None] * depth
    for l in reversed(range(depth)):
        attn, pairs, mlp = saved_all[l]
        back = [None, None]
        for side in (1, 0):
            fetches = l + 1 < depth and side == 0
            back[side] = kernel_call(
                functools.partial(mlp_back_kernel, hidden, len(upstream_chunks[side]), fetches),
                [
                    partial_out,
                    ((half, hidden), bf16),
                    saved((1, hidden), f32),
                    ((half, width), bf16),
                ],
                *upstream_chunks[side],
                mlp_w[l],
                Far(mlp[side][3]) if fetches else mlp[side][3],
                name="mlp_back",
                scratch=[pltpu.VMEM((1, hidden), f32), DMA((1,))]
                + ([pltpu.VMEM(mlp[side][3].shape, f32), DMA((1,))] if fetches else []),
            )
        kept = [back[0][0], back[1][0]]
        if l + 1 == depth:
            kept += [mlp[0][0], mlp[1][0]]
        mlp_grad, *kept = kernel_call(
            functools.partial(mlp_grad_kernel, hidden, len(kept)),
            [saved((width, 2 * hidden), bf16)] + [saved(k.shape, k.dtype) for k in kept],
            mlp[0][1],
            mlp[1][1],
            mlp[0][2],
            mlp[1][2],
            back[0][3],
            back[1][3],
            back[0][1],
            back[1][1],
            *kept,
            name="mlp_grad",
            scratch=[
                pltpu.VMEM((width, hidden), bf16),
                pltpu.VMEM((width, hidden), bf16),
                DMA((2 + len(kept),)),
            ],
        )
        mlp_parts[l] = scatter_grads(mlp_grad)
        (sums,) = reduce_rows(tuple(kept[:2]))
        if l + 1 == depth:
            output_pair = tuple(kept[2:])
        unit_sums[l] = (back[0][2], back[1][2])
        grad_middle, middle_b, sums_two = kernel_call(
            functools.partial(norm_back_two_kernel, gain_row(l, 1)),
            [row_f32, row_bf16, ((4, width), f32)],
            *sums,
            mlp[1][4],
            upstream,
            vecs,
            name="norm_back_two",
        )
        if l + 1 < depth:
            middle_b, sums_two, grad_middle = settle(
                middle_b, attn_parts[l + 1], sums_two, grad_middle
            )
        middle_chunks = gather_rows(middle_b)
        grad_q = [None, None]
        middle_x = [None, None]
        carried = ()
        for side in (0, 1):
            key_parts = (pairs,) if outer > 1 else (attn[0][4], attn[1][4])
            middle_x[side], grad_q[side], *carried = kernel_call(
                functools.partial(
                    attn_back_kernel,
                    feats,
                    heads,
                    len(attn_w[l]),
                    len(key_parts),
                    tile,
                    len(carried) > 0,
                ),
                [
                    ((half, width), bf16),
                    ((half, feats), f32),
                    ((key_rows, feats), f32),
                    ((key_rows, feats), f32),
                ],
                *middle_chunks[side],
                *attn_w[l],
                usable,
                attn[side][4],
                attn[side][1],
                attn[side][2],
                *key_parts,
                *carried,
                name="attn_back",
                scratch=[
                    pltpu.VMEM((key_rows, 2 * feats), bf16),
                    pltpu.VMEM((half, feats), bf16),
                ],
                limit=attn_limit,
            )
        grad_k, grad_v = carried
        if outer > 1:
            grad_k, grad_v = (
                lax.psum_scatter(
                    v, "ctx", scatter_dimension=0, tiled=True, axis_index_groups=outer_groups
                )
                for v in (grad_k, grad_v)
            )

        def project(side, after):
            return kernel_call(
                functools.partial(project_kernel, feats, side * half, len(attn_w[l])),
                [partial_out],
                grad_q[side],
                grad_k,
                grad_v,
                *attn_w[l],
                name="project",
                after=after,
                scratch=[pltpu.VMEM((half, 3 * feats), bf16)],
            )[0]

        far_part = project(1, ())
        near_part = project(0, ())
        pairs_now = [(near_part, far_part)]
        if l == 0:
            pairs_now.append(output_pair)
        sums, *output_sums = reduce_rows(*pairs_now)
        body = functools.partial(norm_back_one_kernel, gain_row(l, 0))
        if l > 0:
            masked = ()
            body = lambda *refs, body=body: body(*refs[:7], None, *refs[7:])
        else:
            masked = (mask,)
        upstream, upstream_b, sums_one = kernel_call(
            body,
            [row_f32, row_bf16, ((2, width), f32)],
            *sums,
            attn[1][5],
            grad_middle,
            vecs,
            *masked,
            name="norm_back_one",
        )
        lines = ()
        if l == 0:
            terms = [sums_two, *unit_sums[0]]
            for k in range(1, depth):
                terms += [*row_sums[k], *unit_sums[k], head_sums[k]]
            packed = kernel_call(
                functools.partial(vector_pack_kernel, depth),
                [((6 * depth + 2, width), f32)],
                sums_one,
                *grad_q,
                grad_v,
                *[Far(v) for v in terms],
                name="vector_pack",
                scratch=[pltpu.VMEM(v.shape, f32) for v in terms] + [DMA((len(terms),))],
            )[0]
            if outer > 1:
                packed = lax.psum(packed, "ctx", axis_index_groups=outer_groups)
            lines = kernel_call(
                functools.partial(vector_lines_kernel, depth, width_own),
                [((fsdp, 32, 2 * width_own), bf16)],
                packed,
                name="vector_lines",
            )
        count = 1 if l > 0 else fsdp
        shapes = [((width, 3 * feats), bf16), ((width, feats), bf16)]
        if l == 0:
            shapes = [((fsdp, width_own + 32, 4 * feats), bf16)]
        sums_now, rows_now = sums_one, upstream
        kept = [sums_one, upstream] + ([sums_two] if l + 1 == depth else [])
        *attn_grads, head_sums[l], upstream_b, sums_one, upstream, sums_kept = [
            *kernel_call(
                functools.partial(attn_grad_kernel, feats, count, len(kept)),
                [saved((width if l > 0 else width_own + 32, 4 * feats), bf16)] * count
                + [saved((2, feats), f32), saved(*row_bf16) if l > 0 else row_bf16]
                + [saved(k.shape, k.dtype) for k in kept],
                attn[0][3],
                attn[1][3],
                attn[0][1],
                attn[1][1],
                *middle_x,
                *grad_q,
                grad_k,
                grad_v,
                upstream_b,
                *(lines or (sums_one,)),
                *kept,
                name="attn_grad",
                scratch=[
                    pltpu.VMEM((all_rows, 3 * feats), bf16),
                    pltpu.VMEM((2, feats), f32),
                ]
                + [pltpu.VMEM(*shape) for shape in shapes]
                + [DMA((count + 3 + len(kept),))],
            ),
            sums_two,
        ][: count + 5]
        if l + 1 == depth:
            sums_two = sums_kept
        if l > 0:
            attn_parts[l] = scatter_grads(attn_grads[0])
            (upstream_b,) = settle(Far(upstream_b), mlp_parts[l])
            upstream_chunks = gather_rows(upstream_b)
        row_sums[l] = (sums_one, sums_two)

    blocks = 3 * depth - 1

    def fetch(sources, after):
        count = sum(v.shape[1] // hidden for v in sources)
        return kernel_call(
            functools.partial(fetch_kernel, len(sources)),
            [((count * width_own, hidden), bf16)],
            *[Far(v) for v in sources],
            name="fetch",
            after=after,
            scratch=[DMA((count,))],
        )[0]

    upper = [v for l in range(1, depth) for v in (mlp_parts[l], attn_parts[l])]
    stacked = (fetch(mlp_parts[:1], (upstream_b,)), fetch(upper, (sums_now,)))
    crossed = [swap_x(v) for v in stacked]
    own_term, *other_terms = attn_grads
    other_terms = [shift_z(term, d + 1) for d, term in enumerate(other_terms)]
    inputs_other = swap_y(rows_now)
    outputs_own, output_token = kernel_call(
        functools.partial(sum_out_kernel, shift_row(depth - 1, 3)),
        [saved((rows, width), f32), TOKEN],
        *output_sums[0],
        Far(saved_all[depth - 1][2][1][4]),
        vecs,
        mask,
        name="sum_out",
        after=(Anywhere(inputs_other),),
        scratch=[pltpu.VMEM((rows, width), f32)] * 2 + [DMA((2,))],
    )
    part, mine, pair = kernel_call(
        functools.partial(shard_sum_kernel, depth),
        [
            ((width_own, 4 * feats), bf16),
            ((24, width_own), f32),
            ((2 * blocks * width_own, hidden), bf16),
        ],
        Far(own_term),
        *[Anywhere(v) for v in (*stacked, *crossed)],
        *other_terms,
        name="shard_sum",
        after=(output_token,),
        scratch=[pltpu.VMEM(own_term.shape, bf16), DMA((5,))],
    )
    others = (inputs_other, swap_y(outputs_own))
    if outer > 1:
        part = lax.psum(part, "ctx", axis_index_groups=outer_groups)
    *placed, place_token = kernel_call(
        functools.partial(place_kernel, depth, hidden, feats),
        [saved(v.shape, f32) for v in (w_qkv, w_out, w_fc1, w_fc2)] + [TOKEN],
        pair,
        swap_core(pair),
        name="place",
        limit=24,
        scratch=[
            pltpu.VMEM((depth, GROUP, width_own, hidden), f32),
            pltpu.VMEM((depth, GROUP, hidden, width_own), f32),
            pltpu.VMEM((depth - 1, GROUP, 3, width_own, feats), f32),
            pltpu.VMEM((depth - 1, GROUP, feats, width_own), f32),
            DMA((16 * depth,)),
        ],
    )
    mine, last_pair = kernel_call(
        functools.partial(vector_plane_kernel, depth),
        [((32, width_own), f32), ((2 * width_own, 4 * feats), bf16)],
        mine,
        swap_xy(mine),
        swap_x(mine),
        swap_y(mine),
        part,
        swap_x(part),
        name="vector_plane",
        after=(place_token, Anywhere(others[1])),
    )
    grad_inputs, outputs = kernel_call(
        functools.partial(place_rows_kernel, 2),
        [saved(inputs.shape, f32)] * 2,
        *(upstream, others[0], outputs_own, others[1]),
        name="place_rows",
        scratch=[DMA((4,))],
    )
    *placed[:2], grad_gains, grad_shifts, grad_fc1_bias, grad_qv_bias = kernel_call(
        functools.partial(
            place_last_kernel, feats, functools.partial(vector_place_kernel, depth, head_dim)
        ),
        [saved(v.shape, f32) for v in (w_qkv, w_out)]
        + [(v.shape, f32) for v in (norm_gains, shifts, fc1_bias, qv_bias)],
        last_pair,
        swap_core(last_pair),
        Far(placed[0]),
        Far(placed[1]),
        mine,
        swap_core(mine),
        name="place_last",
        scratch=[
            pltpu.VMEM((GROUP, 3, width_own, feats), f32),
            pltpu.VMEM((GROUP, feats, width_own), f32),
            DMA((2 * GROUP,)),
        ],
        aliases={2: 0, 3: 1},
    )
    return (
        outputs,
        grad_inputs,
        grad_gains,
        grad_shifts,
        grad_qv_bias,
        grad_fc1_bias,
        *placed,
    )


def solution(mesh):
    rows = P("fsdp", "ctx", None)
    params = (
        P(None, None, "fsdp"),
        P(None, None, "fsdp"),
        P(None, None, "tp", "fsdp"),
        P(None, "tp", "fsdp"),
        P(None, None, "fsdp", "tp"),
        P(None, "tp", "fsdp"),
        P(None, "fsdp", "tp"),
        P(None, "tp", "fsdp"),
    )
    return jax.shard_map(
        per_device,
        mesh=mesh,
        in_specs=(rows, P("fsdp", None), rows) + params,
        out_specs=(rows, rows) + params,
        check_vma=False,
    )
```
